32 devices in a mesh: seq: 8 (over y, x, core), ch: 4 (over z).
Axes of the slice: x: 2, y: 2, z: 4, core: 2. Of those that a mesh axis runs over, the one named last changes fastest.
Arguments:
- inputs: bfloat16 [32, 2048, 768], P(None, 'seq'), may hold values from -6 to 6
- lengths: int32 [32], replicated, may hold values from 256 to 1024, as said below
- input_gain: float32 [768], replicated, may hold values from 0.25 to 1.75
- input_shift: float32 [768], replicated, may hold values from -3 to 3
- conv_weight: bfloat16 [5, 768, 768], replicated, may hold values from -0.09375 to 0.09375
- branch_gain: float32 [768], P('ch'), may hold values from 0.25 to 1.75
- branch_shift: float32 [768], P('ch'), may hold values from -3 to 3
- dilated_tap_weight: bfloat16 [3, 768, 384], P(None, None, 'ch'), may hold values from -0.125 to 0.125
- mixer_gain: float32 [384], P('ch'), may hold values from 0.25 to 1.75
- mixer_shift: float32 [384], P('ch'), may hold values from -3 to 3
- point_weight: bfloat16 [384, 768], P('ch'), may hold values from -0.3125 to 0.3125
- point_bias: float32 [768], P('ch'), may hold values from -3 to 3
- cotangent: bfloat16 [32, 1024, 768], P(None, 'seq'), may hold values from -6 to 6
Outputs:
- result: bfloat16 [32, 1024, 768], P(None, 'seq', 'ch')
- input_grad: bfloat16 [32, 2048, 768], P(None, 'seq', 'ch')
- conv_weight_grad: float32 [5, 768, 768], P(None, None, 'ch')
- input_gain_grad: float32 [768], P('ch')
- input_shift_grad: float32 [768], P('ch')
- branch_gain_grad: float32 [768], P('ch')
- branch_shift_grad: float32 [768], P('ch')
- dilated_weight_grad: float32 [3, 768, 384], P(None, None, 'ch')
- mixer_gain_grad: float32 [384], P('ch')
- mixer_shift_grad: float32 [384], P('ch')
- point_weight_grad: float32 [384, 768], P('ch')
- point_bias_grad: float32 [768], P('ch')
The draws below stay inside these ranges and needn't reach their ends.
Inputs may be any that keep to these rules, and one draw needn't show every extreme that they name: `lengths`: at least one window has all 1024 pooled bins valid.
All inputs are finite; a program needn't handle non-finite values.
Results may differ from the reference program's by a relative error of at most 0.029.
Values may be sent and summed in bfloat16 or wider, within the bound.
A program may use at most 320 MiB of HBM per device.

```python
from functools import partial
import jax
import jax.numpy as jnp
from jax import lax

C = 768
H = 384
K1 = 5
K2 = 3
DILATION_STEP = 14
WIN = 1024
NWIN = 32
PRE = 2048


def draw_lengths(key, part):
    key = jax.random.fold_in(key, 11)
    draw_key, pick_key = jax.random.split(key)
    values = jax.random.randint(draw_key, (NWIN,), WIN // 4, WIN + 1)
    chosen = jax.random.randint(pick_key, (), 0, NWIN)
    return jnp.where(jnp.arange(NWIN) == chosen, WIN, values).astype(jnp.int32)


def shard_levels(own_key, dims, shards, least, largest):
    def one(axis_at, shards_of):
        steps = jax.random.uniform(jax.random.fold_in(jax.random.fold_in(own_key, 6), axis_at), (shards_of,), jnp.float32, least / len(shards), largest / len(shards))
        return jnp.repeat(jnp.exp(steps), dims[axis_at] // shards_of).reshape((-1,) + (1,) * (len(dims) - axis_at - 1))

    gain = one(*shards[0])
    for cut in shards[1:]:
        gain = gain * one(*cut)
    return gain


def centred(rng, shape, scale, most, shards=(), kind=jnp.bfloat16):
    result = jax.random.normal(rng, shape, jnp.float32) * scale
    if len(shards) > 0:
        result = shard_levels(rng, shape, shards, -0.22, 0.18) * result
    return jnp.clip(result, min=-most, max=most).astype(kind)


def setup_inputs(seed: int = 0) -> dict:
    key_list = jax.random.split(jax.random.key(seed), 14)
    inputs = centred(key_list[0], (NWIN, PRE, C), 1.0, 6.0, ((1, 8),))
    lengths = draw_lengths(jax.random.fold_in(key_list[13], 71), 0)
    input_gain = jnp.clip(1.0 + 0.15 * jax.random.normal(key_list[2], (C,), jnp.float32), 0.25, 1.75)
    input_shift = centred(key_list[3], (C,), 0.5, 3.0, (), jnp.float32)
    conv_weight = centred(key_list[4], (K1, C, C), (K1 * C) ** -0.5, 0.09375)
    branch_gain = jnp.clip(1.0 + 0.15 * jax.random.normal(key_list[5], (C,), jnp.float32), 0.25, 1.75)
    branch_shift = centred(key_list[6], (C,), 0.5, 3.0, ((0, 4),), jnp.float32)
    dilated_tap_weight = centred(key_list[7], (K2, C, H), (K2 * C) ** -0.5, 0.125, ((2, 4),))
    mixer_gain = jnp.clip(1.0 + 0.15 * jax.random.normal(key_list[8], (H,), jnp.float32), 0.25, 1.75)
    mixer_shift = centred(key_list[9], (H,), 0.5, 3.0, ((0, 4),), jnp.float32)
    point_weight = centred(key_list[10], (H, C), H ** -0.5, 0.3125, ((0, 4),))
    point_bias = centred(key_list[11], (C,), 0.5, 3.0, ((0, 4),), jnp.float32)
    cotangent = centred(key_list[12], (NWIN, WIN, C), 1.0, 6.0, ((1, 8),))
    return {"inputs": inputs, "lengths": lengths, "input_gain": input_gain, "input_shift": input_shift, "conv_weight": conv_weight, "branch_gain": branch_gain, "branch_shift": branch_shift, "dilated_tap_weight": dilated_tap_weight, "mixer_gain": mixer_gain, "mixer_shift": mixer_shift, "point_weight": point_weight, "point_bias": point_bias, "cotangent": cotangent}


EPS = 1e-05

@jax.custom_vjp
def low(v):
    return lax.optimization_barrier(v.astype(jnp.bfloat16)).astype(jnp.float32)

@jax.custom_vjp
def lower_backward(v):
    return v

def low_keep(v):
    return (low(v), None)

def low_pass(kept, grad):
    return (grad,)

def back_keep(v):
    return (v, None)

def back_low(kept, grad):
    return (low(grad),)
low.defvjp(low_keep, low_pass)
lower_backward.defvjp(back_keep, back_low)

def window_conv(values, weight, spacing):
    taps = weight.shape[0]
    reach = (taps - 1) // 2 * spacing
    length = values.shape[0]
    padded = jnp.pad(values, ((reach, reach), (0, 0)))
    total = jnp.zeros((length, weight.shape[2]), jnp.float32)
    for filter_tap_index in range(taps):
        total = total + jnp.dot(padded[filter_tap_index * spacing:filter_tap_index * spacing + length], weight[filter_tap_index], precision=lax.Precision.HIGHEST, preferred_element_type=jnp.float32)
    return total

def apply_convolution(values, weight, spacing):
    single = jax.checkpoint(partial(window_conv, spacing=spacing))
    return lax.map(lambda window: single(window, weight), values)

def standardize(values, valid_mask, valid_total):
    mean_value = lax.optimization_barrier(jnp.sum(values * valid_mask, axis=(0, 1))) / valid_total
    square_mean = lax.optimization_barrier(jnp.sum(values * values * valid_mask, axis=(0, 1))) / valid_total
    return (values - mean_value) * lax.rsqrt(square_mean - mean_value * mean_value + EPS)

def reference(inputs, lengths, input_gain, input_shift, conv_weight, branch_gain, branch_shift, dilated_tap_weight, mixer_gain, mixer_shift, point_weight, point_bias, cotangent):
    valid_total = jnp.sum(lengths).astype(jnp.float32)
    positions_pre = jnp.arange(2 * WIN, dtype=jnp.int32)
    positions = jnp.arange(WIN, dtype=jnp.int32)
    mask_pre = (positions_pre[None, :] // 2 < lengths[:, None]).astype(jnp.float32)[:, :, None]
    valid_mask = (positions[None, :] < lengths[:, None]).astype(jnp.float32)[:, :, None]

    def forward(inputs, input_gain, input_shift, conv_weight, branch_gain, branch_shift, dilated_tap_weight, mixer_gain, mixer_shift, point_weight, point_bias):
        first_act = low(jax.nn.gelu(input_gain * standardize(inputs, mask_pre, 2.0 * valid_total) + input_shift)) * mask_pre
        conv_out = lower_backward(apply_convolution(first_act, conv_weight, 1))
        pooled = (conv_out[:, 0::2] + conv_out[:, 1::2]) * 0.5
        second_activation = low(jax.nn.gelu(branch_gain * standardize(pooled, valid_mask, valid_total) + branch_shift)) * valid_mask
        dilated_output = lower_backward(apply_convolution(second_activation, dilated_tap_weight, DILATION_STEP))
        third_act = low(jax.nn.gelu(mixer_gain * standardize(dilated_output, valid_mask, valid_total) + mixer_shift)) * valid_mask
        mixed = jnp.einsum('wjh,hc->wjc', third_act, point_weight, precision=lax.Precision.HIGHEST) + point_bias
        return (pooled + mixed) * valid_mask
    primals = (inputs.astype(jnp.float32), input_gain, input_shift, conv_weight.astype(jnp.float32), branch_gain, branch_shift, dilated_tap_weight.astype(jnp.float32), mixer_gain, mixer_shift, point_weight.astype(jnp.float32), point_bias)
    output, pull = jax.vjp(forward, *primals)
    grads = pull(cotangent.astype(jnp.float32))
    return (output.astype(jnp.bfloat16), grads[0].astype(jnp.bfloat16), grads[3], grads[1], grads[2], grads[4], grads[5], grads[6], grads[7], grads[8], grads[9], grads[10])
```

```python
from functools import partial

import jax
import jax.numpy as jnp
from jax import lax
from jax.experimental import pallas as pl
from jax.experimental.pallas import tpu as pltpu
from jax.sharding import PartitionSpec as P

DIL = 14
EDGE = 16
EPS = 1e-05
GC0 = 0.7978845608028654
GC1 = 0.044715
F32 = jnp.float32
BF16 = jnp.bfloat16
MESH = pl.DeviceIdType.MESH
VMEM_LIMIT = 58 * 1024 * 1024


def gelu(z):
    t = jnp.tanh(z * (GC0 + (GC0 * GC1) * (z * z)))
    hz = 0.5 * z
    return hz + hz * t


def gelu_both(z):
    sq = z * z
    t = jnp.tanh(z * (GC0 + (GC0 * GC1) * sq))
    hz = 0.5 * z
    slope = 0.5 + 0.5 * t + hz * (1.0 - t * t) * (GC0 + (3.0 * GC0 * GC1) * sq)
    return hz + hz * t, slope


def gelu_slope(z):
    return gelu_both(z)[1]


def rows_of(shape):
    return lax.broadcasted_iota(jnp.int32, shape, 0)


def norm_of(stats, total):
    mean = stats[0:1] / total
    square = stats[1:2] / total
    return mean, lax.rsqrt(square - mean * mean + EPS)


def mm(a, b):
    return jnp.dot(a, b, preferred_element_type=F32)


def mm_nt(a, b):
    return lax.dot_general(a, b, (((1,), (1,)), ((), ())), preferred_element_type=F32)


def mm_tn(a, b):
    return lax.dot_general(a, b, (((0,), (0,)), ((), ())), preferred_element_type=F32)


def params(**kw):
    return pltpu.CompilerParams(vmem_limit_bytes=VMEM_LIMIT, **kw)


def cost(flops, nbytes):
    return pl.CostEstimate(flops=int(flops), bytes_accessed=int(nbytes), transcendentals=0)


def whole(shape):
    return pl.BlockSpec(shape, lambda t, *_: (0,) * len(shape), pipeline_mode=pl.Buffered(1))


def smem():
    return pl.BlockSpec(memory_space=pltpu.SMEM)


def exchange_kernel(n_seq, n_grp, whole_axis, n_halo, *refs):
    packet = refs[0]
    edges = refs[1 : 1 + n_halo]
    out = refs[1 + n_halo]
    halos = refs[2 + n_halo : 2 + 3 * n_halo]
    buf, send_sem, recv_sem, halo_send, halo_recv = refs[2 + 3 * n_halo :]
    s = lax.axis_index("seq")
    z = lax.axis_index("ch")
    base = 0 if whole_axis else (z // n_grp) * n_grp
    count = n_seq * n_grp
    me = s * n_grp + (z - base)

    def place(q):
        return (q // n_grp, base + q % n_grp)

    barrier = pltpu.get_barrier_semaphore()
    for off in range(1, count):
        pl.semaphore_signal(
            barrier, inc=1, device_id=place((me + off) % count), device_id_type=MESH
        )
    pl.semaphore_wait(barrier, count - 1)
    left = ((s + n_seq - 1) % n_seq, z)
    right = ((s + 1) % n_seq, z)
    copies = []
    for n in range(n_halo):
        low, high = halos[2 * n], halos[2 * n + 1]
        for side, (dst, dev) in enumerate(((high, left), (low, right))):
            copies.append(
                pltpu.make_async_remote_copy(
                    src_ref=edges[n].at[side],
                    dst_ref=dst,
                    send_sem=halo_send.at[2 * n + side],
                    recv_sem=halo_recv.at[2 * n + side],
                    device_id=dev,
                    device_id_type=MESH,
                )
            )
    sends = []
    for off in range(1, count):
        sends.append(
            pltpu.make_async_remote_copy(
                src_ref=packet,
                dst_ref=buf.at[me],
                send_sem=send_sem.at[off],
                recv_sem=recv_sem.at[me],
                device_id=place((me + off) % count),
                device_id_type=MESH,
            )
        )
    for c in sends:
        c.start()
    for c in copies:
        c.start()
    buf[me] = packet[...]
    for off in range(1, count):
        q = (me + off) % count
        pltpu.make_async_remote_copy(
            src_ref=packet,
            dst_ref=buf.at[q],
            send_sem=send_sem.at[off],
            recv_sem=recv_sem.at[q],
            device_id=place(q),
            device_id_type=MESH,
        ).wait_recv()
    acc = buf[0]
    for q in range(1, count):
        acc = acc + buf[q]
    out[...] = acc
    for c in sends:
        c.wait_send()
    for c in copies:
        c.wait()


def exchange(packet, edges, cid, n_grp, whole_axis):
    n_seq = lax.axis_size("seq")
    count = n_seq * n_grp
    n_halo = len(edges)
    halo_shapes = []
    for e in edges:
        halo_shapes += [jax.ShapeDtypeStruct(e.shape[1:], e.dtype)] * 2
    outs = pl.pallas_call(
        partial(exchange_kernel, n_seq, n_grp, whole_axis, n_halo),
        out_shape=[jax.ShapeDtypeStruct(packet.shape, F32)] + halo_shapes,
        in_specs=[pl.BlockSpec(memory_space=pltpu.VMEM)]
        + [pl.BlockSpec(memory_space=pl.ANY)] * n_halo,
        out_specs=[pl.BlockSpec(memory_space=pltpu.VMEM)]
        + [pl.BlockSpec(memory_space=pl.ANY)] * (2 * n_halo),
        scratch_shapes=[
            pltpu.VMEM((count,) + packet.shape, F32),
            pltpu.SemaphoreType.DMA((count,)),
            pltpu.SemaphoreType.DMA((count,)),
            pltpu.SemaphoreType.DMA((max(2 * n_halo, 1),)),
            pltpu.SemaphoreType.DMA((max(2 * n_halo, 1),)),
        ],
        compiler_params=pltpu.CompilerParams(collective_id=cid, has_side_effects=True),
        name=f"exchange{cid}",
    )(packet, *edges)
    return outs[0], outs[1:]


def input_moments_kernel(wb, L, meta, lens, x, out, acc):
    t = pl.program_id(0)

    @pl.when(t == 0)
    def _():
        acc[...] = jnp.zeros_like(acc)

    rows = rows_of((L, x.shape[2]))
    for w in range(wb):
        valid = 2 * lens[meta[2] + t * wb + w] - meta[0] * L
        v = jnp.where(rows < valid, x[w].astype(F32), 0.0)
        v3 = v.reshape(L // 8, 8, v.shape[1])
        acc[0] += jnp.sum(v3, axis=0)
        acc[1] += jnp.sum(v3 * v3, axis=0)

    @pl.when(t == pl.num_programs(0) - 1)
    def _():
        out[0:1] = jnp.sum(acc[0], axis=0, keepdims=True)
        out[1:2] = jnp.sum(acc[1], axis=0, keepdims=True)


def conv_kernel(
    wb, L, meta, lens, x, xl, xr, w_ref, sel, stats, gain, shift, total,
    X5, x2, edge, sums,
):
    t = pl.program_id(0)
    s = meta[0]
    Lp = L // 2
    C = x.shape[2]
    mean, rho = norm_of(stats[...], 2.0 * total[0])
    scale = gain[...] * rho
    offset = shift[...] - mean * scale
    rows = rows_of((L, C))
    row2 = rows_of((2, C))
    row16 = rows_of((16, C))

    @pl.when(t == 0)
    def _():
        sums[...] = jnp.zeros_like(sums)

    for w in range(wb):
        valid = 2 * lens[meta[1] + t * wb + w] - s * L
        a = gelu(x[w].astype(F32) * scale + offset)
        a = jnp.where(rows < valid, a, 0.0).astype(BF16)
        picked = mm(sel[...], a)
        for k in range(5):
            X5[w * Lp : (w + 1) * Lp, k * C : (k + 1) * C] = picked[
                k * Lp : (k + 1) * Lp
            ].astype(BF16)
        la = gelu(xl[w].astype(F32) * scale + offset)
        la = jnp.where((row2 - 2 < valid) & (s > 0), la, 0.0).astype(BF16).astype(F32)
        ra = gelu(xr[w].astype(F32) * scale + offset)
        ra = jnp.where(row2 + L < valid, ra, 0.0).astype(BF16).astype(F32)
        top, end = w * Lp, (w + 1) * Lp
        X5[top : top + 16, 0:C] = (
            picked[0:16] + jnp.where(row16 == 0, la[0:1] + la[1:2], 0.0)
        ).astype(BF16)
        X5[top : top + 16, C : 2 * C] = (
            picked[Lp : Lp + 16] + jnp.where(row16 == 0, la[1:2], 0.0)
        ).astype(BF16)
        X5[end - 16 : end, 3 * C : 4 * C] = (
            picked[4 * Lp - 16 : 4 * Lp] + jnp.where(row16 == 15, ra[0:1], 0.0)
        ).astype(BF16)
        X5[end - 16 : end, 4 * C : 5 * C] = (
            picked[5 * Lp - 16 : 5 * Lp] + jnp.where(row16 == 15, ra[0:1] + ra[1:2], 0.0)
        ).astype(BF16)

    nc = 256
    rowp = rows_of((Lp, nc))
    for n in range(C // nc):
        cols = slice(n * nc, (n + 1) * nc)
        y = 0.5 * mm(X5[...], w_ref[:, cols])
        s0 = jnp.zeros((1, nc), F32)
        s1 = jnp.zeros((1, nc), F32)
        for w in range(wb):
            valid = lens[meta[1] + t * wb + w] - s * Lp
            v = y[w * Lp : (w + 1) * Lp]
            x2[w, :, cols] = v
            edge[0, w, :, cols] = v[:EDGE].astype(BF16)
            edge[1, w, :, cols] = v[Lp - EDGE :].astype(BF16)
            v = jnp.where(rowp < valid, v, 0.0)
            s0 = s0 + jnp.sum(v, axis=0, keepdims=True)
            s1 = s1 + jnp.sum(v * v, axis=0, keepdims=True)
        sums[0:1, cols] += s0
        sums[1:2, cols] += s1


def dilated_kernel(
    wb, Lp, meta, lens, x2, lo, hi, w_ref, stats, gain, shift, total,
    Y3, c2, edge, sums, ext,
):
    t = pl.program_id(0)
    s = meta[0]
    C = x2.shape[2]
    H = w_ref.shape[1]
    mean, rho = norm_of(stats[...], total[0])
    scale = gain[...] * rho
    offset = shift[...] - mean * scale
    rows = rows_of((Lp, C))
    rowe = rows_of((EDGE, C))

    @pl.when(t == 0)
    def _():
        sums[...] = jnp.zeros_like(sums)

    for w in range(wb):
        valid = lens[meta[1] + t * wb + w] - s * Lp
        a = jnp.where(rows < valid, gelu(x2[w] * scale + offset), 0.0)
        al = gelu(lo[w].astype(F32) * scale + offset)
        al = jnp.where((rowe - EDGE < valid) & (s > 0), al, 0.0)
        ah = gelu(hi[w].astype(F32) * scale + offset)
        ah = jnp.where(rowe + Lp < valid, ah, 0.0)
        ext[0:EDGE] = al
        ext[EDGE : EDGE + Lp] = a
        ext[EDGE + Lp :] = ah
        top, end = w * Lp, (w + 1) * Lp
        Y3[top:end, 0:C] = ext[EDGE - DIL : EDGE - DIL + Lp].astype(BF16)
        Y3[top:end, C : 2 * C] = a.astype(BF16)
        Y3[top:end, 2 * C : 3 * C] = ext[EDGE + DIL : EDGE + DIL + Lp].astype(BF16)

    y = mm(Y3[...], w_ref[...])
    rowh = rows_of((Lp, H))
    s0 = jnp.zeros((1, H), F32)
    s1 = jnp.zeros((1, H), F32)
    for w in range(wb):
        valid = lens[meta[1] + t * wb + w] - s * Lp
        v = y[w * Lp : (w + 1) * Lp]
        c2[w] = v
        edge[0, w] = v[:EDGE].astype(BF16)
        edge[1, w] = v[Lp - EDGE :].astype(BF16)
        v = jnp.where(rowh < valid, v, 0.0)
        s0 = s0 + jnp.sum(v, axis=0, keepdims=True)
        s1 = s1 + jnp.sum(v * v, axis=0, keepdims=True)
    sums[0:1] += s0
    sums[1:2] += s1


def point_kernel(
    wb, Lp, g, meta, lens, c2, x2, cot, pw, pwh, pb, stats, gain, shift, total,
    res, dz, edge, sums, pgrad, bgrad, a3s, dos,
):
    t = pl.program_id(0)
    s = meta[0]
    C = cot.shape[2]
    H = c2.shape[2]
    cs = res.shape[3]
    mean, rho = norm_of(stats[...], total[0])
    scale = gain[...] * rho
    offset = shift[...] - mean * scale
    rowc = rows_of((Lp, C))
    rowh = rows_of((Lp, H))

    @pl.when(t == 0)
    def _():
        sums[...] = jnp.zeros_like(sums)
        pgrad[...] = jnp.zeros_like(pgrad)
        bgrad[...] = jnp.zeros_like(bgrad)

    s0 = jnp.zeros((1, H), F32)
    s1 = jnp.zeros((1, H), F32)
    sb = jnp.zeros((1, C), F32)
    for w in range(wb):
        valid = lens[meta[1] + t * wb + w] - s * Lp
        top, end = w * Lp, (w + 1) * Lp
        d = jnp.where(rowc < valid, cot[w].astype(F32), 0.0)
        sb = sb + jnp.sum(d, axis=0, keepdims=True)
        d = d.astype(BF16)
        dos[top:end] = d
        v = c2[w]
        act, slope = gelu_both(v * scale + offset)
        a3s[top:end] = jnp.where(rowh < valid, act, 0.0).astype(BF16)
        dzw = mm_nt(d, pw[...]) * slope
        dz[w] = dzw
        edge[0, w] = dzw[:EDGE].astype(BF16)
        edge[1, w] = dzw[Lp - EDGE :].astype(BF16)
        hat = (v - mean) * rho
        s0 = s0 + jnp.sum(dzw, axis=0, keepdims=True)
        s1 = s1 + jnp.sum(dzw * hat, axis=0, keepdims=True)
    sums[0:1] += s0
    sums[1:2] += s1
    bgrad[...] += sb
    y = mm(a3s[...], pwh[...])
    rowr = rows_of((Lp, y.shape[1]))
    for w in range(wb):
        valid = lens[meta[1] + t * wb + w] - s * Lp
        r = jnp.where(rowr < valid, x2[w] + y[w * Lp : (w + 1) * Lp] + pb[...], 0.0)
        r = r.astype(BF16)
        for k in range(g):
            res[k, w] = r[:, k * cs : (k + 1) * cs]
    pgrad[...] += mm_tn(a3s[...], dos[...])


def dilated_back_kernel(
    wb, Lp, meta, lens, c2, clo, chi, dz3, zlo, zhi, x2, Y3, wt,
    stats3, sums3, gain3, stats2, gain2, shift2, total,
    dz2, edge, sums, wgrad, ext, Z3,
):
    t = pl.program_id(0)
    s = meta[0]
    C = x2.shape[2]
    H = c2.shape[2]
    mean3, rho3 = norm_of(stats3[...], total[0])
    gr3 = gain3[...] * rho3
    sg3 = sums3[0:1] / total[0]
    gg3 = sums3[1:2] / total[0]
    mean2, rho2 = norm_of(stats2[...], total[0])
    scale2 = gain2[...] * rho2
    offset2 = shift2[...] - mean2 * scale2
    rowh = rows_of((Lp, H))
    rowe = rows_of((EDGE, H))
    rowc = rows_of((Lp, C))

    def back(dz, v):
        return gr3 * (dz - (sg3 + (v - mean3) * rho3 * gg3))

    @pl.when(t == 0)
    def _():
        sums[...] = jnp.zeros_like(sums)
        wgrad[...] = jnp.zeros_like(wgrad)

    for w in range(wb):
        valid = lens[meta[1] + t * wb + w] - s * Lp
        d = jnp.where(rowh < valid, back(dz3[w], c2[w]), 0.0)
        dl = back(zlo[w].astype(F32), clo[w].astype(F32))
        dl = jnp.where((rowe - EDGE < valid) & (s > 0), dl, 0.0)
        dh = back(zhi[w].astype(F32), chi[w].astype(F32))
        dh = jnp.where(rowe + Lp < valid, dh, 0.0)
        ext[0:EDGE] = dl
        ext[EDGE : EDGE + Lp] = d
        ext[EDGE + Lp :] = dh
        top, end = w * Lp, (w + 1) * Lp
        Z3[top:end, 0:H] = ext[EDGE + DIL : EDGE + DIL + Lp].astype(BF16)
        Z3[top:end, H : 2 * H] = d.astype(BF16)
        Z3[top:end, 2 * H : 3 * H] = ext[EDGE - DIL : EDGE - DIL + Lp].astype(BF16)

    y = mm(Z3[...], wt[...])
    s0 = jnp.zeros((1, C), F32)
    s1 = jnp.zeros((1, C), F32)
    for w in range(wb):
        valid = lens[meta[1] + t * wb + w] - s * Lp
        v = x2[w]
        dzw = y[w * Lp : (w + 1) * Lp] * gelu_slope(v * scale2 + offset2)
        dzw = jnp.where(rowc < valid, dzw, 0.0)
        dz2[w] = dzw
        edge[0, w] = dzw[0:1]
        edge[1, w] = dzw[Lp - 1 : Lp]
        s0 = s0 + jnp.sum(dzw, axis=0, keepdims=True)
        s1 = s1 + jnp.sum(dzw * ((v - mean2) * rho2), axis=0, keepdims=True)
    sums[0:1] += s0
    sums[1:2] += s1
    wgrad[...] += mm_tn(Z3[:, H : 2 * H], Y3[...])


def conv_back_kernel(
    wb, Lp, g, meta, lens, dz2, zlo, zhi, x2, lo, hi, cot, col, coh, xh, X5, weo, pick,
    stats2, sums2, gain2, stats1, gain1, shift1, total,
    gz, sums, wgrad, ext, D3, acc,
):
    t = pl.program_id(0)
    s = meta[0]
    C = x2.shape[2]
    L = 2 * Lp
    Ch = xh.shape[2]
    cs = gz.shape[3]
    mean2, rho2 = norm_of(stats2[...], total[0])
    gr2 = gain2[...] * rho2
    sg2 = sums2[0:1] / total[0]
    gg2 = sums2[1:2] / total[0]
    mean1, rho1 = norm_of(stats1[...], 2.0 * total[0])
    scale1 = gain1[...] * rho1
    offset1 = shift1[...] - mean1 * scale1
    rowc = rows_of((Lp, C))

    def back(dout, dz, v):
        return 0.5 * (dout + gr2 * (dz - (sg2 + (v - mean2) * rho2 * gg2)))

    @pl.when(t == 0)
    def _():
        sums[...] = jnp.zeros_like(sums)
        acc[...] = jnp.zeros_like(acc)

    for w in range(wb):
        valid = lens[meta[1] + t * wb + w] - s * Lp
        d = back(cot[w].astype(F32), dz2[w], x2[w])
        d = jnp.where(rowc < valid, d, 0.0)
        dl = back(col[w].astype(F32), zlo[w], lo[w, EDGE - 1 : EDGE].astype(F32))
        dl = jnp.where((valid > -1) & (s > 0), dl, 0.0)
        dh = back(coh[w].astype(F32), zhi[w], hi[w, 0:1].astype(F32))
        dh = jnp.where(valid > Lp, dh, 0.0)
        ext[7:8] = dl
        ext[8 : 8 + Lp] = d
        ext[8 + Lp : 9 + Lp] = dh
        top, end = w * Lp, (w + 1) * Lp
        D3[top:end, 0:C] = ext[9 : 9 + Lp].astype(BF16)
        D3[top:end, C : 2 * C] = d.astype(BF16)
        D3[top:end, 2 * C : 3 * C] = ext[7 : 7 + Lp].astype(BF16)

    ye = mm(D3[...], weo[0])
    yo = mm(D3[...], weo[1])
    rowb = rows_of((L, Ch))
    place = 2 * rowb - jnp.where(rowb >= Lp, L - 1, 0)
    s0 = jnp.zeros((1, Ch), F32)
    s1 = jnp.zeros((1, Ch), F32)
    for w in range(wb):
        valid = 2 * lens[meta[1] + t * wb + w] - s * L
        top, end = w * Lp, (w + 1) * Lp
        v = mm(pick[...], xh[w])
        da = jnp.concatenate([ye[top:end], yo[top:end]], axis=0)
        dzw = da * gelu_slope(v * scale1 + offset1)
        dzw = jnp.where(place < valid, dzw, 0.0)
        s0 = s0 + jnp.sum(dzw, axis=0, keepdims=True)
        s1 = s1 + jnp.sum(dzw * ((v - mean1) * rho1), axis=0, keepdims=True)
        dzw = dzw.astype(BF16)
        for k in range(g):
            gz[k, w] = dzw[:, k * cs : (k + 1) * cs]
    sums[0:1] += s0
    sums[1:2] += s1
    h = meta[4]
    dh = D3[:, pl.ds(pl.multiple_of(C + h * Ch, 128), Ch)]
    acc[...] += mm_tn(dh, X5[...])

    @pl.when(t == pl.num_programs(0) - 1)
    def _():
        wgrad[...] = acc[...].astype(BF16)


def input_grad_kernel(
    wb, L, g, meta, lens, x, gz, unpick, stats, sums, gain, total, old, out
):
    t = pl.program_id(0)
    s = meta[0]
    cs = gz.shape[2]
    mean, rho = norm_of(stats[...], 2.0 * total[0])
    gr = gain[...] * rho
    sg = sums[0:1] / (2.0 * total[0])
    gg = sums[1:2] / (2.0 * total[0])
    rows = rows_of((L, cs))
    i = meta[3]
    for w in range(wb):
        valid = 2 * lens[meta[5] + t * wb + w] - s * L
        v = x[w, :, 0:cs].astype(F32)
        for k in range(1, g):
            v = jnp.where(i == k, x[w, :, k * cs : (k + 1) * cs].astype(F32), v)
        dz = mm(unpick[...], gz[w])
        r = gr * (dz - (sg + (v - mean) * rho * gg))
        out[w] = jnp.where(rows < valid, r, 0.0).astype(BF16)


def per_device(
    inputs,
    lengths,
    input_gain,
    input_shift,
    conv_weight,
    branch_gain,
    branch_shift,
    dilated_tap_weight,
    mixer_gain,
    mixer_shift,
    point_weight,
    point_bias,
    cotangent,
):
    NW, L, C = inputs.shape
    Lp = L // 2
    ns, nz = lax.axis_size("seq"), lax.axis_size("ch")
    s, z = lax.axis_index("seq"), lax.axis_index("ch")
    T1 = conv_weight.shape[0]
    T2 = dilated_tap_weight.shape[0]
    R = 2
    g = nz // R
    i, h = z % g, z // g
    nw = NW // g
    cs = C // nz
    Ch = C // R
    H = mixer_gain.shape[0] * nz
    wb = min(nw, max(1, 512 // Lp))
    steps = nw // wb
    nw1 = NW // nz
    wb1 = min(nw1, wb)
    lens = lengths.astype(jnp.int32)
    total = jnp.sum(lens).astype(F32).reshape(1)
    meta = jnp.stack([s, i * nw, z * nw1, i, h, i * nw]).astype(jnp.int32)

    to_right = [(k, k + 1) for k in range(ns - 1)]
    to_left = [(k + 1, k) for k in range(ns - 1)]

    def edge_rows(a, at, n):
        return lax.dynamic_slice(a, (i * nw, at, 0), (nw, n, a.shape[2]))

    xl = lax.ppermute(edge_rows(inputs, L - 2, 2), "seq", to_right)
    xr = lax.ppermute(edge_rows(inputs, 0, 2), "seq", to_left)
    col = lax.ppermute(edge_rows(cotangent, Lp - 1, 1), "seq", to_right)
    coh = lax.ppermute(edge_rows(cotangent, 0, 1), "seq", to_left)

    dw = lax.all_gather(dilated_tap_weight, "ch", axis=2, tiled=True)
    pw = lax.all_gather(point_weight, "ch", axis=0, tiled=True)
    small = jnp.concatenate([branch_gain, branch_shift, point_bias, mixer_gain, mixer_shift])
    small = lax.all_gather(small, "ch", axis=0)
    c3 = C // nz
    h3 = H // nz
    gain2 = small[:, 0:c3].reshape(1, C)
    shift2 = small[:, c3 : 2 * c3].reshape(1, C)
    bias = small[:, 2 * c3 : 3 * c3].reshape(1, C)
    gain3 = small[:, 3 * c3 : 3 * c3 + h3].reshape(1, H)
    shift3 = small[:, 3 * c3 + h3 :].reshape(1, H)
    gain1 = input_gain.reshape(1, C)
    shift1 = input_shift.reshape(1, C)
    own = partial(lax.dynamic_slice_in_dim, start_index=h * Ch, slice_size=Ch, axis=1)

    dwf = dw.reshape(T2 * C, H)
    dwt = jnp.swapaxes(dw, 1, 2).reshape(T2 * H, C)
    pwh = own(pw)
    cw = conv_weight.reshape(T1 * C, C)
    cwh = lax.dynamic_slice_in_dim(conv_weight, h * Ch, Ch, axis=1)
    wt = jnp.swapaxes(cwh, 1, 2).astype(F32)
    weo = jnp.stack(
        [
            jnp.concatenate([wt[0], wt[1] + wt[2], wt[3] + wt[4]], axis=0),
            jnp.concatenate([wt[0] + wt[1], wt[2] + wt[3], wt[4]], axis=0),
        ]
    ).astype(BF16)

    at = jnp.arange(L)
    first = 2 * jnp.arange(Lp)[None, :] + jnp.arange(T1)[:, None] - 2
    first = first.reshape(T1 * Lp, 1)
    sel = ((at[None, :] == first) | (at[None, :] == first + 1)).astype(BF16)
    eo = jnp.concatenate([2 * jnp.arange(Lp), 2 * jnp.arange(Lp) + 1])
    pick = (at[None, :] == eo[:, None]).astype(BF16)
    unpick = pick.T

    stats1 = pl.pallas_call(
        partial(input_moments_kernel, wb1, L),
        grid_spec=pltpu.PrefetchScalarGridSpec(
            num_scalar_prefetch=2,
            grid=(nw1 // wb1,),
            in_specs=[pl.BlockSpec((wb1, L, C), lambda t, m, _: (m[2] // wb1 + t, 0, 0))],
            out_specs=pl.BlockSpec((2, C), lambda t, *_: (0, 0)),
            scratch_shapes=[pltpu.VMEM((2, 8, C), F32)],
        ),
        out_shape=jax.ShapeDtypeStruct((2, C), F32),
        compiler_params=params(),
        cost_estimate=cost(0, nw1 * L * C * 2),
        name="input_moments",
    )(meta, lens, inputs)
    stats1, _ = exchange(stats1, [], 1, nz, True)

    def win(shape, off=1):
        return pl.BlockSpec(shape, lambda t, m, _: (t,) + (0,) * (len(shape) - 1))

    def lead(shape):
        return pl.BlockSpec(shape, lambda t, m, _: (0, t) + (0,) * (len(shape) - 2))

    def arg_win(n, width):
        return pl.BlockSpec((wb, n, width), lambda t, m, _: (m[1] // wb + t, 0, 0))

    X5, x2, edge2, sums = pl.pallas_call(
        partial(conv_kernel, wb, L),
        grid_spec=pltpu.PrefetchScalarGridSpec(
            num_scalar_prefetch=2,
            grid=(steps,),
            in_specs=[
                arg_win(L, C),
                win((wb, 2, C)),
                win((wb, 2, C)),
                whole((T1 * C, C)),
                whole((T1 * Lp, L)),
                whole((2, C)),
                whole((1, C)),
                whole((1, C)),
                smem(),
            ],
            out_specs=[
                win((wb * Lp, T1 * C)),
                win((wb, Lp, C)),
                lead((2, wb, EDGE, C)),
                pl.BlockSpec((2, C), lambda t, *_: (0, 0)),
            ],
        ),
        out_shape=[
            jax.ShapeDtypeStruct((nw * Lp, T1 * C), BF16),
            jax.ShapeDtypeStruct((nw, Lp, C), F32),
            jax.ShapeDtypeStruct((2, nw, EDGE, C), BF16),
            jax.ShapeDtypeStruct((2, C), F32),
        ],
        compiler_params=params(),
        cost_estimate=cost(2 * nw * Lp * T1 * C * C, nw * Lp * C * 20),
        name="conv",
    )(meta, lens, inputs, xl, xr, cw, sel, stats1, gain1, shift1, total)
    stats2, (lo2, hi2) = exchange(sums, [edge2], 2, g, False)

    Y3, c2, edge3, sums = pl.pallas_call(
        partial(dilated_kernel, wb, Lp),
        grid_spec=pltpu.PrefetchScalarGridSpec(
            num_scalar_prefetch=2,
            grid=(steps,),
            in_specs=[
                win((wb, Lp, C)),
                win((wb, EDGE, C)),
                win((wb, EDGE, C)),
                whole((T2 * C, H)),
                whole((2, C)),
                whole((1, C)),
                whole((1, C)),
                smem(),
            ],
            out_specs=[
                win((wb * Lp, T2 * C)),
                win((wb, Lp, H)),
                lead((2, wb, EDGE, H)),
                pl.BlockSpec((2, H), lambda t, *_: (0, 0)),
            ],
            scratch_shapes=[pltpu.VMEM((Lp + 2 * EDGE, C), F32)],
        ),
        out_shape=[
            jax.ShapeDtypeStruct((nw * Lp, T2 * C), BF16),
            jax.ShapeDtypeStruct((nw, Lp, H), F32),
            jax.ShapeDtypeStruct((2, nw, EDGE, H), BF16),
            jax.ShapeDtypeStruct((2, H), F32),
        ],
        compiler_params=params(),
        cost_estimate=cost(2 * nw * Lp * T2 * C * H, nw * Lp * C * 12),
        name="dilated",
    )(meta, lens, x2, lo2, hi2, dwf, stats2, gain2, shift2, total)
    stats3, (lo3, hi3) = exchange(sums, [edge3], 3, g, False)

    res, dz3, edge3, sums, pgrad, bgrad = pl.pallas_call(
        partial(point_kernel, wb, Lp, g),
        grid_spec=pltpu.PrefetchScalarGridSpec(
            num_scalar_prefetch=2,
            grid=(steps,),
            in_specs=[
                win((wb, Lp, H)),
                pl.BlockSpec((wb, Lp, Ch), lambda t, m, _: (t, 0, m[4])),
                arg_win(Lp, C),
                whole((H, C)),
                whole((H, Ch)),
                whole((1, Ch)),
                whole((2, H)),
                whole((1, H)),
                whole((1, H)),
                smem(),
            ],
            out_specs=[
                lead((g, wb, Lp, cs)),
                win((wb, Lp, H)),
                lead((2, wb, EDGE, H)),
                pl.BlockSpec((2, H), lambda t, *_: (0, 0)),
                pl.BlockSpec((H, C), lambda t, *_: (0, 0)),
                pl.BlockSpec((1, C), lambda t, *_: (0, 0)),
            ],
            scratch_shapes=[pltpu.VMEM((wb * Lp, H), BF16), pltpu.VMEM((wb * Lp, C), BF16)],
        ),
        out_shape=[
            jax.ShapeDtypeStruct((g, nw, Lp, cs), BF16),
            jax.ShapeDtypeStruct((nw, Lp, H), F32),
            jax.ShapeDtypeStruct((2, nw, EDGE, H), BF16),
            jax.ShapeDtypeStruct((2, H), F32),
            jax.ShapeDtypeStruct((H, C), F32),
            jax.ShapeDtypeStruct((1, C), F32),
        ],
        compiler_params=params(),
        cost_estimate=cost(6 * nw * Lp * C * H, nw * Lp * C * 10),
        name="point",
    )(meta, lens, c2, x2, cotangent, pw, pwh, own(bias), stats3, gain3, shift3, total)
    sums3, (zlo3, zhi3) = exchange(sums, [edge3], 4, g, False)

    dz2, edge2, sums, wgrad2 = pl.pallas_call(
        partial(dilated_back_kernel, wb, Lp),
        grid_spec=pltpu.PrefetchScalarGridSpec(
            num_scalar_prefetch=2,
            grid=(steps,),
            in_specs=[
                win((wb, Lp, H)),
                win((wb, EDGE, H)),
                win((wb, EDGE, H)),
                win((wb, Lp, H)),
                win((wb, EDGE, H)),
                win((wb, EDGE, H)),
                win((wb, Lp, C)),
                win((wb * Lp, T2 * C)),
                whole((T2 * H, C)),
                whole((2, H)),
                whole((2, H)),
                whole((1, H)),
                whole((2, C)),
                whole((1, C)),
                whole((1, C)),
                smem(),
            ],
            out_specs=[
                win((wb, Lp, C)),
                lead((2, wb, 1, C)),
                pl.BlockSpec((2, C), lambda t, *_: (0, 0)),
                pl.BlockSpec((H, T2 * C), lambda t, *_: (0, 0)),
            ],
            scratch_shapes=[
                pltpu.VMEM((Lp + 2 * EDGE, H), F32),
                pltpu.VMEM((wb * Lp, T2 * H), BF16),
            ],
        ),
        out_shape=[
            jax.ShapeDtypeStruct((nw, Lp, C), F32),
            jax.ShapeDtypeStruct((2, nw, 1, C), F32),
            jax.ShapeDtypeStruct((2, C), F32),
            jax.ShapeDtypeStruct((H, T2 * C), F32),
        ],
        compiler_params=params(),
        cost_estimate=cost(4 * nw * Lp * T2 * C * H, nw * Lp * C * 20),
        name="dilated_back",
    )(
        meta, lens, c2, lo3, hi3, dz3, zlo3, zhi3, x2, Y3, dwt,
        stats3, sums3, gain3, stats2, gain2, shift2, total,
    )
    sums2, (zlo2, zhi2) = exchange(sums, [edge2], 5, g, False)

    def arg_half(n):
        return pl.BlockSpec((wb, n, Ch), lambda t, m, _: (m[1] // wb + t, 0, m[4]))

    gz, sums, wgrad1 = pl.pallas_call(
        partial(conv_back_kernel, wb, Lp, g),
        grid_spec=pltpu.PrefetchScalarGridSpec(
            num_scalar_prefetch=2,
            grid=(steps,),
            in_specs=[
                win((wb, Lp, C)),
                win((wb, 1, C)),
                win((wb, 1, C)),
                win((wb, Lp, C)),
                win((wb, EDGE, C)),
                win((wb, EDGE, C)),
                arg_win(Lp, C),
                win((wb, 1, C)),
                win((wb, 1, C)),
                arg_half(L),
                win((wb * Lp, T1 * C)),
                whole((2, 3 * C, Ch)),
                whole((L, L)),
                whole((2, C)),
                whole((2, C)),
                whole((1, C)),
                whole((2, Ch)),
                whole((1, Ch)),
                whole((1, Ch)),
                smem(),
            ],
            out_specs=[
                lead((g, wb, L, cs)),
                pl.BlockSpec((2, Ch), lambda t, *_: (0, 0)),
                pl.BlockSpec((Ch, T1 * C), lambda t, *_: (0, 0)),
            ],
            scratch_shapes=[
                pltpu.VMEM((Lp + 16, C), F32),
                pltpu.VMEM((wb * Lp, 3 * C), BF16),
                pltpu.VMEM((Ch, T1 * C), F32),
            ],
        ),
        out_shape=[
            jax.ShapeDtypeStruct((g, nw, L, cs), BF16),
            jax.ShapeDtypeStruct((2, Ch), F32),
            jax.ShapeDtypeStruct((Ch, T1 * C), BF16),
        ],
        compiler_params=params(),
        cost_estimate=cost(2 * nw * Lp * 11 * C * Ch, nw * Lp * C * 30),
        name="conv_back",
    )(
        meta, lens, dz2, zlo2, zhi2, x2, lo2, hi2, cotangent, col, coh, inputs, X5, weo, pick,
        stats2, sums2, gain2, own(stats1), own(gain1), own(shift1), total,
    )
    sums1, _ = exchange(sums, [], 6, g, False)

    def member(k):
        return (i + k) % g

    def ring(k):
        return [(b * g + j, b * g + (j + k) % g) for b in range(R) for j in range(g)]

    def pass_on(blocks, k):
        part = lax.dynamic_index_in_dim(blocks, member(k), 0, keepdims=False)
        return lax.ppermute(part, "ch", ring(k))

    mine = partial(lax.dynamic_index_in_dim, axis=0, keepdims=False)
    result = jnp.zeros((NW, Lp, cs), BF16)
    result = lax.dynamic_update_slice(result, mine(res, i), (i * nw, 0, 0))
    for k in range(1, g):
        got = pass_on(res, k)
        result = lax.dynamic_update_slice(result, got, (member(g - k) * nw, 0, 0))

    parts = [(mine(gz, i), i)] + [(pass_on(gz, k), member(g - k)) for k in range(1, g)]
    cols = partial(lax.dynamic_slice_in_dim, start_index=i * cs, slice_size=cs, axis=1)
    stats1h = cols(own(stats1))
    gain1h = cols(own(gain1))
    sums1h = cols(sums1)
    grad = jnp.zeros((NW, L, cs), BF16)
    for part, j in parts:
        meta_j = meta.at[5].set(j * nw)
        grad = pl.pallas_call(
            partial(input_grad_kernel, wb, L, g),
            grid_spec=pltpu.PrefetchScalarGridSpec(
                num_scalar_prefetch=2,
                grid=(steps,),
                in_specs=[
                    pl.BlockSpec((wb, L, Ch), lambda t, m, _: (m[5] // wb + t, 0, m[4])),
                    win((wb, L, cs)),
                    whole((L, L)),
                    whole((2, cs)),
                    whole((2, cs)),
                    whole((1, cs)),
                    smem(),
                    pl.BlockSpec(memory_space=pl.ANY),
                ],
                out_specs=pl.BlockSpec((wb, L, cs), lambda t, m, _: (m[5] // wb + t, 0, 0)),
            ),
            out_shape=jax.ShapeDtypeStruct((NW, L, cs), BF16),
            input_output_aliases={9: 0},
            compiler_params=params(),
            cost_estimate=cost(2 * nw * L * L * cs, nw * L * cs * 8),
            name="input_grad",
        )(meta_j, lens, inputs, part, unpick, stats1h, sums1h, gain1h, total, grad)

    def reduce_rows(partial_sums):
        n = partial_sums.shape[0] // g
        blocks = partial_sums.reshape((g, n) + partial_sums.shape[1:])
        total_rows = mine(blocks, i).astype(F32)
        for k in range(1, g):
            total_rows = total_rows + pass_on(blocks, k).astype(F32)
        return lax.psum(total_rows.astype(BF16), "seq").astype(F32)

    half_h = lambda a: lax.dynamic_slice_in_dim(a, h * (H // R), H // R, axis=0)
    conv_grad = reduce_rows(wgrad1)
    conv_grad = conv_grad.reshape(cs, T1, C).transpose(1, 2, 0)
    dil_grad = reduce_rows(half_h(wgrad2).astype(BF16))
    dil_grad = dil_grad.reshape(H // nz, T2, C).transpose(1, 2, 0)
    point_grad = reduce_rows(half_h(pgrad).astype(BF16))
    bias_grad = lax.psum(bgrad, ("seq", "ch")) / R
    bias_grad = lax.dynamic_slice_in_dim(bias_grad[0], z * cs, cs, axis=0)

    def of_c(a):
        return lax.dynamic_slice_in_dim(a, z * cs, cs, axis=0)

    def of_h(a):
        return lax.dynamic_slice_in_dim(a, z * (H // nz), H // nz, axis=0)

    return (
        result,
        grad,
        conv_grad,
        sums1h[1],
        sums1h[0],
        of_c(sums2[1]),
        of_c(sums2[0]),
        dil_grad,
        of_h(sums3[1]),
        of_h(sums3[0]),
        point_grad,
        bias_grad,
    )


def solution(mesh):
    in_specs = (
        P(None, "seq", None),
        P(),
        P(),
        P(),
        P(),
        P("ch"),
        P("ch"),
        P(None, None, "ch"),
        P("ch"),
        P("ch"),
        P("ch", None),
        P("ch"),
        P(None, "seq", None),
    )
    out_specs = (
        P(None, "seq", "ch"),
        P(None, "seq", "ch"),
        P(None, None, "ch"),
        P("ch"),
        P("ch"),
        P("ch"),
        P("ch"),
        P(None, None, "ch"),
        P("ch"),
        P("ch"),
        P("ch", None),
        P("ch"),
    )
    return jax.shard_map(
        per_device, mesh=mesh, in_specs=in_specs, out_specs=out_specs, check_vma=False
    )
```

```python
from functools import partial
from typing import NamedTuple

import jax
import jax.numpy as jnp
from jax import lax
from jax.experimental import pallas as pl
from jax.experimental.pallas import tpu as pltpu
from jax.sharding import PartitionSpec as P

DIL = 14
EDGE = 16
EPS = 1e-05
GC0 = 0.7978845608028654
GC1 = 0.044715
F32 = jnp.float32
BF16 = jnp.bfloat16
MESH = pl.DeviceIdType.MESH
VMEM_LIMIT = 58 * 1024 * 1024
ANY = pl.BlockSpec(memory_space=pl.ANY)
SMEM = pl.BlockSpec(memory_space=pltpu.SMEM)


class Plan(NamedTuple):
    ns: int
    nz: int
    R: int
    NW: int
    L: int
    C: int
    H: int
    T1: int
    T2: int
    wb: int

    @property
    def g(self):
        return self.nz // self.R

    @property
    def nw(self):
        return self.NW // self.g

    @property
    def Lp(self):
        return self.L // 2

    @property
    def cs(self):
        return self.C // self.nz

    @property
    def Ch(self):
        return self.C // self.R

    @property
    def Hh(self):
        return self.H // self.R

    @property
    def steps(self):
        return self.nw // self.wb

    @property
    def block(self):
        down = 1
        while self.ns % (2 * down) == 0 and (self.cs // 2) % (16 * down) == 0:
            down *= 2
        across = self.ns // down
        wide = -(-(self.T1 * self.C + (self.T2 + 1) * self.C // 2) // (128 * across)) * 128
        return self.cs // down, wide, down, across

    def place(self):
        s, z = lax.axis_index("seq"), lax.axis_index("ch")
        return s, z, lax.rem(z, self.g), lax.div(z, self.g)


def gelu(z):
    t = jnp.tanh(z * (GC0 + (GC0 * GC1) * (z * z)))
    hz = 0.5 * z
    return hz + hz * t


def gelu_both(z):
    sq = z * z
    t = jnp.tanh(z * (GC0 + (GC0 * GC1) * sq))
    hz = 0.5 * z
    slope = 0.5 + 0.5 * t + hz * (1.0 - t * t) * (GC0 + (3.0 * GC0 * GC1) * sq)
    return hz + hz * t, slope


def gelu_slope(z):
    return gelu_both(z)[1]


def rows_of(shape):
    return lax.broadcasted_iota(jnp.int32, shape, 0)


def lanes_of(shape):
    return lax.broadcasted_iota(jnp.int32, shape, 1)


def total_of(lens):
    n = lens[0]
    for k in range(1, lens.shape[0]):
        n = n + lens[k]
    return n.astype(F32)


def norm_of(stats, total):
    mean = stats[0:1] / total
    square = stats[1:2] / total
    return mean, lax.rsqrt(square - mean * mean + EPS)


def column(row, n):
    return jnp.broadcast_to(row, (n, row.shape[1])).T


def mm(a, b):
    return jnp.dot(a, b, preferred_element_type=F32)


def mm_nt(a, b):
    return lax.dot_general(a, b, (((1,), (1,)), ((), ())), preferred_element_type=F32)


def mm_tn(a, b):
    return lax.dot_general(a, b, (((0,), (0,)), ((), ())), preferred_element_type=F32)


def mm_tt(a, b):
    return lax.dot_general(a, b, (((0,), (1,)), ((), ())), preferred_element_type=F32)


def pick_matrix(L):
    r, n = rows_of((L, L)), lanes_of((L, L))
    bin_of = 2 * r - jnp.where(r >= L // 2, L - 1, 0)
    return jnp.where(n == bin_of, 1.0, 0.0).astype(BF16)


class Peers:
    def __init__(self, plan, everyone=False):
        s, z, i, h = plan.place()
        self.ns = plan.ns
        self.grp = plan.nz if everyone else plan.g
        self.base = 0 if everyone else h * plan.g
        self.s, self.z = s, z
        self.count = plan.ns * self.grp
        self.me = s * self.grp + (z - self.base)

    def device(self, q):
        return (lax.div(q, self.grp), self.base + lax.rem(q, self.grp))

    def other(self, off):
        return lax.rem(self.me + off, self.count)

    def greet(self):
        barrier = pltpu.get_barrier_semaphore()
        for off in range(1, self.count):
            pl.semaphore_signal(
                barrier, inc=1, device_id=self.device(self.other(off)), device_id_type=MESH
            )

    def meet(self):
        pl.semaphore_wait(pltpu.get_barrier_semaphore(), self.count - 1)

    def _copy(self, link, slot, off):
        packet, buf, send, recv = link[:4]
        return pltpu.make_async_remote_copy(
            src_ref=packet,
            dst_ref=buf.at[slot],
            send_sem=send.at[off],
            recv_sem=recv.at[slot],
            device_id=self.device(self.other(off)),
            device_id_type=MESH,
        )

    def _halo_copies(self, link, edge, low, high):
        send, recv = link[4:]
        left = (lax.rem(self.s + self.ns - 1, self.ns), self.z)
        right = (lax.rem(self.s + 1, self.ns), self.z)
        return [
            pltpu.make_async_remote_copy(
                src_ref=edge.at[side],
                dst_ref=dst,
                send_sem=send.at[side],
                recv_sem=recv.at[side],
                device_id=dev,
                device_id_type=MESH,
            )
            for side, (dst, dev) in enumerate(((high, left), (low, right)))
        ]

    def start(self, link, halo=None):
        for off in range(1, self.count):
            self._copy(link, self.me, off).start()
        if halo is not None:
            for c in self._halo_copies(link, *halo):
                c.start()

    def finish(self, link, halo=None):
        packet, buf = link[:2]
        buf[self.me] = packet[...]
        for off in range(1, self.count):
            self._copy(link, self.other(off), off).wait_recv()
        acc = buf[0]
        for q in range(1, self.count):
            acc = acc + buf[q]
        for off in range(1, self.count):
            self._copy(link, self.me, off).wait_send()
        if halo is not None:
            for c in self._halo_copies(link, *halo):
                c.wait()
        return acc


def link_scratch(plan, rows, everyone=False):
    count = plan.ns * (plan.nz if everyone else plan.g)
    return [
        pltpu.VMEM((rows, plan.C), F32),
        pltpu.VMEM((count, rows, plan.C), F32),
        pltpu.SemaphoreType.DMA((count,)),
        pltpu.SemaphoreType.DMA((count,)),
        pltpu.SemaphoreType.DMA((2,)),
        pltpu.SemaphoreType.DMA((2,)),
    ]


def first_step():
    return pl.program_id(0) == 0


def last_step():
    return pl.program_id(0) == pl.num_programs(0) - 1


def moments_kernel(plan, nw1, wb1, lens, x, xtop, xend, ctop, cend, g2, s2, pb, g3, s3,
                   stats, par, low, high, acc, edge, *link):
    t = pl.program_id(0)
    peers = Peers(plan, True)
    s, z, i, h = plan.place()
    L, C, nw, nz = plan.L, plan.C, plan.nw, plan.nz

    @pl.when(first_step())
    def _():
        peers.greet()
        acc[...] = jnp.zeros_like(acc)
        n16 = nw * 16
        for side, (xe, ce, places) in enumerate(
            ((xtop, ctop, (0, 1, 0)), (xend, cend, (14, 15, 15)))
        ):
            for k, at in enumerate(places):
                rows, lanes = rows_of((nw, n16)), lanes_of((nw, n16))
                sel = jnp.where(lanes == 16 * rows + at, 1.0, 0.0).astype(BF16)
                block = (xe if k < 2 else ce)[...].reshape(n16, C)
                edge[side, k] = mm(sel, block)

    rows = rows_of((L, C))
    for w in range(wb1):
        valid = 2 * lens[z * nw1 + t * wb1 + w] - s * L
        v = jnp.where(rows < valid, x[w].astype(F32), 0.0)
        v3 = v.reshape(L // 8, 8, C)
        acc[0] += jnp.sum(v3, axis=0)
        acc[1] += jnp.sum(v3 * v3, axis=0)

    @pl.when(last_step())
    def _():
        packet, buf = link[:2]
        packet[...] = jnp.zeros_like(packet)
        packet[0:1] = jnp.sum(acc[0], axis=0, keepdims=True)
        packet[1:2] = jnp.sum(acc[1], axis=0, keepdims=True)
        at = 0
        spans = []
        for ref in (g2, s2, pb, g3, s3):
            n = ref.shape[1]
            packet[2:3, at : at + n] = ref[...]
            spans.append((at, n))
            at += n
        peers.meet()
        halo = (edge, low, high)
        peers.start(link, halo)
        got = peers.finish(link, halo)
        stats[...] = got[0:2]
        par[...] = jnp.zeros_like(par)
        for k in range(nz):
            row = buf[s * nz + k]
            for r, (at, n) in enumerate(spans):
                par[r : r + 1, k * n : (k + 1) * n] = row[2:3, at : at + n]


def conv_kernel(plan, lens, x, hl, hr, w_ref, stats, gain, shift,
                X5, x2, low, high, sums, sel, edge, acc, *link):
    t = pl.program_id(0)
    peers = Peers(plan)
    s, z, i, h = plan.place()
    L, Lp, C, wb = plan.L, plan.Lp, plan.C, plan.wb

    @pl.when(first_step())
    def _():
        peers.greet()
        acc[...] = jnp.zeros_like(acc)
        shape = (Lp, L)
        for k in range(plan.T1):
            at = lanes_of(shape) - (2 * rows_of(shape) + (k - 2))
            sel[k * Lp : (k + 1) * Lp] = jnp.where((at == 0) | (at == 1), 1.0, 0.0).astype(BF16)

    mean, rho = norm_of(stats[...], 2.0 * total_of(lens))
    scale = gain[...] * rho
    offset = shift[...] - mean * scale
    rows = rows_of((L, C))
    row1 = rows_of((1, C))
    row16 = rows_of((16, C))

    for w in range(wb):
        at = t * wb + w
        valid = 2 * lens[i * plan.nw + at] - s * L
        a = gelu(x[w].astype(F32) * scale + offset)
        a = jnp.where(rows < valid, a, 0.0).astype(BF16)
        picked = mm(sel[...], a)
        for k in range(5):
            X5[w * Lp : (w + 1) * Lp, k * C : (k + 1) * C] = picked[
                k * Lp : (k + 1) * Lp
            ].astype(BF16)

        def beside(ref, k, bin_at):
            a = gelu(ref[k, pl.ds(at, 1), :] * scale + offset)
            here = (row1 + bin_at < valid) & (row1 + (s * L + bin_at) >= 0)
            return jnp.where(here, a, 0.0).astype(BF16).astype(F32)

        l0, l1 = beside(hl, 0, -2), beside(hl, 1, -1)
        r0, r1 = beside(hr, 0, L), beside(hr, 1, L + 1)
        top, end = w * Lp, (w + 1) * Lp
        for k, add in ((0, l0 + l1), (1, l1)):
            X5[top : top + 16, k * C : (k + 1) * C] = (
                picked[k * Lp : k * Lp + 16] + jnp.where(row16 == 0, add, 0.0)
            ).astype(BF16)
        for k, add in ((3, r0), (4, r0 + r1)):
            X5[end - 16 : end, k * C : (k + 1) * C] = (
                picked[(k + 1) * Lp - 16 : (k + 1) * Lp] + jnp.where(row16 == 15, add, 0.0)
            ).astype(BF16)

    nc = 256
    rowp = rows_of((Lp, nc))
    for n in range(C // nc):
        cols = slice(n * nc, (n + 1) * nc)
        y = 0.5 * mm(X5[...], w_ref[:, cols])
        s0 = jnp.zeros((1, nc), F32)
        s1 = jnp.zeros((1, nc), F32)
        for w in range(wb):
            at = t * wb + w
            valid = lens[i * plan.nw + at] - s * Lp
            v = y[w * Lp : (w + 1) * Lp]
            x2[w, :, cols] = v
            edge[0, at, :, cols] = v[:EDGE].astype(BF16)
            edge[1, at, :, cols] = v[Lp - EDGE :].astype(BF16)
            v = jnp.where(rowp < valid, v, 0.0)
            s0 = s0 + jnp.sum(v, axis=0, keepdims=True)
            s1 = s1 + jnp.sum(v * v, axis=0, keepdims=True)
        acc[0:1, cols] += s0
        acc[1:2, cols] += s1

    @pl.when(last_step())
    def _():
        link[0][...] = acc[...]
        halo = (edge, low, high)
        peers.meet()
        peers.start(link, halo)
        sums[...] = peers.finish(link, halo)


def dilated_kernel(plan, lens, x2, lo, hi, w_ref, stats, par,
                   Y3, c2, low, high, sums, ext, edge, acc, *link):
    t = pl.program_id(0)
    peers = Peers(plan)
    s, z, i, h = plan.place()
    Lp, C, H, wb = plan.Lp, plan.C, plan.H, plan.wb

    @pl.when(first_step())
    def _():
        peers.greet()
        acc[...] = jnp.zeros_like(acc)

    mean, rho = norm_of(stats[...], total_of(lens))
    scale = par[0:1] * rho
    offset = par[1:2] - mean * scale
    rows = rows_of((Lp, C))
    rowe = rows_of((EDGE, C))

    for w in range(wb):
        valid = lens[i * plan.nw + t * wb + w] - s * Lp
        a = jnp.where(rows < valid, gelu(x2[w] * scale + offset), 0.0)
        al = gelu(lo[w].astype(F32) * scale + offset)
        al = jnp.where((rowe - EDGE < valid) & (s > 0), al, 0.0)
        ah = gelu(hi[w].astype(F32) * scale + offset)
        ah = jnp.where(rowe + Lp < valid, ah, 0.0)
        ext[0:EDGE] = al
        ext[EDGE : EDGE + Lp] = a
        ext[EDGE + Lp :] = ah
        top, end = w * Lp, (w + 1) * Lp
        Y3[top:end, 0:C] = ext[EDGE - DIL : EDGE - DIL + Lp].astype(BF16)
        Y3[top:end, C : 2 * C] = a.astype(BF16)
        Y3[top:end, 2 * C : 3 * C] = ext[EDGE + DIL : EDGE + DIL + Lp].astype(BF16)

    y = mm_nt(Y3[...], w_ref[...])
    rowh = rows_of((Lp, H))
    s0 = jnp.zeros((1, H), F32)
    s1 = jnp.zeros((1, H), F32)
    for w in range(wb):
        at = t * wb + w
        valid = lens[i * plan.nw + at] - s * Lp
        v = y[w * Lp : (w + 1) * Lp]
        c2[w] = v
        edge[0, at] = v[:EDGE].astype(BF16)
        edge[1, at] = v[Lp - EDGE :].astype(BF16)
        v = jnp.where(rowh < valid, v, 0.0)
        s0 = s0 + jnp.sum(v, axis=0, keepdims=True)
        s1 = s1 + jnp.sum(v * v, axis=0, keepdims=True)
    acc[0:1, 0:H] += s0
    acc[1:2, 0:H] += s1

    @pl.when(last_step())
    def _():
        link[0][...] = acc[...]
        halo = (edge, low, high)
        peers.meet()
        peers.start(link, halo)
        sums[...] = peers.finish(link, halo)[:, 0:H]


def point_kernel(plan, lens, c2, x2, cot, pw, pwh, pb, stats, par,
                 res, dz, pgrad, low, high, sums, bsum,
                 a3s, dos, pacc, edge, acc, *link):
    t = pl.program_id(0)
    peers = Peers(plan)
    s, z, i, h = plan.place()
    Lp, C, H, wb, cs = plan.Lp, plan.C, plan.H, plan.wb, plan.cs

    @pl.when(first_step())
    def _():
        peers.greet()
        acc[...] = jnp.zeros_like(acc)
        pacc[...] = jnp.zeros_like(pacc)

    mean, rho = norm_of(stats[...], total_of(lens))
    scale = par[3:4, 0:H] * rho
    offset = par[4:5, 0:H] - mean * scale
    rowc = rows_of((Lp, C))
    rowh = rows_of((Lp, H))

    s0 = jnp.zeros((1, H), F32)
    s1 = jnp.zeros((1, H), F32)
    sb = jnp.zeros((1, C), F32)
    for w in range(wb):
        at = t * wb + w
        valid = lens[i * plan.nw + at] - s * Lp
        top, end = w * Lp, (w + 1) * Lp
        d = jnp.where(rowc < valid, cot[w].astype(F32), 0.0)
        sb = sb + jnp.sum(d, axis=0, keepdims=True)
        d = d.astype(BF16)
        dos[top:end] = d
        v = c2[w]
        act, slope = gelu_both(v * scale + offset)
        a3s[top:end] = jnp.where(rowh < valid, act, 0.0).astype(BF16)
        dzw = mm_nt(d, pw[...]) * slope
        dz[w] = dzw
        edge[0, at] = dzw[:EDGE].astype(BF16)
        edge[1, at] = dzw[Lp - EDGE :].astype(BF16)
        hat = (v - mean) * rho
        s0 = s0 + jnp.sum(dzw, axis=0, keepdims=True)
        s1 = s1 + jnp.sum(dzw * hat, axis=0, keepdims=True)
    acc[0:1, 0:H] += s0
    acc[1:2, 0:H] += s1
    acc[2:3] += sb

    @pl.when(last_step())
    def _():
        link[0][...] = acc[...]
        peers.meet()
        peers.start(link, (edge, low, high))

    y = mm(a3s[...], pwh[...])
    rowr = rows_of((Lp, y.shape[1]))
    for w in range(wb):
        valid = lens[i * plan.nw + t * wb + w] - s * Lp
        r = x2[w] + y[w * Lp : (w + 1) * Lp] + pb[2:3]
        r = jnp.where(rowr < valid, r, 0.0).T.astype(BF16)
        for k in range(plan.g):
            res[k, w] = r[k * cs : (k + 1) * cs]
    pacc[...] += mm_tn(a3s[...], dos[...])

    @pl.when(last_step())
    def _():
        rows = pl.ds(pl.multiple_of(h * plan.Hh, 16), plan.Hh)
        pgrad[...] = pacc[rows].astype(BF16)
        got = peers.finish(link, (edge, low, high))
        sums[...] = got[0:2, 0:H]
        bsum[...] = got[2:3]


def dilated_back_kernel(plan, lens, c2, clo, chi, dz3, zlo, zhi, x2, Y3, w_ref,
                        stats3, sums3, stats2, par, pgrad, res,
                        dz2, grads, low, high, sums, result,
                        ext, Z3, wt, wacc, edge, acc, bulk_send, bulk_recv, own_sem,
                        *link):
    t = pl.program_id(0)
    peers = Peers(plan)
    s, z, i, h = plan.place()
    Lp, C, H, wb, g, nw = plan.Lp, plan.C, plan.H, plan.wb, plan.g, plan.nw

    def own_copy():
        return pltpu.make_async_copy(res.at[i], result.at[pl.ds(i * nw, nw)], own_sem)

    def bulk(off, sender):
        to = lax.rem(i + off, g)
        return pltpu.make_async_remote_copy(
            src_ref=res.at[to],
            dst_ref=result.at[pl.ds(sender * nw, nw)],
            send_sem=bulk_send.at[off],
            recv_sem=bulk_recv.at[off],
            device_id=(s, h * g + to),
            device_id_type=MESH,
        )

    @pl.when(first_step())
    def _():
        peers.greet()
        acc[...] = jnp.zeros_like(acc)
        wacc[...] = jnp.zeros_like(wacc)
        for k in range(plan.T2):
            wt[k * H : (k + 1) * H] = w_ref[:, k * C : (k + 1) * C]
        own_copy().start()

    total = total_of(lens)
    mean3, rho3 = norm_of(stats3[...], total)
    gr3 = par[3:4, 0:H] * rho3
    sg3 = sums3[0:1] / total
    gg3 = sums3[1:2] / total
    mean2, rho2 = norm_of(stats2[...], total)
    scale2 = par[0:1] * rho2
    offset2 = par[1:2] - mean2 * scale2
    rowh = rows_of((Lp, H))
    rowe = rows_of((EDGE, H))
    rowc = rows_of((Lp, C))

    def back(dz, v):
        return gr3 * (dz - (sg3 + (v - mean3) * rho3 * gg3))

    for w in range(wb):
        valid = lens[i * nw + t * wb + w] - s * Lp
        d = jnp.where(rowh < valid, back(dz3[w], c2[w]), 0.0)
        dl = back(zlo[w].astype(F32), clo[w].astype(F32))
        dl = jnp.where((rowe - EDGE < valid) & (s > 0), dl, 0.0)
        dh = back(zhi[w].astype(F32), chi[w].astype(F32))
        dh = jnp.where(rowe + Lp < valid, dh, 0.0)
        ext[0:EDGE] = dl
        ext[EDGE : EDGE + Lp] = d
        ext[EDGE + Lp :] = dh
        top, end = w * Lp, (w + 1) * Lp
        Z3[top:end, 0:H] = ext[EDGE + DIL : EDGE + DIL + Lp].astype(BF16)
        Z3[top:end, H : 2 * H] = d.astype(BF16)
        Z3[top:end, 2 * H : 3 * H] = ext[EDGE - DIL : EDGE - DIL + Lp].astype(BF16)

    y = mm(Z3[...], wt[...])

    @pl.when(first_step())
    def _():
        peers.meet()
        for off in range(1, g):
            bulk(off, i).start()

    s0 = jnp.zeros((1, C), F32)
    s1 = jnp.zeros((1, C), F32)
    for w in range(wb):
        at = t * wb + w
        valid = lens[i * nw + at] - s * Lp
        v = x2[w]
        dzw = y[w * Lp : (w + 1) * Lp] * gelu_slope(v * scale2 + offset2)
        dzw = jnp.where(rowc < valid, dzw, 0.0)
        dz2[w] = dzw
        edge[0, pl.ds(at, 1)] = dzw[0:1]
        edge[1, pl.ds(at, 1)] = dzw[Lp - 1 : Lp]
        s0 = s0 + jnp.sum(dzw, axis=0, keepdims=True)
        s1 = s1 + jnp.sum(dzw * ((v - mean2) * rho2), axis=0, keepdims=True)
    acc[0:1] += s0
    acc[1:2] += s1

    @pl.when(last_step())
    def _():
        link[0][...] = acc[...]
        peers.start(link, (edge, low, high))

    wacc[...] += mm_tn(Z3[:, H : 2 * H], Y3[...])

    @pl.when(last_step())
    def _():
        rows = pl.ds(pl.multiple_of(h * plan.Hh, 16), plan.Hh)
        grads[:, 0 : plan.T2 * C] = wacc[rows].astype(BF16)
        grads[:, plan.T2 * C :] = pgrad[...]
        sums[...] = peers.finish(link, (edge, low, high))
        own_copy().wait()
        for off in range(1, g):
            bulk(off, i).wait_send()
            bulk(off, lax.rem(i + g - off, g)).wait_recv()


def conv_grad_kernel(plan, lens, dz2, zlo, zhi, x2, lo, hi, cot, hl, hr, X5,
                     stats2, sums2, par, grads, D3, blocks, ext, acc):
    t = pl.program_id(0)
    s, z, i, h = plan.place()
    Lp, C, wb, Ch, cs = plan.Lp, plan.C, plan.wb, plan.Ch, plan.cs

    @pl.when(first_step())
    def _():
        acc[...] = jnp.zeros_like(acc)

    total = total_of(lens)
    mean, rho = norm_of(stats2[...], total)
    gr = par[0:1] * rho
    sg = sums2[0:1] / total
    gg = sums2[1:2] / total
    rowc = rows_of((Lp, C))
    row1 = rows_of((1, C))

    def back(dout, dz, v):
        return 0.5 * (dout + gr * (dz - (sg + (v - mean) * rho * gg)))

    for w in range(wb):
        at = t * wb + w
        valid = lens[i * plan.nw + at] - s * Lp
        d = back(cot[w].astype(F32), dz2[w], x2[w])
        d = jnp.where(rowc < valid, d, 0.0)
        dl = back(hl[2, pl.ds(at, 1), :], zlo[pl.ds(at, 1), :], lo[w, EDGE - 1 : EDGE].astype(F32))
        dl = jnp.where((row1 - 1 < valid) & (s > 0), dl, 0.0)
        dh = back(hr[2, pl.ds(at, 1), :], zhi[pl.ds(at, 1), :], hi[w, 0:1].astype(F32))
        dh = jnp.where(row1 + Lp < valid, dh, 0.0)
        ext[7:8] = dl
        ext[8 : 8 + Lp] = d
        ext[8 + Lp : 9 + Lp] = dh
        top, end = w * Lp, (w + 1) * Lp
        D3[top:end, 0:C] = ext[9 : 9 + Lp].astype(BF16)
        D3[top:end, C : 2 * C] = d.astype(BF16)
        D3[top:end, 2 * C : 3 * C] = ext[7 : 7 + Lp].astype(BF16)

    dh = D3[:, pl.ds(pl.multiple_of(C + h * Ch, 128), Ch)]
    acc[...] += mm_tn(dh, X5[...])

    @pl.when(last_step())
    def _():
        rb, wide, down, across = plan.block
        n1, n2 = plan.T1 * C, (plan.T2 + 1) * C // 2
        hs = plan.H // plan.nz
        for k in range(plan.g):
            for q in range(plan.ns):
                r, c = q // across * rb, q % across * wide
                dst = blocks.at[q % 2, q // 2, k]
                a, b = min(c, n1), min(c + wide, n1)
                if b > a:
                    dst[:, 0 : b - a] = acc[k * cs + r : k * cs + r + rb, a:b].astype(BF16)
                a, b = max(c, n1) - n1, min(c + wide, n1 + n2) - n1
                if b > a:
                    side, r2 = r // hs, r % hs
                    dst[:, a + n1 - c : b + n1 - c] = grads[
                        k * hs + r2 : k * hs + r2 + rb, side * n2 + a : side * n2 + b
                    ]


class Reduction:
    def __init__(self, plan, blocks, out, mine, got, mid, spread, half, mate, sems):
        self.plan = plan
        self.blocks, self.out = blocks, out
        self.mine, self.got, self.mid, self.spread = mine, got, mid, spread
        self.half, self.mate = half, mate
        self.sems = sems
        self.s, self.z, self.i, self.h = plan.place()
        self.c = lax.rem(self.s, 2)
        self.m = lax.div(self.s, 2)
        self.chips = plan.ns // 2

    def copy(self, src, dst, sem, device):
        return pltpu.make_async_remote_copy(
            src_ref=src,
            dst_ref=dst,
            send_sem=self.sems.at[0, sem],
            recv_sem=self.sems.at[1, sem],
            device_id=device,
            device_id_type=MESH,
        )

    def pair(self):
        return (2 * self.m + (1 - self.c), self.z)

    def chip(self, off):
        return lax.rem(self.m + off, self.chips)

    def member(self, off):
        return lax.rem(self.i + off, self.plan.g)

    def own0(self):
        return pltpu.make_async_copy(self.blocks.at[self.c], self.mine, self.sems.at[0, 0])

    def phase0(self):
        return self.copy(self.blocks.at[1 - self.c], self.got, 1, self.pair())

    def phase1(self, off, at):
        to = self.chip(off)
        return self.copy(
            self.mid.at[to], self.spread.at[at], 2 + off, (2 * to + self.c, self.z)
        )

    def phase2(self, off):
        to = self.member(off)
        sem = 2 + self.chips + off
        return self.copy(
            self.half.at[to], self.mate.at[off], sem, (self.s, self.h * self.plan.g + to)
        )

    def phase3(self, off, at):
        to = self.chip(off)
        sem = 2 + self.chips + self.plan.g + off
        return self.copy(
            self.out.at[self.c, self.m], self.out.at[self.c, at], sem, (2 * to + self.c, self.z)
        )

    def phase4(self, c):
        sem = 2 + 2 * self.chips + self.plan.g
        return self.copy(self.out.at[self.c], self.out.at[c], sem, self.pair())

    def step0(self):
        self.own0().start()
        self.phase0().start()

    def step1(self):
        self.own0().wait()
        self.phase0().wait()

        @pl.loop(0, self.chips)
        def _(n):
            self.mid[n] = (self.mine[n].astype(F32) + self.got[n].astype(F32)).astype(BF16)

        for off in range(1, self.chips):
            self.phase1(off, self.m).start()

    def step2(self):
        for off in range(1, self.chips):
            self.phase1(off, self.m).wait_send()
            self.phase1(off, self.chip(self.chips - off)).wait_recv()
        self.spread[self.m] = self.mid[self.m]

        @pl.loop(0, self.plan.g)
        def _(n):
            v = self.spread[0, n].astype(F32)
            for k in range(1, self.chips):
                v = v + self.spread[k, n].astype(F32)
            self.half[n] = v.astype(BF16)

        for off in range(1, self.plan.g):
            self.phase2(off).start()

    def step3(self):
        for off in range(1, self.plan.g):
            self.phase2(off).wait()
        v = self.half[self.i].astype(F32)
        for off in range(1, self.plan.g):
            v = v + self.mate[off].astype(F32)
        self.out[self.c, self.m] = v.astype(BF16)
        for off in range(1, self.chips):
            self.phase3(off, self.m).start()

    def step4(self):
        for off in range(1, self.chips):
            self.phase3(off, self.m).wait_send()
            self.phase3(off, self.chip(self.chips - off)).wait_recv()
        self.phase4(self.c).start()

    def step5(self):
        self.phase4(self.c).wait_send()
        self.phase4(1 - self.c).wait_recv()


def conv_back_kernel(plan, lens, D3, x, taps, stats, gain, shift, blocks,
                     gz, sums, summed, wcat, pick, cols, y, part, acc,
                     bulk_send, bulk_recv, own_sem,
                     mine, got, mid, spread, half, mate, out, red_sems, *link):
    t = pl.program_id(0)
    peers = Peers(plan)
    s, z, i, h = plan.place()
    L, Lp, C, wb, g, nw = plan.L, plan.Lp, plan.C, plan.wb, plan.g, plan.nw
    Ch, cs = plan.Ch, plan.cs
    steps = plan.steps
    red = Reduction(plan, blocks, out, mine, got, mid, spread, half, mate, red_sems)

    def own_copy(step):
        return pltpu.make_async_copy(
            part.at[step, i], gz.at[pl.ds(i * nw + step * wb, wb)], own_sem.at[step]
        )

    def bulk(step, off, sender):
        to = lax.rem(i + off, g)
        return pltpu.make_async_remote_copy(
            src_ref=part.at[step, to],
            dst_ref=gz.at[pl.ds(sender * nw + step * wb, wb)],
            send_sem=bulk_send.at[step, off],
            recv_sem=bulk_recv.at[step, off],
            device_id=(s, h * g + to),
            device_id_type=MESH,
        )

    @pl.when(first_step())
    def _():
        peers.greet()
        acc[...] = jnp.zeros_like(acc)
        pick[...] = pick_matrix(L)
        mean, rho = norm_of(stats[...], 2.0 * total_of(lens))
        scale = gain[...] * rho
        for k, row in enumerate((scale, shift[...] - mean * scale, rho, -mean * rho)):
            cols[k] = column(row, L)
        w = [taps[k].astype(F32) for k in range(5)]
        for r, parts in enumerate(
            ((w[0], w[1] + w[2], w[3] + w[4]), (w[0] + w[1], w[2] + w[3], w[4]))
        ):
            for k, v in enumerate(parts):
                wcat[r * Ch : (r + 1) * Ch, k * C : (k + 1) * C] = v.astype(BF16)

    y[...] = mm_nt(wcat[...], D3[...])
    lanes = lanes_of((Ch, L))
    bins = 2 * lanes - jnp.where(lanes >= Lp, L - 1, 0)
    for w in range(wb):
        valid = 2 * lens[i * nw + t * wb + w] - s * L
        top, end = w * Lp, (w + 1) * Lp
        v = mm_tt(x[w], pick[...])
        da = jnp.concatenate([y[0:Ch, top:end], y[Ch:, top:end]], axis=1)
        dzw = da * gelu_slope(v * cols[0] + cols[1])
        dzw = jnp.where(bins < valid, dzw, 0.0)
        acc[0] += dzw
        acc[1] += dzw * (v * cols[2] + cols[3])
        dzw = dzw.astype(BF16)
        for k in range(g):
            part[t, k, w] = dzw[k * cs : (k + 1) * cs]

    @pl.when(first_step())
    def _():
        peers.meet()
        red.step0()

    own_copy(t).start()
    for off in range(1, g):
        bulk(t, off, i).start()

    @pl.when(t == min(1, steps - 1))
    def _():
        red.step1()

    @pl.when(last_step())
    def _():
        red.step2()
        packet = link[0]
        packet[...] = jnp.zeros_like(packet)
        packet[0:1, 0:Ch] = jnp.sum(acc[0].T, axis=0, keepdims=True)
        packet[1:2, 0:Ch] = jnp.sum(acc[1].T, axis=0, keepdims=True)
        peers.start(link)
        red.step3()
        sums[...] = peers.finish(link)[:, 0:Ch]
        red.step4()
        red.step5()
        summed[...] = out[...]
        for step in range(steps):
            own_copy(step).wait()
            for off in range(1, g):
                bulk(step, off, i).wait_send()
                bulk(step, off, lax.rem(i + g - off, g)).wait_recv()


def input_grad_kernel(plan, lens, x, gz, stats, sums, gain, out, pick, cols, xt):
    t = pl.program_id(0)
    s, z, i, h = plan.place()
    L, Ch, cs, wb = plan.L, plan.Ch, plan.cs, plan.wb
    mine = pl.ds(pl.multiple_of(i * cs, 16), cs)

    @pl.when(first_step())
    def _():
        n = 2.0 * total_of(lens)
        mean, rho = norm_of(stats[...], n)
        gr = gain[...] * rho
        gg = sums[1:2] / n * rho
        for k, row in enumerate((gr, -gr * gg, gr * (mean * gg - sums[0:1] / n))):
            xt[...] = column(row, L)
            cols[k] = xt[mine]
        pick[...] = pick_matrix(L)

    lanes = lanes_of((cs, L))
    for w in range(wb):
        valid = 2 * lens[t * wb + w] - s * L
        xt[...] = x[w].astype(F32).T
        v = xt[mine]
        dz = mm(gz[w], pick[...])
        r = cols[0] * dz + v * cols[1] + cols[2]
        out[w] = jnp.where(lanes < valid, r, 0.0).astype(BF16)


def call(kernel, plan, name, steps, ins, outs, scratch, flops, nbytes, cid=None):
    extra = {} if cid is None else dict(collective_id=cid, has_side_effects=True)
    return pl.pallas_call(
        partial(kernel, plan),
        grid=(steps,),
        in_specs=[SMEM] + [spec for spec, _ in ins],
        out_specs=[spec for spec, _, _ in outs],
        out_shape=[jax.ShapeDtypeStruct(shape, dtype) for _, shape, dtype in outs],
        scratch_shapes=scratch,
        compiler_params=pltpu.CompilerParams(vmem_limit_bytes=VMEM_LIMIT, **extra),
        cost_estimate=pl.CostEstimate(
            flops=int(flops), bytes_accessed=int(nbytes), transcendentals=0
        ),
        name=name,
    )


def per_device(
    inputs,
    lengths,
    input_gain,
    input_shift,
    conv_weight,
    branch_gain,
    branch_shift,
    dilated_tap_weight,
    mixer_gain,
    mixer_shift,
    point_weight,
    point_bias,
    cotangent,
):
    NW, L, C = inputs.shape
    Lp = L // 2
    nz = lax.axis_size("ch")
    R = 2
    plan = Plan(
        ns=lax.axis_size("seq"),
        nz=nz,
        R=R,
        NW=NW,
        L=L,
        C=C,
        H=mixer_gain.shape[0] * nz,
        T1=conv_weight.shape[0],
        T2=dilated_tap_weight.shape[0],
        wb=min(NW * R // nz, max(1, 512 // Lp)),
    )
    g, nw, cs, Ch, H, Hh, wb = plan.g, plan.nw, plan.cs, plan.Ch, plan.H, plan.Hh, plan.wb
    T1, T2, steps = plan.T1, plan.T2, plan.steps
    M = wb * Lp
    s, z, i, h = plan.place()
    lens = lengths.astype(jnp.int32)
    gain1 = input_gain.reshape(1, C)
    shift1 = input_shift.reshape(1, C)

    def row(a):
        return a.reshape(1, a.shape[0])

    def grp():
        return lax.rem(lax.axis_index("ch"), g)

    def half():
        return lax.div(lax.axis_index("ch"), g)

    def whole(*shape):
        return pl.BlockSpec(shape, lambda t: (0,) * len(shape), pipeline_mode=pl.Buffered(1))

    def const(*shape):
        return pl.BlockSpec(shape, lambda t: (0,) * len(shape))

    def win(*shape):
        return pl.BlockSpec(shape, lambda t: (t,) + (0,) * (len(shape) - 1))

    def arg_win(n, width):
        return pl.BlockSpec((wb, n, width), lambda t: (grp() * steps + t, 0, 0))

    def ins(*pairs):
        return [p for p in pairs]

    taps2 = jnp.swapaxes(dilated_tap_weight, 1, 2)
    taps2 = jnp.swapaxes(taps2, 0, 1).reshape(H // nz, T2 * C)
    packed = jnp.concatenate([taps2, point_weight], axis=1)
    packed = lax.all_gather(packed, "ch", axis=0, tiled=True)

    nw1 = NW // nz
    wb1 = min(nw1, wb)

    def edge_spec(n):
        return pl.BlockSpec(
            (nw, 16, C), lambda t: (grp(), n, 0), pipeline_mode=pl.Buffered(1)
        )

    pairs = ins(
        (
            pl.BlockSpec((wb1, L, C), lambda t: (lax.axis_index("ch") * (nw1 // wb1) + t, 0, 0)),
            inputs,
        ),
        (edge_spec(0), inputs),
        (edge_spec(L // 16 - 1), inputs),
        (edge_spec(0), cotangent),
        (edge_spec(Lp // 16 - 1), cotangent),
        (whole(1, cs), row(branch_gain)),
        (whole(1, cs), row(branch_shift)),
        (whole(1, cs), row(point_bias)),
        (whole(1, H // nz), row(mixer_gain)),
        (whole(1, H // nz), row(mixer_shift)),
    )
    stats1, par, hl, hr = call(
        lambda plan, *refs: moments_kernel(plan, nw1, wb1, *refs),
        plan,
        "moments",
        nw1 // wb1,
        pairs,
        [
            (const(2, C), (2, C), F32),
            (const(8, C), (8, C), F32),
            (ANY, (3, nw, C), F32),
            (ANY, (3, nw, C), F32),
        ],
        [pltpu.VMEM((2, 8, C), F32), pltpu.VMEM((2, 3, nw, C), F32)]
        + link_scratch(plan, 3, True),
        0,
        nw1 * L * C * 2,
        cid=1,
    )(lens, *[a for _, a in pairs])

    pairs = ins(
        (arg_win(L, C), inputs),
        (whole(3, nw, C), hl),
        (whole(3, nw, C), hr),
        (whole(T1 * C, C), conv_weight.reshape(T1 * C, C)),
        (whole(2, C), stats1),
        (whole(1, C), gain1),
        (whole(1, C), shift1),
    )
    X5, x2, lo2, hi2, stats2 = call(
        conv_kernel,
        plan,
        "conv",
        steps,
        pairs,
        [
            (win(M, T1 * C), (nw * Lp, T1 * C), BF16),
            (win(wb, Lp, C), (nw, Lp, C), F32),
            (ANY, (nw, EDGE, C), BF16),
            (ANY, (nw, EDGE, C), BF16),
            (const(2, C), (2, C), F32),
        ],
        [
            pltpu.VMEM((T1 * Lp, L), BF16),
            pltpu.VMEM((2, nw, EDGE, C), BF16),
            pltpu.VMEM((2, C), F32),
        ]
        + link_scratch(plan, 2),
        2 * nw * Lp * T1 * C * C,
        nw * Lp * C * 20,
        cid=2,
    )(lens, *[a for _, a in pairs])

    packed, x2 = lax.optimization_barrier((packed, x2))
    taps_spec = whole(H, T2 * C)
    pw_spec = pl.BlockSpec((H, C), lambda t: (0, T2), pipeline_mode=pl.Buffered(1))

    pairs = ins(
        (win(wb, Lp, C), x2),
        (win(wb, EDGE, C), lo2),
        (win(wb, EDGE, C), hi2),
        (taps_spec, packed),
        (whole(2, C), stats2),
        (whole(8, C), par),
    )
    Y3, c2, lo3, hi3, stats3 = call(
        dilated_kernel,
        plan,
        "dilated",
        steps,
        pairs,
        [
            (win(M, T2 * C), (nw * Lp, T2 * C), BF16),
            (win(wb, Lp, H), (nw, Lp, H), F32),
            (ANY, (nw, EDGE, H), BF16),
            (ANY, (nw, EDGE, H), BF16),
            (const(2, H), (2, H), F32),
        ],
        [
            pltpu.VMEM((Lp + 2 * EDGE, C), F32),
            pltpu.VMEM((2, nw, EDGE, H), BF16),
            pltpu.VMEM((2, C), F32),
        ]
        + link_scratch(plan, 2),
        2 * nw * Lp * T2 * C * H,
        nw * Lp * C * 12,
        cid=3,
    )(lens, *[a for _, a in pairs])

    pairs = ins(
        (win(wb, Lp, H), c2),
        (pl.BlockSpec((wb, Lp, Ch), lambda t: (t, 0, half())), x2),
        (arg_win(Lp, C), cotangent),
        (pw_spec, packed),
        (
            pl.BlockSpec(
                (H, Ch), lambda t: (0, T2 * R + half()), pipeline_mode=pl.Buffered(1)
            ),
            packed,
        ),
        (pl.BlockSpec((8, Ch), lambda t: (0, half()), pipeline_mode=pl.Buffered(1)), par),
        (whole(2, H), stats3),
        (whole(8, C), par),
    )
    res, dz3, pgrad, zlo3, zhi3, sums3, bsum = call(
        point_kernel,
        plan,
        "point",
        steps,
        pairs,
        [
            (
                pl.BlockSpec((g, wb, cs, Lp), lambda t: (0, t, 0, 0)),
                (g, nw, cs, Lp),
                BF16,
            ),
            (win(wb, Lp, H), (nw, Lp, H), F32),
            (const(Hh, C), (Hh, C), BF16),
            (ANY, (nw, EDGE, H), BF16),
            (ANY, (nw, EDGE, H), BF16),
            (const(2, H), (2, H), F32),
            (const(1, C), (1, C), F32),
        ],
        [
            pltpu.VMEM((M, H), BF16),
            pltpu.VMEM((M, C), BF16),
            pltpu.VMEM((H, C), F32),
            pltpu.VMEM((2, nw, EDGE, H), BF16),
            pltpu.VMEM((3, C), F32),
        ]
        + link_scratch(plan, 3),
        5 * nw * Lp * C * H,
        nw * Lp * C * 10,
        cid=4,
    )(lens, *[a for _, a in pairs])

    pairs = ins(
        (win(wb, Lp, H), c2),
        (win(wb, EDGE, H), lo3),
        (win(wb, EDGE, H), hi3),
        (win(wb, Lp, H), dz3),
        (win(wb, EDGE, H), zlo3),
        (win(wb, EDGE, H), zhi3),
        (win(wb, Lp, C), x2),
        (win(M, T2 * C), Y3),
        (taps_spec, packed),
        (whole(2, H), stats3),
        (whole(2, H), sums3),
        (whole(2, C), stats2),
        (whole(8, C), par),
        (whole(Hh, C), pgrad),
        (ANY, res),
    )
    dz2, grads, zlo2, zhi2, sums2, result = call(
        dilated_back_kernel,
        plan,
        "dilated_back",
        steps,
        pairs,
        [
            (win(wb, Lp, C), (nw, Lp, C), F32),
            (const(Hh, (T2 + 1) * C), (Hh, (T2 + 1) * C), BF16),
            (ANY, (nw, C), F32),
            (ANY, (nw, C), F32),
            (const(2, C), (2, C), F32),
            (ANY, (NW, cs, Lp), BF16),
        ],
        [
            pltpu.VMEM((Lp + 2 * EDGE, H), F32),
            pltpu.VMEM((M, T2 * H), BF16),
            pltpu.VMEM((T2 * H, C), BF16),
            pltpu.VMEM((H, T2 * C), F32),
            pltpu.VMEM((2, nw, C), F32),
            pltpu.VMEM((2, C), F32),
            pltpu.SemaphoreType.DMA((g,)),
            pltpu.SemaphoreType.DMA((g,)),
            pltpu.SemaphoreType.DMA,
        ]
        + link_scratch(plan, 2),
        4 * nw * Lp * T2 * C * H,
        nw * Lp * C * 20,
        cid=5,
    )(lens, *[a for _, a in pairs])

    pairs = ins(
        (win(wb, Lp, C), dz2),
        (whole(nw, C), zlo2),
        (whole(nw, C), zhi2),
        (win(wb, Lp, C), x2),
        (win(wb, EDGE, C), lo2),
        (win(wb, EDGE, C), hi2),
        (arg_win(Lp, C), cotangent),
        (whole(3, nw, C), hl),
        (whole(3, nw, C), hr),
        (win(M, T1 * C), X5),
        (whole(2, C), stats2),
        (whole(2, C), sums2),
        (whole(8, C), par),
        (whole(Hh, (T2 + 1) * C), grads),
    )
    rb, wide, down, across = plan.block
    bshape = (2, plan.ns // 2, g, rb, wide)
    D3, blocks = call(
        conv_grad_kernel,
        plan,
        "conv_grad",
        steps,
        pairs,
        [
            (win(M, 3 * C), (nw * Lp, 3 * C), BF16),
            (const(*bshape), bshape, BF16),
        ],
        [pltpu.VMEM((Lp + 16, C), F32), pltpu.VMEM((Ch, T1 * C), F32)],
        2 * nw * Lp * T1 * C * Ch,
        nw * Lp * C * 30,
    )(lens, *[a for _, a in pairs])

    def half_of(n):
        return pl.BlockSpec((n, Ch), lambda t: (0, half()), pipeline_mode=pl.Buffered(1))

    pairs = ins(
        (win(M, 3 * C), D3),
        (pl.BlockSpec((wb, L, Ch), lambda t: (grp() * steps + t, 0, half())), inputs),
        (
            pl.BlockSpec(
                (T1, Ch, C), lambda t: (0, half(), 0), pipeline_mode=pl.Buffered(1)
            ),
            conv_weight,
        ),
        (half_of(2), stats1),
        (half_of(1), gain1),
        (half_of(1), shift1),
        (ANY, blocks),
    )
    gz, sums1, summed = call(
        conv_back_kernel,
        plan,
        "conv_back",
        steps,
        pairs,
        [
            (ANY, (NW, cs, L), BF16),
            (const(2, Ch), (2, Ch), F32),
            (const(2, plan.ns // 2, rb, wide), (2, plan.ns // 2, rb, wide), BF16),
        ],
        [
            pltpu.VMEM((2 * Ch, 3 * C), BF16),
            pltpu.VMEM((L, L), BF16),
            pltpu.VMEM((4, Ch, L), F32),
            pltpu.VMEM((2 * Ch, M), F32),
            pltpu.VMEM((steps, g, wb, cs, L), BF16),
            pltpu.VMEM((2, Ch, L), F32),
            pltpu.SemaphoreType.DMA((steps, g)),
            pltpu.SemaphoreType.DMA((steps, g)),
            pltpu.SemaphoreType.DMA((steps,)),
            pltpu.VMEM(bshape[1:], BF16),
            pltpu.VMEM(bshape[1:], BF16),
            pltpu.VMEM(bshape[1:], BF16),
            pltpu.VMEM(bshape[1:], BF16),
            pltpu.VMEM((g, rb, wide), BF16),
            pltpu.VMEM((g, rb, wide), BF16),
            pltpu.VMEM((2, plan.ns // 2, rb, wide), BF16),
            pltpu.SemaphoreType.DMA((2, 3 + plan.ns + g)),
        ]
        + link_scratch(plan, 2),
        2 * nw * Lp * 6 * C * Ch,
        nw * Lp * C * 12,
        cid=6,
    )(lens, *[a for _, a in pairs])

    pairs = ins(
        (pl.BlockSpec((wb, L, Ch), lambda t: (t, 0, half())), inputs),
        (win(wb, cs, L), gz),
        (half_of(2), stats1),
        (whole(2, Ch), sums1),
        (half_of(1), gain1),
    )
    (grad,) = call(
        input_grad_kernel,
        plan,
        "input_grad",
        NW // wb,
        pairs,
        [(win(wb, cs, L), (NW, cs, L), BF16)],
        [
            pltpu.VMEM((L, L), BF16),
            pltpu.VMEM((3, cs, L), F32),
            pltpu.VMEM((Ch, L), F32),
        ],
        2 * NW * L * L * cs,
        NW * L * cs * 8,
    )(lens, *[a for _, a in pairs])

    n1, n2, hs = T1 * C, (T2 + 1) * C // 2, H // nz
    flat = jnp.swapaxes(summed, 0, 1).reshape(down, across, rb, wide)
    flat = jnp.swapaxes(flat, 1, 2).reshape(cs, across * wide)
    conv_grad = flat[:, :n1].astype(F32).reshape(cs, T1, C).transpose(1, 2, 0)
    rest = flat[:, n1 : n1 + n2]
    rest = jnp.concatenate([rest[:hs], rest[hs:]], axis=1).astype(F32)
    dil_grad = rest[:, : T2 * C].reshape(hs, T2, C).transpose(1, 2, 0)
    point_grad = rest[:, T2 * C :]

    def of_c(a):
        return lax.dynamic_slice_in_dim(a, z * cs, cs, axis=0)

    def of_h(a):
        return lax.dynamic_slice_in_dim(a, z * (H // nz), H // nz, axis=0)

    def of_i(a):
        return lax.dynamic_slice_in_dim(a, i * cs, cs, axis=0)

    return (
        jnp.swapaxes(result, 1, 2),
        jnp.swapaxes(grad, 1, 2),
        conv_grad,
        of_i(sums1[1]),
        of_i(sums1[0]),
        of_c(sums2[1]),
        of_c(sums2[0]),
        dil_grad,
        of_h(sums3[1]),
        of_h(sums3[0]),
        point_grad,
        of_c(bsum[0]),
    )


def solution(mesh):
    in_specs = (
        P(None, "seq", None),
        P(),
        P(),
        P(),
        P(),
        P("ch"),
        P("ch"),
        P(None, None, "ch"),
        P("ch"),
        P("ch"),
        P("ch", None),
        P("ch"),
        P(None, "seq", None),
    )
    out_specs = (
        P(None, "seq", "ch"),
        P(None, "seq", "ch"),
        P(None, None, "ch"),
        P("ch"),
        P("ch"),
        P("ch"),
        P("ch"),
        P(None, None, "ch"),
        P("ch"),
        P("ch"),
        P("ch", None),
        P("ch"),
    )
    return jax.shard_map(
        per_device, mesh=mesh, in_specs=in_specs, out_specs=out_specs, check_vma=False
    )
```

```python
from functools import partial
from typing import NamedTuple

import jax
import jax.numpy as jnp
from jax import lax
from jax.experimental import pallas as pl
from jax.experimental.pallas import tpu as pltpu
from jax.sharding import PartitionSpec as P

DIL = 14
EDGE = 16
EPS = 1e-05
GC0 = 0.7978845608028654
GC1 = 0.044715
F32 = jnp.float32
BF16 = jnp.bfloat16
MESH = pl.DeviceIdType.MESH
VMEM_LIMIT = 58 * 1024 * 1024
ANY = pl.BlockSpec(memory_space=pl.ANY)
SMEM = pl.BlockSpec(memory_space=pltpu.SMEM)


class Plan(NamedTuple):
    ns: int
    nz: int
    R: int
    NW: int
    L: int
    C: int
    H: int
    T1: int
    T2: int
    wb: int

    @property
    def g(self):
        return self.nz // self.R

    @property
    def nw(self):
        return self.NW // self.g

    @property
    def Lp(self):
        return self.L // 2

    @property
    def cs(self):
        return self.C // self.nz

    @property
    def Ch(self):
        return self.C // self.R

    @property
    def Hh(self):
        return self.H // self.R

    @property
    def steps(self):
        return self.nw // self.wb

    @property
    def block(self):
        down = 1
        while self.ns % (2 * down) == 0 and (self.cs // 2) % (16 * down) == 0:
            down *= 2
        across = self.ns // down
        wide = -(-(self.T1 * self.C + (self.T2 + 1) * self.C // 2) // (128 * across)) * 128
        return self.cs // down, wide, down, across

    def place(self):
        s, z = lax.axis_index("seq"), lax.axis_index("ch")
        return s, z, lax.rem(z, self.g), lax.div(z, self.g)


def gelu(z):
    t = jnp.tanh(z * (GC0 + (GC0 * GC1) * (z * z)))
    hz = 0.5 * z
    return hz + hz * t


def gelu_both(z):
    sq = z * z
    t = jnp.tanh(z * (GC0 + (GC0 * GC1) * sq))
    hz = 0.5 * z
    slope = 0.5 + 0.5 * t + hz * (1.0 - t * t) * (GC0 + (3.0 * GC0 * GC1) * sq)
    return hz + hz * t, slope


def gelu_slope(z):
    return gelu_both(z)[1]


def rows_of(shape):
    return lax.broadcasted_iota(jnp.int32, shape, 0)


def lanes_of(shape):
    return lax.broadcasted_iota(jnp.int32, shape, 1)


def total_of(lens):
    n = lens[0]
    for k in range(1, lens.shape[0]):
        n = n + lens[k]
    return n.astype(F32)


def norm_of(stats, total):
    mean = stats[0:1] / total
    square = stats[1:2] / total
    return mean, lax.rsqrt(square - mean * mean + EPS)


def column(row, n):
    return jnp.broadcast_to(row, (n, row.shape[1])).T


def mm(a, b):
    return jnp.dot(a, b, preferred_element_type=F32)


def mm_nt(a, b):
    return lax.dot_general(a, b, (((1,), (1,)), ((), ())), preferred_element_type=F32)


def mm_tn(a, b):
    return lax.dot_general(a, b, (((0,), (0,)), ((), ())), preferred_element_type=F32)


def mm_tt(a, b):
    return lax.dot_general(a, b, (((0,), (1,)), ((), ())), preferred_element_type=F32)


def pick_matrix(L):
    r, n = rows_of((L, L)), lanes_of((L, L))
    bin_of = 2 * r - jnp.where(r >= L // 2, L - 1, 0)
    return jnp.where(n == bin_of, 1.0, 0.0).astype(BF16)


class Peers:
    def __init__(self, plan, everyone=False):
        s, z, i, h = plan.place()
        self.ns = plan.ns
        self.grp = plan.nz if everyone else plan.g
        self.base = 0 if everyone else h * plan.g
        self.s, self.z = s, z
        self.count = plan.ns * self.grp
        self.me = s * self.grp + (z - self.base)

    def device(self, q):
        return (lax.div(q, self.grp), self.base + lax.rem(q, self.grp))

    def other(self, off):
        return lax.rem(self.me + off, self.count)

    def greet(self, more=()):
        barrier = pltpu.get_barrier_semaphore()
        for off in range(1, self.count):
            pl.semaphore_signal(
                barrier, inc=1, device_id=self.device(self.other(off)), device_id_type=MESH
            )
        for device in more:
            pl.semaphore_signal(barrier, inc=1, device_id=device, device_id_type=MESH)

    def meet(self, more=()):
        pl.semaphore_wait(pltpu.get_barrier_semaphore(), self.count - 1 + len(more))

    def _copy(self, link, slot, off):
        packet, buf, send, recv = link[:4]
        return pltpu.make_async_remote_copy(
            src_ref=packet,
            dst_ref=buf.at[slot],
            send_sem=send.at[off],
            recv_sem=recv.at[slot],
            device_id=self.device(self.other(off)),
            device_id_type=MESH,
        )

    def _halo_copies(self, link, edge, low, high):
        send, recv = link[4:]
        left = (lax.rem(self.s + self.ns - 1, self.ns), self.z)
        right = (lax.rem(self.s + 1, self.ns), self.z)
        return [
            pltpu.make_async_remote_copy(
                src_ref=edge.at[side],
                dst_ref=dst,
                send_sem=send.at[side],
                recv_sem=recv.at[side],
                device_id=dev,
                device_id_type=MESH,
            )
            for side, (dst, dev) in enumerate(((high, left), (low, right)))
        ]

    def start(self, link, halo=None):
        for off in range(1, self.count):
            self._copy(link, self.me, off).start()
        if halo is not None:
            for c in self._halo_copies(link, *halo):
                c.start()

    def finish(self, link, halo=None):
        packet, buf = link[:2]
        buf[self.me] = packet[...]
        for off in range(1, self.count):
            self._copy(link, self.other(off), off).wait_recv()
        acc = buf[0]
        for q in range(1, self.count):
            acc = acc + buf[q]
        for off in range(1, self.count):
            self._copy(link, self.me, off).wait_send()
        if halo is not None:
            for c in self._halo_copies(link, *halo):
                c.wait()
        return acc


def link_scratch(plan, rows, everyone=False):
    count = plan.ns * (plan.nz if everyone else plan.g)
    return [
        pltpu.VMEM((rows, plan.C), F32),
        pltpu.VMEM((count, rows, plan.C), F32),
        pltpu.SemaphoreType.DMA((count,)),
        pltpu.SemaphoreType.DMA((count,)),
        pltpu.SemaphoreType.DMA((2,)),
        pltpu.SemaphoreType.DMA((2,)),
    ]


class Gather:
    def __init__(self, plan, part, full, sems):
        self.plan, self.part, self.full, self.sems = plan, part, full, sems
        self.s, self.z, self.i, self.h = plan.place()
        self.c, self.m = lax.rem(self.s, 2), lax.div(self.s, 2)
        self.chips = plan.ns // 2
        self.every = self.chips // 4
        self.tap = lax.div(self.m, self.every)
        self.owner = lax.rem(self.m, self.every) == 0
        self.rows = plan.H // plan.nz

    def others(self):
        g, nz = self.plan.g, self.plan.nz
        return [(self.s, lax.rem(self.h * g + g + r, nz)) for r in range(nz - g)]

    def copy(self, src, dst, sem, device):
        return pltpu.make_async_remote_copy(
            src_ref=src,
            dst_ref=dst,
            send_sem=self.sems.at[0, sem],
            recv_sem=self.sems.at[1, sem],
            device_id=device,
            device_id_type=MESH,
        )

    def at_rows(self, z):
        rows = pl.ds(pl.multiple_of(z * self.rows, 16), self.rows)
        return self.full.at[self.c, self.tap, rows]

    def own(self):
        return pltpu.make_async_copy(self.part, self.at_rows(self.z), self.sems.at[0, 0])

    def line(self, off, at):
        to = lax.rem(self.z + off, self.plan.nz)
        return self.copy(self.part, self.at_rows(at), off, (self.s, to))

    def chip(self, off):
        to = lax.rem(self.m + off, self.chips)
        whole = self.full.at[self.c, self.tap]
        return self.copy(whole, whole, self.plan.nz + off, (2 * to + self.c, self.z))

    def arrival(self, k, off):
        whole = self.full.at[self.c, k]
        return self.copy(whole, whole, self.plan.nz + off, (2 * k * self.every + self.c, self.z))

    def pair(self, c):
        sem = self.plan.nz + self.chips
        return self.copy(self.full.at[c], self.full.at[c], sem, (2 * self.m + 1 - self.c, self.z))

    def step0(self):
        @pl.when(self.owner)
        def _():
            self.own().start()
            for off in range(1, self.plan.nz):
                self.line(off, self.z).start()

    def step1(self):
        @pl.when(self.owner)
        def _():
            self.own().wait()
            for off in range(1, self.plan.nz):
                self.line(off, self.z).wait_send()
                at = lax.rem(self.z + self.plan.nz - off, self.plan.nz)
                self.line(off, at).wait_recv()
            for off in range(1, self.chips):
                self.chip(off).start()

    def step2(self):
        for k in range(4):
            off = lax.rem(self.m - k * self.every + self.chips, self.chips)

            @pl.when(off != 0)
            def _():
                self.arrival(k, off).wait_recv()

        @pl.when(self.owner)
        def _():
            for off in range(1, self.chips):
                self.chip(off).wait_send()

        self.pair(self.c).start()

    def step3(self):
        self.pair(self.c).wait_send()
        self.pair(1 - self.c).wait_recv()


def first_step():
    return pl.program_id(0) == 0


def last_step():
    return pl.program_id(0) == pl.num_programs(0) - 1


def moments_kernel(plan, nw1, wb1, lens, x, xtop, xend, ctop, cend, g2, s2, pb, g3, s3,
                   stats, par, low, high, acc, edge, *link):
    t = pl.program_id(0)
    peers = Peers(plan, True)
    s, z, i, h = plan.place()
    L, C, nw, nz = plan.L, plan.C, plan.nw, plan.nz

    @pl.when(first_step())
    def _():
        peers.greet()
        acc[...] = jnp.zeros_like(acc)
        n16 = nw * 16
        for side, (xe, ce, places) in enumerate(
            ((xtop, ctop, (0, 1, 0)), (xend, cend, (14, 15, 15)))
        ):
            for k, at in enumerate(places):
                rows, lanes = rows_of((nw, n16)), lanes_of((nw, n16))
                sel = jnp.where(lanes == 16 * rows + at, 1.0, 0.0).astype(BF16)
                block = (xe if k < 2 else ce)[...].reshape(n16, C)
                edge[side, k] = mm(sel, block)

    rows = rows_of((L, C))
    for w in range(wb1):
        valid = 2 * lens[z * nw1 + t * wb1 + w] - s * L
        v = jnp.where(rows < valid, x[w].astype(F32), 0.0)
        v3 = v.reshape(L // 8, 8, C)
        acc[0] += jnp.sum(v3, axis=0)
        acc[1] += jnp.sum(v3 * v3, axis=0)

    @pl.when(last_step())
    def _():
        packet, buf = link[:2]
        packet[...] = jnp.zeros_like(packet)
        packet[0:1] = jnp.sum(acc[0], axis=0, keepdims=True)
        packet[1:2] = jnp.sum(acc[1], axis=0, keepdims=True)
        at = 0
        spans = []
        for ref in (g2, s2, pb, g3, s3):
            n = ref.shape[1]
            packet[2:3, at : at + n] = ref[...]
            spans.append((at, n))
            at += n
        peers.meet()
        halo = (edge, low, high)
        peers.start(link, halo)
        got = peers.finish(link, halo)
        stats[...] = got[0:2]
        par[...] = jnp.zeros_like(par)
        for k in range(nz):
            row = buf[s * nz + k]
            for r, (at, n) in enumerate(spans):
                par[r : r + 1, k * n : (k + 1) * n] = row[2:3, at : at + n]


def conv_kernel(plan, lens, x, hl, hr, w_ref, stats, gain, shift, taps, pw,
                X5, x2, low, high, sums, full,
                sel, edge, acc, part, gather_sems, *link):
    t = pl.program_id(0)
    peers = Peers(plan)
    gather = Gather(plan, part, full, gather_sems)
    s, z, i, h = plan.place()
    L, Lp, C, wb = plan.L, plan.Lp, plan.C, plan.wb

    @pl.when(first_step())
    def _():
        peers.greet(gather.others())
        part[...] = jnp.where(gather.tap == 3, pw[...], taps[0])
        acc[...] = jnp.zeros_like(acc)
        shape = (Lp, L)
        for k in range(plan.T1):
            at = lanes_of(shape) - (2 * rows_of(shape) + (k - 2))
            sel[k * Lp : (k + 1) * Lp] = jnp.where((at == 0) | (at == 1), 1.0, 0.0).astype(BF16)

    mean, rho = norm_of(stats[...], 2.0 * total_of(lens))
    scale = gain[...] * rho
    offset = shift[...] - mean * scale
    rows = rows_of((L, C))
    row1 = rows_of((1, C))
    row16 = rows_of((16, C))

    for w in range(wb):
        at = t * wb + w
        valid = 2 * lens[i * plan.nw + at] - s * L
        a = gelu(x[w].astype(F32) * scale + offset)
        a = jnp.where(rows < valid, a, 0.0).astype(BF16)
        picked = mm(sel[...], a)
        for k in range(5):
            X5[w * Lp : (w + 1) * Lp, k * C : (k + 1) * C] = picked[
                k * Lp : (k + 1) * Lp
            ].astype(BF16)

        def beside(ref, k, bin_at):
            a = gelu(ref[k, pl.ds(at, 1), :] * scale + offset)
            here = (row1 + bin_at < valid) & (row1 + (s * L + bin_at) >= 0)
            return jnp.where(here, a, 0.0).astype(BF16).astype(F32)

        l0, l1 = beside(hl, 0, -2), beside(hl, 1, -1)
        r0, r1 = beside(hr, 0, L), beside(hr, 1, L + 1)
        top, end = w * Lp, (w + 1) * Lp
        for k, add in ((0, l0 + l1), (1, l1)):
            X5[top : top + 16, k * C : (k + 1) * C] = (
                picked[k * Lp : k * Lp + 16] + jnp.where(row16 == 0, add, 0.0)
            ).astype(BF16)
        for k, add in ((3, r0), (4, r0 + r1)):
            X5[end - 16 : end, k * C : (k + 1) * C] = (
                picked[(k + 1) * Lp - 16 : (k + 1) * Lp] + jnp.where(row16 == 15, add, 0.0)
            ).astype(BF16)

    nc = 256
    rowp = rows_of((Lp, nc))
    for n in range(C // nc):
        cols = slice(n * nc, (n + 1) * nc)
        y = 0.5 * mm(X5[...], w_ref[:, cols])
        s0 = jnp.zeros((1, nc), F32)
        s1 = jnp.zeros((1, nc), F32)
        for w in range(wb):
            at = t * wb + w
            valid = lens[i * plan.nw + at] - s * Lp
            v = y[w * Lp : (w + 1) * Lp]
            x2[w, :, cols] = v
            edge[0, at, :, cols] = v[:EDGE].astype(BF16)
            edge[1, at, :, cols] = v[Lp - EDGE :].astype(BF16)
            v = jnp.where(rowp < valid, v, 0.0)
            s0 = s0 + jnp.sum(v, axis=0, keepdims=True)
            s1 = s1 + jnp.sum(v * v, axis=0, keepdims=True)
        acc[0:1, cols] += s0
        acc[1:2, cols] += s1

    steps = plan.steps

    @pl.when(first_step())
    def _():
        peers.meet(gather.others())
        gather.step0()

    @pl.when(t == min(1, steps - 1))
    def _():
        gather.step1()

    @pl.when(t == min(2, steps - 1))
    def _():
        gather.step2()

    @pl.when(last_step())
    def _():
        link[0][...] = acc[...]
        halo = (edge, low, high)
        peers.start(link, halo)
        sums[...] = peers.finish(link, halo)
        gather.step3()


def dilated_kernel(plan, lens, x2, lo, hi, w_ref, stats, par,
                   Y3, c2, low, high, sums, ext, wf, edge, acc, *link):
    t = pl.program_id(0)
    peers = Peers(plan)
    s, z, i, h = plan.place()
    Lp, C, H, wb = plan.Lp, plan.C, plan.H, plan.wb

    @pl.when(first_step())
    def _():
        peers.greet()
        acc[...] = jnp.zeros_like(acc)
        for k in range(plan.T2):
            for c in range(2):
                at = k * C + c * (C // 2)
                wf[:, at : at + C // 2] = w_ref[c, k]

    mean, rho = norm_of(stats[...], total_of(lens))
    scale = par[0:1] * rho
    offset = par[1:2] - mean * scale
    rows = rows_of((Lp, C))
    rowe = rows_of((EDGE, C))

    for w in range(wb):
        valid = lens[i * plan.nw + t * wb + w] - s * Lp
        a = jnp.where(rows < valid, gelu(x2[w] * scale + offset), 0.0)
        al = gelu(lo[w].astype(F32) * scale + offset)
        al = jnp.where((rowe - EDGE < valid) & (s > 0), al, 0.0)
        ah = gelu(hi[w].astype(F32) * scale + offset)
        ah = jnp.where(rowe + Lp < valid, ah, 0.0)
        ext[0:EDGE] = al
        ext[EDGE : EDGE + Lp] = a
        ext[EDGE + Lp :] = ah
        top, end = w * Lp, (w + 1) * Lp
        Y3[top:end, 0:C] = ext[EDGE - DIL : EDGE - DIL + Lp].astype(BF16)
        Y3[top:end, C : 2 * C] = a.astype(BF16)
        Y3[top:end, 2 * C : 3 * C] = ext[EDGE + DIL : EDGE + DIL + Lp].astype(BF16)

    y = mm_nt(Y3[...], wf[...])
    rowh = rows_of((Lp, H))
    s0 = jnp.zeros((1, H), F32)
    s1 = jnp.zeros((1, H), F32)
    for w in range(wb):
        at = t * wb + w
        valid = lens[i * plan.nw + at] - s * Lp
        v = y[w * Lp : (w + 1) * Lp]
        c2[w] = v
        edge[0, at] = v[:EDGE].astype(BF16)
        edge[1, at] = v[Lp - EDGE :].astype(BF16)
        v = jnp.where(rowh < valid, v, 0.0)
        s0 = s0 + jnp.sum(v, axis=0, keepdims=True)
        s1 = s1 + jnp.sum(v * v, axis=0, keepdims=True)
    acc[0:1, 0:H] += s0
    acc[1:2, 0:H] += s1

    @pl.when(last_step())
    def _():
        link[0][...] = acc[...]
        halo = (edge, low, high)
        peers.meet()
        peers.start(link, halo)
        sums[...] = peers.finish(link, halo)[:, 0:H]


def point_kernel(plan, lens, c2, x2, cot, w_ref, pb, stats, par,
                 res, dz, pgrad, low, high, sums, bsum,
                 pw, a3s, dos, pacc, edge, acc, *link):
    t = pl.program_id(0)
    peers = Peers(plan)
    s, z, i, h = plan.place()
    Lp, C, H, wb, cs = plan.Lp, plan.C, plan.H, plan.wb, plan.cs

    @pl.when(first_step())
    def _():
        peers.greet()
        acc[...] = jnp.zeros_like(acc)
        pacc[...] = jnp.zeros_like(pacc)
        for c in range(2):
            pw[:, c * (C // 2) : (c + 1) * (C // 2)] = w_ref[c, 0]

    mean, rho = norm_of(stats[...], total_of(lens))
    scale = par[3:4, 0:H] * rho
    offset = par[4:5, 0:H] - mean * scale
    rowc = rows_of((Lp, C))
    rowh = rows_of((Lp, H))

    s0 = jnp.zeros((1, H), F32)
    s1 = jnp.zeros((1, H), F32)
    sb = jnp.zeros((1, C), F32)
    for w in range(wb):
        at = t * wb + w
        valid = lens[i * plan.nw + at] - s * Lp
        top, end = w * Lp, (w + 1) * Lp
        d = jnp.where(rowc < valid, cot[w].astype(F32), 0.0)
        sb = sb + jnp.sum(d, axis=0, keepdims=True)
        d = d.astype(BF16)
        dos[top:end] = d
        v = c2[w]
        act, slope = gelu_both(v * scale + offset)
        a3s[top:end] = jnp.where(rowh < valid, act, 0.0).astype(BF16)
        dzw = mm_nt(d, pw[...]) * slope
        dz[w] = dzw
        edge[0, at] = dzw[:EDGE].astype(BF16)
        edge[1, at] = dzw[Lp - EDGE :].astype(BF16)
        hat = (v - mean) * rho
        s0 = s0 + jnp.sum(dzw, axis=0, keepdims=True)
        s1 = s1 + jnp.sum(dzw * hat, axis=0, keepdims=True)
    acc[0:1, 0:H] += s0
    acc[1:2, 0:H] += s1
    acc[2:3] += sb

    @pl.when(last_step())
    def _():
        link[0][...] = acc[...]
        peers.meet()
        peers.start(link, (edge, low, high))

    y = mm(a3s[...], w_ref[h, 0])
    rowr = rows_of((Lp, y.shape[1]))
    for w in range(wb):
        valid = lens[i * plan.nw + t * wb + w] - s * Lp
        r = x2[w] + y[w * Lp : (w + 1) * Lp] + pb[2:3]
        r = jnp.where(rowr < valid, r, 0.0).T.astype(BF16)
        for k in range(plan.g):
            res[k, w] = r[k * cs : (k + 1) * cs]
    pacc[...] += mm_tn(a3s[...], dos[...])

    @pl.when(last_step())
    def _():
        rows = pl.ds(pl.multiple_of(h * plan.Hh, 16), plan.Hh)
        pgrad[...] = pacc[rows].astype(BF16)
        got = peers.finish(link, (edge, low, high))
        sums[...] = got[0:2, 0:H]
        bsum[...] = got[2:3]


def dilated_back_kernel(plan, lens, c2, clo, chi, dz3, zlo, zhi, x2, Y3, w_ref,
                        stats3, sums3, stats2, par, pgrad,
                        dz2, grads, low, high, sums,
                        ext, Z3, wt, wacc, edge, acc, *link):
    t = pl.program_id(0)
    peers = Peers(plan)
    s, z, i, h = plan.place()
    Lp, C, H, wb, nw = plan.Lp, plan.C, plan.H, plan.wb, plan.nw

    @pl.when(first_step())
    def _():
        peers.greet()
        acc[...] = jnp.zeros_like(acc)
        wacc[...] = jnp.zeros_like(wacc)
        for k in range(plan.T2):
            for c in range(2):
                cols = slice(c * (C // 2), (c + 1) * (C // 2))
                wt[k * H : (k + 1) * H, cols] = w_ref[c, k]

    total = total_of(lens)
    mean3, rho3 = norm_of(stats3[...], total)
    gr3 = par[3:4, 0:H] * rho3
    sg3 = sums3[0:1] / total
    gg3 = sums3[1:2] / total
    mean2, rho2 = norm_of(stats2[...], total)
    scale2 = par[0:1] * rho2
    offset2 = par[1:2] - mean2 * scale2
    rowh = rows_of((Lp, H))
    rowe = rows_of((EDGE, H))
    rowc = rows_of((Lp, C))

    def back(dz, v):
        return gr3 * (dz - (sg3 + (v - mean3) * rho3 * gg3))

    for w in range(wb):
        valid = lens[i * nw + t * wb + w] - s * Lp
        d = jnp.where(rowh < valid, back(dz3[w], c2[w]), 0.0)
        dl = back(zlo[w].astype(F32), clo[w].astype(F32))
        dl = jnp.where((rowe - EDGE < valid) & (s > 0), dl, 0.0)
        dh = back(zhi[w].astype(F32), chi[w].astype(F32))
        dh = jnp.where(rowe + Lp < valid, dh, 0.0)
        ext[0:EDGE] = dl
        ext[EDGE : EDGE + Lp] = d
        ext[EDGE + Lp :] = dh
        top, end = w * Lp, (w + 1) * Lp
        Z3[top:end, 0:H] = ext[EDGE + DIL : EDGE + DIL + Lp].astype(BF16)
        Z3[top:end, H : 2 * H] = d.astype(BF16)
        Z3[top:end, 2 * H : 3 * H] = ext[EDGE - DIL : EDGE - DIL + Lp].astype(BF16)

    y = mm(Z3[...], wt[...])

    s0 = jnp.zeros((1, C), F32)
    s1 = jnp.zeros((1, C), F32)
    for w in range(wb):
        at = t * wb + w
        valid = lens[i * nw + at] - s * Lp
        v = x2[w]
        dzw = y[w * Lp : (w + 1) * Lp] * gelu_slope(v * scale2 + offset2)
        dzw = jnp.where(rowc < valid, dzw, 0.0)
        dz2[w] = dzw
        edge[0, pl.ds(at, 1)] = dzw[0:1]
        edge[1, pl.ds(at, 1)] = dzw[Lp - 1 : Lp]
        s0 = s0 + jnp.sum(dzw, axis=0, keepdims=True)
        s1 = s1 + jnp.sum(dzw * ((v - mean2) * rho2), axis=0, keepdims=True)
    acc[0:1] += s0
    acc[1:2] += s1

    @pl.when(last_step())
    def _():
        link[0][...] = acc[...]
        peers.meet()
        peers.start(link, (edge, low, high))

    wacc[...] += mm_tn(Z3[:, H : 2 * H], Y3[...])

    @pl.when(last_step())
    def _():
        rows = pl.ds(pl.multiple_of(h * plan.Hh, 16), plan.Hh)
        grads[:, 0 : plan.T2 * C] = wacc[rows].astype(BF16)
        grads[:, plan.T2 * C :] = pgrad[...]
        sums[...] = peers.finish(link, (edge, low, high))


def conv_grad_kernel(plan, lens, dz2, zlo, zhi, x2, lo, hi, cot, hl, hr, X5,
                     stats2, sums2, par, grads, res, D3, blocks, result,
                     ext, acc, bulk_send, bulk_recv, own_sem):
    t = pl.program_id(0)
    s, z, i, h = plan.place()
    Lp, C, wb, Ch, cs = plan.Lp, plan.C, plan.wb, plan.Ch, plan.cs

    g, nw = plan.g, plan.nw

    def own_copy():
        return pltpu.make_async_copy(res.at[i], result.at[pl.ds(i * nw, nw)], own_sem)

    def bulk(off, sender):
        to = lax.rem(i + off, g)
        return pltpu.make_async_remote_copy(
            src_ref=res.at[to],
            dst_ref=result.at[pl.ds(sender * nw, nw)],
            send_sem=bulk_send.at[off],
            recv_sem=bulk_recv.at[off],
            device_id=(s, h * g + to),
            device_id_type=MESH,
        )

    @pl.when(first_step())
    def _():
        acc[...] = jnp.zeros_like(acc)
        barrier = pltpu.get_barrier_semaphore()
        for off in range(1, g):
            pl.semaphore_signal(
                barrier,
                inc=1,
                device_id=(s, h * g + lax.rem(i + off, g)),
                device_id_type=MESH,
            )
        own_copy().start()

    total = total_of(lens)
    mean, rho = norm_of(stats2[...], total)
    gr = par[0:1] * rho
    sg = sums2[0:1] / total
    gg = sums2[1:2] / total
    rowc = rows_of((Lp, C))
    row1 = rows_of((1, C))

    def back(dout, dz, v):
        return 0.5 * (dout + gr * (dz - (sg + (v - mean) * rho * gg)))

    for w in range(wb):
        at = t * wb + w
        valid = lens[i * plan.nw + at] - s * Lp
        d = back(cot[w].astype(F32), dz2[w], x2[w])
        d = jnp.where(rowc < valid, d, 0.0)
        dl = back(hl[2, pl.ds(at, 1), :], zlo[pl.ds(at, 1), :], lo[w, EDGE - 1 : EDGE].astype(F32))
        dl = jnp.where((row1 - 1 < valid) & (s > 0), dl, 0.0)
        dh = back(hr[2, pl.ds(at, 1), :], zhi[pl.ds(at, 1), :], hi[w, 0:1].astype(F32))
        dh = jnp.where(row1 + Lp < valid, dh, 0.0)
        ext[7:8] = dl
        ext[8 : 8 + Lp] = d
        ext[8 + Lp : 9 + Lp] = dh
        top, end = w * Lp, (w + 1) * Lp
        D3[top:end, 0:C] = ext[9 : 9 + Lp].astype(BF16)
        D3[top:end, C : 2 * C] = d.astype(BF16)
        D3[top:end, 2 * C : 3 * C] = ext[7 : 7 + Lp].astype(BF16)

    @pl.when(first_step())
    def _():
        pl.semaphore_wait(pltpu.get_barrier_semaphore(), g - 1)
        for off in range(1, g):
            bulk(off, i).start()

    dh = D3[:, pl.ds(pl.multiple_of(C + h * Ch, 128), Ch)]
    acc[...] += mm_tn(dh, X5[...])

    @pl.when(last_step())
    def _():
        rb, wide, down, across = plan.block
        n1, n2 = plan.T1 * C, (plan.T2 + 1) * C // 2
        hs = plan.H // plan.nz
        for k in range(plan.g):
            for q in range(plan.ns):
                r, c = q // across * rb, q % across * wide
                dst = blocks.at[q % 2, q // 2, k]
                a, b = min(c, n1), min(c + wide, n1)
                if b > a:
                    dst[:, 0 : b - a] = acc[k * cs + r : k * cs + r + rb, a:b].astype(BF16)
                a, b = max(c, n1) - n1, min(c + wide, n1 + n2) - n1
                if b > a:
                    side, r2 = r // hs, r % hs
                    dst[:, a + n1 - c : b + n1 - c] = grads[
                        k * hs + r2 : k * hs + r2 + rb, side * n2 + a : side * n2 + b
                    ]
        own_copy().wait()
        for off in range(1, g):
            bulk(off, i).wait_send()
            bulk(off, lax.rem(i + g - off, g)).wait_recv()


class Reduction:
    def __init__(self, plan, blocks, out, mine, got, mid, spread, half, mate, sems):
        self.plan = plan
        self.blocks, self.out = blocks, out
        self.mine, self.got, self.mid, self.spread = mine, got, mid, spread
        self.half, self.mate = half, mate
        self.sems = sems
        self.s, self.z, self.i, self.h = plan.place()
        self.c = lax.rem(self.s, 2)
        self.m = lax.div(self.s, 2)
        self.chips = plan.ns // 2

    def copy(self, src, dst, sem, device):
        return pltpu.make_async_remote_copy(
            src_ref=src,
            dst_ref=dst,
            send_sem=self.sems.at[0, sem],
            recv_sem=self.sems.at[1, sem],
            device_id=device,
            device_id_type=MESH,
        )

    def pair(self):
        return (2 * self.m + (1 - self.c), self.z)

    def chip(self, off):
        return lax.rem(self.m + off, self.chips)

    def member(self, off):
        return lax.rem(self.i + off, self.plan.g)

    def own0(self):
        return pltpu.make_async_copy(self.blocks.at[self.c], self.mine, self.sems.at[0, 0])

    def phase0(self):
        return self.copy(self.blocks.at[1 - self.c], self.got, 1, self.pair())

    def phase1(self, off, at):
        to = self.chip(off)
        return self.copy(
            self.mid.at[to], self.spread.at[at], 2 + off, (2 * to + self.c, self.z)
        )

    def phase2(self, off):
        to = self.member(off)
        sem = 2 + self.chips + off
        return self.copy(
            self.half.at[to], self.mate.at[off], sem, (self.s, self.h * self.plan.g + to)
        )

    def phase3(self, off, at):
        to = self.chip(off)
        sem = 2 + self.chips + self.plan.g + off
        return self.copy(
            self.out.at[self.c, self.m], self.out.at[self.c, at], sem, (2 * to + self.c, self.z)
        )

    def phase4(self, c):
        sem = 2 + 2 * self.chips + self.plan.g
        return self.copy(self.out.at[self.c], self.out.at[c], sem, self.pair())

    def step0(self):
        self.own0().start()
        self.phase0().start()

    def step1(self):
        self.own0().wait()
        self.phase0().wait()

        @pl.loop(0, self.chips)
        def _(n):
            self.mid[n] = (self.mine[n].astype(F32) + self.got[n].astype(F32)).astype(BF16)

        for off in range(1, self.chips):
            self.phase1(off, self.m).start()

    def step2(self):
        for off in range(1, self.chips):
            self.phase1(off, self.m).wait_send()
            self.phase1(off, self.chip(self.chips - off)).wait_recv()
        self.spread[self.m] = self.mid[self.m]

        @pl.loop(0, self.plan.g)
        def _(n):
            v = self.spread[0, n].astype(F32)
            for k in range(1, self.chips):
                v = v + self.spread[k, n].astype(F32)
            self.half[n] = v.astype(BF16)

        for off in range(1, self.plan.g):
            self.phase2(off).start()

    def step3(self):
        for off in range(1, self.plan.g):
            self.phase2(off).wait()
        v = self.half[self.i].astype(F32)
        for off in range(1, self.plan.g):
            v = v + self.mate[off].astype(F32)
        self.out[self.c, self.m] = v.astype(BF16)
        for off in range(1, self.chips):
            self.phase3(off, self.m).start()

    def step4(self):
        for off in range(1, self.chips):
            self.phase3(off, self.m).wait_send()
            self.phase3(off, self.chip(self.chips - off)).wait_recv()
        self.phase4(self.c).start()

    def step5(self):
        self.phase4(self.c).wait_send()
        self.phase4(1 - self.c).wait_recv()


def conv_back_kernel(plan, lens, D3, x, taps, stats, gain, shift, blocks,
                     gz, sums, summed, wcat, pick, cols, y, part, acc,
                     bulk_send, bulk_recv, own_sem,
                     mine, got, mid, spread, half, mate, out, red_sems, *link):
    t = pl.program_id(0)
    peers = Peers(plan)
    s, z, i, h = plan.place()
    L, Lp, C, wb, g, nw = plan.L, plan.Lp, plan.C, plan.wb, plan.g, plan.nw
    Ch, cs = plan.Ch, plan.cs
    steps = plan.steps
    red = Reduction(plan, blocks, out, mine, got, mid, spread, half, mate, red_sems)

    def own_copy(step):
        return pltpu.make_async_copy(
            part.at[step, i], gz.at[pl.ds(i * nw + step * wb, wb)], own_sem.at[step]
        )

    def bulk(step, off, sender):
        to = lax.rem(i + off, g)
        return pltpu.make_async_remote_copy(
            src_ref=part.at[step, to],
            dst_ref=gz.at[pl.ds(sender * nw + step * wb, wb)],
            send_sem=bulk_send.at[step, off],
            recv_sem=bulk_recv.at[step, off],
            device_id=(s, h * g + to),
            device_id_type=MESH,
        )

    @pl.when(first_step())
    def _():
        peers.greet()
        acc[...] = jnp.zeros_like(acc)
        pick[...] = pick_matrix(L)
        mean, rho = norm_of(stats[...], 2.0 * total_of(lens))
        scale = gain[...] * rho
        for k, row in enumerate((scale, shift[...] - mean * scale, rho, -mean * rho)):
            cols[k] = column(row, L)
        w = [taps[k].astype(F32) for k in range(5)]
        for r, parts in enumerate(
            ((w[0], w[1] + w[2], w[3] + w[4]), (w[0] + w[1], w[2] + w[3], w[4]))
        ):
            for k, v in enumerate(parts):
                wcat[r * Ch : (r + 1) * Ch, k * C : (k + 1) * C] = v.astype(BF16)

    y[...] = mm_nt(wcat[...], D3[...])
    lanes = lanes_of((Ch, L))
    bins = 2 * lanes - jnp.where(lanes >= Lp, L - 1, 0)
    for w in range(wb):
        valid = 2 * lens[i * nw + t * wb + w] - s * L
        top, end = w * Lp, (w + 1) * Lp
        v = mm_tt(x[w], pick[...])
        da = jnp.concatenate([y[0:Ch, top:end], y[Ch:, top:end]], axis=1)
        dzw = da * gelu_slope(v * cols[0] + cols[1])
        dzw = jnp.where(bins < valid, dzw, 0.0)
        acc[0] += dzw
        acc[1] += dzw * (v * cols[2] + cols[3])
        dzw = dzw.astype(BF16)
        for k in range(g):
            part[t, k, w] = dzw[k * cs : (k + 1) * cs]

    @pl.when(first_step())
    def _():
        peers.meet()
        red.step0()

    own_copy(t).start()

    @pl.when(t == min(1, steps - 1))
    def _():
        red.step1()

    @pl.when(last_step())
    def _():
        red.step2()

    for off in range(1, g):
        bulk(t, off, i).start()

    @pl.when(last_step())
    def _():
        packet = link[0]
        packet[...] = jnp.zeros_like(packet)
        packet[0:1, 0:Ch] = jnp.sum(acc[0].T, axis=0, keepdims=True)
        packet[1:2, 0:Ch] = jnp.sum(acc[1].T, axis=0, keepdims=True)
        peers.start(link)
        red.step3()
        sums[...] = peers.finish(link)[:, 0:Ch]
        red.step4()
        red.step5()
        summed[...] = out[...]
        for step in range(steps):
            own_copy(step).wait()
            for off in range(1, g):
                bulk(step, off, i).wait_send()
                bulk(step, off, lax.rem(i + g - off, g)).wait_recv()


def input_grad_kernel(plan, lens, x, gz, stats, sums, gain, result, summed, sums2, sums3, bsum,
                      out, out_result, conv_grad, dil_grad, point_grad,
                      g1, b1, g2, b2, g3, b3, pb, pick, cols, xt):
    t = pl.program_id(0)
    s, z, i, h = plan.place()
    L, Ch, cs, wb = plan.L, plan.Ch, plan.cs, plan.wb
    mine = pl.ds(pl.multiple_of(i * cs, 16), cs)

    @pl.when(first_step())
    def _():
        n = 2.0 * total_of(lens)
        mean, rho = norm_of(stats[...], n)
        gr = gain[...] * rho
        gg = sums[1:2] / n * rho
        for k, row in enumerate((gr, -gr * gg, gr * (mean * gg - sums[0:1] / n))):
            xt[...] = column(row, L)
            cols[k] = xt[mine]
        pick[...] = pick_matrix(L)

        def mine_of(src, at, which, count, *dsts):
            n = dsts[0].shape[1]
            for k in range(count):

                @pl.when(which == k)
                def _():
                    for dst, r in zip(dsts, at):
                        dst[...] = src[r : r + 1, k * n : (k + 1) * n]

        mine_of(sums, (1, 0), i, plan.g, g1, b1)
        mine_of(sums2, (1, 0), z, plan.nz, g2, b2)
        mine_of(sums3, (1, 0), z, plan.nz, g3, b3)
        mine_of(bsum, (0,), z, plan.nz, pb)

    out_result[...] = result[...]
    rb, wide, down, across = plan.block
    every = (plan.NW // wb) // down
    C, n1, hs = plan.C, plan.T1 * plan.C, plan.H // plan.nz

    def spread(r):
        for c in range(across):
            piece = summed[c % 2, c // 2].astype(F32)
            lo, hi = c * wide, (c + 1) * wide
            for k in range(plan.T1):
                a, b = max(lo, k * C), min(hi, (k + 1) * C)
                if b > a:
                    conv_grad[k, :, a - k * C : b - k * C] = piece[:, a - lo : b - lo]
            side, r2 = r * rb // hs, r * rb % hs
            for k in range(2):
                n0 = n1 + k * C
                a, b = max(lo, n0), min(hi, n0 + C)
                if b > a:
                    v = piece[:, a - lo : b - lo]
                    if 2 * side + k < plan.T2:
                        dil_grad[2 * side + k, r2 : r2 + rb, a - n0 : b - n0] = v
                    else:
                        point_grad[r2 : r2 + rb, a - n0 : b - n0] = v

    for r in range(down):
        pl.when(t == r * every)(partial(spread, r))

    lanes = lanes_of((cs, L))
    for w in range(wb):
        valid = 2 * lens[t * wb + w] - s * L
        xt[...] = x[w].astype(F32).T
        v = xt[mine]
        dz = mm(gz[w], pick[...])
        r = cols[0] * dz + v * cols[1] + cols[2]
        out[w] = jnp.where(lanes < valid, r, 0.0).astype(BF16)


def call(kernel, plan, name, steps, ins, outs, scratch, flops, nbytes, cid=None):
    extra = {} if cid is None else dict(collective_id=cid, has_side_effects=True)
    return pl.pallas_call(
        partial(kernel, plan),
        grid=(steps,),
        in_specs=[SMEM] + [spec for spec, _ in ins],
        out_specs=[spec for spec, _, _ in outs],
        out_shape=[jax.ShapeDtypeStruct(shape, dtype) for _, shape, dtype in outs],
        scratch_shapes=scratch,
        compiler_params=pltpu.CompilerParams(vmem_limit_bytes=VMEM_LIMIT, **extra),
        cost_estimate=pl.CostEstimate(
            flops=int(flops), bytes_accessed=int(nbytes), transcendentals=0
        ),
        name=name,
    )


def per_device(
    inputs,
    lengths,
    input_gain,
    input_shift,
    conv_weight,
    branch_gain,
    branch_shift,
    dilated_tap_weight,
    mixer_gain,
    mixer_shift,
    point_weight,
    point_bias,
    cotangent,
):
    NW, L, C = inputs.shape
    Lp = L // 2
    nz = lax.axis_size("ch")
    R = 2
    plan = Plan(
        ns=lax.axis_size("seq"),
        nz=nz,
        R=R,
        NW=NW,
        L=L,
        C=C,
        H=mixer_gain.shape[0] * nz,
        T1=conv_weight.shape[0],
        T2=dilated_tap_weight.shape[0],
        wb=min(NW * R // nz, max(1, 512 // Lp)),
    )
    g, nw, cs, Ch, H, Hh, wb = plan.g, plan.nw, plan.cs, plan.Ch, plan.H, plan.Hh, plan.wb
    T1, T2, steps = plan.T1, plan.T2, plan.steps
    M = wb * Lp
    hs = H // nz
    lens = lengths.astype(jnp.int32)
    gain1 = input_gain.reshape(1, C)
    shift1 = input_shift.reshape(1, C)

    def row(a):
        return a.reshape(1, a.shape[0])

    def grp():
        return lax.rem(lax.axis_index("ch"), g)

    def half():
        return lax.div(lax.axis_index("ch"), g)

    def core():
        return lax.rem(lax.axis_index("seq"), 2)

    def chip4():
        return lax.div(lax.axis_index("seq"), plan.ns // 4)

    def whole(*shape):
        return pl.BlockSpec(shape, lambda t: (0,) * len(shape), pipeline_mode=pl.Buffered(1))

    def const(*shape):
        return pl.BlockSpec(shape, lambda t: (0,) * len(shape))

    def win(*shape):
        return pl.BlockSpec(shape, lambda t: (t,) + (0,) * (len(shape) - 1))

    def arg_win(n, width):
        return pl.BlockSpec((wb, n, width), lambda t: (grp() * steps + t, 0, 0))

    def ins(*pairs):
        return [p for p in pairs]

    nw1 = NW // nz
    wb1 = min(nw1, wb)

    def edge_spec(n):
        return pl.BlockSpec(
            (nw, 16, C), lambda t: (grp(), n, 0), pipeline_mode=pl.Buffered(1)
        )

    pairs = ins(
        (
            pl.BlockSpec((wb1, L, C), lambda t: (lax.axis_index("ch") * (nw1 // wb1) + t, 0, 0)),
            inputs,
        ),
        (edge_spec(0), inputs),
        (edge_spec(L // 16 - 1), inputs),
        (edge_spec(0), cotangent),
        (edge_spec(Lp // 16 - 1), cotangent),
        (whole(1, cs), row(branch_gain)),
        (whole(1, cs), row(branch_shift)),
        (whole(1, cs), row(point_bias)),
        (whole(1, H // nz), row(mixer_gain)),
        (whole(1, H // nz), row(mixer_shift)),
    )
    stats1, par, hl, hr = call(
        lambda plan, *refs: moments_kernel(plan, nw1, wb1, *refs),
        plan,
        "moments",
        nw1 // wb1,
        pairs,
        [
            (const(2, C), (2, C), F32),
            (const(8, C), (8, C), F32),
            (ANY, (3, nw, C), F32),
            (ANY, (3, nw, C), F32),
        ],
        [pltpu.VMEM((2, 8, C), F32), pltpu.VMEM((2, 3, nw, C), F32)]
        + link_scratch(plan, 3, True),
        0,
        nw1 * L * C * 2,
        cid=1,
    )(lens, *[a for _, a in pairs])

    pairs = ins(
        (arg_win(L, C), inputs),
        (whole(3, nw, C), hl),
        (whole(3, nw, C), hr),
        (whole(T1 * C, C), conv_weight.reshape(T1 * C, C)),
        (whole(2, C), stats1),
        (whole(1, C), gain1),
        (whole(1, C), shift1),
        (
            pl.BlockSpec((1, hs, C // 2), lambda t: (jnp.minimum(chip4(), T2 - 1), 0, core())),
            jnp.swapaxes(dilated_tap_weight, 1, 2),
        ),
        (pl.BlockSpec((hs, C // 2), lambda t: (0, core())), point_weight),
    )
    X5, x2, lo2, hi2, stats2, full = call(
        conv_kernel,
        plan,
        "conv",
        steps,
        pairs,
        [
            (win(M, T1 * C), (nw * Lp, T1 * C), BF16),
            (win(wb, Lp, C), (nw, Lp, C), F32),
            (ANY, (nw, EDGE, C), BF16),
            (ANY, (nw, EDGE, C), BF16),
            (const(2, C), (2, C), F32),
            (ANY, (2, T2 + 1, H, C // 2), BF16),
        ],
        [
            pltpu.VMEM((T1 * Lp, L), BF16),
            pltpu.VMEM((2, nw, EDGE, C), BF16),
            pltpu.VMEM((2, C), F32),
            pltpu.VMEM((hs, C // 2), BF16),
            pltpu.SemaphoreType.DMA((2, nz + plan.ns // 2 + 1)),
        ]
        + link_scratch(plan, 2),
        2 * nw * Lp * T1 * C * C,
        nw * Lp * C * 20,
        cid=2,
    )(lens, *[a for _, a in pairs])

    taps_spec = whole(2, T2, H, C // 2)
    pw_spec = pl.BlockSpec(
        (2, 1, H, C // 2), lambda t: (0, T2, 0, 0), pipeline_mode=pl.Buffered(1)
    )

    pairs = ins(
        (win(wb, Lp, C), x2),
        (win(wb, EDGE, C), lo2),
        (win(wb, EDGE, C), hi2),
        (taps_spec, full),
        (whole(2, C), stats2),
        (whole(8, C), par),
    )
    Y3, c2, lo3, hi3, stats3 = call(
        dilated_kernel,
        plan,
        "dilated",
        steps,
        pairs,
        [
            (win(M, T2 * C), (nw * Lp, T2 * C), BF16),
            (win(wb, Lp, H), (nw, Lp, H), F32),
            (ANY, (nw, EDGE, H), BF16),
            (ANY, (nw, EDGE, H), BF16),
            (const(2, H), (2, H), F32),
        ],
        [
            pltpu.VMEM((Lp + 2 * EDGE, C), F32),
            pltpu.VMEM((H, T2 * C), BF16),
            pltpu.VMEM((2, nw, EDGE, H), BF16),
            pltpu.VMEM((2, C), F32),
        ]
        + link_scratch(plan, 2),
        2 * nw * Lp * T2 * C * H,
        nw * Lp * C * 12,
        cid=3,
    )(lens, *[a for _, a in pairs])

    pairs = ins(
        (win(wb, Lp, H), c2),
        (pl.BlockSpec((wb, Lp, Ch), lambda t: (t, 0, half())), x2),
        (arg_win(Lp, C), cotangent),
        (pw_spec, full),
        (pl.BlockSpec((8, Ch), lambda t: (0, half()), pipeline_mode=pl.Buffered(1)), par),
        (whole(2, H), stats3),
        (whole(8, C), par),
    )
    res, dz3, pgrad, zlo3, zhi3, sums3, bsum = call(
        point_kernel,
        plan,
        "point",
        steps,
        pairs,
        [
            (
                pl.BlockSpec((g, wb, cs, Lp), lambda t: (0, t, 0, 0)),
                (g, nw, cs, Lp),
                BF16,
            ),
            (win(wb, Lp, H), (nw, Lp, H), F32),
            (const(Hh, C), (Hh, C), BF16),
            (ANY, (nw, EDGE, H), BF16),
            (ANY, (nw, EDGE, H), BF16),
            (const(2, H), (2, H), F32),
            (const(1, C), (1, C), F32),
        ],
        [
            pltpu.VMEM((H, C), BF16),
            pltpu.VMEM((M, H), BF16),
            pltpu.VMEM((M, C), BF16),
            pltpu.VMEM((H, C), F32),
            pltpu.VMEM((2, nw, EDGE, H), BF16),
            pltpu.VMEM((3, C), F32),
        ]
        + link_scratch(plan, 3),
        5 * nw * Lp * C * H,
        nw * Lp * C * 10,
        cid=4,
    )(lens, *[a for _, a in pairs])

    pairs = ins(
        (win(wb, Lp, H), c2),
        (win(wb, EDGE, H), lo3),
        (win(wb, EDGE, H), hi3),
        (win(wb, Lp, H), dz3),
        (win(wb, EDGE, H), zlo3),
        (win(wb, EDGE, H), zhi3),
        (win(wb, Lp, C), x2),
        (win(M, T2 * C), Y3),
        (taps_spec, full),
        (whole(2, H), stats3),
        (whole(2, H), sums3),
        (whole(2, C), stats2),
        (whole(8, C), par),
        (whole(Hh, C), pgrad),
    )
    dz2, grads, zlo2, zhi2, sums2 = call(
        dilated_back_kernel,
        plan,
        "dilated_back",
        steps,
        pairs,
        [
            (win(wb, Lp, C), (nw, Lp, C), F32),
            (const(Hh, (T2 + 1) * C), (Hh, (T2 + 1) * C), BF16),
            (ANY, (nw, C), F32),
            (ANY, (nw, C), F32),
            (const(2, C), (2, C), F32),
        ],
        [
            pltpu.VMEM((Lp + 2 * EDGE, H), F32),
            pltpu.VMEM((M, T2 * H), BF16),
            pltpu.VMEM((T2 * H, C), BF16),
            pltpu.VMEM((H, T2 * C), F32),
            pltpu.VMEM((2, nw, C), F32),
            pltpu.VMEM((2, C), F32),
        ]
        + link_scratch(plan, 2),
        4 * nw * Lp * T2 * C * H,
        nw * Lp * C * 20,
        cid=5,
    )(lens, *[a for _, a in pairs])

    pairs = ins(
        (win(wb, Lp, C), dz2),
        (whole(nw, C), zlo2),
        (whole(nw, C), zhi2),
        (win(wb, Lp, C), x2),
        (win(wb, EDGE, C), lo2),
        (win(wb, EDGE, C), hi2),
        (arg_win(Lp, C), cotangent),
        (whole(3, nw, C), hl),
        (whole(3, nw, C), hr),
        (win(M, T1 * C), X5),
        (whole(2, C), stats2),
        (whole(2, C), sums2),
        (whole(8, C), par),
        (whole(Hh, (T2 + 1) * C), grads),
        (ANY, res),
    )
    rb, wide, down, across = plan.block
    bshape = (2, plan.ns // 2, g, rb, wide)
    D3, blocks, result = call(
        conv_grad_kernel,
        plan,
        "conv_grad",
        steps,
        pairs,
        [
            (win(M, 3 * C), (nw * Lp, 3 * C), BF16),
            (const(*bshape), bshape, BF16),
            (ANY, (NW, cs, Lp), BF16),
        ],
        [
            pltpu.VMEM((Lp + 16, C), F32),
            pltpu.VMEM((Ch, T1 * C), F32),
            pltpu.SemaphoreType.DMA((g,)),
            pltpu.SemaphoreType.DMA((g,)),
            pltpu.SemaphoreType.DMA,
        ],
        2 * nw * Lp * T1 * C * Ch,
        nw * Lp * C * 30,
        cid=7,
    )(lens, *[a for _, a in pairs])

    def half_of(n):
        return pl.BlockSpec((n, Ch), lambda t: (0, half()), pipeline_mode=pl.Buffered(1))

    pairs = ins(
        (win(M, 3 * C), D3),
        (pl.BlockSpec((wb, L, Ch), lambda t: (grp() * steps + t, 0, half())), inputs),
        (
            pl.BlockSpec(
                (T1, Ch, C), lambda t: (0, half(), 0), pipeline_mode=pl.Buffered(1)
            ),
            conv_weight,
        ),
        (half_of(2), stats1),
        (half_of(1), gain1),
        (half_of(1), shift1),
        (ANY, blocks),
    )
    gz, sums1, summed = call(
        conv_back_kernel,
        plan,
        "conv_back",
        steps,
        pairs,
        [
            (ANY, (NW, cs, L), BF16),
            (const(2, Ch), (2, Ch), F32),
            (const(2, plan.ns // 2, rb, wide), (2, plan.ns // 2, rb, wide), BF16),
        ],
        [
            pltpu.VMEM((2 * Ch, 3 * C), BF16),
            pltpu.VMEM((L, L), BF16),
            pltpu.VMEM((4, Ch, L), F32),
            pltpu.VMEM((2 * Ch, M), F32),
            pltpu.VMEM((steps, g, wb, cs, L), BF16),
            pltpu.VMEM((2, Ch, L), F32),
            pltpu.SemaphoreType.DMA((steps, g)),
            pltpu.SemaphoreType.DMA((steps, g)),
            pltpu.SemaphoreType.DMA((steps,)),
            pltpu.VMEM(bshape[1:], BF16),
            pltpu.VMEM(bshape[1:], BF16),
            pltpu.VMEM(bshape[1:], BF16),
            pltpu.VMEM(bshape[1:], BF16),
            pltpu.VMEM((g, rb, wide), BF16),
            pltpu.VMEM((g, rb, wide), BF16),
            pltpu.VMEM((2, plan.ns // 2, rb, wide), BF16),
            pltpu.SemaphoreType.DMA((2, 3 + plan.ns + g)),
        ]
        + link_scratch(plan, 2),
        2 * nw * Lp * 6 * C * Ch,
        nw * Lp * C * 12,
        cid=6,
    )(lens, *[a for _, a in pairs])

    pairs = ins(
        (pl.BlockSpec((wb, L, Ch), lambda t: (t, 0, half())), inputs),
        (win(wb, cs, L), gz),
        (half_of(2), stats1),
        (whole(2, Ch), sums1),
        (half_of(1), gain1),
        (win(wb, cs, Lp), result),
        (
            pl.BlockSpec((2, across // 2, rb, wide), lambda t: (0, t * down // (NW // wb), 0, 0)),
            summed,
        ),
        (whole(2, C), sums2),
        (whole(2, H), sums3),
        (whole(1, C), bsum),
    )
    outs = call(
        input_grad_kernel,
        plan,
        "input_grad",
        NW // wb,
        pairs,
        [
            (win(wb, cs, L), (NW, cs, L), BF16),
            (win(wb, cs, Lp), (NW, cs, Lp), BF16),
            (
                pl.BlockSpec((T1, rb, C), lambda t: (0, t * down // (NW // wb), 0)),
                (T1, cs, C),
                F32,
            ),
            (const(T2, hs, C), (T2, hs, C), F32),
            (const(hs, C), (hs, C), F32),
        ]
        + [(const(1, n), (1, n), F32) for n in (cs, cs, cs, cs, hs, hs, cs)],
        [
            pltpu.VMEM((L, L), BF16),
            pltpu.VMEM((3, cs, L), F32),
            pltpu.VMEM((Ch, L), F32),
        ],
        2 * NW * L * L * cs,
        NW * L * cs * 8,
    )(lens, *[a for _, a in pairs])
    grad, result, conv_grad, dil_grad, point_grad = outs[:5]
    g1, b1, g2, b2, g3, b3, pb = [a[0] for a in outs[5:]]
    return (
        jnp.swapaxes(result, 1, 2),
        jnp.swapaxes(grad, 1, 2),
        jnp.swapaxes(conv_grad, 1, 2),
        g1,
        b1,
        g2,
        b2,
        jnp.swapaxes(dil_grad, 1, 2),
        g3,
        b3,
        point_grad,
        pb,
    )


def solution(mesh):
    in_specs = (
        P(None, "seq", None),
        P(),
        P(),
        P(),
        P(),
        P("ch"),
        P("ch"),
        P(None, None, "ch"),
        P("ch"),
        P("ch"),
        P("ch", None),
        P("ch"),
        P(None, "seq", None),
    )
    out_specs = (
        P(None, "seq", "ch"),
        P(None, "seq", "ch"),
        P(None, None, "ch"),
        P("ch"),
        P("ch"),
        P("ch"),
        P("ch"),
        P(None, None, "ch"),
        P("ch"),
        P("ch"),
        P("ch", None),
        P("ch"),
    )
    return jax.shard_map(
        per_device, mesh=mesh, in_specs=in_specs, out_specs=out_specs, check_vma=False
    )
```

```python
from functools import partial
from typing import NamedTuple

import jax
import jax.numpy as jnp
from jax import lax
from jax.experimental import pallas as pl
from jax.experimental.pallas import tpu as pltpu
from jax.sharding import PartitionSpec as P

DIL = 14
EDGE = 16
EPS = 1e-05
GC0 = 0.7978845608028654
GC1 = 0.044715
F32 = jnp.float32
BF16 = jnp.bfloat16
MESH = pl.DeviceIdType.MESH
VMEM_LIMIT = 58 * 1024 * 1024
ANY = pl.BlockSpec(memory_space=pl.ANY)
SMEM = pl.BlockSpec(memory_space=pltpu.SMEM)


class Plan(NamedTuple):
    ns: int
    nz: int
    R: int
    NW: int
    L: int
    C: int
    H: int
    T1: int
    T2: int
    wb: int

    @property
    def g(self):
        return self.nz // self.R

    @property
    def nw(self):
        return self.NW // self.g

    @property
    def Lp(self):
        return self.L // 2

    @property
    def cs(self):
        return self.C // self.nz

    @property
    def Ch(self):
        return self.C // self.R

    @property
    def Hh(self):
        return self.H // self.R

    @property
    def steps(self):
        return self.nw // self.wb

    @property
    def block(self):
        down = 1
        while self.ns % (2 * down) == 0 and (self.cs // 2) % (16 * down) == 0:
            down *= 2
        across = self.ns // down
        wide = -(-(self.T1 * self.C + (self.T2 + 1) * self.C // 2) // (128 * across)) * 128
        return self.cs // down, wide, down, across

    def place(self):
        s, z = lax.axis_index("seq"), lax.axis_index("ch")
        return s, z, lax.rem(z, self.g), lax.div(z, self.g)


def gelu(z):
    t = jnp.tanh(z * (GC0 + (GC0 * GC1) * (z * z)))
    hz = 0.5 * z
    return hz + hz * t


def gelu_both(z):
    sq = z * z
    t = jnp.tanh(z * (GC0 + (GC0 * GC1) * sq))
    hz = 0.5 * z
    slope = 0.5 + 0.5 * t + hz * (1.0 - t * t) * (GC0 + (3.0 * GC0 * GC1) * sq)
    return hz + hz * t, slope


def gelu_slope(z):
    return gelu_both(z)[1]


def rows_of(shape):
    return lax.broadcasted_iota(jnp.int32, shape, 0)


def lanes_of(shape):
    return lax.broadcasted_iota(jnp.int32, shape, 1)


def total_of(lens):
    n = lens[0]
    for k in range(1, lens.shape[0]):
        n = n + lens[k]
    return n.astype(F32)


def norm_of(stats, total):
    mean = stats[0:1] / total
    square = stats[1:2] / total
    return mean, lax.rsqrt(square - mean * mean + EPS)


def column(row, n):
    return jnp.broadcast_to(row, (n, row.shape[1])).T


def mm(a, b):
    return jnp.dot(a, b, preferred_element_type=F32)


def mm_nt(a, b):
    return lax.dot_general(a, b, (((1,), (1,)), ((), ())), preferred_element_type=F32)


def mm_tn(a, b):
    return lax.dot_general(a, b, (((0,), (0,)), ((), ())), preferred_element_type=F32)


def mm_tt(a, b):
    return lax.dot_general(a, b, (((0,), (1,)), ((), ())), preferred_element_type=F32)


def pick_matrix(L):
    r, n = rows_of((L, L)), lanes_of((L, L))
    bin_of = 2 * r - jnp.where(r >= L // 2, L - 1, 0)
    return jnp.where(n == bin_of, 1.0, 0.0).astype(BF16)


class Peers:
    def __init__(self, count, me, device):
        self.count, self.me, self.device = count, me, device

    def other(self, off):
        return lax.rem(self.me + off, self.count)

    def greet(self):
        barrier = pltpu.get_barrier_semaphore()
        for off in range(1, self.count):
            pl.semaphore_signal(
                barrier, inc=1, device_id=self.device(self.other(off)), device_id_type=MESH
            )

    def copy(self, link, slot, off):
        packet, buf, send, recv = link
        return pltpu.make_async_remote_copy(
            src_ref=packet,
            dst_ref=buf.at[slot],
            send_sem=send.at[off],
            recv_sem=recv.at[slot],
            device_id=self.device(self.other(off)),
            device_id_type=MESH,
        )

    def start(self, link):
        for off in range(1, self.count):
            self.copy(link, self.me, off).start()

    def finish(self, link):
        packet, buf = link[:2]
        buf[self.me] = packet[...]
        for off in range(1, self.count):
            self.copy(link, self.other(off), off).wait_recv()
        acc = buf[0]
        for q in range(1, self.count):
            acc = acc + buf[q]
        for off in range(1, self.count):
            self.copy(link, self.me, off).wait_send()
        return acc

    def scratch(self, rows, width):
        return [
            pltpu.VMEM((rows, width), F32),
            pltpu.VMEM((self.count, rows, width), F32),
            pltpu.SemaphoreType.DMA((self.count,)),
            pltpu.SemaphoreType.DMA((self.count,)),
        ]


def group_peers(plan):
    s, z, i, h = plan.place()
    g = plan.g
    return Peers(plan.ns * g, s * g + i, lambda q: (lax.div(q, g), h * g + lax.rem(q, g)))


def plane_peers(plan):
    s, z, i, h = plan.place()
    return Peers(plan.ns, s, lambda q: (q, z))


def line_peers(plan):
    s, z, i, h = plan.place()
    return Peers(plan.nz, z, lambda q: (s, q))


def meet(count):
    pl.semaphore_wait(pltpu.get_barrier_semaphore(), count)


class Halo:
    def __init__(self, plan, edge, low, high, sems, parts):
        self.edge, self.low, self.high, self.sems, self.parts = edge, low, high, sems, parts
        s, z, _, _ = plan.place()
        self.left = (lax.rem(s + plan.ns - 1, plan.ns), z)
        self.right = (lax.rem(s + 1, plan.ns), z)
        self.n = low.shape[0] // parts

    def copies(self, part):
        rows = pl.ds(part * self.n, self.n)
        return [
            pltpu.make_async_remote_copy(
                src_ref=self.edge.at[side, rows],
                dst_ref=dst.at[rows],
                send_sem=self.sems.at[0, side, part],
                recv_sem=self.sems.at[1, side, part],
                device_id=dev,
                device_id_type=MESH,
            )
            for side, (dst, dev) in enumerate(((self.high, self.left), (self.low, self.right)))
        ]

    def start(self, part):
        for c in self.copies(part):
            c.start()

    def finish(self):
        for part in range(self.parts):
            for c in self.copies(part):
                c.wait()


def halo_scratch(parts):
    return [pltpu.SemaphoreType.DMA((2, 2, parts))]


class Gather:
    PARTS = 2

    def __init__(self, plan, sems, stripe, part=None, full=None):
        self.plan, self.part, self.full, self.sems = plan, part, full, sems
        self.stripe = stripe
        self.s, self.z, self.i, self.h = plan.place()
        self.c, self.m = lax.rem(self.s, 2), lax.div(self.s, 2)
        self.chips = plan.ns // 2
        self.every = self.chips // 4
        self.tap = lax.div(self.m, self.every)
        self.owner = lax.rem(self.m, self.every) == 0
        self.rows = plan.H // plan.nz

    def copy(self, src, dst, sem, device):
        return pltpu.make_async_remote_copy(
            src_ref=src,
            dst_ref=dst,
            send_sem=self.sems.at[(0,) + sem],
            recv_sem=self.sems.at[(1,) + sem],
            device_id=device,
            device_id_type=MESH,
        )

    def line(self, off, at):
        to = lax.rem(self.z + off, self.plan.nz)
        return self.copy(self.part, self.stripe.at[at], (off,), (self.s, to))

    def own_rows(self):
        return pltpu.make_async_copy(self.part, self.stripe.at[self.z], self.sems.at[0, 0])

    def line_start(self):
        @pl.when(self.owner)
        def _():
            self.own_rows().start()
            for off in range(1, self.plan.nz):
                self.line(off, self.z).start()

    def line_finish(self):
        @pl.when(self.owner)
        def _():
            self.own_rows().wait()
            for off in range(1, self.plan.nz):
                self.line(off, self.z).wait_send()
                at = lax.rem(self.z + self.plan.nz - off, self.plan.nz)
                self.line(off, at).wait_recv()

    def half(self, ref, n):
        rows = self.plan.nz // self.PARTS
        return ref.at[pl.ds(n * rows, rows)]

    def own_stripe(self):
        return pltpu.make_async_copy(
            self.stripe, self.full.at[self.c, self.tap], self.sems.at[0, 0, 0]
        )

    def chip(self, off, n):
        to = lax.rem(self.m + off, self.chips)
        return self.copy(
            self.half(self.stripe, n),
            self.half(self.full.at[self.c, self.tap], n),
            (off, n),
            (2 * to + self.c, self.z),
        )

    def arrival(self, k, off, n):
        whole = self.half(self.full.at[self.c, k], n)
        return self.copy(whole, whole, (off, n), (2 * k * self.every + self.c, self.z))

    def pair(self, c, n):
        part = self.full.at[c, pl.ds(2 * n, 2)]
        return self.copy(part, part, (self.chips, n), (2 * self.m + 1 - self.c, self.z))

    def chips_start(self):
        @pl.when(self.owner)
        def _():
            self.own_stripe().start()
            for off in range(1, self.chips):
                for n in range(self.PARTS):
                    self.chip(off, n).start()

    def pair_start(self):
        for k in range(4):
            off = lax.rem(self.m - k * self.every + self.chips, self.chips)

            @pl.when(off != 0)
            def _():
                for n in range(self.PARTS):
                    self.arrival(k, off, n).wait_recv()

        @pl.when(self.owner)
        def _():
            self.own_stripe().wait()
            for off in range(1, self.chips):
                for n in range(self.PARTS):
                    self.chip(off, n).wait_send()

        for n in range(self.PARTS):
            self.pair(self.c, n).start()

    def pair_finish(self):
        for n in range(self.PARTS):
            self.pair(self.c, n).wait_send()
            self.pair(1 - self.c, n).wait_recv()


def first_step():
    return pl.program_id(0) == 0


def last_step():
    return pl.program_id(0) == pl.num_programs(0) - 1


def moments_kernel(plan, nw1, wb1, lens, x, xtop, xend, ctop, cend, g2, s2, pb, g3, s3,
                   taps, pw, stats, par, low, high, stripe,
                   acc, edge, part, line_sems, halo_sems, *links):
    t = pl.program_id(0)
    plane, line = plane_peers(plan), line_peers(plan)
    halo = Halo(plan, edge, low, high, halo_sems, 1)
    gather = Gather(plan, line_sems, stripe, part=part)
    s, z, i, h = plan.place()
    L, C, nw, nz = plan.L, plan.C, plan.nw, plan.nz

    @pl.when(first_step())
    def _():
        plane.greet()
        line.greet()
        part[...] = jnp.where(gather.tap == 3, pw[...], taps[0])
        acc[...] = jnp.zeros_like(acc)
        n16 = nw * 16
        for side, (xe, ce, places) in enumerate(
            ((xtop, ctop, (0, 1, 0)), (xend, cend, (14, 15, 15)))
        ):
            for k, at in enumerate(places):
                rows, lanes = rows_of((nw, n16)), lanes_of((nw, n16))
                sel = jnp.where(lanes == 16 * rows + at, 1.0, 0.0).astype(BF16)
                block = (xe if k < 2 else ce)[...].reshape(n16, C)
                edge[side, k] = mm(sel, block)

        meet(plane.count + line.count - 2)
        halo.start(0)
        gather.line_start()

    rows = rows_of((L, C))
    for w in range(wb1):
        valid = 2 * lens[z * nw1 + t * wb1 + w] - s * L
        v = jnp.where(rows < valid, x[w].astype(F32), 0.0)
        v3 = v.reshape(L // 8, 8, C)
        acc[0] += jnp.sum(v3, axis=0)
        acc[1] += jnp.sum(v3 * v3, axis=0)

    @pl.when(last_step())
    def _():
        packet, buf = links[0], links[5]
        packet[0:1] = jnp.sum(acc[0], axis=0, keepdims=True)
        packet[1:2] = jnp.sum(acc[1], axis=0, keepdims=True)
        plane.start(links[:4])
        at = 0
        spans = []
        links[4][2:3] = jnp.zeros((1, C), F32)
        for ref in (g2, s2, pb, g3, s3):
            n = ref.shape[1]
            links[4][2:3, at : at + n] = ref[...]
            spans.append((at, n))
            at += n
        links[4][0:2] = plane.finish(links[:4])
        line.start(links[4:])
        stats[...] = line.finish(links[4:])[0:2]
        par[...] = jnp.zeros_like(par)
        for k in range(nz):
            row = buf[k]
            for r, (at, n) in enumerate(spans):
                par[r : r + 1, k * n : (k + 1) * n] = row[2:3, at : at + n]
        halo.finish()
        gather.line_finish()


def conv_kernel(plan, lens, x, hl, hr, w_ref, stats, gain, shift, stripe,
                X5, x2, low, high, sums, full,
                sel, edge, acc, gather_sems, halo_sems, *link):
    t = pl.program_id(0)
    peers = group_peers(plan)
    halo = Halo(plan, edge, low, high, halo_sems, plan.steps)
    gather = Gather(plan, gather_sems, stripe, full=full)
    s, z, i, h = plan.place()
    L, Lp, C, wb = plan.L, plan.Lp, plan.C, plan.wb

    @pl.when(first_step())
    def _():
        peers.greet()
        acc[...] = jnp.zeros_like(acc)
        shape = (Lp, L)
        for k in range(plan.T1):
            at = lanes_of(shape) - (2 * rows_of(shape) + (k - 2))
            sel[k * Lp : (k + 1) * Lp] = jnp.where((at == 0) | (at == 1), 1.0, 0.0).astype(BF16)

    mean, rho = norm_of(stats[...], 2.0 * total_of(lens))
    scale = gain[...] * rho
    offset = shift[...] - mean * scale
    rows = rows_of((L, C))
    row1 = rows_of((1, C))
    row16 = rows_of((16, C))

    for w in range(wb):
        at = t * wb + w
        valid = 2 * lens[i * plan.nw + at] - s * L
        a = gelu(x[w].astype(F32) * scale + offset)
        a = jnp.where(rows < valid, a, 0.0).astype(BF16)
        picked = mm(sel[...], a)
        for k in range(5):
            X5[w * Lp : (w + 1) * Lp, k * C : (k + 1) * C] = picked[
                k * Lp : (k + 1) * Lp
            ].astype(BF16)

        def beside(ref, k, bin_at):
            a = gelu(ref[k, pl.ds(at, 1), :] * scale + offset)
            here = (row1 + bin_at < valid) & (row1 + (s * L + bin_at) >= 0)
            return jnp.where(here, a, 0.0).astype(BF16).astype(F32)

        l0, l1 = beside(hl, 0, -2), beside(hl, 1, -1)
        r0, r1 = beside(hr, 0, L), beside(hr, 1, L + 1)
        top, end = w * Lp, (w + 1) * Lp
        for k, add in ((0, l0 + l1), (1, l1)):
            X5[top : top + 16, k * C : (k + 1) * C] = (
                picked[k * Lp : k * Lp + 16] + jnp.where(row16 == 0, add, 0.0)
            ).astype(BF16)
        for k, add in ((3, r0), (4, r0 + r1)):
            X5[end - 16 : end, k * C : (k + 1) * C] = (
                picked[(k + 1) * Lp - 16 : (k + 1) * Lp] + jnp.where(row16 == 15, add, 0.0)
            ).astype(BF16)

    nc = 256
    rowp = rows_of((Lp, nc))
    for n in range(C // nc):
        cols = slice(n * nc, (n + 1) * nc)
        y = 0.5 * mm(X5[...], w_ref[:, cols])
        s0 = jnp.zeros((1, nc), F32)
        s1 = jnp.zeros((1, nc), F32)
        for w in range(wb):
            at = t * wb + w
            valid = lens[i * plan.nw + at] - s * Lp
            v = y[w * Lp : (w + 1) * Lp]
            x2[w, :, cols] = v
            edge[0, at, :, cols] = v[:EDGE].astype(BF16)
            edge[1, at, :, cols] = v[Lp - EDGE :].astype(BF16)
            v = jnp.where(rowp < valid, v, 0.0)
            s0 = s0 + jnp.sum(v, axis=0, keepdims=True)
            s1 = s1 + jnp.sum(v * v, axis=0, keepdims=True)
        acc[0:1, cols] += s0
        acc[1:2, cols] += s1

    @pl.when(first_step())
    def _():
        meet(peers.count - 1)
        gather.chips_start()

    halo.start(t)

    @pl.when(t == max(plan.steps - 2, 0))
    def _():
        gather.pair_start()

    @pl.when(last_step())
    def _():
        link[0][...] = acc[...]
        peers.start(link)
        sums[...] = peers.finish(link)
        halo.finish()
        gather.pair_finish()


def dilated_kernel(plan, lens, x2, lo, hi, w_ref, stats, par,
                   Y3, c2, low, high, sums, ext, wf, edge, acc, halo_sems, *link):
    t = pl.program_id(0)
    peers = group_peers(plan)
    halo = Halo(plan, edge, low, high, halo_sems, plan.steps)
    s, z, i, h = plan.place()
    Lp, C, H, wb = plan.Lp, plan.C, plan.H, plan.wb

    @pl.when(first_step())
    def _():
        peers.greet()
        acc[...] = jnp.zeros_like(acc)
        for k in range(plan.T2):
            for c in range(2):
                at = k * C + c * (C // 2)
                wf[:, at : at + C // 2] = w_ref[c, k]

    mean, rho = norm_of(stats[...], total_of(lens))
    scale = par[0:1] * rho
    offset = par[1:2] - mean * scale
    rows = rows_of((Lp, C))
    rowe = rows_of((EDGE, C))

    for w in range(wb):
        valid = lens[i * plan.nw + t * wb + w] - s * Lp
        a = jnp.where(rows < valid, gelu(x2[w] * scale + offset), 0.0)
        al = gelu(lo[w].astype(F32) * scale + offset)
        al = jnp.where((rowe - EDGE < valid) & (s > 0), al, 0.0)
        ah = gelu(hi[w].astype(F32) * scale + offset)
        ah = jnp.where(rowe + Lp < valid, ah, 0.0)
        ext[0:EDGE] = al
        ext[EDGE : EDGE + Lp] = a
        ext[EDGE + Lp :] = ah
        top, end = w * Lp, (w + 1) * Lp
        Y3[top:end, 0:C] = ext[EDGE - DIL : EDGE - DIL + Lp].astype(BF16)
        Y3[top:end, C : 2 * C] = a.astype(BF16)
        Y3[top:end, 2 * C : 3 * C] = ext[EDGE + DIL : EDGE + DIL + Lp].astype(BF16)

    y = mm_nt(Y3[...], wf[...])
    rowh = rows_of((Lp, H))
    s0 = jnp.zeros((1, H), F32)
    s1 = jnp.zeros((1, H), F32)
    for w in range(wb):
        at = t * wb + w
        valid = lens[i * plan.nw + at] - s * Lp
        v = y[w * Lp : (w + 1) * Lp]
        c2[w] = v
        edge[0, at] = v[:EDGE].astype(BF16)
        edge[1, at] = v[Lp - EDGE :].astype(BF16)
        v = jnp.where(rowh < valid, v, 0.0)
        s0 = s0 + jnp.sum(v, axis=0, keepdims=True)
        s1 = s1 + jnp.sum(v * v, axis=0, keepdims=True)
    acc[0:1, 0:H] += s0
    acc[1:2, 0:H] += s1

    @pl.when(first_step())
    def _():
        meet(peers.count - 1)

    halo.start(t)

    @pl.when(last_step())
    def _():
        link[0][...] = acc[...]
        peers.start(link)
        sums[...] = peers.finish(link)[:, 0:H]
        halo.finish()


def point_kernel(plan, lens, c2, x2, cot, w_ref, pb, stats, par,
                 res, dz, pgrad, low, high, sums, bsum,
                 pw, a3s, dos, pacc, edge, acc, halo_sems, *link):
    t = pl.program_id(0)
    peers = group_peers(plan)
    halo = Halo(plan, edge, low, high, halo_sems, plan.steps)
    s, z, i, h = plan.place()
    Lp, C, H, wb, cs = plan.Lp, plan.C, plan.H, plan.wb, plan.cs

    @pl.when(first_step())
    def _():
        peers.greet()
        acc[...] = jnp.zeros_like(acc)
        pacc[...] = jnp.zeros_like(pacc)
        for c in range(2):
            pw[:, c * (C // 2) : (c + 1) * (C // 2)] = w_ref[c, 0]

    mean, rho = norm_of(stats[...], total_of(lens))
    scale = par[3:4, 0:H] * rho
    offset = par[4:5, 0:H] - mean * scale
    rowc = rows_of((Lp, C))
    rowh = rows_of((Lp, H))

    s0 = jnp.zeros((1, H), F32)
    s1 = jnp.zeros((1, H), F32)
    sb = jnp.zeros((1, C), F32)
    for w in range(wb):
        at = t * wb + w
        valid = lens[i * plan.nw + at] - s * Lp
        top, end = w * Lp, (w + 1) * Lp
        d = jnp.where(rowc < valid, cot[w].astype(F32), 0.0)
        sb = sb + jnp.sum(d, axis=0, keepdims=True)
        d = d.astype(BF16)
        dos[top:end] = d
        v = c2[w]
        act, slope = gelu_both(v * scale + offset)
        a3s[top:end] = jnp.where(rowh < valid, act, 0.0).astype(BF16)
        dzw = mm_nt(d, pw[...]) * slope
        dz[w] = dzw
        edge[0, at] = dzw[:EDGE].astype(BF16)
        edge[1, at] = dzw[Lp - EDGE :].astype(BF16)
        hat = (v - mean) * rho
        s0 = s0 + jnp.sum(dzw, axis=0, keepdims=True)
        s1 = s1 + jnp.sum(dzw * hat, axis=0, keepdims=True)
    acc[0:1, 0:H] += s0
    acc[0:1, H : 2 * H] += s1
    acc[1:2] += sb

    @pl.when(first_step())
    def _():
        meet(peers.count - 1)

    halo.start(t)

    @pl.when(last_step())
    def _():
        link[0][...] = acc[...]
        peers.start(link)

    y = mm(a3s[...], w_ref[h, 0])
    rowr = rows_of((Lp, y.shape[1]))
    for w in range(wb):
        valid = lens[i * plan.nw + t * wb + w] - s * Lp
        r = x2[w] + y[w * Lp : (w + 1) * Lp] + pb[2:3]
        r = jnp.where(rowr < valid, r, 0.0).T.astype(BF16)
        for k in range(plan.g):
            res[k, w] = r[k * cs : (k + 1) * cs]
    pacc[...] += mm_tn(a3s[...], dos[...])

    @pl.when(last_step())
    def _():
        rows = pl.ds(pl.multiple_of(h * plan.Hh, 16), plan.Hh)
        pgrad[...] = pacc[rows].astype(BF16)
        got = peers.finish(link)
        sums[0:1] = got[0:1, 0:H]
        sums[1:2] = got[0:1, H : 2 * H]
        bsum[...] = got[1:2]
        halo.finish()


def dilated_back_kernel(plan, lens, c2, clo, chi, dz3, zlo, zhi, x2, Y3, w_ref,
                        stats3, sums3, stats2, par, pgrad,
                        dz2, grads, low, high, sums,
                        ext, Z3, wt, wacc, edge, acc, halo_sems, *link):
    t = pl.program_id(0)
    peers = group_peers(plan)
    halo = Halo(plan, edge, low, high, halo_sems, 1)
    s, z, i, h = plan.place()
    Lp, C, H, wb, nw = plan.Lp, plan.C, plan.H, plan.wb, plan.nw

    @pl.when(first_step())
    def _():
        peers.greet()
        acc[...] = jnp.zeros_like(acc)
        wacc[...] = jnp.zeros_like(wacc)
        for k in range(plan.T2):
            for c in range(2):
                cols = slice(c * (C // 2), (c + 1) * (C // 2))
                wt[k * H : (k + 1) * H, cols] = w_ref[c, k]

    total = total_of(lens)
    mean3, rho3 = norm_of(stats3[...], total)
    gr3 = par[3:4, 0:H] * rho3
    sg3 = sums3[0:1] / total
    gg3 = sums3[1:2] / total
    mean2, rho2 = norm_of(stats2[...], total)
    scale2 = par[0:1] * rho2
    offset2 = par[1:2] - mean2 * scale2
    rowh = rows_of((Lp, H))
    rowe = rows_of((EDGE, H))
    rowc = rows_of((Lp, C))

    def back(dz, v):
        return gr3 * (dz - (sg3 + (v - mean3) * rho3 * gg3))

    for w in range(wb):
        valid = lens[i * nw + t * wb + w] - s * Lp
        d = jnp.where(rowh < valid, back(dz3[w], c2[w]), 0.0)
        dl = back(zlo[w].astype(F32), clo[w].astype(F32))
        dl = jnp.where((rowe - EDGE < valid) & (s > 0), dl, 0.0)
        dh = back(zhi[w].astype(F32), chi[w].astype(F32))
        dh = jnp.where(rowe + Lp < valid, dh, 0.0)
        ext[0:EDGE] = dl
        ext[EDGE : EDGE + Lp] = d
        ext[EDGE + Lp :] = dh
        top, end = w * Lp, (w + 1) * Lp
        Z3[top:end, 0:H] = ext[EDGE + DIL : EDGE + DIL + Lp].astype(BF16)
        Z3[top:end, H : 2 * H] = d.astype(BF16)
        Z3[top:end, 2 * H : 3 * H] = ext[EDGE - DIL : EDGE - DIL + Lp].astype(BF16)

    y = mm(Z3[...], wt[...])

    s0 = jnp.zeros((1, C), F32)
    s1 = jnp.zeros((1, C), F32)
    for w in range(wb):
        at = t * wb + w
        valid = lens[i * nw + at] - s * Lp
        v = x2[w]
        dzw = y[w * Lp : (w + 1) * Lp] * gelu_slope(v * scale2 + offset2)
        dzw = jnp.where(rowc < valid, dzw, 0.0)
        dz2[w] = dzw
        edge[0, pl.ds(at, 1)] = dzw[0:1]
        edge[1, pl.ds(at, 1)] = dzw[Lp - 1 : Lp]
        s0 = s0 + jnp.sum(dzw, axis=0, keepdims=True)
        s1 = s1 + jnp.sum(dzw * ((v - mean2) * rho2), axis=0, keepdims=True)
    acc[0:1] += s0
    acc[1:2] += s1

    @pl.when(last_step())
    def _():
        link[0][...] = acc[...]
        meet(peers.count - 1)
        peers.start(link)
        halo.start(0)

    wacc[...] += mm_tn(Z3[:, H : 2 * H], Y3[...])

    @pl.when(last_step())
    def _():
        rows = pl.ds(pl.multiple_of(h * plan.Hh, 16), plan.Hh)
        grads[:, 0 : plan.T2 * C] = wacc[rows].astype(BF16)
        grads[:, plan.T2 * C :] = pgrad[...]
        sums[...] = peers.finish(link)
        halo.finish()


def conv_grad_kernel(plan, lens, dz2, zlo, zhi, x2, lo, hi, cot, hl, hr, X5,
                     stats2, sums2, par, grads, res, D3, blocks, result,
                     ext, acc, bulk_send, bulk_recv, own_sem):
    t = pl.program_id(0)
    s, z, i, h = plan.place()
    Lp, C, wb, Ch, cs = plan.Lp, plan.C, plan.wb, plan.Ch, plan.cs

    g, nw = plan.g, plan.nw

    def own_copy():
        return pltpu.make_async_copy(res.at[i], result.at[pl.ds(i * nw, nw)], own_sem)

    def bulk(off, sender, n):
        to = lax.rem(i + off, g)
        return pltpu.make_async_remote_copy(
            src_ref=res.at[to, pl.ds(n * wb, wb)],
            dst_ref=result.at[pl.ds(sender * nw + n * wb, wb)],
            send_sem=bulk_send.at[off, n],
            recv_sem=bulk_recv.at[off, n],
            device_id=(s, h * g + to),
            device_id_type=MESH,
        )

    @pl.when(first_step())
    def _():
        acc[...] = jnp.zeros_like(acc)
        barrier = pltpu.get_barrier_semaphore()
        for off in range(1, g):
            pl.semaphore_signal(
                barrier,
                inc=1,
                device_id=(s, h * g + lax.rem(i + off, g)),
                device_id_type=MESH,
            )
        own_copy().start()

    total = total_of(lens)
    mean, rho = norm_of(stats2[...], total)
    gr = par[0:1] * rho
    sg = sums2[0:1] / total
    gg = sums2[1:2] / total
    rowc = rows_of((Lp, C))
    row1 = rows_of((1, C))

    def back(dout, dz, v):
        return 0.5 * (dout + gr * (dz - (sg + (v - mean) * rho * gg)))

    for w in range(wb):
        at = t * wb + w
        valid = lens[i * plan.nw + at] - s * Lp
        d = back(cot[w].astype(F32), dz2[w], x2[w])
        d = jnp.where(rowc < valid, d, 0.0)
        dl = back(hl[2, pl.ds(at, 1), :], zlo[pl.ds(at, 1), :], lo[w, EDGE - 1 : EDGE].astype(F32))
        dl = jnp.where((row1 - 1 < valid) & (s > 0), dl, 0.0)
        dh = back(hr[2, pl.ds(at, 1), :], zhi[pl.ds(at, 1), :], hi[w, 0:1].astype(F32))
        dh = jnp.where(row1 + Lp < valid, dh, 0.0)
        ext[7:8] = dl
        ext[8 : 8 + Lp] = d
        ext[8 + Lp : 9 + Lp] = dh
        top, end = w * Lp, (w + 1) * Lp
        D3[top:end, 0:C] = ext[9 : 9 + Lp].astype(BF16)
        D3[top:end, C : 2 * C] = d.astype(BF16)
        D3[top:end, 2 * C : 3 * C] = ext[7 : 7 + Lp].astype(BF16)

    @pl.when(first_step())
    def _():
        pl.semaphore_wait(pltpu.get_barrier_semaphore(), g - 1)
        for off in range(1, g):
            for n in range(plan.steps):
                bulk(off, i, n).start()

    dh = D3[:, pl.ds(pl.multiple_of(C + h * Ch, 128), Ch)]
    acc[...] += mm_tn(dh, X5[...])

    @pl.when(last_step())
    def _():
        rb, wide, down, across = plan.block
        n1, n2 = plan.T1 * C, (plan.T2 + 1) * C // 2
        hs = plan.H // plan.nz
        for k in range(plan.g):
            for q in range(plan.ns):
                r, c = q // across * rb, q % across * wide
                dst = blocks.at[q % 2, q // 2, k]
                a, b = min(c, n1), min(c + wide, n1)
                if b > a:
                    dst[:, 0 : b - a] = acc[k * cs + r : k * cs + r + rb, a:b].astype(BF16)
                a, b = max(c, n1) - n1, min(c + wide, n1 + n2) - n1
                if b > a:
                    side, r2 = r // hs, r % hs
                    dst[:, a + n1 - c : b + n1 - c] = grads[
                        k * hs + r2 : k * hs + r2 + rb, side * n2 + a : side * n2 + b
                    ]
        own_copy().wait()
        for off in range(1, g):
            for n in range(plan.steps):
                bulk(off, i, n).wait_send()
                bulk(off, lax.rem(i + g - off, g), n).wait_recv()


class Reduction:
    def __init__(self, plan, blocks, out, mine, got, mid, spread, half, mate, sems):
        self.plan = plan
        self.blocks, self.out = blocks, out
        self.mine, self.got, self.mid, self.spread = mine, got, mid, spread
        self.half, self.mate = half, mate
        self.sems = sems
        self.s, self.z, self.i, self.h = plan.place()
        self.c = lax.rem(self.s, 2)
        self.m = lax.div(self.s, 2)
        self.chips = plan.ns // 2

    def copy(self, src, dst, sem, device):
        return pltpu.make_async_remote_copy(
            src_ref=src,
            dst_ref=dst,
            send_sem=self.sems.at[(0,) + sem],
            recv_sem=self.sems.at[(1,) + sem],
            device_id=device,
            device_id_type=MESH,
        )

    def pair(self):
        return (2 * self.m + (1 - self.c), self.z)

    def chip(self, off):
        return lax.rem(self.m + off, self.chips)

    def member(self, off):
        return lax.rem(self.i + off, self.plan.g)

    def own0(self):
        return pltpu.make_async_copy(self.blocks.at[self.c], self.mine, self.sems.at[0, 0, 0])

    def phase0(self, n):
        return self.copy(self.blocks.at[1 - self.c, n], self.got.at[n], (1, n), self.pair())

    def phase1(self, off, at, n):
        to = self.chip(off)
        return self.copy(
            self.mid.at[to, n], self.spread.at[at, n], (2 + off, n), (2 * to + self.c, self.z)
        )

    def phase2(self, off):
        to = self.member(off)
        sem = (2 + self.chips + off, 0)
        return self.copy(
            self.half.at[to], self.mate.at[off], sem, (self.s, self.h * self.plan.g + to)
        )

    def phase3(self, off, at):
        to = self.chip(off)
        sem = (2 + self.chips + self.plan.g + off, 0)
        return self.copy(
            self.out.at[self.c, self.m], self.out.at[self.c, at], sem, (2 * to + self.c, self.z)
        )

    def phase4(self, c, n):
        sem = (2 + 2 * self.chips + self.plan.g, n)
        return self.copy(self.out.at[c, n], self.out.at[c, n], sem, self.pair())

    def step0(self):
        self.own0().start()
        for n in range(self.chips):
            self.phase0(n).start()

    def step1(self):
        self.own0().wait()
        for n in range(self.chips):
            self.phase0(n).wait()

        @pl.loop(0, self.chips)
        def _(n):
            self.mid[n] = (self.mine[n].astype(F32) + self.got[n].astype(F32)).astype(BF16)

        for off in range(1, self.chips):
            for n in range(self.plan.g):
                self.phase1(off, self.m, n).start()

    def step2(self):
        for off in range(1, self.chips):
            for n in range(self.plan.g):
                self.phase1(off, self.m, n).wait_send()
                self.phase1(off, self.chip(self.chips - off), n).wait_recv()
        self.spread[self.m] = self.mid[self.m]

        @pl.loop(0, self.plan.g)
        def _(n):
            v = self.spread[0, n].astype(F32)
            for k in range(1, self.chips):
                v = v + self.spread[k, n].astype(F32)
            self.half[n] = v.astype(BF16)

        for off in range(1, self.plan.g):
            self.phase2(off).start()

    def step3(self):
        for off in range(1, self.plan.g):
            self.phase2(off).wait()
        v = self.half[self.i].astype(F32)
        for off in range(1, self.plan.g):
            v = v + self.mate[off].astype(F32)
        self.out[self.c, self.m] = v.astype(BF16)
        for off in range(1, self.chips):
            self.phase3(off, self.m).start()

    def step4(self):
        for off in range(1, self.chips):
            self.phase3(off, self.m).wait_send()
            self.phase3(off, self.chip(self.chips - off)).wait_recv()
        for n in range(self.chips):
            self.phase4(self.c, n).start()

    def step5(self):
        for n in range(self.chips):
            self.phase4(self.c, n).wait_send()
            self.phase4(1 - self.c, n).wait_recv()


def conv_back_kernel(plan, lens, D3, x, taps, stats, gain, shift, blocks,
                     gz, sums, summed, wcat, pick, cols, y, part, acc,
                     bulk_send, bulk_recv, own_sem,
                     mine, got, mid, spread, half, mate, out, red_sems, *link):
    t = pl.program_id(0)
    peers = group_peers(plan)
    s, z, i, h = plan.place()
    L, Lp, C, wb, g, nw = plan.L, plan.Lp, plan.C, plan.wb, plan.g, plan.nw
    Ch, cs = plan.Ch, plan.cs
    steps = plan.steps
    red = Reduction(plan, blocks, out, mine, got, mid, spread, half, mate, red_sems)

    def own_copy(step):
        return pltpu.make_async_copy(
            part.at[step, i], gz.at[pl.ds(i * nw + step * wb, wb)], own_sem.at[step]
        )

    def bulk(step, off, sender):
        to = lax.rem(i + off, g)
        return pltpu.make_async_remote_copy(
            src_ref=part.at[step, to],
            dst_ref=gz.at[pl.ds(sender * nw + step * wb, wb)],
            send_sem=bulk_send.at[step, off],
            recv_sem=bulk_recv.at[step, off],
            device_id=(s, h * g + to),
            device_id_type=MESH,
        )

    @pl.when(first_step())
    def _():
        peers.greet()
        acc[...] = jnp.zeros_like(acc)
        pick[...] = pick_matrix(L)
        mean, rho = norm_of(stats[...], 2.0 * total_of(lens))
        scale = gain[...] * rho
        for k, row in enumerate((scale, shift[...] - mean * scale, rho, -mean * rho)):
            cols[k] = column(row, L)
        w = [taps[k].astype(F32) for k in range(5)]
        for r, parts in enumerate(
            ((w[0], w[1] + w[2], w[3] + w[4]), (w[0] + w[1], w[2] + w[3], w[4]))
        ):
            for k, v in enumerate(parts):
                wcat[r * Ch : (r + 1) * Ch, k * C : (k + 1) * C] = v.astype(BF16)

    y[...] = mm_nt(wcat[...], D3[...])
    lanes = lanes_of((Ch, L))
    bins = 2 * lanes - jnp.where(lanes >= Lp, L - 1, 0)
    for w in range(wb):
        valid = 2 * lens[i * nw + t * wb + w] - s * L
        top, end = w * Lp, (w + 1) * Lp
        v = mm_tt(x[w], pick[...])
        da = jnp.concatenate([y[0:Ch, top:end], y[Ch:, top:end]], axis=1)
        dzw = da * gelu_slope(v * cols[0] + cols[1])
        dzw = jnp.where(bins < valid, dzw, 0.0)
        acc[0] += dzw
        acc[1] += dzw * (v * cols[2] + cols[3])
        dzw = dzw.astype(BF16)
        for k in range(g):
            part[t, k, w] = dzw[k * cs : (k + 1) * cs]

    @pl.when(first_step())
    def _():
        meet(peers.count - 1)
        red.step0()

    own_copy(t).start()

    @pl.when(t == min(1, steps - 1))
    def _():
        red.step1()

    @pl.when(last_step())
    def _():
        red.step2()

    for off in range(1, g):
        bulk(t, off, i).start()

    @pl.when(last_step())
    def _():
        packet = link[0]
        packet[...] = jnp.zeros_like(packet)
        packet[0:1, 0:Ch] = jnp.sum(acc[0].T, axis=0, keepdims=True)
        packet[1:2, 0:Ch] = jnp.sum(acc[1].T, axis=0, keepdims=True)
        peers.start(link)
        red.step3()
        sums[...] = peers.finish(link)[:, 0:Ch]
        red.step4()
        red.step5()
        summed[...] = out[...]
        for step in range(steps):
            own_copy(step).wait()
            for off in range(1, g):
                bulk(step, off, i).wait_send()
                bulk(step, off, lax.rem(i + g - off, g)).wait_recv()


def input_grad_kernel(plan, lens, x, gz, stats, sums, gain, result, summed, sums2, sums3, bsum,
                      out, out_result, conv_grad, dil_grad, point_grad,
                      g1, b1, g2, b2, g3, b3, pb, pick, cols, xt):
    t = pl.program_id(0)
    s, z, i, h = plan.place()
    L, Ch, cs, wb = plan.L, plan.Ch, plan.cs, plan.wb
    mine = pl.ds(pl.multiple_of(i * cs, 16), cs)

    @pl.when(first_step())
    def _():
        n = 2.0 * total_of(lens)
        mean, rho = norm_of(stats[...], n)
        gr = gain[...] * rho
        gg = sums[1:2] / n * rho
        for k, row in enumerate((gr, -gr * gg, gr * (mean * gg - sums[0:1] / n))):
            xt[...] = column(row, L)
            cols[k] = xt[mine]
        pick[...] = pick_matrix(L)

        def mine_of(src, at, which, count, *dsts):
            n = dsts[0].shape[1]
            for k in range(count):

                @pl.when(which == k)
                def _():
                    for dst, r in zip(dsts, at):
                        dst[...] = src[r : r + 1, k * n : (k + 1) * n]

        mine_of(sums, (1, 0), i, plan.g, g1, b1)
        mine_of(sums2, (1, 0), z, plan.nz, g2, b2)
        mine_of(sums3, (1, 0), z, plan.nz, g3, b3)
        mine_of(bsum, (0,), z, plan.nz, pb)

    out_result[...] = result[...]
    rb, wide, down, across = plan.block
    every = (plan.NW // wb) // down
    C, n1, hs = plan.C, plan.T1 * plan.C, plan.H // plan.nz

    def spread(r):
        for c in range(across):
            piece = summed[c % 2, c // 2].astype(F32)
            lo, hi = c * wide, (c + 1) * wide
            for k in range(plan.T1):
                a, b = max(lo, k * C), min(hi, (k + 1) * C)
                if b > a:
                    conv_grad[k, :, a - k * C : b - k * C] = piece[:, a - lo : b - lo]
            side, r2 = r * rb // hs, r * rb % hs
            for k in range(2):
                n0 = n1 + k * C
                a, b = max(lo, n0), min(hi, n0 + C)
                if b > a:
                    v = piece[:, a - lo : b - lo]
                    if 2 * side + k < plan.T2:
                        dil_grad[2 * side + k, r2 : r2 + rb, a - n0 : b - n0] = v
                    else:
                        point_grad[r2 : r2 + rb, a - n0 : b - n0] = v

    for r in range(down):
        pl.when(t == r * every)(partial(spread, r))

    lanes = lanes_of((cs, L))
    for w in range(wb):
        valid = 2 * lens[t * wb + w] - s * L
        xt[...] = x[w].astype(F32).T
        v = xt[mine]
        dz = mm(gz[w], pick[...])
        r = cols[0] * dz + v * cols[1] + cols[2]
        out[w] = jnp.where(lanes < valid, r, 0.0).astype(BF16)


def call(kernel, plan, name, steps, ins, outs, scratch, flops, nbytes, cid=None):
    extra = {} if cid is None else dict(collective_id=cid, has_side_effects=True)
    return pl.pallas_call(
        partial(kernel, plan),
        grid=(steps,),
        in_specs=[SMEM] + [spec for spec, _ in ins],
        out_specs=[spec for spec, _, _ in outs],
        out_shape=[jax.ShapeDtypeStruct(shape, dtype) for _, shape, dtype in outs],
        scratch_shapes=scratch,
        compiler_params=pltpu.CompilerParams(vmem_limit_bytes=VMEM_LIMIT, **extra),
        cost_estimate=pl.CostEstimate(
            flops=int(flops), bytes_accessed=int(nbytes), transcendentals=0
        ),
        name=name,
    )


def per_device(
    inputs,
    lengths,
    input_gain,
    input_shift,
    conv_weight,
    branch_gain,
    branch_shift,
    dilated_tap_weight,
    mixer_gain,
    mixer_shift,
    point_weight,
    point_bias,
    cotangent,
):
    NW, L, C = inputs.shape
    Lp = L // 2
    nz = lax.axis_size("ch")
    R = 2
    plan = Plan(
        ns=lax.axis_size("seq"),
        nz=nz,
        R=R,
        NW=NW,
        L=L,
        C=C,
        H=mixer_gain.shape[0] * nz,
        T1=conv_weight.shape[0],
        T2=dilated_tap_weight.shape[0],
        wb=min(NW * R // nz, max(1, 512 // Lp)),
    )
    g, nw, cs, Ch, H, Hh, wb = plan.g, plan.nw, plan.cs, plan.Ch, plan.H, plan.Hh, plan.wb
    T1, T2, steps = plan.T1, plan.T2, plan.steps
    M = wb * Lp
    hs = H // nz
    lens = lengths.astype(jnp.int32)
    gain1 = input_gain.reshape(1, C)
    shift1 = input_shift.reshape(1, C)

    def row(a):
        return a.reshape(1, a.shape[0])

    def grp():
        return lax.rem(lax.axis_index("ch"), g)

    def half():
        return lax.div(lax.axis_index("ch"), g)

    def core():
        return lax.rem(lax.axis_index("seq"), 2)

    def chip4():
        return lax.div(lax.axis_index("seq"), plan.ns // 4)

    def whole(*shape):
        return pl.BlockSpec(shape, lambda t: (0,) * len(shape), pipeline_mode=pl.Buffered(1))

    def const(*shape):
        return pl.BlockSpec(shape, lambda t: (0,) * len(shape))

    def win(*shape):
        return pl.BlockSpec(shape, lambda t: (t,) + (0,) * (len(shape) - 1))

    def arg_win(n, width):
        return pl.BlockSpec((wb, n, width), lambda t: (grp() * steps + t, 0, 0))

    def ins(*pairs):
        return [p for p in pairs]

    nw1 = NW // nz
    wb1 = min(nw1, wb)

    def edge_spec(n):
        return pl.BlockSpec(
            (nw, 16, C), lambda t: (grp(), n, 0), pipeline_mode=pl.Buffered(1)
        )

    pairs = ins(
        (
            pl.BlockSpec((wb1, L, C), lambda t: (lax.axis_index("ch") * (nw1 // wb1) + t, 0, 0)),
            inputs,
        ),
        (edge_spec(0), inputs),
        (edge_spec(L // 16 - 1), inputs),
        (edge_spec(0), cotangent),
        (edge_spec(Lp // 16 - 1), cotangent),
        (whole(1, cs), row(branch_gain)),
        (whole(1, cs), row(branch_shift)),
        (whole(1, cs), row(point_bias)),
        (whole(1, H // nz), row(mixer_gain)),
        (whole(1, H // nz), row(mixer_shift)),
        (
            pl.BlockSpec((1, hs, C // 2), lambda t: (jnp.minimum(chip4(), T2 - 1), 0, core())),
            jnp.swapaxes(dilated_tap_weight, 1, 2),
        ),
        (pl.BlockSpec((hs, C // 2), lambda t: (0, core())), point_weight),
    )
    plane, line, group = plane_peers(plan), line_peers(plan), group_peers(plan)
    stats1, par, hl, hr, stripe = call(
        lambda plan, *refs: moments_kernel(plan, nw1, wb1, *refs),
        plan,
        "moments",
        nw1 // wb1,
        pairs,
        [
            (const(2, C), (2, C), F32),
            (const(8, C), (8, C), F32),
            (ANY, (3, nw, C), F32),
            (ANY, (3, nw, C), F32),
            (ANY, (nz, hs, C // 2), BF16),
        ],
        [
            pltpu.VMEM((2, 8, C), F32),
            pltpu.VMEM((2, 3, nw, C), F32),
            pltpu.VMEM((hs, C // 2), BF16),
            pltpu.SemaphoreType.DMA((2, nz)),
        ]
        + halo_scratch(1)
        + plane.scratch(2, C)
        + line.scratch(3, C),
        0,
        nw1 * L * C * 2,
        cid=1,
    )(lens, *[a for _, a in pairs])

    pairs = ins(
        (arg_win(L, C), inputs),
        (whole(3, nw, C), hl),
        (whole(3, nw, C), hr),
        (whole(T1 * C, C), conv_weight.reshape(T1 * C, C)),
        (whole(2, C), stats1),
        (whole(1, C), gain1),
        (whole(1, C), shift1),
        (ANY, stripe),
    )
    X5, x2, lo2, hi2, stats2, full = call(
        conv_kernel,
        plan,
        "conv",
        steps,
        pairs,
        [
            (win(M, T1 * C), (nw * Lp, T1 * C), BF16),
            (win(wb, Lp, C), (nw, Lp, C), F32),
            (ANY, (nw, EDGE, C), BF16),
            (ANY, (nw, EDGE, C), BF16),
            (const(2, C), (2, C), F32),
            (ANY, (2, T2 + 1, nz, hs, C // 2), BF16),
        ],
        [
            pltpu.VMEM((T1 * Lp, L), BF16),
            pltpu.VMEM((2, nw, EDGE, C), BF16),
            pltpu.VMEM((2, C), F32),
            pltpu.SemaphoreType.DMA((2, plan.ns // 2 + 1, Gather.PARTS)),
        ]
        + halo_scratch(steps)
        + group.scratch(2, C),
        2 * nw * Lp * T1 * C * C,
        nw * Lp * C * 20,
        cid=2,
    )(lens, *[a for _, a in pairs])

    full = full.reshape(2, T2 + 1, H, C // 2)
    taps_spec = whole(2, T2, H, C // 2)
    pw_spec = pl.BlockSpec(
        (2, 1, H, C // 2), lambda t: (0, T2, 0, 0), pipeline_mode=pl.Buffered(1)
    )

    pairs = ins(
        (win(wb, Lp, C), x2),
        (win(wb, EDGE, C), lo2),
        (win(wb, EDGE, C), hi2),
        (taps_spec, full),
        (whole(2, C), stats2),
        (whole(8, C), par),
    )
    Y3, c2, lo3, hi3, stats3 = call(
        dilated_kernel,
        plan,
        "dilated",
        steps,
        pairs,
        [
            (win(M, T2 * C), (nw * Lp, T2 * C), BF16),
            (win(wb, Lp, H), (nw, Lp, H), F32),
            (ANY, (nw, EDGE, H), BF16),
            (ANY, (nw, EDGE, H), BF16),
            (const(2, H), (2, H), F32),
        ],
        [
            pltpu.VMEM((Lp + 2 * EDGE, C), F32),
            pltpu.VMEM((H, T2 * C), BF16),
            pltpu.VMEM((2, nw, EDGE, H), BF16),
            pltpu.VMEM((2, C), F32),
        ]
        + halo_scratch(steps)
        + group.scratch(2, C),
        2 * nw * Lp * T2 * C * H,
        nw * Lp * C * 12,
        cid=3,
    )(lens, *[a for _, a in pairs])

    pairs = ins(
        (win(wb, Lp, H), c2),
        (pl.BlockSpec((wb, Lp, Ch), lambda t: (t, 0, half())), x2),
        (arg_win(Lp, C), cotangent),
        (pw_spec, full),
        (pl.BlockSpec((8, Ch), lambda t: (0, half()), pipeline_mode=pl.Buffered(1)), par),
        (whole(2, H), stats3),
        (whole(8, C), par),
    )
    res, dz3, pgrad, zlo3, zhi3, sums3, bsum = call(
        point_kernel,
        plan,
        "point",
        steps,
        pairs,
        [
            (
                pl.BlockSpec((g, wb, cs, Lp), lambda t: (0, t, 0, 0)),
                (g, nw, cs, Lp),
                BF16,
            ),
            (win(wb, Lp, H), (nw, Lp, H), F32),
            (const(Hh, C), (Hh, C), BF16),
            (ANY, (nw, EDGE, H), BF16),
            (ANY, (nw, EDGE, H), BF16),
            (const(2, H), (2, H), F32),
            (const(1, C), (1, C), F32),
        ],
        [
            pltpu.VMEM((H, C), BF16),
            pltpu.VMEM((M, H), BF16),
            pltpu.VMEM((M, C), BF16),
            pltpu.VMEM((H, C), F32),
            pltpu.VMEM((2, nw, EDGE, H), BF16),
            pltpu.VMEM((2, C), F32),
        ]
        + halo_scratch(steps)
        + group.scratch(2, C),
        5 * nw * Lp * C * H,
        nw * Lp * C * 10,
        cid=4,
    )(lens, *[a for _, a in pairs])

    pairs = ins(
        (win(wb, Lp, H), c2),
        (win(wb, EDGE, H), lo3),
        (win(wb, EDGE, H), hi3),
        (win(wb, Lp, H), dz3),
        (win(wb, EDGE, H), zlo3),
        (win(wb, EDGE, H), zhi3),
        (win(wb, Lp, C), x2),
        (win(M, T2 * C), Y3),
        (taps_spec, full),
        (whole(2, H), stats3),
        (whole(2, H), sums3),
        (whole(2, C), stats2),
        (whole(8, C), par),
        (whole(Hh, C), pgrad),
    )
    dz2, grads, zlo2, zhi2, sums2 = call(
        dilated_back_kernel,
        plan,
        "dilated_back",
        steps,
        pairs,
        [
            (win(wb, Lp, C), (nw, Lp, C), F32),
            (const(Hh, (T2 + 1) * C), (Hh, (T2 + 1) * C), BF16),
            (ANY, (nw, C), F32),
            (ANY, (nw, C), F32),
            (const(2, C), (2, C), F32),
        ],
        [
            pltpu.VMEM((Lp + 2 * EDGE, H), F32),
            pltpu.VMEM((M, T2 * H), BF16),
            pltpu.VMEM((T2 * H, C), BF16),
            pltpu.VMEM((H, T2 * C), F32),
            pltpu.VMEM((2, nw, C), F32),
            pltpu.VMEM((2, C), F32),
        ]
        + halo_scratch(1)
        + group.scratch(2, C),
        4 * nw * Lp * T2 * C * H,
        nw * Lp * C * 20,
        cid=5,
    )(lens, *[a for _, a in pairs])

    pairs = ins(
        (win(wb, Lp, C), dz2),
        (whole(nw, C), zlo2),
        (whole(nw, C), zhi2),
        (win(wb, Lp, C), x2),
        (win(wb, EDGE, C), lo2),
        (win(wb, EDGE, C), hi2),
        (arg_win(Lp, C), cotangent),
        (whole(3, nw, C), hl),
        (whole(3, nw, C), hr),
        (win(M, T1 * C), X5),
        (whole(2, C), stats2),
        (whole(2, C), sums2),
        (whole(8, C), par),
        (whole(Hh, (T2 + 1) * C), grads),
        (ANY, res),
    )
    rb, wide, down, across = plan.block
    bshape = (2, plan.ns // 2, g, rb, wide)
    D3, blocks, result = call(
        conv_grad_kernel,
        plan,
        "conv_grad",
        steps,
        pairs,
        [
            (win(M, 3 * C), (nw * Lp, 3 * C), BF16),
            (const(*bshape), bshape, BF16),
            (ANY, (NW, cs, Lp), BF16),
        ],
        [
            pltpu.VMEM((Lp + 16, C), F32),
            pltpu.VMEM((Ch, T1 * C), F32),
            pltpu.SemaphoreType.DMA((g, steps)),
            pltpu.SemaphoreType.DMA((g, steps)),
            pltpu.SemaphoreType.DMA,
        ],
        2 * nw * Lp * T1 * C * Ch,
        nw * Lp * C * 30,
        cid=7,
    )(lens, *[a for _, a in pairs])

    def half_of(n):
        return pl.BlockSpec((n, Ch), lambda t: (0, half()), pipeline_mode=pl.Buffered(1))

    pairs = ins(
        (win(M, 3 * C), D3),
        (pl.BlockSpec((wb, L, Ch), lambda t: (grp() * steps + t, 0, half())), inputs),
        (
            pl.BlockSpec(
                (T1, Ch, C), lambda t: (0, half(), 0), pipeline_mode=pl.Buffered(1)
            ),
            conv_weight,
        ),
        (half_of(2), stats1),
        (half_of(1), gain1),
        (half_of(1), shift1),
        (ANY, blocks),
    )
    gz, sums1, summed = call(
        conv_back_kernel,
        plan,
        "conv_back",
        steps,
        pairs,
        [
            (ANY, (NW, cs, L), BF16),
            (const(2, Ch), (2, Ch), F32),
            (const(2, plan.ns // 2, rb, wide), (2, plan.ns // 2, rb, wide), BF16),
        ],
        [
            pltpu.VMEM((2 * Ch, 3 * C), BF16),
            pltpu.VMEM((L, L), BF16),
            pltpu.VMEM((4, Ch, L), F32),
            pltpu.VMEM((2 * Ch, M), F32),
            pltpu.VMEM((steps, g, wb, cs, L), BF16),
            pltpu.VMEM((2, Ch, L), F32),
            pltpu.SemaphoreType.DMA((steps, g)),
            pltpu.SemaphoreType.DMA((steps, g)),
            pltpu.SemaphoreType.DMA((steps,)),
            pltpu.VMEM(bshape[1:], BF16),
            pltpu.VMEM(bshape[1:], BF16),
            pltpu.VMEM(bshape[1:], BF16),
            pltpu.VMEM(bshape[1:], BF16),
            pltpu.VMEM((g, rb, wide), BF16),
            pltpu.VMEM((g, rb, wide), BF16),
            pltpu.VMEM((2, plan.ns // 2, rb, wide), BF16),
            pltpu.SemaphoreType.DMA((2, 3 + plan.ns + g, max(plan.ns // 2, g))),
        ]
        + group.scratch(2, C),
        2 * nw * Lp * 6 * C * Ch,
        nw * Lp * C * 12,
        cid=6,
    )(lens, *[a for _, a in pairs])

    pairs = ins(
        (pl.BlockSpec((wb, L, Ch), lambda t: (t, 0, half())), inputs),
        (win(wb, cs, L), gz),
        (half_of(2), stats1),
        (whole(2, Ch), sums1),
        (half_of(1), gain1),
        (win(wb, cs, Lp), result),
        (
            pl.BlockSpec((2, across // 2, rb, wide), lambda t: (0, t * down // (NW // wb), 0, 0)),
            summed,
        ),
        (whole(2, C), sums2),
        (whole(2, H), sums3),
        (whole(1, C), bsum),
    )
    outs = call(
        input_grad_kernel,
        plan,
        "input_grad",
        NW // wb,
        pairs,
        [
            (win(wb, cs, L), (NW, cs, L), BF16),
            (win(wb, cs, Lp), (NW, cs, Lp), BF16),
            (
                pl.BlockSpec((T1, rb, C), lambda t: (0, t * down // (NW // wb), 0)),
                (T1, cs, C),
                F32,
            ),
            (const(T2, hs, C), (T2, hs, C), F32),
            (const(hs, C), (hs, C), F32),
        ]
        + [(const(1, n), (1, n), F32) for n in (cs, cs, cs, cs, hs, hs, cs)],
        [
            pltpu.VMEM((L, L), BF16),
            pltpu.VMEM((3, cs, L), F32),
            pltpu.VMEM((Ch, L), F32),
        ],
        2 * NW * L * L * cs,
        NW * L * cs * 8,
    )(lens, *[a for _, a in pairs])
    grad, result, conv_grad, dil_grad, point_grad = outs[:5]
    g1, b1, g2, b2, g3, b3, pb = [a[0] for a in outs[5:]]
    return (
        jnp.swapaxes(result, 1, 2),
        jnp.swapaxes(grad, 1, 2),
        jnp.swapaxes(conv_grad, 1, 2),
        g1,
        b1,
        g2,
        b2,
        jnp.swapaxes(dil_grad, 1, 2),
        g3,
        b3,
        point_grad,
        pb,
    )


def solution(mesh):
    in_specs = (
        P(None, "seq", None),
        P(),
        P(),
        P(),
        P(),
        P("ch"),
        P("ch"),
        P(None, None, "ch"),
        P("ch"),
        P("ch"),
        P("ch", None),
        P("ch"),
        P(None, "seq", None),
    )
    out_specs = (
        P(None, "seq", "ch"),
        P(None, "seq", "ch"),
        P(None, None, "ch"),
        P("ch"),
        P("ch"),
        P("ch"),
        P("ch"),
        P(None, None, "ch"),
        P("ch"),
        P("ch"),
        P("ch", None),
        P("ch"),
    )
    return jax.shard_map(
        per_device, mesh=mesh, in_specs=in_specs, out_specs=out_specs, check_vma=False
    )
```

```python
from functools import partial
from typing import NamedTuple

import jax
import jax.numpy as jnp
from jax import lax
from jax.experimental import pallas as pl
from jax.experimental.pallas import tpu as pltpu
from jax.sharding import PartitionSpec as P

DIL = 14
EDGE = 16
EPS = 1e-05
GC0 = 0.7978845608028654
GC1 = 0.044715
F32 = jnp.float32
BF16 = jnp.bfloat16
MESH = pl.DeviceIdType.MESH
VMEM_LIMIT = 58 * 1024 * 1024
ANY = pl.BlockSpec(memory_space=pl.ANY)
SMEM = pl.BlockSpec(memory_space=pltpu.SMEM)


class Plan(NamedTuple):
    ns: int
    nz: int
    R: int
    NW: int
    L: int
    C: int
    H: int
    T1: int
    T2: int
    wb: int

    @property
    def g(self):
        return self.nz // self.R

    @property
    def nw(self):
        return self.NW // self.g

    @property
    def Lp(self):
        return self.L // 2

    @property
    def cs(self):
        return self.C // self.nz

    @property
    def Ch(self):
        return self.C // self.R

    @property
    def Hh(self):
        return self.H // self.R

    @property
    def steps(self):
        return self.nw // self.wb

    @property
    def chips(self):
        return self.ns // 2

    @property
    def rb(self):
        return self.cs // self.chips

    def place(self):
        s, z = lax.axis_index("seq"), lax.axis_index("ch")
        return s, z, lax.rem(z, self.g), lax.div(z, self.g)


def gelu(z):
    t = jnp.tanh(z * (GC0 + (GC0 * GC1) * (z * z)))
    hz = 0.5 * z
    return hz + hz * t


def gelu_both(z):
    sq = z * z
    t = jnp.tanh(z * (GC0 + (GC0 * GC1) * sq))
    hz = 0.5 * z
    slope = 0.5 + 0.5 * t + hz * (1.0 - t * t) * (GC0 + (3.0 * GC0 * GC1) * sq)
    return hz + hz * t, slope


def gelu_slope(z):
    return gelu_both(z)[1]


def rows_of(shape):
    return lax.broadcasted_iota(jnp.int32, shape, 0)


def lanes_of(shape):
    return lax.broadcasted_iota(jnp.int32, shape, 1)


def total_of(lens):
    n = lens[0]
    for k in range(1, lens.shape[0]):
        n = n + lens[k]
    return n.astype(F32)


def norm_of(stats, total):
    mean = stats[0:1] / total
    square = stats[1:2] / total
    return mean, lax.rsqrt(square - mean * mean + EPS)


def column(row, n):
    return jnp.broadcast_to(row, (n, row.shape[1])).T


def mm(a, b):
    return jnp.dot(a, b, preferred_element_type=F32)


def mm_nt(a, b):
    return lax.dot_general(a, b, (((1,), (1,)), ((), ())), preferred_element_type=F32)


def mm_tn(a, b):
    return lax.dot_general(a, b, (((0,), (0,)), ((), ())), preferred_element_type=F32)


def mm_tt(a, b):
    return lax.dot_general(a, b, (((0,), (1,)), ((), ())), preferred_element_type=F32)


def pick_matrix(L):
    r, n = rows_of((L, L)), lanes_of((L, L))
    bin_of = 2 * r - jnp.where(r >= L // 2, L - 1, 0)
    return jnp.where(n == bin_of, 1.0, 0.0).astype(BF16)


class Peers:
    def __init__(self, count, me, device):
        self.count, self.me, self.device = count, me, device

    def other(self, off):
        return lax.rem(self.me + off, self.count)

    def greet(self):
        barrier = pltpu.get_barrier_semaphore()
        for off in range(1, self.count):
            pl.semaphore_signal(
                barrier, inc=1, device_id=self.device(self.other(off)), device_id_type=MESH
            )

    def copy(self, link, slot, off):
        packet, buf, send, recv = link
        return pltpu.make_async_remote_copy(
            src_ref=packet,
            dst_ref=buf.at[slot],
            send_sem=send.at[off],
            recv_sem=recv.at[slot],
            device_id=self.device(self.other(off)),
            device_id_type=MESH,
        )

    def start(self, link):
        for off in range(1, self.count):
            self.copy(link, self.me, off).start()

    def finish(self, link):
        packet, buf = link[:2]
        buf[self.me] = packet[...]
        for off in range(1, self.count):
            self.copy(link, self.other(off), off).wait_recv()
        acc = buf[0]
        for q in range(1, self.count):
            acc = acc + buf[q]
        for off in range(1, self.count):
            self.copy(link, self.me, off).wait_send()
        return acc

    def scratch(self, rows, width):
        return [
            pltpu.VMEM((rows, width), F32),
            pltpu.VMEM((self.count, rows, width), F32),
            pltpu.SemaphoreType.DMA((self.count,)),
            pltpu.SemaphoreType.DMA((self.count,)),
        ]


def group_peers(plan):
    s, z, i, h = plan.place()
    g = plan.g
    return Peers(plan.ns * g, s * g + i, lambda q: (lax.div(q, g), h * g + lax.rem(q, g)))


def plane_peers(plan):
    s, z, i, h = plan.place()
    return Peers(plan.ns, s, lambda q: (q, z))


def line_peers(plan):
    s, z, i, h = plan.place()
    return Peers(plan.nz, z, lambda q: (s, q))


def meet(count):
    pl.semaphore_wait(pltpu.get_barrier_semaphore(), count)


class Halo:
    def __init__(self, plan, edge, low, high, sems, parts):
        self.edge, self.low, self.high, self.sems, self.parts = edge, low, high, sems, parts
        s, z, _, _ = plan.place()
        self.left = (lax.rem(s + plan.ns - 1, plan.ns), z)
        self.right = (lax.rem(s + 1, plan.ns), z)
        self.n = low.shape[0] // parts

    def copies(self, part):
        rows = pl.ds(part * self.n, self.n)
        return [
            pltpu.make_async_remote_copy(
                src_ref=self.edge.at[side, rows],
                dst_ref=dst.at[rows],
                send_sem=self.sems.at[0, side, part],
                recv_sem=self.sems.at[1, side, part],
                device_id=dev,
                device_id_type=MESH,
            )
            for side, (dst, dev) in enumerate(((self.high, self.left), (self.low, self.right)))
        ]

    def start(self, part):
        for c in self.copies(part):
            c.start()

    def finish(self):
        for part in range(self.parts):
            for c in self.copies(part):
                c.wait()


def halo_scratch(parts):
    return [pltpu.SemaphoreType.DMA((2, 2, parts))]


class Gather:
    PARTS = 2

    def __init__(self, plan, sems, stripe, part=None, full=None):
        self.plan, self.part, self.full, self.sems = plan, part, full, sems
        self.stripe = stripe
        self.s, self.z, self.i, self.h = plan.place()
        self.c, self.m = lax.rem(self.s, 2), lax.div(self.s, 2)
        self.chips = plan.ns // 2
        self.every = self.chips // 4
        self.tap = lax.div(self.m, self.every)
        self.owner = lax.rem(self.m, self.every) == 0
        self.rows = plan.H // plan.nz

    def copy(self, src, dst, sem, device):
        return pltpu.make_async_remote_copy(
            src_ref=src,
            dst_ref=dst,
            send_sem=self.sems.at[(0,) + sem],
            recv_sem=self.sems.at[(1,) + sem],
            device_id=device,
            device_id_type=MESH,
        )

    def line(self, off, at):
        to = lax.rem(self.z + off, self.plan.nz)
        return self.copy(self.part, self.stripe.at[at], (off,), (self.s, to))

    def own_rows(self):
        return pltpu.make_async_copy(self.part, self.stripe.at[self.z], self.sems.at[0, 0])

    def line_start(self):
        @pl.when(self.owner)
        def _():
            self.own_rows().start()
            for off in range(1, self.plan.nz):
                self.line(off, self.z).start()

    def line_finish(self):
        @pl.when(self.owner)
        def _():
            self.own_rows().wait()
            for off in range(1, self.plan.nz):
                self.line(off, self.z).wait_send()
                at = lax.rem(self.z + self.plan.nz - off, self.plan.nz)
                self.line(off, at).wait_recv()

    def half(self, ref, n):
        rows = self.plan.nz // self.PARTS
        return ref.at[pl.ds(n * rows, rows)]

    def own_stripe(self):
        return pltpu.make_async_copy(
            self.stripe, self.full.at[self.c, self.tap], self.sems.at[0, 0, 0]
        )

    def chip(self, off, n):
        to = lax.rem(self.m + off, self.chips)
        return self.copy(
            self.half(self.stripe, n),
            self.half(self.full.at[self.c, self.tap], n),
            (off, n),
            (2 * to + self.c, self.z),
        )

    def arrival(self, k, off, n):
        whole = self.half(self.full.at[self.c, k], n)
        return self.copy(whole, whole, (off, n), (2 * k * self.every + self.c, self.z))

    def pair(self, c, n):
        part = self.full.at[c, pl.ds(2 * n, 2)]
        return self.copy(part, part, (self.chips, n), (2 * self.m + 1 - self.c, self.z))

    def chips_start(self):
        @pl.when(self.owner)
        def _():
            self.own_stripe().start()
            for off in range(1, self.chips):
                for n in range(self.PARTS):
                    self.chip(off, n).start()

    def pair_start(self):
        for k in range(4):
            off = lax.rem(self.m - k * self.every + self.chips, self.chips)

            @pl.when(off != 0)
            def _():
                for n in range(self.PARTS):
                    self.arrival(k, off, n).wait_recv()

        @pl.when(self.owner)
        def _():
            self.own_stripe().wait()
            for off in range(1, self.chips):
                for n in range(self.PARTS):
                    self.chip(off, n).wait_send()

        for n in range(self.PARTS):
            self.pair(self.c, n).start()

    def pair_finish(self):
        for n in range(self.PARTS):
            self.pair(self.c, n).wait_send()
            self.pair(1 - self.c, n).wait_recv()


def first_step():
    return pl.program_id(0) == 0


def last_step():
    return pl.program_id(0) == pl.num_programs(0) - 1


def moments_kernel(plan, nw1, wb1, lens, x, xtop, xend, ctop, cend, g2, s2, pb, g3, s3,
                   taps, pw, stats, par, low, high, stripe,
                   acc, edge, part, line_sems, halo_sems, *links):
    t = pl.program_id(0)
    plane, line = plane_peers(plan), line_peers(plan)
    halo = Halo(plan, edge, low, high, halo_sems, 1)
    gather = Gather(plan, line_sems, stripe, part=part)
    s, z, i, h = plan.place()
    L, C, nw, nz = plan.L, plan.C, plan.nw, plan.nz

    @pl.when(first_step())
    def _():
        plane.greet()
        line.greet()
        part[...] = jnp.where(gather.tap == 3, pw[...], taps[0])
        acc[...] = jnp.zeros_like(acc)
        n16 = nw * 16
        for side, (xe, ce, places) in enumerate(
            ((xtop, ctop, (0, 1, 0)), (xend, cend, (14, 15, 15)))
        ):
            for k, at in enumerate(places):
                rows, lanes = rows_of((nw, n16)), lanes_of((nw, n16))
                sel = jnp.where(lanes == 16 * rows + at, 1.0, 0.0).astype(BF16)
                block = (xe if k < 2 else ce)[...].reshape(n16, C)
                edge[side, k] = mm(sel, block)

        meet(plane.count + line.count - 2)
        halo.start(0)
        gather.line_start()

    rows = rows_of((L, C))
    for w in range(wb1):
        valid = 2 * lens[z * nw1 + t * wb1 + w] - s * L
        v = jnp.where(rows < valid, x[w].astype(F32), 0.0)
        v3 = v.reshape(L // 8, 8, C)
        acc[0] += jnp.sum(v3, axis=0)
        acc[1] += jnp.sum(v3 * v3, axis=0)

    @pl.when(last_step())
    def _():
        packet, buf = links[0], links[5]
        packet[0:1] = jnp.sum(acc[0], axis=0, keepdims=True)
        packet[1:2] = jnp.sum(acc[1], axis=0, keepdims=True)
        plane.start(links[:4])
        at = 0
        spans = []
        links[4][2:3] = jnp.zeros((1, C), F32)
        for ref in (g2, s2, pb, g3, s3):
            n = ref.shape[1]
            links[4][2:3, at : at + n] = ref[...]
            spans.append((at, n))
            at += n
        links[4][0:2] = plane.finish(links[:4])
        line.start(links[4:])
        stats[...] = line.finish(links[4:])[0:2]
        par[...] = jnp.zeros_like(par)
        for k in range(nz):
            row = buf[k]
            for r, (at, n) in enumerate(spans):
                par[r : r + 1, k * n : (k + 1) * n] = row[2:3, at : at + n]
        halo.finish()
        gather.line_finish()


def conv_kernel(plan, lens, x, hl, hr, w_ref, stats, gain, shift, stripe,
                X5, x2, low, high, sums, full,
                sel, edge, acc, gather_sems, halo_sems, *link):
    t = pl.program_id(0)
    peers = group_peers(plan)
    halo = Halo(plan, edge, low, high, halo_sems, plan.steps)
    gather = Gather(plan, gather_sems, stripe, full=full)
    s, z, i, h = plan.place()
    L, Lp, C, wb = plan.L, plan.Lp, plan.C, plan.wb

    @pl.when(first_step())
    def _():
        peers.greet()
        acc[...] = jnp.zeros_like(acc)
        shape = (Lp, L)
        for k in range(plan.T1):
            at = lanes_of(shape) - (2 * rows_of(shape) + (k - 2))
            sel[k * Lp : (k + 1) * Lp] = jnp.where((at == 0) | (at == 1), 1.0, 0.0).astype(BF16)

    mean, rho = norm_of(stats[...], 2.0 * total_of(lens))
    scale = gain[...] * rho
    offset = shift[...] - mean * scale
    rows = rows_of((L, C))
    row1 = rows_of((1, C))
    row16 = rows_of((16, C))

    for w in range(wb):
        at = t * wb + w
        valid = 2 * lens[i * plan.nw + at] - s * L
        a = gelu(x[w].astype(F32) * scale + offset)
        a = jnp.where(rows < valid, a, 0.0).astype(BF16)
        picked = mm(sel[...], a)
        for k in range(5):
            X5[w * Lp : (w + 1) * Lp, k * C : (k + 1) * C] = picked[
                k * Lp : (k + 1) * Lp
            ].astype(BF16)

        def beside(ref, k, bin_at):
            a = gelu(ref[k, pl.ds(at, 1), :] * scale + offset)
            here = (row1 + bin_at < valid) & (row1 + (s * L + bin_at) >= 0)
            return jnp.where(here, a, 0.0).astype(BF16).astype(F32)

        l0, l1 = beside(hl, 0, -2), beside(hl, 1, -1)
        r0, r1 = beside(hr, 0, L), beside(hr, 1, L + 1)
        top, end = w * Lp, (w + 1) * Lp
        for k, add in ((0, l0 + l1), (1, l1)):
            X5[top : top + 16, k * C : (k + 1) * C] = (
                picked[k * Lp : k * Lp + 16] + jnp.where(row16 == 0, add, 0.0)
            ).astype(BF16)
        for k, add in ((3, r0), (4, r0 + r1)):
            X5[end - 16 : end, k * C : (k + 1) * C] = (
                picked[(k + 1) * Lp - 16 : (k + 1) * Lp] + jnp.where(row16 == 15, add, 0.0)
            ).astype(BF16)

    nc = 256
    rowp = rows_of((Lp, nc))
    for n in range(C // nc):
        cols = slice(n * nc, (n + 1) * nc)
        y = 0.5 * mm(X5[...], w_ref[:, cols])
        s0 = jnp.zeros((1, nc), F32)
        s1 = jnp.zeros((1, nc), F32)
        for w in range(wb):
            at = t * wb + w
            valid = lens[i * plan.nw + at] - s * Lp
            v = y[w * Lp : (w + 1) * Lp]
            x2[w, :, cols] = v
            edge[0, at, :, cols] = v[:EDGE].astype(BF16)
            edge[1, at, :, cols] = v[Lp - EDGE :].astype(BF16)
            v = jnp.where(rowp < valid, v, 0.0)
            s0 = s0 + jnp.sum(v, axis=0, keepdims=True)
            s1 = s1 + jnp.sum(v * v, axis=0, keepdims=True)
        acc[0:1, cols] += s0
        acc[1:2, cols] += s1

    @pl.when(first_step())
    def _():
        meet(peers.count - 1)
        gather.chips_start()

    halo.start(t)

    @pl.when(t == max(plan.steps - 2, 0))
    def _():
        gather.pair_start()

    @pl.when(last_step())
    def _():
        link[0][...] = acc[...]
        peers.start(link)
        sums[...] = peers.finish(link)
        halo.finish()
        gather.pair_finish()


def dilated_kernel(plan, lens, x2, lo, hi, w_ref, stats, par,
                   Y3, c2, low, high, sums, ext, wf, edge, acc, halo_sems, *link):
    t = pl.program_id(0)
    peers = group_peers(plan)
    halo = Halo(plan, edge, low, high, halo_sems, plan.steps)
    s, z, i, h = plan.place()
    Lp, C, H, wb = plan.Lp, plan.C, plan.H, plan.wb

    @pl.when(first_step())
    def _():
        peers.greet()
        acc[...] = jnp.zeros_like(acc)
        for k in range(plan.T2):
            for c in range(2):
                at = k * C + c * (C // 2)
                wf[:, at : at + C // 2] = w_ref[c, k]

    mean, rho = norm_of(stats[...], total_of(lens))
    scale = par[0:1] * rho
    offset = par[1:2] - mean * scale
    rows = rows_of((Lp, C))
    rowe = rows_of((EDGE, C))

    for w in range(wb):
        valid = lens[i * plan.nw + t * wb + w] - s * Lp
        a = jnp.where(rows < valid, gelu(x2[w] * scale + offset), 0.0)
        al = gelu(lo[w].astype(F32) * scale + offset)
        al = jnp.where((rowe - EDGE < valid) & (s > 0), al, 0.0)
        ah = gelu(hi[w].astype(F32) * scale + offset)
        ah = jnp.where(rowe + Lp < valid, ah, 0.0)
        ext[0:EDGE] = al
        ext[EDGE : EDGE + Lp] = a
        ext[EDGE + Lp :] = ah
        top, end = w * Lp, (w + 1) * Lp
        Y3[top:end, 0:C] = ext[EDGE - DIL : EDGE - DIL + Lp].astype(BF16)
        Y3[top:end, C : 2 * C] = a.astype(BF16)
        Y3[top:end, 2 * C : 3 * C] = ext[EDGE + DIL : EDGE + DIL + Lp].astype(BF16)

    y = mm_nt(Y3[...], wf[...])
    rowh = rows_of((Lp, H))
    s0 = jnp.zeros((1, H), F32)
    s1 = jnp.zeros((1, H), F32)
    for w in range(wb):
        at = t * wb + w
        valid = lens[i * plan.nw + at] - s * Lp
        v = y[w * Lp : (w + 1) * Lp]
        c2[w] = v
        edge[0, at] = v[:EDGE].astype(BF16)
        edge[1, at] = v[Lp - EDGE :].astype(BF16)
        v = jnp.where(rowh < valid, v, 0.0)
        s0 = s0 + jnp.sum(v, axis=0, keepdims=True)
        s1 = s1 + jnp.sum(v * v, axis=0, keepdims=True)
    acc[0:1, 0:H] += s0
    acc[1:2, 0:H] += s1

    @pl.when(first_step())
    def _():
        meet(peers.count - 1)

    halo.start(t)

    @pl.when(last_step())
    def _():
        link[0][...] = acc[...]
        peers.start(link)
        sums[...] = peers.finish(link)[:, 0:H]
        halo.finish()


def point_kernel(plan, lens, c2, x2, cot, w_ref, pb, stats, par,
                 res, dz, pgrad, low, high, sums, bsum,
                 pw, a3s, dos, pacc, edge, acc, halo_sems, *link):
    t = pl.program_id(0)
    peers = group_peers(plan)
    halo = Halo(plan, edge, low, high, halo_sems, plan.steps)
    s, z, i, h = plan.place()
    Lp, C, H, wb, cs = plan.Lp, plan.C, plan.H, plan.wb, plan.cs

    @pl.when(first_step())
    def _():
        peers.greet()
        acc[...] = jnp.zeros_like(acc)
        pacc[...] = jnp.zeros_like(pacc)
        for c in range(2):
            pw[:, c * (C // 2) : (c + 1) * (C // 2)] = w_ref[c, 0]

    mean, rho = norm_of(stats[...], total_of(lens))
    scale = par[3:4, 0:H] * rho
    offset = par[4:5, 0:H] - mean * scale
    rowc = rows_of((Lp, C))
    rowh = rows_of((Lp, H))

    s0 = jnp.zeros((1, H), F32)
    s1 = jnp.zeros((1, H), F32)
    sb = jnp.zeros((1, C), F32)
    for w in range(wb):
        at = t * wb + w
        valid = lens[i * plan.nw + at] - s * Lp
        top, end = w * Lp, (w + 1) * Lp
        d = jnp.where(rowc < valid, cot[w].astype(F32), 0.0)
        sb = sb + jnp.sum(d, axis=0, keepdims=True)
        d = d.astype(BF16)
        dos[top:end] = d
        v = c2[w]
        act, slope = gelu_both(v * scale + offset)
        a3s[top:end] = jnp.where(rowh < valid, act, 0.0).astype(BF16)
        dzw = mm_nt(d, pw[...]) * slope
        dz[w] = dzw
        edge[0, at] = dzw[:EDGE].astype(BF16)
        edge[1, at] = dzw[Lp - EDGE :].astype(BF16)
        hat = (v - mean) * rho
        s0 = s0 + jnp.sum(dzw, axis=0, keepdims=True)
        s1 = s1 + jnp.sum(dzw * hat, axis=0, keepdims=True)
    acc[0:1, 0:H] += s0
    acc[0:1, H : 2 * H] += s1
    acc[1:2] += sb

    @pl.when(first_step())
    def _():
        meet(peers.count - 1)

    halo.start(t)

    @pl.when(last_step())
    def _():
        link[0][...] = acc[...]
        peers.start(link)

    y = mm(a3s[...], w_ref[h, 0])
    rowr = rows_of((Lp, y.shape[1]))
    for w in range(wb):
        valid = lens[i * plan.nw + t * wb + w] - s * Lp
        r = x2[w] + y[w * Lp : (w + 1) * Lp] + pb[2:3]
        r = jnp.where(rowr < valid, r, 0.0).T.astype(BF16)
        for k in range(plan.g):
            res[k, w] = r[k * cs : (k + 1) * cs]
    pacc[...] += mm_tn(a3s[...], dos[...])

    @pl.when(last_step())
    def _():
        rows = pl.ds(pl.multiple_of(h * plan.Hh, 16), plan.Hh)
        pgrad[...] = pacc[rows].astype(BF16)
        got = peers.finish(link)
        sums[0:1] = got[0:1, 0:H]
        sums[1:2] = got[0:1, H : 2 * H]
        bsum[...] = got[1:2]
        halo.finish()


def dilated_back_kernel(plan, lens, c2, clo, chi, dz3, zlo, zhi, x2, Y3, w_ref,
                        stats3, sums3, stats2, par, pgrad, res,
                        dz2, grads, low, high, sums, res_got,
                        ext, Z3, wt, wacc, edge, acc, bulk_sems, halo_sems, *link):
    t = pl.program_id(0)
    peers = group_peers(plan)
    halo = Halo(plan, edge, low, high, halo_sems, 1)
    s, z, i, h = plan.place()
    Lp, C, H, wb, nw, g = plan.Lp, plan.C, plan.H, plan.wb, plan.nw, plan.g

    def bulk(off, n):
        to = lax.rem(i + off, g)
        rows = pl.ds(n * wb, wb)
        return pltpu.make_async_remote_copy(
            src_ref=res.at[to, rows],
            dst_ref=res_got.at[off, rows],
            send_sem=bulk_sems.at[0, off, n],
            recv_sem=bulk_sems.at[1, off, n],
            device_id=(s, h * g + to),
            device_id_type=MESH,
        )

    parts = [(off, n) for off in range(1, g) for n in range(plan.steps)]

    @pl.when(first_step())
    def _():
        peers.greet()
        acc[...] = jnp.zeros_like(acc)
        wacc[...] = jnp.zeros_like(wacc)
        for k in range(plan.T2):
            for c in range(2):
                cols = slice(c * (C // 2), (c + 1) * (C // 2))
                wt[k * H : (k + 1) * H, cols] = w_ref[c, k]

        meet(peers.count - 1)
        for part in parts:
            bulk(*part).start()

    total = total_of(lens)
    mean3, rho3 = norm_of(stats3[...], total)
    gr3 = par[3:4, 0:H] * rho3
    sg3 = sums3[0:1] / total
    gg3 = sums3[1:2] / total
    mean2, rho2 = norm_of(stats2[...], total)
    scale2 = par[0:1] * rho2
    offset2 = par[1:2] - mean2 * scale2
    rowh = rows_of((Lp, H))
    rowe = rows_of((EDGE, H))
    rowc = rows_of((Lp, C))

    def back(dz, v):
        return gr3 * (dz - (sg3 + (v - mean3) * rho3 * gg3))

    for w in range(wb):
        valid = lens[i * nw + t * wb + w] - s * Lp
        d = jnp.where(rowh < valid, back(dz3[w], c2[w]), 0.0)
        dl = back(zlo[w].astype(F32), clo[w].astype(F32))
        dl = jnp.where((rowe - EDGE < valid) & (s > 0), dl, 0.0)
        dh = back(zhi[w].astype(F32), chi[w].astype(F32))
        dh = jnp.where(rowe + Lp < valid, dh, 0.0)
        ext[0:EDGE] = dl
        ext[EDGE : EDGE + Lp] = d
        ext[EDGE + Lp :] = dh
        top, end = w * Lp, (w + 1) * Lp
        Z3[top:end, 0:H] = ext[EDGE + DIL : EDGE + DIL + Lp].astype(BF16)
        Z3[top:end, H : 2 * H] = d.astype(BF16)
        Z3[top:end, 2 * H : 3 * H] = ext[EDGE - DIL : EDGE - DIL + Lp].astype(BF16)

    y = mm(Z3[...], wt[...])

    s0 = jnp.zeros((1, C), F32)
    s1 = jnp.zeros((1, C), F32)
    for w in range(wb):
        at = t * wb + w
        valid = lens[i * nw + at] - s * Lp
        v = x2[w]
        dzw = y[w * Lp : (w + 1) * Lp] * gelu_slope(v * scale2 + offset2)
        dzw = jnp.where(rowc < valid, dzw, 0.0)
        dz2[w] = dzw
        edge[0, pl.ds(at, 1)] = dzw[0:1]
        edge[1, pl.ds(at, 1)] = dzw[Lp - 1 : Lp]
        s0 = s0 + jnp.sum(dzw, axis=0, keepdims=True)
        s1 = s1 + jnp.sum(dzw * ((v - mean2) * rho2), axis=0, keepdims=True)
    acc[0:1] += s0
    acc[1:2] += s1

    @pl.when(last_step())
    def _():
        link[0][...] = acc[...]
        peers.start(link)
        halo.start(0)

    wacc[...] += mm_tn(Z3[:, H : 2 * H], Y3[...])

    @pl.when(last_step())
    def _():
        rows = pl.ds(pl.multiple_of(h * plan.Hh, 16), plan.Hh)
        grads[:, 0 : plan.T2 * C] = wacc[rows].astype(BF16)
        grads[:, plan.T2 * C :] = pgrad[...]
        sums[...] = peers.finish(link)
        halo.finish()
        for part in parts:
            bulk(*part).wait()


class Reduction:
    SEMS = 3

    def __init__(self, plan, out, give, mine, got, mid, spread, half, mate, sems):
        self.plan, self.out = plan, out
        self.give, self.mine, self.got, self.mid, self.spread = give, mine, got, mid, spread
        self.half, self.mate = half, mate
        self.sems = sems
        self.s, self.z, self.i, self.h = plan.place()
        self.c = lax.rem(self.s, 2)
        self.m = lax.div(self.s, 2)
        self.chips = plan.chips

    @staticmethod
    def scratch(plan):
        taps, wide = plan.T1 + 2, plan.C // 2
        full = (taps, plan.chips, plan.g, plan.rb, wide)
        part = (taps, plan.g, plan.rb, wide)
        return [
            pltpu.VMEM((taps, 2, plan.chips, plan.rb, wide), BF16),
            *[pltpu.VMEM(full, BF16)] * 5,
            *[pltpu.VMEM(part, BF16)] * 2,
            pltpu.SemaphoreType.DMA((2, taps, Reduction.SEMS + 2 * plan.chips + plan.g)),
        ]

    def copy(self, src, dst, tap, sem, device):
        return pltpu.make_async_remote_copy(
            src_ref=src,
            dst_ref=dst,
            send_sem=self.sems.at[0, tap, sem],
            recv_sem=self.sems.at[1, tap, sem],
            device_id=device,
            device_id_type=MESH,
        )

    def pair(self):
        return (2 * self.m + (1 - self.c), self.z)

    def chip(self, off):
        return lax.rem(self.m + off, self.chips)

    def phase0(self, k):
        return self.copy(self.give.at[k], self.got.at[k], k, 0, self.pair())

    def phase1(self, k, off, at):
        to = self.chip(off)
        dst = self.spread.at[k, at]
        return self.copy(self.mid.at[k, to], dst, k, 1 + off, (2 * to + self.c, self.z))

    def phase2(self, k, off):
        to = lax.rem(self.i + off, self.plan.g)
        device = (self.s, self.h * self.plan.g + to)
        return self.copy(
            self.half.at[k, to], self.mate.at[k, off], k, 1 + self.chips + off, device
        )

    def phase3(self, k, off, at):
        to = self.chip(off)
        sem = 1 + self.chips + self.plan.g + off
        src, dst = self.out.at[k, self.c, self.m], self.out.at[k, self.c, at]
        return self.copy(src, dst, k, sem, (2 * to + self.c, self.z))

    def phase4(self, k, c):
        return self.copy(self.out.at[k, c], self.out.at[k, c], k, 1, self.pair())

    def put(self, k, rows):
        wide = self.plan.C // 2
        for j in range(self.plan.g):
            for m in range(self.chips):
                v = rows(j, m)
                left, right = v[:, :wide], v[:, wide:]
                self.mine[k, m, j] = jnp.where(self.c == 0, left, right).astype(BF16)
                self.give[k, m, j] = jnp.where(self.c == 0, right, left).astype(BF16)
        self.phase0(k).start()

    def step1(self, k):
        self.phase0(k).wait()
        self.mid[k] = (self.mine[k].astype(F32) + self.got[k].astype(F32)).astype(BF16)
        for off in range(1, self.chips):
            self.phase1(k, off, self.m).start()

    def step2(self, k):
        for off in range(1, self.chips):
            self.phase1(k, off, self.m).wait_send()
            self.phase1(k, off, self.chip(self.chips - off)).wait_recv()
        self.spread[k, self.m] = self.mid[k, self.m]
        v = self.spread[k, 0].astype(F32)
        for n in range(1, self.chips):
            v = v + self.spread[k, n].astype(F32)
        self.half[k] = v.astype(BF16)
        for off in range(1, self.plan.g):
            self.phase2(k, off).start()

    def step3(self, k):
        for off in range(1, self.plan.g):
            self.phase2(k, off).wait()
        v = self.half[k, self.i].astype(F32)
        for off in range(1, self.plan.g):
            v = v + self.mate[k, off].astype(F32)
        self.out[k, self.c, self.m] = v.astype(BF16)
        for off in range(1, self.chips):
            self.phase3(k, off, self.m).start()

    def step4(self, k):
        for off in range(1, self.chips):
            self.phase3(k, off, self.m).wait_send()
            self.phase3(k, off, self.chip(self.chips - off)).wait_recv()
        self.phase4(k, self.c).start()

    def step5(self, k):
        self.phase4(k, self.c).wait_send()
        self.phase4(k, 1 - self.c).wait_recv()

    def stages(self):
        return [self.step1, self.step2, self.step3, self.step4]


def tail_kernel(plan, lens, dz2, zlo, zhi, x2, lo, hi, cot, hl, hr, x, X5, taps, grads,
                stats2, sums2, par, stats1, gain1, shift1,
                gz, gz_got, sums, summed,
                ext, D3, D0T, wcat, pick, cols, y, part, acc, bulk_sems, *rest):
    t = pl.program_id(0)
    s, z, i, h = plan.place()
    L, Lp, C, wb, g, nw = plan.L, plan.Lp, plan.C, plan.wb, plan.g, plan.nw
    Ch, cs, T1 = plan.Ch, plan.cs, plan.T1
    M = wb * Lp
    nD = plan.steps
    last = nD + T1 - 1
    peers = group_peers(plan)
    red = Reduction(plan, *rest[:9])
    link = rest[9:]

    def bulk(step, off, n):
        to = lax.rem(i + off, g)
        n2 = wb // 2
        return pltpu.make_async_remote_copy(
            src_ref=part.at[step, to, pl.ds(n * n2, n2)],
            dst_ref=gz_got.at[off, pl.ds(step * wb + n * n2, n2)],
            send_sem=bulk_sems.at[0, step, off, n],
            recv_sem=bulk_sems.at[1, step, off, n],
            device_id=(s, h * g + to),
            device_id_type=MESH,
        )

    others = [(off, n) for off in range(1, g) for n in range(2)]

    def send(step):
        for other in others:
            bulk(step, *other).start()

    def when(at):
        return pl.when(t == min(at, last))

    @when(0)
    def _():
        peers.greet()
        acc[...] = jnp.zeros_like(acc)
        pick[...] = pick_matrix(L)
        mean, rho = norm_of(stats1[...], 2.0 * total_of(lens))
        scale = gain1[...] * rho
        for k, row in enumerate((scale, shift1[...] - mean * scale, rho, -mean * rho)):
            cols[k] = column(row, L)
        w = [taps[k].astype(F32) for k in range(5)]
        for r, parts in enumerate(
            ((w[0], w[1] + w[2], w[3] + w[4]), (w[0] + w[1], w[2] + w[3], w[4]))
        ):
            for k, v in enumerate(parts):
                wcat[r * Ch : (r + 1) * Ch, k * C : (k + 1) * C] = v.astype(BF16)

    @pl.when(t < nD)
    def _():
        total = total_of(lens)
        mean, rho = norm_of(stats2[...], total)
        gr = par[0:1] * rho
        sg = sums2[0:1] / total
        gg = sums2[1:2] / total
        rowc = rows_of((Lp, C))
        row1 = rows_of((1, C))

        def back(dout, dz, v):
            return 0.5 * (dout + gr * (dz - (sg + (v - mean) * rho * gg)))

        for w in range(wb):
            at = t * wb + w
            valid = lens[i * nw + at] - s * Lp
            d = back(cot[w].astype(F32), dz2[w], x2[w])
            d = jnp.where(rowc < valid, d, 0.0)
            one = pl.ds(at, 1)
            dl = back(hl[2, one, :], zlo[one, :], lo[w, EDGE - 1 : EDGE].astype(F32))
            dl = jnp.where((row1 - 1 < valid) & (s > 0), dl, 0.0)
            dh = back(hr[2, one, :], zhi[one, :], hi[w, 0:1].astype(F32))
            dh = jnp.where(row1 + Lp < valid, dh, 0.0)
            ext[7:8] = dl
            ext[8 : 8 + Lp] = d
            ext[8 + Lp : 9 + Lp] = dh
            top, end = w * Lp, (w + 1) * Lp
            D3[top:end, 0:C] = ext[9 : 9 + Lp].astype(BF16)
            D3[top:end, C : 2 * C] = d.astype(BF16)
            D3[top:end, 2 * C : 3 * C] = ext[7 : 7 + Lp].astype(BF16)

        y[:, 0:M] = mm_nt(wcat[...], D3[...])
        half = D3[:, pl.ds(pl.multiple_of(C + h * Ch, 128), Ch)]
        D0T[:, pl.ds(pl.multiple_of(t * M, 128), M)] = half.T
        lanes = lanes_of((Ch, L))
        bins = 2 * lanes - jnp.where(lanes >= Lp, L - 1, 0)
        for w in range(wb):
            valid = 2 * lens[i * nw + t * wb + w] - s * L
            top, end = w * Lp, (w + 1) * Lp
            v = mm_tt(x[w], pick[...])
            da = jnp.concatenate([y[0:Ch, top:end], y[Ch:, top:end]], axis=1)
            dzw = da * gelu_slope(v * cols[0] + cols[1])
            dzw = jnp.where(bins < valid, dzw, 0.0)
            acc[0] += dzw
            acc[1] += dzw * (v * cols[2] + cols[3])
            dzw = dzw.astype(BF16)
            for k in range(g):
                part[t, k, w] = dzw[k * cs : (k + 1) * cs]
        gz[...] = part[t, i]

    @when(0)
    def _():
        meet(peers.count - 1)
        hs = plan.H // plan.nz
        rb = plan.rb
        for u in range(2):

            def rows(j, m, u=u):
                side, r = m * rb // hs, m * rb % hs
                at = (2 * side + u) * C
                return grads[j * hs + r : j * hs + r + rb, at : at + C].astype(F32)

            red.put(T1 + u, rows)

    early = max(nD // 2, 1)

    @pl.when(t < early)
    def _():
        send(t)

    for n, stage in enumerate(red.stages()):

        @when(1 + n)
        def _():
            for u in range(2):
                stage(T1 + u)

    @when(nD - 1)
    def _():
        packet = link[0]
        packet[...] = jnp.zeros_like(packet)
        packet[0:1, 0:Ch] = jnp.sum(acc[0].T, axis=0, keepdims=True)
        packet[1:2, 0:Ch] = jnp.sum(acc[1].T, axis=0, keepdims=True)
        peers.start(link)

    @pl.when(t >= nD)
    def _():
        k = t - nD
        y[0:Ch, 0:C] = mm(D0T[...], X5[...])
        rb = plan.rb
        red.put(k, lambda j, m: y[j * cs + m * rb : j * cs + (m + 1) * rb, 0:C])
        for n, stage in enumerate(red.stages()):
            pl.when(k > n)(partial(stage, k - 1 - n))

    for step in range(early, nD - 1):

        @when(nD + 1 + step - early)
        def _():
            send(step)

    @when(last)
    def _():
        for n, stage in enumerate(red.stages()):
            for k in range(T1 - 1 - n, T1):
                if k >= 0:
                    stage(k)
            if n == 1 and nD - 1 >= early:
                send(nD - 1)
        sums[...] = peers.finish(link)[:, 0:Ch]
        for k in range(T1 + 2):
            red.step5(k)
        summed[...] = red.out[...]
        for step in range(nD):
            for other in others:
                bulk(step, *other).wait()


def input_grad_kernel(plan, lens, x, gz, gz_got, stats, sums, gain, res, res_got, summed,
                      sums2, sums3, bsum,
                      out, out_result, conv_grad, dil_grad, point_grad,
                      g1, b1, g2, b2, g3, b3, pb, pick, cols, xt):
    t = pl.program_id(0)
    s, z, i, h = plan.place()
    L, Ch, cs, wb = plan.L, plan.Ch, plan.cs, plan.wb
    mine = pl.ds(pl.multiple_of(i * cs, 16), cs)

    @pl.when(first_step())
    def _():
        n = 2.0 * total_of(lens)
        mean, rho = norm_of(stats[...], n)
        gr = gain[...] * rho
        gg = sums[1:2] / n * rho
        for k, row in enumerate((gr, -gr * gg, gr * (mean * gg - sums[0:1] / n))):
            xt[...] = column(row, L)
            cols[k] = xt[mine]
        pick[...] = pick_matrix(L)

        def mine_of(src, at, which, count, *dsts):
            n = dsts[0].shape[1]
            for k in range(count):

                @pl.when(which == k)
                def _():
                    for dst, r in zip(dsts, at):
                        dst[...] = src[r : r + 1, k * n : (k + 1) * n]

        mine_of(sums, (1, 0), i, plan.g, g1, b1)
        mine_of(sums2, (1, 0), z, plan.nz, g2, b2)
        mine_of(sums3, (1, 0), z, plan.nz, g3, b3)
        mine_of(bsum, (0,), z, plan.nz, pb)

    own = lax.div(t, plan.steps) == i
    for w in range(wb):
        out_result[w] = jnp.where(own, res[0, w].astype(F32), res_got[0, w].astype(F32)).astype(BF16)

    C, T1, hs, rb, wide = plan.C, plan.T1, plan.H // plan.nz, plan.rb, plan.C // 2
    count = plan.NW // wb
    turns = min(count, plan.chips)
    per, every = plan.chips // turns, count // turns

    def spread(turn):
        for n in range(per):
            m = turn * per + n
            side, r = m * rb // hs, m * rb % hs
            for c in range(2):
                at = slice(c * wide, (c + 1) * wide)
                for k in range(T1):
                    conv_grad[k, n * rb : (n + 1) * rb, at] = summed[k, c, n].astype(F32)
                for u in range(2):
                    v = summed[T1 + u, c, n].astype(F32)
                    if 2 * side + u < plan.T2:
                        dil_grad[2 * side + u, r : r + rb, at] = v
                    else:
                        point_grad[r : r + rb, at] = v

    for turn in range(turns):
        pl.when(t == turn * every)(partial(spread, turn))

    lanes = lanes_of((cs, L))
    for w in range(wb):
        valid = 2 * lens[t * wb + w] - s * L
        xt[...] = x[w].astype(F32).T
        v = xt[mine]
        dz = mm(jnp.where(own, gz[w].astype(F32), gz_got[0, w].astype(F32)).astype(BF16), pick[...])
        r = cols[0] * dz + v * cols[1] + cols[2]
        out[w] = jnp.where(lanes < valid, r, 0.0).astype(BF16)


def call(kernel, plan, name, steps, ins, outs, scratch, flops, nbytes, cid=None):
    extra = {} if cid is None else dict(collective_id=cid, has_side_effects=True)
    return pl.pallas_call(
        partial(kernel, plan),
        grid=(steps,),
        in_specs=[SMEM] + [spec for spec, _ in ins],
        out_specs=[spec for spec, _, _ in outs],
        out_shape=[jax.ShapeDtypeStruct(shape, dtype) for _, shape, dtype in outs],
        scratch_shapes=scratch,
        compiler_params=pltpu.CompilerParams(vmem_limit_bytes=VMEM_LIMIT, **extra),
        cost_estimate=pl.CostEstimate(
            flops=int(flops), bytes_accessed=int(nbytes), transcendentals=0
        ),
        name=name,
    )


def per_device(
    inputs,
    lengths,
    input_gain,
    input_shift,
    conv_weight,
    branch_gain,
    branch_shift,
    dilated_tap_weight,
    mixer_gain,
    mixer_shift,
    point_weight,
    point_bias,
    cotangent,
):
    NW, L, C = inputs.shape
    Lp = L // 2
    nz = lax.axis_size("ch")
    R = 2
    plan = Plan(
        ns=lax.axis_size("seq"),
        nz=nz,
        R=R,
        NW=NW,
        L=L,
        C=C,
        H=mixer_gain.shape[0] * nz,
        T1=conv_weight.shape[0],
        T2=dilated_tap_weight.shape[0],
        wb=min(NW * R // nz, max(1, 512 // Lp)),
    )
    g, nw, cs, Ch, H, Hh, wb = plan.g, plan.nw, plan.cs, plan.Ch, plan.H, plan.Hh, plan.wb
    T1, T2, steps = plan.T1, plan.T2, plan.steps
    M = wb * Lp
    hs = H // nz
    lens = lengths.astype(jnp.int32)
    gain1 = input_gain.reshape(1, C)
    shift1 = input_shift.reshape(1, C)

    def row(a):
        return a.reshape(1, a.shape[0])

    def grp():
        return lax.rem(lax.axis_index("ch"), g)

    def half():
        return lax.div(lax.axis_index("ch"), g)

    def core():
        return lax.rem(lax.axis_index("seq"), 2)

    def chip4():
        return lax.div(lax.axis_index("seq"), plan.ns // 4)

    def whole(*shape):
        return pl.BlockSpec(shape, lambda t: (0,) * len(shape), pipeline_mode=pl.Buffered(1))

    def const(*shape):
        return pl.BlockSpec(shape, lambda t: (0,) * len(shape))

    def win(*shape):
        return pl.BlockSpec(shape, lambda t: (t,) + (0,) * (len(shape) - 1))

    def arg_win(n, width):
        return pl.BlockSpec((wb, n, width), lambda t: (grp() * steps + t, 0, 0))

    def ins(*pairs):
        return [p for p in pairs]

    nw1 = NW // nz
    wb1 = min(nw1, wb)

    def edge_spec(n):
        return pl.BlockSpec(
            (nw, 16, C), lambda t: (grp(), n, 0), pipeline_mode=pl.Buffered(1)
        )

    pairs = ins(
        (
            pl.BlockSpec((wb1, L, C), lambda t: (lax.axis_index("ch") * (nw1 // wb1) + t, 0, 0)),
            inputs,
        ),
        (edge_spec(0), inputs),
        (edge_spec(L // 16 - 1), inputs),
        (edge_spec(0), cotangent),
        (edge_spec(Lp // 16 - 1), cotangent),
        (whole(1, cs), row(branch_gain)),
        (whole(1, cs), row(branch_shift)),
        (whole(1, cs), row(point_bias)),
        (whole(1, H // nz), row(mixer_gain)),
        (whole(1, H // nz), row(mixer_shift)),
        (
            pl.BlockSpec((1, hs, C // 2), lambda t: (jnp.minimum(chip4(), T2 - 1), 0, core())),
            jnp.swapaxes(dilated_tap_weight, 1, 2),
        ),
        (pl.BlockSpec((hs, C // 2), lambda t: (0, core())), point_weight),
    )
    plane, line, group = plane_peers(plan), line_peers(plan), group_peers(plan)
    stats1, par, hl, hr, stripe = call(
        lambda plan, *refs: moments_kernel(plan, nw1, wb1, *refs),
        plan,
        "moments",
        nw1 // wb1,
        pairs,
        [
            (const(2, C), (2, C), F32),
            (const(8, C), (8, C), F32),
            (ANY, (3, nw, C), F32),
            (ANY, (3, nw, C), F32),
            (ANY, (nz, hs, C // 2), BF16),
        ],
        [
            pltpu.VMEM((2, 8, C), F32),
            pltpu.VMEM((2, 3, nw, C), F32),
            pltpu.VMEM((hs, C // 2), BF16),
            pltpu.SemaphoreType.DMA((2, nz)),
        ]
        + halo_scratch(1)
        + plane.scratch(2, C)
        + line.scratch(3, C),
        0,
        nw1 * L * C * 2,
        cid=1,
    )(lens, *[a for _, a in pairs])

    pairs = ins(
        (arg_win(L, C), inputs),
        (whole(3, nw, C), hl),
        (whole(3, nw, C), hr),
        (whole(T1 * C, C), conv_weight.reshape(T1 * C, C)),
        (whole(2, C), stats1),
        (whole(1, C), gain1),
        (whole(1, C), shift1),
        (ANY, stripe),
    )
    X5, x2, lo2, hi2, stats2, full = call(
        conv_kernel,
        plan,
        "conv",
        steps,
        pairs,
        [
            (win(M, T1 * C), (nw * Lp, T1 * C), BF16),
            (win(wb, Lp, C), (nw, Lp, C), F32),
            (ANY, (nw, EDGE, C), BF16),
            (ANY, (nw, EDGE, C), BF16),
            (const(2, C), (2, C), F32),
            (ANY, (2, T2 + 1, nz, hs, C // 2), BF16),
        ],
        [
            pltpu.VMEM((T1 * Lp, L), BF16),
            pltpu.VMEM((2, nw, EDGE, C), BF16),
            pltpu.VMEM((2, C), F32),
            pltpu.SemaphoreType.DMA((2, plan.ns // 2 + 1, Gather.PARTS)),
        ]
        + halo_scratch(steps)
        + group.scratch(2, C),
        2 * nw * Lp * T1 * C * C,
        nw * Lp * C * 20,
        cid=2,
    )(lens, *[a for _, a in pairs])

    full = full.reshape(2, T2 + 1, H, C // 2)
    taps_spec = whole(2, T2, H, C // 2)
    pw_spec = pl.BlockSpec(
        (2, 1, H, C // 2), lambda t: (0, T2, 0, 0), pipeline_mode=pl.Buffered(1)
    )

    pairs = ins(
        (win(wb, Lp, C), x2),
        (win(wb, EDGE, C), lo2),
        (win(wb, EDGE, C), hi2),
        (taps_spec, full),
        (whole(2, C), stats2),
        (whole(8, C), par),
    )
    Y3, c2, lo3, hi3, stats3 = call(
        dilated_kernel,
        plan,
        "dilated",
        steps,
        pairs,
        [
            (win(M, T2 * C), (nw * Lp, T2 * C), BF16),
            (win(wb, Lp, H), (nw, Lp, H), F32),
            (ANY, (nw, EDGE, H), BF16),
            (ANY, (nw, EDGE, H), BF16),
            (const(2, H), (2, H), F32),
        ],
        [
            pltpu.VMEM((Lp + 2 * EDGE, C), F32),
            pltpu.VMEM((H, T2 * C), BF16),
            pltpu.VMEM((2, nw, EDGE, H), BF16),
            pltpu.VMEM((2, C), F32),
        ]
        + halo_scratch(steps)
        + group.scratch(2, C),
        2 * nw * Lp * T2 * C * H,
        nw * Lp * C * 12,
        cid=3,
    )(lens, *[a for _, a in pairs])

    pairs = ins(
        (win(wb, Lp, H), c2),
        (pl.BlockSpec((wb, Lp, Ch), lambda t: (t, 0, half())), x2),
        (arg_win(Lp, C), cotangent),
        (pw_spec, full),
        (pl.BlockSpec((8, Ch), lambda t: (0, half()), pipeline_mode=pl.Buffered(1)), par),
        (whole(2, H), stats3),
        (whole(8, C), par),
    )
    res, dz3, pgrad, zlo3, zhi3, sums3, bsum = call(
        point_kernel,
        plan,
        "point",
        steps,
        pairs,
        [
            (
                pl.BlockSpec((g, wb, cs, Lp), lambda t: (0, t, 0, 0)),
                (g, nw, cs, Lp),
                BF16,
            ),
            (win(wb, Lp, H), (nw, Lp, H), F32),
            (const(Hh, C), (Hh, C), BF16),
            (ANY, (nw, EDGE, H), BF16),
            (ANY, (nw, EDGE, H), BF16),
            (const(2, H), (2, H), F32),
            (const(1, C), (1, C), F32),
        ],
        [
            pltpu.VMEM((H, C), BF16),
            pltpu.VMEM((M, H), BF16),
            pltpu.VMEM((M, C), BF16),
            pltpu.VMEM((H, C), F32),
            pltpu.VMEM((2, nw, EDGE, H), BF16),
            pltpu.VMEM((2, C), F32),
        ]
        + halo_scratch(steps)
        + group.scratch(2, C),
        5 * nw * Lp * C * H,
        nw * Lp * C * 10,
        cid=4,
    )(lens, *[a for _, a in pairs])

    pairs = ins(
        (win(wb, Lp, H), c2),
        (win(wb, EDGE, H), lo3),
        (win(wb, EDGE, H), hi3),
        (win(wb, Lp, H), dz3),
        (win(wb, EDGE, H), zlo3),
        (win(wb, EDGE, H), zhi3),
        (win(wb, Lp, C), x2),
        (win(M, T2 * C), Y3),
        (taps_spec, full),
        (whole(2, H), stats3),
        (whole(2, H), sums3),
        (whole(2, C), stats2),
        (whole(8, C), par),
        (whole(Hh, C), pgrad),
        (ANY, res),
    )
    dz2, grads, zlo2, zhi2, sums2, res_got = call(
        dilated_back_kernel,
        plan,
        "dilated_back",
        steps,
        pairs,
        [
            (win(wb, Lp, C), (nw, Lp, C), F32),
            (const(Hh, (T2 + 1) * C), (Hh, (T2 + 1) * C), BF16),
            (ANY, (nw, C), F32),
            (ANY, (nw, C), F32),
            (const(2, C), (2, C), F32),
            (ANY, (g, nw, cs, Lp), BF16),
        ],
        [
            pltpu.VMEM((Lp + 2 * EDGE, H), F32),
            pltpu.VMEM((M, T2 * H), BF16),
            pltpu.VMEM((T2 * H, C), BF16),
            pltpu.VMEM((H, T2 * C), F32),
            pltpu.VMEM((2, nw, C), F32),
            pltpu.VMEM((2, C), F32),
            pltpu.SemaphoreType.DMA((2, g, steps)),
        ]
        + halo_scratch(1)
        + group.scratch(2, C),
        4 * nw * Lp * T2 * C * H,
        nw * Lp * C * 20,
        cid=5,
    )(lens, *[a for _, a in pairs])

    def half_of(n):
        return pl.BlockSpec((n, Ch), lambda t: (0, half()), pipeline_mode=pl.Buffered(1))

    def early(*shape):
        return pl.BlockSpec(
            shape, lambda t: (jnp.minimum(t, steps - 1),) + (0,) * (len(shape) - 1)
        )

    chips, rb = plan.chips, plan.rb
    sshape = (T1 + 2, 2, chips, rb, C // 2)
    pairs = ins(
        (early(wb, Lp, C), dz2),
        (whole(nw, C), zlo2),
        (whole(nw, C), zhi2),
        (early(wb, Lp, C), x2),
        (early(wb, EDGE, C), lo2),
        (early(wb, EDGE, C), hi2),
        (
            pl.BlockSpec(
                (wb, Lp, C), lambda t: (grp() * steps + jnp.minimum(t, steps - 1), 0, 0)
            ),
            cotangent,
        ),
        (whole(3, nw, C), hl),
        (whole(3, nw, C), hr),
        (
            pl.BlockSpec(
                (wb, L, Ch), lambda t: (grp() * steps + jnp.minimum(t, steps - 1), 0, half())
            ),
            inputs,
        ),
        (pl.BlockSpec((nw * Lp, C), lambda t: (0, jnp.maximum(t - steps, 0))), X5),
        (
            pl.BlockSpec(
                (T1, Ch, C), lambda t: (0, half(), 0), pipeline_mode=pl.Buffered(1)
            ),
            conv_weight,
        ),
        (whole(Hh, (T2 + 1) * C), grads),
        (whole(2, C), stats2),
        (whole(2, C), sums2),
        (whole(8, C), par),
        (half_of(2), stats1),
        (half_of(1), gain1),
        (half_of(1), shift1),
    )
    gz, gz_got, sums1, summed = call(
        tail_kernel,
        plan,
        "tail",
        steps + T1,
        pairs,
        [
            (early(wb, cs, L), (nw, cs, L), BF16),
            (ANY, (g, nw, cs, L), BF16),
            (const(2, Ch), (2, Ch), F32),
            (const(*sshape), sshape, BF16),
        ],
        [
            pltpu.VMEM((Lp + 16, C), F32),
            pltpu.VMEM((M, 3 * C), BF16),
            pltpu.VMEM((Ch, nw * Lp), BF16),
            pltpu.VMEM((2 * Ch, 3 * C), BF16),
            pltpu.VMEM((L, L), BF16),
            pltpu.VMEM((4, Ch, L), F32),
            pltpu.VMEM((2 * Ch, max(M, C)), F32),
            pltpu.VMEM((steps, g, wb, cs, L), BF16),
            pltpu.VMEM((2, Ch, L), F32),
            pltpu.SemaphoreType.DMA((2, steps, g, 2)),
        ]
        + Reduction.scratch(plan)
        + group.scratch(2, C),
        2 * nw * Lp * (6 + T1) * C * Ch,
        nw * Lp * C * 40,
        cid=6,
    )(lens, *[a for _, a in pairs])

    count = NW // wb
    turns = min(count, chips)

    def own_block(t):
        return jnp.where(lax.div(t, steps) == grp(), lax.rem(t, steps), 0)

    def got_slot(t):
        off = lax.rem(grp() - lax.div(t, steps) + g, g)
        return jnp.maximum(off, 1), jnp.where(off > 0, lax.rem(t, steps), 0)

    pairs = ins(
        (pl.BlockSpec((wb, L, Ch), lambda t: (t, 0, half())), inputs),
        (pl.BlockSpec((wb, cs, L), lambda t: (own_block(t), 0, 0)), gz),
        (pl.BlockSpec((1, wb, cs, L), lambda t: got_slot(t) + (0, 0)), gz_got),
        (half_of(2), stats1),
        (whole(2, Ch), sums1),
        (half_of(1), gain1),
        (pl.BlockSpec((1, wb, cs, Lp), lambda t: (grp(), own_block(t), 0, 0)), res),
        (pl.BlockSpec((1, wb, cs, Lp), lambda t: got_slot(t) + (0, 0)), res_got),
        (
            pl.BlockSpec(
                (T1 + 2, 2, chips // turns, rb, C // 2),
                lambda t: (0, 0, t * turns // count, 0, 0),
            ),
            summed,
        ),
        (whole(2, C), sums2),
        (whole(2, H), sums3),
        (whole(1, C), bsum),
    )
    outs = call(
        input_grad_kernel,
        plan,
        "input_grad",
        NW // wb,
        pairs,
        [
            (win(wb, cs, L), (NW, cs, L), BF16),
            (win(wb, cs, Lp), (NW, cs, Lp), BF16),
            (
                pl.BlockSpec((T1, cs // turns, C), lambda t: (0, t * turns // count, 0)),
                (T1, cs, C),
                F32,
            ),
            (const(T2, hs, C), (T2, hs, C), F32),
            (const(hs, C), (hs, C), F32),
        ]
        + [(const(1, n), (1, n), F32) for n in (cs, cs, cs, cs, hs, hs, cs)],
        [
            pltpu.VMEM((L, L), BF16),
            pltpu.VMEM((3, cs, L), F32),
            pltpu.VMEM((Ch, L), F32),
        ],
        2 * NW * L * L * cs,
        NW * L * cs * 8,
    )(lens, *[a for _, a in pairs])
    grad, result, conv_grad, dil_grad, point_grad = outs[:5]
    g1, b1, g2, b2, g3, b3, pb = [a[0] for a in outs[5:]]
    return (
        jnp.swapaxes(result, 1, 2),
        jnp.swapaxes(grad, 1, 2),
        jnp.swapaxes(conv_grad, 1, 2),
        g1,
        b1,
        g2,
        b2,
        jnp.swapaxes(dil_grad, 1, 2),
        g3,
        b3,
        point_grad,
        pb,
    )


def solution(mesh):
    in_specs = (
        P(None, "seq", None),
        P(),
        P(),
        P(),
        P(),
        P("ch"),
        P("ch"),
        P(None, None, "ch"),
        P("ch"),
        P("ch"),
        P("ch", None),
        P("ch"),
        P(None, "seq", None),
    )
    out_specs = (
        P(None, "seq", "ch"),
        P(None, "seq", "ch"),
        P(None, None, "ch"),
        P("ch"),
        P("ch"),
        P("ch"),
        P("ch"),
        P(None, None, "ch"),
        P("ch"),
        P("ch"),
        P("ch", None),
        P("ch"),
    )
    return jax.shard_map(
        per_device, mesh=mesh, in_specs=in_specs, out_specs=out_specs, check_vma=False
    )
```

```python
from functools import partial
from typing import NamedTuple

import jax
import jax.numpy as jnp
from jax import lax
from jax.experimental import pallas as pl
from jax.experimental.pallas import tpu as pltpu
from jax.sharding import PartitionSpec as P

DIL = 14
EDGE = 16
EPS = 1e-05
GC0 = 0.7978845608028654
GC1 = 0.044715
F32 = jnp.float32
BF16 = jnp.bfloat16
MESH = pl.DeviceIdType.MESH
VMEM_LIMIT = 58 * 1024 * 1024
ANY = pl.BlockSpec(memory_space=pl.ANY)
SMEM = pl.BlockSpec(memory_space=pltpu.SMEM)


class Plan(NamedTuple):
    ns: int
    nz: int
    R: int
    NW: int
    L: int
    C: int
    H: int
    T1: int
    T2: int
    wb: int

    @property
    def g(self):
        return self.nz // self.R

    @property
    def nw(self):
        return self.NW // self.g

    @property
    def Lp(self):
        return self.L // 2

    @property
    def cs(self):
        return self.C // self.nz

    @property
    def Ch(self):
        return self.C // self.R

    @property
    def Hh(self):
        return self.H // self.R

    @property
    def steps(self):
        return self.nw // self.wb

    @property
    def chips(self):
        return self.ns // 2

    @property
    def rb(self):
        return self.cs // self.chips

    def place(self):
        s, z = lax.axis_index("seq"), lax.axis_index("ch")
        return s, z, lax.rem(z, self.g), lax.div(z, self.g)


def gelu(z):
    t = jnp.tanh(z * (GC0 + (GC0 * GC1) * (z * z)))
    return z * (0.5 + 0.5 * t)


def gelu_both(z):
    sq = z * z
    t = jnp.tanh(z * (GC0 + (GC0 * GC1) * sq))
    h = 0.5 + 0.5 * t
    v = z * h
    return v, h + v * (1.0 - t) * (GC0 + (3.0 * GC0 * GC1) * sq)


def gelu_slope(z):
    return gelu_both(z)[1]


def fold(v):
    return jnp.sum(v.reshape(v.shape[0] // 8, 8, v.shape[1]), axis=0)


def unfold(v):
    return jnp.sum(v, axis=0, keepdims=True)


def rows_of(shape):
    return lax.broadcasted_iota(jnp.int32, shape, 0)


def lanes_of(shape):
    return lax.broadcasted_iota(jnp.int32, shape, 1)


def total_of(lens):
    n = lens[0]
    for k in range(1, lens.shape[0]):
        n = n + lens[k]
    return n.astype(F32)


def norm_of(stats, total):
    mean = stats[0:1] / total
    square = stats[1:2] / total
    return mean, lax.rsqrt(square - mean * mean + EPS)


def column(row, n):
    return jnp.broadcast_to(row, (n, row.shape[1])).T


def mm(a, b):
    return jnp.dot(a, b, preferred_element_type=F32)


def mm_nt(a, b):
    return lax.dot_general(a, b, (((1,), (1,)), ((), ())), preferred_element_type=F32)


def mm_tn(a, b):
    return lax.dot_general(a, b, (((0,), (0,)), ((), ())), preferred_element_type=F32)


def mm_tt(a, b):
    return lax.dot_general(a, b, (((0,), (1,)), ((), ())), preferred_element_type=F32)


def eye_matrix(n, m, first):
    return jnp.where(lanes_of((n, m)) == rows_of((n, m)) + first, 1.0, 0.0).astype(BF16)


def pick_matrix(L):
    r, n = rows_of((L, L)), lanes_of((L, L))
    bin_of = 2 * r - jnp.where(r >= L // 2, L - 1, 0)
    return jnp.where(n == bin_of, 1.0, 0.0).astype(BF16)


class Peers:
    def __init__(self, count, me, device):
        self.count, self.me, self.device = count, me, device

    def other(self, off):
        return lax.rem(self.me + off, self.count)

    def greet(self):
        barrier = pltpu.get_barrier_semaphore()
        for off in range(1, self.count):
            pl.semaphore_signal(
                barrier, inc=1, device_id=self.device(self.other(off)), device_id_type=MESH
            )

    def copy(self, link, slot, off):
        packet, buf, send, recv = link
        return pltpu.make_async_remote_copy(
            src_ref=packet,
            dst_ref=buf.at[slot],
            send_sem=send.at[off],
            recv_sem=recv.at[slot],
            device_id=self.device(self.other(off)),
            device_id_type=MESH,
        )

    def start(self, link):
        for off in range(1, self.count):
            self.copy(link, self.me, off).start()

    def finish(self, link):
        packet, buf = link[:2]
        buf[self.me] = packet[...]
        for off in range(1, self.count):
            self.copy(link, self.other(off), off).wait_recv()
        acc = buf[0]
        for q in range(1, self.count):
            acc = acc + buf[q]
        for off in range(1, self.count):
            self.copy(link, self.me, off).wait_send()
        return acc

    def scratch(self, rows, width):
        return [
            pltpu.VMEM((rows, width), F32),
            pltpu.VMEM((self.count, rows, width), F32),
            pltpu.SemaphoreType.DMA((self.count,)),
            pltpu.SemaphoreType.DMA((self.count,)),
        ]


def group_peers(plan):
    s, z, i, h = plan.place()
    g = plan.g
    return Peers(plan.ns * g, s * g + i, lambda q: (lax.div(q, g), h * g + lax.rem(q, g)))


def plane_peers(plan):
    s, z, i, h = plan.place()
    return Peers(plan.ns, s, lambda q: (q, z))


def line_peers(plan):
    s, z, i, h = plan.place()
    return Peers(plan.nz, z, lambda q: (s, q))


def meet(count):
    pl.semaphore_wait(pltpu.get_barrier_semaphore(), count)


class Halo:
    def __init__(self, plan, edge, low, high, sems, parts):
        self.edge, self.low, self.high, self.sems, self.parts = edge, low, high, sems, parts
        s, z, _, _ = plan.place()
        self.left = (lax.rem(s + plan.ns - 1, plan.ns), z)
        self.right = (lax.rem(s + 1, plan.ns), z)
        self.n = low.shape[0] // parts

    def copies(self, part):
        rows = pl.ds(part * self.n, self.n)
        return [
            pltpu.make_async_remote_copy(
                src_ref=self.edge.at[side, rows],
                dst_ref=dst.at[rows],
                send_sem=self.sems.at[0, side, part],
                recv_sem=self.sems.at[1, side, part],
                device_id=dev,
                device_id_type=MESH,
            )
            for side, (dst, dev) in enumerate(((self.high, self.left), (self.low, self.right)))
        ]

    def start(self, part):
        for c in self.copies(part):
            c.start()

    def finish(self):
        for part in range(self.parts):
            for c in self.copies(part):
                c.wait()


def halo_scratch(parts):
    return [pltpu.SemaphoreType.DMA((2, 2, parts))]


class Gather:
    PARTS = 2

    def __init__(self, plan, sems, stripe, part=None, full=None):
        self.plan, self.part, self.full, self.sems = plan, part, full, sems
        self.stripe = stripe
        self.s, self.z, self.i, self.h = plan.place()
        self.c, self.m = lax.rem(self.s, 2), lax.div(self.s, 2)
        self.chips = plan.ns // 2
        self.every = self.chips // 4
        self.tap = lax.div(self.m, self.every)
        self.owner = lax.rem(self.m, self.every) == 0
        self.rows = plan.H // plan.nz

    def copy(self, src, dst, sem, device):
        return pltpu.make_async_remote_copy(
            src_ref=src,
            dst_ref=dst,
            send_sem=self.sems.at[(0,) + sem],
            recv_sem=self.sems.at[(1,) + sem],
            device_id=device,
            device_id_type=MESH,
        )

    def line(self, off, at):
        to = lax.rem(self.z + off, self.plan.nz)
        return self.copy(self.part, self.stripe.at[at], (off,), (self.s, to))

    def own_rows(self):
        return pltpu.make_async_copy(self.part, self.stripe.at[self.z], self.sems.at[0, 0])

    def line_start(self):
        @pl.when(self.owner)
        def _():
            self.own_rows().start()
            for off in range(1, self.plan.nz):
                self.line(off, self.z).start()

    def line_finish(self):
        @pl.when(self.owner)
        def _():
            self.own_rows().wait()
            for off in range(1, self.plan.nz):
                self.line(off, self.z).wait_send()
                at = lax.rem(self.z + self.plan.nz - off, self.plan.nz)
                self.line(off, at).wait_recv()

    def half(self, ref, n):
        rows = self.plan.nz // self.PARTS
        return ref.at[pl.ds(n * rows, rows)]

    def own_stripe(self):
        return pltpu.make_async_copy(
            self.stripe, self.full.at[self.c, self.tap], self.sems.at[0, 0, 0]
        )

    def chip(self, off, n):
        to = lax.rem(self.m + off, self.chips)
        return self.copy(
            self.half(self.stripe, n),
            self.half(self.full.at[self.c, self.tap], n),
            (off, n),
            (2 * to + self.c, self.z),
        )

    def arrival(self, k, off, n):
        whole = self.half(self.full.at[self.c, k], n)
        return self.copy(whole, whole, (off, n), (2 * k * self.every + self.c, self.z))

    def pair(self, c, n):
        part = self.full.at[c, pl.ds(2 * n, 2)]
        return self.copy(part, part, (self.chips, n), (2 * self.m + 1 - self.c, self.z))

    def chips_start(self):
        @pl.when(self.owner)
        def _():
            self.own_stripe().start()
            for off in range(1, self.chips):
                for n in range(self.PARTS):
                    self.chip(off, n).start()

    def pair_start(self):
        for k in range(4):
            off = lax.rem(self.m - k * self.every + self.chips, self.chips)

            @pl.when(off != 0)
            def _():
                for n in range(self.PARTS):
                    self.arrival(k, off, n).wait_recv()

        @pl.when(self.owner)
        def _():
            self.own_stripe().wait()
            for off in range(1, self.chips):
                for n in range(self.PARTS):
                    self.chip(off, n).wait_send()

        for n in range(self.PARTS):
            self.pair(self.c, n).start()

    def pair_finish(self):
        for n in range(self.PARTS):
            self.pair(self.c, n).wait_send()
            self.pair(1 - self.c, n).wait_recv()


def first_step():
    return pl.program_id(0) == 0


def last_step():
    return pl.program_id(0) == pl.num_programs(0) - 1


def moments_kernel(plan, nw1, wb1, lens, x, xtop, xend, ctop, cend, g2, s2, pb, g3, s3,
                   taps, pw, stats, par, low, high, stripe,
                   acc, edge, part, line_sems, halo_sems, *links):
    t = pl.program_id(0)
    plane, line = plane_peers(plan), line_peers(plan)
    halo = Halo(plan, edge, low, high, halo_sems, 1)
    gather = Gather(plan, line_sems, stripe, part=part)
    s, z, i, h = plan.place()
    L, C, nw, nz = plan.L, plan.C, plan.nw, plan.nz

    @pl.when(first_step())
    def _():
        plane.greet()
        line.greet()
        part[...] = jnp.where(gather.tap == 3, pw[...], taps[0])
        acc[...] = jnp.zeros_like(acc)
        n16 = nw * 16
        for side, (xe, ce, places) in enumerate(
            ((xtop, ctop, (0, 1, 0)), (xend, cend, (14, 15, 15)))
        ):
            for k, at in enumerate(places):
                rows, lanes = rows_of((nw, n16)), lanes_of((nw, n16))
                sel = jnp.where(lanes == 16 * rows + at, 1.0, 0.0).astype(BF16)
                block = (xe if k < 2 else ce)[...].reshape(n16, C)
                edge[side, k] = mm(sel, block)

        meet(plane.count + line.count - 2)
        halo.start(0)
        gather.line_start()

    rows = rows_of((L, C))
    for w in range(wb1):
        valid = 2 * lens[z * nw1 + t * wb1 + w] - s * L
        v = jnp.where(rows < valid, x[w].astype(F32), 0.0)
        v3 = v.reshape(L // 8, 8, C)
        acc[0] += jnp.sum(v3, axis=0)
        acc[1] += jnp.sum(v3 * v3, axis=0)

    @pl.when(last_step())
    def _():
        packet, buf = links[0], links[5]
        packet[0:1] = jnp.sum(acc[0], axis=0, keepdims=True)
        packet[1:2] = jnp.sum(acc[1], axis=0, keepdims=True)
        plane.start(links[:4])
        at = 0
        spans = []
        links[4][2:3] = jnp.zeros((1, C), F32)
        for ref in (g2, s2, pb, g3, s3):
            n = ref.shape[1]
            links[4][2:3, at : at + n] = ref[...]
            spans.append((at, n))
            at += n
        links[4][0:2] = plane.finish(links[:4])
        line.start(links[4:])
        stats[...] = line.finish(links[4:])[0:2]
        par[...] = jnp.zeros_like(par)
        for k in range(nz):
            row = buf[k]
            for r, (at, n) in enumerate(spans):
                par[r : r + 1, k * n : (k + 1) * n] = row[2:3, at : at + n]
        halo.finish()
        gather.line_finish()


def conv_kernel(plan, lens, x, hl, hr, w_ref, stats, gain, shift, stripe,
                X5, x2, low, high, sums, full,
                sel, edge, acc, gather_sems, halo_sems, *link):
    t = pl.program_id(0)
    peers = group_peers(plan)
    halo = Halo(plan, edge, low, high, halo_sems, plan.steps)
    gather = Gather(plan, gather_sems, stripe, full=full)
    s, z, i, h = plan.place()
    L, Lp, C, wb = plan.L, plan.Lp, plan.C, plan.wb

    @pl.when(first_step())
    def _():
        peers.greet()
        acc[...] = jnp.zeros_like(acc)
        shape = (Lp, L)
        for k in range(plan.T1):
            at = lanes_of(shape) - (2 * rows_of(shape) + (k - 2))
            sel[k * Lp : (k + 1) * Lp] = jnp.where((at == 0) | (at == 1), 1.0, 0.0).astype(BF16)

    mean, rho = norm_of(stats[...], 2.0 * total_of(lens))
    scale = gain[...] * rho
    offset = shift[...] - mean * scale
    rows = rows_of((L, C))
    row1 = rows_of((1, C))
    row16 = rows_of((16, C))

    for w in range(wb):
        at = t * wb + w
        valid = 2 * lens[i * plan.nw + at] - s * L
        a = gelu(x[w].astype(F32) * scale + offset)
        a = jnp.where(rows < valid, a, 0.0).astype(BF16)
        picked = mm(sel[...], a)
        for k in range(5):
            X5[w * Lp : (w + 1) * Lp, k * C : (k + 1) * C] = picked[
                k * Lp : (k + 1) * Lp
            ].astype(BF16)

        def beside(ref, k, bin_at):
            a = gelu(ref[k, pl.ds(at, 1), :] * scale + offset)
            here = (row1 + bin_at < valid) & (row1 + (s * L + bin_at) >= 0)
            return jnp.where(here, a, 0.0).astype(BF16).astype(F32)

        l0, l1 = beside(hl, 0, -2), beside(hl, 1, -1)
        r0, r1 = beside(hr, 0, L), beside(hr, 1, L + 1)
        top, end = w * Lp, (w + 1) * Lp
        for k, add in ((0, l0 + l1), (1, l1)):
            X5[top : top + 16, k * C : (k + 1) * C] = (
                picked[k * Lp : k * Lp + 16] + jnp.where(row16 == 0, add, 0.0)
            ).astype(BF16)
        for k, add in ((3, r0), (4, r0 + r1)):
            X5[end - 16 : end, k * C : (k + 1) * C] = (
                picked[(k + 1) * Lp - 16 : (k + 1) * Lp] + jnp.where(row16 == 15, add, 0.0)
            ).astype(BF16)

    nc = 256
    rowp = rows_of((Lp, nc))
    for n in range(C // nc):
        cols = slice(n * nc, (n + 1) * nc)
        y = 0.5 * mm(X5[...], w_ref[:, cols])
        s0 = jnp.zeros((1, nc), F32)
        s1 = jnp.zeros((1, nc), F32)
        for w in range(wb):
            at = t * wb + w
            valid = lens[i * plan.nw + at] - s * Lp
            v = y[w * Lp : (w + 1) * Lp]
            x2[w, :, cols] = v
            edge[0, at, :, cols] = v[:EDGE].astype(BF16)
            edge[1, at, :, cols] = v[Lp - EDGE :].astype(BF16)
            v = jnp.where(rowp < valid, v, 0.0)
            s0 = s0 + jnp.sum(v, axis=0, keepdims=True)
            s1 = s1 + jnp.sum(v * v, axis=0, keepdims=True)
        acc[0:1, cols] += s0
        acc[1:2, cols] += s1

    @pl.when(first_step())
    def _():
        meet(peers.count - 1)
        gather.chips_start()

    halo.start(t)

    @pl.when(last_step())
    def _():
        link[0][...] = acc[...]
        peers.start(link)
        gather.pair_start()
        sums[...] = peers.finish(link)
        halo.finish()
        gather.pair_finish()


def dilated_kernel(plan, lens, x2, lo, hi, w_ref, stats, par,
                   Y3, c2, low, high, sums, ext, wf, edge, acc, halo_sems, *link):
    t = pl.program_id(0)
    peers = group_peers(plan)
    halo = Halo(plan, edge, low, high, halo_sems, plan.steps)
    s, z, i, h = plan.place()
    Lp, C, H, wb = plan.Lp, plan.C, plan.H, plan.wb

    @pl.when(first_step())
    def _():
        peers.greet()
        acc[...] = jnp.zeros_like(acc)
        for k in range(plan.T2):
            for c in range(2):
                at = k * C + c * (C // 2)
                wf[:, at : at + C // 2] = w_ref[c, k]

    mean, rho = norm_of(stats[...], total_of(lens))
    scale = par[0:1] * rho
    offset = par[1:2] - mean * scale
    rows = rows_of((Lp, C))
    rowe = rows_of((EDGE, C))

    rowh = rows_of((Lp, H))
    sums0, sums1 = jnp.zeros((8, H), F32), jnp.zeros((8, H), F32)
    nh = min(2, wb)
    for first in range(0, wb, wb // nh):
        span = range(first, first + wb // nh)
        for w in span:
            valid = lens[i * plan.nw + t * wb + w] - s * Lp
            a = jnp.where(rows < valid, gelu(x2[w] * scale + offset), 0.0)
            al = gelu(lo[w].astype(F32) * scale + offset)
            al = jnp.where((rowe - EDGE < valid) & (s > 0), al, 0.0)
            ah = gelu(hi[w].astype(F32) * scale + offset)
            ah = jnp.where(rowe + Lp < valid, ah, 0.0)
            ext[w, 0:EDGE] = al
            ext[w, EDGE : EDGE + Lp] = a
            ext[w, EDGE + Lp :] = ah
            top, end = w * Lp, (w + 1) * Lp
            Y3[top:end, 0:C] = ext[w, EDGE - DIL : EDGE - DIL + Lp].astype(BF16)
            Y3[top:end, C : 2 * C] = a.astype(BF16)
            Y3[top:end, 2 * C : 3 * C] = ext[w, EDGE + DIL : EDGE + DIL + Lp].astype(BF16)
        y = mm_nt(Y3[first * Lp : (first + wb // nh) * Lp], wf[...])
        for w in span:
            at = t * wb + w
            valid = lens[i * plan.nw + at] - s * Lp
            v = y[(w - first) * Lp : (w - first + 1) * Lp]
            c2[w] = v
            edge[0, at] = v[:EDGE].astype(BF16)
            edge[1, at] = v[Lp - EDGE :].astype(BF16)
            v = jnp.where(rowh < valid, v, 0.0)
            sums0 = sums0 + fold(v)
            sums1 = sums1 + fold(v * v)
    acc[0:1, 0:H] += unfold(sums0)
    acc[1:2, 0:H] += unfold(sums1)

    @pl.when(first_step())
    def _():
        meet(peers.count - 1)

    halo.start(t)

    @pl.when(last_step())
    def _():
        link[0][...] = acc[...]
        peers.start(link)
        sums[...] = peers.finish(link)[:, 0:H]
        halo.finish()


def point_kernel(plan, lens, c2, x2, cot, w_ref, pb, stats, par,
                 res, dz, pgrad, low, high, sums, bsum,
                 pw, a3s, dos, pacc, edge, acc, halo_sems, *link):
    t = pl.program_id(0)
    peers = group_peers(plan)
    halo = Halo(plan, edge, low, high, halo_sems, plan.steps)
    s, z, i, h = plan.place()
    Lp, C, H, wb, cs = plan.Lp, plan.C, plan.H, plan.wb, plan.cs

    @pl.when(first_step())
    def _():
        peers.greet()
        acc[...] = jnp.zeros_like(acc)
        pacc[...] = jnp.zeros_like(pacc)
        for c in range(2):
            pw[:, c * (C // 2) : (c + 1) * (C // 2)] = w_ref[c, 0]

    mean, rho = norm_of(stats[...], total_of(lens))
    scale = par[3:4, 0:H] * rho
    offset = par[4:5, 0:H] - mean * scale
    shift = -mean * rho
    rowc = rows_of((Lp, C))
    rowh = rows_of((Lp, H))

    bias = jnp.zeros((8, C), F32)
    for w in range(wb):
        valid = lens[i * plan.nw + t * wb + w] - s * Lp
        d = jnp.where(rowc < valid, cot[w].astype(F32), 0.0)
        bias = bias + fold(d)
        dos[w * Lp : (w + 1) * Lp] = d.astype(BF16)
    da = mm_nt(dos[...], pw[...])
    s0, s1 = jnp.zeros((8, H), F32), jnp.zeros((8, H), F32)
    for w in range(wb):
        at = t * wb + w
        valid = lens[i * plan.nw + at] - s * Lp
        top, end = w * Lp, (w + 1) * Lp
        v = c2[w]
        act, slope = gelu_both(v * scale + offset)
        a3s[top:end] = jnp.where(rowh < valid, act, 0.0).astype(BF16)
        dzw = da[top:end] * slope
        dz[w] = dzw
        edge[0, at] = dzw[:EDGE].astype(BF16)
        edge[1, at] = dzw[Lp - EDGE :].astype(BF16)
        s0 = s0 + fold(dzw)
        s1 = s1 + fold(dzw * (v * rho + shift))
    y = mm(a3s[...], w_ref[h, 0])
    pacc[...] += mm_tn(a3s[...], dos[...])
    rowr = rows_of((Lp, y.shape[1]))
    for w in range(wb):
        valid = lens[i * plan.nw + t * wb + w] - s * Lp
        r = x2[w] + y[w * Lp : (w + 1) * Lp] + pb[2:3]
        r = jnp.where(rowr < valid, r, 0.0).T.astype(BF16)
        for k in range(plan.g):
            res[k, w] = r[k * cs : (k + 1) * cs]
    acc[0:1, 0:H] += unfold(s0)
    acc[0:1, H : 2 * H] += unfold(s1)
    acc[1:2] += unfold(bias)

    @pl.when(first_step())
    def _():
        meet(peers.count - 1)

    halo.start(t)

    @pl.when(last_step())
    def _():
        link[0][...] = acc[...]
        peers.start(link)
        rows = pl.ds(pl.multiple_of(h * plan.Hh, 16), plan.Hh)
        pgrad[...] = pacc[rows].astype(BF16)
        got = peers.finish(link)
        sums[0:1] = got[0:1, 0:H]
        sums[1:2] = got[0:1, H : 2 * H]
        bsum[...] = got[1:2]
        halo.finish()


def dilated_back_kernel(plan, lens, c2, clo, chi, dz3, zlo, zhi, x2, Y3, w_ref,
                        stats3, sums3, stats2, par, pgrad, res,
                        dz2, grads, low, high, sums, res_got,
                        ext, Z3, wt, wacc, edge, acc, bulk_sems, halo_sems, *link):
    t = pl.program_id(0)
    peers = group_peers(plan)
    halo = Halo(plan, edge, low, high, halo_sems, 1)
    s, z, i, h = plan.place()
    Lp, C, H, wb, nw, g = plan.Lp, plan.C, plan.H, plan.wb, plan.nw, plan.g

    def bulk(off, n):
        to = lax.rem(i + off, g)
        rows = pl.ds(n * wb, wb)
        return pltpu.make_async_remote_copy(
            src_ref=res.at[to, rows],
            dst_ref=res_got.at[off, rows],
            send_sem=bulk_sems.at[0, off, n],
            recv_sem=bulk_sems.at[1, off, n],
            device_id=(s, h * g + to),
            device_id_type=MESH,
        )

    parts = [(off, n) for off in range(1, g) for n in range(plan.steps)]

    @pl.when(first_step())
    def _():
        peers.greet()
        acc[...] = jnp.zeros_like(acc)
        wacc[...] = jnp.zeros_like(wacc)
        for k in range(plan.T2):
            for c in range(2):
                cols = slice(c * (C // 2), (c + 1) * (C // 2))
                wt[k * H : (k + 1) * H, cols] = w_ref[c, k]

        meet(peers.count - 1)
        for part in parts:
            bulk(*part).start()

    total = total_of(lens)
    mean3, rho3 = norm_of(stats3[...], total)
    gr3 = par[3:4, 0:H] * rho3
    sg3 = sums3[0:1] / total
    gg3 = sums3[1:2] / total
    mean2, rho2 = norm_of(stats2[...], total)
    scale2 = par[0:1] * rho2
    offset2 = par[1:2] - mean2 * scale2
    rowh = rows_of((Lp, H))
    rowe = rows_of((EDGE, H))
    rowc = rows_of((Lp, C))

    by_v = -gr3 * rho3 * gg3
    by_1 = gr3 * (mean3 * rho3 * gg3 - sg3)
    shift2 = -mean2 * rho2

    def back(dz, v):
        return gr3 * dz + by_v * v + by_1

    for w in range(wb):
        valid = lens[i * nw + t * wb + w] - s * Lp
        d = jnp.where(rowh < valid, back(dz3[w], c2[w]), 0.0)
        dl = back(zlo[w].astype(F32), clo[w].astype(F32))
        dl = jnp.where((rowe - EDGE < valid) & (s > 0), dl, 0.0)
        dh = back(zhi[w].astype(F32), chi[w].astype(F32))
        dh = jnp.where(rowe + Lp < valid, dh, 0.0)
        ext[w, 0:EDGE] = dl
        ext[w, EDGE : EDGE + Lp] = d
        ext[w, EDGE + Lp :] = dh
        top, end = w * Lp, (w + 1) * Lp
        Z3[top:end, 0:H] = ext[w, EDGE + DIL : EDGE + DIL + Lp].astype(BF16)
        Z3[top:end, H : 2 * H] = d.astype(BF16)
        Z3[top:end, 2 * H : 3 * H] = ext[w, EDGE - DIL : EDGE - DIL + Lp].astype(BF16)

    y = mm(Z3[...], wt[...])

    wacc[...] += mm_tn(Z3[:, H : 2 * H], Y3[...])
    s0, s1 = jnp.zeros((8, C), F32), jnp.zeros((8, C), F32)
    for w in range(wb):
        at = t * wb + w
        valid = lens[i * nw + at] - s * Lp
        v = x2[w]
        dzw = y[w * Lp : (w + 1) * Lp] * gelu_slope(v * scale2 + offset2)
        dzw = jnp.where(rowc < valid, dzw, 0.0)
        dz2[w] = dzw
        edge[0, pl.ds(at, 1)] = dzw[0:1]
        edge[1, pl.ds(at, 1)] = dzw[Lp - 1 : Lp]
        s0 = s0 + fold(dzw)
        s1 = s1 + fold(dzw * (v * rho2 + shift2))
    acc[0:1] += unfold(s0)
    acc[1:2] += unfold(s1)

    @pl.when(last_step())
    def _():
        link[0][...] = acc[...]
        peers.start(link)
        halo.start(0)

    @pl.when(last_step())
    def _():
        rows = pl.ds(pl.multiple_of(h * plan.Hh, 16), plan.Hh)
        grads[:, 0 : plan.T2 * C] = wacc[rows].astype(BF16)
        grads[:, plan.T2 * C :] = pgrad[...]
        sums[...] = peers.finish(link)
        halo.finish()
        for part in parts:
            bulk(*part).wait()


class Reduction:
    SEMS = 3

    def __init__(self, plan, out, give, mine, got, mid, spread, half, mate, sems):
        self.plan, self.out = plan, out
        self.give, self.mine, self.got, self.mid, self.spread = give, mine, got, mid, spread
        self.half, self.mate = half, mate
        self.sems = sems
        self.s, self.z, self.i, self.h = plan.place()
        self.c = lax.rem(self.s, 2)
        self.m = lax.div(self.s, 2)
        self.chips = plan.chips

    @staticmethod
    def scratch(plan):
        taps, wide = plan.T1 + 2, plan.C // 2
        full = (taps, plan.chips, plan.g, plan.rb, wide)
        part = (taps, plan.g, plan.rb, wide)
        return [
            pltpu.VMEM((taps, 2, plan.chips, plan.rb, wide), BF16),
            *[pltpu.VMEM(full, BF16)] * 5,
            *[pltpu.VMEM(part, BF16)] * 2,
            pltpu.SemaphoreType.DMA((2, taps, Reduction.SEMS + 2 * plan.chips + plan.g)),
        ]

    def copy(self, src, dst, tap, sem, device):
        return pltpu.make_async_remote_copy(
            src_ref=src,
            dst_ref=dst,
            send_sem=self.sems.at[0, tap, sem],
            recv_sem=self.sems.at[1, tap, sem],
            device_id=device,
            device_id_type=MESH,
        )

    def pair(self):
        return (2 * self.m + (1 - self.c), self.z)

    def chip(self, off):
        return lax.rem(self.m + off, self.chips)

    def phase0(self, k):
        return self.copy(self.give.at[k], self.got.at[k], k, 0, self.pair())

    def phase1(self, k, off, at):
        to = self.chip(off)
        dst = self.spread.at[k, at]
        return self.copy(self.mid.at[k, to], dst, k, 1 + off, (2 * to + self.c, self.z))

    def phase2(self, k, off):
        to = lax.rem(self.i + off, self.plan.g)
        device = (self.s, self.h * self.plan.g + to)
        return self.copy(
            self.half.at[k, to], self.mate.at[k, off], k, 1 + self.chips + off, device
        )

    def phase3(self, k, off, at):
        to = self.chip(off)
        sem = 1 + self.chips + self.plan.g + off
        src, dst = self.out.at[k, self.c, self.m], self.out.at[k, self.c, at]
        return self.copy(src, dst, k, sem, (2 * to + self.c, self.z))

    def phase4(self, k, c):
        return self.copy(self.out.at[k, c], self.out.at[k, c], k, 1, self.pair())

    def put(self, k, rows):
        wide = self.plan.C // 2
        for j in range(self.plan.g):
            for m in range(self.chips):
                v = rows(j, m)
                left, right = v[:, :wide], v[:, wide:]
                self.mine[k, m, j] = jnp.where(self.c == 0, left, right).astype(BF16)
                self.give[k, m, j] = jnp.where(self.c == 0, right, left).astype(BF16)
        self.phase0(k).start()

    def step1(self, k):
        self.phase0(k).wait()
        self.mid[k] = (self.mine[k].astype(F32) + self.got[k].astype(F32)).astype(BF16)
        for off in range(1, self.chips):
            self.phase1(k, off, self.m).start()

    def step2(self, k):
        for off in range(1, self.chips):
            self.phase1(k, off, self.m).wait_send()
            self.phase1(k, off, self.chip(self.chips - off)).wait_recv()
        self.spread[k, self.m] = self.mid[k, self.m]
        v = self.spread[k, 0].astype(F32)
        for n in range(1, self.chips):
            v = v + self.spread[k, n].astype(F32)
        self.half[k] = v.astype(BF16)
        for off in range(1, self.plan.g):
            self.phase2(k, off).start()

    def step3(self, k):
        for off in range(1, self.plan.g):
            self.phase2(k, off).wait()
        v = self.half[k, self.i].astype(F32)
        for off in range(1, self.plan.g):
            v = v + self.mate[k, off].astype(F32)
        self.out[k, self.c, self.m] = v.astype(BF16)
        for off in range(1, self.chips):
            self.phase3(k, off, self.m).start()

    def step4(self, k):
        for off in range(1, self.chips):
            self.phase3(k, off, self.m).wait_send()
            self.phase3(k, off, self.chip(self.chips - off)).wait_recv()
        self.phase4(k, self.c).start()

    def step5(self, k):
        self.phase4(k, self.c).wait_send()
        self.phase4(k, 1 - self.c).wait_recv()

    def stages(self):
        return [self.step1, self.step2, self.step3, self.step4]


def tail_kernel(plan, lens, dz2, zlo, zhi, x2, lo, hi, cot, hl, hr, x, X5, taps, grads,
                stats2, sums2, par, stats1, gain1, shift1,
                gz, gz_got, sums, summed,
                ext, D3, D0T, wcat, pick, eye, cols, y, part, acc, bulk_sems, *rest):
    t = pl.program_id(0)
    s, z, i, h = plan.place()
    L, Lp, C, wb, g, nw = plan.L, plan.Lp, plan.C, plan.wb, plan.g, plan.nw
    Ch, cs, T1 = plan.Ch, plan.cs, plan.T1
    M = wb * Lp
    nD = plan.steps
    last = nD + T1 - 1
    peers = group_peers(plan)
    red = Reduction(plan, *rest[:9])
    link = rest[9:]

    def bulk(step, off, n):
        to = lax.rem(i + off, g)
        n2 = wb // 2
        return pltpu.make_async_remote_copy(
            src_ref=part.at[step, to, pl.ds(n * n2, n2)],
            dst_ref=gz_got.at[off, pl.ds(step * wb + n * n2, n2)],
            send_sem=bulk_sems.at[0, step, off, n],
            recv_sem=bulk_sems.at[1, step, off, n],
            device_id=(s, h * g + to),
            device_id_type=MESH,
        )

    others = [(off, n) for off in range(1, g) for n in range(2)]

    def send(step):
        for other in others:
            bulk(step, *other).start()

    def when(at):
        return pl.when(t == min(at, last))

    @when(0)
    def _():
        peers.greet()
        acc[...] = jnp.zeros_like(acc)
        pick[...] = pick_matrix(L)
        eye[...] = eye_matrix(Ch, Ch, 0)
        mean, rho = norm_of(stats1[...], 2.0 * total_of(lens))
        scale = gain1[...] * rho
        for k, row in enumerate((scale, shift1[...] - mean * scale, rho, -mean * rho)):
            cols[k] = column(row, L)
        w = [taps[k].astype(F32) for k in range(5)]
        for r, parts in enumerate(
            ((w[0], w[1] + w[2], w[3] + w[4]), (w[0] + w[1], w[2] + w[3], w[4]))
        ):
            for k, v in enumerate(parts):
                wcat[r * Ch : (r + 1) * Ch, k * C : (k + 1) * C] = v.astype(BF16)

    @pl.when(t < nD)
    def _():
        total = total_of(lens)
        mean, rho = norm_of(stats2[...], total)
        gr = par[0:1] * rho
        sg = sums2[0:1] / total
        gg = sums2[1:2] / total
        rowc = rows_of((Lp, C))
        row1 = rows_of((1, C))

        by_dz = 0.5 * gr
        by_v = -0.5 * gr * rho * gg
        by_1 = 0.5 * gr * (mean * rho * gg - sg)
        lanes = lanes_of((Ch, L))

        def back(dout, dz, v):
            return 0.5 * dout + by_dz * dz + by_v * v + by_1

        def grad_of(w):
            at = t * wb + w
            valid = lens[i * nw + at] - s * Lp
            d = back(cot[w].astype(F32), dz2[w], x2[w])
            d = jnp.where(rowc < valid, d, 0.0)
            one = pl.ds(at, 1)
            dl = back(hl[2, one, :], zlo[one, :], lo[w, EDGE - 1 : EDGE].astype(F32))
            dl = jnp.where((row1 - 1 < valid) & (s > 0), dl, 0.0)
            dh = back(hr[2, one, :], zhi[one, :], hi[w, 0:1].astype(F32))
            dh = jnp.where(row1 + Lp < valid, dh, 0.0)
            ext[w, 7:8] = dl
            ext[w, 8 : 8 + Lp] = d
            ext[w, 8 + Lp : 9 + Lp] = dh
            top, end = w * Lp, (w + 1) * Lp
            D3[top:end, 0:C] = ext[w, 9 : 9 + Lp].astype(BF16)
            D3[top:end, C : 2 * C] = d.astype(BF16)
            D3[top:end, 2 * C : 3 * C] = ext[w, 7 : 7 + Lp].astype(BF16)

        def through(w):
            valid = 2 * lens[i * nw + t * wb + w] - s * L
            top, end = w * Lp, (w + 1) * Lp
            v = mm_nt(eye[...], x[w])
            da = jnp.concatenate([y[0:Ch, top:end], y[Ch:, top:end]], axis=1)
            da = mm(da.astype(BF16), pick[...])
            dzw = da * gelu_slope(v * cols[0] + cols[1])
            dzw = jnp.where(lanes < valid, dzw, 0.0)
            acc[0] += dzw
            acc[1] += dzw * (v * cols[2] + cols[3])
            dzw = dzw.astype(BF16)
            for k in range(g):
                part[t, k, w] = dzw[k * cs : (k + 1) * cs]

        nh = 2 if wb % 2 == 0 and wb * Lp // 2 % 128 == 0 else 1
        n = wb // nh
        for hf in range(nh):
            for w in range(hf * n, (hf + 1) * n):
                grad_of(w)
            rows = slice(hf * n * Lp, (hf + 1) * n * Lp)
            y[:, rows] = mm_nt(wcat[...], D3[rows])
        half = D3[:, pl.ds(pl.multiple_of(C + h * Ch, 128), Ch)]
        D0T[:, pl.ds(pl.multiple_of(t * M, 128), M)] = half.T
        for w in range(wb):
            through(w)
        gz[...] = part[t, i]

    @when(0)
    def _():
        meet(peers.count - 1)
        hs = plan.H // plan.nz
        rb = plan.rb
        for u in range(2):

            def rows(j, m, u=u):
                side, r = m * rb // hs, m * rb % hs
                at = (2 * side + u) * C
                return grads[j * hs + r : j * hs + r + rb, at : at + C].astype(F32)

            red.put(T1 + u, rows)

    @pl.when(t < nD)
    def _():
        send(t)

    stages = red.stages()
    for n, stage in enumerate(stages[:2]):

        @when(1 + n)
        def _():
            for u in range(2):
                stage(T1 + u)

    @when(nD - 1)
    def _():
        packet = link[0]
        packet[...] = jnp.zeros_like(packet)
        packet[0:1, 0:Ch] = jnp.sum(acc[0].T, axis=0, keepdims=True)
        packet[1:2, 0:Ch] = jnp.sum(acc[1].T, axis=0, keepdims=True)
        peers.start(link)

    @pl.when(t >= nD)
    def _():
        k = t - nD
        y[0:Ch, 0:C] = mm(D0T[...], X5[...])
        rb = plan.rb
        red.put(k, lambda j, m: y[j * cs + m * rb : j * cs + (m + 1) * rb, 0:C])
        for n, stage in enumerate(stages[:2]):
            pl.when(k > n)(partial(stage, k - 1 - n))

    @when(last)
    def _():
        for n, stage in enumerate(stages[:2]):
            for k in range(T1 - 1 - n, T1):
                stage(k)
        for stage in stages[2:]:
            for k in (T1, T1 + 1, *range(T1)):
                stage(k)
        sums[...] = peers.finish(link)[:, 0:Ch]
        for k in range(T1 + 2):
            red.step5(k)
        summed[...] = red.out[...]
        for step in range(nD):
            for other in others:
                bulk(step, *other).wait()


def input_grad_kernel(plan, lens, x, gz, gz_got, stats, sums, gain, res, res_got, summed,
                      sums2, sums3, bsum,
                      out, out_result, conv_grad, dil_grad, point_grad,
                      g1, b1, g2, b2, g3, b3, pb, eye, cols, xt):
    t = pl.program_id(0)
    s, z, i, h = plan.place()
    L, Ch, cs, wb = plan.L, plan.Ch, plan.cs, plan.wb
    mine = pl.ds(pl.multiple_of(i * cs, 16), cs)

    @pl.when(first_step())
    def _():
        n = 2.0 * total_of(lens)
        mean, rho = norm_of(stats[...], n)
        gr = gain[...] * rho
        gg = sums[1:2] / n * rho
        for k, row in enumerate((gr, -gr * gg, gr * (mean * gg - sums[0:1] / n))):
            xt[...] = column(row, L)
            cols[k] = xt[mine]
        eye[...] = eye_matrix(cs, Ch, i * cs)

        def mine_of(src, at, which, count, *dsts):
            n = dsts[0].shape[1]
            for k in range(count):

                @pl.when(which == k)
                def _():
                    for dst, r in zip(dsts, at):
                        dst[...] = src[r : r + 1, k * n : (k + 1) * n]

        mine_of(sums, (1, 0), i, plan.g, g1, b1)
        mine_of(sums2, (1, 0), z, plan.nz, g2, b2)
        mine_of(sums3, (1, 0), z, plan.nz, g3, b3)
        mine_of(bsum, (0,), z, plan.nz, pb)

    own = lax.div(t, plan.steps) == i
    for w in range(wb):
        out_result[w] = jnp.where(own, res[0, w].astype(F32), res_got[0, w].astype(F32)).astype(BF16)

    C, T1, hs, rb, wide = plan.C, plan.T1, plan.H // plan.nz, plan.rb, plan.C // 2
    count = plan.NW // wb
    turns = min(count, plan.chips)
    per, every = plan.chips // turns, count // turns

    def spread(turn):
        for n in range(per):
            m = turn * per + n
            side, r = m * rb // hs, m * rb % hs
            for c in range(2):
                at = slice(c * wide, (c + 1) * wide)
                for k in range(T1):
                    conv_grad[k, n * rb : (n + 1) * rb, at] = summed[k, c, n].astype(F32)
                for u in range(2):
                    v = summed[T1 + u, c, n].astype(F32)
                    if 2 * side + u < plan.T2:
                        dil_grad[2 * side + u, r : r + rb, at] = v
                    else:
                        point_grad[r : r + rb, at] = v

    for turn in range(turns):
        pl.when(t == turn * every)(partial(spread, turn))

    lanes = lanes_of((cs, L))
    for w in range(wb):
        valid = 2 * lens[t * wb + w] - s * L
        v = mm_nt(eye[...], x[w])
        dz = jnp.where(own, gz[w].astype(F32), gz_got[0, w].astype(F32))
        r = cols[0] * dz + v * cols[1] + cols[2]
        out[w] = jnp.where(lanes < valid, r, 0.0).astype(BF16)


def call(kernel, plan, name, steps, ins, outs, scratch, flops, nbytes, cid=None):
    extra = {} if cid is None else dict(collective_id=cid, has_side_effects=True)
    return pl.pallas_call(
        partial(kernel, plan),
        grid=(steps,),
        in_specs=[SMEM] + [spec for spec, _ in ins],
        out_specs=[spec for spec, _, _ in outs],
        out_shape=[jax.ShapeDtypeStruct(shape, dtype) for _, shape, dtype in outs],
        scratch_shapes=scratch,
        compiler_params=pltpu.CompilerParams(vmem_limit_bytes=VMEM_LIMIT, **extra),
        cost_estimate=pl.CostEstimate(
            flops=int(flops), bytes_accessed=int(nbytes), transcendentals=0
        ),
        name=name,
    )


def per_device(
    inputs,
    lengths,
    input_gain,
    input_shift,
    conv_weight,
    branch_gain,
    branch_shift,
    dilated_tap_weight,
    mixer_gain,
    mixer_shift,
    point_weight,
    point_bias,
    cotangent,
):
    NW, L, C = inputs.shape
    Lp = L // 2
    nz = lax.axis_size("ch")
    R = 2
    plan = Plan(
        ns=lax.axis_size("seq"),
        nz=nz,
        R=R,
        NW=NW,
        L=L,
        C=C,
        H=mixer_gain.shape[0] * nz,
        T1=conv_weight.shape[0],
        T2=dilated_tap_weight.shape[0],
        wb=min(NW * R // nz, max(1, 512 // Lp)),
    )
    g, nw, cs, Ch, H, Hh, wb = plan.g, plan.nw, plan.cs, plan.Ch, plan.H, plan.Hh, plan.wb
    T1, T2, steps = plan.T1, plan.T2, plan.steps
    M = wb * Lp
    hs = H // nz
    lens = lengths.astype(jnp.int32)
    gain1 = input_gain.reshape(1, C)
    shift1 = input_shift.reshape(1, C)

    def row(a):
        return a.reshape(1, a.shape[0])

    def grp():
        return lax.rem(lax.axis_index("ch"), g)

    def half():
        return lax.div(lax.axis_index("ch"), g)

    def core():
        return lax.rem(lax.axis_index("seq"), 2)

    def chip4():
        return lax.div(lax.axis_index("seq"), plan.ns // 4)

    def whole(*shape):
        return pl.BlockSpec(shape, lambda t: (0,) * len(shape), pipeline_mode=pl.Buffered(1))

    def const(*shape):
        return pl.BlockSpec(shape, lambda t: (0,) * len(shape))

    def win(*shape):
        return pl.BlockSpec(shape, lambda t: (t,) + (0,) * (len(shape) - 1))

    def arg_win(n, width):
        return pl.BlockSpec((wb, n, width), lambda t: (grp() * steps + t, 0, 0))

    def ins(*pairs):
        return [p for p in pairs]

    nw1 = NW // nz
    wb1 = min(nw1, wb)

    def edge_spec(n):
        return pl.BlockSpec(
            (nw, 16, C), lambda t: (grp(), n, 0), pipeline_mode=pl.Buffered(1)
        )

    pairs = ins(
        (
            pl.BlockSpec((wb1, L, C), lambda t: (lax.axis_index("ch") * (nw1 // wb1) + t, 0, 0)),
            inputs,
        ),
        (edge_spec(0), inputs),
        (edge_spec(L // 16 - 1), inputs),
        (edge_spec(0), cotangent),
        (edge_spec(Lp // 16 - 1), cotangent),
        (whole(1, cs), row(branch_gain)),
        (whole(1, cs), row(branch_shift)),
        (whole(1, cs), row(point_bias)),
        (whole(1, H // nz), row(mixer_gain)),
        (whole(1, H // nz), row(mixer_shift)),
        (
            pl.BlockSpec((1, hs, C // 2), lambda t: (jnp.minimum(chip4(), T2 - 1), 0, core())),
            jnp.swapaxes(dilated_tap_weight, 1, 2),
        ),
        (pl.BlockSpec((hs, C // 2), lambda t: (0, core())), point_weight),
    )
    plane, line, group = plane_peers(plan), line_peers(plan), group_peers(plan)
    stats1, par, hl, hr, stripe = call(
        lambda plan, *refs: moments_kernel(plan, nw1, wb1, *refs),
        plan,
        "moments",
        nw1 // wb1,
        pairs,
        [
            (const(2, C), (2, C), F32),
            (const(8, C), (8, C), F32),
            (ANY, (3, nw, C), F32),
            (ANY, (3, nw, C), F32),
            (ANY, (nz, hs, C // 2), BF16),
        ],
        [
            pltpu.VMEM((2, 8, C), F32),
            pltpu.VMEM((2, 3, nw, C), F32),
            pltpu.VMEM((hs, C // 2), BF16),
            pltpu.SemaphoreType.DMA((2, nz)),
        ]
        + halo_scratch(1)
        + plane.scratch(2, C)
        + line.scratch(3, C),
        0,
        nw1 * L * C * 2,
        cid=1,
    )(lens, *[a for _, a in pairs])

    pairs = ins(
        (arg_win(L, C), inputs),
        (whole(3, nw, C), hl),
        (whole(3, nw, C), hr),
        (whole(T1 * C, C), conv_weight.reshape(T1 * C, C)),
        (whole(2, C), stats1),
        (whole(1, C), gain1),
        (whole(1, C), shift1),
        (ANY, stripe),
    )
    X5, x2, lo2, hi2, stats2, full = call(
        conv_kernel,
        plan,
        "conv",
        steps,
        pairs,
        [
            (win(M, T1 * C), (nw * Lp, T1 * C), BF16),
            (win(wb, Lp, C), (nw, Lp, C), F32),
            (ANY, (nw, EDGE, C), BF16),
            (ANY, (nw, EDGE, C), BF16),
            (const(2, C), (2, C), F32),
            (ANY, (2, T2 + 1, nz, hs, C // 2), BF16),
        ],
        [
            pltpu.VMEM((T1 * Lp, L), BF16),
            pltpu.VMEM((2, nw, EDGE, C), BF16),
            pltpu.VMEM((2, C), F32),
            pltpu.SemaphoreType.DMA((2, plan.ns // 2 + 1, Gather.PARTS)),
        ]
        + halo_scratch(steps)
        + group.scratch(2, C),
        2 * nw * Lp * T1 * C * C,
        nw * Lp * C * 20,
        cid=2,
    )(lens, *[a for _, a in pairs])

    full = full.reshape(2, T2 + 1, H, C // 2)
    taps_spec = whole(2, T2, H, C // 2)
    pw_spec = pl.BlockSpec(
        (2, 1, H, C // 2), lambda t: (0, T2, 0, 0), pipeline_mode=pl.Buffered(1)
    )

    pairs = ins(
        (win(wb, Lp, C), x2),
        (win(wb, EDGE, C), lo2),
        (win(wb, EDGE, C), hi2),
        (taps_spec, full),
        (whole(2, C), stats2),
        (whole(8, C), par),
    )
    Y3, c2, lo3, hi3, stats3 = call(
        dilated_kernel,
        plan,
        "dilated",
        steps,
        pairs,
        [
            (win(M, T2 * C), (nw * Lp, T2 * C), BF16),
            (win(wb, Lp, H), (nw, Lp, H), F32),
            (ANY, (nw, EDGE, H), BF16),
            (ANY, (nw, EDGE, H), BF16),
            (const(2, H), (2, H), F32),
        ],
        [
            pltpu.VMEM((wb, Lp + 2 * EDGE, C), F32),
            pltpu.VMEM((H, T2 * C), BF16),
            pltpu.VMEM((2, nw, EDGE, H), BF16),
            pltpu.VMEM((2, C), F32),
        ]
        + halo_scratch(steps)
        + group.scratch(2, C),
        2 * nw * Lp * T2 * C * H,
        nw * Lp * C * 12,
        cid=3,
    )(lens, *[a for _, a in pairs])

    pairs = ins(
        (win(wb, Lp, H), c2),
        (pl.BlockSpec((wb, Lp, Ch), lambda t: (t, 0, half())), x2),
        (arg_win(Lp, C), cotangent),
        (pw_spec, full),
        (pl.BlockSpec((8, Ch), lambda t: (0, half()), pipeline_mode=pl.Buffered(1)), par),
        (whole(2, H), stats3),
        (whole(8, C), par),
    )
    res, dz3, pgrad, zlo3, zhi3, sums3, bsum = call(
        point_kernel,
        plan,
        "point",
        steps,
        pairs,
        [
            (
                pl.BlockSpec((g, wb, cs, Lp), lambda t: (0, t, 0, 0)),
                (g, nw, cs, Lp),
                BF16,
            ),
            (win(wb, Lp, H), (nw, Lp, H), F32),
            (const(Hh, C), (Hh, C), BF16),
            (ANY, (nw, EDGE, H), BF16),
            (ANY, (nw, EDGE, H), BF16),
            (const(2, H), (2, H), F32),
            (const(1, C), (1, C), F32),
        ],
        [
            pltpu.VMEM((H, C), BF16),
            pltpu.VMEM((M, H), BF16),
            pltpu.VMEM((M, C), BF16),
            pltpu.VMEM((H, C), F32),
            pltpu.VMEM((2, nw, EDGE, H), BF16),
            pltpu.VMEM((2, C), F32),
        ]
        + halo_scratch(steps)
        + group.scratch(2, C),
        5 * nw * Lp * C * H,
        nw * Lp * C * 10,
        cid=4,
    )(lens, *[a for _, a in pairs])

    pairs = ins(
        (win(wb, Lp, H), c2),
        (win(wb, EDGE, H), lo3),
        (win(wb, EDGE, H), hi3),
        (win(wb, Lp, H), dz3),
        (win(wb, EDGE, H), zlo3),
        (win(wb, EDGE, H), zhi3),
        (win(wb, Lp, C), x2),
        (win(M, T2 * C), Y3),
        (taps_spec, full),
        (whole(2, H), stats3),
        (whole(2, H), sums3),
        (whole(2, C), stats2),
        (whole(8, C), par),
        (whole(Hh, C), pgrad),
        (ANY, res),
    )
    dz2, grads, zlo2, zhi2, sums2, res_got = call(
        dilated_back_kernel,
        plan,
        "dilated_back",
        steps,
        pairs,
        [
            (win(wb, Lp, C), (nw, Lp, C), F32),
            (const(Hh, (T2 + 1) * C), (Hh, (T2 + 1) * C), BF16),
            (ANY, (nw, C), F32),
            (ANY, (nw, C), F32),
            (const(2, C), (2, C), F32),
            (ANY, (g, nw, cs, Lp), BF16),
        ],
        [
            pltpu.VMEM((wb, Lp + 2 * EDGE, H), F32),
            pltpu.VMEM((M, T2 * H), BF16),
            pltpu.VMEM((T2 * H, C), BF16),
            pltpu.VMEM((H, T2 * C), F32),
            pltpu.VMEM((2, nw, C), F32),
            pltpu.VMEM((2, C), F32),
            pltpu.SemaphoreType.DMA((2, g, steps)),
        ]
        + halo_scratch(1)
        + group.scratch(2, C),
        4 * nw * Lp * T2 * C * H,
        nw * Lp * C * 20,
        cid=5,
    )(lens, *[a for _, a in pairs])

    def half_of(n):
        return pl.BlockSpec((n, Ch), lambda t: (0, half()), pipeline_mode=pl.Buffered(1))

    def early(*shape):
        return pl.BlockSpec(
            shape, lambda t: (jnp.minimum(t, steps - 1),) + (0,) * (len(shape) - 1)
        )

    chips, rb = plan.chips, plan.rb
    sshape = (T1 + 2, 2, chips, rb, C // 2)
    pairs = ins(
        (early(wb, Lp, C), dz2),
        (whole(nw, C), zlo2),
        (whole(nw, C), zhi2),
        (early(wb, Lp, C), x2),
        (early(wb, EDGE, C), lo2),
        (early(wb, EDGE, C), hi2),
        (
            pl.BlockSpec(
                (wb, Lp, C), lambda t: (grp() * steps + jnp.minimum(t, steps - 1), 0, 0)
            ),
            cotangent,
        ),
        (whole(3, nw, C), hl),
        (whole(3, nw, C), hr),
        (
            pl.BlockSpec(
                (wb, L, Ch), lambda t: (grp() * steps + jnp.minimum(t, steps - 1), 0, half())
            ),
            inputs,
        ),
        (pl.BlockSpec((nw * Lp, C), lambda t: (0, jnp.maximum(t - steps, 0))), X5),
        (
            pl.BlockSpec(
                (T1, Ch, C), lambda t: (0, half(), 0), pipeline_mode=pl.Buffered(1)
            ),
            conv_weight,
        ),
        (whole(Hh, (T2 + 1) * C), grads),
        (whole(2, C), stats2),
        (whole(2, C), sums2),
        (whole(8, C), par),
        (half_of(2), stats1),
        (half_of(1), gain1),
        (half_of(1), shift1),
    )
    gz, gz_got, sums1, summed = call(
        tail_kernel,
        plan,
        "tail",
        steps + T1,
        pairs,
        [
            (early(wb, cs, L), (nw, cs, L), BF16),
            (ANY, (g, nw, cs, L), BF16),
            (const(2, Ch), (2, Ch), F32),
            (const(*sshape), sshape, BF16),
        ],
        [
            pltpu.VMEM((wb, Lp + 16, C), F32),
            pltpu.VMEM((M, 3 * C), BF16),
            pltpu.VMEM((Ch, nw * Lp), BF16),
            pltpu.VMEM((2 * Ch, 3 * C), BF16),
            pltpu.VMEM((L, L), BF16),
            pltpu.VMEM((Ch, Ch), BF16),
            pltpu.VMEM((4, Ch, L), F32),
            pltpu.VMEM((2 * Ch, max(M, C)), F32),
            pltpu.VMEM((steps, g, wb, cs, L), BF16),
            pltpu.VMEM((2, Ch, L), F32),
            pltpu.SemaphoreType.DMA((2, steps, g, 2)),
        ]
        + Reduction.scratch(plan)
        + group.scratch(2, C),
        2 * nw * Lp * (6 + T1) * C * Ch,
        nw * Lp * C * 40,
        cid=6,
    )(lens, *[a for _, a in pairs])

    count = NW // wb
    turns = min(count, chips)

    def own_block(t):
        return jnp.where(lax.div(t, steps) == grp(), lax.rem(t, steps), 0)

    def got_slot(t):
        off = lax.rem(grp() - lax.div(t, steps) + g, g)
        return jnp.maximum(off, 1), jnp.where(off > 0, lax.rem(t, steps), 0)

    pairs = ins(
        (pl.BlockSpec((wb, L, Ch), lambda t: (t, 0, half())), inputs),
        (pl.BlockSpec((wb, cs, L), lambda t: (own_block(t), 0, 0)), gz),
        (pl.BlockSpec((1, wb, cs, L), lambda t: got_slot(t) + (0, 0)), gz_got),
        (half_of(2), stats1),
        (whole(2, Ch), sums1),
        (half_of(1), gain1),
        (pl.BlockSpec((1, wb, cs, Lp), lambda t: (grp(), own_block(t), 0, 0)), res),
        (pl.BlockSpec((1, wb, cs, Lp), lambda t: got_slot(t) + (0, 0)), res_got),
        (
            pl.BlockSpec(
                (T1 + 2, 2, chips // turns, rb, C // 2),
                lambda t: (0, 0, t * turns // count, 0, 0),
            ),
            summed,
        ),
        (whole(2, C), sums2),
        (whole(2, H), sums3),
        (whole(1, C), bsum),
    )
    outs = call(
        input_grad_kernel,
        plan,
        "input_grad",
        NW // wb,
        pairs,
        [
            (win(wb, cs, L), (NW, cs, L), BF16),
            (win(wb, cs, Lp), (NW, cs, Lp), BF16),
            (
                pl.BlockSpec((T1, cs // turns, C), lambda t: (0, t * turns // count, 0)),
                (T1, cs, C),
                F32,
            ),
            (const(T2, hs, C), (T2, hs, C), F32),
            (const(hs, C), (hs, C), F32),
        ]
        + [(const(1, n), (1, n), F32) for n in (cs, cs, cs, cs, hs, hs, cs)],
        [
            pltpu.VMEM((cs, Ch), BF16),
            pltpu.VMEM((3, cs, L), F32),
            pltpu.VMEM((Ch, L), F32),
        ],
        2 * NW * L * Ch * cs,
        NW * L * cs * 8,
    )(lens, *[a for _, a in pairs])
    grad, result, conv_grad, dil_grad, point_grad = outs[:5]
    g1, b1, g2, b2, g3, b3, pb = [a[0] for a in outs[5:]]
    return (
        jnp.swapaxes(result, 1, 2),
        jnp.swapaxes(grad, 1, 2),
        jnp.swapaxes(conv_grad, 1, 2),
        g1,
        b1,
        g2,
        b2,
        jnp.swapaxes(dil_grad, 1, 2),
        g3,
        b3,
        point_grad,
        pb,
    )


def solution(mesh):
    in_specs = (
        P(None, "seq", None),
        P(),
        P(),
        P(),
        P(),
        P("ch"),
        P("ch"),
        P(None, None, "ch"),
        P("ch"),
        P("ch"),
        P("ch", None),
        P("ch"),
        P(None, "seq", None),
    )
    out_specs = (
        P(None, "seq", "ch"),
        P(None, "seq", "ch"),
        P(None, None, "ch"),
        P("ch"),
        P("ch"),
        P("ch"),
        P("ch"),
        P(None, None, "ch"),
        P("ch"),
        P("ch"),
        P("ch", None),
        P("ch"),
    )
    return jax.shard_map(
        per_device, mesh=mesh, in_specs=in_specs, out_specs=out_specs, check_vma=False
    )
```

```python
from functools import partial
from typing import NamedTuple

import jax
import jax.numpy as jnp
from jax import lax
from jax.experimental import pallas as pl
from jax.experimental.pallas import tpu as pltpu
from jax.sharding import PartitionSpec as P

DIL = 14
EDGE = 16
EPS = 1e-05
GC0 = 0.7978845608028654
GC1 = 0.044715
F32 = jnp.float32
BF16 = jnp.bfloat16
MESH = pl.DeviceIdType.MESH
VMEM_LIMIT = 58 * 1024 * 1024
ANY = pl.BlockSpec(memory_space=pl.ANY)
SMEM = pl.BlockSpec(memory_space=pltpu.SMEM)


class Plan(NamedTuple):
    ns: int
    nz: int
    R: int
    NW: int
    L: int
    C: int
    H: int
    T1: int
    T2: int
    wb: int

    @property
    def g(self):
        return self.nz // self.R

    @property
    def nw(self):
        return self.NW // self.g

    @property
    def Lp(self):
        return self.L // 2

    @property
    def cs(self):
        return self.C // self.nz

    @property
    def Ch(self):
        return self.C // self.R

    @property
    def Hh(self):
        return self.H // self.R

    @property
    def steps(self):
        return self.nw // self.wb

    @property
    def chips(self):
        return self.ns // 2

    @property
    def rb(self):
        return self.cs // self.chips

    def place(self):
        s, z = lax.axis_index("seq"), lax.axis_index("ch")
        return s, z, lax.rem(z, self.g), lax.div(z, self.g)


def gelu(z):
    t = jnp.tanh(z * (GC0 + (GC0 * GC1) * (z * z)))
    return z * (0.5 + 0.5 * t)


def gelu_both(z):
    sq = z * z
    t = jnp.tanh(z * (GC0 + (GC0 * GC1) * sq))
    h = 0.5 + 0.5 * t
    v = z * h
    return v, h + v * (1.0 - t) * (GC0 + (3.0 * GC0 * GC1) * sq)


def gelu_slope(z):
    return gelu_both(z)[1]


def fold(v):
    return jnp.sum(v.reshape(v.shape[0] // 8, 8, v.shape[1]), axis=0)


def unfold(v):
    return jnp.sum(v, axis=0, keepdims=True)


def rows_of(shape):
    return lax.broadcasted_iota(jnp.int32, shape, 0)


def lanes_of(shape):
    return lax.broadcasted_iota(jnp.int32, shape, 1)


def total_of(lens):
    n = lens[0]
    for k in range(1, lens.shape[0]):
        n = n + lens[k]
    return n.astype(F32)


def norm_of(stats, total):
    mean = stats[0:1] / total
    square = stats[1:2] / total
    return mean, lax.rsqrt(square - mean * mean + EPS)


def column(row, n):
    return jnp.broadcast_to(row, (n, row.shape[1])).T


def mm(a, b):
    return jnp.dot(a, b, preferred_element_type=F32)


def mm_nt(a, b):
    return lax.dot_general(a, b, (((1,), (1,)), ((), ())), preferred_element_type=F32)


def mm_tn(a, b):
    return lax.dot_general(a, b, (((0,), (0,)), ((), ())), preferred_element_type=F32)


def mm_tt(a, b):
    return lax.dot_general(a, b, (((0,), (1,)), ((), ())), preferred_element_type=F32)


def eye_matrix(n, m, first):
    return jnp.where(lanes_of((n, m)) == rows_of((n, m)) + first, 1.0, 0.0).astype(BF16)


def pick_matrix(L):
    r, n = rows_of((L, L)), lanes_of((L, L))
    bin_of = 2 * r - jnp.where(r >= L // 2, L - 1, 0)
    return jnp.where(n == bin_of, 1.0, 0.0).astype(BF16)


class Peers:
    def __init__(self, count, me, device):
        self.count, self.me, self.device = count, me, device

    def other(self, off):
        return lax.rem(self.me + off, self.count)

    def greet(self, more=()):
        barrier = pltpu.get_barrier_semaphore()
        devices = [self.device(self.other(off)) for off in range(1, self.count)]
        for device in (*devices, *more):
            pl.semaphore_signal(barrier, inc=1, device_id=device, device_id_type=MESH)

    def copy(self, link, slot, off):
        packet, buf, send, recv = link
        return pltpu.make_async_remote_copy(
            src_ref=packet,
            dst_ref=buf.at[slot],
            send_sem=send.at[off],
            recv_sem=recv.at[slot],
            device_id=self.device(self.other(off)),
            device_id_type=MESH,
        )

    def start(self, link):
        for off in range(1, self.count):
            self.copy(link, self.me, off).start()

    def finish(self, link):
        packet, buf = link[:2]
        buf[self.me] = packet[...]
        for off in range(1, self.count):
            self.copy(link, self.other(off), off).wait_recv()
        acc = buf[0]
        for q in range(1, self.count):
            acc = acc + buf[q]
        for off in range(1, self.count):
            self.copy(link, self.me, off).wait_send()
        return acc

    def scratch(self, rows, width):
        return [
            pltpu.VMEM((rows, width), F32),
            pltpu.VMEM((self.count, rows, width), F32),
            pltpu.SemaphoreType.DMA((self.count,)),
            pltpu.SemaphoreType.DMA((self.count,)),
        ]


def group_peers(plan):
    s, z, i, h = plan.place()
    g = plan.g
    return Peers(plan.ns * g, s * g + i, lambda q: (lax.div(q, g), h * g + lax.rem(q, g)))


def plane_peers(plan):
    s, z, i, h = plan.place()
    return Peers(plan.ns, s, lambda q: (q, z))


def line_peers(plan):
    s, z, i, h = plan.place()
    return Peers(plan.nz, z, lambda q: (s, q))


def meet(count):
    pl.semaphore_wait(pltpu.get_barrier_semaphore(), count)


class Halo:
    def __init__(self, plan, edge, low, high, sems, parts):
        self.edge, self.low, self.high, self.sems, self.parts = edge, low, high, sems, parts
        s, z, _, _ = plan.place()
        self.left = (lax.rem(s + plan.ns - 1, plan.ns), z)
        self.right = (lax.rem(s + 1, plan.ns), z)
        self.n = low.shape[0] // parts

    def copies(self, part):
        rows = pl.ds(part * self.n, self.n)
        return [
            pltpu.make_async_remote_copy(
                src_ref=self.edge.at[side, rows],
                dst_ref=dst.at[rows],
                send_sem=self.sems.at[0, side, part],
                recv_sem=self.sems.at[1, side, part],
                device_id=dev,
                device_id_type=MESH,
            )
            for side, (dst, dev) in enumerate(((self.high, self.left), (self.low, self.right)))
        ]

    def start(self, part):
        for c in self.copies(part):
            c.start()

    def finish(self):
        for part in range(self.parts):
            for c in self.copies(part):
                c.wait()


def halo_scratch(parts):
    return [pltpu.SemaphoreType.DMA((2, 2, parts))]


class Gather:
    PARTS = 2

    def __init__(self, plan, sems, line_sems, part, stripe, full):
        self.plan, self.part, self.full, self.sems = plan, part, full, sems
        self.stripe, self.line_sems = stripe, line_sems
        self.s, self.z, self.i, self.h = plan.place()
        self.c, self.m = lax.rem(self.s, 2), lax.div(self.s, 2)
        self.chips = plan.ns // 2
        self.every = self.chips // 4
        self.tap = lax.div(self.m, self.every)
        self.owner = lax.rem(self.m, self.every) == 0
        self.rows = plan.H // plan.nz

    def others(self):
        g, nz = self.plan.g, self.plan.nz
        return [(self.s, lax.rem(self.h * g + g + r, nz)) for r in range(nz - g)]

    def copy(self, src, dst, sem, device):
        return pltpu.make_async_remote_copy(
            src_ref=src,
            dst_ref=dst,
            send_sem=self.sems.at[(0,) + sem],
            recv_sem=self.sems.at[(1,) + sem],
            device_id=device,
            device_id_type=MESH,
        )

    def line(self, off, at):
        to = lax.rem(self.z + off, self.plan.nz)
        return pltpu.make_async_remote_copy(
            src_ref=self.part,
            dst_ref=self.stripe.at[at],
            send_sem=self.line_sems.at[0, off],
            recv_sem=self.line_sems.at[1, off],
            device_id=(self.s, to),
            device_id_type=MESH,
        )

    def own_rows(self):
        return pltpu.make_async_copy(
            self.part, self.stripe.at[self.z], self.line_sems.at[0, 0]
        )

    def line_start(self):
        @pl.when(self.owner)
        def _():
            self.own_rows().start()
            for off in range(1, self.plan.nz):
                self.line(off, self.z).start()

    def line_finish(self):
        @pl.when(self.owner)
        def _():
            self.own_rows().wait()
            for off in range(1, self.plan.nz):
                self.line(off, self.z).wait_send()
                at = lax.rem(self.z + self.plan.nz - off, self.plan.nz)
                self.line(off, at).wait_recv()

    def half(self, ref, n):
        rows = self.plan.nz // self.PARTS
        return ref.at[pl.ds(n * rows, rows)]

    def own_stripe(self):
        return pltpu.make_async_copy(
            self.stripe, self.full.at[self.c, self.tap], self.sems.at[0, 0, 0]
        )

    def chip(self, off, n):
        to = lax.rem(self.m + off, self.chips)
        return self.copy(
            self.half(self.stripe, n),
            self.half(self.full.at[self.c, self.tap], n),
            (off, n),
            (2 * to + self.c, self.z),
        )

    def arrival(self, k, off, n):
        whole = self.half(self.full.at[self.c, k], n)
        return self.copy(whole, whole, (off, n), (2 * k * self.every + self.c, self.z))

    def pair(self, c, n):
        part = self.full.at[c, pl.ds(2 * n, 2)]
        return self.copy(part, part, (self.chips, n), (2 * self.m + 1 - self.c, self.z))

    def chips_start(self):
        @pl.when(self.owner)
        def _():
            self.own_stripe().start()
            for off in range(1, self.chips):
                for n in range(self.PARTS):
                    self.chip(off, n).start()

    def pair_start(self):
        for k in range(4):
            off = lax.rem(self.m - k * self.every + self.chips, self.chips)

            @pl.when(off != 0)
            def _():
                for n in range(self.PARTS):
                    self.arrival(k, off, n).wait_recv()

        @pl.when(self.owner)
        def _():
            self.own_stripe().wait()
            for off in range(1, self.chips):
                for n in range(self.PARTS):
                    self.chip(off, n).wait_send()

        for n in range(self.PARTS):
            self.pair(self.c, n).start()

    def pair_finish(self):
        for n in range(self.PARTS):
            self.pair(self.c, n).wait_send()
            self.pair(1 - self.c, n).wait_recv()


def first_step():
    return pl.program_id(0) == 0


def last_step():
    return pl.program_id(0) == pl.num_programs(0) - 1


def moments_kernel(plan, nw1, wb1, lens, x, xtop, xend, ctop, cend, g2, s2, pb, g3, s3,
                   stats, par, low, high, acc, edge, halo_sems, *links):
    t = pl.program_id(0)
    plane, line = plane_peers(plan), line_peers(plan)
    halo = Halo(plan, edge, low, high, halo_sems, 1)
    s, z, i, h = plan.place()
    L, C, nw, nz = plan.L, plan.C, plan.nw, plan.nz

    @pl.when(first_step())
    def _():
        plane.greet()
        line.greet()
        acc[...] = jnp.zeros_like(acc)
        n16 = nw * 16
        for side, (xe, ce, places) in enumerate(
            ((xtop, ctop, (0, 1, 0)), (xend, cend, (14, 15, 15)))
        ):
            for k, at in enumerate(places):
                rows, lanes = rows_of((nw, n16)), lanes_of((nw, n16))
                sel = jnp.where(lanes == 16 * rows + at, 1.0, 0.0).astype(BF16)
                block = (xe if k < 2 else ce)[...].reshape(n16, C)
                edge[side, k] = mm(sel, block)


    rows = rows_of((L, C))
    for w in range(wb1):
        valid = 2 * lens[z * nw1 + t * wb1 + w] - s * L
        v = jnp.where(rows < valid, x[w].astype(F32), 0.0)
        v3 = v.reshape(L // 8, 8, C)
        acc[0] += jnp.sum(v3, axis=0)
        acc[1] += jnp.sum(v3 * v3, axis=0)

    @pl.when(last_step())
    def _():
        packet, buf = links[0], links[5]
        packet[0:1] = jnp.sum(acc[0], axis=0, keepdims=True)
        packet[1:2] = jnp.sum(acc[1], axis=0, keepdims=True)
        meet(plane.count + line.count - 2)
        plane.start(links[:4])
        halo.start(0)
        at = 0
        spans = []
        links[4][2:3] = jnp.zeros((1, C), F32)
        for ref in (g2, s2, pb, g3, s3):
            n = ref.shape[1]
            links[4][2:3, at : at + n] = ref[...]
            spans.append((at, n))
            at += n
        links[4][0:2] = plane.finish(links[:4])
        line.start(links[4:])
        stats[...] = line.finish(links[4:])[0:2]
        par[...] = jnp.zeros_like(par)
        for k in range(nz):
            row = buf[k]
            for r, (at, n) in enumerate(spans):
                par[r : r + 1, k * n : (k + 1) * n] = row[2:3, at : at + n]
        halo.finish()


def conv_kernel(plan, lens, x, hl, hr, w_hbm, stats, gain, shift, taps, pw,
                X5, x2, low, high, sums, full, stripe,
                sel, edge, acc, w_ref, w_sem, part, line_sems, gather_sems, halo_sems,
                *link):
    t = pl.program_id(0)
    peers = group_peers(plan)
    halo = Halo(plan, edge, low, high, halo_sems, plan.steps)
    gather = Gather(plan, gather_sems, line_sems, part, stripe, full)
    w_copy = pltpu.make_async_copy(w_hbm, w_ref, w_sem)
    s, z, i, h = plan.place()
    L, Lp, C, wb = plan.L, plan.Lp, plan.C, plan.wb

    @pl.when(first_step())
    def _():
        w_copy.start()
        peers.greet(gather.others())
        part[...] = jnp.where(gather.tap == 3, pw[...], taps[0])
        meet(peers.count - 1 + len(gather.others()))
        gather.line_start()
        acc[...] = jnp.zeros_like(acc)
        shape = (Lp, L)
        for k in range(plan.T1):
            at = lanes_of(shape) - (2 * rows_of(shape) + (k - 2))
            sel[k * Lp : (k + 1) * Lp] = jnp.where((at == 0) | (at == 1), 1.0, 0.0).astype(BF16)

    mean, rho = norm_of(stats[...], 2.0 * total_of(lens))
    scale = gain[...] * rho
    offset = shift[...] - mean * scale
    rows = rows_of((L, C))
    row1 = rows_of((1, C))
    row16 = rows_of((16, C))

    for w in range(wb):
        at = t * wb + w
        valid = 2 * lens[i * plan.nw + at] - s * L
        a = gelu(x[w].astype(F32) * scale + offset)
        a = jnp.where(rows < valid, a, 0.0).astype(BF16)
        picked = mm(sel[...], a)
        for k in range(5):
            X5[w * Lp : (w + 1) * Lp, k * C : (k + 1) * C] = picked[
                k * Lp : (k + 1) * Lp
            ].astype(BF16)

        def beside(ref, k, bin_at):
            a = gelu(ref[k, pl.ds(at, 1), :] * scale + offset)
            here = (row1 + bin_at < valid) & (row1 + (s * L + bin_at) >= 0)
            return jnp.where(here, a, 0.0).astype(BF16).astype(F32)

        l0, l1 = beside(hl, 0, -2), beside(hl, 1, -1)
        r0, r1 = beside(hr, 0, L), beside(hr, 1, L + 1)
        top, end = w * Lp, (w + 1) * Lp
        for k, add in ((0, l0 + l1), (1, l1)):
            X5[top : top + 16, k * C : (k + 1) * C] = (
                picked[k * Lp : k * Lp + 16] + jnp.where(row16 == 0, add, 0.0)
            ).astype(BF16)
        for k, add in ((3, r0), (4, r0 + r1)):
            X5[end - 16 : end, k * C : (k + 1) * C] = (
                picked[(k + 1) * Lp - 16 : (k + 1) * Lp] + jnp.where(row16 == 15, add, 0.0)
            ).astype(BF16)

    @pl.when(first_step())
    def _():
        w_copy.wait()

    nc = 256
    rowp = rows_of((Lp, nc))
    for n in range(C // nc):
        cols = slice(n * nc, (n + 1) * nc)
        y = 0.5 * mm(X5[...], w_ref[:, cols])
        s0 = jnp.zeros((1, nc), F32)
        s1 = jnp.zeros((1, nc), F32)
        for w in range(wb):
            at = t * wb + w
            valid = lens[i * plan.nw + at] - s * Lp
            v = y[w * Lp : (w + 1) * Lp]
            x2[w, :, cols] = v
            edge[0, at, :, cols] = v[:EDGE].astype(BF16)
            edge[1, at, :, cols] = v[Lp - EDGE :].astype(BF16)
            v = jnp.where(rowp < valid, v, 0.0)
            s0 = s0 + jnp.sum(v, axis=0, keepdims=True)
            s1 = s1 + jnp.sum(v * v, axis=0, keepdims=True)
        acc[0:1, cols] += s0
        acc[1:2, cols] += s1

    @pl.when(t == min(1, plan.steps - 1))
    def _():
        gather.line_finish()
        gather.chips_start()

    halo.start(t)

    @pl.when(last_step())
    def _():
        link[0][...] = acc[...]
        peers.start(link)
        gather.pair_start()
        sums[...] = peers.finish(link)
        halo.finish()
        gather.pair_finish()


def dilated_kernel(plan, lens, x2, lo, hi, w_ref, stats, par,
                   Y3, c2, low, high, sums, ext, wf, edge, acc, halo_sems, *link):
    t = pl.program_id(0)
    peers = group_peers(plan)
    halo = Halo(plan, edge, low, high, halo_sems, plan.steps)
    s, z, i, h = plan.place()
    Lp, C, H, wb = plan.Lp, plan.C, plan.H, plan.wb

    @pl.when(first_step())
    def _():
        peers.greet()
        acc[...] = jnp.zeros_like(acc)
        for k in range(plan.T2):
            for c in range(2):
                at = k * C + c * (C // 2)
                wf[:, at : at + C // 2] = w_ref[c, k]

    mean, rho = norm_of(stats[...], total_of(lens))
    scale = par[0:1] * rho
    offset = par[1:2] - mean * scale
    rows = rows_of((Lp, C))
    rowe = rows_of((EDGE, C))

    rowh = rows_of((Lp, H))
    sums0, sums1 = jnp.zeros((8, H), F32), jnp.zeros((8, H), F32)
    nh = min(2, wb)
    for first in range(0, wb, wb // nh):
        span = range(first, first + wb // nh)
        for w in span:
            valid = lens[i * plan.nw + t * wb + w] - s * Lp
            a = jnp.where(rows < valid, gelu(x2[w] * scale + offset), 0.0)
            al = gelu(lo[w].astype(F32) * scale + offset)
            al = jnp.where((rowe - EDGE < valid) & (s > 0), al, 0.0)
            ah = gelu(hi[w].astype(F32) * scale + offset)
            ah = jnp.where(rowe + Lp < valid, ah, 0.0)
            ext[w, 0:EDGE] = al
            ext[w, EDGE : EDGE + Lp] = a
            ext[w, EDGE + Lp :] = ah
            top, end = w * Lp, (w + 1) * Lp
            Y3[top:end, 0:C] = ext[w, EDGE - DIL : EDGE - DIL + Lp].astype(BF16)
            Y3[top:end, C : 2 * C] = a.astype(BF16)
            Y3[top:end, 2 * C : 3 * C] = ext[w, EDGE + DIL : EDGE + DIL + Lp].astype(BF16)
        y = mm_nt(Y3[first * Lp : (first + wb // nh) * Lp], wf[...])
        for w in span:
            at = t * wb + w
            valid = lens[i * plan.nw + at] - s * Lp
            v = y[(w - first) * Lp : (w - first + 1) * Lp]
            c2[w] = v
            edge[0, at] = v[:EDGE].astype(BF16)
            edge[1, at] = v[Lp - EDGE :].astype(BF16)
            v = jnp.where(rowh < valid, v, 0.0)
            sums0 = sums0 + fold(v)
            sums1 = sums1 + fold(v * v)
    acc[0:1, 0:H] += unfold(sums0)
    acc[1:2, 0:H] += unfold(sums1)

    @pl.when(first_step())
    def _():
        meet(peers.count - 1)

    halo.start(t)

    @pl.when(last_step())
    def _():
        link[0][...] = acc[...]
        peers.start(link)
        sums[...] = peers.finish(link)[:, 0:H]
        halo.finish()


def point_kernel(plan, lens, c2, x2, cot, w_ref, pb, stats, par,
                 res, dz, pgrad, low, high, sums, bsum,
                 pw, a3s, a3T, dos, edge, acc, halo_sems, *link):
    t = pl.program_id(0)
    peers = group_peers(plan)
    halo = Halo(plan, edge, low, high, halo_sems, plan.steps)
    s, z, i, h = plan.place()
    Lp, C, H, wb, cs = plan.Lp, plan.C, plan.H, plan.wb, plan.cs
    M = wb * Lp

    @pl.when(first_step())
    def _():
        peers.greet()
        acc[...] = jnp.zeros_like(acc)
        for c in range(2):
            pw[:, c * (C // 2) : (c + 1) * (C // 2)] = w_ref[c, 0]

    @pl.when(t < plan.steps)
    def _():
        mean, rho = norm_of(stats[...], total_of(lens))
        scale = par[3:4, 0:H] * rho
        offset = par[4:5, 0:H] - mean * scale
        shift = -mean * rho
        rowc = rows_of((Lp, C))
        rowh = rows_of((Lp, H))
        block = pl.ds(pl.multiple_of(t * M, 128), M)
        bias = jnp.zeros((8, C), F32)
        parts = []
        for w in range(wb):
            valid = lens[i * plan.nw + t * wb + w] - s * Lp
            d = jnp.where(rowc < valid, cot[w].astype(F32), 0.0)
            bias = bias + fold(d)
            parts.append(d.astype(BF16))
        d = jnp.concatenate(parts, axis=0)
        dos[block] = d
        da = mm_nt(d, pw[...])
        s0, s1 = jnp.zeros((8, H), F32), jnp.zeros((8, H), F32)
        parts = []
        for w in range(wb):
            at = t * wb + w
            valid = lens[i * plan.nw + at] - s * Lp
            top, end = w * Lp, (w + 1) * Lp
            v = c2[w]
            act, slope = gelu_both(v * scale + offset)
            parts.append(jnp.where(rowh < valid, act, 0.0).astype(BF16))
            dzw = da[top:end] * slope
            dz[w] = dzw
            edge[0, at] = dzw[:EDGE].astype(BF16)
            edge[1, at] = dzw[Lp - EDGE :].astype(BF16)
            s0 = s0 + fold(dzw)
            s1 = s1 + fold(dzw * (v * rho + shift))
        a3 = jnp.concatenate(parts, axis=0)
        a3s[block] = a3
        a3T[:, block] = a3.T
        acc[0:1, 0:H] += unfold(s0)
        acc[0:1, H : 2 * H] += unfold(s1)
        acc[1:2] += unfold(bias)

    @pl.when(first_step())
    def _():
        meet(peers.count - 1)

    @pl.when(t < plan.steps)
    def _():
        halo.start(t)

    @pl.when(t == plan.steps - 1)
    def _():
        link[0][...] = acc[...]
        peers.start(link)

    @pl.when(t >= plan.steps)
    def _():
        u = t - plan.steps
        n = plan.nw // 2
        y = mm(a3s[pl.ds(pl.multiple_of(u * n * Lp, 128), n * Lp)], w_ref[h, 0])
        rowr = rows_of((Lp, y.shape[1]))
        for w in range(n):
            valid = lens[i * plan.nw + u * n + w] - s * Lp
            r = x2[w] + y[w * Lp : (w + 1) * Lp] + pb[2:3]
            r = jnp.where(rowr < valid, r, 0.0).astype(BF16).T
            for k in range(plan.g):
                res[k, w] = r[k * cs : (k + 1) * cs]

    @pl.when(last_step())
    def _():
        rows = pl.ds(pl.multiple_of(h * plan.Hh, 16), plan.Hh)
        pgrad[...] = mm(a3T[rows], dos[...]).astype(BF16)
        got = peers.finish(link)
        sums[0:1] = got[0:1, 0:H]
        sums[1:2] = got[0:1, H : 2 * H]
        bsum[...] = got[1:2]
        halo.finish()


def dilated_back_kernel(plan, lens, c2, clo, chi, dz3, zlo, zhi, x2, Y3, w_ref,
                        stats3, sums3, stats2, par, res,
                        dz2, grads, low, high, sums, res_got,
                        ext, Z3, wt, dcT, edge, acc, bulk_sems, halo_sems, *link):
    t = pl.program_id(0)
    peers = group_peers(plan)
    halo = Halo(plan, edge, low, high, halo_sems, 1)
    s, z, i, h = plan.place()
    Lp, C, H, wb, nw, g = plan.Lp, plan.C, plan.H, plan.wb, plan.nw, plan.g

    def bulk(off, n):
        to = lax.rem(i + off, g)
        rows = pl.ds(n * wb, wb)
        return pltpu.make_async_remote_copy(
            src_ref=res.at[to, rows],
            dst_ref=res_got.at[off, rows],
            send_sem=bulk_sems.at[0, off, n],
            recv_sem=bulk_sems.at[1, off, n],
            device_id=(s, h * g + to),
            device_id_type=MESH,
        )

    parts = [(off, n) for off in range(1, g) for n in range(plan.steps)]

    @pl.when(first_step())
    def _():
        peers.greet()
        acc[...] = jnp.zeros_like(acc)
        for k in range(plan.T2):
            for c in range(2):
                cols = slice(c * (C // 2), (c + 1) * (C // 2))
                wt[k * H : (k + 1) * H, cols] = w_ref[c, k]

        meet(peers.count - 1)
        for part in parts:
            bulk(*part).start()

    @pl.when(t < plan.steps)
    def _():
        total = total_of(lens)
        mean3, rho3 = norm_of(stats3[...], total)
        gr3 = par[3:4, 0:H] * rho3
        sg3 = sums3[0:1] / total
        gg3 = sums3[1:2] / total
        mean2, rho2 = norm_of(stats2[...], total)
        scale2 = par[0:1] * rho2
        offset2 = par[1:2] - mean2 * scale2
        rowh = rows_of((Lp, H))
        rowe = rows_of((EDGE, H))
        rowc = rows_of((Lp, C))

        by_v = -gr3 * rho3 * gg3
        by_1 = gr3 * (mean3 * rho3 * gg3 - sg3)
        shift2 = -mean2 * rho2

        def back(dz, v):
            return gr3 * dz + by_v * v + by_1

        for w in range(wb):
            valid = lens[i * nw + t * wb + w] - s * Lp
            d = jnp.where(rowh < valid, back(dz3[w], c2[w]), 0.0)
            dl = back(zlo[w].astype(F32), clo[w].astype(F32))
            dl = jnp.where((rowe - EDGE < valid) & (s > 0), dl, 0.0)
            dh = back(zhi[w].astype(F32), chi[w].astype(F32))
            dh = jnp.where(rowe + Lp < valid, dh, 0.0)
            ext[w, 0:EDGE] = dl
            ext[w, EDGE : EDGE + Lp] = d
            ext[w, EDGE + Lp :] = dh
            top, end = w * Lp, (w + 1) * Lp
            Z3[top:end, 0:H] = ext[w, EDGE + DIL : EDGE + DIL + Lp].astype(BF16)
            Z3[top:end, H : 2 * H] = d.astype(BF16)
            Z3[top:end, 2 * H : 3 * H] = ext[w, EDGE - DIL : EDGE - DIL + Lp].astype(BF16)

        y = mm(Z3[...], wt[...])

        M = wb * Lp
        dcT[:, pl.ds(pl.multiple_of(t * M, 128), M)] = Z3[:, H : 2 * H].T
        s0, s1 = jnp.zeros((8, C), F32), jnp.zeros((8, C), F32)
        for w in range(wb):
            at = t * wb + w
            valid = lens[i * nw + at] - s * Lp
            v = x2[w]
            dzw = y[w * Lp : (w + 1) * Lp] * gelu_slope(v * scale2 + offset2)
            dzw = jnp.where(rowc < valid, dzw, 0.0)
            dz2[w] = dzw
            edge[0, pl.ds(at, 1)] = dzw[0:1]
            edge[1, pl.ds(at, 1)] = dzw[Lp - 1 : Lp]
            s0 = s0 + fold(dzw)
            s1 = s1 + fold(dzw * (v * rho2 + shift2))
        acc[0:1] += unfold(s0)
        acc[1:2] += unfold(s1)

    @pl.when(t == plan.steps - 1)
    def _():
        link[0][...] = acc[...]
        peers.start(link)
        halo.start(0)

    @pl.when(t >= plan.steps)
    def _():
        rows = pl.ds(pl.multiple_of(h * plan.Hh, 16), plan.Hh)
        grads[...] = mm(dcT[rows], Y3[...]).astype(BF16)

    @pl.when(last_step())
    def _():
        sums[...] = peers.finish(link)
        halo.finish()
        for part in parts:
            bulk(*part).wait()


class Reduction:
    SEMS = 3

    def __init__(self, plan, out, give, mine, got, mid, spread, half, mate, sems):
        self.plan, self.out = plan, out
        self.give, self.mine, self.got, self.mid, self.spread = give, mine, got, mid, spread
        self.half, self.mate = half, mate
        self.sems = sems
        self.s, self.z, self.i, self.h = plan.place()
        self.c = lax.rem(self.s, 2)
        self.m = lax.div(self.s, 2)
        self.chips = plan.chips

    @staticmethod
    def scratch(plan):
        taps, wide = plan.T1 + 2, plan.C // 2
        full = (taps, plan.chips, plan.g, plan.rb, wide)
        part = (taps, plan.g, plan.rb, wide)
        return [
            pltpu.VMEM((taps, 2, plan.chips, plan.rb, wide), BF16),
            *[pltpu.VMEM(full, BF16)] * 5,
            *[pltpu.VMEM(part, BF16)] * 2,
            pltpu.SemaphoreType.DMA((2, taps, Reduction.SEMS + 2 * plan.chips + plan.g)),
        ]

    def copy(self, src, dst, tap, sem, device):
        return pltpu.make_async_remote_copy(
            src_ref=src,
            dst_ref=dst,
            send_sem=self.sems.at[0, tap, sem],
            recv_sem=self.sems.at[1, tap, sem],
            device_id=device,
            device_id_type=MESH,
        )

    def pair(self):
        return (2 * self.m + (1 - self.c), self.z)

    def chip(self, off):
        return lax.rem(self.m + off, self.chips)

    def phase0(self, k):
        return self.copy(self.give.at[k], self.got.at[k], k, 0, self.pair())

    def phase1(self, k, off, at):
        to = self.chip(off)
        dst = self.spread.at[k, at]
        return self.copy(self.mid.at[k, to], dst, k, 1 + off, (2 * to + self.c, self.z))

    def phase2(self, k, off):
        to = lax.rem(self.i + off, self.plan.g)
        device = (self.s, self.h * self.plan.g + to)
        return self.copy(
            self.half.at[k, to], self.mate.at[k, off], k, 1 + self.chips + off, device
        )

    def phase3(self, k, off, at):
        to = self.chip(off)
        sem = 1 + self.chips + self.plan.g + off
        src, dst = self.out.at[k, self.c, self.m], self.out.at[k, self.c, at]
        return self.copy(src, dst, k, sem, (2 * to + self.c, self.z))

    def phase4(self, k, c):
        return self.copy(self.out.at[k, c], self.out.at[k, c], k, 1, self.pair())

    def put(self, k, rows):
        wide = self.plan.C // 2
        for j in range(self.plan.g):
            for m in range(self.chips):
                v = rows(j, m)
                left, right = v[:, :wide], v[:, wide:]
                self.mine[k, m, j] = jnp.where(self.c == 0, left, right).astype(BF16)
                self.give[k, m, j] = jnp.where(self.c == 0, right, left).astype(BF16)
        self.phase0(k).start()

    def step1(self, k):
        self.phase0(k).wait()
        self.mid[k] = (self.mine[k].astype(F32) + self.got[k].astype(F32)).astype(BF16)
        for off in range(1, self.chips):
            self.phase1(k, off, self.m).start()

    def step2(self, k):
        for off in range(1, self.chips):
            self.phase1(k, off, self.m).wait_send()
            self.phase1(k, off, self.chip(self.chips - off)).wait_recv()
        self.spread[k, self.m] = self.mid[k, self.m]
        v = self.spread[k, 0].astype(F32)
        for n in range(1, self.chips):
            v = v + self.spread[k, n].astype(F32)
        self.half[k] = v.astype(BF16)
        for off in range(1, self.plan.g):
            self.phase2(k, off).start()

    def step3(self, k):
        for off in range(1, self.plan.g):
            self.phase2(k, off).wait()
        v = self.half[k, self.i].astype(F32)
        for off in range(1, self.plan.g):
            v = v + self.mate[k, off].astype(F32)
        self.out[k, self.c, self.m] = v.astype(BF16)
        for off in range(1, self.chips):
            self.phase3(k, off, self.m).start()

    def step4(self, k):
        for off in range(1, self.chips):
            self.phase3(k, off, self.m).wait_send()
            self.phase3(k, off, self.chip(self.chips - off)).wait_recv()
        self.phase4(k, self.c).start()

    def step5(self, k):
        self.phase4(k, self.c).wait_send()
        self.phase4(k, 1 - self.c).wait_recv()

    def stages(self):
        return [self.step1, self.step2, self.step3, self.step4]


def tail_kernel(plan, lens, dz2, zlo, zhi, x2, lo, hi, cot, hl, hr, x, X5_hbm, taps, grads, pgrad,
                stats2, sums2, par, stats1, gain1, shift1,
                gz, gz_got, sums, summed,
                ext, D3, D0T, wcat, pick, eye, cols, y, part, acc, X5, X5_sems, bulk_sems, *rest):
    t = pl.program_id(0)
    s, z, i, h = plan.place()
    L, Lp, C, wb, g, nw = plan.L, plan.Lp, plan.C, plan.wb, plan.g, plan.nw
    Ch, cs, T1 = plan.Ch, plan.cs, plan.T1
    M = wb * Lp
    nD = plan.steps
    last = nD + T1 - 1
    peers = group_peers(plan)
    red = Reduction(plan, *rest[:9])
    link = rest[9:]

    def bulk(step, off, n):
        to = lax.rem(i + off, g)
        n2 = wb // 2
        return pltpu.make_async_remote_copy(
            src_ref=part.at[step, to, pl.ds(n * n2, n2)],
            dst_ref=gz_got.at[off, pl.ds(step * wb + n * n2, n2)],
            send_sem=bulk_sems.at[0, step, off, n],
            recv_sem=bulk_sems.at[1, step, off, n],
            device_id=(s, h * g + to),
            device_id_type=MESH,
        )

    def X5_copy(k):
        cols = pl.ds(pl.multiple_of(k * C, 128), C)
        return pltpu.make_async_copy(X5_hbm.at[:, cols], X5.at[k % 2], X5_sems.at[k % 2])

    others = [(off, n) for off in range(1, g) for n in range(2)]

    def send(step, n):
        for off in range(1, g):
            bulk(step, off, n).start()

    def when(at):
        return pl.when(t == min(at, last))

    @when(0)
    def _():
        peers.greet()
        acc[...] = jnp.zeros_like(acc)
        pick[...] = pick_matrix(L)
        eye[...] = eye_matrix(Ch, Ch, 0)
        mean, rho = norm_of(stats1[...], 2.0 * total_of(lens))
        scale = gain1[...] * rho
        for k, row in enumerate((scale, shift1[...] - mean * scale, rho, -mean * rho)):
            cols[k] = column(row, L)
        w = [taps[k].astype(F32) for k in range(5)]
        for r, parts in enumerate(
            ((w[0], w[1] + w[2], w[3] + w[4]), (w[0] + w[1], w[2] + w[3], w[4]))
        ):
            for k, v in enumerate(parts):
                wcat[r * Ch : (r + 1) * Ch, k * C : (k + 1) * C] = v.astype(BF16)

    @pl.when(t < nD)
    def _():
        total = total_of(lens)
        mean, rho = norm_of(stats2[...], total)
        gr = par[0:1] * rho
        sg = sums2[0:1] / total
        gg = sums2[1:2] / total
        rowc = rows_of((Lp, C))
        row1 = rows_of((1, C))

        by_dz = 0.5 * gr
        by_v = -0.5 * gr * rho * gg
        by_1 = 0.5 * gr * (mean * rho * gg - sg)
        lanes = lanes_of((Ch, L))

        def back(dout, dz, v):
            return 0.5 * dout + by_dz * dz + by_v * v + by_1

        def grad_of(w):
            at = t * wb + w
            valid = lens[i * nw + at] - s * Lp
            d = back(cot[w].astype(F32), dz2[w], x2[w])
            d = jnp.where(rowc < valid, d, 0.0)
            one = pl.ds(at, 1)
            dl = back(hl[2, one, :], zlo[one, :], lo[w, EDGE - 1 : EDGE].astype(F32))
            dl = jnp.where((row1 - 1 < valid) & (s > 0), dl, 0.0)
            dh = back(hr[2, one, :], zhi[one, :], hi[w, 0:1].astype(F32))
            dh = jnp.where(row1 + Lp < valid, dh, 0.0)
            ext[w, 7:8] = dl
            ext[w, 8 : 8 + Lp] = d
            ext[w, 8 + Lp : 9 + Lp] = dh
            top, end = w * Lp, (w + 1) * Lp
            D3[top:end, 0:C] = ext[w, 9 : 9 + Lp].astype(BF16)
            D3[top:end, C : 2 * C] = d.astype(BF16)
            D3[top:end, 2 * C : 3 * C] = ext[w, 7 : 7 + Lp].astype(BF16)

        def through(w):
            valid = 2 * lens[i * nw + t * wb + w] - s * L
            top, end = w * Lp, (w + 1) * Lp
            v = mm_nt(eye[...], x[w])
            da = jnp.concatenate([y[0:Ch, top:end], y[Ch:, top:end]], axis=1)
            da = mm(da.astype(BF16), pick[...])
            dzw = da * gelu_slope(v * cols[0] + cols[1])
            dzw = jnp.where(lanes < valid, dzw, 0.0)
            acc[0] += dzw
            acc[1] += dzw * (v * cols[2] + cols[3])
            dzw = dzw.astype(BF16)
            for k in range(g):
                part[t, k, w] = dzw[k * cs : (k + 1) * cs]

        nh = 2 if wb % 2 == 0 and wb * Lp // 2 % 128 == 0 else 1
        n = wb // nh
        for hf in range(nh):
            for w in range(hf * n, (hf + 1) * n):
                grad_of(w)
            rows = slice(hf * n * Lp, (hf + 1) * n * Lp)
            y[:, rows] = mm_nt(wcat[...], D3[rows])
        half = D3[:, pl.ds(pl.multiple_of(C + h * Ch, 128), Ch)]
        D0T[:, pl.ds(pl.multiple_of(t * M, 128), M)] = half.T
        for w in range(wb):
            through(w)
        gz[...] = part[t, i]

    @when(0)
    def _():
        meet(peers.count - 1)
        hs = plan.H // plan.nz
        rb = plan.rb
        for u in range(2):

            def rows(j, m, u=u):
                side, r = m * rb // hs, m * rb % hs
                n = 2 * side + u
                rows = slice(j * hs + r, j * hs + r + rb)
                v = grads[rows, n * C : (n + 1) * C] if n < plan.T2 else pgrad[rows]
                return v.astype(F32)

            red.put(T1 + u, rows)

    early = max(nD // 2, 1)

    @pl.when(t < early)
    def _():
        send(t, 0)
        send(t, 1)

    @when(nD - 1)
    def _():
        X5_copy(0).start()

    stages = red.stages()
    for n, at in enumerate((1, 2, nD, nD + 3)):

        @when(at)
        def _():
            for u in range(2):
                stages[n](T1 + u)

    @when(nD - 1)
    def _():
        packet = link[0]
        packet[...] = jnp.zeros_like(packet)
        packet[0:1, 0:Ch] = jnp.sum(acc[0].T, axis=0, keepdims=True)
        packet[1:2, 0:Ch] = jnp.sum(acc[1].T, axis=0, keepdims=True)
        peers.start(link)

    @pl.when(t >= nD)
    def _():
        k = t - nD

        @pl.when(k < T1 - 1)
        def _():
            X5_copy(k + 1).start()

        X5_copy(k).wait()
        y[0:Ch, 0:C] = mm(D0T[...], X5[lax.rem(k, 2)])
        rb = plan.rb
        red.put(k, lambda j, m: y[j * cs + m * rb : j * cs + (m + 1) * rb, 0:C])
        for n, stage in enumerate(stages[:2]):
            pl.when(k > n)(partial(stage, k - 1 - n))

    held = [(step, n) for step in range(early, nD) for n in range(2)]
    for at, pair in zip((nD, nD + 1, nD + 3), held[:3]):

        @when(at)
        def _():
            send(*pair)

    @when(last)
    def _():
        for n, stage in enumerate(stages[:2]):
            for k in range(T1 - 1 - n, T1):
                stage(k)
        for pair in held[3:]:
            send(*pair)
        for stage in stages[2:]:
            for k in range(T1):
                stage(k)
        sums[...] = peers.finish(link)[:, 0:Ch]
        for k in range(T1 + 2):
            red.step5(k)
        summed[...] = red.out[...]
        for step in range(nD):
            for other in others:
                bulk(step, *other).wait()


def input_grad_kernel(plan, lens, x, gz, gz_got, stats, sums, gain, res, res_got, summed,
                      sums2, sums3, bsum,
                      out, out_result, conv_grad, dil_grad, point_grad,
                      g1, b1, g2, b2, g3, b3, pb, eye, cols, xt):
    t = pl.program_id(0)
    s, z, i, h = plan.place()
    L, Ch, cs, wb = plan.L, plan.Ch, plan.cs, plan.wb
    mine = pl.ds(pl.multiple_of(i * cs, 16), cs)

    @pl.when(first_step())
    def _():
        n = 2.0 * total_of(lens)
        mean, rho = norm_of(stats[...], n)
        gr = gain[...] * rho
        gg = sums[1:2] / n * rho
        for k, row in enumerate((gr, -gr * gg, gr * (mean * gg - sums[0:1] / n))):
            xt[...] = column(row, L)
            cols[k] = xt[mine]
        eye[...] = eye_matrix(cs, Ch, i * cs)

        def mine_of(src, at, which, count, *dsts):
            n = dsts[0].shape[1]
            for k in range(count):

                @pl.when(which == k)
                def _():
                    for dst, r in zip(dsts, at):
                        dst[...] = src[r : r + 1, k * n : (k + 1) * n]

        mine_of(sums, (1, 0), i, plan.g, g1, b1)
        mine_of(sums2, (1, 0), z, plan.nz, g2, b2)
        mine_of(sums3, (1, 0), z, plan.nz, g3, b3)
        mine_of(bsum, (0,), z, plan.nz, pb)

    own = lax.div(t, plan.steps) == i
    for w in range(wb):
        out_result[w] = jnp.where(own, res[0, w].astype(F32), res_got[0, w].astype(F32)).astype(BF16)

    C, T1, hs, rb, wide = plan.C, plan.T1, plan.H // plan.nz, plan.rb, plan.C // 2
    count = plan.NW // wb
    turns = min(count, plan.chips)
    per, every = plan.chips // turns, count // turns

    def spread(turn):
        for n in range(per):
            m = turn * per + n
            side, r = m * rb // hs, m * rb % hs
            for c in range(2):
                at = slice(c * wide, (c + 1) * wide)
                for k in range(T1):
                    conv_grad[k, n * rb : (n + 1) * rb, at] = summed[k, c, n].astype(F32)
                for u in range(2):
                    v = summed[T1 + u, c, n].astype(F32)
                    if 2 * side + u < plan.T2:
                        dil_grad[2 * side + u, r : r + rb, at] = v
                    else:
                        point_grad[r : r + rb, at] = v

    for turn in range(turns):
        pl.when(t == turn * every)(partial(spread, turn))

    lanes = lanes_of((cs, L))
    for w in range(wb):
        valid = 2 * lens[t * wb + w] - s * L
        v = mm_nt(eye[...], x[w])
        dz = jnp.where(own, gz[w].astype(F32), gz_got[0, w].astype(F32))
        r = cols[0] * dz + v * cols[1] + cols[2]
        out[w] = jnp.where(lanes < valid, r, 0.0).astype(BF16)


def call(kernel, plan, name, steps, ins, outs, scratch, flops, nbytes, cid=None):
    extra = {} if cid is None else dict(collective_id=cid, has_side_effects=True)
    return pl.pallas_call(
        partial(kernel, plan),
        grid=(steps,),
        in_specs=[SMEM] + [spec for spec, _ in ins],
        out_specs=[spec for spec, _, _ in outs],
        out_shape=[jax.ShapeDtypeStruct(shape, dtype) for _, shape, dtype in outs],
        scratch_shapes=scratch,
        compiler_params=pltpu.CompilerParams(vmem_limit_bytes=VMEM_LIMIT, **extra),
        cost_estimate=pl.CostEstimate(
            flops=int(flops), bytes_accessed=int(nbytes), transcendentals=0
        ),
        name=name,
    )


def per_device(
    inputs,
    lengths,
    input_gain,
    input_shift,
    conv_weight,
    branch_gain,
    branch_shift,
    dilated_tap_weight,
    mixer_gain,
    mixer_shift,
    point_weight,
    point_bias,
    cotangent,
):
    NW, L, C = inputs.shape
    Lp = L // 2
    nz = lax.axis_size("ch")
    R = 2
    plan = Plan(
        ns=lax.axis_size("seq"),
        nz=nz,
        R=R,
        NW=NW,
        L=L,
        C=C,
        H=mixer_gain.shape[0] * nz,
        T1=conv_weight.shape[0],
        T2=dilated_tap_weight.shape[0],
        wb=min(NW * R // nz, max(1, 512 // Lp)),
    )
    g, nw, cs, Ch, H, Hh, wb = plan.g, plan.nw, plan.cs, plan.Ch, plan.H, plan.Hh, plan.wb
    T1, T2, steps = plan.T1, plan.T2, plan.steps
    M = wb * Lp
    hs = H // nz
    lens = lengths.astype(jnp.int32)
    gain1 = input_gain.reshape(1, C)
    shift1 = input_shift.reshape(1, C)

    def row(a):
        return a.reshape(1, a.shape[0])

    def grp():
        return lax.rem(lax.axis_index("ch"), g)

    def half():
        return lax.div(lax.axis_index("ch"), g)

    def core():
        return lax.rem(lax.axis_index("seq"), 2)

    def chip4():
        return lax.div(lax.axis_index("seq"), plan.ns // 4)

    def whole(*shape):
        return pl.BlockSpec(shape, lambda t: (0,) * len(shape), pipeline_mode=pl.Buffered(1))

    def const(*shape):
        return pl.BlockSpec(shape, lambda t: (0,) * len(shape))

    def win(*shape):
        return pl.BlockSpec(shape, lambda t: (t,) + (0,) * (len(shape) - 1))

    def arg_win(n, width):
        return pl.BlockSpec((wb, n, width), lambda t: (grp() * steps + t, 0, 0))

    def ins(*pairs):
        return [p for p in pairs]

    nw1 = NW // nz
    wb1 = min(nw1, wb)

    def edge_spec(n):
        return pl.BlockSpec(
            (nw, 16, C), lambda t: (grp(), n, 0), pipeline_mode=pl.Buffered(1)
        )

    pairs = ins(
        (
            pl.BlockSpec((wb1, L, C), lambda t: (lax.axis_index("ch") * (nw1 // wb1) + t, 0, 0)),
            inputs,
        ),
        (edge_spec(0), inputs),
        (edge_spec(L // 16 - 1), inputs),
        (edge_spec(0), cotangent),
        (edge_spec(Lp // 16 - 1), cotangent),
        (whole(1, cs), row(branch_gain)),
        (whole(1, cs), row(branch_shift)),
        (whole(1, cs), row(point_bias)),
        (whole(1, H // nz), row(mixer_gain)),
        (whole(1, H // nz), row(mixer_shift)),
    )
    plane, line, group = plane_peers(plan), line_peers(plan), group_peers(plan)
    stats1, par, hl, hr = call(
        lambda plan, *refs: moments_kernel(plan, nw1, wb1, *refs),
        plan,
        "moments",
        nw1 // wb1,
        pairs,
        [
            (const(2, C), (2, C), F32),
            (const(8, C), (8, C), F32),
            (ANY, (3, nw, C), F32),
            (ANY, (3, nw, C), F32),
        ],
        [
            pltpu.VMEM((2, 8, C), F32),
            pltpu.VMEM((2, 3, nw, C), F32),
        ]
        + halo_scratch(1)
        + plane.scratch(2, C)
        + line.scratch(3, C),
        0,
        nw1 * L * C * 2,
        cid=1,
    )(lens, *[a for _, a in pairs])

    pairs = ins(
        (arg_win(L, C), inputs),
        (whole(3, nw, C), hl),
        (whole(3, nw, C), hr),
        (ANY, conv_weight.reshape(T1 * C, C)),
        (whole(2, C), stats1),
        (whole(1, C), gain1),
        (whole(1, C), shift1),
        (
            pl.BlockSpec((1, hs, C // 2), lambda t: (jnp.minimum(chip4(), T2 - 1), 0, core())),
            jnp.swapaxes(dilated_tap_weight, 1, 2),
        ),
        (pl.BlockSpec((hs, C // 2), lambda t: (0, core())), point_weight),
    )
    X5, x2, lo2, hi2, stats2, full, _ = call(
        conv_kernel,
        plan,
        "conv",
        steps,
        pairs,
        [
            (win(M, T1 * C), (nw * Lp, T1 * C), BF16),
            (win(wb, Lp, C), (nw, Lp, C), F32),
            (ANY, (nw, EDGE, C), BF16),
            (ANY, (nw, EDGE, C), BF16),
            (const(2, C), (2, C), F32),
            (ANY, (2, T2 + 1, nz, hs, C // 2), BF16),
            (ANY, (nz, hs, C // 2), BF16),
        ],
        [
            pltpu.VMEM((T1 * Lp, L), BF16),
            pltpu.VMEM((2, nw, EDGE, C), BF16),
            pltpu.VMEM((2, C), F32),
            pltpu.VMEM((T1 * C, C), BF16),
            pltpu.SemaphoreType.DMA,
            pltpu.VMEM((hs, C // 2), BF16),
            pltpu.SemaphoreType.DMA((2, nz)),
            pltpu.SemaphoreType.DMA((2, plan.ns // 2 + 1, Gather.PARTS)),
        ]
        + halo_scratch(steps)
        + group.scratch(2, C),
        2 * nw * Lp * T1 * C * C,
        nw * Lp * C * 20,
        cid=2,
    )(lens, *[a for _, a in pairs])

    full = full.reshape(2, T2 + 1, H, C // 2)
    taps_spec = whole(2, T2, H, C // 2)
    pw_spec = pl.BlockSpec(
        (2, 1, H, C // 2), lambda t: (0, T2, 0, 0), pipeline_mode=pl.Buffered(1)
    )

    pairs = ins(
        (win(wb, Lp, C), x2),
        (win(wb, EDGE, C), lo2),
        (win(wb, EDGE, C), hi2),
        (taps_spec, full),
        (whole(2, C), stats2),
        (whole(8, C), par),
    )
    Y3, c2, lo3, hi3, stats3 = call(
        dilated_kernel,
        plan,
        "dilated",
        steps,
        pairs,
        [
            (win(M, T2 * C), (nw * Lp, T2 * C), BF16),
            (win(wb, Lp, H), (nw, Lp, H), F32),
            (ANY, (nw, EDGE, H), BF16),
            (ANY, (nw, EDGE, H), BF16),
            (const(2, H), (2, H), F32),
        ],
        [
            pltpu.VMEM((wb, Lp + 2 * EDGE, C), F32),
            pltpu.VMEM((H, T2 * C), BF16),
            pltpu.VMEM((2, nw, EDGE, H), BF16),
            pltpu.VMEM((2, C), F32),
        ]
        + halo_scratch(steps)
        + group.scratch(2, C),
        2 * nw * Lp * T2 * C * H,
        nw * Lp * C * 12,
        cid=3,
    )(lens, *[a for _, a in pairs])

    def early(*shape):
        return pl.BlockSpec(
            shape, lambda t: (jnp.minimum(t, steps - 1),) + (0,) * (len(shape) - 1)
        )

    def late(t):
        return jnp.maximum(t - steps, 0)

    pairs = ins(
        (early(wb, Lp, H), c2),
        (pl.BlockSpec((nw // 2, Lp, Ch), lambda t: (late(t), 0, half())), x2),
        (
            pl.BlockSpec(
                (wb, Lp, C), lambda t: (grp() * steps + jnp.minimum(t, steps - 1), 0, 0)
            ),
            cotangent,
        ),
        (pw_spec, full),
        (pl.BlockSpec((8, Ch), lambda t: (0, half()), pipeline_mode=pl.Buffered(1)), par),
        (whole(2, H), stats3),
        (whole(8, C), par),
    )
    res, dz3, pgrad, zlo3, zhi3, sums3, bsum = call(
        point_kernel,
        plan,
        "point",
        steps + 2,
        pairs,
        [
            (
                pl.BlockSpec((g, nw // 2, cs, Lp), lambda t: (0, late(t), 0, 0)),
                (g, nw, cs, Lp),
                BF16,
            ),
            (early(wb, Lp, H), (nw, Lp, H), F32),
            (const(Hh, C), (Hh, C), BF16),
            (ANY, (nw, EDGE, H), BF16),
            (ANY, (nw, EDGE, H), BF16),
            (const(2, H), (2, H), F32),
            (const(1, C), (1, C), F32),
        ],
        [
            pltpu.VMEM((H, C), BF16),
            pltpu.VMEM((nw * Lp, H), BF16),
            pltpu.VMEM((H, nw * Lp), BF16),
            pltpu.VMEM((nw * Lp, C), BF16),
            pltpu.VMEM((2, nw, EDGE, H), BF16),
            pltpu.VMEM((2, C), F32),
        ]
        + halo_scratch(steps)
        + group.scratch(2, C),
        5 * nw * Lp * C * H,
        nw * Lp * C * 10,
        cid=4,
    )(lens, *[a for _, a in pairs])

    pairs = ins(
        (early(wb, Lp, H), c2),
        (early(wb, EDGE, H), lo3),
        (early(wb, EDGE, H), hi3),
        (early(wb, Lp, H), dz3),
        (early(wb, EDGE, H), zlo3),
        (early(wb, EDGE, H), zhi3),
        (early(wb, Lp, C), x2),
        (pl.BlockSpec((nw * Lp, C), lambda t: (0, late(t))), Y3),
        (taps_spec, full),
        (whole(2, H), stats3),
        (whole(2, H), sums3),
        (whole(2, C), stats2),
        (whole(8, C), par),
        (ANY, res),
    )
    dz2, grads, zlo2, zhi2, sums2, res_got = call(
        dilated_back_kernel,
        plan,
        "dilated_back",
        steps + T2,
        pairs,
        [
            (early(wb, Lp, C), (nw, Lp, C), F32),
            (pl.BlockSpec((Hh, C), lambda t: (0, late(t))), (Hh, T2 * C), BF16),
            (ANY, (nw, C), F32),
            (ANY, (nw, C), F32),
            (const(2, C), (2, C), F32),
            (ANY, (g, nw, cs, Lp), BF16),
        ],
        [
            pltpu.VMEM((wb, Lp + 2 * EDGE, H), F32),
            pltpu.VMEM((M, T2 * H), BF16),
            pltpu.VMEM((T2 * H, C), BF16),
            pltpu.VMEM((H, nw * Lp), BF16),
            pltpu.VMEM((2, nw, C), F32),
            pltpu.VMEM((2, C), F32),
            pltpu.SemaphoreType.DMA((2, g, steps)),
        ]
        + halo_scratch(1)
        + group.scratch(2, C),
        4 * nw * Lp * T2 * C * H,
        nw * Lp * C * 20,
        cid=5,
    )(lens, *[a for _, a in pairs])

    def half_of(n):
        return pl.BlockSpec((n, Ch), lambda t: (0, half()), pipeline_mode=pl.Buffered(1))

    chips, rb = plan.chips, plan.rb
    sshape = (T1 + 2, 2, chips, rb, C // 2)
    pairs = ins(
        (early(wb, Lp, C), dz2),
        (whole(nw, C), zlo2),
        (whole(nw, C), zhi2),
        (early(wb, Lp, C), x2),
        (early(wb, EDGE, C), lo2),
        (early(wb, EDGE, C), hi2),
        (
            pl.BlockSpec(
                (wb, Lp, C), lambda t: (grp() * steps + jnp.minimum(t, steps - 1), 0, 0)
            ),
            cotangent,
        ),
        (whole(3, nw, C), hl),
        (whole(3, nw, C), hr),
        (
            pl.BlockSpec(
                (wb, L, Ch), lambda t: (grp() * steps + jnp.minimum(t, steps - 1), 0, half())
            ),
            inputs,
        ),
        (ANY, X5),
        (
            pl.BlockSpec(
                (T1, Ch, C), lambda t: (0, half(), 0), pipeline_mode=pl.Buffered(1)
            ),
            conv_weight,
        ),
        (whole(Hh, T2 * C), grads),
        (whole(Hh, C), pgrad),
        (whole(2, C), stats2),
        (whole(2, C), sums2),
        (whole(8, C), par),
        (half_of(2), stats1),
        (half_of(1), gain1),
        (half_of(1), shift1),
    )
    gz, gz_got, sums1, summed = call(
        tail_kernel,
        plan,
        "tail",
        steps + T1,
        pairs,
        [
            (early(wb, cs, L), (nw, cs, L), BF16),
            (ANY, (g, nw, cs, L), BF16),
            (const(2, Ch), (2, Ch), F32),
            (const(*sshape), sshape, BF16),
        ],
        [
            pltpu.VMEM((wb, Lp + 16, C), F32),
            pltpu.VMEM((M, 3 * C), BF16),
            pltpu.VMEM((Ch, nw * Lp), BF16),
            pltpu.VMEM((2 * Ch, 3 * C), BF16),
            pltpu.VMEM((L, L), BF16),
            pltpu.VMEM((Ch, Ch), BF16),
            pltpu.VMEM((4, Ch, L), F32),
            pltpu.VMEM((2 * Ch, max(M, C)), F32),
            pltpu.VMEM((steps, g, wb, cs, L), BF16),
            pltpu.VMEM((2, Ch, L), F32),
            pltpu.VMEM((2, nw * Lp, C), BF16),
            pltpu.SemaphoreType.DMA((2,)),
            pltpu.SemaphoreType.DMA((2, steps, g, 2)),
        ]
        + Reduction.scratch(plan)
        + group.scratch(2, C),
        2 * nw * Lp * (6 + T1) * C * Ch,
        nw * Lp * C * 40,
        cid=6,
    )(lens, *[a for _, a in pairs])

    count = NW // wb
    turns = min(count, chips)

    def own_block(t):
        return jnp.where(lax.div(t, steps) == grp(), lax.rem(t, steps), 0)

    def got_slot(t):
        off = lax.rem(grp() - lax.div(t, steps) + g, g)
        return jnp.maximum(off, 1), jnp.where(off > 0, lax.rem(t, steps), 0)

    pairs = ins(
        (pl.BlockSpec((wb, L, Ch), lambda t: (t, 0, half())), inputs),
        (pl.BlockSpec((wb, cs, L), lambda t: (own_block(t), 0, 0)), gz),
        (pl.BlockSpec((1, wb, cs, L), lambda t: got_slot(t) + (0, 0)), gz_got),
        (half_of(2), stats1),
        (whole(2, Ch), sums1),
        (half_of(1), gain1),
        (pl.BlockSpec((1, wb, cs, Lp), lambda t: (grp(), own_block(t), 0, 0)), res),
        (pl.BlockSpec((1, wb, cs, Lp), lambda t: got_slot(t) + (0, 0)), res_got),
        (
            pl.BlockSpec(
                (T1 + 2, 2, chips // turns, rb, C // 2),
                lambda t: (0, 0, t * turns // count, 0, 0),
            ),
            summed,
        ),
        (whole(2, C), sums2),
        (whole(2, H), sums3),
        (whole(1, C), bsum),
    )
    outs = call(
        input_grad_kernel,
        plan,
        "input_grad",
        NW // wb,
        pairs,
        [
            (win(wb, cs, L), (NW, cs, L), BF16),
            (win(wb, cs, Lp), (NW, cs, Lp), BF16),
            (
                pl.BlockSpec((T1, cs // turns, C), lambda t: (0, t * turns // count, 0)),
                (T1, cs, C),
                F32,
            ),
            (const(T2, hs, C), (T2, hs, C), F32),
            (const(hs, C), (hs, C), F32),
        ]
        + [(const(1, n), (1, n), F32) for n in (cs, cs, cs, cs, hs, hs, cs)],
        [
            pltpu.VMEM((cs, Ch), BF16),
            pltpu.VMEM((3, cs, L), F32),
            pltpu.VMEM((Ch, L), F32),
        ],
        2 * NW * L * Ch * cs,
        NW * L * cs * 8,
    )(lens, *[a for _, a in pairs])
    grad, result, conv_grad, dil_grad, point_grad = outs[:5]
    g1, b1, g2, b2, g3, b3, pb = [a[0] for a in outs[5:]]
    return (
        jnp.swapaxes(result, 1, 2),
        jnp.swapaxes(grad, 1, 2),
        jnp.swapaxes(conv_grad, 1, 2),
        g1,
        b1,
        g2,
        b2,
        jnp.swapaxes(dil_grad, 1, 2),
        g3,
        b3,
        point_grad,
        pb,
    )


def solution(mesh):
    in_specs = (
        P(None, "seq", None),
        P(),
        P(),
        P(),
        P(),
        P("ch"),
        P("ch"),
        P(None, None, "ch"),
        P("ch"),
        P("ch"),
        P("ch", None),
        P("ch"),
        P(None, "seq", None),
    )
    out_specs = (
        P(None, "seq", "ch"),
        P(None, "seq", "ch"),
        P(None, None, "ch"),
        P("ch"),
        P("ch"),
        P("ch"),
        P("ch"),
        P(None, None, "ch"),
        P("ch"),
        P("ch"),
        P("ch", None),
        P("ch"),
    )
    return jax.shard_map(
        per_device, mesh=mesh, in_specs=in_specs, out_specs=out_specs, check_vma=False
    )
```

```python
from functools import partial
from typing import NamedTuple

import jax
import jax.numpy as jnp
from jax import lax
from jax.experimental import pallas as pl
from jax.experimental.pallas import tpu as pltpu
from jax.sharding import PartitionSpec as P

DIL = 14
EDGE = 16
EPS = 1e-05
GC0 = 0.7978845608028654
GC1 = 0.044715
F32 = jnp.float32
BF16 = jnp.bfloat16
MESH = pl.DeviceIdType.MESH
VMEM_LIMIT = 58 * 1024 * 1024
ANY = pl.BlockSpec(memory_space=pl.ANY)
SMEM = pl.BlockSpec(memory_space=pltpu.SMEM)


class Plan(NamedTuple):
    ns: int
    nz: int
    R: int
    NW: int
    L: int
    C: int
    H: int
    T1: int
    T2: int
    wb: int

    @property
    def g(self):
        return self.nz // self.R

    @property
    def nw(self):
        return self.NW // self.g

    @property
    def Lp(self):
        return self.L // 2

    @property
    def cs(self):
        return self.C // self.nz

    @property
    def Ch(self):
        return self.C // self.R

    @property
    def Hh(self):
        return self.H // self.R

    @property
    def steps(self):
        return self.nw // self.wb

    @property
    def chips(self):
        return self.ns // 2

    @property
    def rb(self):
        return self.cs // self.chips

    def place(self):
        s, z = lax.axis_index("seq"), lax.axis_index("ch")
        return s, z, lax.rem(z, self.g), lax.div(z, self.g)


def gelu(z):
    t = jnp.tanh(z * (GC0 + (GC0 * GC1) * (z * z)))
    return z * (0.5 + 0.5 * t)


def gelu_both(z):
    sq = z * z
    t = jnp.tanh(z * (GC0 + (GC0 * GC1) * sq))
    h = 0.5 + 0.5 * t
    v = z * h
    return v, h + v * (1.0 - t) * (GC0 + (3.0 * GC0 * GC1) * sq)


def gelu_slope(z):
    return gelu_both(z)[1]


def fold(v):
    return jnp.sum(v.reshape(v.shape[0] // 8, 8, v.shape[1]), axis=0)


def unfold(v):
    return jnp.sum(v, axis=0, keepdims=True)


def rows_of(shape):
    return lax.broadcasted_iota(jnp.int32, shape, 0)


def lanes_of(shape):
    return lax.broadcasted_iota(jnp.int32, shape, 1)


def total_of(lens):
    n = lens[0]
    for k in range(1, lens.shape[0]):
        n = n + lens[k]
    return n.astype(F32)


def norm_of(stats, total):
    mean = stats[0:1] / total
    square = stats[1:2] / total
    return mean, lax.rsqrt(square - mean * mean + EPS)


def flat(ref):
    return ref[...].reshape(1, ref.shape[0])


def column(row, n):
    return jnp.broadcast_to(row, (n, row.shape[1])).T


def mm(a, b):
    return jnp.dot(a, b, preferred_element_type=F32)


def mm_nt(a, b):
    return lax.dot_general(a, b, (((1,), (1,)), ((), ())), preferred_element_type=F32)


def mm_tn(a, b):
    return lax.dot_general(a, b, (((0,), (0,)), ((), ())), preferred_element_type=F32)


def mm_tt(a, b):
    return lax.dot_general(a, b, (((0,), (1,)), ((), ())), preferred_element_type=F32)


def eye_matrix(n, m, first):
    return jnp.where(lanes_of((n, m)) == rows_of((n, m)) + first, 1.0, 0.0).astype(BF16)


def pick_matrix(L):
    r, n = rows_of((L, L)), lanes_of((L, L))
    bin_of = 2 * r - jnp.where(r >= L // 2, L - 1, 0)
    return jnp.where(n == bin_of, 1.0, 0.0).astype(BF16)


class Peers:
    def __init__(self, count, me, device):
        self.count, self.me, self.device = count, me, device

    def other(self, off):
        return lax.rem(self.me + off, self.count)

    def greet(self, more=()):
        barrier = pltpu.get_barrier_semaphore()
        devices = [self.device(self.other(off)) for off in range(1, self.count)]
        for device in (*devices, *more):
            pl.semaphore_signal(barrier, inc=1, device_id=device, device_id_type=MESH)

    def copy(self, link, slot, off):
        packet, buf, send, recv = link
        return pltpu.make_async_remote_copy(
            src_ref=packet,
            dst_ref=buf.at[slot],
            send_sem=send.at[off],
            recv_sem=recv.at[slot],
            device_id=self.device(self.other(off)),
            device_id_type=MESH,
        )

    def start(self, link):
        for off in range(1, self.count):
            self.copy(link, self.me, off).start()

    def finish(self, link):
        packet, buf = link[:2]
        buf[self.me] = packet[...]
        for off in range(1, self.count):
            self.copy(link, self.other(off), off).wait_recv()
        acc = buf[0]
        for q in range(1, self.count):
            acc = acc + buf[q]
        for off in range(1, self.count):
            self.copy(link, self.me, off).wait_send()
        return acc

    def scratch(self, rows, width):
        return [
            pltpu.VMEM((rows, width), F32),
            pltpu.VMEM((self.count, rows, width), F32),
            pltpu.SemaphoreType.DMA((self.count,)),
            pltpu.SemaphoreType.DMA((self.count,)),
        ]


def group_peers(plan):
    s, z, i, h = plan.place()
    g = plan.g
    return Peers(plan.ns * g, s * g + i, lambda q: (lax.div(q, g), h * g + lax.rem(q, g)))


def plane_peers(plan):
    s, z, i, h = plan.place()
    return Peers(plan.ns, s, lambda q: (q, z))


def line_peers(plan):
    s, z, i, h = plan.place()
    return Peers(plan.nz, z, lambda q: (s, q))


def meet(count):
    pl.semaphore_wait(pltpu.get_barrier_semaphore(), count)


class Halo:
    def __init__(self, plan, edge, low, high, sems, parts):
        self.edge, self.low, self.high, self.sems, self.parts = edge, low, high, sems, parts
        s, z, _, _ = plan.place()
        self.left = (lax.rem(s + plan.ns - 1, plan.ns), z)
        self.right = (lax.rem(s + 1, plan.ns), z)
        self.n = low.shape[0] // parts

    def copies(self, part):
        rows = pl.ds(part * self.n, self.n)
        return [
            pltpu.make_async_remote_copy(
                src_ref=self.edge.at[side, rows],
                dst_ref=dst.at[rows],
                send_sem=self.sems.at[0, side, part],
                recv_sem=self.sems.at[1, side, part],
                device_id=dev,
                device_id_type=MESH,
            )
            for side, (dst, dev) in enumerate(((self.high, self.left), (self.low, self.right)))
        ]

    def start(self, part):
        for c in self.copies(part):
            c.start()

    def finish(self):
        for part in range(self.parts):
            for c in self.copies(part):
                c.wait()


def halo_scratch(parts):
    return [pltpu.SemaphoreType.DMA((2, 2, parts))]


class Gather:
    PARTS = 2

    def __init__(self, plan, sems, line_sems, part, stripe, full):
        self.plan, self.part, self.full, self.sems = plan, part, full, sems
        self.stripe, self.line_sems = stripe, line_sems
        self.s, self.z, self.i, self.h = plan.place()
        self.c, self.m = lax.rem(self.s, 2), lax.div(self.s, 2)
        self.chips = plan.ns // 2
        self.every = self.chips // 4
        self.tap = lax.div(self.m, self.every)
        self.owner = lax.rem(self.m, self.every) == 0
        self.rows = plan.H // plan.nz

    def others(self):
        g, nz = self.plan.g, self.plan.nz
        return [(self.s, lax.rem(self.h * g + g + r, nz)) for r in range(nz - g)]

    def copy(self, src, dst, sem, device):
        return pltpu.make_async_remote_copy(
            src_ref=src,
            dst_ref=dst,
            send_sem=self.sems.at[(0,) + sem],
            recv_sem=self.sems.at[(1,) + sem],
            device_id=device,
            device_id_type=MESH,
        )

    def line(self, off, at):
        to = lax.rem(self.z + off, self.plan.nz)
        return pltpu.make_async_remote_copy(
            src_ref=self.part,
            dst_ref=self.stripe.at[at],
            send_sem=self.line_sems.at[0, off],
            recv_sem=self.line_sems.at[1, off],
            device_id=(self.s, to),
            device_id_type=MESH,
        )

    def own_rows(self):
        return pltpu.make_async_copy(
            self.part, self.stripe.at[self.z], self.line_sems.at[0, 0]
        )

    def line_start(self):
        @pl.when(self.owner)
        def _():
            self.own_rows().start()
            for off in range(1, self.plan.nz):
                self.line(off, self.z).start()

    def line_finish(self):
        @pl.when(self.owner)
        def _():
            self.own_rows().wait()
            for off in range(1, self.plan.nz):
                self.line(off, self.z).wait_send()
                at = lax.rem(self.z + self.plan.nz - off, self.plan.nz)
                self.line(off, at).wait_recv()

    def half(self, ref, n):
        rows = self.plan.nz // self.PARTS
        return ref.at[pl.ds(n * rows, rows)]

    def own_stripe(self):
        return pltpu.make_async_copy(
            self.stripe, self.full.at[self.c, self.tap], self.sems.at[0, 0, 0]
        )

    def chip(self, off, n):
        to = lax.rem(self.m + off, self.chips)
        return self.copy(
            self.half(self.stripe, n),
            self.half(self.full.at[self.c, self.tap], n),
            (off, n),
            (2 * to + self.c, self.z),
        )

    def arrival(self, k, off, n):
        whole = self.half(self.full.at[self.c, k], n)
        return self.copy(whole, whole, (off, n), (2 * k * self.every + self.c, self.z))

    def pair(self, c, n):
        part = self.full.at[c, pl.ds(2 * n, 2)]
        return self.copy(part, part, (self.chips, n), (2 * self.m + 1 - self.c, self.z))

    def chips_start(self):
        @pl.when(self.owner)
        def _():
            self.own_stripe().start()
            for off in range(1, self.chips):
                for n in range(self.PARTS):
                    self.chip(off, n).start()

    def pair_start(self):
        for k in range(4):
            off = lax.rem(self.m - k * self.every + self.chips, self.chips)

            @pl.when(off != 0)
            def _():
                for n in range(self.PARTS):
                    self.arrival(k, off, n).wait_recv()

        @pl.when(self.owner)
        def _():
            self.own_stripe().wait()
            for off in range(1, self.chips):
                for n in range(self.PARTS):
                    self.chip(off, n).wait_send()

        for n in range(self.PARTS):
            self.pair(self.c, n).start()

    def pair_finish(self):
        for n in range(self.PARTS):
            self.pair(self.c, n).wait_send()
            self.pair(1 - self.c, n).wait_recv()


def first_step():
    return pl.program_id(0) == 0


def last_step():
    return pl.program_id(0) == pl.num_programs(0) - 1


def head_kernel(plan, nm, lens, x, xtop, xend, ctop, cend, g2, s2, pb, g3, s3,
                w_hbm, gain, shift, taps, pw,
                X5, x2, low, high, sums, stats, par, hl_out, hr_out, full, stripe,
                macc, hl, hr, xedge, sel, edge, acc, w_ref, w_sem, part,
                line_sems, gather_sems, xhalo_sems, halo_sems, *links):
    t = pl.program_id(0)
    peers, plane, line = group_peers(plan), plane_peers(plan), line_peers(plan)
    xhalo = Halo(plan, xedge, hl, hr, xhalo_sems, 1)
    halo = Halo(plan, edge, low, high, halo_sems, plan.steps)
    gather = Gather(plan, gather_sems, line_sems, part, stripe, full)
    w_copy = pltpu.make_async_copy(w_hbm, w_ref, w_sem)
    plane_link, line_link, link = links[:4], links[4:8], links[8:]
    s, z, i, h = plan.place()
    L, Lp, C, nw, nz, wb = plan.L, plan.Lp, plan.C, plan.nw, plan.nz, plan.wb
    share = plan.NW // nz
    c = t - nm

    @pl.when(first_step())
    def _():
        w_copy.start()
        peers.greet(gather.others())
        part[...] = jnp.where(gather.tap == 3, pw[...], taps[0])
        macc[...] = jnp.zeros_like(macc)
        acc[...] = jnp.zeros_like(acc)
        n16 = nw * 16
        for side, (xe, ce, places) in enumerate(
            ((xtop, ctop, (0, 1, 0)), (xend, cend, (14, 15, 15)))
        ):
            for k, at in enumerate(places):
                rows, lanes = rows_of((nw, n16)), lanes_of((nw, n16))
                one = jnp.where(lanes == 16 * rows + at, 1.0, 0.0).astype(BF16)
                block = (xe if k < 2 else ce)[...].reshape(n16, C)
                xedge[side, k] = mm(one, block)
        shape = (Lp, L)
        for k in range(plan.T1):
            at = lanes_of(shape) - (2 * rows_of(shape) + (k - 2))
            sel[k * Lp : (k + 1) * Lp] = jnp.where((at == 0) | (at == 1), 1.0, 0.0).astype(BF16)

    @pl.when(c < 0)
    def _():
        rows = rows_of((L, C))
        for w in range(min(share, wb)):
            at = lax.rem(z * share, wb) + w
            valid = 2 * lens[z * share + t * wb + w] - s * L
            v = jnp.where(rows < valid, x[at].astype(F32), 0.0)
            macc[0] += fold(v)
            macc[1] += fold(v * v)

    @pl.when(c == -1)
    def _():
        packet, more = plane_link[0], line_link[0]
        packet[0:1] = unfold(macc[0])
        packet[1:2] = unfold(macc[1])
        meet(peers.count - 1 + len(gather.others()))
        plane.start(plane_link)
        xhalo.start(0)
        at = 0
        spans = []
        more[2:3] = jnp.zeros((1, C), F32)
        for ref in (g2, s2, pb, g3, s3):
            n = ref.shape[1]
            more[2:3, at : at + n] = ref[...]
            spans.append((at, n))
            at += n
        more[0:2] = plane.finish(plane_link)
        line.start(line_link)
        gather.line_start()
        stats[...] = line.finish(line_link)[0:2]
        par[...] = jnp.zeros_like(par)
        for k in range(nz):
            row = line_link[1][k]
            for r, (at, n) in enumerate(spans):
                par[r : r + 1, k * n : (k + 1) * n] = row[2:3, at : at + n]
        par[5:6] = flat(gain)
        par[6:7] = flat(shift)
        xhalo.finish()
        hl_out[...] = hl[...]
        hr_out[...] = hr[...]
        w_copy.wait()

    @pl.when(c >= 0)
    def _():
        mean, rho = norm_of(stats[...], 2.0 * total_of(lens))
        scale = flat(gain) * rho
        offset = flat(shift) - mean * scale
        rows = rows_of((L, C))
        row1 = rows_of((1, C))
        row16 = rows_of((16, C))
        for w in range(wb):
            at = c * wb + w
            valid = 2 * lens[i * nw + at] - s * L
            a = gelu(x[w].astype(F32) * scale + offset)
            a = jnp.where(rows < valid, a, 0.0).astype(BF16)
            picked = mm(sel[...], a)
            for k in range(5):
                X5[w * Lp : (w + 1) * Lp, k * C : (k + 1) * C] = picked[
                    k * Lp : (k + 1) * Lp
                ].astype(BF16)

            def beside(ref, k, bin_at):
                a = gelu(ref[k, pl.ds(at, 1), :] * scale + offset)
                here = (row1 + bin_at < valid) & (row1 + (s * L + bin_at) >= 0)
                return jnp.where(here, a, 0.0).astype(BF16).astype(F32)

            l0, l1 = beside(hl, 0, -2), beside(hl, 1, -1)
            r0, r1 = beside(hr, 0, L), beside(hr, 1, L + 1)
            top, end = w * Lp, (w + 1) * Lp
            for k, add in ((0, l0 + l1), (1, l1)):
                X5[top : top + 16, k * C : (k + 1) * C] = (
                    picked[k * Lp : k * Lp + 16] + jnp.where(row16 == 0, add, 0.0)
                ).astype(BF16)
            for k, add in ((3, r0), (4, r0 + r1)):
                X5[end - 16 : end, k * C : (k + 1) * C] = (
                    picked[(k + 1) * Lp - 16 : (k + 1) * Lp] + jnp.where(row16 == 15, add, 0.0)
                ).astype(BF16)

        nc = 256
        rowp = rows_of((Lp, nc))
        for n in range(C // nc):
            cols = slice(n * nc, (n + 1) * nc)
            y = 0.5 * mm(X5[...], w_ref[:, cols])
            s0 = jnp.zeros((8, nc), F32)
            s1 = jnp.zeros((8, nc), F32)
            for w in range(wb):
                at = c * wb + w
                valid = lens[i * nw + at] - s * Lp
                v = y[w * Lp : (w + 1) * Lp]
                x2[w, :, cols] = v
                edge[0, at, :, cols] = v[:EDGE].astype(BF16)
                edge[1, at, :, cols] = v[Lp - EDGE :].astype(BF16)
                v = jnp.where(rowp < valid, v, 0.0)
                s0 = s0 + fold(v)
                s1 = s1 + fold(v * v)
            acc[0:1, cols] += unfold(s0)
            acc[1:2, cols] += unfold(s1)
        halo.start(c)

    @pl.when(c == 0)
    def _():
        gather.line_finish()
        gather.chips_start()

    @pl.when(last_step())
    def _():
        link[0][...] = acc[...]
        peers.start(link)
        gather.pair_start()
        sums[...] = peers.finish(link)
        halo.finish()
        gather.pair_finish()


def dilated_kernel(plan, lens, x2, lo, hi, w_ref, stats, par,
                   Y3, c2, low, high, sums, ext, wf, edge, acc, halo_sems, *link):
    t = pl.program_id(0)
    peers = group_peers(plan)
    halo = Halo(plan, edge, low, high, halo_sems, plan.steps)
    s, z, i, h = plan.place()
    Lp, C, H, wb = plan.Lp, plan.C, plan.H, plan.wb

    @pl.when(first_step())
    def _():
        peers.greet()
        acc[...] = jnp.zeros_like(acc)
        for k in range(plan.T2):
            for c in range(2):
                at = k * C + c * (C // 2)
                wf[:, at : at + C // 2] = w_ref[c, k]

    mean, rho = norm_of(stats[...], total_of(lens))
    scale = par[0:1] * rho
    offset = par[1:2] - mean * scale
    rows = rows_of((Lp, C))
    rowe = rows_of((EDGE, C))

    rowh = rows_of((Lp, H))
    sums0, sums1 = jnp.zeros((8, H), F32), jnp.zeros((8, H), F32)
    nh = min(2, wb)
    for first in range(0, wb, wb // nh):
        span = range(first, first + wb // nh)
        for w in span:
            valid = lens[i * plan.nw + t * wb + w] - s * Lp
            a = jnp.where(rows < valid, gelu(x2[w] * scale + offset), 0.0)
            al = gelu(lo[w].astype(F32) * scale + offset)
            al = jnp.where((rowe - EDGE < valid) & (s > 0), al, 0.0)
            ah = gelu(hi[w].astype(F32) * scale + offset)
            ah = jnp.where(rowe + Lp < valid, ah, 0.0)
            ext[w, 0:EDGE] = al
            ext[w, EDGE : EDGE + Lp] = a
            ext[w, EDGE + Lp :] = ah
            top, end = w * Lp, (w + 1) * Lp
            Y3[top:end, 0:C] = ext[w, EDGE - DIL : EDGE - DIL + Lp].astype(BF16)
            Y3[top:end, C : 2 * C] = a.astype(BF16)
            Y3[top:end, 2 * C : 3 * C] = ext[w, EDGE + DIL : EDGE + DIL + Lp].astype(BF16)
        y = mm_nt(Y3[first * Lp : (first + wb // nh) * Lp], wf[...])
        for w in span:
            at = t * wb + w
            valid = lens[i * plan.nw + at] - s * Lp
            v = y[(w - first) * Lp : (w - first + 1) * Lp]
            c2[w] = v
            edge[0, at] = v[:EDGE].astype(BF16)
            edge[1, at] = v[Lp - EDGE :].astype(BF16)
            v = jnp.where(rowh < valid, v, 0.0)
            sums0 = sums0 + fold(v)
            sums1 = sums1 + fold(v * v)
    acc[0:1, 0:H] += unfold(sums0)
    acc[1:2, 0:H] += unfold(sums1)

    @pl.when(first_step())
    def _():
        meet(peers.count - 1)

    halo.start(t)

    @pl.when(last_step())
    def _():
        link[0][...] = acc[...]
        peers.start(link)
        sums[...] = peers.finish(link)[:, 0:H]
        halo.finish()


def point_kernel(plan, lens, c2, x2, cot, w_ref, pb, stats, par,
                 res, dz, pgrad, low, high, sums, bsum,
                 pw, a3s, a3T, dos, edge, acc, halo_sems, *link):
    t = pl.program_id(0)
    peers = group_peers(plan)
    halo = Halo(plan, edge, low, high, halo_sems, plan.steps)
    s, z, i, h = plan.place()
    Lp, C, H, wb, cs = plan.Lp, plan.C, plan.H, plan.wb, plan.cs
    M = wb * Lp

    @pl.when(first_step())
    def _():
        peers.greet()
        acc[...] = jnp.zeros_like(acc)
        for c in range(2):
            pw[:, c * (C // 2) : (c + 1) * (C // 2)] = w_ref[c, 0]

    @pl.when(t < plan.steps)
    def _():
        mean, rho = norm_of(stats[...], total_of(lens))
        scale = par[3:4, 0:H] * rho
        offset = par[4:5, 0:H] - mean * scale
        shift = -mean * rho
        rowc = rows_of((Lp, C))
        rowh = rows_of((Lp, H))
        block = pl.ds(pl.multiple_of(t * M, 128), M)
        bias = jnp.zeros((8, C), F32)
        parts = []
        for w in range(wb):
            valid = lens[i * plan.nw + t * wb + w] - s * Lp
            d = jnp.where(rowc < valid, cot[w].astype(F32), 0.0)
            bias = bias + fold(d)
            parts.append(d.astype(BF16))
        d = jnp.concatenate(parts, axis=0)
        dos[block] = d
        da = mm_nt(d, pw[...])
        s0, s1 = jnp.zeros((8, H), F32), jnp.zeros((8, H), F32)
        parts = []
        for w in range(wb):
            at = t * wb + w
            valid = lens[i * plan.nw + at] - s * Lp
            top, end = w * Lp, (w + 1) * Lp
            v = c2[w]
            act, slope = gelu_both(v * scale + offset)
            parts.append(jnp.where(rowh < valid, act, 0.0).astype(BF16))
            dzw = da[top:end] * slope
            dz[w] = dzw
            edge[0, at] = dzw[:EDGE].astype(BF16)
            edge[1, at] = dzw[Lp - EDGE :].astype(BF16)
            s0 = s0 + fold(dzw)
            s1 = s1 + fold(dzw * (v * rho + shift))
        a3 = jnp.concatenate(parts, axis=0)
        a3s[block] = a3
        a3T[:, block] = a3.T
        acc[0:1, 0:H] += unfold(s0)
        acc[0:1, H : 2 * H] += unfold(s1)
        acc[1:2] += unfold(bias)

    @pl.when(first_step())
    def _():
        meet(peers.count - 1)

    @pl.when(t < plan.steps)
    def _():
        halo.start(t)

    @pl.when(t == plan.steps - 1)
    def _():
        link[0][...] = acc[...]
        peers.start(link)

    @pl.when(t >= plan.steps)
    def _():
        u = t - plan.steps
        n = plan.nw // 2
        y = mm(a3s[pl.ds(pl.multiple_of(u * n * Lp, 128), n * Lp)], w_ref[h, 0])
        rowr = rows_of((Lp, y.shape[1]))
        for w in range(n):
            valid = lens[i * plan.nw + u * n + w] - s * Lp
            r = x2[w] + y[w * Lp : (w + 1) * Lp] + pb[2:3]
            r = jnp.where(rowr < valid, r, 0.0).astype(BF16).T
            for k in range(plan.g):
                res[k, w] = r[k * cs : (k + 1) * cs]

    @pl.when(last_step())
    def _():
        rows = pl.ds(pl.multiple_of(h * plan.Hh, 16), plan.Hh)
        pgrad[...] = mm(a3T[rows], dos[...]).astype(BF16)
        got = peers.finish(link)
        sums[0:1] = got[0:1, 0:H]
        sums[1:2] = got[0:1, H : 2 * H]
        bsum[...] = got[1:2]
        halo.finish()


def dilated_back_kernel(plan, lens, c2, clo, chi, dz3, zlo, zhi, x2, Y3, w_ref,
                        stats3, sums3, stats2, par, res,
                        dz2, grads, low, high, sums, res_got,
                        ext, Z3, wt, dcT, edge, acc, bulk_sems, halo_sems, *link):
    t = pl.program_id(0)
    peers = group_peers(plan)
    halo = Halo(plan, edge, low, high, halo_sems, 1)
    s, z, i, h = plan.place()
    Lp, C, H, wb, nw, g = plan.Lp, plan.C, plan.H, plan.wb, plan.nw, plan.g

    def bulk(off, n):
        to = lax.rem(i + off, g)
        rows = pl.ds(n * wb, wb)
        return pltpu.make_async_remote_copy(
            src_ref=res.at[to, rows],
            dst_ref=res_got.at[off, rows],
            send_sem=bulk_sems.at[0, off, n],
            recv_sem=bulk_sems.at[1, off, n],
            device_id=(s, h * g + to),
            device_id_type=MESH,
        )

    parts = [(off, n) for off in range(1, g) for n in range(plan.steps)]

    @pl.when(first_step())
    def _():
        peers.greet()
        acc[...] = jnp.zeros_like(acc)
        for k in range(plan.T2):
            for c in range(2):
                cols = slice(c * (C // 2), (c + 1) * (C // 2))
                wt[k * H : (k + 1) * H, cols] = w_ref[c, k]

        meet(peers.count - 1)
        for part in parts:
            bulk(*part).start()

    @pl.when(t < plan.steps)
    def _():
        total = total_of(lens)
        mean3, rho3 = norm_of(stats3[...], total)
        gr3 = par[3:4, 0:H] * rho3
        sg3 = sums3[0:1] / total
        gg3 = sums3[1:2] / total
        mean2, rho2 = norm_of(stats2[...], total)
        scale2 = par[0:1] * rho2
        offset2 = par[1:2] - mean2 * scale2
        rowh = rows_of((Lp, H))
        rowe = rows_of((EDGE, H))
        rowc = rows_of((Lp, C))

        by_v = -gr3 * rho3 * gg3
        by_1 = gr3 * (mean3 * rho3 * gg3 - sg3)
        shift2 = -mean2 * rho2

        def back(dz, v):
            return gr3 * dz + by_v * v + by_1

        for w in range(wb):
            valid = lens[i * nw + t * wb + w] - s * Lp
            d = jnp.where(rowh < valid, back(dz3[w], c2[w]), 0.0)
            dl = back(zlo[w].astype(F32), clo[w].astype(F32))
            dl = jnp.where((rowe - EDGE < valid) & (s > 0), dl, 0.0)
            dh = back(zhi[w].astype(F32), chi[w].astype(F32))
            dh = jnp.where(rowe + Lp < valid, dh, 0.0)
            ext[w, 0:EDGE] = dl
            ext[w, EDGE : EDGE + Lp] = d
            ext[w, EDGE + Lp :] = dh
            top, end = w * Lp, (w + 1) * Lp
            Z3[top:end, 0:H] = ext[w, EDGE + DIL : EDGE + DIL + Lp].astype(BF16)
            Z3[top:end, H : 2 * H] = d.astype(BF16)
            Z3[top:end, 2 * H : 3 * H] = ext[w, EDGE - DIL : EDGE - DIL + Lp].astype(BF16)

        y = mm(Z3[...], wt[...])

        M = wb * Lp
        dcT[:, pl.ds(pl.multiple_of(t * M, 128), M)] = Z3[:, H : 2 * H].T
        s0, s1 = jnp.zeros((8, C), F32), jnp.zeros((8, C), F32)
        for w in range(wb):
            at = t * wb + w
            valid = lens[i * nw + at] - s * Lp
            v = x2[w]
            dzw = y[w * Lp : (w + 1) * Lp] * gelu_slope(v * scale2 + offset2)
            dzw = jnp.where(rowc < valid, dzw, 0.0)
            dz2[w] = dzw
            edge[0, pl.ds(at, 1)] = dzw[0:1]
            edge[1, pl.ds(at, 1)] = dzw[Lp - 1 : Lp]
            s0 = s0 + fold(dzw)
            s1 = s1 + fold(dzw * (v * rho2 + shift2))
        acc[0:1] += unfold(s0)
        acc[1:2] += unfold(s1)

    @pl.when(t == plan.steps - 1)
    def _():
        link[0][...] = acc[...]
        peers.start(link)
        halo.start(0)

    @pl.when(t >= plan.steps)
    def _():
        rows = pl.ds(pl.multiple_of(h * plan.Hh, 16), plan.Hh)
        grads[...] = mm(dcT[rows], Y3[...]).astype(BF16)

    @pl.when(last_step())
    def _():
        sums[...] = peers.finish(link)
        halo.finish()
        for part in parts:
            bulk(*part).wait()


class Reduction:
    SEMS = 3

    def __init__(self, plan, out, give, mine, got, mid, spread, half, mate, sems):
        self.plan, self.out = plan, out
        self.give, self.mine, self.got, self.mid, self.spread = give, mine, got, mid, spread
        self.half, self.mate = half, mate
        self.sems = sems
        self.s, self.z, self.i, self.h = plan.place()
        self.c = lax.rem(self.s, 2)
        self.m = lax.div(self.s, 2)
        self.chips = plan.chips

    @staticmethod
    def scratch(plan):
        taps, wide = plan.T1 + 2, plan.C // 2
        full = (taps, plan.chips, plan.g, plan.rb, wide)
        part = (taps, plan.g, plan.rb, wide)
        return [
            pltpu.VMEM((taps, 2, plan.chips, plan.rb, wide), BF16),
            *[pltpu.VMEM(full, BF16)] * 5,
            *[pltpu.VMEM(part, BF16)] * 2,
            pltpu.SemaphoreType.DMA((2, taps, Reduction.SEMS + 2 * plan.chips + plan.g)),
        ]

    def copy(self, src, dst, tap, sem, device):
        return pltpu.make_async_remote_copy(
            src_ref=src,
            dst_ref=dst,
            send_sem=self.sems.at[0, tap, sem],
            recv_sem=self.sems.at[1, tap, sem],
            device_id=device,
            device_id_type=MESH,
        )

    def pair(self):
        return (2 * self.m + (1 - self.c), self.z)

    def chip(self, off):
        return lax.rem(self.m + off, self.chips)

    def phase0(self, k):
        return self.copy(self.give.at[k], self.got.at[k], k, 0, self.pair())

    def phase1(self, k, off, at):
        to = self.chip(off)
        dst = self.spread.at[k, at]
        return self.copy(self.mid.at[k, to], dst, k, 1 + off, (2 * to + self.c, self.z))

    def phase2(self, k, off):
        to = lax.rem(self.i + off, self.plan.g)
        device = (self.s, self.h * self.plan.g + to)
        return self.copy(
            self.half.at[k, to], self.mate.at[k, off], k, 1 + self.chips + off, device
        )

    def phase3(self, k, off, at):
        to = self.chip(off)
        sem = 1 + self.chips + self.plan.g + off
        src, dst = self.out.at[k, self.c, self.m], self.out.at[k, self.c, at]
        return self.copy(src, dst, k, sem, (2 * to + self.c, self.z))

    def phase4(self, k, c):
        return self.copy(self.out.at[k, c], self.out.at[k, c], k, 1, self.pair())

    def put(self, k, rows):
        wide = self.plan.C // 2
        for j in range(self.plan.g):
            for m in range(self.chips):
                v = rows(j, m)
                left, right = v[:, :wide], v[:, wide:]
                self.mine[k, m, j] = jnp.where(self.c == 0, left, right).astype(BF16)
                self.give[k, m, j] = jnp.where(self.c == 0, right, left).astype(BF16)
        self.phase0(k).start()

    def step1(self, k):
        self.phase0(k).wait()
        self.mid[k] = (self.mine[k].astype(F32) + self.got[k].astype(F32)).astype(BF16)
        for off in range(1, self.chips):
            self.phase1(k, off, self.m).start()

    def step2(self, k):
        for off in range(1, self.chips):
            self.phase1(k, off, self.m).wait_send()
            self.phase1(k, off, self.chip(self.chips - off)).wait_recv()
        self.spread[k, self.m] = self.mid[k, self.m]
        v = self.spread[k, 0].astype(F32)
        for n in range(1, self.chips):
            v = v + self.spread[k, n].astype(F32)
        self.half[k] = v.astype(BF16)
        for off in range(1, self.plan.g):
            self.phase2(k, off).start()

    def step3(self, k):
        for off in range(1, self.plan.g):
            self.phase2(k, off).wait()
        v = self.half[k, self.i].astype(F32)
        for off in range(1, self.plan.g):
            v = v + self.mate[k, off].astype(F32)
        self.out[k, self.c, self.m] = v.astype(BF16)
        for off in range(1, self.chips):
            self.phase3(k, off, self.m).start()

    def step4(self, k):
        for off in range(1, self.chips):
            self.phase3(k, off, self.m).wait_send()
            self.phase3(k, off, self.chip(self.chips - off)).wait_recv()
        self.phase4(k, self.c).start()

    def step5(self, k):
        self.phase4(k, self.c).wait_send()
        self.phase4(k, 1 - self.c).wait_recv()

    def stages(self):
        return [self.step1, self.step2, self.step3, self.step4]


def tail_kernel(plan, lens, dz2, zlo, zhi, x2, lo, hi, cot, hl, hr, x, X5_hbm, taps, grads, pgrad,
                stats2, sums2, par, stats1, par1,
                gz, gz_got, sums, summed,
                ext, D3, D0T, wcat, pick, eye, cols, y, part, acc, X5, X5_sems, bulk_sems, *rest):
    t = pl.program_id(0)
    s, z, i, h = plan.place()
    L, Lp, C, wb, g, nw = plan.L, plan.Lp, plan.C, plan.wb, plan.g, plan.nw
    Ch, cs, T1 = plan.Ch, plan.cs, plan.T1
    M = wb * Lp
    nD = plan.steps
    last = nD + T1 - 1
    peers = group_peers(plan)
    red = Reduction(plan, *rest[:9])
    link = rest[9:]

    def bulk(step, off, n):
        to = lax.rem(i + off, g)
        n2 = wb // 2
        return pltpu.make_async_remote_copy(
            src_ref=part.at[step, to, pl.ds(n * n2, n2)],
            dst_ref=gz_got.at[off, pl.ds(step * wb + n * n2, n2)],
            send_sem=bulk_sems.at[0, step, off, n],
            recv_sem=bulk_sems.at[1, step, off, n],
            device_id=(s, h * g + to),
            device_id_type=MESH,
        )

    def X5_copy(k):
        cols = pl.ds(pl.multiple_of(k * C, 128), C)
        return pltpu.make_async_copy(X5_hbm.at[:, cols], X5.at[k % 2], X5_sems.at[k % 2])

    others = [(off, n) for off in range(1, g) for n in range(2)]

    def send(step, n):
        for off in range(1, g):
            bulk(step, off, n).start()

    def when(at):
        return pl.when(t == min(at, last))

    @when(0)
    def _():
        peers.greet()
        acc[...] = jnp.zeros_like(acc)
        pick[...] = pick_matrix(L)
        eye[...] = eye_matrix(Ch, Ch, 0)
        mean, rho = norm_of(stats1[...], 2.0 * total_of(lens))
        scale = par1[5:6] * rho
        for k, row in enumerate((scale, par1[6:7] - mean * scale, rho, -mean * rho)):
            cols[k] = column(row, L)
        w = [taps[k].astype(F32) for k in range(5)]
        for r, parts in enumerate(
            ((w[0], w[1] + w[2], w[3] + w[4]), (w[0] + w[1], w[2] + w[3], w[4]))
        ):
            for k, v in enumerate(parts):
                wcat[r * Ch : (r + 1) * Ch, k * C : (k + 1) * C] = v.astype(BF16)

    @pl.when(t < nD)
    def _():
        total = total_of(lens)
        mean, rho = norm_of(stats2[...], total)
        gr = par[0:1] * rho
        sg = sums2[0:1] / total
        gg = sums2[1:2] / total
        rowc = rows_of((Lp, C))
        row1 = rows_of((1, C))

        by_dz = 0.5 * gr
        by_v = -0.5 * gr * rho * gg
        by_1 = 0.5 * gr * (mean * rho * gg - sg)
        lanes = lanes_of((Ch, L))

        def back(dout, dz, v):
            return 0.5 * dout + by_dz * dz + by_v * v + by_1

        def grad_of(w):
            at = t * wb + w
            valid = lens[i * nw + at] - s * Lp
            d = back(cot[w].astype(F32), dz2[w], x2[w])
            d = jnp.where(rowc < valid, d, 0.0)
            one = pl.ds(at, 1)
            dl = back(hl[2, one, :], zlo[one, :], lo[w, EDGE - 1 : EDGE].astype(F32))
            dl = jnp.where((row1 - 1 < valid) & (s > 0), dl, 0.0)
            dh = back(hr[2, one, :], zhi[one, :], hi[w, 0:1].astype(F32))
            dh = jnp.where(row1 + Lp < valid, dh, 0.0)
            ext[w, 7:8] = dl
            ext[w, 8 : 8 + Lp] = d
            ext[w, 8 + Lp : 9 + Lp] = dh
            top, end = w * Lp, (w + 1) * Lp
            D3[top:end, 0:C] = ext[w, 9 : 9 + Lp].astype(BF16)
            D3[top:end, C : 2 * C] = d.astype(BF16)
            D3[top:end, 2 * C : 3 * C] = ext[w, 7 : 7 + Lp].astype(BF16)

        def through(w):
            valid = 2 * lens[i * nw + t * wb + w] - s * L
            top, end = w * Lp, (w + 1) * Lp
            v = mm_nt(eye[...], x[w])
            da = jnp.concatenate([y[0:Ch, top:end], y[Ch:, top:end]], axis=1)
            da = mm(da.astype(BF16), pick[...])
            dzw = da * gelu_slope(v * cols[0] + cols[1])
            dzw = jnp.where(lanes < valid, dzw, 0.0)
            acc[0] += dzw
            acc[1] += dzw * (v * cols[2] + cols[3])
            dzw = dzw.astype(BF16)
            for k in range(g):
                part[t, k, w] = dzw[k * cs : (k + 1) * cs]

        nh = 2 if wb % 2 == 0 and wb * Lp // 2 % 128 == 0 else 1
        n = wb // nh
        for hf in range(nh):
            for w in range(hf * n, (hf + 1) * n):
                grad_of(w)
            rows = slice(hf * n * Lp, (hf + 1) * n * Lp)
            y[:, rows] = mm_nt(wcat[...], D3[rows])
        half = D3[:, pl.ds(pl.multiple_of(C + h * Ch, 128), Ch)]
        D0T[:, pl.ds(pl.multiple_of(t * M, 128), M)] = half.T
        for w in range(wb):
            through(w)
        gz[...] = part[t, i]

    @when(0)
    def _():
        meet(peers.count - 1)
        hs = plan.H // plan.nz
        rb = plan.rb
        for u in range(2):

            def rows(j, m, u=u):
                side, r = m * rb // hs, m * rb % hs
                n = 2 * side + u
                rows = slice(j * hs + r, j * hs + r + rb)
                v = grads[rows, n * C : (n + 1) * C] if n < plan.T2 else pgrad[rows]
                return v.astype(F32)

            red.put(T1 + u, rows)

    early = max(nD // 2, 1)

    @pl.when(t < early)
    def _():
        send(t, 0)
        send(t, 1)

    @when(nD - 1)
    def _():
        X5_copy(0).start()

    stages = red.stages()
    for n, at in enumerate((1, 2, nD, nD + 3)):

        @when(at)
        def _():
            for u in range(2):
                stages[n](T1 + u)

    @when(nD - 1)
    def _():
        packet = link[0]
        packet[...] = jnp.zeros_like(packet)
        packet[0:1, 0:Ch] = jnp.sum(acc[0].T, axis=0, keepdims=True)
        packet[1:2, 0:Ch] = jnp.sum(acc[1].T, axis=0, keepdims=True)
        peers.start(link)

    @pl.when(t >= nD)
    def _():
        k = t - nD

        @pl.when(k < T1 - 1)
        def _():
            X5_copy(k + 1).start()

        X5_copy(k).wait()
        y[0:Ch, 0:C] = mm(D0T[...], X5[lax.rem(k, 2)])
        rb = plan.rb
        red.put(k, lambda j, m: y[j * cs + m * rb : j * cs + (m + 1) * rb, 0:C])
        for n, stage in enumerate(stages[:2]):
            pl.when(k > n)(partial(stage, k - 1 - n))

    held = [(step, n) for step in range(early, nD) for n in range(2)]
    for at, pair in zip((nD, nD + 1, nD + 3), held[:3]):

        @when(at)
        def _():
            send(*pair)

    @when(last)
    def _():
        for n, stage in enumerate(stages[:2]):
            for k in range(T1 - 1 - n, T1):
                stage(k)
        for pair in held[3:]:
            send(*pair)
        for stage in stages[2:]:
            for k in range(T1):
                stage(k)
        sums[...] = peers.finish(link)[:, 0:Ch]
        for k in range(T1 + 2):
            red.step5(k)
        summed[...] = red.out[...]
        for step in range(nD):
            for other in others:
                bulk(step, *other).wait()


def input_grad_kernel(plan, lens, x, gz, gz_got, stats, sums, par1, res, res_got, summed,
                      sums2, sums3, bsum,
                      out, out_result, conv_grad, dil_grad, point_grad,
                      g1, b1, g2, b2, g3, b3, pb, eye, cols, xt):
    t = pl.program_id(0)
    s, z, i, h = plan.place()
    L, Ch, cs, wb = plan.L, plan.Ch, plan.cs, plan.wb
    mine = pl.ds(pl.multiple_of(i * cs, 16), cs)

    @pl.when(first_step())
    def _():
        n = 2.0 * total_of(lens)
        mean, rho = norm_of(stats[...], n)
        gr = par1[5:6] * rho
        gg = sums[1:2] / n * rho
        for k, row in enumerate((gr, -gr * gg, gr * (mean * gg - sums[0:1] / n))):
            xt[...] = column(row, L)
            cols[k] = xt[mine]
        eye[...] = eye_matrix(cs, Ch, i * cs)

        def mine_of(src, at, which, count, *dsts):
            n = dsts[0].shape[1]
            for k in range(count):

                @pl.when(which == k)
                def _():
                    for dst, r in zip(dsts, at):
                        dst[...] = src[r : r + 1, k * n : (k + 1) * n]

        mine_of(sums, (1, 0), i, plan.g, g1, b1)
        mine_of(sums2, (1, 0), z, plan.nz, g2, b2)
        mine_of(sums3, (1, 0), z, plan.nz, g3, b3)
        mine_of(bsum, (0,), z, plan.nz, pb)

    own = lax.div(t, plan.steps) == i
    for w in range(wb):
        out_result[w] = jnp.where(own, res[0, w].astype(F32), res_got[0, w].astype(F32)).astype(BF16)

    C, T1, hs, rb, wide = plan.C, plan.T1, plan.H // plan.nz, plan.rb, plan.C // 2
    count = plan.NW // wb
    turns = min(count, plan.chips)
    per, every = plan.chips // turns, count // turns

    def spread(turn):
        for n in range(per):
            m = turn * per + n
            side, r = m * rb // hs, m * rb % hs
            for c in range(2):
                at = slice(c * wide, (c + 1) * wide)
                for k in range(T1):
                    conv_grad[k, n * rb : (n + 1) * rb, at] = summed[k, c, n].astype(F32)
                for u in range(2):
                    v = summed[T1 + u, c, n].astype(F32)
                    if 2 * side + u < plan.T2:
                        dil_grad[2 * side + u, r : r + rb, at] = v
                    else:
                        point_grad[r : r + rb, at] = v

    for turn in range(turns):
        pl.when(t == turn * every)(partial(spread, turn))

    lanes = lanes_of((cs, L))
    for w in range(wb):
        valid = 2 * lens[t * wb + w] - s * L
        v = mm_nt(eye[...], x[w])
        dz = jnp.where(own, gz[w].astype(F32), gz_got[0, w].astype(F32))
        r = cols[0] * dz + v * cols[1] + cols[2]
        out[w] = jnp.where(lanes < valid, r, 0.0).astype(BF16)


def call(kernel, plan, name, steps, ins, outs, scratch, flops, nbytes, cid=None):
    extra = {} if cid is None else dict(collective_id=cid, has_side_effects=True)
    return pl.pallas_call(
        partial(kernel, plan),
        grid=(steps,),
        in_specs=[SMEM] + [spec for spec, _ in ins],
        out_specs=[spec for spec, _, _ in outs],
        out_shape=[jax.ShapeDtypeStruct(shape, dtype) for _, shape, dtype in outs],
        scratch_shapes=scratch,
        compiler_params=pltpu.CompilerParams(vmem_limit_bytes=VMEM_LIMIT, **extra),
        cost_estimate=pl.CostEstimate(
            flops=int(flops), bytes_accessed=int(nbytes), transcendentals=0
        ),
        name=name,
    )


def per_device(
    inputs,
    lengths,
    input_gain,
    input_shift,
    conv_weight,
    branch_gain,
    branch_shift,
    dilated_tap_weight,
    mixer_gain,
    mixer_shift,
    point_weight,
    point_bias,
    cotangent,
):
    NW, L, C = inputs.shape
    Lp = L // 2
    nz = lax.axis_size("ch")
    R = 2
    plan = Plan(
        ns=lax.axis_size("seq"),
        nz=nz,
        R=R,
        NW=NW,
        L=L,
        C=C,
        H=mixer_gain.shape[0] * nz,
        T1=conv_weight.shape[0],
        T2=dilated_tap_weight.shape[0],
        wb=min(NW * R // nz, max(1, 512 // Lp)),
    )
    g, nw, cs, Ch, H, Hh, wb = plan.g, plan.nw, plan.cs, plan.Ch, plan.H, plan.Hh, plan.wb
    T1, T2, steps = plan.T1, plan.T2, plan.steps
    M = wb * Lp
    hs = H // nz
    lens = lengths.astype(jnp.int32)

    def row(a):
        return a.reshape(1, a.shape[0])

    def grp():
        return lax.rem(lax.axis_index("ch"), g)

    def half():
        return lax.div(lax.axis_index("ch"), g)

    def core():
        return lax.rem(lax.axis_index("seq"), 2)

    def chip4():
        return lax.div(lax.axis_index("seq"), plan.ns // 4)

    def whole(*shape):
        return pl.BlockSpec(shape, lambda t: (0,) * len(shape), pipeline_mode=pl.Buffered(1))

    def const(*shape):
        return pl.BlockSpec(shape, lambda t: (0,) * len(shape))

    def win(*shape):
        return pl.BlockSpec(shape, lambda t: (t,) + (0,) * (len(shape) - 1))

    def arg_win(n, width):
        return pl.BlockSpec((wb, n, width), lambda t: (grp() * steps + t, 0, 0))

    def ins(*pairs):
        return [p for p in pairs]

    share = NW // nz
    nm = max(1, share // wb)

    def edge_spec(n):
        return pl.BlockSpec(
            (nw, 16, C), lambda t: (grp(), n, 0), pipeline_mode=pl.Buffered(1)
        )

    def head_block(t):
        own = lax.div(lax.axis_index("ch") * share, wb) + t
        return jnp.where(t < nm, own, grp() * steps + t - nm), 0, 0

    def after(*shape):
        return pl.BlockSpec(
            shape, lambda t: (jnp.maximum(t - nm, 0),) + (0,) * (len(shape) - 1)
        )

    pairs = ins(
        (pl.BlockSpec((wb, L, C), head_block), inputs),
        (edge_spec(0), inputs),
        (edge_spec(L // 16 - 1), inputs),
        (edge_spec(0), cotangent),
        (edge_spec(Lp // 16 - 1), cotangent),
        (whole(1, cs), row(branch_gain)),
        (whole(1, cs), row(branch_shift)),
        (whole(1, cs), row(point_bias)),
        (whole(1, H // nz), row(mixer_gain)),
        (whole(1, H // nz), row(mixer_shift)),
        (ANY, conv_weight.reshape(T1 * C, C)),
        (whole(C), input_gain),
        (whole(C), input_shift),
        (
            pl.BlockSpec(
                (1, hs, C // 2),
                lambda t: (jnp.minimum(chip4(), T2 - 1), 0, core()),
                pipeline_mode=pl.Buffered(1),
            ),
            jnp.swapaxes(dilated_tap_weight, 1, 2),
        ),
        (
            pl.BlockSpec(
                (hs, C // 2), lambda t: (0, core()), pipeline_mode=pl.Buffered(1)
            ),
            point_weight,
        ),
    )
    plane, line, group = plane_peers(plan), line_peers(plan), group_peers(plan)
    X5, x2, lo2, hi2, stats2, stats1, par, hl, hr, full, _ = call(
        lambda plan, *refs: head_kernel(plan, nm, *refs),
        plan,
        "head",
        nm + steps,
        pairs,
        [
            (after(M, T1 * C), (nw * Lp, T1 * C), BF16),
            (after(wb, Lp, C), (nw, Lp, C), F32),
            (ANY, (nw, EDGE, C), BF16),
            (ANY, (nw, EDGE, C), BF16),
            (const(2, C), (2, C), F32),
            (const(2, C), (2, C), F32),
            (const(8, C), (8, C), F32),
            (const(3, nw, C), (3, nw, C), F32),
            (const(3, nw, C), (3, nw, C), F32),
            (ANY, (2, T2 + 1, nz, hs, C // 2), BF16),
            (ANY, (nz, hs, C // 2), BF16),
        ],
        [
            pltpu.VMEM((2, 8, C), F32),
            pltpu.VMEM((3, nw, C), F32),
            pltpu.VMEM((3, nw, C), F32),
            pltpu.VMEM((2, 3, nw, C), F32),
            pltpu.VMEM((T1 * Lp, L), BF16),
            pltpu.VMEM((2, nw, EDGE, C), BF16),
            pltpu.VMEM((2, C), F32),
            pltpu.VMEM((T1 * C, C), BF16),
            pltpu.SemaphoreType.DMA,
            pltpu.VMEM((hs, C // 2), BF16),
            pltpu.SemaphoreType.DMA((2, nz)),
            pltpu.SemaphoreType.DMA((2, plan.ns // 2 + 1, Gather.PARTS)),
        ]
        + halo_scratch(1)
        + halo_scratch(steps)
        + plane.scratch(2, C)
        + line.scratch(3, C)
        + group.scratch(2, C),
        2 * nw * Lp * T1 * C * C,
        nw * Lp * C * 20,
        cid=1,
    )(lens, *[a for _, a in pairs])

    full = full.reshape(2, T2 + 1, H, C // 2)
    taps_spec = whole(2, T2, H, C // 2)
    pw_spec = pl.BlockSpec(
        (2, 1, H, C // 2), lambda t: (0, T2, 0, 0), pipeline_mode=pl.Buffered(1)
    )

    pairs = ins(
        (win(wb, Lp, C), x2),
        (win(wb, EDGE, C), lo2),
        (win(wb, EDGE, C), hi2),
        (taps_spec, full),
        (whole(2, C), stats2),
        (whole(8, C), par),
    )
    Y3, c2, lo3, hi3, stats3 = call(
        dilated_kernel,
        plan,
        "dilated",
        steps,
        pairs,
        [
            (win(M, T2 * C), (nw * Lp, T2 * C), BF16),
            (win(wb, Lp, H), (nw, Lp, H), F32),
            (ANY, (nw, EDGE, H), BF16),
            (ANY, (nw, EDGE, H), BF16),
            (const(2, H), (2, H), F32),
        ],
        [
            pltpu.VMEM((wb, Lp + 2 * EDGE, C), F32),
            pltpu.VMEM((H, T2 * C), BF16),
            pltpu.VMEM((2, nw, EDGE, H), BF16),
            pltpu.VMEM((2, C), F32),
        ]
        + halo_scratch(steps)
        + group.scratch(2, C),
        2 * nw * Lp * T2 * C * H,
        nw * Lp * C * 12,
        cid=3,
    )(lens, *[a for _, a in pairs])

    def early(*shape):
        return pl.BlockSpec(
            shape, lambda t: (jnp.minimum(t, steps - 1),) + (0,) * (len(shape) - 1)
        )

    def late(t):
        return jnp.maximum(t - steps, 0)

    pairs = ins(
        (early(wb, Lp, H), c2),
        (pl.BlockSpec((nw // 2, Lp, Ch), lambda t: (late(t), 0, half())), x2),
        (
            pl.BlockSpec(
                (wb, Lp, C), lambda t: (grp() * steps + jnp.minimum(t, steps - 1), 0, 0)
            ),
            cotangent,
        ),
        (pw_spec, full),
        (pl.BlockSpec((8, Ch), lambda t: (0, half()), pipeline_mode=pl.Buffered(1)), par),
        (whole(2, H), stats3),
        (whole(8, C), par),
    )
    res, dz3, pgrad, zlo3, zhi3, sums3, bsum = call(
        point_kernel,
        plan,
        "point",
        steps + 2,
        pairs,
        [
            (
                pl.BlockSpec((g, nw // 2, cs, Lp), lambda t: (0, late(t), 0, 0)),
                (g, nw, cs, Lp),
                BF16,
            ),
            (early(wb, Lp, H), (nw, Lp, H), F32),
            (const(Hh, C), (Hh, C), BF16),
            (ANY, (nw, EDGE, H), BF16),
            (ANY, (nw, EDGE, H), BF16),
            (const(2, H), (2, H), F32),
            (const(1, C), (1, C), F32),
        ],
        [
            pltpu.VMEM((H, C), BF16),
            pltpu.VMEM((nw * Lp, H), BF16),
            pltpu.VMEM((H, nw * Lp), BF16),
            pltpu.VMEM((nw * Lp, C), BF16),
            pltpu.VMEM((2, nw, EDGE, H), BF16),
            pltpu.VMEM((2, C), F32),
        ]
        + halo_scratch(steps)
        + group.scratch(2, C),
        5 * nw * Lp * C * H,
        nw * Lp * C * 10,
        cid=4,
    )(lens, *[a for _, a in pairs])

    pairs = ins(
        (early(wb, Lp, H), c2),
        (early(wb, EDGE, H), lo3),
        (early(wb, EDGE, H), hi3),
        (early(wb, Lp, H), dz3),
        (early(wb, EDGE, H), zlo3),
        (early(wb, EDGE, H), zhi3),
        (early(wb, Lp, C), x2),
        (pl.BlockSpec((nw * Lp, C), lambda t: (0, late(t))), Y3),
        (taps_spec, full),
        (whole(2, H), stats3),
        (whole(2, H), sums3),
        (whole(2, C), stats2),
        (whole(8, C), par),
        (ANY, res),
    )
    dz2, grads, zlo2, zhi2, sums2, res_got = call(
        dilated_back_kernel,
        plan,
        "dilated_back",
        steps + T2,
        pairs,
        [
            (early(wb, Lp, C), (nw, Lp, C), F32),
            (pl.BlockSpec((Hh, C), lambda t: (0, late(t))), (Hh, T2 * C), BF16),
            (ANY, (nw, C), F32),
            (ANY, (nw, C), F32),
            (const(2, C), (2, C), F32),
            (ANY, (g, nw, cs, Lp), BF16),
        ],
        [
            pltpu.VMEM((wb, Lp + 2 * EDGE, H), F32),
            pltpu.VMEM((M, T2 * H), BF16),
            pltpu.VMEM((T2 * H, C), BF16),
            pltpu.VMEM((H, nw * Lp), BF16),
            pltpu.VMEM((2, nw, C), F32),
            pltpu.VMEM((2, C), F32),
            pltpu.SemaphoreType.DMA((2, g, steps)),
        ]
        + halo_scratch(1)
        + group.scratch(2, C),
        4 * nw * Lp * T2 * C * H,
        nw * Lp * C * 20,
        cid=5,
    )(lens, *[a for _, a in pairs])

    def half_of(n):
        return pl.BlockSpec((n, Ch), lambda t: (0, half()), pipeline_mode=pl.Buffered(1))

    chips, rb = plan.chips, plan.rb
    sshape = (T1 + 2, 2, chips, rb, C // 2)
    pairs = ins(
        (early(wb, Lp, C), dz2),
        (whole(nw, C), zlo2),
        (whole(nw, C), zhi2),
        (early(wb, Lp, C), x2),
        (early(wb, EDGE, C), lo2),
        (early(wb, EDGE, C), hi2),
        (
            pl.BlockSpec(
                (wb, Lp, C), lambda t: (grp() * steps + jnp.minimum(t, steps - 1), 0, 0)
            ),
            cotangent,
        ),
        (whole(3, nw, C), hl),
        (whole(3, nw, C), hr),
        (
            pl.BlockSpec(
                (wb, L, Ch), lambda t: (grp() * steps + jnp.minimum(t, steps - 1), 0, half())
            ),
            inputs,
        ),
        (ANY, X5),
        (
            pl.BlockSpec(
                (T1, Ch, C), lambda t: (0, half(), 0), pipeline_mode=pl.Buffered(1)
            ),
            conv_weight,
        ),
        (whole(Hh, T2 * C), grads),
        (whole(Hh, C), pgrad),
        (whole(2, C), stats2),
        (whole(2, C), sums2),
        (whole(8, C), par),
        (half_of(2), stats1),
        (half_of(8), par),
    )
    gz, gz_got, sums1, summed = call(
        tail_kernel,
        plan,
        "tail",
        steps + T1,
        pairs,
        [
            (early(wb, cs, L), (nw, cs, L), BF16),
            (ANY, (g, nw, cs, L), BF16),
            (const(2, Ch), (2, Ch), F32),
            (const(*sshape), sshape, BF16),
        ],
        [
            pltpu.VMEM((wb, Lp + 16, C), F32),
            pltpu.VMEM((M, 3 * C), BF16),
            pltpu.VMEM((Ch, nw * Lp), BF16),
            pltpu.VMEM((2 * Ch, 3 * C), BF16),
            pltpu.VMEM((L, L), BF16),
            pltpu.VMEM((Ch, Ch), BF16),
            pltpu.VMEM((4, Ch, L), F32),
            pltpu.VMEM((2 * Ch, max(M, C)), F32),
            pltpu.VMEM((steps, g, wb, cs, L), BF16),
            pltpu.VMEM((2, Ch, L), F32),
            pltpu.VMEM((2, nw * Lp, C), BF16),
            pltpu.SemaphoreType.DMA((2,)),
            pltpu.SemaphoreType.DMA((2, steps, g, 2)),
        ]
        + Reduction.scratch(plan)
        + group.scratch(2, C),
        2 * nw * Lp * (6 + T1) * C * Ch,
        nw * Lp * C * 40,
        cid=6,
    )(lens, *[a for _, a in pairs])

    count = NW // wb
    turns = min(count, chips)

    def own_block(t):
        return jnp.where(lax.div(t, steps) == grp(), lax.rem(t, steps), 0)

    def got_slot(t):
        off = lax.rem(grp() - lax.div(t, steps) + g, g)
        return jnp.maximum(off, 1), jnp.where(off > 0, lax.rem(t, steps), 0)

    pairs = ins(
        (pl.BlockSpec((wb, L, Ch), lambda t: (t, 0, half())), inputs),
        (pl.BlockSpec((wb, cs, L), lambda t: (own_block(t), 0, 0)), gz),
        (pl.BlockSpec((1, wb, cs, L), lambda t: got_slot(t) + (0, 0)), gz_got),
        (half_of(2), stats1),
        (whole(2, Ch), sums1),
        (half_of(8), par),
        (pl.BlockSpec((1, wb, cs, Lp), lambda t: (grp(), own_block(t), 0, 0)), res),
        (pl.BlockSpec((1, wb, cs, Lp), lambda t: got_slot(t) + (0, 0)), res_got),
        (
            pl.BlockSpec(
                (T1 + 2, 2, chips // turns, rb, C // 2),
                lambda t: (0, 0, t * turns // count, 0, 0),
            ),
            summed,
        ),
        (whole(2, C), sums2),
        (whole(2, H), sums3),
        (whole(1, C), bsum),
    )
    outs = call(
        input_grad_kernel,
        plan,
        "input_grad",
        NW // wb,
        pairs,
        [
            (win(wb, cs, L), (NW, cs, L), BF16),
            (win(wb, cs, Lp), (NW, cs, Lp), BF16),
            (
                pl.BlockSpec((T1, cs // turns, C), lambda t: (0, t * turns // count, 0)),
                (T1, cs, C),
                F32,
            ),
            (const(T2, hs, C), (T2, hs, C), F32),
            (const(hs, C), (hs, C), F32),
        ]
        + [(const(1, n), (1, n), F32) for n in (cs, cs, cs, cs, hs, hs, cs)],
        [
            pltpu.VMEM((cs, Ch), BF16),
            pltpu.VMEM((3, cs, L), F32),
            pltpu.VMEM((Ch, L), F32),
        ],
        2 * NW * L * Ch * cs,
        NW * L * cs * 8,
    )(lens, *[a for _, a in pairs])
    grad, result, conv_grad, dil_grad, point_grad = outs[:5]
    g1, b1, g2, b2, g3, b3, pb = [a[0] for a in outs[5:]]
    return (
        jnp.swapaxes(result, 1, 2),
        jnp.swapaxes(grad, 1, 2),
        jnp.swapaxes(conv_grad, 1, 2),
        g1,
        b1,
        g2,
        b2,
        jnp.swapaxes(dil_grad, 1, 2),
        g3,
        b3,
        point_grad,
        pb,
    )


def solution(mesh):
    in_specs = (
        P(None, "seq", None),
        P(),
        P(),
        P(),
        P(),
        P("ch"),
        P("ch"),
        P(None, None, "ch"),
        P("ch"),
        P("ch"),
        P("ch", None),
        P("ch"),
        P(None, "seq", None),
    )
    out_specs = (
        P(None, "seq", "ch"),
        P(None, "seq", "ch"),
        P(None, None, "ch"),
        P("ch"),
        P("ch"),
        P("ch"),
        P("ch"),
        P(None, None, "ch"),
        P("ch"),
        P("ch"),
        P("ch", None),
        P("ch"),
    )
    return jax.shard_map(
        per_device, mesh=mesh, in_specs=in_specs, out_specs=out_specs, check_vma=False
    )
```

```python
from functools import partial
from typing import NamedTuple

import jax
import jax.numpy as jnp
from jax import lax
from jax.experimental import pallas as pl
from jax.experimental.pallas import tpu as pltpu
from jax.sharding import PartitionSpec as P

DIL = 14
EDGE = 16
EPS = 1e-05
GC0 = 0.7978845608028654
GC1 = 0.044715
F32 = jnp.float32
BF16 = jnp.bfloat16
MESH = pl.DeviceIdType.MESH
VMEM_LIMIT = 58 * 1024 * 1024
ANY = pl.BlockSpec(memory_space=pl.ANY)
SMEM = pl.BlockSpec(memory_space=pltpu.SMEM)


class Plan(NamedTuple):
    ns: int
    nz: int
    R: int
    NW: int
    L: int
    C: int
    H: int
    T1: int
    T2: int
    wb: int

    @property
    def g(self):
        return self.nz // self.R

    @property
    def nw(self):
        return self.NW // self.g

    @property
    def Lp(self):
        return self.L // 2

    @property
    def cs(self):
        return self.C // self.nz

    @property
    def Ch(self):
        return self.C // self.R

    @property
    def Hh(self):
        return self.H // self.R

    @property
    def steps(self):
        return self.nw // self.wb

    @property
    def res_parts(self):
        return max(1, self.steps - 1)

    @property
    def chips(self):
        return self.ns // 2

    @property
    def rb(self):
        return self.cs // self.chips

    def place(self):
        s, z = lax.axis_index("seq"), lax.axis_index("ch")
        return s, z, lax.rem(z, self.g), lax.div(z, self.g)


def gelu(z):
    t = jnp.tanh(z * (GC0 + (GC0 * GC1) * (z * z)))
    return z * (0.5 + 0.5 * t)


def gelu_both(z):
    sq = z * z
    t = jnp.tanh(z * (GC0 + (GC0 * GC1) * sq))
    h = 0.5 + 0.5 * t
    v = z * h
    return v, h + v * (1.0 - t) * (GC0 + (3.0 * GC0 * GC1) * sq)


def gelu_slope(z):
    return gelu_both(z)[1]


def fold(v):
    return jnp.sum(v.reshape(v.shape[0] // 8, 8, v.shape[1]), axis=0)


def unfold(v):
    return jnp.sum(v, axis=0, keepdims=True)


def rows_of(shape):
    return lax.broadcasted_iota(jnp.int32, shape, 0)


def lanes_of(shape):
    return lax.broadcasted_iota(jnp.int32, shape, 1)


def total_of(lens):
    n = lens[0]
    for k in range(1, lens.shape[0]):
        n = n + lens[k]
    return n.astype(F32)


def norm_of(stats, total):
    mean = stats[0:1] / total
    square = stats[1:2] / total
    return mean, lax.rsqrt(square - mean * mean + EPS)


def flat(ref):
    return ref[...].reshape(1, ref.shape[0])


def column(row, n):
    return jnp.broadcast_to(row, (n, row.shape[1])).T


def mm(a, b):
    return jnp.dot(a, b, preferred_element_type=F32)


def mm_nt(a, b):
    return lax.dot_general(a, b, (((1,), (1,)), ((), ())), preferred_element_type=F32)


def mm_tn(a, b):
    return lax.dot_general(a, b, (((0,), (0,)), ((), ())), preferred_element_type=F32)


def mm_tt(a, b):
    return lax.dot_general(a, b, (((0,), (1,)), ((), ())), preferred_element_type=F32)


def eye_matrix(n, m, first):
    return jnp.where(lanes_of((n, m)) == rows_of((n, m)) + first, 1.0, 0.0).astype(BF16)


def pick_matrix(L):
    r, n = rows_of((L, L)), lanes_of((L, L))
    bin_of = 2 * r - jnp.where(r >= L // 2, L - 1, 0)
    return jnp.where(n == bin_of, 1.0, 0.0).astype(BF16)


class Peers:
    def __init__(self, count, me, device):
        self.count, self.me, self.device = count, me, device

    def other(self, off):
        return lax.rem(self.me + off, self.count)

    def greet(self, more=()):
        barrier = pltpu.get_barrier_semaphore()
        devices = [self.device(self.other(off)) for off in range(1, self.count)]
        for device in (*devices, *more):
            pl.semaphore_signal(barrier, inc=1, device_id=device, device_id_type=MESH)

    def copy(self, link, slot, off):
        packet, buf, send, recv = link
        return pltpu.make_async_remote_copy(
            src_ref=packet,
            dst_ref=buf.at[slot],
            send_sem=send.at[off],
            recv_sem=recv.at[slot],
            device_id=self.device(self.other(off)),
            device_id_type=MESH,
        )

    def start(self, link):
        for off in range(1, self.count):
            self.copy(link, self.me, off).start()

    def finish(self, link):
        packet, buf = link[:2]
        buf[self.me] = packet[...]
        for off in range(1, self.count):
            self.copy(link, self.other(off), off).wait_recv()
        acc = buf[0]
        for q in range(1, self.count):
            acc = acc + buf[q]
        for off in range(1, self.count):
            self.copy(link, self.me, off).wait_send()
        return acc

    def scratch(self, rows, width):
        return [
            pltpu.VMEM((rows, width), F32),
            pltpu.VMEM((self.count, rows, width), F32),
            pltpu.SemaphoreType.DMA((self.count,)),
            pltpu.SemaphoreType.DMA((self.count,)),
        ]


def group_peers(plan):
    s, z, i, h = plan.place()
    g = plan.g
    return Peers(plan.ns * g, s * g + i, lambda q: (lax.div(q, g), h * g + lax.rem(q, g)))


def plane_peers(plan):
    s, z, i, h = plan.place()
    return Peers(plan.ns, s, lambda q: (q, z))


def line_peers(plan):
    s, z, i, h = plan.place()
    return Peers(plan.nz, z, lambda q: (s, q))


def meet(count):
    pl.semaphore_wait(pltpu.get_barrier_semaphore(), count)


class Halo:
    def __init__(self, plan, edge, low, high, sems, parts):
        self.edge, self.low, self.high, self.sems, self.parts = edge, low, high, sems, parts
        s, z, _, _ = plan.place()
        self.left = (lax.rem(s + plan.ns - 1, plan.ns), z)
        self.right = (lax.rem(s + 1, plan.ns), z)
        self.n = low.shape[0] // parts

    def copies(self, part):
        rows = pl.ds(part * self.n, self.n)
        return [
            pltpu.make_async_remote_copy(
                src_ref=self.edge.at[side, rows],
                dst_ref=dst.at[rows],
                send_sem=self.sems.at[0, side, part],
                recv_sem=self.sems.at[1, side, part],
                device_id=dev,
                device_id_type=MESH,
            )
            for side, (dst, dev) in enumerate(((self.high, self.left), (self.low, self.right)))
        ]

    def start(self, part):
        for c in self.copies(part):
            c.start()

    def finish(self):
        for part in range(self.parts):
            for c in self.copies(part):
                c.wait()


def halo_scratch(parts):
    return [pltpu.SemaphoreType.DMA((2, 2, parts))]


class Gather:
    PARTS = 2

    def __init__(self, plan, sems, line_sems, part, stripe, full):
        self.plan, self.part, self.full, self.sems = plan, part, full, sems
        self.stripe, self.line_sems = stripe, line_sems
        self.s, self.z, self.i, self.h = plan.place()
        self.c, self.m = lax.rem(self.s, 2), lax.div(self.s, 2)
        self.chips = plan.ns // 2
        self.every = self.chips // 4
        self.tap = lax.div(self.m, self.every)
        self.owner = lax.rem(self.m, self.every) == 0
        self.rows = plan.H // plan.nz

    def others(self):
        g, nz = self.plan.g, self.plan.nz
        return [(self.s, lax.rem(self.h * g + g + r, nz)) for r in range(nz - g)]

    def copy(self, src, dst, sem, device):
        return pltpu.make_async_remote_copy(
            src_ref=src,
            dst_ref=dst,
            send_sem=self.sems.at[(0,) + sem],
            recv_sem=self.sems.at[(1,) + sem],
            device_id=device,
            device_id_type=MESH,
        )

    def line(self, off, at):
        to = lax.rem(self.z + off, self.plan.nz)
        return pltpu.make_async_remote_copy(
            src_ref=self.part,
            dst_ref=self.stripe.at[at],
            send_sem=self.line_sems.at[0, off],
            recv_sem=self.line_sems.at[1, off],
            device_id=(self.s, to),
            device_id_type=MESH,
        )

    def own_rows(self):
        return pltpu.make_async_copy(
            self.part, self.stripe.at[self.z], self.line_sems.at[0, 0]
        )

    def line_start(self):
        @pl.when(self.owner)
        def _():
            self.own_rows().start()
            for off in range(1, self.plan.nz):
                self.line(off, self.z).start()

    def line_finish(self):
        @pl.when(self.owner)
        def _():
            self.own_rows().wait()
            for off in range(1, self.plan.nz):
                self.line(off, self.z).wait_send()
                at = lax.rem(self.z + self.plan.nz - off, self.plan.nz)
                self.line(off, at).wait_recv()

    def half(self, ref, n):
        rows = self.plan.nz // self.PARTS
        return ref.at[pl.ds(n * rows, rows)]

    def own_stripe(self):
        return pltpu.make_async_copy(
            self.stripe, self.full.at[self.c, self.tap], self.sems.at[0, 0, 0]
        )

    def chip(self, off, n):
        to = lax.rem(self.m + off, self.chips)
        return self.copy(
            self.half(self.stripe, n),
            self.half(self.full.at[self.c, self.tap], n),
            (off, n),
            (2 * to + self.c, self.z),
        )

    def arrival(self, k, off, n):
        whole = self.half(self.full.at[self.c, k], n)
        return self.copy(whole, whole, (off, n), (2 * k * self.every + self.c, self.z))

    def pair(self, c, n):
        part = self.full.at[c, pl.ds(2 * n, 2)]
        return self.copy(part, part, (self.chips, n), (2 * self.m + 1 - self.c, self.z))

    def chips_start(self):
        @pl.when(self.owner)
        def _():
            self.own_stripe().start()
            for off in range(1, self.chips):
                for n in range(self.PARTS):
                    self.chip(off, n).start()

    def pair_start(self):
        for k in range(4):
            off = lax.rem(self.m - k * self.every + self.chips, self.chips)

            @pl.when(off != 0)
            def _():
                for n in range(self.PARTS):
                    self.arrival(k, off, n).wait_recv()

        @pl.when(self.owner)
        def _():
            self.own_stripe().wait()
            for off in range(1, self.chips):
                for n in range(self.PARTS):
                    self.chip(off, n).wait_send()

        for n in range(self.PARTS):
            self.pair(self.c, n).start()

    def pair_finish(self):
        for n in range(self.PARTS):
            self.pair(self.c, n).wait_send()
            self.pair(1 - self.c, n).wait_recv()


def first_step():
    return pl.program_id(0) == 0


def last_step():
    return pl.program_id(0) == pl.num_programs(0) - 1


def head_kernel(plan, nm, lens, x, xtop, xend, ctop, cend, g2, s2, pb, g3, s3,
                w_hbm, gain, shift, taps, pw,
                X5, x2, low, high, sums, stats, par, hl_out, hr_out, full, stripe,
                macc, hl, hr, xedge, sel, edge, acc, w_ref, w_sem, part,
                line_sems, gather_sems, xhalo_sems, halo_sems, *links):
    t = pl.program_id(0)
    peers, plane, line = group_peers(plan), plane_peers(plan), line_peers(plan)
    xhalo = Halo(plan, xedge, hl, hr, xhalo_sems, 1)
    halo = Halo(plan, edge, low, high, halo_sems, plan.steps)
    gather = Gather(plan, gather_sems, line_sems, part, stripe, full)
    w_copy = pltpu.make_async_copy(w_hbm, w_ref, w_sem)
    plane_link, line_link, link = links[:4], links[4:8], links[8:]
    s, z, i, h = plan.place()
    L, Lp, C, nw, nz, wb = plan.L, plan.Lp, plan.C, plan.nw, plan.nz, plan.wb
    share = plan.NW // nz
    c = t - nm

    @pl.when(first_step())
    def _():
        w_copy.start()
        peers.greet(gather.others())
        part[...] = jnp.where(gather.tap == 3, pw[...], taps[0])
        macc[...] = jnp.zeros_like(macc)
        acc[...] = jnp.zeros_like(acc)
        n16 = nw * 16
        for side, (xe, ce, places) in enumerate(
            ((xtop, ctop, (0, 1, 0)), (xend, cend, (14, 15, 15)))
        ):
            for k, at in enumerate(places):
                rows, lanes = rows_of((nw, n16)), lanes_of((nw, n16))
                one = jnp.where(lanes == 16 * rows + at, 1.0, 0.0).astype(BF16)
                block = (xe if k < 2 else ce)[...].reshape(n16, C)
                xedge[side, k] = mm(one, block)
        shape = (Lp, L)
        for k in range(plan.T1):
            at = lanes_of(shape) - (2 * rows_of(shape) + (k - 2))
            sel[k * Lp : (k + 1) * Lp] = jnp.where((at == 0) | (at == 1), 1.0, 0.0).astype(BF16)

    @pl.when(c < 0)
    def _():
        rows = rows_of((L, C))
        for w in range(min(share, wb)):
            at = lax.rem(z * share, wb) + w
            valid = 2 * lens[z * share + t * wb + w] - s * L
            v = jnp.where(rows < valid, x[at].astype(F32), 0.0)
            macc[0] += fold(v)
            macc[1] += fold(v * v)

    @pl.when(c == -1)
    def _():
        packet, more = plane_link[0], line_link[0]
        packet[0:1] = unfold(macc[0])
        packet[1:2] = unfold(macc[1])
        meet(peers.count - 1 + len(gather.others()))
        plane.start(plane_link)
        xhalo.start(0)
        at = 0
        spans = []
        more[2:3] = jnp.zeros((1, C), F32)
        for ref in (g2, s2, pb, g3, s3):
            n = ref.shape[1]
            more[2:3, at : at + n] = ref[...]
            spans.append((at, n))
            at += n
        more[0:2] = plane.finish(plane_link)
        line.start(line_link)
        gather.line_start()
        stats[...] = line.finish(line_link)[0:2]
        par[...] = jnp.zeros_like(par)
        for k in range(nz):
            row = line_link[1][k]
            for r, (at, n) in enumerate(spans):
                par[r : r + 1, k * n : (k + 1) * n] = row[2:3, at : at + n]
        par[5:6] = flat(gain)
        par[6:7] = flat(shift)
        xhalo.finish()
        hl_out[...] = hl[...]
        hr_out[...] = hr[...]
        w_copy.wait()

    @pl.when(c >= 0)
    def _():
        mean, rho = norm_of(stats[...], 2.0 * total_of(lens))
        scale = flat(gain) * rho
        offset = flat(shift) - mean * scale
        rows = rows_of((L, C))
        row1 = rows_of((1, C))
        row16 = rows_of((16, C))
        def activate(w):
            at = c * wb + w
            valid = 2 * lens[i * nw + at] - s * L
            a = gelu(x[w].astype(F32) * scale + offset)
            a = jnp.where(rows < valid, a, 0.0).astype(BF16)
            picked = mm(sel[...], a)
            for k in range(5):
                X5[w * Lp : (w + 1) * Lp, k * C : (k + 1) * C] = picked[
                    k * Lp : (k + 1) * Lp
                ].astype(BF16)

            def beside(ref, k, bin_at):
                a = gelu(ref[k, pl.ds(at, 1), :] * scale + offset)
                here = (row1 + bin_at < valid) & (row1 + (s * L + bin_at) >= 0)
                return jnp.where(here, a, 0.0).astype(BF16).astype(F32)

            l0, l1 = beside(hl, 0, -2), beside(hl, 1, -1)
            r0, r1 = beside(hr, 0, L), beside(hr, 1, L + 1)
            top, end = w * Lp, (w + 1) * Lp
            for k, add in ((0, l0 + l1), (1, l1)):
                X5[top : top + 16, k * C : (k + 1) * C] = (
                    picked[k * Lp : k * Lp + 16] + jnp.where(row16 == 0, add, 0.0)
                ).astype(BF16)
            for k, add in ((3, r0), (4, r0 + r1)):
                X5[end - 16 : end, k * C : (k + 1) * C] = (
                    picked[(k + 1) * Lp - 16 : (k + 1) * Lp] + jnp.where(row16 == 15, add, 0.0)
                ).astype(BF16)

        nc = 256
        rowp = rows_of((Lp, nc))

        def convolve(first, count):
            span = slice(first * Lp, (first + count) * Lp)
            for n in range(C // nc):
                cols = slice(n * nc, (n + 1) * nc)
                y = 0.5 * mm(X5[span], w_ref[:, cols])
                s0 = jnp.zeros((8, nc), F32)
                s1 = jnp.zeros((8, nc), F32)
                for w in range(first, first + count):
                    at = c * wb + w
                    valid = lens[i * nw + at] - s * Lp
                    v = y[(w - first) * Lp : (w - first + 1) * Lp]
                    x2[w, :, cols] = v
                    edge[0, at, :, cols] = v[:EDGE].astype(BF16)
                    edge[1, at, :, cols] = v[Lp - EDGE :].astype(BF16)
                    v = jnp.where(rowp < valid, v, 0.0)
                    s0 = s0 + fold(v)
                    s1 = s1 + fold(v * v)
                acc[0:1, cols] += unfold(s0)
                acc[1:2, cols] += unfold(s1)

        count = max(1, wb // 2)
        for first in range(0, wb, count):
            for w in range(first, first + count):
                activate(w)
            convolve(first, count)
        halo.start(c)

    @pl.when(c == 0)
    def _():
        gather.line_finish()
        gather.chips_start()

    @pl.when(last_step())
    def _():
        link[0][...] = acc[...]
        peers.start(link)
        gather.pair_start()
        sums[...] = peers.finish(link)
        halo.finish()
        gather.pair_finish()


def dilated_kernel(plan, lens, x2, lo, hi, w_ref, stats, par,
                   Y3, c2, low, high, sums, ext, wf, edge, acc, halo_sems, *link):
    t = pl.program_id(0)
    peers = group_peers(plan)
    halo = Halo(plan, edge, low, high, halo_sems, plan.steps)
    s, z, i, h = plan.place()
    Lp, C, H, wb = plan.Lp, plan.C, plan.H, plan.wb

    @pl.when(first_step())
    def _():
        peers.greet()
        acc[...] = jnp.zeros_like(acc)
        for k in range(plan.T2):
            for c in range(2):
                at = k * C + c * (C // 2)
                wf[:, at : at + C // 2] = w_ref[c, k]

    mean, rho = norm_of(stats[...], total_of(lens))
    scale = par[0:1] * rho
    offset = par[1:2] - mean * scale
    rows = rows_of((Lp, C))
    rowe = rows_of((EDGE, C))

    rowh = rows_of((Lp, H))
    sums0, sums1 = jnp.zeros((8, H), F32), jnp.zeros((8, H), F32)
    nh = min(2, wb)
    for first in range(0, wb, wb // nh):
        span = range(first, first + wb // nh)
        for w in span:
            valid = lens[i * plan.nw + t * wb + w] - s * Lp
            a = jnp.where(rows < valid, gelu(x2[w] * scale + offset), 0.0)
            al = gelu(lo[w].astype(F32) * scale + offset)
            al = jnp.where((rowe - EDGE < valid) & (s > 0), al, 0.0)
            ah = gelu(hi[w].astype(F32) * scale + offset)
            ah = jnp.where(rowe + Lp < valid, ah, 0.0)
            ext[w, 0:EDGE] = al
            ext[w, EDGE : EDGE + Lp] = a
            ext[w, EDGE + Lp :] = ah
            top, end = w * Lp, (w + 1) * Lp
            Y3[top:end, 0:C] = ext[w, EDGE - DIL : EDGE - DIL + Lp].astype(BF16)
            Y3[top:end, C : 2 * C] = a.astype(BF16)
            Y3[top:end, 2 * C : 3 * C] = ext[w, EDGE + DIL : EDGE + DIL + Lp].astype(BF16)
        y = mm_nt(Y3[first * Lp : (first + wb // nh) * Lp], wf[...])
        for w in span:
            at = t * wb + w
            valid = lens[i * plan.nw + at] - s * Lp
            v = y[(w - first) * Lp : (w - first + 1) * Lp]
            c2[w] = v
            edge[0, at] = v[:EDGE].astype(BF16)
            edge[1, at] = v[Lp - EDGE :].astype(BF16)
            v = jnp.where(rowh < valid, v, 0.0)
            sums0 = sums0 + fold(v)
            sums1 = sums1 + fold(v * v)
    acc[0:1, 0:H] += unfold(sums0)
    acc[1:2, 0:H] += unfold(sums1)

    @pl.when(first_step())
    def _():
        meet(peers.count - 1)

    halo.start(t)

    @pl.when(last_step())
    def _():
        link[0][...] = acc[...]
        peers.start(link)
        sums[...] = peers.finish(link)[:, 0:H]
        halo.finish()


def point_kernel(plan, lens, c2, x2, cot, w_ref, pb, stats, par,
                 res, dz, pgrad, low, high, sums, bsum,
                 pw, a3s, a3T, dos, edge, acc, halo_sems, *link):
    t = pl.program_id(0)
    peers = group_peers(plan)
    halo = Halo(plan, edge, low, high, halo_sems, plan.steps)
    s, z, i, h = plan.place()
    Lp, C, H, wb, cs = plan.Lp, plan.C, plan.H, plan.wb, plan.cs
    M = wb * Lp

    @pl.when(first_step())
    def _():
        peers.greet()
        acc[...] = jnp.zeros_like(acc)
        for c in range(2):
            pw[:, c * (C // 2) : (c + 1) * (C // 2)] = w_ref[c, 0]

    @pl.when(t < plan.steps)
    def _():
        mean, rho = norm_of(stats[...], total_of(lens))
        scale = par[3:4, 0:H] * rho
        offset = par[4:5, 0:H] - mean * scale
        shift = -mean * rho
        rowc = rows_of((Lp, C))
        rowh = rows_of((Lp, H))
        block = pl.ds(pl.multiple_of(t * M, 128), M)
        bias = jnp.zeros((8, C), F32)
        parts = []
        for w in range(wb):
            valid = lens[i * plan.nw + t * wb + w] - s * Lp
            d = jnp.where(rowc < valid, cot[w].astype(F32), 0.0)
            bias = bias + fold(d)
            parts.append(d.astype(BF16))
        d = jnp.concatenate(parts, axis=0)
        dos[block] = d
        da = mm_nt(d, pw[...])
        s0, s1 = jnp.zeros((8, H), F32), jnp.zeros((8, H), F32)
        parts = []
        for w in range(wb):
            at = t * wb + w
            valid = lens[i * plan.nw + at] - s * Lp
            top, end = w * Lp, (w + 1) * Lp
            v = c2[w]
            act, slope = gelu_both(v * scale + offset)
            parts.append(jnp.where(rowh < valid, act, 0.0).astype(BF16))
            dzw = da[top:end] * slope
            dz[w] = dzw
            edge[0, at] = dzw[:EDGE].astype(BF16)
            edge[1, at] = dzw[Lp - EDGE :].astype(BF16)
            s0 = s0 + fold(dzw)
            s1 = s1 + fold(dzw * (v * rho + shift))
        a3 = jnp.concatenate(parts, axis=0)
        a3s[block] = a3
        a3T[:, block] = a3.T
        acc[0:1, 0:H] += unfold(s0)
        acc[0:1, H : 2 * H] += unfold(s1)
        acc[1:2] += unfold(bias)

    @pl.when(first_step())
    def _():
        meet(peers.count - 1)

    @pl.when(t < plan.steps)
    def _():
        halo.start(t)

    @pl.when(t == plan.steps - 1)
    def _():
        link[0][...] = acc[...]
        peers.start(link)

    @pl.when(t >= plan.steps)
    def _():
        u = t - plan.steps
        n = plan.nw // 2
        y = mm(a3s[pl.ds(pl.multiple_of(u * n * Lp, 128), n * Lp)], w_ref[h, 0])
        rowr = rows_of((Lp, y.shape[1]))
        for w in range(n):
            valid = lens[i * plan.nw + u * n + w] - s * Lp
            r = x2[w] + y[w * Lp : (w + 1) * Lp] + pb[2:3]
            r = jnp.where(rowr < valid, r, 0.0).astype(BF16).T
            for k in range(plan.g):
                res[k, w] = r[k * cs : (k + 1) * cs]

    @pl.when(last_step())
    def _():
        rows = pl.ds(pl.multiple_of(h * plan.Hh, 16), plan.Hh)
        pgrad[...] = mm(a3T[rows], dos[...]).astype(BF16)
        got = peers.finish(link)
        sums[0:1] = got[0:1, 0:H]
        sums[1:2] = got[0:1, H : 2 * H]
        bsum[...] = got[1:2]
        halo.finish()


def dilated_back_kernel(plan, lens, c2, clo, chi, dz3, zlo, zhi, x2, Y3, w_ref,
                        stats3, sums3, stats2, par, res,
                        dz2, grads, low, high, sums, res_got,
                        ext, Z3, wt, dcT, edge, acc, bulk_sems, halo_sems, *link):
    t = pl.program_id(0)
    peers = group_peers(plan)
    halo = Halo(plan, edge, low, high, halo_sems, 1)
    s, z, i, h = plan.place()
    Lp, C, H, wb, nw, g = plan.Lp, plan.C, plan.H, plan.wb, plan.nw, plan.g

    def bulk(off, n):
        to = lax.rem(i + off, g)
        rows = pl.ds(n * wb, wb)
        return pltpu.make_async_remote_copy(
            src_ref=res.at[to, rows],
            dst_ref=res_got.at[off, rows],
            send_sem=bulk_sems.at[0, off, n],
            recv_sem=bulk_sems.at[1, off, n],
            device_id=(s, h * g + to),
            device_id_type=MESH,
        )

    parts = [(off, n) for off in range(1, g) for n in range(plan.res_parts)]

    @pl.when(first_step())
    def _():
        peers.greet()
        acc[...] = jnp.zeros_like(acc)
        for k in range(plan.T2):
            for c in range(2):
                cols = slice(c * (C // 2), (c + 1) * (C // 2))
                wt[k * H : (k + 1) * H, cols] = w_ref[c, k]

        meet(peers.count - 1)
        for part in parts:
            bulk(*part).start()

    @pl.when(t < plan.steps)
    def _():
        total = total_of(lens)
        mean3, rho3 = norm_of(stats3[...], total)
        gr3 = par[3:4, 0:H] * rho3
        sg3 = sums3[0:1] / total
        gg3 = sums3[1:2] / total
        mean2, rho2 = norm_of(stats2[...], total)
        scale2 = par[0:1] * rho2
        offset2 = par[1:2] - mean2 * scale2
        rowh = rows_of((Lp, H))
        rowe = rows_of((EDGE, H))
        rowc = rows_of((Lp, C))

        by_v = -gr3 * rho3 * gg3
        by_1 = gr3 * (mean3 * rho3 * gg3 - sg3)
        shift2 = -mean2 * rho2

        def back(dz, v):
            return gr3 * dz + by_v * v + by_1

        for w in range(wb):
            valid = lens[i * nw + t * wb + w] - s * Lp
            d = jnp.where(rowh < valid, back(dz3[w], c2[w]), 0.0)
            dl = back(zlo[w].astype(F32), clo[w].astype(F32))
            dl = jnp.where((rowe - EDGE < valid) & (s > 0), dl, 0.0)
            dh = back(zhi[w].astype(F32), chi[w].astype(F32))
            dh = jnp.where(rowe + Lp < valid, dh, 0.0)
            ext[w, 0:EDGE] = dl
            ext[w, EDGE : EDGE + Lp] = d
            ext[w, EDGE + Lp :] = dh
            top, end = w * Lp, (w + 1) * Lp
            Z3[top:end, 0:H] = ext[w, EDGE + DIL : EDGE + DIL + Lp].astype(BF16)
            Z3[top:end, H : 2 * H] = d.astype(BF16)
            Z3[top:end, 2 * H : 3 * H] = ext[w, EDGE - DIL : EDGE - DIL + Lp].astype(BF16)

        y = mm(Z3[...], wt[...])

        M = wb * Lp
        dcT[:, pl.ds(pl.multiple_of(t * M, 128), M)] = Z3[:, H : 2 * H].T
        s0, s1 = jnp.zeros((8, C), F32), jnp.zeros((8, C), F32)
        for w in range(wb):
            at = t * wb + w
            valid = lens[i * nw + at] - s * Lp
            v = x2[w]
            dzw = y[w * Lp : (w + 1) * Lp] * gelu_slope(v * scale2 + offset2)
            dzw = jnp.where(rowc < valid, dzw, 0.0)
            dz2[w] = dzw
            edge[0, pl.ds(at, 1)] = dzw[0:1]
            edge[1, pl.ds(at, 1)] = dzw[Lp - 1 : Lp]
            s0 = s0 + fold(dzw)
            s1 = s1 + fold(dzw * (v * rho2 + shift2))
        acc[0:1] += unfold(s0)
        acc[1:2] += unfold(s1)

    @pl.when(t == plan.steps - 1)
    def _():
        link[0][...] = acc[...]
        peers.start(link)
        halo.start(0)

    @pl.when(t >= plan.steps)
    def _():
        rows = pl.ds(pl.multiple_of(h * plan.Hh, 16), plan.Hh)
        grads[...] = mm(dcT[rows], Y3[...]).astype(BF16)

    @pl.when(last_step())
    def _():
        sums[...] = peers.finish(link)
        halo.finish()
        for part in parts:
            bulk(*part).wait()


class Reduction:
    SEMS = 3

    def __init__(self, plan, out, give, mine, got, spread, half, mate, sems):
        self.plan, self.out = plan, out
        self.give, self.mine, self.got, self.spread = give, mine, got, spread
        self.half, self.mate = half, mate
        self.sems = sems
        self.s, self.z, self.i, self.h = plan.place()
        self.c = lax.rem(self.s, 2)
        self.m = lax.div(self.s, 2)
        self.chips = plan.chips

    @staticmethod
    def scratch(plan):
        taps, wide = plan.T1 + 2, plan.C // 2
        full = (taps, plan.chips, plan.g, plan.rb, wide)
        part = (taps, plan.g, plan.rb, wide)
        return [
            pltpu.VMEM((taps, 2, plan.chips, plan.rb, wide), BF16),
            *[pltpu.VMEM(full, BF16)] * 4,
            *[pltpu.VMEM(part, BF16)] * 2,
            pltpu.SemaphoreType.DMA((2, taps, Reduction.SEMS + 2 * plan.chips + plan.g)),
        ]

    def copy(self, src, dst, tap, sem, device):
        return pltpu.make_async_remote_copy(
            src_ref=src,
            dst_ref=dst,
            send_sem=self.sems.at[0, tap, sem],
            recv_sem=self.sems.at[1, tap, sem],
            device_id=device,
            device_id_type=MESH,
        )

    def pair(self):
        return (2 * self.m + (1 - self.c), self.z)

    def chip(self, off):
        return lax.rem(self.m + off, self.chips)

    def phase0(self, k):
        return self.copy(self.give.at[k], self.got.at[k], k, 0, self.pair())

    def phase1(self, k, off, at):
        to = self.chip(off)
        dst = self.spread.at[k, at]
        return self.copy(self.mine.at[k, to], dst, k, 1 + off, (2 * to + self.c, self.z))

    def phase2(self, k, off):
        to = lax.rem(self.i + off, self.plan.g)
        device = (self.s, self.h * self.plan.g + to)
        return self.copy(
            self.half.at[k, to], self.mate.at[k, off], k, 1 + self.chips + off, device
        )

    def phase3(self, k, off, at):
        to = self.chip(off)
        sem = 1 + self.chips + self.plan.g + off
        src, dst = self.out.at[k, self.c, self.m], self.out.at[k, self.c, at]
        return self.copy(src, dst, k, sem, (2 * to + self.c, self.z))

    def phase4(self, k, c):
        return self.copy(self.out.at[k, c], self.out.at[k, c], k, 1, self.pair())

    def put(self, k, rows):
        wide = self.plan.C // 2
        for j in range(self.plan.g):
            for m in range(self.chips):
                v = rows(j, m)
                left, right = v[:, :wide], v[:, wide:]
                self.mine[k, m, j] = jnp.where(self.c == 0, left, right).astype(BF16)
                self.give[k, m, j] = jnp.where(self.c == 0, right, left).astype(BF16)
        self.phase0(k).start()

    def step1(self, k):
        self.phase0(k).wait()
        self.mine[k] = (self.mine[k].astype(F32) + self.got[k].astype(F32)).astype(BF16)
        for off in range(1, self.chips):
            self.phase1(k, off, self.m).start()

    def step2(self, k):
        for off in range(1, self.chips):
            self.phase1(k, off, self.m).wait_send()
            self.phase1(k, off, self.chip(self.chips - off)).wait_recv()
        self.spread[k, self.m] = self.mine[k, self.m]
        v = self.spread[k, 0].astype(F32)
        for n in range(1, self.chips):
            v = v + self.spread[k, n].astype(F32)
        self.half[k] = v.astype(BF16)
        for off in range(1, self.plan.g):
            self.phase2(k, off).start()

    def step3(self, k):
        for off in range(1, self.plan.g):
            self.phase2(k, off).wait()
        v = self.half[k, self.i].astype(F32)
        for off in range(1, self.plan.g):
            v = v + self.mate[k, off].astype(F32)
        self.out[k, self.c, self.m] = v.astype(BF16)
        for off in range(1, self.chips):
            self.phase3(k, off, self.m).start()

    def step4(self, k):
        for off in range(1, self.chips):
            self.phase3(k, off, self.m).wait_send()
            self.phase3(k, off, self.chip(self.chips - off)).wait_recv()
        self.phase4(k, self.c).start()

    def step5(self, k):
        self.phase4(k, self.c).wait_send()
        self.phase4(k, 1 - self.c).wait_recv()

    def stages(self):
        return [self.step1, self.step2, self.step3, self.step4]


def tail_turns(plan):
    nD, T1 = plan.steps, plan.T1
    turns = [("x", 0)] + [("d", n) for n in range(1, nD)]
    xs, ws = [("x", n) for n in range(1, nD)], [("w", n) for n in range(T1)]
    while xs or ws:
        turns += ws[:1] + xs[:1]
        xs, ws = xs[1:], ws[1:]
    return turns


def tail_kernel(plan, lens, dz2, zlo, zhi, x2, lo, hi, cot, hl, hr, x, X5_hbm, taps, grads, pgrad,
                stats2, sums2, par, stats1, par1, res,
                gz, gz_got, sums, summed, res_got,
                ext, D3, D0T, wcat, pick, eye, cols, y, part, split, acc, X5, X5_sems, bulk_sems, res_sems, *rest):
    t = pl.program_id(0)
    s, z, i, h = plan.place()
    L, Lp, C, wb, g, nw = plan.L, plan.Lp, plan.C, plan.wb, plan.g, plan.nw
    Ch, cs, T1 = plan.Ch, plan.cs, plan.T1
    M = wb * Lp
    nD = plan.steps
    turns = tail_turns(plan)
    last = len(turns) - 1
    peers = group_peers(plan)
    red = Reduction(plan, *rest[:8])
    link = rest[8:]

    def bulk(step, off, n):
        to = lax.rem(i + off, g)
        n2 = wb // 2
        return pltpu.make_async_remote_copy(
            src_ref=part.at[step, off - 1, pl.ds(n * n2, n2)],
            dst_ref=gz_got.at[off, pl.ds(step * wb + n * n2, n2)],
            send_sem=bulk_sems.at[0, step, off, n],
            recv_sem=bulk_sems.at[1, step, off, n],
            device_id=(s, h * g + to),
            device_id_type=MESH,
        )

    def res_copy(off, n):
        to = lax.rem(i + off, g)
        return pltpu.make_async_remote_copy(
            src_ref=res.at[to, pl.ds(n * wb, wb)],
            dst_ref=res_got.at[off],
            send_sem=res_sems.at[0, off, n],
            recv_sem=res_sems.at[1, off, n],
            device_id=(s, h * g + to),
            device_id_type=MESH,
        )

    res_parts = [(off, n) for off in range(1, g) for n in range(plan.res_parts, nD)]

    def X5_copy(k):
        cols = pl.ds(pl.multiple_of(k * C, 128), C)
        return pltpu.make_async_copy(X5_hbm.at[:, cols], X5.at[k % 2], X5_sems.at[k % 2])

    others = [(off, n) for off in range(1, g) for n in range(2)]

    def send(step, n):
        for off in range(1, g):
            bulk(step, off, n).start()

    def when(at):
        return pl.when(t == min(at, last))

    def turn_of(kind):
        steps = [(n, k) for n, (what, k) in enumerate(turns) if what == kind]
        index = jnp.int32(0)
        here = False
        for n, k in steps:
            index = jnp.where(t == n, k, index)
            here = (t == n) | here
        return here, index

    @when(0)
    def _():
        peers.greet()
        acc[...] = jnp.zeros_like(acc)
        pick[...] = pick_matrix(L)
        eye[...] = eye_matrix(Ch, Ch, 0)
        mean, rho = norm_of(stats1[...], 2.0 * total_of(lens))
        scale = par1[5:6] * rho
        for k, row in enumerate((scale, par1[6:7] - mean * scale, rho, -mean * rho)):
            cols[k] = column(row, L)
        for first in range(0, Ch, 64):
            rows = slice(first, min(first + 64, Ch))
            for r, parts in enumerate((((0,), (1, 2), (3, 4)), ((0, 1), (2, 3), (4,)))):
                for k, which in enumerate(parts):
                    v = taps[which[0], rows]
                    if len(which) > 1:
                        v = (v.astype(F32) + taps[which[1], rows].astype(F32)).astype(BF16)
                    at = r * Ch
                    wcat[at + rows.start : at + rows.stop, k * C : (k + 1) * C] = v
        meet(peers.count - 1)
        for part_n in res_parts:
            res_copy(*part_n).start()

    @pl.when(t < nD)
    def _():
        total = total_of(lens)
        mean, rho = norm_of(stats2[...], total)
        gr = par[0:1] * rho
        sg = sums2[0:1] / total
        gg = sums2[1:2] / total
        rowc = rows_of((Lp, C))
        row1 = rows_of((1, C))

        by_dz = 0.5 * gr
        by_v = -0.5 * gr * rho * gg
        by_1 = 0.5 * gr * (mean * rho * gg - sg)

        def back(dout, dz, v):
            return 0.5 * dout + by_dz * dz + by_v * v + by_1

        def grad_of(w):
            at = t * wb + w
            valid = lens[i * nw + at] - s * Lp
            d = back(cot[w].astype(F32), dz2[w], x2[w])
            d = jnp.where(rowc < valid, d, 0.0)
            one = pl.ds(at, 1)
            dl = back(hl[2, one, :], zlo[one, :], lo[w, EDGE - 1 : EDGE].astype(F32))
            dl = jnp.where((row1 - 1 < valid) & (s > 0), dl, 0.0)
            dh = back(hr[2, one, :], zhi[one, :], hi[w, 0:1].astype(F32))
            dh = jnp.where(row1 + Lp < valid, dh, 0.0)
            ext[w, 7:8] = dl
            ext[w, 8 : 8 + Lp] = d
            ext[w, 8 + Lp : 9 + Lp] = dh
            top, end = w * Lp, (w + 1) * Lp
            D3[t, top:end, 0:C] = ext[w, 9 : 9 + Lp].astype(BF16)
            D3[t, top:end, C : 2 * C] = d.astype(BF16)
            D3[t, top:end, 2 * C : 3 * C] = ext[w, 7 : 7 + Lp].astype(BF16)

        for w in range(wb):
            grad_of(w)
        half = D3[t, :, pl.ds(pl.multiple_of(C + h * Ch, 128), Ch)]
        D0T[:, pl.ds(pl.multiple_of(t * M, 128), M)] = half.T

    here_x, bx = turn_of("x")

    @pl.when(here_x)
    def _():
        lanes = lanes_of((Ch, L))

        def through(w):
            valid = 2 * lens[i * nw + bx * wb + w] - s * L
            top, end = w * Lp, (w + 1) * Lp
            v = mm_nt(eye[...], x[w])
            da = jnp.concatenate([y[0:Ch, top:end], y[Ch:, top:end]], axis=1)
            da = mm(da.astype(BF16), pick[...])
            dzw = da * gelu_slope(v * cols[0] + cols[1])
            dzw = jnp.where(lanes < valid, dzw, 0.0)
            acc[0] += dzw
            acc[1] += dzw * (v * cols[2] + cols[3])
            split[w % 2] = dzw.astype(BF16)
            for off in range(g):
                rows = pl.ds(pl.multiple_of(lax.rem(i + off, g) * cs, 16), cs)
                if off == 0:
                    gz[w] = split[w % 2, rows]
                else:
                    part[bx, off - 1, w] = split[w % 2, rows]

        nh = 2 if wb % 2 == 0 and wb * Lp // 2 % 128 == 0 else 1
        n = wb // nh
        for hf in range(nh):
            rows = slice(hf * n * Lp, (hf + 1) * n * Lp)
            y[:, rows] = mm_nt(wcat[...], D3[bx, rows])
            for w in range(hf * n, (hf + 1) * n):
                through(w)
        send(bx, 0)

    @pl.when(here_x & (bx < nD - 1))
    def _():
        send(bx, 1)

    @when(0)
    def _():
        hs = plan.H // plan.nz
        rb = plan.rb
        for u in range(2):

            def rows(j, m, u=u):
                side, r = m * rb // hs, m * rb % hs
                n = 2 * side + u
                rows = slice(j * hs + r, j * hs + r + rb)
                v = grads[rows, n * C : (n + 1) * C] if n < plan.T2 else pgrad[rows]
                return v.astype(F32)

            red.put(T1 + u, rows)

    @when(nD - 1)
    def _():
        X5_copy(0).start()

    stages = red.stages()
    for n, at in enumerate((1, 2, nD + 2, nD + 5)):

        @when(at)
        def _():
            for u in range(2):
                stages[n](T1 + u)

    @when([n for n, turn in enumerate(turns) if turn == ("x", nD - 1)][0])
    def _():
        packet = link[0]
        packet[...] = jnp.zeros_like(packet)
        packet[0:1, 0:Ch] = jnp.sum(acc[0].T, axis=0, keepdims=True)
        packet[1:2, 0:Ch] = jnp.sum(acc[1].T, axis=0, keepdims=True)
        peers.start(link)

    here_w, k = turn_of("w")

    @pl.when(here_w)
    def _():
        @pl.when(k < T1 - 1)
        def _():
            X5_copy(k + 1).start()

        X5_copy(k).wait()
        y[0:Ch, 0:C] = mm(D0T[...], X5[lax.rem(k, 2)])
        rb = plan.rb
        red.put(k, lambda j, m: y[j * cs + m * rb : j * cs + (m + 1) * rb, 0:C])
        for n, stage in enumerate(stages[:2]):
            pl.when(k > n)(partial(stage, k - 1 - n))

    @when(last)
    def _():
        for n, stage in enumerate(stages[:2]):
            for k in range(T1 - 1 - n, T1):
                stage(k)
        send(nD - 1, 1)
        for stage in stages[2:]:
            for k in range(T1):
                stage(k)
        sums[...] = peers.finish(link)[:, 0:Ch]
        for k in range(T1 + 2):
            red.step5(k)
        own = pltpu.make_async_copy(red.out, summed, X5_sems.at[0])
        own.start()
        for step in range(nD):
            for other in others:
                bulk(step, *other).wait()
        own.wait()
        for part_n in res_parts:
            res_copy(*part_n).wait()


def input_grad_kernel(plan, lens, x, gz, gz_got, stats, sums, par1, res, res_got, res_more, summed,
                      sums2, sums3, bsum,
                      out, out_result, conv_grad, dil_grad, point_grad,
                      g1, b1, g2, b2, g3, b3, pb, eye, cols, xt):
    t = pl.program_id(0)
    s, z, i, h = plan.place()
    L, Ch, cs, wb = plan.L, plan.Ch, plan.cs, plan.wb
    mine = pl.ds(pl.multiple_of(i * cs, 16), cs)

    @pl.when(first_step())
    def _():
        n = 2.0 * total_of(lens)
        mean, rho = norm_of(stats[...], n)
        gr = par1[5:6] * rho
        gg = sums[1:2] / n * rho
        for k, row in enumerate((gr, -gr * gg, gr * (mean * gg - sums[0:1] / n))):
            xt[...] = column(row, L)
            cols[k] = xt[mine]
        eye[...] = eye_matrix(cs, Ch, i * cs)

        def mine_of(src, at, which, count, *dsts):
            n = dsts[0].shape[1]
            for k in range(count):

                @pl.when(which == k)
                def _():
                    for dst, r in zip(dsts, at):
                        dst[...] = src[r : r + 1, k * n : (k + 1) * n]

        mine_of(sums, (1, 0), i, plan.g, g1, b1)
        mine_of(sums2, (1, 0), z, plan.nz, g2, b2)
        mine_of(sums3, (1, 0), z, plan.nz, g3, b3)
        mine_of(bsum, (0,), z, plan.nz, pb)

    own = lax.div(t, plan.steps) == i
    early = lax.rem(t, plan.steps) < plan.res_parts
    for w in range(wb):
        got = jnp.where(early, res_got[0, w].astype(F32), res_more[0, w].astype(F32))
        out_result[w] = jnp.where(own, res[0, w].astype(F32), got).astype(BF16)

    C, T1, hs, rb, wide = plan.C, plan.T1, plan.H // plan.nz, plan.rb, plan.C // 2
    count = plan.NW // wb
    turns = min(count, plan.chips)
    per, every = plan.chips // turns, count // turns

    def spread(turn):
        for n in range(per):
            m = turn * per + n
            side, r = m * rb // hs, m * rb % hs
            for c in range(2):
                at = slice(c * wide, (c + 1) * wide)
                for k in range(T1):
                    conv_grad[k, n * rb : (n + 1) * rb, at] = summed[k, c, n].astype(F32)
                for u in range(2):
                    v = summed[T1 + u, c, n].astype(F32)
                    if 2 * side + u < plan.T2:
                        dil_grad[2 * side + u, r : r + rb, at] = v
                    else:
                        point_grad[r : r + rb, at] = v

    for turn in range(turns):
        pl.when(t == turn * every)(partial(spread, turn))

    lanes = lanes_of((cs, L))
    for w in range(wb):
        valid = 2 * lens[t * wb + w] - s * L
        v = mm_nt(eye[...], x[w])
        dz = jnp.where(own, gz[w].astype(F32), gz_got[0, w].astype(F32))
        r = cols[0] * dz + v * cols[1] + cols[2]
        out[w] = jnp.where(lanes < valid, r, 0.0).astype(BF16)


def call(kernel, plan, name, steps, ins, outs, scratch, flops, nbytes, cid=None):
    extra = {} if cid is None else dict(collective_id=cid, has_side_effects=True)
    return pl.pallas_call(
        partial(kernel, plan),
        grid=(steps,),
        in_specs=[SMEM] + [spec for spec, _ in ins],
        out_specs=[spec for spec, _, _ in outs],
        out_shape=[jax.ShapeDtypeStruct(shape, dtype) for _, shape, dtype in outs],
        scratch_shapes=scratch,
        compiler_params=pltpu.CompilerParams(vmem_limit_bytes=VMEM_LIMIT, **extra),
        cost_estimate=pl.CostEstimate(
            flops=int(flops), bytes_accessed=int(nbytes), transcendentals=0
        ),
        name=name,
    )


def per_device(
    inputs,
    lengths,
    input_gain,
    input_shift,
    conv_weight,
    branch_gain,
    branch_shift,
    dilated_tap_weight,
    mixer_gain,
    mixer_shift,
    point_weight,
    point_bias,
    cotangent,
):
    NW, L, C = inputs.shape
    Lp = L // 2
    nz = lax.axis_size("ch")
    R = 2
    plan = Plan(
        ns=lax.axis_size("seq"),
        nz=nz,
        R=R,
        NW=NW,
        L=L,
        C=C,
        H=mixer_gain.shape[0] * nz,
        T1=conv_weight.shape[0],
        T2=dilated_tap_weight.shape[0],
        wb=min(NW * R // nz, max(1, 512 // Lp)),
    )
    g, nw, cs, Ch, H, Hh, wb = plan.g, plan.nw, plan.cs, plan.Ch, plan.H, plan.Hh, plan.wb
    T1, T2, steps = plan.T1, plan.T2, plan.steps
    M = wb * Lp
    hs = H // nz
    lens = lengths.astype(jnp.int32)

    def row(a):
        return a.reshape(1, a.shape[0])

    def grp():
        return lax.rem(lax.axis_index("ch"), g)

    def half():
        return lax.div(lax.axis_index("ch"), g)

    def core():
        return lax.rem(lax.axis_index("seq"), 2)

    def chip4():
        return lax.div(lax.axis_index("seq"), plan.ns // 4)

    def whole(*shape):
        return pl.BlockSpec(shape, lambda t: (0,) * len(shape), pipeline_mode=pl.Buffered(1))

    def const(*shape):
        return pl.BlockSpec(shape, lambda t: (0,) * len(shape))

    def win(*shape):
        return pl.BlockSpec(shape, lambda t: (t,) + (0,) * (len(shape) - 1))

    def arg_win(n, width):
        return pl.BlockSpec((wb, n, width), lambda t: (grp() * steps + t, 0, 0))

    def ins(*pairs):
        return [p for p in pairs]

    share = NW // nz
    nm = max(1, share // wb)

    def edge_spec(n):
        return pl.BlockSpec(
            (nw, 16, C), lambda t: (grp(), n, 0), pipeline_mode=pl.Buffered(1)
        )

    def head_block(t):
        own = lax.div(lax.axis_index("ch") * share, wb) + t
        return jnp.where(t < nm, own, grp() * steps + t - nm), 0, 0

    def after(*shape):
        return pl.BlockSpec(
            shape, lambda t: (jnp.maximum(t - nm, 0),) + (0,) * (len(shape) - 1)
        )

    pairs = ins(
        (pl.BlockSpec((wb, L, C), head_block), inputs),
        (edge_spec(0), inputs),
        (edge_spec(L // 16 - 1), inputs),
        (edge_spec(0), cotangent),
        (edge_spec(Lp // 16 - 1), cotangent),
        (whole(1, cs), row(branch_gain)),
        (whole(1, cs), row(branch_shift)),
        (whole(1, cs), row(point_bias)),
        (whole(1, H // nz), row(mixer_gain)),
        (whole(1, H // nz), row(mixer_shift)),
        (ANY, conv_weight.reshape(T1 * C, C)),
        (whole(C), input_gain),
        (whole(C), input_shift),
        (
            pl.BlockSpec(
                (1, hs, C // 2),
                lambda t: (jnp.minimum(chip4(), T2 - 1), 0, core()),
                pipeline_mode=pl.Buffered(1),
            ),
            jnp.swapaxes(dilated_tap_weight, 1, 2),
        ),
        (
            pl.BlockSpec(
                (hs, C // 2), lambda t: (0, core()), pipeline_mode=pl.Buffered(1)
            ),
            point_weight,
        ),
    )
    plane, line, group = plane_peers(plan), line_peers(plan), group_peers(plan)
    X5, x2, lo2, hi2, stats2, stats1, par, hl, hr, full, _ = call(
        lambda plan, *refs: head_kernel(plan, nm, *refs),
        plan,
        "head",
        nm + steps,
        pairs,
        [
            (after(M, T1 * C), (nw * Lp, T1 * C), BF16),
            (after(wb, Lp, C), (nw, Lp, C), F32),
            (ANY, (nw, EDGE, C), BF16),
            (ANY, (nw, EDGE, C), BF16),
            (const(2, C), (2, C), F32),
            (const(2, C), (2, C), F32),
            (const(8, C), (8, C), F32),
            (const(3, nw, C), (3, nw, C), F32),
            (const(3, nw, C), (3, nw, C), F32),
            (ANY, (2, T2 + 1, nz, hs, C // 2), BF16),
            (ANY, (nz, hs, C // 2), BF16),
        ],
        [
            pltpu.VMEM((2, 8, C), F32),
            pltpu.VMEM((3, nw, C), F32),
            pltpu.VMEM((3, nw, C), F32),
            pltpu.VMEM((2, 3, nw, C), F32),
            pltpu.VMEM((T1 * Lp, L), BF16),
            pltpu.VMEM((2, nw, EDGE, C), BF16),
            pltpu.VMEM((2, C), F32),
            pltpu.VMEM((T1 * C, C), BF16),
            pltpu.SemaphoreType.DMA,
            pltpu.VMEM((hs, C // 2), BF16),
            pltpu.SemaphoreType.DMA((2, nz)),
            pltpu.SemaphoreType.DMA((2, plan.ns // 2 + 1, Gather.PARTS)),
        ]
        + halo_scratch(1)
        + halo_scratch(steps)
        + plane.scratch(2, C)
        + line.scratch(3, C)
        + group.scratch(2, C),
        2 * nw * Lp * T1 * C * C,
        nw * Lp * C * 20,
        cid=1,
    )(lens, *[a for _, a in pairs])

    full = full.reshape(2, T2 + 1, H, C // 2)
    taps_spec = whole(2, T2, H, C // 2)
    pw_spec = pl.BlockSpec(
        (2, 1, H, C // 2), lambda t: (0, T2, 0, 0), pipeline_mode=pl.Buffered(1)
    )

    pairs = ins(
        (win(wb, Lp, C), x2),
        (win(wb, EDGE, C), lo2),
        (win(wb, EDGE, C), hi2),
        (taps_spec, full),
        (whole(2, C), stats2),
        (whole(8, C), par),
    )
    Y3, c2, lo3, hi3, stats3 = call(
        dilated_kernel,
        plan,
        "dilated",
        steps,
        pairs,
        [
            (win(M, T2 * C), (nw * Lp, T2 * C), BF16),
            (win(wb, Lp, H), (nw, Lp, H), F32),
            (ANY, (nw, EDGE, H), BF16),
            (ANY, (nw, EDGE, H), BF16),
            (const(2, H), (2, H), F32),
        ],
        [
            pltpu.VMEM((wb, Lp + 2 * EDGE, C), F32),
            pltpu.VMEM((H, T2 * C), BF16),
            pltpu.VMEM((2, nw, EDGE, H), BF16),
            pltpu.VMEM((2, C), F32),
        ]
        + halo_scratch(steps)
        + group.scratch(2, C),
        2 * nw * Lp * T2 * C * H,
        nw * Lp * C * 12,
        cid=3,
    )(lens, *[a for _, a in pairs])

    def early(*shape):
        return pl.BlockSpec(
            shape, lambda t: (jnp.minimum(t, steps - 1),) + (0,) * (len(shape) - 1)
        )

    def late(t):
        return jnp.maximum(t - steps, 0)

    pairs = ins(
        (early(wb, Lp, H), c2),
        (pl.BlockSpec((nw // 2, Lp, Ch), lambda t: (late(t), 0, half())), x2),
        (
            pl.BlockSpec(
                (wb, Lp, C), lambda t: (grp() * steps + jnp.minimum(t, steps - 1), 0, 0)
            ),
            cotangent,
        ),
        (pw_spec, full),
        (pl.BlockSpec((8, Ch), lambda t: (0, half()), pipeline_mode=pl.Buffered(1)), par),
        (whole(2, H), stats3),
        (whole(8, C), par),
    )
    res, dz3, pgrad, zlo3, zhi3, sums3, bsum = call(
        point_kernel,
        plan,
        "point",
        steps + 2,
        pairs,
        [
            (
                pl.BlockSpec((g, nw // 2, cs, Lp), lambda t: (0, late(t), 0, 0)),
                (g, nw, cs, Lp),
                BF16,
            ),
            (early(wb, Lp, H), (nw, Lp, H), F32),
            (const(Hh, C), (Hh, C), BF16),
            (ANY, (nw, EDGE, H), BF16),
            (ANY, (nw, EDGE, H), BF16),
            (const(2, H), (2, H), F32),
            (const(1, C), (1, C), F32),
        ],
        [
            pltpu.VMEM((H, C), BF16),
            pltpu.VMEM((nw * Lp, H), BF16),
            pltpu.VMEM((H, nw * Lp), BF16),
            pltpu.VMEM((nw * Lp, C), BF16),
            pltpu.VMEM((2, nw, EDGE, H), BF16),
            pltpu.VMEM((2, C), F32),
        ]
        + halo_scratch(steps)
        + group.scratch(2, C),
        5 * nw * Lp * C * H,
        nw * Lp * C * 10,
        cid=4,
    )(lens, *[a for _, a in pairs])

    pairs = ins(
        (early(wb, Lp, H), c2),
        (early(wb, EDGE, H), lo3),
        (early(wb, EDGE, H), hi3),
        (early(wb, Lp, H), dz3),
        (early(wb, EDGE, H), zlo3),
        (early(wb, EDGE, H), zhi3),
        (early(wb, Lp, C), x2),
        (pl.BlockSpec((nw * Lp, C), lambda t: (0, late(t))), Y3),
        (taps_spec, full),
        (whole(2, H), stats3),
        (whole(2, H), sums3),
        (whole(2, C), stats2),
        (whole(8, C), par),
        (ANY, res),
    )
    dz2, grads, zlo2, zhi2, sums2, res_got = call(
        dilated_back_kernel,
        plan,
        "dilated_back",
        steps + T2,
        pairs,
        [
            (early(wb, Lp, C), (nw, Lp, C), F32),
            (pl.BlockSpec((Hh, C), lambda t: (0, late(t))), (Hh, T2 * C), BF16),
            (ANY, (nw, C), F32),
            (ANY, (nw, C), F32),
            (const(2, C), (2, C), F32),
            (ANY, (g, nw, cs, Lp), BF16),
        ],
        [
            pltpu.VMEM((wb, Lp + 2 * EDGE, H), F32),
            pltpu.VMEM((M, T2 * H), BF16),
            pltpu.VMEM((T2 * H, C), BF16),
            pltpu.VMEM((H, nw * Lp), BF16),
            pltpu.VMEM((2, nw, C), F32),
            pltpu.VMEM((2, C), F32),
            pltpu.SemaphoreType.DMA((2, g, steps)),
        ]
        + halo_scratch(1)
        + group.scratch(2, C),
        4 * nw * Lp * T2 * C * H,
        nw * Lp * C * 20,
        cid=5,
    )(lens, *[a for _, a in pairs])

    def half_of(n):
        return pl.BlockSpec((n, Ch), lambda t: (0, half()), pipeline_mode=pl.Buffered(1))

    chips, rb = plan.chips, plan.rb
    turns_t = tail_turns(plan)

    def x_block(t):
        block = jnp.int32(0)
        for n, (what, k) in enumerate(turns_t):
            if what == "x":
                block = jnp.where(t >= n, k, block)
        return block

    sshape = (T1 + 2, 2, chips, rb, C // 2)
    pairs = ins(
        (early(wb, Lp, C), dz2),
        (whole(nw, C), zlo2),
        (whole(nw, C), zhi2),
        (early(wb, Lp, C), x2),
        (early(wb, EDGE, C), lo2),
        (early(wb, EDGE, C), hi2),
        (
            pl.BlockSpec(
                (wb, Lp, C), lambda t: (grp() * steps + jnp.minimum(t, steps - 1), 0, 0)
            ),
            cotangent,
        ),
        (whole(3, nw, C), hl),
        (whole(3, nw, C), hr),
        (
            pl.BlockSpec(
                (wb, L, Ch), lambda t: (grp() * steps + x_block(t), 0, half())
            ),
            inputs,
        ),
        (ANY, X5),
        (
            pl.BlockSpec(
                (T1, Ch, C), lambda t: (0, half(), 0), pipeline_mode=pl.Buffered(1)
            ),
            conv_weight,
        ),
        (whole(Hh, T2 * C), grads),
        (whole(Hh, C), pgrad),
        (whole(2, C), stats2),
        (whole(2, C), sums2),
        (whole(8, C), par),
        (half_of(2), stats1),
        (half_of(8), par),
        (ANY, res),
    )
    gz, gz_got, sums1, summed, res_more = call(
        tail_kernel,
        plan,
        "tail",
        len(turns_t),
        pairs,
        [
            (
                pl.BlockSpec((wb, cs, L), lambda t: (x_block(t), 0, 0)),
                (nw, cs, L),
                BF16,
            ),
            (ANY, (g, nw, cs, L), BF16),
            (const(2, Ch), (2, Ch), F32),
            (ANY, sshape, BF16),
            (ANY, (g, wb, cs, Lp), BF16),
        ],
        [
            pltpu.VMEM((wb, Lp + 16, C), F32),
            pltpu.VMEM((steps, M, 3 * C), BF16),
            pltpu.VMEM((Ch, nw * Lp), BF16),
            pltpu.VMEM((2 * Ch, 3 * C), BF16),
            pltpu.VMEM((L, L), BF16),
            pltpu.VMEM((Ch, Ch), BF16),
            pltpu.VMEM((4, Ch, L), F32),
            pltpu.VMEM((2 * Ch, max(M, C)), F32),
            pltpu.VMEM((steps, g - 1, wb, cs, L), BF16),
            pltpu.VMEM((2, Ch, L), BF16),
            pltpu.VMEM((2, Ch, L), F32),
            pltpu.VMEM((2, nw * Lp, C), BF16),
            pltpu.SemaphoreType.DMA((2,)),
            pltpu.SemaphoreType.DMA((2, steps, g, 2)),
            pltpu.SemaphoreType.DMA((2, g, steps)),
        ]
        + Reduction.scratch(plan)
        + group.scratch(2, C),
        2 * nw * Lp * (6 + T1) * C * Ch,
        nw * Lp * C * 40,
        cid=6,
    )(lens, *[a for _, a in pairs])

    count = NW // wb
    turns = min(count, chips)

    def own_block(t):
        return jnp.where(lax.div(t, steps) == grp(), lax.rem(t, steps), 0)

    def got_slot(t):
        off = lax.rem(grp() - lax.div(t, steps) + g, g)
        return jnp.maximum(off, 1), jnp.where(off > 0, lax.rem(t, steps), 0)

    pairs = ins(
        (pl.BlockSpec((wb, L, Ch), lambda t: (t, 0, half())), inputs),
        (pl.BlockSpec((wb, cs, L), lambda t: (own_block(t), 0, 0)), gz),
        (pl.BlockSpec((1, wb, cs, L), lambda t: got_slot(t) + (0, 0)), gz_got),
        (half_of(2), stats1),
        (whole(2, Ch), sums1),
        (half_of(8), par),
        (pl.BlockSpec((1, wb, cs, Lp), lambda t: (grp(), own_block(t), 0, 0)), res),
        (pl.BlockSpec((1, wb, cs, Lp), lambda t: got_slot(t) + (0, 0)), res_got),
        (pl.BlockSpec((1, wb, cs, Lp), lambda t: (got_slot(t)[0], 0, 0, 0)), res_more),
        (
            pl.BlockSpec(
                (T1 + 2, 2, chips // turns, rb, C // 2),
                lambda t: (0, 0, t * turns // count, 0, 0),
            ),
            summed,
        ),
        (whole(2, C), sums2),
        (whole(2, H), sums3),
        (whole(1, C), bsum),
    )
    outs = call(
        input_grad_kernel,
        plan,
        "input_grad",
        NW // wb,
        pairs,
        [
            (win(wb, cs, L), (NW, cs, L), BF16),
            (win(wb, cs, Lp), (NW, cs, Lp), BF16),
            (
                pl.BlockSpec((T1, cs // turns, C), lambda t: (0, t * turns // count, 0)),
                (T1, cs, C),
                F32,
            ),
            (const(T2, hs, C), (T2, hs, C), F32),
            (const(hs, C), (hs, C), F32),
        ]
        + [(const(1, n), (1, n), F32) for n in (cs, cs, cs, cs, hs, hs, cs)],
        [
            pltpu.VMEM((cs, Ch), BF16),
            pltpu.VMEM((3, cs, L), F32),
            pltpu.VMEM((Ch, L), F32),
        ],
        2 * NW * L * Ch * cs,
        NW * L * cs * 8,
    )(lens, *[a for _, a in pairs])
    grad, result, conv_grad, dil_grad, point_grad = outs[:5]
    g1, b1, g2, b2, g3, b3, pb = [a[0] for a in outs[5:]]
    return (
        jnp.swapaxes(result, 1, 2),
        jnp.swapaxes(grad, 1, 2),
        jnp.swapaxes(conv_grad, 1, 2),
        g1,
        b1,
        g2,
        b2,
        jnp.swapaxes(dil_grad, 1, 2),
        g3,
        b3,
        point_grad,
        pb,
    )


def solution(mesh):
    in_specs = (
        P(None, "seq", None),
        P(),
        P(),
        P(),
        P(),
        P("ch"),
        P("ch"),
        P(None, None, "ch"),
        P("ch"),
        P("ch"),
        P("ch", None),
        P("ch"),
        P(None, "seq", None),
    )
    out_specs = (
        P(None, "seq", "ch"),
        P(None, "seq", "ch"),
        P(None, None, "ch"),
        P("ch"),
        P("ch"),
        P("ch"),
        P("ch"),
        P(None, None, "ch"),
        P("ch"),
        P("ch"),
        P("ch", None),
        P("ch"),
    )
    return jax.shard_map(
        per_device, mesh=mesh, in_specs=in_specs, out_specs=out_specs, check_vma=False
    )
```

```python
from functools import partial
from typing import NamedTuple

import jax
import jax.numpy as jnp
from jax import lax
from jax.experimental import pallas as pl
from jax.experimental.pallas import tpu as pltpu
from jax.sharding import PartitionSpec as P

DIL = 14
EDGE = 16
EPS = 1e-05
GC0 = 0.7978845608028654
GC1 = 0.044715
F32 = jnp.float32
BF16 = jnp.bfloat16
MESH = pl.DeviceIdType.MESH
VMEM_LIMIT = 58 * 1024 * 1024
ANY = pl.BlockSpec(memory_space=pl.ANY)
SMEM = pl.BlockSpec(memory_space=pltpu.SMEM)


ST1, GAIN2, SHIFT2, BIAS, GAIN3, SHIFT3, GAIN1, SHIFT1, ST2, ST3, SU3, BSUM, SU2 = (
    0, 2, 3, 4, 5, 6, 7, 8, 9, 11, 13, 15, 16
)
STATE = 24


class Plan(NamedTuple):
    ns: int
    nz: int
    R: int
    NW: int
    L: int
    C: int
    H: int
    T1: int
    T2: int
    wb: int

    @property
    def g(self):
        return self.nz // self.R

    @property
    def nw(self):
        return self.NW // self.g

    @property
    def Lp(self):
        return self.L // 2

    @property
    def cs(self):
        return self.C // self.nz

    @property
    def Ch(self):
        return self.C // self.R

    @property
    def Hh(self):
        return self.H // self.R

    @property
    def steps(self):
        return self.nw // self.wb

    @property
    def res_parts(self):
        return max(1, self.steps - 1)

    @property
    def chips(self):
        return self.ns // 2

    @property
    def cut(self):
        return self.res_parts * self.wb

    @property
    def rb(self):
        return self.cs // self.chips

    def place(self):
        s, z = lax.axis_index("seq"), lax.axis_index("ch")
        return s, z, lax.rem(z, self.g), lax.div(z, self.g)


def gelu(z):
    t = jnp.tanh(z * (GC0 + (GC0 * GC1) * (z * z)))
    return z * (0.5 + 0.5 * t)


def gelu_both(z):
    sq = z * z
    t = jnp.tanh(z * (GC0 + (GC0 * GC1) * sq))
    h = 0.5 + 0.5 * t
    v = z * h
    return v, h + v * (1.0 - t) * (GC0 + (3.0 * GC0 * GC1) * sq)


def gelu_slope(z):
    return gelu_both(z)[1]


def fold(v):
    return jnp.sum(v.reshape(v.shape[0] // 8, 8, v.shape[1]), axis=0)


def unfold(v):
    return jnp.sum(v, axis=0, keepdims=True)


def rows_of(shape):
    return lax.broadcasted_iota(jnp.int32, shape, 0)


def lanes_of(shape):
    return lax.broadcasted_iota(jnp.int32, shape, 1)


def total_of(lens):
    n = lens[0]
    for k in range(1, lens.shape[0]):
        n = n + lens[k]
    return n.astype(F32)


def norm_of(stats, total):
    mean = stats[0:1] / total
    square = stats[1:2] / total
    return mean, lax.rsqrt(square - mean * mean + EPS)


def flat(ref):
    return ref[...].reshape(1, ref.shape[0])


def column(row, n):
    return jnp.broadcast_to(row, (n, row.shape[1])).T


def mm(a, b):
    return jnp.dot(a, b, preferred_element_type=F32)


def mm_nt(a, b):
    return lax.dot_general(a, b, (((1,), (1,)), ((), ())), preferred_element_type=F32)


def mm_tn(a, b):
    return lax.dot_general(a, b, (((0,), (0,)), ((), ())), preferred_element_type=F32)


def mm_tt(a, b):
    return lax.dot_general(a, b, (((0,), (1,)), ((), ())), preferred_element_type=F32)


def eye_matrix(n, m, first):
    return jnp.where(lanes_of((n, m)) == rows_of((n, m)) + first, 1.0, 0.0).astype(BF16)


def pick_matrix(L):
    r, n = rows_of((L, L)), lanes_of((L, L))
    bin_of = 2 * r - jnp.where(r >= L // 2, L - 1, 0)
    return jnp.where(n == bin_of, 1.0, 0.0).astype(BF16)


def remote(src, dst, send, recv, device):
    return pltpu.make_async_remote_copy(
        src_ref=src,
        dst_ref=dst,
        send_sem=send,
        recv_sem=recv,
        device_id=device,
        device_id_type=MESH,
    )


def wrap(v, n):
    return jnp.where(v >= n, v - n, v)


def greet(devices):
    barrier = pltpu.get_barrier_semaphore()
    for device in devices:
        pl.semaphore_signal(barrier, inc=1, device_id=device, device_id_type=MESH)


def meet(devices):
    pl.semaphore_wait(pltpu.get_barrier_semaphore(), len(devices))


class Peers:
    def __init__(self, me, others):
        self.me, self.others = me, others
        self.count = len(others) + 1

    def start(self, link):
        packet, buf, sems = link
        for device in self.others:
            remote(packet, buf.at[self.me], sems.at[0], sems.at[1], device).start()

    def finish(self, link):
        packet, buf, sems = link
        buf[self.me] = packet[...]
        rest = buf.at[pl.ds(0, self.count - 1)]
        done = remote(rest, rest, sems.at[0], sems.at[1], self.others[0])
        done.wait_recv()
        acc = buf[0]
        for q in range(1, self.count):
            acc = acc + buf[q]
        done.wait_send()
        return acc

    def scratch(self, rows, width):
        return [
            pltpu.VMEM((rows, width), F32),
            pltpu.VMEM((self.count, rows, width), F32),
            pltpu.SemaphoreType.DMA((2,)),
        ]


def group_peers(plan):
    s, z, i, h = plan.place()
    g = plan.g
    others = [
        (wrap(s + a, plan.ns), h * g + wrap(i + b, g))
        for a in range(plan.ns)
        for b in range(g)
        if a or b
    ]
    return Peers(s * g + i, others)


def plane_peers(plan):
    s, z, i, h = plan.place()
    return Peers(s, [(wrap(s + a, plan.ns), z) for a in range(1, plan.ns)])


def line_peers(plan):
    s, z, i, h = plan.place()
    return Peers(z, [(s, wrap(z + a, plan.nz)) for a in range(1, plan.nz)])


class Halo:
    def __init__(self, plan, edge, land, sems):
        self.edge, self.land, self.sems = edge, land, sems
        s, z, _, _ = plan.place()
        self.to = ((wrap(s + plan.ns - 1, plan.ns), z), (wrap(s + 1, plan.ns), z))

    def copy(self, side, rows):
        return remote(
            self.edge.at[side, rows],
            self.land.at[1 - side, rows],
            self.sems.at[0, side],
            self.sems.at[1, side],
            self.to[side],
        )

    def start(self, first, count):
        for side in range(2):
            self.copy(side, pl.ds(first, count)).start()

    def finish(self):
        for side in range(2):
            done = self.copy(side, pl.ds(0, self.land.shape[1]))
            done.wait_recv()
            done.wait_send()


HALO_SEMS = pltpu.SemaphoreType.DMA((2, 2))


class Gather:
    def __init__(self, plan, part, full, sems):
        self.plan, self.part, self.full, self.sems = plan, part, full, sems
        self.s, self.z, self.i, self.h = plan.place()
        self.c, self.m = lax.rem(self.s, 2), lax.div(self.s, 2)
        self.chips = plan.chips
        self.every = self.chips // 4
        self.tap = lax.div(self.m, self.every)
        self.owner = lax.rem(self.m, self.every) == 0
        self.mine = full.at[self.c, self.tap]

    def others(self):
        g, nz = self.plan.g, self.plan.nz
        return [(self.s, wrap(self.h * g + g + r, nz)) for r in range(nz - g)]

    def far(self, off):
        return (2 * wrap(self.m + off, self.chips) + self.c, self.z)

    def own(self):
        return pltpu.make_async_copy(self.part, self.mine.at[self.z], self.sems.at[0, 0])

    def line(self, off):
        device = (self.s, wrap(self.z + off, self.plan.nz))
        return remote(
            self.part, self.mine.at[self.z], self.sems.at[0, 1], self.sems.at[1, 1], device
        )

    def chip(self, off):
        return remote(self.mine, self.mine, self.sems.at[0, 2], self.sems.at[1, 2], self.far(off))

    def pair(self):
        half = self.full.at[self.c]
        device = (2 * self.m + 1 - self.c, self.z)
        return remote(half, half, self.sems.at[0, 3], self.sems.at[1, 3], device)

    def line_start(self):
        @pl.when(self.owner)
        def _():
            self.own().start()
            for off in range(1, self.plan.nz):
                self.line(off).start()

    def line_finish(self):
        @pl.when(self.owner)
        def _():
            self.own().wait()
            rest = self.mine.at[pl.ds(0, self.plan.nz - 1)]
            device = (self.s, wrap(self.z + 1, self.plan.nz))
            done = remote(rest, rest, self.sems.at[0, 1], self.sems.at[1, 1], device)
            done.wait_recv()
            done.wait_send()

    def chips_start(self):
        @pl.when(self.owner)
        def _():
            for off in range(1, self.chips):
                self.chip(off).start()

    def pair_start(self):
        def taken(count):
            rest = self.full.at[self.c, pl.ds(0, count)]
            return remote(rest, rest, self.sems.at[0, 2], self.sems.at[1, 2], self.far(1))

        @pl.when(self.owner)
        def _():
            taken(3).wait_recv()
            for off in range(1, self.chips):
                self.chip(off).wait_send()

        if self.every > 1:

            @pl.when(jnp.logical_not(self.owner))
            def _():
                taken(4).wait_recv()

        self.pair().start()

    def pair_finish(self):
        done = self.pair()
        done.wait_recv()
        done.wait_send()


def first_step():
    return pl.program_id(0) == 0


def last_step():
    return pl.program_id(0) == pl.num_programs(0) - 1


def keep_state(old, new):
    new[...] = old[...]


def head_kernel(plan, nm, lens, x, xtop, xend, ctop, cend, g2, s2, pb, g3, s3,
                w_hbm, gain, shift, taps, pw,
                X5, x2, land, state, beyond_out, full,
                macc, beyond, xedge, sel, edge, acc, w_ref, w_sem, part,
                gather_sems, xhalo_sems, halo_sems, *links):
    t = pl.program_id(0)
    peers, plane, line = group_peers(plan), plane_peers(plan), line_peers(plan)
    xhalo = Halo(plan, xedge, beyond, xhalo_sems)
    halo = Halo(plan, edge, land, halo_sems)
    gather = Gather(plan, part, full, gather_sems)
    w_copy = pltpu.make_async_copy(w_hbm, w_ref, w_sem)
    plane_link, line_link, link = links[:3], links[3:6], links[6:]
    s, z, i, h = plan.place()
    L, Lp, C, nw, nz, wb = plan.L, plan.Lp, plan.C, plan.nw, plan.nz, plan.wb
    share = plan.NW // nz
    c = t - nm
    everyone = peers.others + gather.others()

    @pl.when(first_step())
    def _():
        w_copy.start()
        greet(everyone)
        part[...] = jnp.where(gather.tap == 3, pw[...], taps[0])
        macc[...] = jnp.zeros_like(macc)
        acc[...] = jnp.zeros_like(acc)
        state[...] = jnp.zeros_like(state)
        state[GAIN1 : GAIN1 + 1] = flat(gain)
        state[SHIFT1 : SHIFT1 + 1] = flat(shift)
        n16 = nw * 16
        for side, (xe, ce, places) in enumerate(
            ((xtop, ctop, (0, 1, 0)), (xend, cend, (14, 15, 15)))
        ):
            for k, at in enumerate(places):
                rows, lanes = rows_of((nw, n16)), lanes_of((nw, n16))
                one = jnp.where(lanes == 16 * rows + at, 1.0, 0.0).astype(BF16)
                block = (xe if k < 2 else ce)[...].reshape(n16, C)
                xedge[side, k] = mm(one, block)
        shape = (Lp, L)
        for k in range(plan.T1):
            at = lanes_of(shape) - (2 * rows_of(shape) + (k - 2))
            sel[k * Lp : (k + 1) * Lp] = jnp.where((at == 0) | (at == 1), 1.0, 0.0).astype(BF16)

    @pl.when(c < 0)
    def _():
        rows = rows_of((L, C))
        for w in range(min(share, wb)):
            at = lax.rem(z * share, wb) + w
            valid = 2 * lens[z * share + t * wb + w] - s * L
            v = jnp.where(rows < valid, x[at].astype(F32), 0.0)
            macc[0] += fold(v)
            macc[1] += fold(v * v)

    @pl.when(c == -1)
    def _():
        packet, more = plane_link[0], line_link[0]
        packet[0:1] = unfold(macc[0])
        packet[1:2] = unfold(macc[1])
        meet(everyone)
        plane.start(plane_link)
        xhalo.start(0, 3)
        at = 0
        spans = []
        more[2:3] = jnp.zeros((1, C), F32)
        for ref in (g2, s2, pb, g3, s3):
            n = ref.shape[1]
            more[2:3, at : at + n] = ref[...]
            spans.append((at, n))
            at += n
        more[0:2] = plane.finish(plane_link)
        line.start(line_link)
        gather.line_start()
        state[ST1 : ST1 + 2] = line.finish(line_link)[0:2]
        for k in range(nz):
            row = line_link[1][k]
            for r, (at, n) in zip((GAIN2, SHIFT2, BIAS, GAIN3, SHIFT3), spans):
                state[r : r + 1, k * n : (k + 1) * n] = row[2:3, at : at + n]
        xhalo.finish()
        beyond_out[...] = beyond[...]
        w_copy.wait()

    @pl.when(c >= 0)
    def _():
        mean, rho = norm_of(state[ST1 : ST1 + 2], 2.0 * total_of(lens))
        scale = state[GAIN1 : GAIN1 + 1] * rho
        offset = state[SHIFT1 : SHIFT1 + 1] - mean * scale
        rows = rows_of((L, C))
        row1 = rows_of((1, C))
        row16 = rows_of((16, C))
        def activate(w):
            at = c * wb + w
            valid = 2 * lens[i * nw + at] - s * L
            a = gelu(x[w].astype(F32) * scale + offset)
            a = jnp.where(rows < valid, a, 0.0).astype(BF16)
            picked = mm(sel[...], a)
            for k in range(5):
                X5[w * Lp : (w + 1) * Lp, k * C : (k + 1) * C] = picked[
                    k * Lp : (k + 1) * Lp
                ].astype(BF16)

            def beside(side, k, bin_at):
                a = gelu(beyond[side, k, pl.ds(at, 1), :] * scale + offset)
                here = (row1 + bin_at < valid) & (row1 + (s * L + bin_at) >= 0)
                return jnp.where(here, a, 0.0).astype(BF16).astype(F32)

            l0, l1 = beside(0, 0, -2), beside(0, 1, -1)
            r0, r1 = beside(1, 0, L), beside(1, 1, L + 1)
            top, end = w * Lp, (w + 1) * Lp
            for k, add in ((0, l0 + l1), (1, l1)):
                X5[top : top + 16, k * C : (k + 1) * C] = (
                    picked[k * Lp : k * Lp + 16] + jnp.where(row16 == 0, add, 0.0)
                ).astype(BF16)
            for k, add in ((3, r0), (4, r0 + r1)):
                X5[end - 16 : end, k * C : (k + 1) * C] = (
                    picked[(k + 1) * Lp - 16 : (k + 1) * Lp] + jnp.where(row16 == 15, add, 0.0)
                ).astype(BF16)

        nc = 256
        rowp = rows_of((Lp, nc))

        def convolve(first, count):
            span = slice(first * Lp, (first + count) * Lp)
            for n in range(C // nc):
                cols = slice(n * nc, (n + 1) * nc)
                y = 0.5 * mm(X5[span], w_ref[:, cols])
                s0 = jnp.zeros((8, nc), F32)
                s1 = jnp.zeros((8, nc), F32)
                for w in range(first, first + count):
                    at = c * wb + w
                    valid = lens[i * nw + at] - s * Lp
                    v = y[(w - first) * Lp : (w - first + 1) * Lp]
                    x2[w, :, cols] = v
                    edge[0, at, :, cols] = v[:EDGE].astype(BF16)
                    edge[1, at, :, cols] = v[Lp - EDGE :].astype(BF16)
                    v = jnp.where(rowp < valid, v, 0.0)
                    s0 = s0 + fold(v)
                    s1 = s1 + fold(v * v)
                acc[0:1, cols] += unfold(s0)
                acc[1:2, cols] += unfold(s1)

        count = max(1, wb // 2)
        for first in range(0, wb, count):
            for w in range(first, first + count):
                activate(w)
            convolve(first, count)
        halo.start(c * wb, wb)

    @pl.when(c == 0)
    def _():
        gather.line_finish()
        gather.chips_start()

    @pl.when(last_step())
    def _():
        link[0][...] = acc[...]
        peers.start(link)
        gather.pair_start()
        state[ST2 : ST2 + 2] = peers.finish(link)
        halo.finish()
        gather.pair_finish()


def dilated_kernel(plan, lens, x2, x2land, w_ref, old,
                   Y3, c2, land, state, ext, wf, edge, acc, halo_sems, *link):
    t = pl.program_id(0)
    peers = group_peers(plan)
    halo = Halo(plan, edge, land, halo_sems)
    s, z, i, h = plan.place()
    Lp, C, H, wb = plan.Lp, plan.C, plan.H, plan.wb

    @pl.when(first_step())
    def _():
        greet(peers.others)
        acc[...] = jnp.zeros_like(acc)
        for k in range(plan.T2):
            for c in range(2):
                at = k * C + c * (C // 2)
                wf[:, at : at + C // 2] = w_ref[c, k]

    mean, rho = norm_of(old[ST2 : ST2 + 2], total_of(lens))
    scale = old[GAIN2 : GAIN2 + 1] * rho
    offset = old[SHIFT2 : SHIFT2 + 1] - mean * scale
    rows = rows_of((Lp, C))
    rowe = rows_of((EDGE, C))

    rowh = rows_of((Lp, H))
    sums0, sums1 = jnp.zeros((8, H), F32), jnp.zeros((8, H), F32)
    nh = min(2, wb)
    for first in range(0, wb, wb // nh):
        span = range(first, first + wb // nh)
        for w in span:
            valid = lens[i * plan.nw + t * wb + w] - s * Lp
            a = jnp.where(rows < valid, gelu(x2[w] * scale + offset), 0.0)
            al = gelu(x2land[0, w].astype(F32) * scale + offset)
            al = jnp.where((rowe - EDGE < valid) & (s > 0), al, 0.0)
            ah = gelu(x2land[1, w].astype(F32) * scale + offset)
            ah = jnp.where(rowe + Lp < valid, ah, 0.0)
            ext[w, 0:EDGE] = al
            ext[w, EDGE : EDGE + Lp] = a
            ext[w, EDGE + Lp :] = ah
            top, end = w * Lp, (w + 1) * Lp
            Y3[top:end, 0:C] = ext[w, EDGE - DIL : EDGE - DIL + Lp].astype(BF16)
            Y3[top:end, C : 2 * C] = a.astype(BF16)
            Y3[top:end, 2 * C : 3 * C] = ext[w, EDGE + DIL : EDGE + DIL + Lp].astype(BF16)
        y = mm_nt(Y3[first * Lp : (first + wb // nh) * Lp], wf[...])
        for w in span:
            at = t * wb + w
            valid = lens[i * plan.nw + at] - s * Lp
            v = y[(w - first) * Lp : (w - first + 1) * Lp]
            c2[w] = v
            edge[0, at] = v[:EDGE].astype(BF16)
            edge[1, at] = v[Lp - EDGE :].astype(BF16)
            v = jnp.where(rowh < valid, v, 0.0)
            sums0 = sums0 + fold(v)
            sums1 = sums1 + fold(v * v)
    acc[0:1, 0:H] += unfold(sums0)
    acc[0:1, H:] += unfold(sums1)

    @pl.when(first_step())
    def _():
        meet(peers.others)

    halo.start(t * wb, wb)

    @pl.when(last_step())
    def _():
        link[0][...] = acc[...]
        peers.start(link)
        keep_state(old, state)
        got = peers.finish(link)
        state[ST3 : ST3 + 1, 0:H] = got[:, 0:H]
        state[ST3 + 1 : ST3 + 2, 0:H] = got[:, H:]
        halo.finish()


def point_kernel(plan, lens, c2, x2, cot, w_ref, old, half_state,
                 res, dz, pgrad, land, state,
                 pw, a3s, a3T, dos, edge, acc, halo_sems, *link):
    t = pl.program_id(0)
    peers = group_peers(plan)
    halo = Halo(plan, edge, land, halo_sems)
    s, z, i, h = plan.place()
    Lp, C, H, wb, cs = plan.Lp, plan.C, plan.H, plan.wb, plan.cs
    M = wb * Lp

    @pl.when(first_step())
    def _():
        greet(peers.others)
        acc[...] = jnp.zeros_like(acc)
        for c in range(2):
            pw[:, c * (C // 2) : (c + 1) * (C // 2)] = w_ref[c, 0]

    @pl.when(t < plan.steps)
    def _():
        mean, rho = norm_of(old[ST3 : ST3 + 2, 0:H], total_of(lens))
        scale = old[GAIN3 : GAIN3 + 1, 0:H] * rho
        offset = old[SHIFT3 : SHIFT3 + 1, 0:H] - mean * scale
        shift = -mean * rho
        rowc = rows_of((Lp, C))
        rowh = rows_of((Lp, H))
        block = pl.ds(pl.multiple_of(t * M, 128), M)
        bias = jnp.zeros((8, C), F32)
        parts = []
        for w in range(wb):
            valid = lens[i * plan.nw + t * wb + w] - s * Lp
            d = jnp.where(rowc < valid, cot[w].astype(F32), 0.0)
            bias = bias + fold(d)
            parts.append(d.astype(BF16))
        d = jnp.concatenate(parts, axis=0)
        dos[block] = d
        da = mm_nt(d, pw[...])
        s0, s1 = jnp.zeros((8, H), F32), jnp.zeros((8, H), F32)
        parts = []
        for w in range(wb):
            at = t * wb + w
            valid = lens[i * plan.nw + at] - s * Lp
            top, end = w * Lp, (w + 1) * Lp
            v = c2[w]
            act, slope = gelu_both(v * scale + offset)
            parts.append(jnp.where(rowh < valid, act, 0.0).astype(BF16))
            dzw = da[top:end] * slope
            dz[w] = dzw
            edge[0, at] = dzw[:EDGE].astype(BF16)
            edge[1, at] = dzw[Lp - EDGE :].astype(BF16)
            s0 = s0 + fold(dzw)
            s1 = s1 + fold(dzw * (v * rho + shift))
        a3 = jnp.concatenate(parts, axis=0)
        a3s[block] = a3
        a3T[:, block] = a3.T
        acc[0:1, 0:H] += unfold(s0)
        acc[0:1, H : 2 * H] += unfold(s1)
        acc[1:2] += unfold(bias)

    @pl.when(first_step())
    def _():
        meet(peers.others)

    @pl.when(t < plan.steps)
    def _():
        halo.start(t * wb, wb)

    @pl.when(t == plan.steps - 1)
    def _():
        link[0][...] = acc[...]
        peers.start(link)

    @pl.when(t >= plan.steps)
    def _():
        u = t - plan.steps
        n = plan.nw // 2
        y = mm(a3s[pl.ds(pl.multiple_of(u * n * Lp, 128), n * Lp)], w_ref[h, 0])
        rowr = rows_of((Lp, y.shape[1]))
        for w in range(n):
            valid = lens[i * plan.nw + u * n + w] - s * Lp
            r = x2[w] + y[w * Lp : (w + 1) * Lp] + half_state[BIAS : BIAS + 1]
            r = jnp.where(rowr < valid, r, 0.0).astype(BF16).T
            for k in range(plan.g):
                res[k, w] = r[k * cs : (k + 1) * cs]

    @pl.when(last_step())
    def _():
        rows = pl.ds(pl.multiple_of(h * plan.Hh, 16), plan.Hh)
        pgrad[...] = mm(a3T[rows], dos[...]).astype(BF16)
        keep_state(old, state)
        got = peers.finish(link)
        state[SU3 : SU3 + 1, 0:H] = got[0:1, 0:H]
        state[SU3 + 1 : SU3 + 2, 0:H] = got[0:1, H : 2 * H]
        state[BSUM : BSUM + 1] = got[1:2]
        halo.finish()


def dilated_back_kernel(plan, lens, c2, cland, dz3, dland, x2, Y3, w_ref, old, res,
                        dz2, grads, land, state, res_got,
                        ext, Z3, wt, dcT, edge, acc, bulk_sems, halo_sems, *link):
    t = pl.program_id(0)
    peers = group_peers(plan)
    halo = Halo(plan, edge, land, halo_sems)
    s, z, i, h = plan.place()
    Lp, C, H, wb, nw, g = plan.Lp, plan.C, plan.H, plan.wb, plan.nw, plan.g

    def bulk(off):
        to = wrap(i + off, g)
        rows = pl.ds(0, plan.cut)
        return remote(
            res.at[to, rows],
            res_got.at[off, rows],
            bulk_sems.at[0, off],
            bulk_sems.at[1, off],
            (s, h * g + to),
        )

    @pl.when(first_step())
    def _():
        greet(peers.others)
        acc[...] = jnp.zeros_like(acc)
        for k in range(plan.T2):
            for c in range(2):
                cols = slice(c * (C // 2), (c + 1) * (C // 2))
                wt[k * H : (k + 1) * H, cols] = w_ref[c, k]
        meet(peers.others)
        for off in range(1, g):
            bulk(off).start()

    @pl.when(t < plan.steps)
    def _():
        total = total_of(lens)
        mean3, rho3 = norm_of(old[ST3 : ST3 + 2, 0:H], total)
        gr3 = old[GAIN3 : GAIN3 + 1, 0:H] * rho3
        sg3 = old[SU3 : SU3 + 1, 0:H] / total
        gg3 = old[SU3 + 1 : SU3 + 2, 0:H] / total
        mean2, rho2 = norm_of(old[ST2 : ST2 + 2], total)
        scale2 = old[GAIN2 : GAIN2 + 1] * rho2
        offset2 = old[SHIFT2 : SHIFT2 + 1] - mean2 * scale2
        rowh = rows_of((Lp, H))
        rowe = rows_of((EDGE, H))
        rowc = rows_of((Lp, C))

        by_v = -gr3 * rho3 * gg3
        by_1 = gr3 * (mean3 * rho3 * gg3 - sg3)
        shift2 = -mean2 * rho2

        def back(dz, v):
            return gr3 * dz + by_v * v + by_1

        for w in range(wb):
            valid = lens[i * nw + t * wb + w] - s * Lp
            d = jnp.where(rowh < valid, back(dz3[w], c2[w]), 0.0)
            dl = back(dland[0, w].astype(F32), cland[0, w].astype(F32))
            dl = jnp.where((rowe - EDGE < valid) & (s > 0), dl, 0.0)
            dh = back(dland[1, w].astype(F32), cland[1, w].astype(F32))
            dh = jnp.where(rowe + Lp < valid, dh, 0.0)
            ext[w, 0:EDGE] = dl
            ext[w, EDGE : EDGE + Lp] = d
            ext[w, EDGE + Lp :] = dh
            top, end = w * Lp, (w + 1) * Lp
            Z3[top:end, 0:H] = ext[w, EDGE + DIL : EDGE + DIL + Lp].astype(BF16)
            Z3[top:end, H : 2 * H] = d.astype(BF16)
            Z3[top:end, 2 * H : 3 * H] = ext[w, EDGE - DIL : EDGE - DIL + Lp].astype(BF16)

        y = mm(Z3[...], wt[...])

        M = wb * Lp
        dcT[:, pl.ds(pl.multiple_of(t * M, 128), M)] = Z3[:, H : 2 * H].T
        s0, s1 = jnp.zeros((8, C), F32), jnp.zeros((8, C), F32)
        for w in range(wb):
            at = t * wb + w
            valid = lens[i * nw + at] - s * Lp
            v = x2[w]
            dzw = y[w * Lp : (w + 1) * Lp] * gelu_slope(v * scale2 + offset2)
            dzw = jnp.where(rowc < valid, dzw, 0.0)
            dz2[w] = dzw
            edge[0, pl.ds(at, 1)] = dzw[0:1]
            edge[1, pl.ds(at, 1)] = dzw[Lp - 1 : Lp]
            s0 = s0 + fold(dzw)
            s1 = s1 + fold(dzw * (v * rho2 + shift2))
        acc[0:1] += unfold(s0)
        acc[1:2] += unfold(s1)

    @pl.when(t == plan.steps - 1)
    def _():
        link[0][...] = acc[...]
        peers.start(link)
        halo.start(0, nw)

    @pl.when(t >= plan.steps)
    def _():
        rows = pl.ds(pl.multiple_of(h * plan.Hh, 16), plan.Hh)
        grads[...] = mm(dcT[rows], Y3[...]).astype(BF16)

    @pl.when(last_step())
    def _():
        keep_state(old, state)
        state[SU2 : SU2 + 2] = peers.finish(link)
        halo.finish()
        for off in range(1, g):
            bulk(off).wait()


class Reduction:
    def __init__(self, plan, batches, out, give, mine, got, spread, half, mate, sems):
        self.plan, self.batches, self.out = plan, batches, out
        self.give, self.mine, self.got, self.spread = give, mine, got, spread
        self.half, self.mate = half, mate
        self.sems = sems
        self.s, self.z, self.i, self.h = plan.place()
        self.c = lax.rem(self.s, 2)
        self.m = lax.div(self.s, 2)
        self.chips = plan.chips

    @staticmethod
    def scratch(plan, batches):
        taps, wide = plan.T1 + 2, plan.C // 2
        full = (taps, plan.chips, plan.g, plan.rb, wide)
        part = (taps, plan.g, plan.rb, wide)
        return [
            pltpu.VMEM((taps, 2, plan.chips, plan.rb, wide), BF16),
            *[pltpu.VMEM(full, BF16)] * 4,
            *[pltpu.VMEM(part, BF16)] * 2,
            pltpu.SemaphoreType.DMA((2, len(batches), 5)),
        ]

    def copy(self, b, phase, src, dst, device):
        return remote(src, dst, self.sems.at[0, b, phase], self.sems.at[1, b, phase], device)

    def finish(self, b, phase, ref, device):
        done = self.copy(b, phase, ref, ref, device)
        done.wait_recv()
        done.wait_send()

    def taps(self, b):
        return pl.ds(*self.batches[b])

    def pair(self):
        return (2 * self.m + (1 - self.c), self.z)

    def far(self, off):
        return (2 * wrap(self.m + off, self.chips) + self.c, self.z)

    def member(self, off):
        return (self.s, self.h * self.plan.g + wrap(self.i + off, self.plan.g))

    def put(self, k, rows):
        wide = self.plan.C // 2
        for j in range(self.plan.g):
            for m in range(self.chips):
                v = rows(j, m)
                left, right = v[:, :wide], v[:, wide:]
                self.mine[k, m, j] = jnp.where(self.c == 0, left, right).astype(BF16)
                self.give[k, m, j] = jnp.where(self.c == 0, right, left).astype(BF16)

    def step0(self, b):
        taps = self.taps(b)
        self.copy(b, 0, self.give.at[taps], self.got.at[taps], self.pair()).start()

    def step1(self, b):
        taps = self.taps(b)
        self.finish(b, 0, self.got.at[taps], self.pair())
        first, count = self.batches[b]
        for k in range(first, first + count):
            v = self.mine[k].astype(F32) + self.got[k].astype(F32)
            self.mine[k] = v.astype(BF16)
        for off in range(1, self.chips):
            src = self.mine.at[taps, wrap(self.m + off, self.chips)]
            self.copy(b, 1, src, self.spread.at[taps, self.m], self.far(off)).start()

    def step2(self, b):
        taps = self.taps(b)
        self.finish(b, 1, self.spread.at[taps, pl.ds(0, self.chips - 1)], self.far(1))
        first, count = self.batches[b]
        for k in range(first, first + count):
            self.spread[k, self.m] = self.mine[k, self.m]
            v = self.spread[k, 0].astype(F32)
            for n in range(1, self.chips):
                v = v + self.spread[k, n].astype(F32)
            self.half[k] = v.astype(BF16)
        for off in range(1, self.plan.g):
            src = self.half.at[taps, wrap(self.i + off, self.plan.g)]
            self.copy(b, 2, src, self.mate.at[taps, off], self.member(off)).start()

    def step3(self, b):
        taps = self.taps(b)
        self.finish(b, 2, self.mate.at[taps, pl.ds(1, self.plan.g - 1)], self.member(1))
        first, count = self.batches[b]
        for k in range(first, first + count):
            v = self.half[k, self.i].astype(F32)
            for off in range(1, self.plan.g):
                v = v + self.mate[k, off].astype(F32)
            self.out[k, self.c, self.m] = v.astype(BF16)
        mine = self.out.at[taps, self.c, self.m]
        for off in range(1, self.chips):
            self.copy(b, 3, mine, mine, self.far(off)).start()

    def step4(self, b):
        taps = self.taps(b)
        self.finish(b, 3, self.out.at[taps, self.c, pl.ds(0, self.chips - 1)], self.far(1))
        mine = self.out.at[taps, self.c]
        self.copy(b, 4, mine, mine, self.pair()).start()

    def step5(self, b):
        self.finish(b, 4, self.out.at[self.taps(b), self.c], self.pair())


def tail_turns(plan):
    nD, T1 = plan.steps, plan.T1
    turns = [("x", 0)] + [("d", n) for n in range(1, nD)]
    xs, ws = [("x", n) for n in range(1, nD)], [("w", n) for n in range(T1)]
    turns += ws[:3]
    ws = ws[3:]
    while xs or ws:
        turns += xs[:1] + ws[:1]
        xs, ws = xs[1:], ws[1:]
    return turns


def tail_batches(plan):
    return [(plan.T1, 2), (0, 3), (3, plan.T1 - 3)]


def tail_kernel(plan, lens, dz2, dzland, x2, x2land, cot, beyond, x, X5_hbm, taps, grads, pgrad,
                old, half_state, res,
                gz, gz_got, sums, summed, res_got,
                ext, D3, D0T, wcat, pick, eye, cols, y, part, split, acc, X5, X5_sems,
                bulk_sems, res_sems, *rest):
    t = pl.program_id(0)
    s, z, i, h = plan.place()
    L, Lp, C, wb, g, nw = plan.L, plan.Lp, plan.C, plan.wb, plan.g, plan.nw
    Ch, cs, T1 = plan.Ch, plan.cs, plan.T1
    M = wb * Lp
    nD = plan.steps
    turns = tail_turns(plan)
    last = len(turns) - 1
    peers = group_peers(plan)
    red = Reduction(plan, tail_batches(plan), *rest[:8])
    link = rest[8:]

    def member(off):
        return (s, h * g + wrap(i + off, g))

    def send(step, n):
        count = wb // 2
        for off in range(1, g):
            rows = pl.ds(step * wb + n * count, count)
            remote(
                part.at[off - 1, rows],
                gz_got.at[off, rows],
                bulk_sems.at[0, off],
                bulk_sems.at[1, off],
                member(off),
            ).start()

    def res_copy(off):
        rows = pl.ds(plan.cut, nw - plan.cut)
        return remote(
            res.at[wrap(i + off, g), rows],
            res_got.at[off],
            res_sems.at[0, off],
            res_sems.at[1, off],
            member(off),
        )

    res_offs = range(1, g) if plan.cut < nw else ()

    def X5_copy(k):
        cols = pl.ds(pl.multiple_of(k * C, 128), C)
        return pltpu.make_async_copy(X5_hbm.at[:, cols], X5.at[k % 2], X5_sems.at[k % 2])

    def when(at):
        return pl.when(t == min(at, last))

    def turn(kind, k):
        return turns.index((kind, k)) if (kind, k) in turns else last

    def turn_of(kind):
        index = jnp.int32(0)
        here = False
        for n, (what, k) in enumerate(turns):
            if what == kind:
                index = jnp.where(t == n, k, index)
                here = (t == n) | here
        return here, index

    @when(0)
    def _():
        greet(peers.others)
        acc[...] = jnp.zeros_like(acc)
        pick[...] = pick_matrix(L)
        eye[...] = eye_matrix(Ch, Ch, 0)
        mean, rho = norm_of(half_state[ST1 : ST1 + 2], 2.0 * total_of(lens))
        scale = half_state[GAIN1 : GAIN1 + 1] * rho
        offset = half_state[SHIFT1 : SHIFT1 + 1] - mean * scale
        for k, row in enumerate((scale, offset, rho, -mean * rho)):
            cols[k] = column(row, L)
        for first in range(0, Ch, 64):
            rows = slice(first, min(first + 64, Ch))
            for r, parts in enumerate((((0,), (1, 2), (3, 4)), ((0, 1), (2, 3), (4,)))):
                for k, which in enumerate(parts):
                    v = taps[which[0], rows]
                    if len(which) > 1:
                        v = (v.astype(F32) + taps[which[1], rows].astype(F32)).astype(BF16)
                    at = r * Ch
                    wcat[at + rows.start : at + rows.stop, k * C : (k + 1) * C] = v
        meet(peers.others)
        for off in res_offs:
            res_copy(off).start()

    @pl.when(t < nD)
    def _():
        total = total_of(lens)
        mean, rho = norm_of(old[ST2 : ST2 + 2], total)
        gr = old[GAIN2 : GAIN2 + 1] * rho
        sg = old[SU2 : SU2 + 1] / total
        gg = old[SU2 + 1 : SU2 + 2] / total
        rowc = rows_of((Lp, C))
        row1 = rows_of((1, C))

        by_dz = 0.5 * gr
        by_v = -0.5 * gr * rho * gg
        by_1 = 0.5 * gr * (mean * rho * gg - sg)

        def back(dout, dz, v):
            return 0.5 * dout + by_dz * dz + by_v * v + by_1

        def grad_of(w):
            at = t * wb + w
            valid = lens[i * nw + at] - s * Lp
            d = back(cot[w].astype(F32), dz2[w], x2[w])
            d = jnp.where(rowc < valid, d, 0.0)
            one = pl.ds(at, 1)
            dl = back(beyond[0, 2, one, :], dzland[0, one, :], x2land[0, w, EDGE - 1 : EDGE].astype(F32))
            dl = jnp.where((row1 - 1 < valid) & (s > 0), dl, 0.0)
            dh = back(beyond[1, 2, one, :], dzland[1, one, :], x2land[1, w, 0:1].astype(F32))
            dh = jnp.where(row1 + Lp < valid, dh, 0.0)
            ext[w, 7:8] = dl
            ext[w, 8 : 8 + Lp] = d
            ext[w, 8 + Lp : 9 + Lp] = dh
            top, end = w * Lp, (w + 1) * Lp
            D3[t, top:end, 0:C] = ext[w, 9 : 9 + Lp].astype(BF16)
            D3[t, top:end, C : 2 * C] = d.astype(BF16)
            D3[t, top:end, 2 * C : 3 * C] = ext[w, 7 : 7 + Lp].astype(BF16)

        for w in range(wb):
            grad_of(w)
        half = D3[t, :, pl.ds(pl.multiple_of(C + h * Ch, 128), Ch)]
        D0T[:, pl.ds(pl.multiple_of(t * M, 128), M)] = half.T

    here_x, bx = turn_of("x")

    @pl.when(here_x)
    def _():
        lanes = lanes_of((Ch, L))

        def through(w):
            valid = 2 * lens[i * nw + bx * wb + w] - s * L
            top, end = w * Lp, (w + 1) * Lp
            v = mm_nt(eye[...], x[w])
            da = jnp.concatenate([y[0:Ch, top:end], y[Ch:, top:end]], axis=1)
            da = mm(da.astype(BF16), pick[...])
            dzw = da * gelu_slope(v * cols[0] + cols[1])
            dzw = jnp.where(lanes < valid, dzw, 0.0)
            acc[0] += dzw
            acc[1] += dzw * (v * cols[2] + cols[3])
            split[w % 2] = dzw.astype(BF16)
            for off in range(g):
                rows = pl.ds(pl.multiple_of(lax.rem(i + off, g) * cs, 16), cs)
                if off == 0:
                    gz[w] = split[w % 2, rows]
                else:
                    part[off - 1, bx * wb + w] = split[w % 2, rows]

        nh = 2 if wb % 2 == 0 and wb * Lp // 2 % 128 == 0 else 1
        n = wb // nh
        for hf in range(nh):
            rows = slice(hf * n * Lp, (hf + 1) * n * Lp)
            y[:, rows] = mm_nt(wcat[...], D3[bx, rows])
            for w in range(hf * n, (hf + 1) * n):
                through(w)
        send(bx, 0)

    @pl.when(here_x & (bx < nD - 1))
    def _():
        send(bx, 1)

    @when(0)
    def _():
        hs = plan.H // plan.nz
        rb = plan.rb
        for u in range(2):

            def rows(j, m, u=u):
                side, r = m * rb // hs, m * rb % hs
                n = 2 * side + u
                rows = slice(j * hs + r, j * hs + r + rb)
                v = grads[rows, n * C : (n + 1) * C] if n < plan.T2 else pgrad[rows]
                return v.astype(F32)

            red.put(T1 + u, rows)
        red.step0(0)

    @when(nD - 1)
    def _():
        X5_copy(0).start()

    here_w, k = turn_of("w")

    @pl.when(here_w)
    def _():
        @pl.when(k < T1 - 1)
        def _():
            X5_copy(k + 1).start()

        X5_copy(k).wait()
        y[0:Ch, 0:C] = mm(D0T[...], X5[lax.rem(k, 2)])
        rb = plan.rb
        red.put(k, lambda j, m: y[j * cs + m * rb : j * cs + (m + 1) * rb, 0:C])

    for at, step, batch in (
        (turn("w", 2), red.step0, 1),
        (turn("w", T1 - 1), red.step0, 2),
        (1, red.step1, 0),
        (turn("w", 1), red.step2, 0),
        (turn("x", 1), red.step1, 1),
        (turn("x", 2), red.step3, 0),
        (turn("x", 2), red.step2, 1),
        (turn("x", 3), red.step4, 0),
    ):

        @when(at)
        def _():
            step(batch)

    @when(turn("x", nD - 1))
    def _():
        packet = link[0]
        packet[...] = jnp.zeros_like(packet)
        packet[0:1, 0:Ch] = jnp.sum(acc[0].T, axis=0, keepdims=True)
        packet[1:2, 0:Ch] = jnp.sum(acc[1].T, axis=0, keepdims=True)
        peers.start(link)

    @when(last)
    def _():
        red.step1(2)
        red.step3(1)
        red.step2(2)
        send(nD - 1, 1)
        red.step4(1)
        red.step3(2)
        sums[...] = peers.finish(link)[:, 0:Ch]
        red.step4(2)
        for b in range(3):
            red.step5(b)
        own = pltpu.make_async_copy(red.out, summed, X5_sems.at[0])
        own.start()
        for off in range(1, g):
            done = remote(
                part.at[off - 1],
                gz_got.at[off],
                bulk_sems.at[0, off],
                bulk_sems.at[1, off],
                member(off),
            )
            done.wait_recv()
            done.wait_send()
        for off in res_offs:
            res_copy(off).wait()
        own.wait()


def input_grad_kernel(plan, lens, x, gz, gz_got, sums, res, res_got, res_more, summed,
                      state, half_state,
                      out, out_result, conv_grad, dil_grad, point_grad,
                      g1, b1, g2, b2, g3, b3, pb, eye, cols, xt):
    t = pl.program_id(0)
    s, z, i, h = plan.place()
    L, Ch, cs, wb = plan.L, plan.Ch, plan.cs, plan.wb
    mine = pl.ds(pl.multiple_of(i * cs, 16), cs)

    @pl.when(first_step())
    def _():
        n = 2.0 * total_of(lens)
        mean, rho = norm_of(half_state[ST1 : ST1 + 2], n)
        gr = half_state[GAIN1 : GAIN1 + 1] * rho
        gg = sums[1:2] / n * rho
        for k, row in enumerate((gr, -gr * gg, gr * (mean * gg - sums[0:1] / n))):
            xt[...] = column(row, L)
            cols[k] = xt[mine]
        eye[...] = eye_matrix(cs, Ch, i * cs)

        def mine_of(src, at, which, count, *dsts):
            n = dsts[0].shape[1]
            for k in range(count):

                @pl.when(which == k)
                def _():
                    for dst, r in zip(dsts, at):
                        dst[...] = src[r : r + 1, k * n : (k + 1) * n]

        mine_of(sums, (1, 0), i, plan.g, g1, b1)
        mine_of(state, (SU2 + 1, SU2), z, plan.nz, g2, b2)
        mine_of(state, (SU3 + 1, SU3), z, plan.nz, g3, b3)
        mine_of(state, (BSUM,), z, plan.nz, pb)

    own = lax.div(t, plan.steps) == i
    early = lax.rem(t, plan.steps) < plan.res_parts
    for w in range(wb):
        got = jnp.where(early, res_got[0, w].astype(F32), res_more[0, w % res_more.shape[1]].astype(F32))
        out_result[w] = jnp.where(own, res[0, w].astype(F32), got).astype(BF16)

    C, T1, hs, rb, wide = plan.C, plan.T1, plan.H // plan.nz, plan.rb, plan.C // 2
    count = plan.NW // wb
    turns = min(count, plan.chips)
    per, every = plan.chips // turns, count // turns

    def spread(turn):
        for n in range(per):
            m = turn * per + n
            side, r = m * rb // hs, m * rb % hs
            for c in range(2):
                at = slice(c * wide, (c + 1) * wide)
                for k in range(T1):
                    conv_grad[k, n * rb : (n + 1) * rb, at] = summed[k, c, n].astype(F32)
                for u in range(2):
                    v = summed[T1 + u, c, n].astype(F32)
                    if 2 * side + u < plan.T2:
                        dil_grad[2 * side + u, r : r + rb, at] = v
                    else:
                        point_grad[r : r + rb, at] = v

    for turn in range(turns):
        pl.when(t == turn * every)(partial(spread, turn))

    lanes = lanes_of((cs, L))
    for w in range(wb):
        valid = 2 * lens[t * wb + w] - s * L
        v = mm_nt(eye[...], x[w])
        dz = jnp.where(own, gz[w].astype(F32), gz_got[0, w].astype(F32))
        r = cols[0] * dz + v * cols[1] + cols[2]
        out[w] = jnp.where(lanes < valid, r, 0.0).astype(BF16)


def call(kernel, plan, name, steps, ins, outs, scratch, flops, nbytes, cid=None):
    extra = {} if cid is None else dict(collective_id=cid, has_side_effects=True)
    return pl.pallas_call(
        partial(kernel, plan),
        grid=(steps,),
        in_specs=[SMEM] + [spec for spec, _ in ins],
        out_specs=[spec for spec, _, _ in outs],
        out_shape=[jax.ShapeDtypeStruct(shape, dtype) for _, shape, dtype in outs],
        scratch_shapes=scratch,
        compiler_params=pltpu.CompilerParams(vmem_limit_bytes=VMEM_LIMIT, **extra),
        cost_estimate=pl.CostEstimate(
            flops=int(flops), bytes_accessed=int(nbytes), transcendentals=0
        ),
        name=name,
    )


def per_device(
    inputs,
    lengths,
    input_gain,
    input_shift,
    conv_weight,
    branch_gain,
    branch_shift,
    dilated_tap_weight,
    mixer_gain,
    mixer_shift,
    point_weight,
    point_bias,
    cotangent,
):
    NW, L, C = inputs.shape
    Lp = L // 2
    nz = lax.axis_size("ch")
    R = 2
    plan = Plan(
        ns=lax.axis_size("seq"),
        nz=nz,
        R=R,
        NW=NW,
        L=L,
        C=C,
        H=mixer_gain.shape[0] * nz,
        T1=conv_weight.shape[0],
        T2=dilated_tap_weight.shape[0],
        wb=min(NW * R // nz, max(1, 512 // Lp)),
    )
    g, nw, cs, Ch, H, Hh, wb = plan.g, plan.nw, plan.cs, plan.Ch, plan.H, plan.Hh, plan.wb
    T1, T2, steps = plan.T1, plan.T2, plan.steps
    M = wb * Lp
    hs = H // nz
    lens = lengths.astype(jnp.int32)

    def row(a):
        return a.reshape(1, a.shape[0])

    def grp():
        return lax.rem(lax.axis_index("ch"), g)

    def half():
        return lax.div(lax.axis_index("ch"), g)

    def core():
        return lax.rem(lax.axis_index("seq"), 2)

    def chip4():
        return lax.div(lax.axis_index("seq"), plan.ns // 4)

    def whole(*shape):
        return pl.BlockSpec(shape, lambda t: (0,) * len(shape), pipeline_mode=pl.Buffered(1))

    def const(*shape):
        return pl.BlockSpec(shape, lambda t: (0,) * len(shape))

    def win(*shape):
        return pl.BlockSpec(shape, lambda t: (t,) + (0,) * (len(shape) - 1))

    def arg_win(n, width):
        return pl.BlockSpec((wb, n, width), lambda t: (grp() * steps + t, 0, 0))

    def ins(*pairs):
        return [p for p in pairs]

    share = NW // nz
    nm = max(1, share // wb)

    def edge_spec(n):
        return pl.BlockSpec(
            (nw, 16, C), lambda t: (grp(), n, 0), pipeline_mode=pl.Buffered(1)
        )

    def head_block(t):
        own = lax.div(lax.axis_index("ch") * share, wb) + t
        return jnp.where(t < nm, own, grp() * steps + t - nm), 0, 0

    def after(*shape):
        return pl.BlockSpec(
            shape, lambda t: (jnp.maximum(t - nm, 0),) + (0,) * (len(shape) - 1)
        )

    pairs = ins(
        (pl.BlockSpec((wb, L, C), head_block), inputs),
        (edge_spec(0), inputs),
        (edge_spec(L // 16 - 1), inputs),
        (edge_spec(0), cotangent),
        (edge_spec(Lp // 16 - 1), cotangent),
        (whole(1, cs), row(branch_gain)),
        (whole(1, cs), row(branch_shift)),
        (whole(1, cs), row(point_bias)),
        (whole(1, H // nz), row(mixer_gain)),
        (whole(1, H // nz), row(mixer_shift)),
        (ANY, conv_weight.reshape(T1 * C, C)),
        (whole(C), input_gain),
        (whole(C), input_shift),
        (
            pl.BlockSpec(
                (1, hs, C // 2),
                lambda t: (jnp.minimum(chip4(), T2 - 1), 0, core()),
                pipeline_mode=pl.Buffered(1),
            ),
            jnp.swapaxes(dilated_tap_weight, 1, 2),
        ),
        (
            pl.BlockSpec(
                (hs, C // 2), lambda t: (0, core()), pipeline_mode=pl.Buffered(1)
            ),
            point_weight,
        ),
    )
    plane, line, group = plane_peers(plan), line_peers(plan), group_peers(plan)
    state_shape = (STATE, C)
    edges2, edges3 = (2, nw, EDGE, C), (2, nw, EDGE, H)
    X5, x2, land2, state, beyond, full = call(
        lambda plan, *refs: head_kernel(plan, nm, *refs),
        plan,
        "head",
        nm + steps,
        pairs,
        [
            (after(M, T1 * C), (nw * Lp, T1 * C), BF16),
            (after(wb, Lp, C), (nw, Lp, C), F32),
            (ANY, edges2, BF16),
            (const(*state_shape), state_shape, F32),
            (const(2, 3, nw, C), (2, 3, nw, C), F32),
            (ANY, (2, T2 + 1, nz, hs, C // 2), BF16),
        ],
        [
            pltpu.VMEM((2, 8, C), F32),
            pltpu.VMEM((2, 3, nw, C), F32),
            pltpu.VMEM((2, 3, nw, C), F32),
            pltpu.VMEM((T1 * Lp, L), BF16),
            pltpu.VMEM(edges2, BF16),
            pltpu.VMEM((2, C), F32),
            pltpu.VMEM((T1 * C, C), BF16),
            pltpu.SemaphoreType.DMA,
            pltpu.VMEM((hs, C // 2), BF16),
            pltpu.SemaphoreType.DMA((2, 4)),
            HALO_SEMS,
            HALO_SEMS,
        ]
        + plane.scratch(2, C)
        + line.scratch(3, C)
        + group.scratch(2, C),
        2 * nw * Lp * T1 * C * C,
        nw * Lp * C * 20,
        cid=1,
    )(lens, *[a for _, a in pairs])

    full = full.reshape(2, T2 + 1, H, C // 2)
    taps_spec = whole(2, T2, H, C // 2)
    pw_spec = pl.BlockSpec(
        (2, 1, H, C // 2), lambda t: (0, T2, 0, 0), pipeline_mode=pl.Buffered(1)
    )

    def early(*shape):
        return pl.BlockSpec(
            shape, lambda t: (jnp.minimum(t, steps - 1),) + (0,) * (len(shape) - 1)
        )

    def early_land(width):
        return pl.BlockSpec(
            (2, wb, EDGE, width), lambda t: (0, jnp.minimum(t, steps - 1), 0, 0)
        )

    def late(t):
        return jnp.maximum(t - steps, 0)

    def half_of(n):
        return pl.BlockSpec((n, Ch), lambda t: (0, half()), pipeline_mode=pl.Buffered(1))

    cot_spec = pl.BlockSpec(
        (wb, Lp, C), lambda t: (grp() * steps + jnp.minimum(t, steps - 1), 0, 0)
    )

    pairs = ins(
        (early(wb, Lp, C), x2),
        (early_land(C), land2),
        (taps_spec, full),
        (whole(*state_shape), state),
    )
    Y3, c2, land3, state = call(
        dilated_kernel,
        plan,
        "dilated",
        steps,
        pairs,
        [
            (win(M, T2 * C), (nw * Lp, T2 * C), BF16),
            (win(wb, Lp, H), (nw, Lp, H), F32),
            (ANY, edges3, BF16),
            (const(*state_shape), state_shape, F32),
        ],
        [
            pltpu.VMEM((wb, Lp + 2 * EDGE, C), F32),
            pltpu.VMEM((H, T2 * C), BF16),
            pltpu.VMEM(edges3, BF16),
            pltpu.VMEM((1, 2 * H), F32),
            HALO_SEMS,
        ]
        + group.scratch(1, 2 * H),
        2 * nw * Lp * T2 * C * H,
        nw * Lp * C * 12,
        cid=3,
    )(lens, *[a for _, a in pairs])

    pairs = ins(
        (early(wb, Lp, H), c2),
        (pl.BlockSpec((nw // 2, Lp, Ch), lambda t: (late(t), 0, half())), x2),
        (cot_spec, cotangent),
        (pw_spec, full),
        (whole(*state_shape), state),
        (half_of(STATE), state),
    )
    res, dz3, pgrad, dland3, state = call(
        point_kernel,
        plan,
        "point",
        steps + 2,
        pairs,
        [
            (
                pl.BlockSpec((g, nw // 2, cs, Lp), lambda t: (0, late(t), 0, 0)),
                (g, nw, cs, Lp),
                BF16,
            ),
            (early(wb, Lp, H), (nw, Lp, H), F32),
            (const(Hh, C), (Hh, C), BF16),
            (ANY, edges3, BF16),
            (const(*state_shape), state_shape, F32),
        ],
        [
            pltpu.VMEM((H, C), BF16),
            pltpu.VMEM((nw * Lp, H), BF16),
            pltpu.VMEM((H, nw * Lp), BF16),
            pltpu.VMEM((nw * Lp, C), BF16),
            pltpu.VMEM(edges3, BF16),
            pltpu.VMEM((2, C), F32),
            HALO_SEMS,
        ]
        + group.scratch(2, C),
        5 * nw * Lp * C * H,
        nw * Lp * C * 10,
        cid=4,
    )(lens, *[a for _, a in pairs])

    pairs = ins(
        (early(wb, Lp, H), c2),
        (early_land(H), land3),
        (early(wb, Lp, H), dz3),
        (early_land(H), dland3),
        (early(wb, Lp, C), x2),
        (pl.BlockSpec((nw * Lp, C), lambda t: (0, late(t))), Y3),
        (taps_spec, full),
        (whole(*state_shape), state),
        (ANY, res),
    )
    dz2, grads, dland2, state, res_got = call(
        dilated_back_kernel,
        plan,
        "dilated_back",
        steps + T2,
        pairs,
        [
            (early(wb, Lp, C), (nw, Lp, C), F32),
            (pl.BlockSpec((Hh, C), lambda t: (0, late(t))), (Hh, T2 * C), BF16),
            (ANY, (2, nw, C), F32),
            (const(*state_shape), state_shape, F32),
            (ANY, (g, nw, cs, Lp), BF16),
        ],
        [
            pltpu.VMEM((wb, Lp + 2 * EDGE, H), F32),
            pltpu.VMEM((M, T2 * H), BF16),
            pltpu.VMEM((T2 * H, C), BF16),
            pltpu.VMEM((H, nw * Lp), BF16),
            pltpu.VMEM((2, nw, C), F32),
            pltpu.VMEM((2, C), F32),
            pltpu.SemaphoreType.DMA((2, g)),
            HALO_SEMS,
        ]
        + group.scratch(2, C),
        4 * nw * Lp * T2 * C * H,
        nw * Lp * C * 20,
        cid=5,
    )(lens, *[a for _, a in pairs])

    chips, rb = plan.chips, plan.rb
    turns_t = tail_turns(plan)
    rest = max(nw - plan.cut, 1)

    def x_block(t):
        block = jnp.int32(0)
        for n, (what, k) in enumerate(turns_t):
            if what == "x":
                block = jnp.where(t >= n, k, block)
        return block

    sshape = (T1 + 2, 2, chips, rb, C // 2)
    pairs = ins(
        (early(wb, Lp, C), dz2),
        (whole(2, nw, C), dland2),
        (early(wb, Lp, C), x2),
        (early_land(C), land2),
        (cot_spec, cotangent),
        (whole(2, 3, nw, C), beyond),
        (
            pl.BlockSpec(
                (wb, L, Ch), lambda t: (grp() * steps + x_block(t), 0, half())
            ),
            inputs,
        ),
        (ANY, X5),
        (
            pl.BlockSpec(
                (T1, Ch, C), lambda t: (0, half(), 0), pipeline_mode=pl.Buffered(1)
            ),
            conv_weight,
        ),
        (whole(Hh, T2 * C), grads),
        (whole(Hh, C), pgrad),
        (whole(*state_shape), state),
        (half_of(STATE), state),
        (ANY, res),
    )
    gz, gz_got, sums1, summed, res_more = call(
        tail_kernel,
        plan,
        "tail",
        len(turns_t),
        pairs,
        [
            (pl.BlockSpec((wb, cs, L), lambda t: (x_block(t), 0, 0)), (nw, cs, L), BF16),
            (ANY, (g, nw, cs, L), BF16),
            (const(2, Ch), (2, Ch), F32),
            (ANY, sshape, BF16),
            (ANY, (g, rest, cs, Lp), BF16),
        ],
        [
            pltpu.VMEM((wb, Lp + 16, C), F32),
            pltpu.VMEM((steps, M, 3 * C), BF16),
            pltpu.VMEM((Ch, nw * Lp), BF16),
            pltpu.VMEM((2 * Ch, 3 * C), BF16),
            pltpu.VMEM((L, L), BF16),
            pltpu.VMEM((Ch, Ch), BF16),
            pltpu.VMEM((4, Ch, L), F32),
            pltpu.VMEM((2 * Ch, max(M, C)), F32),
            pltpu.VMEM((g - 1, nw, cs, L), BF16),
            pltpu.VMEM((2, Ch, L), BF16),
            pltpu.VMEM((2, Ch, L), F32),
            pltpu.VMEM((2, nw * Lp, C), BF16),
            pltpu.SemaphoreType.DMA((2,)),
            pltpu.SemaphoreType.DMA((2, g)),
            pltpu.SemaphoreType.DMA((2, g)),
        ]
        + Reduction.scratch(plan, tail_batches(plan))
        + group.scratch(2, C),
        2 * nw * Lp * (6 + T1) * C * Ch,
        nw * Lp * C * 40,
        cid=6,
    )(lens, *[a for _, a in pairs])

    count = NW // wb
    turns = min(count, chips)

    def own_block(t):
        return jnp.where(lax.div(t, steps) == grp(), lax.rem(t, steps), 0)

    def got_slot(t):
        off = lax.rem(grp() - lax.div(t, steps) + g, g)
        return jnp.maximum(off, 1), jnp.where(off > 0, lax.rem(t, steps), 0)

    pairs = ins(
        (pl.BlockSpec((wb, L, Ch), lambda t: (t, 0, half())), inputs),
        (pl.BlockSpec((wb, cs, L), lambda t: (own_block(t), 0, 0)), gz),
        (pl.BlockSpec((1, wb, cs, L), lambda t: got_slot(t) + (0, 0)), gz_got),
        (whole(2, Ch), sums1),
        (pl.BlockSpec((1, wb, cs, Lp), lambda t: (grp(), own_block(t), 0, 0)), res),
        (pl.BlockSpec((1, wb, cs, Lp), lambda t: got_slot(t) + (0, 0)), res_got),
        (
            pl.BlockSpec((1, min(wb, rest), cs, Lp), lambda t: (got_slot(t)[0], 0, 0, 0)),
            res_more,
        ),
        (
            pl.BlockSpec(
                (T1 + 2, 2, chips // turns, rb, C // 2),
                lambda t: (0, 0, t * turns // count, 0, 0),
            ),
            summed,
        ),
        (whole(*state_shape), state),
        (half_of(STATE), state),
    )
    outs = call(
        input_grad_kernel,
        plan,
        "input_grad",
        NW // wb,
        pairs,
        [
            (win(wb, cs, L), (NW, cs, L), BF16),
            (win(wb, cs, Lp), (NW, cs, Lp), BF16),
            (
                pl.BlockSpec((T1, cs // turns, C), lambda t: (0, t * turns // count, 0)),
                (T1, cs, C),
                F32,
            ),
            (const(T2, hs, C), (T2, hs, C), F32),
            (const(hs, C), (hs, C), F32),
        ]
        + [(const(1, n), (1, n), F32) for n in (cs, cs, cs, cs, hs, hs, cs)],
        [
            pltpu.VMEM((cs, Ch), BF16),
            pltpu.VMEM((3, cs, L), F32),
            pltpu.VMEM((Ch, L), F32),
        ],
        2 * NW * L * Ch * cs,
        NW * L * cs * 8,
    )(lens, *[a for _, a in pairs])
    grad, result, conv_grad, dil_grad, point_grad = outs[:5]
    g1, b1, g2, b2, g3, b3, pb = [a[0] for a in outs[5:]]
    return (
        jnp.swapaxes(result, 1, 2),
        jnp.swapaxes(grad, 1, 2),
        jnp.swapaxes(conv_grad, 1, 2),
        g1,
        b1,
        g2,
        b2,
        jnp.swapaxes(dil_grad, 1, 2),
        g3,
        b3,
        point_grad,
        pb,
    )


def solution(mesh):
    in_specs = (
        P(None, "seq", None),
        P(),
        P(),
        P(),
        P(),
        P("ch"),
        P("ch"),
        P(None, None, "ch"),
        P("ch"),
        P("ch"),
        P("ch", None),
        P("ch"),
        P(None, "seq", None),
    )
    out_specs = (
        P(None, "seq", "ch"),
        P(None, "seq", "ch"),
        P(None, None, "ch"),
        P("ch"),
        P("ch"),
        P("ch"),
        P("ch"),
        P(None, None, "ch"),
        P("ch"),
        P("ch"),
        P("ch", None),
        P("ch"),
    )
    return jax.shard_map(
        per_device, mesh=mesh, in_specs=in_specs, out_specs=out_specs, check_vma=False
    )
```

```python
from functools import partial
from typing import NamedTuple

import jax
import jax.numpy as jnp
from jax import lax
from jax.experimental import pallas as pl
from jax.experimental.pallas import tpu as pltpu
from jax.sharding import PartitionSpec as P

DIL = 14
EDGE = 16
EPS = 1e-05
GC0 = 0.7978845608028654
GC1 = 0.044715
F32 = jnp.float32
BF16 = jnp.bfloat16
MESH = pl.DeviceIdType.MESH
VMEM_LIMIT = 58 * 1024 * 1024
ANY = pl.BlockSpec(memory_space=pl.ANY)
SMEM = pl.BlockSpec(memory_space=pltpu.SMEM)


ST1, GAIN2, SHIFT2, BIAS, GAIN3, SHIFT3, GAIN1, SHIFT1, ST2, ST3, SU3, BSUM, SU2 = (
    0, 2, 3, 4, 5, 6, 7, 8, 9, 11, 13, 15, 16
)
STATE = 24


class Plan(NamedTuple):
    ns: int
    nz: int
    R: int
    NW: int
    L: int
    C: int
    H: int
    T1: int
    T2: int
    wb: int

    @property
    def g(self):
        return self.nz // self.R

    @property
    def nw(self):
        return self.NW // self.g

    @property
    def Lp(self):
        return self.L // 2

    @property
    def cs(self):
        return self.C // self.nz

    @property
    def Ch(self):
        return self.C // self.R

    @property
    def Hh(self):
        return self.H // self.R

    @property
    def steps(self):
        return self.nw // self.wb

    @property
    def chips(self):
        return self.ns // 2

    @property
    def ahead(self):
        return max(1, self.steps // 2)

    @property
    def cut(self):
        return self.ahead * self.wb

    @property
    def rb(self):
        return self.cs // self.chips

    def place(self):
        s, z = lax.axis_index("seq"), lax.axis_index("ch")
        return s, z, lax.rem(z, self.g), lax.div(z, self.g)


def gelu(z):
    t = jnp.tanh(z * (GC0 + (GC0 * GC1) * (z * z)))
    return z * (0.5 + 0.5 * t)


def gelu_both(z):
    sq = z * z
    t = jnp.tanh(z * (GC0 + (GC0 * GC1) * sq))
    h = 0.5 + 0.5 * t
    v = z * h
    return v, h + v * (1.0 - t) * (GC0 + (3.0 * GC0 * GC1) * sq)


def gelu_slope(z):
    return gelu_both(z)[1]


def fold(v):
    return jnp.sum(v.reshape(v.shape[0] // 8, 8, v.shape[1]), axis=0)


def unfold(v):
    return jnp.sum(v, axis=0, keepdims=True)


def rows_of(shape):
    return lax.broadcasted_iota(jnp.int32, shape, 0)


def lanes_of(shape):
    return lax.broadcasted_iota(jnp.int32, shape, 1)


def total_of(lens):
    n = lens[0]
    for k in range(1, lens.shape[0]):
        n = n + lens[k]
    return n.astype(F32)


def norm_of(stats, total):
    mean = stats[0:1] / total
    square = stats[1:2] / total
    return mean, lax.rsqrt(square - mean * mean + EPS)


def flat(ref):
    return ref[...].reshape(1, ref.shape[0])


def column(row, n):
    return jnp.broadcast_to(row, (n, row.shape[1])).T


def mm(a, b):
    return jnp.dot(a, b, preferred_element_type=F32)


def mm_nt(a, b):
    return lax.dot_general(a, b, (((1,), (1,)), ((), ())), preferred_element_type=F32)


def mm_tn(a, b):
    return lax.dot_general(a, b, (((0,), (0,)), ((), ())), preferred_element_type=F32)


def mm_tt(a, b):
    return lax.dot_general(a, b, (((0,), (1,)), ((), ())), preferred_element_type=F32)


def eye_matrix(n, m, first):
    return jnp.where(lanes_of((n, m)) == rows_of((n, m)) + first, 1.0, 0.0).astype(BF16)


def pick_matrix(L):
    r, n = rows_of((L, L)), lanes_of((L, L))
    bin_of = 2 * r - jnp.where(r >= L // 2, L - 1, 0)
    return jnp.where(n == bin_of, 1.0, 0.0).astype(BF16)


def remote(src, dst, send, recv, device):
    return pltpu.make_async_remote_copy(
        src_ref=src,
        dst_ref=dst,
        send_sem=send,
        recv_sem=recv,
        device_id=device,
        device_id_type=MESH,
    )


def wrap(v, n):
    return jnp.where(v >= n, v - n, v)


def greet(devices):
    barrier = pltpu.get_barrier_semaphore()
    for device in devices:
        pl.semaphore_signal(barrier, inc=1, device_id=device, device_id_type=MESH)


def meet(devices):
    pl.semaphore_wait(pltpu.get_barrier_semaphore(), len(devices))


class Peers:
    def __init__(self, me, others):
        self.me, self.others = me, others
        self.count = len(others) + 1

    def start(self, link):
        packet, buf, sems = link
        for device in self.others:
            remote(packet, buf.at[self.me], sems.at[0], sems.at[1], device).start()

    def finish(self, link):
        packet, buf, sems = link
        buf[self.me] = packet[...]
        rest = buf.at[pl.ds(0, self.count - 1)]
        done = remote(rest, rest, sems.at[0], sems.at[1], self.others[0])
        done.wait_recv()
        acc = buf[0]
        for q in range(1, self.count):
            acc = acc + buf[q]
        done.wait_send()
        return acc

    def scratch(self, rows, width):
        return [
            pltpu.VMEM((rows, width), F32),
            pltpu.VMEM((self.count, rows, width), F32),
            pltpu.SemaphoreType.DMA((2,)),
        ]


def group_peers(plan):
    s, z, i, h = plan.place()
    g = plan.g
    others = [
        (wrap(s + a, plan.ns), h * g + wrap(i + b, g))
        for a in range(plan.ns)
        for b in range(g)
        if a or b
    ]
    return Peers(s * g + i, others)


def plane_peers(plan):
    s, z, i, h = plan.place()
    return Peers(s, [(wrap(s + a, plan.ns), z) for a in range(1, plan.ns)])


def line_peers(plan):
    s, z, i, h = plan.place()
    return Peers(z, [(s, wrap(z + a, plan.nz)) for a in range(1, plan.nz)])


class Halo:
    def __init__(self, plan, edge, land, sems):
        self.edge, self.land, self.sems = edge, land, sems
        s, z, _, _ = plan.place()
        self.to = ((wrap(s + plan.ns - 1, plan.ns), z), (wrap(s + 1, plan.ns), z))

    def copy(self, side, rows):
        return remote(
            self.edge.at[side, rows],
            self.land.at[1 - side, rows],
            self.sems.at[0, side],
            self.sems.at[1, side],
            self.to[side],
        )

    def start(self, first, count):
        for side in range(2):
            self.copy(side, pl.ds(first, count)).start()

    def finish(self):
        for side in range(2):
            done = self.copy(side, pl.ds(0, self.land.shape[1]))
            done.wait_recv()
            done.wait_send()


HALO_SEMS = pltpu.SemaphoreType.DMA((2, 2))


class Gather:
    def __init__(self, plan, part, full, sems):
        self.plan, self.part, self.full, self.sems = plan, part, full, sems
        self.s, self.z, self.i, self.h = plan.place()
        self.c, self.m = lax.rem(self.s, 2), lax.div(self.s, 2)
        self.chips = plan.chips
        self.every = self.chips // 4
        self.tap = lax.div(self.m, self.every)
        self.owner = lax.rem(self.m, self.every) == 0
        self.mine = full.at[self.c, self.tap]

    def others(self):
        g, nz = self.plan.g, self.plan.nz
        return [(self.s, wrap(self.h * g + g + r, nz)) for r in range(nz - g)]

    def far(self, off):
        return (2 * wrap(self.m + off, self.chips) + self.c, self.z)

    def own(self):
        return pltpu.make_async_copy(self.part, self.mine.at[self.z], self.sems.at[0, 0])

    def line(self, off):
        device = (self.s, wrap(self.z + off, self.plan.nz))
        return remote(
            self.part, self.mine.at[self.z], self.sems.at[0, 1], self.sems.at[1, 1], device
        )

    def chip(self, off):
        return remote(self.mine, self.mine, self.sems.at[0, 2], self.sems.at[1, 2], self.far(off))

    def pair(self):
        half = self.full.at[self.c]
        device = (2 * self.m + 1 - self.c, self.z)
        return remote(half, half, self.sems.at[0, 3], self.sems.at[1, 3], device)

    def line_start(self):
        @pl.when(self.owner)
        def _():
            self.own().start()
            for off in range(1, self.plan.nz):
                self.line(off).start()

    def line_finish(self):
        @pl.when(self.owner)
        def _():
            self.own().wait()
            rest = self.mine.at[pl.ds(0, self.plan.nz - 1)]
            device = (self.s, wrap(self.z + 1, self.plan.nz))
            done = remote(rest, rest, self.sems.at[0, 1], self.sems.at[1, 1], device)
            done.wait_recv()
            done.wait_send()

    def chips_start(self):
        @pl.when(self.owner)
        def _():
            for off in range(1, self.chips):
                self.chip(off).start()

    def pair_start(self):
        def taken(count):
            rest = self.full.at[self.c, pl.ds(0, count)]
            return remote(rest, rest, self.sems.at[0, 2], self.sems.at[1, 2], self.far(1))

        @pl.when(self.owner)
        def _():
            taken(3).wait_recv()
            for off in range(1, self.chips):
                self.chip(off).wait_send()

        if self.every > 1:

            @pl.when(jnp.logical_not(self.owner))
            def _():
                taken(4).wait_recv()

        self.pair().start()

    def pair_finish(self):
        done = self.pair()
        done.wait_recv()
        done.wait_send()


def first_step():
    return pl.program_id(0) == 0


def last_step():
    return pl.program_id(0) == pl.num_programs(0) - 1


def keep_state(old, new):
    new[...] = old[...]


def head_kernel(plan, nm, lens, x, xtop, xend, ctop, cend, g2, s2, pb, g3, s3,
                w_hbm, gain, shift, taps, pw,
                X5, x2, land, state, beyond_out, full,
                macc, beyond, xedge, sel, edge, acc, w_ref, w_sem, part,
                gather_sems, xhalo_sems, halo_sems, *links):
    t = pl.program_id(0)
    peers, plane, line = group_peers(plan), plane_peers(plan), line_peers(plan)
    xhalo = Halo(plan, xedge, beyond, xhalo_sems)
    halo = Halo(plan, edge, land, halo_sems)
    gather = Gather(plan, part, full, gather_sems)
    w_copy = pltpu.make_async_copy(w_hbm, w_ref, w_sem)
    plane_link, line_link, link = links[:3], links[3:6], links[6:]
    s, z, i, h = plan.place()
    L, Lp, C, nw, nz, wb = plan.L, plan.Lp, plan.C, plan.nw, plan.nz, plan.wb
    share = plan.NW // nz
    c = t - nm
    everyone = peers.others + gather.others()

    @pl.when(first_step())
    def _():
        w_copy.start()
        greet(everyone)
        part[...] = jnp.where(gather.tap == 3, pw[...], taps[0])
        macc[...] = jnp.zeros_like(macc)
        acc[...] = jnp.zeros_like(acc)
        state[...] = jnp.zeros_like(state)
        state[GAIN1 : GAIN1 + 1] = flat(gain)
        state[SHIFT1 : SHIFT1 + 1] = flat(shift)
        n16 = nw * 16
        for side, (xe, ce, places) in enumerate(
            ((xtop, ctop, (0, 1, 0)), (xend, cend, (14, 15, 15)))
        ):
            for k, at in enumerate(places):
                rows, lanes = rows_of((nw, n16)), lanes_of((nw, n16))
                one = jnp.where(lanes == 16 * rows + at, 1.0, 0.0).astype(BF16)
                block = (xe if k < 2 else ce)[...].reshape(n16, C)
                xedge[side, k] = mm(one, block)
        shape = (Lp, L)
        for k in range(plan.T1):
            at = lanes_of(shape) - (2 * rows_of(shape) + (k - 2))
            sel[k * Lp : (k + 1) * Lp] = jnp.where((at == 0) | (at == 1), 1.0, 0.0).astype(BF16)

    @pl.when(c < 0)
    def _():
        rows = rows_of((L, C))
        for w in range(min(share, wb)):
            at = lax.rem(z * share, wb) + w
            valid = 2 * lens[z * share + t * wb + w] - s * L
            v = jnp.where(rows < valid, x[at].astype(F32), 0.0)
            macc[0] += fold(v)
            macc[1] += fold(v * v)

    @pl.when(c == -1)
    def _():
        packet, more = plane_link[0], line_link[0]
        packet[0:1] = unfold(macc[0])
        packet[1:2] = unfold(macc[1])
        meet(everyone)
        plane.start(plane_link)
        xhalo.start(0, 3)
        at = 0
        spans = []
        more[2:3] = jnp.zeros((1, C), F32)
        for ref in (g2, s2, pb, g3, s3):
            n = ref.shape[1]
            more[2:3, at : at + n] = ref[...]
            spans.append((at, n))
            at += n
        more[0:2] = plane.finish(plane_link)
        line.start(line_link)
        gather.line_start()
        state[ST1 : ST1 + 2] = line.finish(line_link)[0:2]
        for k in range(nz):
            row = line_link[1][k]
            for r, (at, n) in zip((GAIN2, SHIFT2, BIAS, GAIN3, SHIFT3), spans):
                state[r : r + 1, k * n : (k + 1) * n] = row[2:3, at : at + n]
        xhalo.finish()
        beyond_out[...] = beyond[...]
        w_copy.wait()

    @pl.when(c >= 0)
    def _():
        mean, rho = norm_of(state[ST1 : ST1 + 2], 2.0 * total_of(lens))
        scale = state[GAIN1 : GAIN1 + 1] * rho
        offset = state[SHIFT1 : SHIFT1 + 1] - mean * scale
        rows = rows_of((L, C))
        row1 = rows_of((1, C))
        row16 = rows_of((16, C))
        def activate(w):
            at = c * wb + w
            valid = 2 * lens[i * nw + at] - s * L
            a = gelu(x[w].astype(F32) * scale + offset)
            a = jnp.where(rows < valid, a, 0.0).astype(BF16)
            picked = mm(sel[...], a)
            for k in range(5):
                X5[w * Lp : (w + 1) * Lp, k * C : (k + 1) * C] = picked[
                    k * Lp : (k + 1) * Lp
                ].astype(BF16)

            def beside(side, k, bin_at):
                a = gelu(beyond[side, k, pl.ds(at, 1), :] * scale + offset)
                here = (row1 + bin_at < valid) & (row1 + (s * L + bin_at) >= 0)
                return jnp.where(here, a, 0.0).astype(BF16).astype(F32)

            l0, l1 = beside(0, 0, -2), beside(0, 1, -1)
            r0, r1 = beside(1, 0, L), beside(1, 1, L + 1)
            top, end = w * Lp, (w + 1) * Lp
            for k, add in ((0, l0 + l1), (1, l1)):
                X5[top : top + 16, k * C : (k + 1) * C] = (
                    picked[k * Lp : k * Lp + 16] + jnp.where(row16 == 0, add, 0.0)
                ).astype(BF16)
            for k, add in ((3, r0), (4, r0 + r1)):
                X5[end - 16 : end, k * C : (k + 1) * C] = (
                    picked[(k + 1) * Lp - 16 : (k + 1) * Lp] + jnp.where(row16 == 15, add, 0.0)
                ).astype(BF16)

        nc = 256
        rowp = rows_of((Lp, nc))

        def convolve(first, count):
            span = slice(first * Lp, (first + count) * Lp)
            for n in range(C // nc):
                cols = slice(n * nc, (n + 1) * nc)
                y = 0.5 * mm(X5[span], w_ref[:, cols])
                s0 = jnp.zeros((8, nc), F32)
                s1 = jnp.zeros((8, nc), F32)
                for w in range(first, first + count):
                    at = c * wb + w
                    valid = lens[i * nw + at] - s * Lp
                    v = y[(w - first) * Lp : (w - first + 1) * Lp]
                    x2[w, :, cols] = v
                    edge[0, at, :, cols] = v[:EDGE].astype(BF16)
                    edge[1, at, :, cols] = v[Lp - EDGE :].astype(BF16)
                    v = jnp.where(rowp < valid, v, 0.0)
                    s0 = s0 + fold(v)
                    s1 = s1 + fold(v * v)
                acc[0:1, cols] += unfold(s0)
                acc[1:2, cols] += unfold(s1)

        count = max(1, wb // 2)
        for first in range(0, wb, count):
            for w in range(first, first + count):
                activate(w)
            convolve(first, count)
        halo.start(c * wb, wb)

    @pl.when(c == 0)
    def _():
        gather.line_finish()
        gather.chips_start()

    @pl.when(last_step())
    def _():
        link[0][...] = acc[...]
        peers.start(link)
        gather.pair_start()
        state[ST2 : ST2 + 2] = peers.finish(link)
        halo.finish()
        gather.pair_finish()


def dilated_kernel(plan, lens, x2, x2land, w_ref, old,
                   Y3, c2, land, state, ext, wf, edge, acc, halo_sems, *link):
    t = pl.program_id(0)
    peers = group_peers(plan)
    halo = Halo(plan, edge, land, halo_sems)
    s, z, i, h = plan.place()
    Lp, C, H, wb = plan.Lp, plan.C, plan.H, plan.wb

    @pl.when(first_step())
    def _():
        greet(peers.others)
        acc[...] = jnp.zeros_like(acc)
        for k in range(plan.T2):
            for c in range(2):
                at = k * C + c * (C // 2)
                wf[:, at : at + C // 2] = w_ref[c, k]

    mean, rho = norm_of(old[ST2 : ST2 + 2], total_of(lens))
    scale = old[GAIN2 : GAIN2 + 1] * rho
    offset = old[SHIFT2 : SHIFT2 + 1] - mean * scale
    rows = rows_of((Lp, C))
    rowe = rows_of((EDGE, C))

    rowh = rows_of((Lp, H))
    sums0, sums1 = jnp.zeros((8, H), F32), jnp.zeros((8, H), F32)
    nh = min(2, wb)
    for first in range(0, wb, wb // nh):
        span = range(first, first + wb // nh)
        for w in span:
            valid = lens[i * plan.nw + t * wb + w] - s * Lp
            a = jnp.where(rows < valid, gelu(x2[w] * scale + offset), 0.0)
            al = gelu(x2land[0, w].astype(F32) * scale + offset)
            al = jnp.where((rowe - EDGE < valid) & (s > 0), al, 0.0)
            ah = gelu(x2land[1, w].astype(F32) * scale + offset)
            ah = jnp.where(rowe + Lp < valid, ah, 0.0)
            ext[w, 0:EDGE] = al
            ext[w, EDGE : EDGE + Lp] = a
            ext[w, EDGE + Lp :] = ah
            top, end = w * Lp, (w + 1) * Lp
            Y3[top:end, 0:C] = ext[w, EDGE - DIL : EDGE - DIL + Lp].astype(BF16)
            Y3[top:end, C : 2 * C] = a.astype(BF16)
            Y3[top:end, 2 * C : 3 * C] = ext[w, EDGE + DIL : EDGE + DIL + Lp].astype(BF16)
        y = mm_nt(Y3[first * Lp : (first + wb // nh) * Lp], wf[...])
        for w in span:
            at = t * wb + w
            valid = lens[i * plan.nw + at] - s * Lp
            v = y[(w - first) * Lp : (w - first + 1) * Lp]
            c2[w] = v
            edge[0, at] = v[:EDGE].astype(BF16)
            edge[1, at] = v[Lp - EDGE :].astype(BF16)
            v = jnp.where(rowh < valid, v, 0.0)
            sums0 = sums0 + fold(v)
            sums1 = sums1 + fold(v * v)
    acc[0:1, 0:H] += unfold(sums0)
    acc[0:1, H:] += unfold(sums1)

    @pl.when(first_step())
    def _():
        meet(peers.others)

    halo.start(t * wb, wb)

    @pl.when(last_step())
    def _():
        link[0][...] = acc[...]
        peers.start(link)
        keep_state(old, state)
        got = peers.finish(link)
        state[ST3 : ST3 + 1, 0:H] = got[:, 0:H]
        state[ST3 + 1 : ST3 + 2, 0:H] = got[:, H:]
        halo.finish()


def point_kernel(plan, lens, c2, x2, cot, w_ref, old, half_state,
                 res, dz, pgrad, land, state, res_got,
                 pw, a3s, a3T, dos, edge, acc, halo_sems, bulk_sems, *link):
    t = pl.program_id(0)
    peers = group_peers(plan)
    halo = Halo(plan, edge, land, halo_sems)
    s, z, i, h = plan.place()
    Lp, C, H, wb, cs = plan.Lp, plan.C, plan.H, plan.wb, plan.cs
    M = wb * Lp
    g, steps, ahead = plan.g, plan.steps, plan.ahead

    def bulk(off, rows):
        to = wrap(i + off, g)
        return remote(
            res.at[to, rows],
            res_got.at[off, rows],
            bulk_sems.at[0, off],
            bulk_sems.at[1, off],
            (s, h * g + to),
        )

    def result_of(block):
        y = mm(a3s[pl.ds(pl.multiple_of(block * M, 128), M)], w_ref[h, 0])
        rowr = rows_of((Lp, y.shape[1]))
        for w in range(wb):
            at = block * wb + w
            valid = lens[i * plan.nw + at] - s * Lp
            r = x2[w] + y[w * Lp : (w + 1) * Lp] + half_state[BIAS : BIAS + 1]
            r = jnp.where(rowr < valid, r, 0.0).astype(BF16).T
            for k in range(g):
                res[k, at] = r[k * cs : (k + 1) * cs]

    @pl.when(first_step())
    def _():
        greet(peers.others)
        acc[...] = jnp.zeros_like(acc)
        for c in range(2):
            pw[:, c * (C // 2) : (c + 1) * (C // 2)] = w_ref[c, 0]

    @pl.when(t < plan.steps)
    def _():
        mean, rho = norm_of(old[ST3 : ST3 + 2, 0:H], total_of(lens))
        scale = old[GAIN3 : GAIN3 + 1, 0:H] * rho
        offset = old[SHIFT3 : SHIFT3 + 1, 0:H] - mean * scale
        shift = -mean * rho
        rowc = rows_of((Lp, C))
        rowh = rows_of((Lp, H))
        block = pl.ds(pl.multiple_of(t * M, 128), M)
        bias = jnp.zeros((8, C), F32)
        parts = []
        for w in range(wb):
            valid = lens[i * plan.nw + t * wb + w] - s * Lp
            d = jnp.where(rowc < valid, cot[w].astype(F32), 0.0)
            bias = bias + fold(d)
            parts.append(d.astype(BF16))
        d = jnp.concatenate(parts, axis=0)
        dos[block] = d
        da = mm_nt(d, pw[...])
        s0, s1 = jnp.zeros((8, H), F32), jnp.zeros((8, H), F32)
        parts = []
        for w in range(wb):
            at = t * wb + w
            valid = lens[i * plan.nw + at] - s * Lp
            top, end = w * Lp, (w + 1) * Lp
            v = c2[w]
            act, slope = gelu_both(v * scale + offset)
            parts.append(jnp.where(rowh < valid, act, 0.0).astype(BF16))
            dzw = da[top:end] * slope
            dz[w] = dzw
            edge[0, at] = dzw[:EDGE].astype(BF16)
            edge[1, at] = dzw[Lp - EDGE :].astype(BF16)
            s0 = s0 + fold(dzw)
            s1 = s1 + fold(dzw * (v * rho + shift))
        a3 = jnp.concatenate(parts, axis=0)
        a3s[block] = a3
        a3T[:, block] = a3.T
        acc[0:1, 0:H] += unfold(s0)
        acc[0:1, H : 2 * H] += unfold(s1)
        acc[1:2] += unfold(bias)

    @pl.when(first_step())
    def _():
        meet(peers.others)

    @pl.when(t < steps)
    def _():
        halo.start(t * wb, wb)

    @pl.when(t < ahead)
    def _():
        result_of(t)
        for off in range(1, g):
            bulk(off, pl.ds(t * wb, wb)).start()

    @pl.when(t == steps - 1)
    def _():
        link[0][...] = acc[...]
        peers.start(link)

    @pl.when(t >= steps)
    def _():
        result_of(t - steps + ahead)

    @pl.when(last_step())
    def _():
        rows = pl.ds(pl.multiple_of(h * plan.Hh, 16), plan.Hh)
        pgrad[...] = mm(a3T[rows], dos[...]).astype(BF16)
        keep_state(old, state)
        got = peers.finish(link)
        state[SU3 : SU3 + 1, 0:H] = got[0:1, 0:H]
        state[SU3 + 1 : SU3 + 2, 0:H] = got[0:1, H : 2 * H]
        state[BSUM : BSUM + 1] = got[1:2]
        halo.finish()
        for off in range(1, g):
            bulk(off, pl.ds(0, plan.cut)).wait()


def dilated_back_kernel(plan, lens, c2, cland, dz3, dland, x2, Y3, w_ref, old, res,
                        dz2, grads, land, state, res_got,
                        ext, Z3, wt, dcT, edge, acc, bulk_sems, halo_sems, *link):
    t = pl.program_id(0)
    peers = group_peers(plan)
    halo = Halo(plan, edge, land, halo_sems)
    s, z, i, h = plan.place()
    Lp, C, H, wb, nw, g = plan.Lp, plan.C, plan.H, plan.wb, plan.nw, plan.g

    def bulk(off):
        to = wrap(i + off, g)
        return remote(
            res.at[to, pl.ds(plan.cut, nw - plan.cut)],
            res_got.at[off],
            bulk_sems.at[0, off],
            bulk_sems.at[1, off],
            (s, h * g + to),
        )

    offs = range(1, g) if plan.cut < nw else ()

    @pl.when(first_step())
    def _():
        greet(peers.others)
        acc[...] = jnp.zeros_like(acc)
        for k in range(plan.T2):
            for c in range(2):
                cols = slice(c * (C // 2), (c + 1) * (C // 2))
                wt[k * H : (k + 1) * H, cols] = w_ref[c, k]
        meet(peers.others)
        for off in offs:
            bulk(off).start()

    @pl.when(t < plan.steps)
    def _():
        total = total_of(lens)
        mean3, rho3 = norm_of(old[ST3 : ST3 + 2, 0:H], total)
        gr3 = old[GAIN3 : GAIN3 + 1, 0:H] * rho3
        sg3 = old[SU3 : SU3 + 1, 0:H] / total
        gg3 = old[SU3 + 1 : SU3 + 2, 0:H] / total
        mean2, rho2 = norm_of(old[ST2 : ST2 + 2], total)
        scale2 = old[GAIN2 : GAIN2 + 1] * rho2
        offset2 = old[SHIFT2 : SHIFT2 + 1] - mean2 * scale2
        rowh = rows_of((Lp, H))
        rowe = rows_of((EDGE, H))
        rowc = rows_of((Lp, C))

        by_v = -gr3 * rho3 * gg3
        by_1 = gr3 * (mean3 * rho3 * gg3 - sg3)
        shift2 = -mean2 * rho2

        def back(dz, v):
            return gr3 * dz + by_v * v + by_1

        for w in range(wb):
            valid = lens[i * nw + t * wb + w] - s * Lp
            d = jnp.where(rowh < valid, back(dz3[w], c2[w]), 0.0)
            dl = back(dland[0, w].astype(F32), cland[0, w].astype(F32))
            dl = jnp.where((rowe - EDGE < valid) & (s > 0), dl, 0.0)
            dh = back(dland[1, w].astype(F32), cland[1, w].astype(F32))
            dh = jnp.where(rowe + Lp < valid, dh, 0.0)
            ext[w, 0:EDGE] = dl
            ext[w, EDGE : EDGE + Lp] = d
            ext[w, EDGE + Lp :] = dh
            top, end = w * Lp, (w + 1) * Lp
            Z3[top:end, 0:H] = ext[w, EDGE + DIL : EDGE + DIL + Lp].astype(BF16)
            Z3[top:end, H : 2 * H] = d.astype(BF16)
            Z3[top:end, 2 * H : 3 * H] = ext[w, EDGE - DIL : EDGE - DIL + Lp].astype(BF16)

        y = mm(Z3[...], wt[...])

        M = wb * Lp
        dcT[:, pl.ds(pl.multiple_of(t * M, 128), M)] = Z3[:, H : 2 * H].T
        s0, s1 = jnp.zeros((8, C), F32), jnp.zeros((8, C), F32)
        for w in range(wb):
            at = t * wb + w
            valid = lens[i * nw + at] - s * Lp
            v = x2[w]
            dzw = y[w * Lp : (w + 1) * Lp] * gelu_slope(v * scale2 + offset2)
            dzw = jnp.where(rowc < valid, dzw, 0.0)
            dz2[w] = dzw
            edge[0, pl.ds(at, 1)] = dzw[0:1]
            edge[1, pl.ds(at, 1)] = dzw[Lp - 1 : Lp]
            s0 = s0 + fold(dzw)
            s1 = s1 + fold(dzw * (v * rho2 + shift2))
        acc[0:1] += unfold(s0)
        acc[1:2] += unfold(s1)

    @pl.when(t == plan.steps - 1)
    def _():
        link[0][...] = acc[...]
        peers.start(link)
        halo.start(0, nw)

    @pl.when(t >= plan.steps)
    def _():
        rows = pl.ds(pl.multiple_of(h * plan.Hh, 16), plan.Hh)
        grads[...] = mm(dcT[rows], Y3[...]).astype(BF16)

    @pl.when(last_step())
    def _():
        keep_state(old, state)
        state[SU2 : SU2 + 2] = peers.finish(link)
        halo.finish()
        for off in offs:
            bulk(off).wait()


class Reduction:
    def __init__(self, plan, batches, out, give, mine, got, spread, half, mate, sems):
        self.plan, self.batches, self.out = plan, batches, out
        self.give, self.mine, self.got, self.spread = give, mine, got, spread
        self.half, self.mate = half, mate
        self.sems = sems
        self.s, self.z, self.i, self.h = plan.place()
        self.c = lax.rem(self.s, 2)
        self.m = lax.div(self.s, 2)
        self.chips = plan.chips

    @staticmethod
    def scratch(plan, batches):
        taps, wide = plan.T1 + 2, plan.C // 2
        full = (taps, plan.chips, plan.g, plan.rb, wide)
        part = (taps, plan.g, plan.rb, wide)
        return [
            pltpu.VMEM((taps, 2, plan.chips, plan.rb, wide), BF16),
            *[pltpu.VMEM(full, BF16)] * 4,
            *[pltpu.VMEM(part, BF16)] * 2,
            pltpu.SemaphoreType.DMA((2, len(batches), 5)),
        ]

    def copy(self, b, phase, src, dst, device):
        return remote(src, dst, self.sems.at[0, b, phase], self.sems.at[1, b, phase], device)

    def finish(self, b, phase, ref, device):
        done = self.copy(b, phase, ref, ref, device)
        done.wait_recv()
        done.wait_send()

    def taps(self, b):
        return pl.ds(*self.batches[b])

    def pair(self):
        return (2 * self.m + (1 - self.c), self.z)

    def far(self, off):
        return (2 * wrap(self.m + off, self.chips) + self.c, self.z)

    def member(self, off):
        return (self.s, self.h * self.plan.g + wrap(self.i + off, self.plan.g))

    def put(self, k, rows):
        wide = self.plan.C // 2
        for j in range(self.plan.g):
            for m in range(self.chips):
                v = rows(j, m)
                left, right = v[:, :wide], v[:, wide:]
                self.mine[k, m, j] = jnp.where(self.c == 0, left, right).astype(BF16)
                self.give[k, m, j] = jnp.where(self.c == 0, right, left).astype(BF16)

    def step0(self, b):
        taps = self.taps(b)
        self.copy(b, 0, self.give.at[taps], self.got.at[taps], self.pair()).start()

    def step1(self, b):
        taps = self.taps(b)
        self.finish(b, 0, self.got.at[taps], self.pair())
        first, count = self.batches[b]
        for k in range(first, first + count):
            v = self.mine[k].astype(F32) + self.got[k].astype(F32)
            self.mine[k] = v.astype(BF16)
        for off in range(1, self.chips):
            src = self.mine.at[taps, wrap(self.m + off, self.chips)]
            self.copy(b, 1, src, self.spread.at[taps, self.m], self.far(off)).start()

    def step2(self, b):
        taps = self.taps(b)
        self.finish(b, 1, self.spread.at[taps, pl.ds(0, self.chips - 1)], self.far(1))
        first, count = self.batches[b]
        for k in range(first, first + count):
            self.spread[k, self.m] = self.mine[k, self.m]
            v = self.spread[k, 0].astype(F32)
            for n in range(1, self.chips):
                v = v + self.spread[k, n].astype(F32)
            self.half[k] = v.astype(BF16)
        for off in range(1, self.plan.g):
            src = self.half.at[taps, wrap(self.i + off, self.plan.g)]
            self.copy(b, 2, src, self.mate.at[taps, off], self.member(off)).start()

    def step3(self, b):
        taps = self.taps(b)
        self.finish(b, 2, self.mate.at[taps, pl.ds(1, self.plan.g - 1)], self.member(1))
        first, count = self.batches[b]
        for k in range(first, first + count):
            v = self.half[k, self.i].astype(F32)
            for off in range(1, self.plan.g):
                v = v + self.mate[k, off].astype(F32)
            self.out[k, self.c, self.m] = v.astype(BF16)
        mine = self.out.at[taps, self.c, self.m]
        for off in range(1, self.chips):
            self.copy(b, 3, mine, mine, self.far(off)).start()

    def step4(self, b):
        taps = self.taps(b)
        self.finish(b, 3, self.out.at[taps, self.c, pl.ds(0, self.chips - 1)], self.far(1))
        mine = self.out.at[taps, self.c]
        self.copy(b, 4, mine, mine, self.pair()).start()

    def step5(self, b):
        self.finish(b, 4, self.out.at[self.taps(b), self.c], self.pair())


def tail_turns(plan):
    return [("x", n) for n in range(plan.steps)] + [("w", n) for n in range(plan.T1)]


def tail_batches(plan):
    return [(plan.T1, 2), (0, 3), (3, plan.T1 - 3)]


def tail_kernel(plan, lens, dz2, dzland, x2, x2land, cot, beyond, x, X5_hbm, taps, grads, pgrad,
                old, half_state,
                gz, gz_got, sums, summed,
                ext, D3, D0T, wcat, pick, eye, cols, y, part, split, acc, X5, X5_sems,
                bulk_sems, *rest):
    t = pl.program_id(0)
    s, z, i, h = plan.place()
    L, Lp, C, wb, g, nw = plan.L, plan.Lp, plan.C, plan.wb, plan.g, plan.nw
    Ch, cs, T1 = plan.Ch, plan.cs, plan.T1
    M = wb * Lp
    nD = plan.steps
    turns = tail_turns(plan)
    last = len(turns) - 1
    peers = group_peers(plan)
    red = Reduction(plan, tail_batches(plan), *rest[:8])
    link = rest[8:]

    def member(off):
        return (s, h * g + wrap(i + off, g))

    def send(step):
        rows = pl.ds(step * wb, wb)
        for off in range(1, g):
            remote(
                part.at[off - 1, rows],
                gz_got.at[off, rows],
                bulk_sems.at[0, off],
                bulk_sems.at[1, off],
                member(off),
            ).start()

    def X5_copy(k):
        cols = pl.ds(pl.multiple_of(k * C, 128), C)
        return pltpu.make_async_copy(X5_hbm.at[:, cols], X5.at[k % 2], X5_sems.at[k % 2])

    def when(at):
        return pl.when(t == min(at, last))

    def turn(kind, k):
        return turns.index((kind, k)) if (kind, k) in turns else last

    def turn_of(kind):
        index = jnp.int32(0)
        here = False
        for n, (what, k) in enumerate(turns):
            if what == kind:
                index = jnp.where(t == n, k, index)
                here = (t == n) | here
        return here, index

    @when(0)
    def _():
        greet(peers.others)
        acc[...] = jnp.zeros_like(acc)
        pick[...] = pick_matrix(L)
        eye[...] = eye_matrix(Ch, Ch, 0)
        mean, rho = norm_of(half_state[ST1 : ST1 + 2], 2.0 * total_of(lens))
        scale = half_state[GAIN1 : GAIN1 + 1] * rho
        offset = half_state[SHIFT1 : SHIFT1 + 1] - mean * scale
        for k, row in enumerate((scale, offset, rho, -mean * rho)):
            cols[k] = column(row, L)
        for first in range(0, Ch, 64):
            rows = slice(first, min(first + 64, Ch))
            for r, parts in enumerate((((0,), (1, 2), (3, 4)), ((0, 1), (2, 3), (4,)))):
                for k, which in enumerate(parts):
                    v = taps[which[0], rows]
                    if len(which) > 1:
                        v = (v.astype(F32) + taps[which[1], rows].astype(F32)).astype(BF16)
                    at = r * Ch
                    wcat[at + rows.start : at + rows.stop, k * C : (k + 1) * C] = v
        meet(peers.others)

    @pl.when(t < nD)
    def _():
        total = total_of(lens)
        mean, rho = norm_of(old[ST2 : ST2 + 2], total)
        gr = old[GAIN2 : GAIN2 + 1] * rho
        sg = old[SU2 : SU2 + 1] / total
        gg = old[SU2 + 1 : SU2 + 2] / total
        rowc = rows_of((Lp, C))
        row1 = rows_of((1, C))

        by_dz = 0.5 * gr
        by_v = -0.5 * gr * rho * gg
        by_1 = 0.5 * gr * (mean * rho * gg - sg)

        def back(dout, dz, v):
            return 0.5 * dout + by_dz * dz + by_v * v + by_1

        def grad_of(w):
            at = t * wb + w
            valid = lens[i * nw + at] - s * Lp
            d = back(cot[w].astype(F32), dz2[w], x2[w])
            d = jnp.where(rowc < valid, d, 0.0)
            one = pl.ds(at, 1)
            dl = back(beyond[0, 2, one, :], dzland[0, one, :], x2land[0, w, EDGE - 1 : EDGE].astype(F32))
            dl = jnp.where((row1 - 1 < valid) & (s > 0), dl, 0.0)
            dh = back(beyond[1, 2, one, :], dzland[1, one, :], x2land[1, w, 0:1].astype(F32))
            dh = jnp.where(row1 + Lp < valid, dh, 0.0)
            ext[w, 7:8] = dl
            ext[w, 8 : 8 + Lp] = d
            ext[w, 8 + Lp : 9 + Lp] = dh
            top, end = w * Lp, (w + 1) * Lp
            D3[top:end, 0:C] = ext[w, 9 : 9 + Lp].astype(BF16)
            D3[top:end, C : 2 * C] = d.astype(BF16)
            D3[top:end, 2 * C : 3 * C] = ext[w, 7 : 7 + Lp].astype(BF16)

        for w in range(wb):
            grad_of(w)
        half = D3[:, pl.ds(pl.multiple_of(C + h * Ch, 128), Ch)]
        D0T[:, pl.ds(pl.multiple_of(t * M, 128), M)] = half.T

    here_x, bx = turn_of("x")

    @pl.when(here_x)
    def _():
        lanes = lanes_of((Ch, L))

        def through(w):
            valid = 2 * lens[i * nw + bx * wb + w] - s * L
            top, end = w * Lp, (w + 1) * Lp
            v = mm_nt(eye[...], x[w])
            da = jnp.concatenate([y[0:Ch, top:end], y[Ch:, top:end]], axis=1)
            da = mm(da.astype(BF16), pick[...])
            dzw = da * gelu_slope(v * cols[0] + cols[1])
            dzw = jnp.where(lanes < valid, dzw, 0.0)
            acc[0] += dzw
            acc[1] += dzw * (v * cols[2] + cols[3])
            split[w % 2] = dzw.astype(BF16)
            for off in range(g):
                rows = pl.ds(pl.multiple_of(lax.rem(i + off, g) * cs, 16), cs)
                if off == 0:
                    gz[w] = split[w % 2, rows]
                else:
                    part[off - 1, bx * wb + w] = split[w % 2, rows]

        nh = 2 if wb % 2 == 0 and wb * Lp // 2 % 128 == 0 else 1
        n = wb // nh
        for hf in range(nh):
            rows = slice(hf * n * Lp, (hf + 1) * n * Lp)
            y[:, rows] = mm_nt(wcat[...], D3[rows])
            for w in range(hf * n, (hf + 1) * n):
                through(w)
        send(bx)

    @when(0)
    def _():
        hs = plan.H // plan.nz
        rb = plan.rb
        for u in range(2):

            def rows(j, m, u=u):
                side, r = m * rb // hs, m * rb % hs
                n = 2 * side + u
                rows = slice(j * hs + r, j * hs + r + rb)
                v = grads[rows, n * C : (n + 1) * C] if n < plan.T2 else pgrad[rows]
                return v.astype(F32)

            red.put(T1 + u, rows)
        red.step0(0)

    @when(nD - 1)
    def _():
        X5_copy(0).start()

    here_w, k = turn_of("w")

    @pl.when(here_w)
    def _():
        @pl.when(k < T1 - 1)
        def _():
            X5_copy(k + 1).start()

        X5_copy(k).wait()
        y[0:Ch, 0:C] = mm(D0T[...], X5[lax.rem(k, 2)])
        rb = plan.rb
        red.put(k, lambda j, m: y[j * cs + m * rb : j * cs + (m + 1) * rb, 0:C])

    for at, step, batch in (
        (1, red.step1, 0),
        (nD - 1, red.step2, 0),
        (turn("w", 2), red.step0, 1),
        (turn("w", 3), red.step1, 1),
        (turn("w", T1 - 1), red.step0, 2),
    ):

        @when(at)
        def _():
            step(batch)

    @when(turn("x", nD - 1))
    def _():
        packet = link[0]
        packet[...] = jnp.zeros_like(packet)
        packet[0:1, 0:Ch] = jnp.sum(acc[0].T, axis=0, keepdims=True)
        packet[1:2, 0:Ch] = jnp.sum(acc[1].T, axis=0, keepdims=True)
        peers.start(link)

    @when(last)
    def _():
        red.step1(2)
        red.step2(1)
        red.step3(0)
        red.step2(2)
        red.step3(1)
        red.step4(0)
        red.step3(2)
        red.step4(1)
        sums[...] = peers.finish(link)[:, 0:Ch]
        red.step4(2)
        for b in range(3):
            red.step5(b)
        own = pltpu.make_async_copy(red.out, summed, X5_sems.at[0])
        own.start()
        for off in range(1, g):
            done = remote(
                part.at[off - 1],
                gz_got.at[off],
                bulk_sems.at[0, off],
                bulk_sems.at[1, off],
                member(off),
            )
            done.wait_recv()
            done.wait_send()
        own.wait()


def input_grad_kernel(plan, wg, lens, x, gz, gz_got, sums, res, res_got, res_more, summed,
                      state, half_state,
                      out, out_result, conv_grad, dil_grad, point_grad,
                      g1, b1, g2, b2, g3, b3, pb, eye, cols, xt):
    t = pl.program_id(0)
    s, z, i, h = plan.place()
    L, Ch, cs = plan.L, plan.Ch, plan.cs
    turn = plan.nw // wg
    mine = pl.ds(pl.multiple_of(i * cs, 16), cs)

    @pl.when(first_step())
    def _():
        n = 2.0 * total_of(lens)
        mean, rho = norm_of(half_state[ST1 : ST1 + 2], n)
        gr = half_state[GAIN1 : GAIN1 + 1] * rho
        gg = sums[1:2] / n * rho
        for k, row in enumerate((gr, -gr * gg, gr * (mean * gg - sums[0:1] / n))):
            xt[...] = column(row, L)
            cols[k] = xt[mine]
        eye[...] = eye_matrix(cs, Ch, i * cs)

        def mine_of(src, at, which, count, *dsts):
            n = dsts[0].shape[1]
            for k in range(count):

                @pl.when(which == k)
                def _():
                    for dst, r in zip(dsts, at):
                        dst[...] = src[r : r + 1, k * n : (k + 1) * n]

        mine_of(sums, (1, 0), i, plan.g, g1, b1)
        mine_of(state, (SU2 + 1, SU2), z, plan.nz, g2, b2)
        mine_of(state, (SU3 + 1, SU3), z, plan.nz, g3, b3)
        mine_of(state, (BSUM,), z, plan.nz, pb)

    own = lax.div(t, turn) == i
    early = lax.rem(t, turn) * wg < plan.cut
    for w in range(wg):
        got = jnp.where(early, res_got[0, w].astype(F32), res_more[0, w].astype(F32))
        out_result[w] = jnp.where(own, res[0, w].astype(F32), got).astype(BF16)

    C, T1, hs, rb, wide = plan.C, plan.T1, plan.H // plan.nz, plan.rb, plan.C // 2
    count = plan.NW // wg
    turns = min(count, plan.chips)
    per, every = plan.chips // turns, count // turns

    def spread(chunk):
        for n in range(per):
            m = chunk * per + n
            side, r = m * rb // hs, m * rb % hs
            for c in range(2):
                at = slice(c * wide, (c + 1) * wide)
                for k in range(T1):
                    conv_grad[k, n * rb : (n + 1) * rb, at] = summed[k, c, n].astype(F32)
                for u in range(2):
                    v = summed[T1 + u, c, n].astype(F32)
                    if 2 * side + u < plan.T2:
                        dil_grad[2 * side + u, r : r + rb, at] = v
                    else:
                        point_grad[r : r + rb, at] = v

    for chunk in range(turns):
        pl.when(t == chunk * every)(partial(spread, chunk))

    lanes = lanes_of((cs, L))
    for w in range(wg):
        valid = 2 * lens[t * wg + w] - s * L
        v = mm_nt(eye[...], x[w])
        dz = jnp.where(own, gz[w].astype(F32), gz_got[0, w].astype(F32))
        r = cols[0] * dz + v * cols[1] + cols[2]
        out[w] = jnp.where(lanes < valid, r, 0.0).astype(BF16)


def call(kernel, plan, name, steps, ins, outs, scratch, flops, nbytes, cid=None):
    extra = {} if cid is None else dict(collective_id=cid, has_side_effects=True)
    return pl.pallas_call(
        partial(kernel, plan),
        grid=(steps,),
        in_specs=[SMEM] + [spec for spec, _ in ins],
        out_specs=[spec for spec, _, _ in outs],
        out_shape=[jax.ShapeDtypeStruct(shape, dtype) for _, shape, dtype in outs],
        scratch_shapes=scratch,
        compiler_params=pltpu.CompilerParams(vmem_limit_bytes=VMEM_LIMIT, **extra),
        cost_estimate=pl.CostEstimate(
            flops=int(flops), bytes_accessed=int(nbytes), transcendentals=0
        ),
        name=name,
    )


def per_device(
    inputs,
    lengths,
    input_gain,
    input_shift,
    conv_weight,
    branch_gain,
    branch_shift,
    dilated_tap_weight,
    mixer_gain,
    mixer_shift,
    point_weight,
    point_bias,
    cotangent,
):
    NW, L, C = inputs.shape
    Lp = L // 2
    nz = lax.axis_size("ch")
    R = 2
    plan = Plan(
        ns=lax.axis_size("seq"),
        nz=nz,
        R=R,
        NW=NW,
        L=L,
        C=C,
        H=mixer_gain.shape[0] * nz,
        T1=conv_weight.shape[0],
        T2=dilated_tap_weight.shape[0],
        wb=min(NW * R // nz, max(1, 512 // Lp)),
    )
    g, nw, cs, Ch, H, Hh, wb = plan.g, plan.nw, plan.cs, plan.Ch, plan.H, plan.Hh, plan.wb
    T1, T2, steps = plan.T1, plan.T2, plan.steps
    M = wb * Lp
    hs = H // nz
    lens = lengths.astype(jnp.int32)

    def row(a):
        return a.reshape(1, a.shape[0])

    def grp():
        return lax.rem(lax.axis_index("ch"), g)

    def half():
        return lax.div(lax.axis_index("ch"), g)

    def core():
        return lax.rem(lax.axis_index("seq"), 2)

    def chip4():
        return lax.div(lax.axis_index("seq"), plan.ns // 4)

    def whole(*shape):
        return pl.BlockSpec(shape, lambda t: (0,) * len(shape), pipeline_mode=pl.Buffered(1))

    def const(*shape):
        return pl.BlockSpec(shape, lambda t: (0,) * len(shape))

    def win(*shape):
        return pl.BlockSpec(shape, lambda t: (t,) + (0,) * (len(shape) - 1))

    def arg_win(n, width):
        return pl.BlockSpec((wb, n, width), lambda t: (grp() * steps + t, 0, 0))

    def ins(*pairs):
        return [p for p in pairs]

    share = NW // nz
    nm = max(1, share // wb)

    def edge_spec(n):
        return pl.BlockSpec(
            (nw, 16, C), lambda t: (grp(), n, 0), pipeline_mode=pl.Buffered(1)
        )

    def head_block(t):
        own = lax.div(lax.axis_index("ch") * share, wb) + t
        return jnp.where(t < nm, own, grp() * steps + t - nm), 0, 0

    def after(*shape):
        return pl.BlockSpec(
            shape, lambda t: (jnp.maximum(t - nm, 0),) + (0,) * (len(shape) - 1)
        )

    pairs = ins(
        (pl.BlockSpec((wb, L, C), head_block), inputs),
        (edge_spec(0), inputs),
        (edge_spec(L // 16 - 1), inputs),
        (edge_spec(0), cotangent),
        (edge_spec(Lp // 16 - 1), cotangent),
        (whole(1, cs), row(branch_gain)),
        (whole(1, cs), row(branch_shift)),
        (whole(1, cs), row(point_bias)),
        (whole(1, H // nz), row(mixer_gain)),
        (whole(1, H // nz), row(mixer_shift)),
        (ANY, conv_weight.reshape(T1 * C, C)),
        (whole(C), input_gain),
        (whole(C), input_shift),
        (
            pl.BlockSpec(
                (1, hs, C // 2),
                lambda t: (jnp.minimum(chip4(), T2 - 1), 0, core()),
                pipeline_mode=pl.Buffered(1),
            ),
            jnp.swapaxes(dilated_tap_weight, 1, 2),
        ),
        (
            pl.BlockSpec(
                (hs, C // 2), lambda t: (0, core()), pipeline_mode=pl.Buffered(1)
            ),
            point_weight,
        ),
    )
    plane, line, group = plane_peers(plan), line_peers(plan), group_peers(plan)
    state_shape = (STATE, C)
    edges2, edges3 = (2, nw, EDGE, C), (2, nw, EDGE, H)
    X5, x2, land2, state, beyond, full = call(
        lambda plan, *refs: head_kernel(plan, nm, *refs),
        plan,
        "head",
        nm + steps,
        pairs,
        [
            (after(M, T1 * C), (nw * Lp, T1 * C), BF16),
            (after(wb, Lp, C), (nw, Lp, C), F32),
            (ANY, edges2, BF16),
            (const(*state_shape), state_shape, F32),
            (const(2, 3, nw, C), (2, 3, nw, C), F32),
            (ANY, (2, T2 + 1, nz, hs, C // 2), BF16),
        ],
        [
            pltpu.VMEM((2, 8, C), F32),
            pltpu.VMEM((2, 3, nw, C), F32),
            pltpu.VMEM((2, 3, nw, C), F32),
            pltpu.VMEM((T1 * Lp, L), BF16),
            pltpu.VMEM(edges2, BF16),
            pltpu.VMEM((2, C), F32),
            pltpu.VMEM((T1 * C, C), BF16),
            pltpu.SemaphoreType.DMA,
            pltpu.VMEM((hs, C // 2), BF16),
            pltpu.SemaphoreType.DMA((2, 4)),
            HALO_SEMS,
            HALO_SEMS,
        ]
        + plane.scratch(2, C)
        + line.scratch(3, C)
        + group.scratch(2, C),
        2 * nw * Lp * T1 * C * C,
        nw * Lp * C * 20,
        cid=1,
    )(lens, *[a for _, a in pairs])

    full = full.reshape(2, T2 + 1, H, C // 2)
    taps_spec = whole(2, T2, H, C // 2)
    pw_spec = pl.BlockSpec(
        (2, 1, H, C // 2), lambda t: (0, T2, 0, 0), pipeline_mode=pl.Buffered(1)
    )

    def early(*shape):
        return pl.BlockSpec(
            shape, lambda t: (jnp.minimum(t, steps - 1),) + (0,) * (len(shape) - 1)
        )

    def early_land(width):
        return pl.BlockSpec(
            (2, wb, EDGE, width), lambda t: (0, jnp.minimum(t, steps - 1), 0, 0)
        )

    ahead, cut = plan.ahead, plan.cut
    rest = max(nw - cut, 1)

    def late(t):
        return jnp.maximum(t - steps, 0)

    def half_of(n):
        return pl.BlockSpec((n, Ch), lambda t: (0, half()), pipeline_mode=pl.Buffered(1))

    cot_spec = pl.BlockSpec(
        (wb, Lp, C), lambda t: (grp() * steps + jnp.minimum(t, steps - 1), 0, 0)
    )

    pairs = ins(
        (early(wb, Lp, C), x2),
        (early_land(C), land2),
        (taps_spec, full),
        (whole(*state_shape), state),
    )
    Y3, c2, land3, state = call(
        dilated_kernel,
        plan,
        "dilated",
        steps,
        pairs,
        [
            (win(M, T2 * C), (nw * Lp, T2 * C), BF16),
            (win(wb, Lp, H), (nw, Lp, H), F32),
            (ANY, edges3, BF16),
            (const(*state_shape), state_shape, F32),
        ],
        [
            pltpu.VMEM((wb, Lp + 2 * EDGE, C), F32),
            pltpu.VMEM((H, T2 * C), BF16),
            pltpu.VMEM(edges3, BF16),
            pltpu.VMEM((1, 2 * H), F32),
            HALO_SEMS,
        ]
        + group.scratch(1, 2 * H),
        2 * nw * Lp * T2 * C * H,
        nw * Lp * C * 12,
        cid=3,
    )(lens, *[a for _, a in pairs])

    pairs = ins(
        (early(wb, Lp, H), c2),
        (
            pl.BlockSpec(
                (wb, Lp, Ch),
                lambda t: (
                    jnp.where(t < steps, jnp.minimum(t, ahead - 1), late(t) + ahead),
                    0,
                    half(),
                ),
            ),
            x2,
        ),
        (cot_spec, cotangent),
        (pw_spec, full),
        (whole(*state_shape), state),
        (half_of(STATE), state),
    )
    res, dz3, pgrad, dland3, state, res_got = call(
        point_kernel,
        plan,
        "point",
        2 * steps - ahead,
        pairs,
        [
            (const(g, nw, cs, Lp), (g, nw, cs, Lp), BF16),
            (early(wb, Lp, H), (nw, Lp, H), F32),
            (const(Hh, C), (Hh, C), BF16),
            (ANY, edges3, BF16),
            (const(*state_shape), state_shape, F32),
            (ANY, (g, cut, cs, Lp), BF16),
        ],
        [
            pltpu.VMEM((H, C), BF16),
            pltpu.VMEM((nw * Lp, H), BF16),
            pltpu.VMEM((H, nw * Lp), BF16),
            pltpu.VMEM((nw * Lp, C), BF16),
            pltpu.VMEM(edges3, BF16),
            pltpu.VMEM((2, C), F32),
            HALO_SEMS,
            pltpu.SemaphoreType.DMA((2, g)),
        ]
        + group.scratch(2, C),
        5 * nw * Lp * C * H,
        nw * Lp * C * 10,
        cid=4,
    )(lens, *[a for _, a in pairs])

    pairs = ins(
        (early(wb, Lp, H), c2),
        (early_land(H), land3),
        (early(wb, Lp, H), dz3),
        (early_land(H), dland3),
        (early(wb, Lp, C), x2),
        (pl.BlockSpec((nw * Lp, C), lambda t: (0, late(t))), Y3),
        (taps_spec, full),
        (whole(*state_shape), state),
        (ANY, res),
    )
    dz2, grads, dland2, state, res_more = call(
        dilated_back_kernel,
        plan,
        "dilated_back",
        steps + T2,
        pairs,
        [
            (early(wb, Lp, C), (nw, Lp, C), F32),
            (pl.BlockSpec((Hh, C), lambda t: (0, late(t))), (Hh, T2 * C), BF16),
            (ANY, (2, nw, C), F32),
            (const(*state_shape), state_shape, F32),
            (ANY, (g, rest, cs, Lp), BF16),
        ],
        [
            pltpu.VMEM((wb, Lp + 2 * EDGE, H), F32),
            pltpu.VMEM((M, T2 * H), BF16),
            pltpu.VMEM((T2 * H, C), BF16),
            pltpu.VMEM((H, nw * Lp), BF16),
            pltpu.VMEM((2, nw, C), F32),
            pltpu.VMEM((2, C), F32),
            pltpu.SemaphoreType.DMA((2, g)),
            HALO_SEMS,
        ]
        + group.scratch(2, C),
        4 * nw * Lp * T2 * C * H,
        nw * Lp * C * 20,
        cid=5,
    )(lens, *[a for _, a in pairs])

    chips, rb = plan.chips, plan.rb
    turns_t = tail_turns(plan)

    def x_block(t):
        block = jnp.int32(0)
        for n, (what, k) in enumerate(turns_t):
            if what == "x":
                block = jnp.where(t >= n, k, block)
        return block

    sshape = (T1 + 2, 2, chips, rb, C // 2)
    pairs = ins(
        (early(wb, Lp, C), dz2),
        (whole(2, nw, C), dland2),
        (early(wb, Lp, C), x2),
        (early_land(C), land2),
        (cot_spec, cotangent),
        (whole(2, 3, nw, C), beyond),
        (
            pl.BlockSpec(
                (wb, L, Ch), lambda t: (grp() * steps + x_block(t), 0, half())
            ),
            inputs,
        ),
        (ANY, X5),
        (
            pl.BlockSpec(
                (T1, Ch, C), lambda t: (0, half(), 0), pipeline_mode=pl.Buffered(1)
            ),
            conv_weight,
        ),
        (whole(Hh, T2 * C), grads),
        (whole(Hh, C), pgrad),
        (whole(*state_shape), state),
        (half_of(STATE), state),
    )
    gz, gz_got, sums1, summed = call(
        tail_kernel,
        plan,
        "tail",
        len(turns_t),
        pairs,
        [
            (pl.BlockSpec((wb, cs, L), lambda t: (x_block(t), 0, 0)), (nw, cs, L), BF16),
            (ANY, (g, nw, cs, L), BF16),
            (const(2, Ch), (2, Ch), F32),
            (ANY, sshape, BF16),
        ],
        [
            pltpu.VMEM((wb, Lp + 16, C), F32),
            pltpu.VMEM((M, 3 * C), BF16),
            pltpu.VMEM((Ch, nw * Lp), BF16),
            pltpu.VMEM((2 * Ch, 3 * C), BF16),
            pltpu.VMEM((L, L), BF16),
            pltpu.VMEM((Ch, Ch), BF16),
            pltpu.VMEM((4, Ch, L), F32),
            pltpu.VMEM((2 * Ch, max(M, C)), F32),
            pltpu.VMEM((g - 1, nw, cs, L), BF16),
            pltpu.VMEM((2, Ch, L), BF16),
            pltpu.VMEM((2, Ch, L), F32),
            pltpu.VMEM((2, nw * Lp, C), BF16),
            pltpu.SemaphoreType.DMA((2,)),
            pltpu.SemaphoreType.DMA((2, g)),
        ]
        + Reduction.scratch(plan, tail_batches(plan))
        + group.scratch(2, C),
        2 * nw * Lp * (6 + T1) * C * Ch,
        nw * Lp * C * 40,
        cid=6,
    )(lens, *[a for _, a in pairs])

    wg = min(2 * wb, cut)
    count = NW // wg
    turn = nw // wg
    turns = min(count, chips)

    def own_block(t):
        return jnp.where(lax.div(t, turn) == grp(), lax.rem(t, turn), 0)

    def got_slot(t):
        off = lax.rem(grp() - lax.div(t, turn) + g, g)
        return jnp.maximum(off, 1), jnp.where(off > 0, lax.rem(t, turn), 0)

    def got_part(t, first, blocks):
        slot, block = got_slot(t)
        return slot, jnp.clip(block - first, 0, blocks - 1), 0, 0

    pairs = ins(
        (pl.BlockSpec((wg, L, Ch), lambda t: (t, 0, half())), inputs),
        (pl.BlockSpec((wg, cs, L), lambda t: (own_block(t), 0, 0)), gz),
        (pl.BlockSpec((1, wg, cs, L), lambda t: got_slot(t) + (0, 0)), gz_got),
        (whole(2, Ch), sums1),
        (pl.BlockSpec((1, wg, cs, Lp), lambda t: (grp(), own_block(t), 0, 0)), res),
        (
            pl.BlockSpec((1, wg, cs, Lp), lambda t: got_part(t, 0, cut // wg)),
            res_got,
        ),
        (
            pl.BlockSpec(
                (1, wg, cs, Lp), lambda t: got_part(t, cut // wg, max((nw - cut) // wg, 1))
            ),
            res_more if nw > cut else res_got,
        ),
        (
            pl.BlockSpec(
                (T1 + 2, 2, chips // turns, rb, C // 2),
                lambda t: (0, 0, t * turns // count, 0, 0),
            ),
            summed,
        ),
        (whole(*state_shape), state),
        (half_of(STATE), state),
    )
    outs = call(
        lambda plan, *refs: input_grad_kernel(plan, wg, *refs),
        plan,
        "input_grad",
        count,
        pairs,
        [
            (win(wg, cs, L), (NW, cs, L), BF16),
            (win(wg, cs, Lp), (NW, cs, Lp), BF16),
            (
                pl.BlockSpec((T1, cs // turns, C), lambda t: (0, t * turns // count, 0)),
                (T1, cs, C),
                F32,
            ),
            (const(T2, hs, C), (T2, hs, C), F32),
            (const(hs, C), (hs, C), F32),
        ]
        + [(const(1, n), (1, n), F32) for n in (cs, cs, cs, cs, hs, hs, cs)],
        [
            pltpu.VMEM((cs, Ch), BF16),
            pltpu.VMEM((3, cs, L), F32),
            pltpu.VMEM((Ch, L), F32),
        ],
        2 * NW * L * Ch * cs,
        NW * L * cs * 8,
    )(lens, *[a for _, a in pairs])
    grad, result, conv_grad, dil_grad, point_grad = outs[:5]
    g1, b1, g2, b2, g3, b3, pb = [a[0] for a in outs[5:]]
    return (
        jnp.swapaxes(result, 1, 2),
        jnp.swapaxes(grad, 1, 2),
        jnp.swapaxes(conv_grad, 1, 2),
        g1,
        b1,
        g2,
        b2,
        jnp.swapaxes(dil_grad, 1, 2),
        g3,
        b3,
        point_grad,
        pb,
    )


def solution(mesh):
    in_specs = (
        P(None, "seq", None),
        P(),
        P(),
        P(),
        P(),
        P("ch"),
        P("ch"),
        P(None, None, "ch"),
        P("ch"),
        P("ch"),
        P("ch", None),
        P("ch"),
        P(None, "seq", None),
    )
    out_specs = (
        P(None, "seq", "ch"),
        P(None, "seq", "ch"),
        P(None, None, "ch"),
        P("ch"),
        P("ch"),
        P("ch"),
        P("ch"),
        P(None, None, "ch"),
        P("ch"),
        P("ch"),
        P("ch", None),
        P("ch"),
    )
    return jax.shard_map(
        per_device, mesh=mesh, in_specs=in_specs, out_specs=out_specs, check_vma=False
    )
```

```python
from functools import partial
from typing import NamedTuple

import jax
import jax.numpy as jnp
from jax import lax
from jax.experimental import pallas as pl
from jax.experimental.pallas import tpu as pltpu
from jax.sharding import PartitionSpec as P

DIL = 14
EDGE = 16
EPS = 1e-05
GC0 = 0.7978845608028654
GC1 = 0.044715
F32 = jnp.float32
BF16 = jnp.bfloat16
MESH = pl.DeviceIdType.MESH
VMEM_LIMIT = 58 * 1024 * 1024
ANY = pl.BlockSpec(memory_space=pl.ANY)
SMEM = pl.BlockSpec(memory_space=pltpu.SMEM)


ST1, GAIN2, SHIFT2, BIAS, GAIN3, SHIFT3, GAIN1, SHIFT1, ST2, ST3, SU3, BSUM, SU2 = (
    0, 2, 3, 4, 5, 6, 7, 8, 9, 11, 13, 15, 16
)
STATE = 24


class Plan(NamedTuple):
    ns: int
    nz: int
    R: int
    NW: int
    L: int
    C: int
    H: int
    T1: int
    T2: int
    wb: int

    @property
    def g(self):
        return self.nz // self.R

    @property
    def nw(self):
        return self.NW // self.g

    @property
    def Lp(self):
        return self.L // 2

    @property
    def cs(self):
        return self.C // self.nz

    @property
    def Ch(self):
        return self.C // self.R

    @property
    def Hh(self):
        return self.H // self.R

    @property
    def steps(self):
        return self.nw // self.wb

    @property
    def res_parts(self):
        return max(1, self.steps // 2)

    @property
    def chips(self):
        return self.ns // 2

    @property
    def cut(self):
        return self.res_parts * self.wb

    @property
    def rb(self):
        return self.cs // self.chips

    def place(self):
        s, z = lax.axis_index("seq"), lax.axis_index("ch")
        return s, z, lax.rem(z, self.g), lax.div(z, self.g)


def gelu(z):
    t = jnp.tanh(z * (GC0 + (GC0 * GC1) * (z * z)))
    return z * (0.5 + 0.5 * t)


def gelu_both(z):
    sq = z * z
    t = jnp.tanh(z * (GC0 + (GC0 * GC1) * sq))
    h = 0.5 + 0.5 * t
    v = z * h
    return v, h + v * (1.0 - t) * (GC0 + (3.0 * GC0 * GC1) * sq)


def gelu_slope(z):
    return gelu_both(z)[1]


def fold(v):
    return jnp.sum(v.reshape(v.shape[0] // 8, 8, v.shape[1]), axis=0)


def unfold(v):
    return jnp.sum(v, axis=0, keepdims=True)


def rows_of(shape):
    return lax.broadcasted_iota(jnp.int32, shape, 0)


def lanes_of(shape):
    return lax.broadcasted_iota(jnp.int32, shape, 1)


def total_of(lens):
    n = lens[0]
    for k in range(1, lens.shape[0]):
        n = n + lens[k]
    return n.astype(F32)


def norm_of(stats, total):
    mean = stats[0:1] / total
    square = stats[1:2] / total
    return mean, lax.rsqrt(square - mean * mean + EPS)


def flat(ref):
    return ref[...].reshape(1, ref.shape[0])


def column(row, n):
    return jnp.broadcast_to(row, (n, row.shape[1])).T


def mm(a, b):
    return jnp.dot(a, b, preferred_element_type=F32)


def mm_nt(a, b):
    return lax.dot_general(a, b, (((1,), (1,)), ((), ())), preferred_element_type=F32)


def mm_tn(a, b):
    return lax.dot_general(a, b, (((0,), (0,)), ((), ())), preferred_element_type=F32)


def mm_tt(a, b):
    return lax.dot_general(a, b, (((0,), (1,)), ((), ())), preferred_element_type=F32)


def eye_matrix(n, m, first):
    return jnp.where(lanes_of((n, m)) == rows_of((n, m)) + first, 1.0, 0.0).astype(BF16)


def pick_matrix(L):
    r, n = rows_of((L, L)), lanes_of((L, L))
    bin_of = 2 * r - jnp.where(r >= L // 2, L - 1, 0)
    return jnp.where(n == bin_of, 1.0, 0.0).astype(BF16)


def remote(src, dst, send, recv, device):
    return pltpu.make_async_remote_copy(
        src_ref=src,
        dst_ref=dst,
        send_sem=send,
        recv_sem=recv,
        device_id=device,
        device_id_type=MESH,
    )


def wrap(v, n):
    return jnp.where(v >= n, v - n, v)


def greet(devices):
    barrier = pltpu.get_barrier_semaphore()
    for device in devices:
        pl.semaphore_signal(barrier, inc=1, device_id=device, device_id_type=MESH)


def meet(devices):
    pl.semaphore_wait(pltpu.get_barrier_semaphore(), len(devices))


class Peers:
    def __init__(self, me, others):
        self.me, self.others = me, others
        self.count = len(others) + 1

    def start(self, link):
        packet, buf, sems = link
        for device in self.others:
            remote(packet, buf.at[self.me], sems.at[0], sems.at[1], device).start()

    def finish(self, link):
        packet, buf, sems = link
        buf[self.me] = packet[...]
        rest = buf.at[pl.ds(0, self.count - 1)]
        done = remote(rest, rest, sems.at[0], sems.at[1], self.others[0])
        done.wait_recv()
        acc = buf[0]
        for q in range(1, self.count):
            acc = acc + buf[q]
        done.wait_send()
        return acc

    def scratch(self, rows, width):
        return [
            pltpu.VMEM((rows, width), F32),
            pltpu.VMEM((self.count, rows, width), F32),
            pltpu.SemaphoreType.DMA((2,)),
        ]


def group_peers(plan):
    s, z, i, h = plan.place()
    g = plan.g
    others = [
        (wrap(s + a, plan.ns), h * g + wrap(i + b, g))
        for a in range(plan.ns)
        for b in range(g)
        if a or b
    ]
    return Peers(s * g + i, others)


def plane_peers(plan):
    s, z, i, h = plan.place()
    return Peers(s, [(wrap(s + a, plan.ns), z) for a in range(1, plan.ns)])


def line_peers(plan):
    s, z, i, h = plan.place()
    return Peers(z, [(s, wrap(z + a, plan.nz)) for a in range(1, plan.nz)])


class Halo:
    def __init__(self, plan, edge, land, sems):
        self.edge, self.land, self.sems = edge, land, sems
        s, z, _, _ = plan.place()
        self.to = ((wrap(s + plan.ns - 1, plan.ns), z), (wrap(s + 1, plan.ns), z))

    def copy(self, side, rows):
        return remote(
            self.edge.at[side, rows],
            self.land.at[1 - side, rows],
            self.sems.at[0, side],
            self.sems.at[1, side],
            self.to[side],
        )

    def start(self, first, count):
        for side in range(2):
            self.copy(side, pl.ds(first, count)).start()

    def finish(self):
        for side in range(2):
            done = self.copy(side, pl.ds(0, self.land.shape[1]))
            done.wait_recv()
            done.wait_send()


HALO_SEMS = pltpu.SemaphoreType.DMA((2, 2))


class Gather:
    def __init__(self, plan, part, full, sems):
        self.plan, self.part, self.full, self.sems = plan, part, full, sems
        self.s, self.z, self.i, self.h = plan.place()
        self.c, self.m = lax.rem(self.s, 2), lax.div(self.s, 2)
        self.chips = plan.chips
        self.every = self.chips // 4
        self.tap = lax.div(self.m, self.every)
        self.owner = lax.rem(self.m, self.every) == 0
        self.mine = full.at[self.c, self.tap]

    def others(self):
        g, nz = self.plan.g, self.plan.nz
        return [(self.s, wrap(self.h * g + g + r, nz)) for r in range(nz - g)]

    def far(self, off):
        return (2 * wrap(self.m + off, self.chips) + self.c, self.z)

    def own(self):
        return pltpu.make_async_copy(self.part, self.mine.at[self.z], self.sems.at[0, 0])

    def line(self, off):
        device = (self.s, wrap(self.z + off, self.plan.nz))
        return remote(
            self.part, self.mine.at[self.z], self.sems.at[0, 1], self.sems.at[1, 1], device
        )

    def chip(self, off):
        return remote(self.mine, self.mine, self.sems.at[0, 2], self.sems.at[1, 2], self.far(off))

    def pair(self):
        half = self.full.at[self.c]
        device = (2 * self.m + 1 - self.c, self.z)
        return remote(half, half, self.sems.at[0, 3], self.sems.at[1, 3], device)

    def line_start(self):
        @pl.when(self.owner)
        def _():
            self.own().start()
            for off in range(1, self.plan.nz):
                self.line(off).start()

    def line_finish(self):
        @pl.when(self.owner)
        def _():
            self.own().wait()
            rest = self.mine.at[pl.ds(0, self.plan.nz - 1)]
            device = (self.s, wrap(self.z + 1, self.plan.nz))
            done = remote(rest, rest, self.sems.at[0, 1], self.sems.at[1, 1], device)
            done.wait_recv()
            done.wait_send()

    def chips_start(self):
        @pl.when(self.owner)
        def _():
            for off in range(1, self.chips):
                self.chip(off).start()

    def pair_start(self):
        def taken(count):
            rest = self.full.at[self.c, pl.ds(0, count)]
            return remote(rest, rest, self.sems.at[0, 2], self.sems.at[1, 2], self.far(1))

        @pl.when(self.owner)
        def _():
            taken(3).wait_recv()
            for off in range(1, self.chips):
                self.chip(off).wait_send()

        if self.every > 1:

            @pl.when(jnp.logical_not(self.owner))
            def _():
                taken(4).wait_recv()

        self.pair().start()

    def pair_finish(self):
        done = self.pair()
        done.wait_recv()
        done.wait_send()


def first_step():
    return pl.program_id(0) == 0


def last_step():
    return pl.program_id(0) == pl.num_programs(0) - 1


def keep_state(old, new):
    new[...] = old[...]


def head_kernel(plan, nm, lens, x, xtop, xend, ctop, cend, g2, s2, pb, g3, s3,
                w_hbm, gain, shift, taps, pw,
                X5, x2, land, state, beyond_out, full,
                macc, beyond, xedge, sel, edge, acc, w_ref, w_sem, part,
                gather_sems, xhalo_sems, halo_sems, *links):
    t = pl.program_id(0)
    peers, plane, line = group_peers(plan), plane_peers(plan), line_peers(plan)
    xhalo = Halo(plan, xedge, beyond, xhalo_sems)
    halo = Halo(plan, edge, land, halo_sems)
    gather = Gather(plan, part, full, gather_sems)
    w_copy = pltpu.make_async_copy(w_hbm, w_ref, w_sem)
    plane_link, line_link, link = links[:3], links[3:6], links[6:]
    s, z, i, h = plan.place()
    L, Lp, C, nw, nz, wb = plan.L, plan.Lp, plan.C, plan.nw, plan.nz, plan.wb
    share = plan.NW // nz
    c = t - nm
    everyone = peers.others + gather.others()

    @pl.when(first_step())
    def _():
        w_copy.start()
        greet(everyone)
        part[...] = jnp.where(gather.tap == 3, pw[...], taps[0])
        macc[...] = jnp.zeros_like(macc)
        acc[...] = jnp.zeros_like(acc)
        state[...] = jnp.zeros_like(state)
        state[GAIN1 : GAIN1 + 1] = flat(gain)
        state[SHIFT1 : SHIFT1 + 1] = flat(shift)
        n16 = nw * 16
        for side, (xe, ce, places) in enumerate(
            ((xtop, ctop, (0, 1, 0)), (xend, cend, (14, 15, 15)))
        ):
            for k, at in enumerate(places):
                rows, lanes = rows_of((nw, n16)), lanes_of((nw, n16))
                one = jnp.where(lanes == 16 * rows + at, 1.0, 0.0).astype(BF16)
                block = (xe if k < 2 else ce)[...].reshape(n16, C)
                xedge[side, k] = mm(one, block)
        shape = (Lp, L)
        for k in range(plan.T1):
            at = lanes_of(shape) - (2 * rows_of(shape) + (k - 2))
            sel[k * Lp : (k + 1) * Lp] = jnp.where((at == 0) | (at == 1), 1.0, 0.0).astype(BF16)

    @pl.when(c < 0)
    def _():
        rows = rows_of((L, C))
        for w in range(min(share, wb)):
            at = lax.rem(z * share, wb) + w
            valid = 2 * lens[z * share + t * wb + w] - s * L
            v = jnp.where(rows < valid, x[at].astype(F32), 0.0)
            macc[0] += fold(v)
            macc[1] += fold(v * v)

    @pl.when(c == -1)
    def _():
        packet, more = plane_link[0], line_link[0]
        packet[0:1] = unfold(macc[0])
        packet[1:2] = unfold(macc[1])
        meet(everyone)
        plane.start(plane_link)
        xhalo.start(0, 3)
        at = 0
        spans = []
        more[2:3] = jnp.zeros((1, C), F32)
        for ref in (g2, s2, pb, g3, s3):
            n = ref.shape[1]
            more[2:3, at : at + n] = ref[...]
            spans.append((at, n))
            at += n
        more[0:2] = plane.finish(plane_link)
        line.start(line_link)
        gather.line_start()
        state[ST1 : ST1 + 2] = line.finish(line_link)[0:2]
        for k in range(nz):
            row = line_link[1][k]
            for r, (at, n) in zip((GAIN2, SHIFT2, BIAS, GAIN3, SHIFT3), spans):
                state[r : r + 1, k * n : (k + 1) * n] = row[2:3, at : at + n]
        xhalo.finish()
        beyond_out[...] = beyond[...]
        w_copy.wait()

    @pl.when(c >= 0)
    def _():
        mean, rho = norm_of(state[ST1 : ST1 + 2], 2.0 * total_of(lens))
        scale = state[GAIN1 : GAIN1 + 1] * rho
        offset = state[SHIFT1 : SHIFT1 + 1] - mean * scale
        rows = rows_of((L, C))
        row1 = rows_of((1, C))
        row16 = rows_of((16, C))
        def activate(w):
            at = c * wb + w
            valid = 2 * lens[i * nw + at] - s * L
            a = gelu(x[w].astype(F32) * scale + offset)
            a = jnp.where(rows < valid, a, 0.0).astype(BF16)
            picked = mm(sel[...], a)
            for k in range(5):
                X5[w * Lp : (w + 1) * Lp, k * C : (k + 1) * C] = picked[
                    k * Lp : (k + 1) * Lp
                ].astype(BF16)

            def beside(side, k, bin_at):
                a = gelu(beyond[side, k, pl.ds(at, 1), :] * scale + offset)
                here = (row1 + bin_at < valid) & (row1 + (s * L + bin_at) >= 0)
                return jnp.where(here, a, 0.0).astype(BF16).astype(F32)

            l0, l1 = beside(0, 0, -2), beside(0, 1, -1)
            r0, r1 = beside(1, 0, L), beside(1, 1, L + 1)
            top, end = w * Lp, (w + 1) * Lp
            for k, add in ((0, l0 + l1), (1, l1)):
                X5[top : top + 16, k * C : (k + 1) * C] = (
                    picked[k * Lp : k * Lp + 16] + jnp.where(row16 == 0, add, 0.0)
                ).astype(BF16)
            for k, add in ((3, r0), (4, r0 + r1)):
                X5[end - 16 : end, k * C : (k + 1) * C] = (
                    picked[(k + 1) * Lp - 16 : (k + 1) * Lp] + jnp.where(row16 == 15, add, 0.0)
                ).astype(BF16)

        nc = 256
        rowp = rows_of((Lp, nc))

        def convolve(first, count):
            span = slice(first * Lp, (first + count) * Lp)
            for n in range(C // nc):
                cols = slice(n * nc, (n + 1) * nc)
                y = 0.5 * mm(X5[span], w_ref[:, cols])
                s0 = jnp.zeros((8, nc), F32)
                s1 = jnp.zeros((8, nc), F32)
                for w in range(first, first + count):
                    at = c * wb + w
                    valid = lens[i * nw + at] - s * Lp
                    v = y[(w - first) * Lp : (w - first + 1) * Lp]
                    x2[w, :, cols] = v
                    edge[0, at, :, cols] = v[:EDGE].astype(BF16)
                    edge[1, at, :, cols] = v[Lp - EDGE :].astype(BF16)
                    v = jnp.where(rowp < valid, v, 0.0)
                    s0 = s0 + fold(v)
                    s1 = s1 + fold(v * v)
                acc[0:1, cols] += unfold(s0)
                acc[1:2, cols] += unfold(s1)

        count = max(1, wb // 2)
        for first in range(0, wb, count):
            for w in range(first, first + count):
                activate(w)
            convolve(first, count)
        halo.start(c * wb, wb)

    @pl.when(c == 0)
    def _():
        gather.line_finish()
        gather.chips_start()

    @pl.when(last_step())
    def _():
        link[0][...] = acc[...]
        peers.start(link)
        gather.pair_start()
        state[ST2 : ST2 + 2] = peers.finish(link)
        halo.finish()
        gather.pair_finish()


def dilated_kernel(plan, lens, x2, x2land, w_ref, old,
                   Y3, c2, land, state, ext, wf, edge, acc, halo_sems, *link):
    t = pl.program_id(0)
    peers = group_peers(plan)
    halo = Halo(plan, edge, land, halo_sems)
    s, z, i, h = plan.place()
    Lp, C, H, wb = plan.Lp, plan.C, plan.H, plan.wb

    @pl.when(first_step())
    def _():
        greet(peers.others)
        acc[...] = jnp.zeros_like(acc)
        for k in range(plan.T2):
            for c in range(2):
                at = k * C + c * (C // 2)
                wf[:, at : at + C // 2] = w_ref[c, k]

    mean, rho = norm_of(old[ST2 : ST2 + 2], total_of(lens))
    scale = old[GAIN2 : GAIN2 + 1] * rho
    offset = old[SHIFT2 : SHIFT2 + 1] - mean * scale
    rows = rows_of((Lp, C))
    rowe = rows_of((EDGE, C))

    rowh = rows_of((Lp, H))
    sums0, sums1 = jnp.zeros((8, H), F32), jnp.zeros((8, H), F32)
    nh = min(2, wb)
    for first in range(0, wb, wb // nh):
        span = range(first, first + wb // nh)
        for w in span:
            valid = lens[i * plan.nw + t * wb + w] - s * Lp
            a = jnp.where(rows < valid, gelu(x2[w] * scale + offset), 0.0)
            al = gelu(x2land[0, w].astype(F32) * scale + offset)
            al = jnp.where((rowe - EDGE < valid) & (s > 0), al, 0.0)
            ah = gelu(x2land[1, w].astype(F32) * scale + offset)
            ah = jnp.where(rowe + Lp < valid, ah, 0.0)
            ext[w, 0:EDGE] = al
            ext[w, EDGE : EDGE + Lp] = a
            ext[w, EDGE + Lp :] = ah
            top, end = w * Lp, (w + 1) * Lp
            Y3[top:end, 0:C] = ext[w, EDGE - DIL : EDGE - DIL + Lp].astype(BF16)
            Y3[top:end, C : 2 * C] = a.astype(BF16)
            Y3[top:end, 2 * C : 3 * C] = ext[w, EDGE + DIL : EDGE + DIL + Lp].astype(BF16)
        y = mm_nt(Y3[first * Lp : (first + wb // nh) * Lp], wf[...])
        for w in span:
            at = t * wb + w
            valid = lens[i * plan.nw + at] - s * Lp
            v = y[(w - first) * Lp : (w - first + 1) * Lp]
            c2[w] = v
            edge[0, at] = v[:EDGE].astype(BF16)
            edge[1, at] = v[Lp - EDGE :].astype(BF16)
            v = jnp.where(rowh < valid, v, 0.0)
            sums0 = sums0 + fold(v)
            sums1 = sums1 + fold(v * v)
    acc[0:1, 0:H] += unfold(sums0)
    acc[0:1, H:] += unfold(sums1)

    @pl.when(first_step())
    def _():
        meet(peers.others)

    halo.start(t * wb, wb)

    @pl.when(last_step())
    def _():
        link[0][...] = acc[...]
        peers.start(link)
        keep_state(old, state)
        got = peers.finish(link)
        state[ST3 : ST3 + 1, 0:H] = got[:, 0:H]
        state[ST3 + 1 : ST3 + 2, 0:H] = got[:, H:]
        halo.finish()


def point_kernel(plan, lens, c2, x2, cot, w_ref, old, half_state,
                 res, dz, pgrad, land, state,
                 pw, a3s, a3T, dos, edge, acc, halo_sems, *link):
    t = pl.program_id(0)
    peers = group_peers(plan)
    halo = Halo(plan, edge, land, halo_sems)
    s, z, i, h = plan.place()
    Lp, C, H, wb, cs = plan.Lp, plan.C, plan.H, plan.wb, plan.cs
    M = wb * Lp

    @pl.when(first_step())
    def _():
        greet(peers.others)
        acc[...] = jnp.zeros_like(acc)
        for c in range(2):
            pw[:, c * (C // 2) : (c + 1) * (C // 2)] = w_ref[c, 0]

    @pl.when(t < plan.steps)
    def _():
        mean, rho = norm_of(old[ST3 : ST3 + 2, 0:H], total_of(lens))
        scale = old[GAIN3 : GAIN3 + 1, 0:H] * rho
        offset = old[SHIFT3 : SHIFT3 + 1, 0:H] - mean * scale
        shift = -mean * rho
        rowc = rows_of((Lp, C))
        rowh = rows_of((Lp, H))
        block = pl.ds(pl.multiple_of(t * M, 128), M)
        bias = jnp.zeros((8, C), F32)
        parts = []
        for w in range(wb):
            valid = lens[i * plan.nw + t * wb + w] - s * Lp
            d = jnp.where(rowc < valid, cot[w].astype(F32), 0.0)
            bias = bias + fold(d)
            parts.append(d.astype(BF16))
        d = jnp.concatenate(parts, axis=0)
        dos[block] = d
        da = mm_nt(d, pw[...])
        s0, s1 = jnp.zeros((8, H), F32), jnp.zeros((8, H), F32)
        parts = []
        for w in range(wb):
            at = t * wb + w
            valid = lens[i * plan.nw + at] - s * Lp
            top, end = w * Lp, (w + 1) * Lp
            v = c2[w]
            act, slope = gelu_both(v * scale + offset)
            parts.append(jnp.where(rowh < valid, act, 0.0).astype(BF16))
            dzw = da[top:end] * slope
            dz[w] = dzw
            edge[0, at] = dzw[:EDGE].astype(BF16)
            edge[1, at] = dzw[Lp - EDGE :].astype(BF16)
            s0 = s0 + fold(dzw)
            s1 = s1 + fold(dzw * (v * rho + shift))
        a3 = jnp.concatenate(parts, axis=0)
        a3s[block] = a3
        a3T[:, block] = a3.T
        acc[0:1, 0:H] += unfold(s0)
        acc[0:1, H : 2 * H] += unfold(s1)
        acc[1:2] += unfold(bias)

    @pl.when(first_step())
    def _():
        meet(peers.others)

    @pl.when(t < plan.steps)
    def _():
        halo.start(t * wb, wb)

    @pl.when(t == plan.steps - 1)
    def _():
        link[0][...] = acc[...]
        peers.start(link)

    @pl.when(t >= plan.steps)
    def _():
        u = t - plan.steps
        n = plan.nw // 2
        y = mm(a3s[pl.ds(pl.multiple_of(u * n * Lp, 128), n * Lp)], w_ref[h, 0])
        rowr = rows_of((Lp, y.shape[1]))
        for w in range(n):
            valid = lens[i * plan.nw + u * n + w] - s * Lp
            r = x2[w] + y[w * Lp : (w + 1) * Lp] + half_state[BIAS : BIAS + 1]
            r = jnp.where(rowr < valid, r, 0.0).astype(BF16).T
            for k in range(plan.g):
                res[k, w] = r[k * cs : (k + 1) * cs]

    @pl.when(last_step())
    def _():
        rows = pl.ds(pl.multiple_of(h * plan.Hh, 16), plan.Hh)
        pgrad[...] = mm(a3T[rows], dos[...]).astype(BF16)
        keep_state(old, state)
        got = peers.finish(link)
        state[SU3 : SU3 + 1, 0:H] = got[0:1, 0:H]
        state[SU3 + 1 : SU3 + 2, 0:H] = got[0:1, H : 2 * H]
        state[BSUM : BSUM + 1] = got[1:2]
        halo.finish()


def dilated_back_kernel(plan, lens, c2, cland, dz3, dland, x2, Y3, w_ref, old, res,
                        dz2, grads, land, state, res_got,
                        ext, Z3, wt, dcT, edge, acc, bulk_sems, halo_sems, *link):
    t = pl.program_id(0)
    peers = group_peers(plan)
    halo = Halo(plan, edge, land, halo_sems)
    s, z, i, h = plan.place()
    Lp, C, H, wb, nw, g = plan.Lp, plan.C, plan.H, plan.wb, plan.nw, plan.g

    def bulk(off):
        to = wrap(i + off, g)
        rows = pl.ds(0, plan.cut)
        return remote(
            res.at[to, rows],
            res_got.at[off, rows],
            bulk_sems.at[0, off],
            bulk_sems.at[1, off],
            (s, h * g + to),
        )

    @pl.when(first_step())
    def _():
        greet(peers.others)
        acc[...] = jnp.zeros_like(acc)
        for k in range(plan.T2):
            for c in range(2):
                cols = slice(c * (C // 2), (c + 1) * (C // 2))
                wt[k * H : (k + 1) * H, cols] = w_ref[c, k]
        meet(peers.others)
        for off in range(1, g):
            bulk(off).start()

    @pl.when(t < plan.steps)
    def _():
        total = total_of(lens)
        mean3, rho3 = norm_of(old[ST3 : ST3 + 2, 0:H], total)
        gr3 = old[GAIN3 : GAIN3 + 1, 0:H] * rho3
        sg3 = old[SU3 : SU3 + 1, 0:H] / total
        gg3 = old[SU3 + 1 : SU3 + 2, 0:H] / total
        mean2, rho2 = norm_of(old[ST2 : ST2 + 2], total)
        scale2 = old[GAIN2 : GAIN2 + 1] * rho2
        offset2 = old[SHIFT2 : SHIFT2 + 1] - mean2 * scale2
        rowh = rows_of((Lp, H))
        rowe = rows_of((EDGE, H))
        rowc = rows_of((Lp, C))

        by_v = -gr3 * rho3 * gg3
        by_1 = gr3 * (mean3 * rho3 * gg3 - sg3)
        shift2 = -mean2 * rho2

        def back(dz, v):
            return gr3 * dz + by_v * v + by_1

        for w in range(wb):
            valid = lens[i * nw + t * wb + w] - s * Lp
            d = jnp.where(rowh < valid, back(dz3[w], c2[w]), 0.0)
            dl = back(dland[0, w].astype(F32), cland[0, w].astype(F32))
            dl = jnp.where((rowe - EDGE < valid) & (s > 0), dl, 0.0)
            dh = back(dland[1, w].astype(F32), cland[1, w].astype(F32))
            dh = jnp.where(rowe + Lp < valid, dh, 0.0)
            ext[w, 0:EDGE] = dl
            ext[w, EDGE : EDGE + Lp] = d
            ext[w, EDGE + Lp :] = dh
            top, end = w * Lp, (w + 1) * Lp
            Z3[top:end, 0:H] = ext[w, EDGE + DIL : EDGE + DIL + Lp].astype(BF16)
            Z3[top:end, H : 2 * H] = d.astype(BF16)
            Z3[top:end, 2 * H : 3 * H] = ext[w, EDGE - DIL : EDGE - DIL + Lp].astype(BF16)

        y = mm(Z3[...], wt[...])

        M = wb * Lp
        dcT[:, pl.ds(pl.multiple_of(t * M, 128), M)] = Z3[:, H : 2 * H].T
        s0, s1 = jnp.zeros((8, C), F32), jnp.zeros((8, C), F32)
        for w in range(wb):
            at = t * wb + w
            valid = lens[i * nw + at] - s * Lp
            v = x2[w]
            dzw = y[w * Lp : (w + 1) * Lp] * gelu_slope(v * scale2 + offset2)
            dzw = jnp.where(rowc < valid, dzw, 0.0)
            dz2[w] = dzw
            edge[0, pl.ds(at, 1)] = dzw[0:1]
            edge[1, pl.ds(at, 1)] = dzw[Lp - 1 : Lp]
            s0 = s0 + fold(dzw)
            s1 = s1 + fold(dzw * (v * rho2 + shift2))
        acc[0:1] += unfold(s0)
        acc[1:2] += unfold(s1)

    @pl.when(t == plan.steps - 1)
    def _():
        link[0][...] = acc[...]
        peers.start(link)
        halo.start(0, nw)

    @pl.when(t >= plan.steps)
    def _():
        rows = pl.ds(pl.multiple_of(h * plan.Hh, 16), plan.Hh)
        grads[...] = mm(dcT[rows], Y3[...]).astype(BF16)

    @pl.when(last_step())
    def _():
        keep_state(old, state)
        state[SU2 : SU2 + 2] = peers.finish(link)
        halo.finish()
        for off in range(1, g):
            bulk(off).wait()


class Reduction:
    def __init__(self, plan, batches, out, give, mine, got, spread, half, mate, sems):
        self.plan, self.batches, self.out = plan, batches, out
        self.give, self.mine, self.got, self.spread = give, mine, got, spread
        self.half, self.mate = half, mate
        self.sems = sems
        self.s, self.z, self.i, self.h = plan.place()
        self.c = lax.rem(self.s, 2)
        self.m = lax.div(self.s, 2)
        self.chips = plan.chips

    @staticmethod
    def scratch(plan, batches):
        taps, wide = plan.T1 + 2, plan.C // 2
        full = (taps, plan.chips, plan.g, plan.rb, wide)
        part = (taps, plan.g, plan.rb, wide)
        return [
            pltpu.VMEM((taps, 2, plan.chips, plan.rb, wide), BF16),
            *[pltpu.VMEM(full, BF16)] * 4,
            *[pltpu.VMEM(part, BF16)] * 2,
            pltpu.SemaphoreType.DMA((2, len(batches), 5)),
        ]

    def copy(self, b, phase, src, dst, device):
        return remote(src, dst, self.sems.at[0, b, phase], self.sems.at[1, b, phase], device)

    def finish(self, b, phase, ref, device):
        done = self.copy(b, phase, ref, ref, device)
        done.wait_recv()
        done.wait_send()

    def taps(self, b):
        return pl.ds(*self.batches[b])

    def pair(self):
        return (2 * self.m + (1 - self.c), self.z)

    def far(self, off):
        return (2 * wrap(self.m + off, self.chips) + self.c, self.z)

    def member(self, off):
        return (self.s, self.h * self.plan.g + wrap(self.i + off, self.plan.g))

    def put(self, k, rows):
        wide = self.plan.C // 2
        for j in range(self.plan.g):
            for m in range(self.chips):
                v = rows(j, m)
                left, right = v[:, :wide], v[:, wide:]
                self.mine[k, m, j] = jnp.where(self.c == 0, left, right).astype(BF16)
                self.give[k, m, j] = jnp.where(self.c == 0, right, left).astype(BF16)

    def step0(self, b):
        taps = self.taps(b)
        self.copy(b, 0, self.give.at[taps], self.got.at[taps], self.pair()).start()

    def step1(self, b):
        taps = self.taps(b)
        self.finish(b, 0, self.got.at[taps], self.pair())
        first, count = self.batches[b]
        for k in range(first, first + count):
            v = self.mine[k].astype(F32) + self.got[k].astype(F32)
            self.mine[k] = v.astype(BF16)
        for off in range(1, self.chips):
            src = self.mine.at[taps, wrap(self.m + off, self.chips)]
            self.copy(b, 1, src, self.spread.at[taps, self.m], self.far(off)).start()

    def step2(self, b):
        taps = self.taps(b)
        self.finish(b, 1, self.spread.at[taps, pl.ds(0, self.chips - 1)], self.far(1))
        first, count = self.batches[b]
        for k in range(first, first + count):
            self.spread[k, self.m] = self.mine[k, self.m]
            v = self.spread[k, 0].astype(F32)
            for n in range(1, self.chips):
                v = v + self.spread[k, n].astype(F32)
            self.half[k] = v.astype(BF16)
        for off in range(1, self.plan.g):
            src = self.half.at[taps, wrap(self.i + off, self.plan.g)]
            self.copy(b, 2, src, self.mate.at[taps, off], self.member(off)).start()

    def step3(self, b):
        taps = self.taps(b)
        self.finish(b, 2, self.mate.at[taps, pl.ds(1, self.plan.g - 1)], self.member(1))
        first, count = self.batches[b]
        for k in range(first, first + count):
            v = self.half[k, self.i].astype(F32)
            for off in range(1, self.plan.g):
                v = v + self.mate[k, off].astype(F32)
            self.out[k, self.c, self.m] = v.astype(BF16)
        mine = self.out.at[taps, self.c, self.m]
        for off in range(1, self.chips):
            self.copy(b, 3, mine, mine, self.far(off)).start()

    def step4(self, b):
        taps = self.taps(b)
        self.finish(b, 3, self.out.at[taps, self.c, pl.ds(0, self.chips - 1)], self.far(1))
        mine = self.out.at[taps, self.c]
        self.copy(b, 4, mine, mine, self.pair()).start()

    def step5(self, b):
        self.finish(b, 4, self.out.at[self.taps(b), self.c], self.pair())


def tail_turns(plan):
    nD = plan.steps
    first = (nD + 1) // 2
    turns = [("x", n) for n in range(first)] + [("d", n) for n in range(first, nD)]
    turns += [("w", n) for n in range(plan.T1)]
    return turns + [("x", n) for n in range(first, nD)]


def tail_batches(plan):
    return [(plan.T1, 2), (0, 3), (3, plan.T1 - 3)]


def tail_kernel(plan, lens, dz2, dzland, x2, x2land, cot, beyond, x, X5_hbm, taps, grads, pgrad,
                old, half_state, res,
                gz, gz_got, sums, summed, res_got,
                ext, D3, D0T, wcat, pick, eye, cols, y, part, split, acc, X5, X5_sems,
                bulk_sems, res_sems, *rest):
    t = pl.program_id(0)
    s, z, i, h = plan.place()
    L, Lp, C, wb, g, nw = plan.L, plan.Lp, plan.C, plan.wb, plan.g, plan.nw
    Ch, cs, T1 = plan.Ch, plan.cs, plan.T1
    M = wb * Lp
    nD = plan.steps
    turns = tail_turns(plan)
    last = len(turns) - 1
    peers = group_peers(plan)
    red = Reduction(plan, tail_batches(plan), *rest[:8])
    link = rest[8:]

    def member(off):
        return (s, h * g + wrap(i + off, g))

    def send(step):
        rows = pl.ds(step * wb, wb)
        for off in range(1, g):
            remote(
                part.at[off - 1, rows],
                gz_got.at[off, rows],
                bulk_sems.at[0, off],
                bulk_sems.at[1, off],
                member(off),
            ).start()

    def res_copy(off):
        rows = pl.ds(plan.cut, nw - plan.cut)
        return remote(
            res.at[wrap(i + off, g), rows],
            res_got.at[off],
            res_sems.at[0, off],
            res_sems.at[1, off],
            member(off),
        )

    res_offs = range(1, g) if plan.cut < nw else ()

    def X5_copy(k):
        cols = pl.ds(pl.multiple_of(k * C, 128), C)
        return pltpu.make_async_copy(X5_hbm.at[:, cols], X5.at[k % 2], X5_sems.at[k % 2])

    def when(at):
        return pl.when(t == min(at, last))

    def turn(kind, k):
        return turns.index((kind, k)) if (kind, k) in turns else last

    def turn_of(kind):
        index = jnp.int32(0)
        here = False
        for n, (what, k) in enumerate(turns):
            if what == kind:
                index = jnp.where(t == n, k, index)
                here = (t == n) | here
        return here, index

    @when(0)
    def _():
        greet(peers.others)
        acc[...] = jnp.zeros_like(acc)
        pick[...] = pick_matrix(L)
        eye[...] = eye_matrix(Ch, Ch, 0)
        mean, rho = norm_of(half_state[ST1 : ST1 + 2], 2.0 * total_of(lens))
        scale = half_state[GAIN1 : GAIN1 + 1] * rho
        offset = half_state[SHIFT1 : SHIFT1 + 1] - mean * scale
        for k, row in enumerate((scale, offset, rho, -mean * rho)):
            cols[k] = column(row, L)
        for first in range(0, Ch, 64):
            rows = slice(first, min(first + 64, Ch))
            for r, parts in enumerate((((0,), (1, 2), (3, 4)), ((0, 1), (2, 3), (4,)))):
                for k, which in enumerate(parts):
                    v = taps[which[0], rows]
                    if len(which) > 1:
                        v = (v.astype(F32) + taps[which[1], rows].astype(F32)).astype(BF16)
                    at = r * Ch
                    wcat[at + rows.start : at + rows.stop, k * C : (k + 1) * C] = v
        meet(peers.others)

    @pl.when(t < nD)
    def _():
        total = total_of(lens)
        mean, rho = norm_of(old[ST2 : ST2 + 2], total)
        gr = old[GAIN2 : GAIN2 + 1] * rho
        sg = old[SU2 : SU2 + 1] / total
        gg = old[SU2 + 1 : SU2 + 2] / total
        rowc = rows_of((Lp, C))
        row1 = rows_of((1, C))

        by_dz = 0.5 * gr
        by_v = -0.5 * gr * rho * gg
        by_1 = 0.5 * gr * (mean * rho * gg - sg)

        def back(dout, dz, v):
            return 0.5 * dout + by_dz * dz + by_v * v + by_1

        def grad_of(w):
            at = t * wb + w
            valid = lens[i * nw + at] - s * Lp
            d = back(cot[w].astype(F32), dz2[w], x2[w])
            d = jnp.where(rowc < valid, d, 0.0)
            one = pl.ds(at, 1)
            dl = back(beyond[0, 2, one, :], dzland[0, one, :], x2land[0, w, EDGE - 1 : EDGE].astype(F32))
            dl = jnp.where((row1 - 1 < valid) & (s > 0), dl, 0.0)
            dh = back(beyond[1, 2, one, :], dzland[1, one, :], x2land[1, w, 0:1].astype(F32))
            dh = jnp.where(row1 + Lp < valid, dh, 0.0)
            ext[w, 7:8] = dl
            ext[w, 8 : 8 + Lp] = d
            ext[w, 8 + Lp : 9 + Lp] = dh
            top, end = w * Lp, (w + 1) * Lp
            D3[t, top:end, 0:C] = ext[w, 9 : 9 + Lp].astype(BF16)
            D3[t, top:end, C : 2 * C] = d.astype(BF16)
            D3[t, top:end, 2 * C : 3 * C] = ext[w, 7 : 7 + Lp].astype(BF16)

        for w in range(wb):
            grad_of(w)
        half = D3[t, :, pl.ds(pl.multiple_of(C + h * Ch, 128), Ch)]
        D0T[:, pl.ds(pl.multiple_of(t * M, 128), M)] = half.T

    here_x, bx = turn_of("x")

    @pl.when(here_x)
    def _():
        lanes = lanes_of((Ch, L))

        def through(w):
            valid = 2 * lens[i * nw + bx * wb + w] - s * L
            top, end = w * Lp, (w + 1) * Lp
            v = mm_nt(eye[...], x[w])
            da = jnp.concatenate([y[0:Ch, top:end], y[Ch:, top:end]], axis=1)
            da = mm(da.astype(BF16), pick[...])
            dzw = da * gelu_slope(v * cols[0] + cols[1])
            dzw = jnp.where(lanes < valid, dzw, 0.0)
            acc[0] += dzw
            acc[1] += dzw * (v * cols[2] + cols[3])
            split[w % 2] = dzw.astype(BF16)
            for off in range(g):
                rows = pl.ds(pl.multiple_of(lax.rem(i + off, g) * cs, 16), cs)
                if off == 0:
                    gz[w] = split[w % 2, rows]
                else:
                    part[off - 1, bx * wb + w] = split[w % 2, rows]

        nh = 2 if wb % 2 == 0 and wb * Lp // 2 % 128 == 0 else 1
        n = wb // nh
        for hf in range(nh):
            rows = slice(hf * n * Lp, (hf + 1) * n * Lp)
            y[:, rows] = mm_nt(wcat[...], D3[bx, rows])
            for w in range(hf * n, (hf + 1) * n):
                through(w)

    @when(0)
    def _():
        hs = plan.H // plan.nz
        rb = plan.rb
        for u in range(2):

            def rows(j, m, u=u):
                side, r = m * rb // hs, m * rb % hs
                n = 2 * side + u
                rows = slice(j * hs + r, j * hs + r + rb)
                v = grads[rows, n * C : (n + 1) * C] if n < plan.T2 else pgrad[rows]
                return v.astype(F32)

            red.put(T1 + u, rows)
        red.step0(0)

    @when(nD - 1)
    def _():
        X5_copy(0).start()

    here_w, k = turn_of("w")

    @pl.when(here_w)
    def _():
        @pl.when(k < T1 - 1)
        def _():
            X5_copy(k + 1).start()

        X5_copy(k).wait()
        y[0:Ch, 0:C] = mm(D0T[...], X5[lax.rem(k, 2)])
        rb = plan.rb
        red.put(k, lambda j, m: y[j * cs + m * rb : j * cs + (m + 1) * rb, 0:C])

    after_w = turn("w", T1 - 1)
    x2nd = max(turn("x", (nD + 1) // 2), after_w)
    x3rd = max(turn("x", nD - 1), after_w)
    for at, step, batch in (
        (1, red.step1, 0),
        (max(nD - 1, 2), red.step2, 0),
        (turn("w", 2), red.step0, 1),
        (turn("w", 3), red.step1, 1),
        (turn("w", T1 - 1), red.step3, 0),
        (turn("w", T1 - 1), red.step0, 2),
        (x2nd, red.step1, 2),
        (x2nd, red.step2, 1),
        (x2nd, red.step4, 0),
        (x3rd, red.step2, 2),
    ):

        @when(at)
        def _():
            step(batch)

    @pl.when(here_x)
    def _():
        send(bx)

    @when((nD + 1) // 2 - 1)
    def _():
        for off in res_offs:
            res_copy(off).start()

    @when(turn("x", nD - 1))
    def _():
        packet = link[0]
        packet[...] = jnp.zeros_like(packet)
        packet[0:1, 0:Ch] = jnp.sum(acc[0].T, axis=0, keepdims=True)
        packet[1:2, 0:Ch] = jnp.sum(acc[1].T, axis=0, keepdims=True)
        peers.start(link)

    @when(last)
    def _():
        red.step3(1)
        red.step3(2)
        red.step4(1)
        sums[...] = peers.finish(link)[:, 0:Ch]
        red.step4(2)
        for b in range(3):
            red.step5(b)
        own = pltpu.make_async_copy(red.out, summed, X5_sems.at[0])
        own.start()
        for off in range(1, g):
            done = remote(
                part.at[off - 1],
                gz_got.at[off],
                bulk_sems.at[0, off],
                bulk_sems.at[1, off],
                member(off),
            )
            done.wait_recv()
            done.wait_send()
        for off in res_offs:
            res_copy(off).wait()
        own.wait()


def input_grad_kernel(plan, wg, lens, x, gz, gz_got, sums, res, res_got, res_more, summed,
                      state, half_state,
                      out, out_result, conv_grad, dil_grad, point_grad,
                      g1, b1, g2, b2, g3, b3, pb, eye, cols, xt):
    t = pl.program_id(0)
    s, z, i, h = plan.place()
    L, Ch, cs = plan.L, plan.Ch, plan.cs
    turn = plan.nw // wg
    mine = pl.ds(pl.multiple_of(i * cs, 16), cs)

    @pl.when(first_step())
    def _():
        n = 2.0 * total_of(lens)
        mean, rho = norm_of(half_state[ST1 : ST1 + 2], n)
        gr = half_state[GAIN1 : GAIN1 + 1] * rho
        gg = sums[1:2] / n * rho
        for k, row in enumerate((gr, -gr * gg, gr * (mean * gg - sums[0:1] / n))):
            xt[...] = column(row, L)
            cols[k] = xt[mine]
        eye[...] = eye_matrix(cs, Ch, i * cs)

        def mine_of(src, at, which, count, *dsts):
            n = dsts[0].shape[1]
            for k in range(count):

                @pl.when(which == k)
                def _():
                    for dst, r in zip(dsts, at):
                        dst[...] = src[r : r + 1, k * n : (k + 1) * n]

        mine_of(sums, (1, 0), i, plan.g, g1, b1)
        mine_of(state, (SU2 + 1, SU2), z, plan.nz, g2, b2)
        mine_of(state, (SU3 + 1, SU3), z, plan.nz, g3, b3)
        mine_of(state, (BSUM,), z, plan.nz, pb)

    own = lax.div(t, turn) == i
    early = lax.rem(t, turn) * wg < plan.cut
    for w in range(wg):
        got = jnp.where(early, res_got[0, w].astype(F32), res_more[0, w].astype(F32))
        out_result[w] = jnp.where(own, res[0, w].astype(F32), got).astype(BF16)

    C, T1, hs, rb, wide = plan.C, plan.T1, plan.H // plan.nz, plan.rb, plan.C // 2
    count = plan.NW // wg
    turns = min(count, plan.chips)
    per, every = plan.chips // turns, count // turns

    def spread(chunk):
        for n in range(per):
            m = chunk * per + n
            side, r = m * rb // hs, m * rb % hs
            for c in range(2):
                at = slice(c * wide, (c + 1) * wide)
                for k in range(T1):
                    conv_grad[k, n * rb : (n + 1) * rb, at] = summed[k, c, n].astype(F32)
                for u in range(2):
                    v = summed[T1 + u, c, n].astype(F32)
                    if 2 * side + u < plan.T2:
                        dil_grad[2 * side + u, r : r + rb, at] = v
                    else:
                        point_grad[r : r + rb, at] = v

    for chunk in range(turns):
        pl.when(t == chunk * every)(partial(spread, chunk))

    lanes = lanes_of((cs, L))
    for w in range(wg):
        valid = 2 * lens[t * wg + w] - s * L
        v = mm_nt(eye[...], x[w])
        dz = jnp.where(own, gz[w].astype(F32), gz_got[0, w].astype(F32))
        r = cols[0] * dz + v * cols[1] + cols[2]
        out[w] = jnp.where(lanes < valid, r, 0.0).astype(BF16)


def call(kernel, plan, name, steps, ins, outs, scratch, flops, nbytes, cid=None):
    extra = {} if cid is None else dict(collective_id=cid, has_side_effects=True)
    return pl.pallas_call(
        partial(kernel, plan),
        grid=(steps,),
        in_specs=[SMEM] + [spec for spec, _ in ins],
        out_specs=[spec for spec, _, _ in outs],
        out_shape=[jax.ShapeDtypeStruct(shape, dtype) for _, shape, dtype in outs],
        scratch_shapes=scratch,
        compiler_params=pltpu.CompilerParams(vmem_limit_bytes=VMEM_LIMIT, **extra),
        cost_estimate=pl.CostEstimate(
            flops=int(flops), bytes_accessed=int(nbytes), transcendentals=0
        ),
        name=name,
    )


def per_device(
    inputs,
    lengths,
    input_gain,
    input_shift,
    conv_weight,
    branch_gain,
    branch_shift,
    dilated_tap_weight,
    mixer_gain,
    mixer_shift,
    point_weight,
    point_bias,
    cotangent,
):
    NW, L, C = inputs.shape
    Lp = L // 2
    nz = lax.axis_size("ch")
    R = 2
    plan = Plan(
        ns=lax.axis_size("seq"),
        nz=nz,
        R=R,
        NW=NW,
        L=L,
        C=C,
        H=mixer_gain.shape[0] * nz,
        T1=conv_weight.shape[0],
        T2=dilated_tap_weight.shape[0],
        wb=min(NW * R // nz, max(1, 512 // Lp)),
    )
    g, nw, cs, Ch, H, Hh, wb = plan.g, plan.nw, plan.cs, plan.Ch, plan.H, plan.Hh, plan.wb
    T1, T2, steps = plan.T1, plan.T2, plan.steps
    M = wb * Lp
    hs = H // nz
    lens = lengths.astype(jnp.int32)

    def row(a):
        return a.reshape(1, a.shape[0])

    def grp():
        return lax.rem(lax.axis_index("ch"), g)

    def half():
        return lax.div(lax.axis_index("ch"), g)

    def core():
        return lax.rem(lax.axis_index("seq"), 2)

    def chip4():
        return lax.div(lax.axis_index("seq"), plan.ns // 4)

    def whole(*shape):
        return pl.BlockSpec(shape, lambda t: (0,) * len(shape), pipeline_mode=pl.Buffered(1))

    def const(*shape):
        return pl.BlockSpec(shape, lambda t: (0,) * len(shape))

    def win(*shape):
        return pl.BlockSpec(shape, lambda t: (t,) + (0,) * (len(shape) - 1))

    def arg_win(n, width):
        return pl.BlockSpec((wb, n, width), lambda t: (grp() * steps + t, 0, 0))

    def ins(*pairs):
        return [p for p in pairs]

    share = NW // nz
    nm = max(1, share // wb)

    def edge_spec(n):
        return pl.BlockSpec(
            (nw, 16, C), lambda t: (grp(), n, 0), pipeline_mode=pl.Buffered(1)
        )

    def head_block(t):
        own = lax.div(lax.axis_index("ch") * share, wb) + t
        return jnp.where(t < nm, own, grp() * steps + t - nm), 0, 0

    def after(*shape):
        return pl.BlockSpec(
            shape, lambda t: (jnp.maximum(t - nm, 0),) + (0,) * (len(shape) - 1)
        )

    pairs = ins(
        (pl.BlockSpec((wb, L, C), head_block), inputs),
        (edge_spec(0), inputs),
        (edge_spec(L // 16 - 1), inputs),
        (edge_spec(0), cotangent),
        (edge_spec(Lp // 16 - 1), cotangent),
        (whole(1, cs), row(branch_gain)),
        (whole(1, cs), row(branch_shift)),
        (whole(1, cs), row(point_bias)),
        (whole(1, H // nz), row(mixer_gain)),
        (whole(1, H // nz), row(mixer_shift)),
        (ANY, conv_weight.reshape(T1 * C, C)),
        (whole(C), input_gain),
        (whole(C), input_shift),
        (
            pl.BlockSpec(
                (1, hs, C // 2),
                lambda t: (jnp.minimum(chip4(), T2 - 1), 0, core()),
                pipeline_mode=pl.Buffered(1),
            ),
            jnp.swapaxes(dilated_tap_weight, 1, 2),
        ),
        (
            pl.BlockSpec(
                (hs, C // 2), lambda t: (0, core()), pipeline_mode=pl.Buffered(1)
            ),
            point_weight,
        ),
    )
    plane, line, group = plane_peers(plan), line_peers(plan), group_peers(plan)
    state_shape = (STATE, C)
    edges2, edges3 = (2, nw, EDGE, C), (2, nw, EDGE, H)
    X5, x2, land2, state, beyond, full = call(
        lambda plan, *refs: head_kernel(plan, nm, *refs),
        plan,
        "head",
        nm + steps,
        pairs,
        [
            (after(M, T1 * C), (nw * Lp, T1 * C), BF16),
            (after(wb, Lp, C), (nw, Lp, C), F32),
            (ANY, edges2, BF16),
            (const(*state_shape), state_shape, F32),
            (const(2, 3, nw, C), (2, 3, nw, C), F32),
            (ANY, (2, T2 + 1, nz, hs, C // 2), BF16),
        ],
        [
            pltpu.VMEM((2, 8, C), F32),
            pltpu.VMEM((2, 3, nw, C), F32),
            pltpu.VMEM((2, 3, nw, C), F32),
            pltpu.VMEM((T1 * Lp, L), BF16),
            pltpu.VMEM(edges2, BF16),
            pltpu.VMEM((2, C), F32),
            pltpu.VMEM((T1 * C, C), BF16),
            pltpu.SemaphoreType.DMA,
            pltpu.VMEM((hs, C // 2), BF16),
            pltpu.SemaphoreType.DMA((2, 4)),
            HALO_SEMS,
            HALO_SEMS,
        ]
        + plane.scratch(2, C)
        + line.scratch(3, C)
        + group.scratch(2, C),
        2 * nw * Lp * T1 * C * C,
        nw * Lp * C * 20,
        cid=1,
    )(lens, *[a for _, a in pairs])

    full = full.reshape(2, T2 + 1, H, C // 2)
    taps_spec = whole(2, T2, H, C // 2)
    pw_spec = pl.BlockSpec(
        (2, 1, H, C // 2), lambda t: (0, T2, 0, 0), pipeline_mode=pl.Buffered(1)
    )

    def early(*shape):
        return pl.BlockSpec(
            shape, lambda t: (jnp.minimum(t, steps - 1),) + (0,) * (len(shape) - 1)
        )

    def early_land(width):
        return pl.BlockSpec(
            (2, wb, EDGE, width), lambda t: (0, jnp.minimum(t, steps - 1), 0, 0)
        )

    def late(t):
        return jnp.maximum(t - steps, 0)

    def half_of(n):
        return pl.BlockSpec((n, Ch), lambda t: (0, half()), pipeline_mode=pl.Buffered(1))

    cot_spec = pl.BlockSpec(
        (wb, Lp, C), lambda t: (grp() * steps + jnp.minimum(t, steps - 1), 0, 0)
    )

    pairs = ins(
        (early(wb, Lp, C), x2),
        (early_land(C), land2),
        (taps_spec, full),
        (whole(*state_shape), state),
    )
    Y3, c2, land3, state = call(
        dilated_kernel,
        plan,
        "dilated",
        steps,
        pairs,
        [
            (win(M, T2 * C), (nw * Lp, T2 * C), BF16),
            (win(wb, Lp, H), (nw, Lp, H), F32),
            (ANY, edges3, BF16),
            (const(*state_shape), state_shape, F32),
        ],
        [
            pltpu.VMEM((wb, Lp + 2 * EDGE, C), F32),
            pltpu.VMEM((H, T2 * C), BF16),
            pltpu.VMEM(edges3, BF16),
            pltpu.VMEM((1, 2 * H), F32),
            HALO_SEMS,
        ]
        + group.scratch(1, 2 * H),
        2 * nw * Lp * T2 * C * H,
        nw * Lp * C * 12,
        cid=3,
    )(lens, *[a for _, a in pairs])

    pairs = ins(
        (early(wb, Lp, H), c2),
        (pl.BlockSpec((nw // 2, Lp, Ch), lambda t: (late(t), 0, half())), x2),
        (cot_spec, cotangent),
        (pw_spec, full),
        (whole(*state_shape), state),
        (half_of(STATE), state),
    )
    res, dz3, pgrad, dland3, state = call(
        point_kernel,
        plan,
        "point",
        steps + 2,
        pairs,
        [
            (
                pl.BlockSpec((g, nw // 2, cs, Lp), lambda t: (0, late(t), 0, 0)),
                (g, nw, cs, Lp),
                BF16,
            ),
            (early(wb, Lp, H), (nw, Lp, H), F32),
            (const(Hh, C), (Hh, C), BF16),
            (ANY, edges3, BF16),
            (const(*state_shape), state_shape, F32),
        ],
        [
            pltpu.VMEM((H, C), BF16),
            pltpu.VMEM((nw * Lp, H), BF16),
            pltpu.VMEM((H, nw * Lp), BF16),
            pltpu.VMEM((nw * Lp, C), BF16),
            pltpu.VMEM(edges3, BF16),
            pltpu.VMEM((2, C), F32),
            HALO_SEMS,
        ]
        + group.scratch(2, C),
        5 * nw * Lp * C * H,
        nw * Lp * C * 10,
        cid=4,
    )(lens, *[a for _, a in pairs])

    pairs = ins(
        (early(wb, Lp, H), c2),
        (early_land(H), land3),
        (early(wb, Lp, H), dz3),
        (early_land(H), dland3),
        (early(wb, Lp, C), x2),
        (pl.BlockSpec((nw * Lp, C), lambda t: (0, late(t))), Y3),
        (taps_spec, full),
        (whole(*state_shape), state),
        (ANY, res),
    )
    dz2, grads, dland2, state, res_got = call(
        dilated_back_kernel,
        plan,
        "dilated_back",
        steps + T2,
        pairs,
        [
            (early(wb, Lp, C), (nw, Lp, C), F32),
            (pl.BlockSpec((Hh, C), lambda t: (0, late(t))), (Hh, T2 * C), BF16),
            (ANY, (2, nw, C), F32),
            (const(*state_shape), state_shape, F32),
            (ANY, (g, nw, cs, Lp), BF16),
        ],
        [
            pltpu.VMEM((wb, Lp + 2 * EDGE, H), F32),
            pltpu.VMEM((M, T2 * H), BF16),
            pltpu.VMEM((T2 * H, C), BF16),
            pltpu.VMEM((H, nw * Lp), BF16),
            pltpu.VMEM((2, nw, C), F32),
            pltpu.VMEM((2, C), F32),
            pltpu.SemaphoreType.DMA((2, g)),
            HALO_SEMS,
        ]
        + group.scratch(2, C),
        4 * nw * Lp * T2 * C * H,
        nw * Lp * C * 20,
        cid=5,
    )(lens, *[a for _, a in pairs])

    chips, rb = plan.chips, plan.rb
    turns_t = tail_turns(plan)
    cut = plan.cut
    rest = max(nw - cut, 1)

    def x_block(t):
        block = jnp.int32(0)
        for n, (what, k) in enumerate(turns_t):
            if what == "x":
                block = jnp.where(t >= n, k, block)
        return block

    sshape = (T1 + 2, 2, chips, rb, C // 2)
    pairs = ins(
        (early(wb, Lp, C), dz2),
        (whole(2, nw, C), dland2),
        (early(wb, Lp, C), x2),
        (early_land(C), land2),
        (cot_spec, cotangent),
        (whole(2, 3, nw, C), beyond),
        (
            pl.BlockSpec(
                (wb, L, Ch), lambda t: (grp() * steps + x_block(t), 0, half())
            ),
            inputs,
        ),
        (ANY, X5),
        (
            pl.BlockSpec(
                (T1, Ch, C), lambda t: (0, half(), 0), pipeline_mode=pl.Buffered(1)
            ),
            conv_weight,
        ),
        (whole(Hh, T2 * C), grads),
        (whole(Hh, C), pgrad),
        (whole(*state_shape), state),
        (half_of(STATE), state),
        (ANY, res),
    )
    gz, gz_got, sums1, summed, res_more = call(
        tail_kernel,
        plan,
        "tail",
        len(turns_t),
        pairs,
        [
            (pl.BlockSpec((wb, cs, L), lambda t: (x_block(t), 0, 0)), (nw, cs, L), BF16),
            (ANY, (g, nw, cs, L), BF16),
            (const(2, Ch), (2, Ch), F32),
            (ANY, sshape, BF16),
            (ANY, (g, rest, cs, Lp), BF16),
        ],
        [
            pltpu.VMEM((wb, Lp + 16, C), F32),
            pltpu.VMEM((steps, M, 3 * C), BF16),
            pltpu.VMEM((Ch, nw * Lp), BF16),
            pltpu.VMEM((2 * Ch, 3 * C), BF16),
            pltpu.VMEM((L, L), BF16),
            pltpu.VMEM((Ch, Ch), BF16),
            pltpu.VMEM((4, Ch, L), F32),
            pltpu.VMEM((2 * Ch, max(M, C)), F32),
            pltpu.VMEM((g - 1, nw, cs, L), BF16),
            pltpu.VMEM((2, Ch, L), BF16),
            pltpu.VMEM((2, Ch, L), F32),
            pltpu.VMEM((2, nw * Lp, C), BF16),
            pltpu.SemaphoreType.DMA((2,)),
            pltpu.SemaphoreType.DMA((2, g)),
            pltpu.SemaphoreType.DMA((2, g)),
        ]
        + Reduction.scratch(plan, tail_batches(plan))
        + group.scratch(2, C),
        2 * nw * Lp * (6 + T1) * C * Ch,
        nw * Lp * C * 40,
        cid=6,
    )(lens, *[a for _, a in pairs])

    wg = min(2 * wb, cut)
    count = NW // wg
    turn = nw // wg
    turns = min(count, chips)

    def own_block(t):
        return jnp.where(lax.div(t, turn) == grp(), lax.rem(t, turn), 0)

    def got_slot(t):
        off = lax.rem(grp() - lax.div(t, turn) + g, g)
        return jnp.maximum(off, 1), jnp.where(off > 0, lax.rem(t, turn), 0)

    def got_part(t, first, blocks):
        slot, block = got_slot(t)
        return slot, jnp.clip(block - first, 0, blocks - 1), 0, 0

    pairs = ins(
        (pl.BlockSpec((wg, L, Ch), lambda t: (t, 0, half())), inputs),
        (pl.BlockSpec((wg, cs, L), lambda t: (own_block(t), 0, 0)), gz),
        (pl.BlockSpec((1, wg, cs, L), lambda t: got_slot(t) + (0, 0)), gz_got),
        (whole(2, Ch), sums1),
        (pl.BlockSpec((1, wg, cs, Lp), lambda t: (grp(), own_block(t), 0, 0)), res),
        (
            pl.BlockSpec((1, wg, cs, Lp), lambda t: got_part(t, 0, cut // wg)),
            res_got,
        ),
        (
            pl.BlockSpec(
                (1, wg, cs, Lp), lambda t: got_part(t, cut // wg, max((nw - cut) // wg, 1))
            ),
            res_more if nw > cut else res_got,
        ),
        (
            pl.BlockSpec(
                (T1 + 2, 2, chips // turns, rb, C // 2),
                lambda t: (0, 0, t * turns // count, 0, 0),
            ),
            summed,
        ),
        (whole(*state_shape), state),
        (half_of(STATE), state),
    )
    outs = call(
        lambda plan, *refs: input_grad_kernel(plan, wg, *refs),
        plan,
        "input_grad",
        count,
        pairs,
        [
            (win(wg, cs, L), (NW, cs, L), BF16),
            (win(wg, cs, Lp), (NW, cs, Lp), BF16),
            (
                pl.BlockSpec((T1, cs // turns, C), lambda t: (0, t * turns // count, 0)),
                (T1, cs, C),
                F32,
            ),
            (const(T2, hs, C), (T2, hs, C), F32),
            (const(hs, C), (hs, C), F32),
        ]
        + [(const(1, n), (1, n), F32) for n in (cs, cs, cs, cs, hs, hs, cs)],
        [
            pltpu.VMEM((cs, Ch), BF16),
            pltpu.VMEM((3, cs, L), F32),
            pltpu.VMEM((Ch, L), F32),
        ],
        2 * NW * L * Ch * cs,
        NW * L * cs * 8,
    )(lens, *[a for _, a in pairs])
    grad, result, conv_grad, dil_grad, point_grad = outs[:5]
    g1, b1, g2, b2, g3, b3, pb = [a[0] for a in outs[5:]]
    return (
        jnp.swapaxes(result, 1, 2),
        jnp.swapaxes(grad, 1, 2),
        jnp.swapaxes(conv_grad, 1, 2),
        g1,
        b1,
        g2,
        b2,
        jnp.swapaxes(dil_grad, 1, 2),
        g3,
        b3,
        point_grad,
        pb,
    )


def solution(mesh):
    in_specs = (
        P(None, "seq", None),
        P(),
        P(),
        P(),
        P(),
        P("ch"),
        P("ch"),
        P(None, None, "ch"),
        P("ch"),
        P("ch"),
        P("ch", None),
        P("ch"),
        P(None, "seq", None),
    )
    out_specs = (
        P(None, "seq", "ch"),
        P(None, "seq", "ch"),
        P(None, None, "ch"),
        P("ch"),
        P("ch"),
        P("ch"),
        P("ch"),
        P(None, None, "ch"),
        P("ch"),
        P("ch"),
        P("ch", None),
        P("ch"),
    )
    return jax.shard_map(
        per_device, mesh=mesh, in_specs=in_specs, out_specs=out_specs, check_vma=False
    )
```

```python
from functools import partial
from typing import NamedTuple

import jax
import jax.numpy as jnp
from jax import lax
from jax.experimental import pallas as pl
from jax.experimental.pallas import tpu as pltpu
from jax.sharding import PartitionSpec as P

DIL = 14
EDGE = 16
EPS = 1e-05
GC0 = 0.7978845608028654
GC1 = 0.044715
F32 = jnp.float32
BF16 = jnp.bfloat16
MESH = pl.DeviceIdType.MESH
VMEM_LIMIT = 58 * 1024 * 1024
ANY = pl.BlockSpec(memory_space=pl.ANY)
SMEM = pl.BlockSpec(memory_space=pltpu.SMEM)


ST1, GAIN2, SHIFT2, BIAS, GAIN3, SHIFT3, GAIN1, SHIFT1, ST2, ST3, SU3, BSUM, SU2 = (
    0, 2, 3, 4, 5, 6, 7, 8, 9, 11, 13, 15, 16
)
STATE = 24


class Plan(NamedTuple):
    ns: int
    nz: int
    R: int
    NW: int
    L: int
    C: int
    H: int
    T1: int
    T2: int
    wb: int

    @property
    def g(self):
        return self.nz // self.R

    @property
    def nw(self):
        return self.NW // self.g

    @property
    def Lp(self):
        return self.L // 2

    @property
    def cs(self):
        return self.C // self.nz

    @property
    def Ch(self):
        return self.C // self.R

    @property
    def Hh(self):
        return self.H // self.R

    @property
    def steps(self):
        return self.nw // self.wb

    @property
    def chips(self):
        return self.ns // 2

    @property
    def rb(self):
        return self.cs // self.chips

    def place(self):
        s, z = lax.axis_index("seq"), lax.axis_index("ch")
        return s, z, lax.rem(z, self.g), lax.div(z, self.g)


def gelu(z):
    t = jnp.tanh(z * (GC0 + (GC0 * GC1) * (z * z)))
    return z * (0.5 + 0.5 * t)


def gelu_both(z):
    sq = z * z
    t = jnp.tanh(z * (GC0 + (GC0 * GC1) * sq))
    h = 0.5 + 0.5 * t
    v = z * h
    return v, h + v * (1.0 - t) * (GC0 + (3.0 * GC0 * GC1) * sq)


def gelu_slope(z):
    return gelu_both(z)[1]


def fold(v):
    return jnp.sum(v.reshape(v.shape[0] // 8, 8, v.shape[1]), axis=0)


def unfold(v):
    return jnp.sum(v, axis=0, keepdims=True)


def part_of(v, which, n):
    out = v[0:n]
    for k in range(1, v.shape[0] // n):
        out = jnp.where(which == k, v[k * n : (k + 1) * n], out)
    return out


def rows_of(shape):
    return lax.broadcasted_iota(jnp.int32, shape, 0)


def lanes_of(shape):
    return lax.broadcasted_iota(jnp.int32, shape, 1)


def total_of(lens):
    n = lens[0]
    for k in range(1, lens.shape[0]):
        n = n + lens[k]
    return n.astype(F32)


def norm_of(stats, total):
    mean = stats[0:1] / total
    square = stats[1:2] / total
    return mean, lax.rsqrt(square - mean * mean + EPS)


def flat(ref):
    return ref[...].reshape(1, ref.shape[0])


def column(row, n):
    return jnp.broadcast_to(row, (n, row.shape[1])).T


def mm(a, b):
    return jnp.dot(a, b, preferred_element_type=F32)


def mm_nt(a, b):
    return lax.dot_general(a, b, (((1,), (1,)), ((), ())), preferred_element_type=F32)


def mm_tn(a, b):
    return lax.dot_general(a, b, (((0,), (0,)), ((), ())), preferred_element_type=F32)


def mm_tt(a, b):
    return lax.dot_general(a, b, (((0,), (1,)), ((), ())), preferred_element_type=F32)


def eye_matrix(n, m, first):
    return jnp.where(lanes_of((n, m)) == rows_of((n, m)) + first, 1.0, 0.0).astype(BF16)


def pick_matrix(L):
    r, n = rows_of((L, L)), lanes_of((L, L))
    bin_of = 2 * r - jnp.where(r >= L // 2, L - 1, 0)
    return jnp.where(n == bin_of, 1.0, 0.0).astype(BF16)


def remote(src, dst, send, recv, device):
    return pltpu.make_async_remote_copy(
        src_ref=src,
        dst_ref=dst,
        send_sem=send,
        recv_sem=recv,
        device_id=device,
        device_id_type=MESH,
    )


def wrap(v, n):
    return jnp.where(v >= n, v - n, v)


def greet(devices):
    barrier = pltpu.get_barrier_semaphore()
    for device in devices:
        pl.semaphore_signal(barrier, inc=1, device_id=device, device_id_type=MESH)


def meet(devices):
    pl.semaphore_wait(pltpu.get_barrier_semaphore(), len(devices))


class Peers:
    def __init__(self, me, others):
        self.me, self.others = me, others
        self.count = len(others) + 1

    def start(self, link):
        packet, buf, sems = link
        for device in self.others:
            remote(packet, buf.at[self.me], sems.at[0], sems.at[1], device).start()

    def finish(self, link):
        packet, buf, sems = link
        buf[self.me] = packet[...]
        rest = buf.at[pl.ds(0, self.count - 1)]
        done = remote(rest, rest, sems.at[0], sems.at[1], self.others[0])
        done.wait_recv()
        acc = buf[0]
        for q in range(1, self.count):
            acc = acc + buf[q]
        done.wait_send()
        return acc

    def scratch(self, rows, width):
        return [
            pltpu.VMEM((rows, width), F32),
            pltpu.VMEM((self.count, rows, width), F32),
            pltpu.SemaphoreType.DMA((2,)),
        ]


def group_peers(plan):
    s, z, i, h = plan.place()
    g = plan.g
    others = [
        (wrap(s + a, plan.ns), h * g + wrap(i + b, g))
        for a in range(plan.ns)
        for b in range(g)
        if a or b
    ]
    return Peers(s * g + i, others)


def plane_peers(plan):
    s, z, i, h = plan.place()
    return Peers(s, [(wrap(s + a, plan.ns), z) for a in range(1, plan.ns)])


def line_peers(plan):
    s, z, i, h = plan.place()
    return Peers(z, [(s, wrap(z + a, plan.nz)) for a in range(1, plan.nz)])


class Halo:
    def __init__(self, plan, edge, land, sems):
        self.edge, self.land, self.sems = edge, land, sems
        s, z, _, _ = plan.place()
        self.to = ((wrap(s + plan.ns - 1, plan.ns), z), (wrap(s + 1, plan.ns), z))

    def copy(self, side, rows):
        return remote(
            self.edge.at[side, rows],
            self.land.at[1 - side, rows],
            self.sems.at[0, side],
            self.sems.at[1, side],
            self.to[side],
        )

    def start(self, first, count):
        for side in range(2):
            self.copy(side, pl.ds(first, count)).start()

    def finish(self):
        for side in range(2):
            done = self.copy(side, pl.ds(0, self.land.shape[1]))
            done.wait_recv()
            done.wait_send()


HALO_SEMS = pltpu.SemaphoreType.DMA((2, 2))


class Gather:
    def __init__(self, plan, part, full, sems):
        self.plan, self.part, self.full, self.sems = plan, part, full, sems
        self.s, self.z, self.i, self.h = plan.place()
        self.c, self.m = lax.rem(self.s, 2), lax.div(self.s, 2)
        self.chips = plan.chips
        self.every = self.chips // 4
        self.tap = lax.div(self.m, self.every)
        self.owner = lax.rem(self.m, self.every) == 0
        self.mine = full.at[self.c, self.tap]

    def others(self):
        g, nz = self.plan.g, self.plan.nz
        return [(self.s, wrap(self.h * g + g + r, nz)) for r in range(nz - g)]

    def far(self, off):
        return (2 * wrap(self.m + off, self.chips) + self.c, self.z)

    def own(self):
        return pltpu.make_async_copy(self.part, self.mine.at[self.z], self.sems.at[0, 0])

    def line(self, off):
        device = (self.s, wrap(self.z + off, self.plan.nz))
        return remote(
            self.part, self.mine.at[self.z], self.sems.at[0, 1], self.sems.at[1, 1], device
        )

    def chip(self, off):
        return remote(self.mine, self.mine, self.sems.at[0, 2], self.sems.at[1, 2], self.far(off))

    def pair(self):
        half = self.full.at[self.c]
        device = (2 * self.m + 1 - self.c, self.z)
        return remote(half, half, self.sems.at[0, 3], self.sems.at[1, 3], device)

    def line_start(self):
        @pl.when(self.owner)
        def _():
            self.own().start()
            for off in range(1, self.plan.nz):
                self.line(off).start()

    def line_finish(self):
        @pl.when(self.owner)
        def _():
            self.own().wait()
            rest = self.mine.at[pl.ds(0, self.plan.nz - 1)]
            device = (self.s, wrap(self.z + 1, self.plan.nz))
            done = remote(rest, rest, self.sems.at[0, 1], self.sems.at[1, 1], device)
            done.wait_recv()
            done.wait_send()

    def chips_start(self):
        @pl.when(self.owner)
        def _():
            for off in range(1, self.chips):
                self.chip(off).start()

    def pair_start(self):
        def taken(count):
            rest = self.full.at[self.c, pl.ds(0, count)]
            return remote(rest, rest, self.sems.at[0, 2], self.sems.at[1, 2], self.far(1))

        @pl.when(self.owner)
        def _():
            taken(3).wait_recv()
            for off in range(1, self.chips):
                self.chip(off).wait_send()

        if self.every > 1:

            @pl.when(jnp.logical_not(self.owner))
            def _():
                taken(4).wait_recv()

        self.pair().start()

    def pair_finish(self):
        done = self.pair()
        done.wait_recv()
        done.wait_send()


def first_step():
    return pl.program_id(0) == 0


def last_step():
    return pl.program_id(0) == pl.num_programs(0) - 1


def keep_state(old, new):
    new[...] = old[...]


def head_kernel(plan, nm, lens, x, xtop, xend, ctop, cend, g2, s2, pb, g3, s3,
                w_hbm, gain, shift, taps, pw,
                X5, x2, land, state, beyond_out, full,
                macc, beyond, xedge, sel, edge, acc, w_ref, w_sem, part,
                gather_sems, xhalo_sems, halo_sems, *links):
    t = pl.program_id(0)
    peers, plane, line = group_peers(plan), plane_peers(plan), line_peers(plan)
    xhalo = Halo(plan, xedge, beyond, xhalo_sems)
    halo = Halo(plan, edge, land, halo_sems)
    gather = Gather(plan, part, full, gather_sems)
    w_copy = pltpu.make_async_copy(w_hbm, w_ref, w_sem)
    plane_link, line_link, link = links[:3], links[3:6], links[6:]
    s, z, i, h = plan.place()
    L, Lp, C, nw, nz, wb = plan.L, plan.Lp, plan.C, plan.nw, plan.nz, plan.wb
    share = plan.NW // nz
    c = t - nm
    everyone = peers.others + gather.others()

    @pl.when(first_step())
    def _():
        w_copy.start()
        greet(everyone)
        part[...] = jnp.where(gather.tap == 3, pw[...], taps[0])
        macc[...] = jnp.zeros_like(macc)
        acc[...] = jnp.zeros_like(acc)
        state[...] = jnp.zeros_like(state)
        state[GAIN1 : GAIN1 + 1] = flat(gain)
        state[SHIFT1 : SHIFT1 + 1] = flat(shift)
        n16 = nw * 16
        for side, (xe, ce, places) in enumerate(
            ((xtop, ctop, (0, 1, 0)), (xend, cend, (14, 15, 15)))
        ):
            for k, at in enumerate(places):
                rows, lanes = rows_of((nw, n16)), lanes_of((nw, n16))
                one = jnp.where(lanes == 16 * rows + at, 1.0, 0.0).astype(BF16)
                block = (xe if k < 2 else ce)[...].reshape(n16, C)
                xedge[side, k] = mm(one, block)
        shape = (Lp, L)
        for k in range(plan.T1):
            at = lanes_of(shape) - (2 * rows_of(shape) + (k - 2))
            sel[k * Lp : (k + 1) * Lp] = jnp.where((at == 0) | (at == 1), 1.0, 0.0).astype(BF16)

    @pl.when(c < 0)
    def _():
        rows = rows_of((L, C))
        for w in range(min(share, wb)):
            at = lax.rem(z * share, wb) + w
            valid = 2 * lens[z * share + t * wb + w] - s * L
            v = jnp.where(rows < valid, x[at].astype(F32), 0.0)
            macc[0] += fold(v)
            macc[1] += fold(v * v)

    @pl.when(c == -1)
    def _():
        packet, more = plane_link[0], line_link[0]
        packet[0:1] = unfold(macc[0])
        packet[1:2] = unfold(macc[1])
        meet(everyone)
        plane.start(plane_link)
        xhalo.start(0, 3)
        at = 0
        spans = []
        more[2:3] = jnp.zeros((1, C), F32)
        for ref in (g2, s2, pb, g3, s3):
            n = ref.shape[1]
            more[2:3, at : at + n] = ref[...]
            spans.append((at, n))
            at += n
        more[0:2] = plane.finish(plane_link)
        line.start(line_link)
        gather.line_start()
        state[ST1 : ST1 + 2] = line.finish(line_link)[0:2]
        for k in range(nz):
            row = line_link[1][k]
            for r, (at, n) in zip((GAIN2, SHIFT2, BIAS, GAIN3, SHIFT3), spans):
                state[r : r + 1, k * n : (k + 1) * n] = row[2:3, at : at + n]
        xhalo.finish()
        beyond_out[...] = beyond[...]
        w_copy.wait()

    @pl.when(c >= 0)
    def _():
        mean, rho = norm_of(state[ST1 : ST1 + 2], 2.0 * total_of(lens))
        scale = state[GAIN1 : GAIN1 + 1] * rho
        offset = state[SHIFT1 : SHIFT1 + 1] - mean * scale
        rows = rows_of((L, C))
        row1 = rows_of((1, C))
        row16 = rows_of((16, C))
        def activate(w):
            at = c * wb + w
            valid = 2 * lens[i * nw + at] - s * L
            a = gelu(x[w].astype(F32) * scale + offset)
            a = jnp.where(rows < valid, a, 0.0).astype(BF16)
            picked = mm(sel[...], a)
            for k in range(5):
                X5[w * Lp : (w + 1) * Lp, k * C : (k + 1) * C] = picked[
                    k * Lp : (k + 1) * Lp
                ].astype(BF16)

            def beside(side, k, bin_at):
                a = gelu(beyond[side, k, pl.ds(at, 1), :] * scale + offset)
                here = (row1 + bin_at < valid) & (row1 + (s * L + bin_at) >= 0)
                return jnp.where(here, a, 0.0).astype(BF16).astype(F32)

            l0, l1 = beside(0, 0, -2), beside(0, 1, -1)
            r0, r1 = beside(1, 0, L), beside(1, 1, L + 1)
            top, end = w * Lp, (w + 1) * Lp
            for k, add in ((0, l0 + l1), (1, l1)):
                X5[top : top + 16, k * C : (k + 1) * C] = (
                    picked[k * Lp : k * Lp + 16] + jnp.where(row16 == 0, add, 0.0)
                ).astype(BF16)
            for k, add in ((3, r0), (4, r0 + r1)):
                X5[end - 16 : end, k * C : (k + 1) * C] = (
                    picked[(k + 1) * Lp - 16 : (k + 1) * Lp] + jnp.where(row16 == 15, add, 0.0)
                ).astype(BF16)

        nc = 256
        rowp = rows_of((Lp, nc))

        def convolve(first, count):
            span = slice(first * Lp, (first + count) * Lp)
            for n in range(C // nc):
                cols = slice(n * nc, (n + 1) * nc)
                y = 0.5 * mm(X5[span], w_ref[:, cols])
                s0 = jnp.zeros((8, nc), F32)
                s1 = jnp.zeros((8, nc), F32)
                for w in range(first, first + count):
                    at = c * wb + w
                    valid = lens[i * nw + at] - s * Lp
                    v = y[(w - first) * Lp : (w - first + 1) * Lp]
                    x2[w, :, cols] = v
                    edge[0, at, :, cols] = v[:EDGE].astype(BF16)
                    edge[1, at, :, cols] = v[Lp - EDGE :].astype(BF16)
                    v = jnp.where(rowp < valid, v, 0.0)
                    s0 = s0 + fold(v)
                    s1 = s1 + fold(v * v)
                acc[0:1, cols] += unfold(s0)
                acc[1:2, cols] += unfold(s1)

        count = max(1, wb // 2)
        for first in range(0, wb, count):
            for w in range(first, first + count):
                activate(w)
            convolve(first, count)
        halo.start(c * wb, wb)

    @pl.when(c == 0)
    def _():
        gather.line_finish()
        gather.chips_start()

    @pl.when(last_step())
    def _():
        link[0][...] = acc[...]
        peers.start(link)
        gather.pair_start()
        state[ST2 : ST2 + 2] = peers.finish(link)
        halo.finish()
        gather.pair_finish()


def dilated_kernel(plan, lens, x2, x2land, w_ref, old,
                   Y3, c2, land, state, ext, wf, edge, acc, halo_sems, *link):
    t = pl.program_id(0)
    peers = group_peers(plan)
    halo = Halo(plan, edge, land, halo_sems)
    s, z, i, h = plan.place()
    Lp, C, H, wb = plan.Lp, plan.C, plan.H, plan.wb

    @pl.when(first_step())
    def _():
        greet(peers.others)
        acc[...] = jnp.zeros_like(acc)
        for k in range(plan.T2):
            for c in range(2):
                at = k * C + c * (C // 2)
                wf[:, at : at + C // 2] = w_ref[c, k]

    mean, rho = norm_of(old[ST2 : ST2 + 2], total_of(lens))
    scale = old[GAIN2 : GAIN2 + 1] * rho
    offset = old[SHIFT2 : SHIFT2 + 1] - mean * scale
    rows = rows_of((Lp, C))
    rowe = rows_of((EDGE, C))

    rowh = rows_of((Lp, H))
    sums0, sums1 = jnp.zeros((8, H), F32), jnp.zeros((8, H), F32)
    nh = min(2, wb)
    for first in range(0, wb, wb // nh):
        span = range(first, first + wb // nh)
        for w in span:
            valid = lens[i * plan.nw + t * wb + w] - s * Lp
            a = jnp.where(rows < valid, gelu(x2[w] * scale + offset), 0.0)
            al = gelu(x2land[0, w].astype(F32) * scale + offset)
            al = jnp.where((rowe - EDGE < valid) & (s > 0), al, 0.0)
            ah = gelu(x2land[1, w].astype(F32) * scale + offset)
            ah = jnp.where(rowe + Lp < valid, ah, 0.0)
            ext[w, 0:EDGE] = al
            ext[w, EDGE : EDGE + Lp] = a
            ext[w, EDGE + Lp :] = ah
            top, end = w * Lp, (w + 1) * Lp
            Y3[top:end, 0:C] = ext[w, EDGE - DIL : EDGE - DIL + Lp].astype(BF16)
            Y3[top:end, C : 2 * C] = a.astype(BF16)
            Y3[top:end, 2 * C : 3 * C] = ext[w, EDGE + DIL : EDGE + DIL + Lp].astype(BF16)
        y = mm_nt(Y3[first * Lp : (first + wb // nh) * Lp], wf[...])
        for w in span:
            at = t * wb + w
            valid = lens[i * plan.nw + at] - s * Lp
            v = y[(w - first) * Lp : (w - first + 1) * Lp]
            c2[w] = v
            edge[0, at] = v[:EDGE].astype(BF16)
            edge[1, at] = v[Lp - EDGE :].astype(BF16)
            v = jnp.where(rowh < valid, v, 0.0)
            sums0 = sums0 + fold(v)
            sums1 = sums1 + fold(v * v)
    acc[0:1, 0:H] += unfold(sums0)
    acc[0:1, H:] += unfold(sums1)

    @pl.when(first_step())
    def _():
        meet(peers.others)

    halo.start(t * wb, wb)

    @pl.when(last_step())
    def _():
        link[0][...] = acc[...]
        peers.start(link)
        keep_state(old, state)
        got = peers.finish(link)
        state[ST3 : ST3 + 1, 0:H] = got[:, 0:H]
        state[ST3 + 1 : ST3 + 2, 0:H] = got[:, H:]
        halo.finish()


def point_kernel(plan, lens, c2, x2, cot, w_ref, old, half_state,
                 res, res_other, dz, pgrad, land, state,
                 pw, a3s, a3T, dos, edge, acc, halo_sems, *link):
    t = pl.program_id(0)
    peers = group_peers(plan)
    halo = Halo(plan, edge, land, halo_sems)
    s, z, i, h = plan.place()
    Lp, C, H, wb, cs = plan.Lp, plan.C, plan.H, plan.wb, plan.cs
    M = wb * Lp

    @pl.when(first_step())
    def _():
        greet(peers.others)
        acc[...] = jnp.zeros_like(acc)
        for c in range(2):
            pw[:, c * (C // 2) : (c + 1) * (C // 2)] = w_ref[c, 0]

    @pl.when(t < plan.steps)
    def _():
        mean, rho = norm_of(old[ST3 : ST3 + 2, 0:H], total_of(lens))
        scale = old[GAIN3 : GAIN3 + 1, 0:H] * rho
        offset = old[SHIFT3 : SHIFT3 + 1, 0:H] - mean * scale
        shift = -mean * rho
        rowc = rows_of((Lp, C))
        rowh = rows_of((Lp, H))
        block = pl.ds(pl.multiple_of(t * M, 128), M)
        bias = jnp.zeros((8, C), F32)
        parts = []
        for w in range(wb):
            valid = lens[i * plan.nw + t * wb + w] - s * Lp
            d = jnp.where(rowc < valid, cot[w].astype(F32), 0.0)
            bias = bias + fold(d)
            parts.append(d.astype(BF16))
        d = jnp.concatenate(parts, axis=0)
        dos[block] = d
        da = mm_nt(d, pw[...])
        s0, s1 = jnp.zeros((8, H), F32), jnp.zeros((8, H), F32)
        parts = []
        for w in range(wb):
            at = t * wb + w
            valid = lens[i * plan.nw + at] - s * Lp
            top, end = w * Lp, (w + 1) * Lp
            v = c2[w]
            act, slope = gelu_both(v * scale + offset)
            parts.append(jnp.where(rowh < valid, act, 0.0).astype(BF16))
            dzw = da[top:end] * slope
            dz[w] = dzw
            edge[0, at] = dzw[:EDGE].astype(BF16)
            edge[1, at] = dzw[Lp - EDGE :].astype(BF16)
            s0 = s0 + fold(dzw)
            s1 = s1 + fold(dzw * (v * rho + shift))
        a3 = jnp.concatenate(parts, axis=0)
        a3s[block] = a3
        a3T[:, block] = a3.T
        acc[0:1, 0:H] += unfold(s0)
        acc[0:1, H : 2 * H] += unfold(s1)
        acc[1:2] += unfold(bias)

    @pl.when(first_step())
    def _():
        meet(peers.others)

    @pl.when(t < plan.steps)
    def _():
        halo.start(t * wb, wb)

    @pl.when(t == plan.steps - 1)
    def _():
        link[0][...] = acc[...]
        peers.start(link)

    @pl.when(t >= plan.steps)
    def _():
        u = t - plan.steps
        n = plan.nw // 2
        y = mm(a3s[pl.ds(pl.multiple_of(u * n * Lp, 128), n * Lp)], w_ref[h, 0])
        rowr = rows_of((Lp, y.shape[1]))
        for w in range(n):
            valid = lens[i * plan.nw + u * n + w] - s * Lp
            r = x2[w] + y[w * Lp : (w + 1) * Lp] + half_state[BIAS : BIAS + 1]
            r = jnp.where(rowr < valid, r, 0.0).astype(BF16).T
            res[w] = part_of(r, i, cs)
            for off in range(1, plan.g):
                res_other[off - 1, w] = part_of(r, wrap(i + off, plan.g), cs)

    @pl.when(last_step())
    def _():
        rows = pl.ds(pl.multiple_of(h * plan.Hh, 16), plan.Hh)
        pgrad[...] = mm(a3T[rows], dos[...]).astype(BF16)
        keep_state(old, state)
        got = peers.finish(link)
        state[SU3 : SU3 + 1, 0:H] = got[0:1, 0:H]
        state[SU3 + 1 : SU3 + 2, 0:H] = got[0:1, H : 2 * H]
        state[BSUM : BSUM + 1] = got[1:2]
        halo.finish()


def dilated_back_kernel(plan, lens, c2, cland, dz3, dland, x2, Y3, w_ref, old,
                        dz2, grads, land, state,
                        ext, Z3, wt, dcT, edge, acc, halo_sems, *link):
    t = pl.program_id(0)
    peers = group_peers(plan)
    halo = Halo(plan, edge, land, halo_sems)
    s, z, i, h = plan.place()
    Lp, C, H, wb, nw = plan.Lp, plan.C, plan.H, plan.wb, plan.nw

    @pl.when(first_step())
    def _():
        greet(peers.others)
        acc[...] = jnp.zeros_like(acc)
        for k in range(plan.T2):
            for c in range(2):
                cols = slice(c * (C // 2), (c + 1) * (C // 2))
                wt[k * H : (k + 1) * H, cols] = w_ref[c, k]

    @pl.when(t < plan.steps)
    def _():
        total = total_of(lens)
        mean3, rho3 = norm_of(old[ST3 : ST3 + 2, 0:H], total)
        gr3 = old[GAIN3 : GAIN3 + 1, 0:H] * rho3
        sg3 = old[SU3 : SU3 + 1, 0:H] / total
        gg3 = old[SU3 + 1 : SU3 + 2, 0:H] / total
        mean2, rho2 = norm_of(old[ST2 : ST2 + 2], total)
        scale2 = old[GAIN2 : GAIN2 + 1] * rho2
        offset2 = old[SHIFT2 : SHIFT2 + 1] - mean2 * scale2
        rowh = rows_of((Lp, H))
        rowe = rows_of((EDGE, H))
        rowc = rows_of((Lp, C))

        by_v = -gr3 * rho3 * gg3
        by_1 = gr3 * (mean3 * rho3 * gg3 - sg3)
        shift2 = -mean2 * rho2

        def back(dz, v):
            return gr3 * dz + by_v * v + by_1

        for w in range(wb):
            valid = lens[i * nw + t * wb + w] - s * Lp
            d = jnp.where(rowh < valid, back(dz3[w], c2[w]), 0.0)
            dl = back(dland[0, w].astype(F32), cland[0, w].astype(F32))
            dl = jnp.where((rowe - EDGE < valid) & (s > 0), dl, 0.0)
            dh = back(dland[1, w].astype(F32), cland[1, w].astype(F32))
            dh = jnp.where(rowe + Lp < valid, dh, 0.0)
            ext[w, 0:EDGE] = dl
            ext[w, EDGE : EDGE + Lp] = d
            ext[w, EDGE + Lp :] = dh
            top, end = w * Lp, (w + 1) * Lp
            Z3[top:end, 0:H] = ext[w, EDGE + DIL : EDGE + DIL + Lp].astype(BF16)
            Z3[top:end, H : 2 * H] = d.astype(BF16)
            Z3[top:end, 2 * H : 3 * H] = ext[w, EDGE - DIL : EDGE - DIL + Lp].astype(BF16)

        y = mm(Z3[...], wt[...])

        M = wb * Lp
        dcT[:, pl.ds(pl.multiple_of(t * M, 128), M)] = Z3[:, H : 2 * H].T
        s0, s1 = jnp.zeros((8, C), F32), jnp.zeros((8, C), F32)
        for w in range(wb):
            at = t * wb + w
            valid = lens[i * nw + at] - s * Lp
            v = x2[w]
            dzw = y[w * Lp : (w + 1) * Lp] * gelu_slope(v * scale2 + offset2)
            dzw = jnp.where(rowc < valid, dzw, 0.0)
            dz2[w] = dzw
            edge[0, pl.ds(at, 1)] = dzw[0:1]
            edge[1, pl.ds(at, 1)] = dzw[Lp - 1 : Lp]
            s0 = s0 + fold(dzw)
            s1 = s1 + fold(dzw * (v * rho2 + shift2))
        acc[0:1] += unfold(s0)
        acc[1:2] += unfold(s1)

    @pl.when(t == plan.steps - 1)
    def _():
        link[0][...] = acc[...]
        meet(peers.others)
        peers.start(link)
        halo.start(0, nw)

    @pl.when(t >= plan.steps)
    def _():
        rows = pl.ds(pl.multiple_of(h * plan.Hh, 16), plan.Hh)
        grads[...] = mm(dcT[rows], Y3[...]).astype(BF16)

    @pl.when(last_step())
    def _():
        keep_state(old, state)
        state[SU2 : SU2 + 2] = peers.finish(link)
        halo.finish()


class Reduction:
    def __init__(self, plan, batches, out, give, mine, got, spread, half, mate, sems):
        self.plan, self.batches, self.out = plan, batches, out
        self.give, self.mine, self.got, self.spread = give, mine, got, spread
        self.half, self.mate = half, mate
        self.sems = sems
        self.s, self.z, self.i, self.h = plan.place()
        self.c = lax.rem(self.s, 2)
        self.m = lax.div(self.s, 2)
        self.chips = plan.chips

    @staticmethod
    def scratch(plan, batches):
        taps, wide = plan.T1 + 2, plan.C // 2
        full = (taps, plan.chips, plan.g, plan.rb, wide)
        part = (taps, plan.g, plan.rb, wide)
        return [
            pltpu.VMEM((taps, 2, plan.chips, plan.rb, wide), BF16),
            *[pltpu.VMEM(full, BF16)] * 4,
            *[pltpu.VMEM(part, BF16)] * 2,
            pltpu.SemaphoreType.DMA((2, len(batches), 5)),
        ]

    def copy(self, b, phase, src, dst, device):
        return remote(src, dst, self.sems.at[0, b, phase], self.sems.at[1, b, phase], device)

    def finish(self, b, phase, ref, device):
        done = self.copy(b, phase, ref, ref, device)
        done.wait_recv()
        done.wait_send()

    def taps(self, b):
        return pl.ds(*self.batches[b])

    def pair(self):
        return (2 * self.m + (1 - self.c), self.z)

    def far(self, off):
        return (2 * wrap(self.m + off, self.chips) + self.c, self.z)

    def member(self, off):
        return (self.s, self.h * self.plan.g + wrap(self.i + off, self.plan.g))

    def put(self, k, rows):
        wide = self.plan.C // 2
        for j in range(self.plan.g):
            for m in range(self.chips):
                v = rows(j, m)
                left, right = v[:, :wide], v[:, wide:]
                self.mine[k, m, j] = jnp.where(self.c == 0, left, right).astype(BF16)
                self.give[k, m, j] = jnp.where(self.c == 0, right, left).astype(BF16)

    def step0(self, b):
        taps = self.taps(b)
        self.copy(b, 0, self.give.at[taps], self.got.at[taps], self.pair()).start()

    def step1(self, b):
        taps = self.taps(b)
        self.finish(b, 0, self.got.at[taps], self.pair())
        first, count = self.batches[b]
        for k in range(first, first + count):
            v = self.mine[k].astype(F32) + self.got[k].astype(F32)
            self.mine[k] = v.astype(BF16)
        for off in range(1, self.chips):
            src = self.mine.at[taps, wrap(self.m + off, self.chips)]
            self.copy(b, 1, src, self.spread.at[taps, self.m], self.far(off)).start()

    def step2(self, b):
        taps = self.taps(b)
        self.finish(b, 1, self.spread.at[taps, pl.ds(0, self.chips - 1)], self.far(1))
        first, count = self.batches[b]
        for k in range(first, first + count):
            self.spread[k, self.m] = self.mine[k, self.m]
            v = self.spread[k, 0].astype(F32)
            for n in range(1, self.chips):
                v = v + self.spread[k, n].astype(F32)
            self.half[k] = v.astype(BF16)
        for off in range(1, self.plan.g):
            src = self.half.at[taps, wrap(self.i + off, self.plan.g)]
            self.copy(b, 2, src, self.mate.at[taps, off], self.member(off)).start()

    def step3(self, b):
        taps = self.taps(b)
        self.finish(b, 2, self.mate.at[taps, pl.ds(1, self.plan.g - 1)], self.member(1))
        first, count = self.batches[b]
        for k in range(first, first + count):
            v = self.half[k, self.i].astype(F32)
            for off in range(1, self.plan.g):
                v = v + self.mate[k, off].astype(F32)
            self.out[k, self.c, self.m] = v.astype(BF16)
        mine = self.out.at[taps, self.c, self.m]
        for off in range(1, self.chips):
            self.copy(b, 3, mine, mine, self.far(off)).start()

    def step4(self, b):
        taps = self.taps(b)
        self.finish(b, 3, self.out.at[taps, self.c, pl.ds(0, self.chips - 1)], self.far(1))
        mine = self.out.at[taps, self.c]
        self.copy(b, 4, mine, mine, self.pair()).start()

    def step5(self, b):
        self.finish(b, 4, self.out.at[self.taps(b), self.c], self.pair())


def conv_back_kernel(plan, lens, dz2, dzland, x2, x2land, cot, beyond, x, taps, old, half_state,
                     gz, gz_other, dT, sums,
                     ext, D3, wcat, pick, eye, cols, y, acc):
    t = pl.program_id(0)
    s, z, i, h = plan.place()
    L, Lp, C, wb, g, nw = plan.L, plan.Lp, plan.C, plan.wb, plan.g, plan.nw
    Ch, cs = plan.Ch, plan.cs
    M = wb * Lp

    @pl.when(first_step())
    def _():
        acc[...] = jnp.zeros_like(acc)
        pick[...] = pick_matrix(L)
        eye[...] = eye_matrix(Ch, Ch, 0)
        mean, rho = norm_of(half_state[ST1 : ST1 + 2], 2.0 * total_of(lens))
        scale = half_state[GAIN1 : GAIN1 + 1] * rho
        offset = half_state[SHIFT1 : SHIFT1 + 1] - mean * scale
        for k, row in enumerate((scale, offset, rho, -mean * rho)):
            cols[k] = column(row, L)
        for first in range(0, Ch, 64):
            rows = slice(first, min(first + 64, Ch))
            for r, parts in enumerate((((0,), (1, 2), (3, 4)), ((0, 1), (2, 3), (4,)))):
                for k, which in enumerate(parts):
                    v = taps[which[0], rows]
                    if len(which) > 1:
                        v = (v.astype(F32) + taps[which[1], rows].astype(F32)).astype(BF16)
                    at = r * Ch
                    wcat[at + rows.start : at + rows.stop, k * C : (k + 1) * C] = v

    total = total_of(lens)
    mean, rho = norm_of(old[ST2 : ST2 + 2], total)
    gr = old[GAIN2 : GAIN2 + 1] * rho
    sg = old[SU2 : SU2 + 1] / total
    gg = old[SU2 + 1 : SU2 + 2] / total
    rowc = rows_of((Lp, C))
    row1 = rows_of((1, C))

    by_dz = 0.5 * gr
    by_v = -0.5 * gr * rho * gg
    by_1 = 0.5 * gr * (mean * rho * gg - sg)

    def back(dout, dz, v):
        return 0.5 * dout + by_dz * dz + by_v * v + by_1

    def grad_of(w):
        at = t * wb + w
        valid = lens[i * nw + at] - s * Lp
        d = back(cot[w].astype(F32), dz2[w], x2[w])
        d = jnp.where(rowc < valid, d, 0.0)
        one = pl.ds(at, 1)
        dl = back(beyond[0, 2, one, :], dzland[0, one, :], x2land[0, w, EDGE - 1 : EDGE].astype(F32))
        dl = jnp.where((row1 - 1 < valid) & (s > 0), dl, 0.0)
        dh = back(beyond[1, 2, one, :], dzland[1, one, :], x2land[1, w, 0:1].astype(F32))
        dh = jnp.where(row1 + Lp < valid, dh, 0.0)
        ext[w, 7:8] = dl
        ext[w, 8 : 8 + Lp] = d
        ext[w, 8 + Lp : 9 + Lp] = dh
        top, end = w * Lp, (w + 1) * Lp
        D3[top:end, 0:C] = ext[w, 9 : 9 + Lp].astype(BF16)
        D3[top:end, C : 2 * C] = d.astype(BF16)
        D3[top:end, 2 * C : 3 * C] = ext[w, 7 : 7 + Lp].astype(BF16)

    for w in range(wb):
        grad_of(w)
    half = D3[:, pl.ds(pl.multiple_of(C + h * Ch, 128), Ch)]
    dT[:, pl.ds(pl.multiple_of(t * M, 128), M)] = half.T

    lanes = lanes_of((Ch, L))

    def through(w):
        valid = 2 * lens[i * nw + t * wb + w] - s * L
        top, end = w * Lp, (w + 1) * Lp
        v = mm_nt(eye[...], x[w])
        da = jnp.concatenate([y[0:Ch, top:end], y[Ch:, top:end]], axis=1)
        da = mm(da.astype(BF16), pick[...])
        dzw = da * gelu_slope(v * cols[0] + cols[1])
        dzw = jnp.where(lanes < valid, dzw, 0.0)
        acc[0] += dzw
        acc[1] += dzw * (v * cols[2] + cols[3])
        dzw = dzw.astype(BF16)
        gz[w] = part_of(dzw, i, cs)
        for off in range(1, g):
            gz_other[off - 1, w] = part_of(dzw, wrap(i + off, g), cs)

    nh = 2 if wb % 2 == 0 and wb * Lp // 2 % 128 == 0 else 1
    n = wb // nh
    for hf in range(nh):
        rows = slice(hf * n * Lp, (hf + 1) * n * Lp)
        y[:, rows] = mm_nt(wcat[...], D3[rows])
        for w in range(hf * n, (hf + 1) * n):
            through(w)

    @pl.when(last_step())
    def _():
        sums[0:1] = unfold(acc[0].T)
        sums[1:2] = unfold(acc[1].T)


def grad_batches(plan):
    return [(plan.T1, 2)] + [(k, min(2, plan.T1 - k)) for k in range(0, plan.T1, 2)]


def conv_grad_kernel(plan, lens, X5, dT, grads, pgrad, partial_sums, gz,
                     gz_got, sums, summed, own_sem, bulk_sems, *rest):
    t = pl.program_id(0)
    s, z, i, h = plan.place()
    C, g, nw, wb, cs, T1 = plan.C, plan.g, plan.nw, plan.wb, plan.cs, plan.T1
    last = T1 - 1
    peers = group_peers(plan)
    batches = grad_batches(plan)
    red = Reduction(plan, batches, *rest[:8])
    link = rest[8:]
    first = nw - nw // 4

    def send(off, at, count):
        rows = pl.ds(at, count)
        return remote(
            gz.at[off - 1, rows],
            gz_got.at[off - 1, rows],
            bulk_sems.at[0, off],
            bulk_sems.at[1, off],
            (s, h * g + wrap(i + off, g)),
        )

    def when(at):
        return pl.when(t == min(at, last))

    @when(0)
    def _():
        greet(peers.others)
        hs = plan.H // plan.nz
        rb = plan.rb
        for u in range(2):

            def rows(j, m, u=u):
                side, r = m * rb // hs, m * rb % hs
                n = 2 * side + u
                rows = slice(j * hs + r, j * hs + r + rb)
                v = grads[rows, n * C : (n + 1) * C] if n < plan.T2 else pgrad[rows]
                return v.astype(F32)

            red.put(T1 + u, rows)
        meet(peers.others)
        red.step0(0)
        packet = link[0]
        packet[...] = jnp.zeros_like(packet)
        packet[:, 0 : plan.Ch] = partial_sums[...]
        peers.start(link)
        for off in range(1, g):
            send(off, 0, first).start()

    tap = mm(dT[...], X5[...])
    rb = plan.rb
    red.put(t, lambda j, m: tap[j * cs + m * rb : j * cs + (m + 1) * rb])

    for at, step, batch in (
        (1, red.step0, 1),
        (1, red.step1, 0),
        (2, red.step1, 1),
        (3, red.step0, 2),
        (3, red.step2, 0),
        (4, red.step0, 3),
        (4, red.step1, 2),
    ):

        @when(at)
        def _():
            step(batch)

    @when(last)
    def _():
        red.step2(1)
        red.step1(3)
        red.step2(2)
        red.step2(3)
        for off in range(1, g):
            send(off, first, nw - first).start()
        for b in range(len(batches)):
            red.step3(b)
            if b:
                red.step4(b - 1)
        red.step4(len(batches) - 1)
        sums[...] = peers.finish(link)[:, 0 : plan.Ch]
        for b in range(len(batches)):
            red.step5(b)
        own = pltpu.make_async_copy(red.out, summed, own_sem)
        own.start()
        for off in range(1, g):
            done = send(off, 0, nw)
            done.wait_recv()
            done.wait_send()
        own.wait()


def input_grad_kernel(plan, wg, lens, x, gz, gz_got, sums, res, res_got, summed,
                      state, half_state,
                      out, out_result, conv_grad, dil_grad, point_grad,
                      g1, b1, g2, b2, g3, b3, pb, eye, cols, xt):
    t = pl.program_id(0)
    s, z, i, h = plan.place()
    L, Ch, cs = plan.L, plan.Ch, plan.cs
    turn = plan.nw // wg
    mine = pl.ds(pl.multiple_of(i * cs, 16), cs)

    @pl.when(first_step())
    def _():
        n = 2.0 * total_of(lens)
        mean, rho = norm_of(half_state[ST1 : ST1 + 2], n)
        gr = half_state[GAIN1 : GAIN1 + 1] * rho
        gg = sums[1:2] / n * rho
        for k, row in enumerate((gr, -gr * gg, gr * (mean * gg - sums[0:1] / n))):
            xt[...] = column(row, L)
            cols[k] = xt[mine]
        eye[...] = eye_matrix(cs, Ch, i * cs)

        def mine_of(src, at, which, count, *dsts):
            n = dsts[0].shape[1]
            for k in range(count):

                @pl.when(which == k)
                def _():
                    for dst, r in zip(dsts, at):
                        dst[...] = src[r : r + 1, k * n : (k + 1) * n]

        mine_of(sums, (1, 0), i, plan.g, g1, b1)
        mine_of(state, (SU2 + 1, SU2), z, plan.nz, g2, b2)
        mine_of(state, (SU3 + 1, SU3), z, plan.nz, g3, b3)
        mine_of(state, (BSUM,), z, plan.nz, pb)

    own = lax.div(t, turn) == i
    for w in range(wg):
        out_result[w] = jnp.where(own, res[w], res_got[0, w])

    C, T1, hs, rb, wide = plan.C, plan.T1, plan.H // plan.nz, plan.rb, plan.C // 2
    count = plan.NW // wg
    turns = min(count, plan.chips)
    per, every = plan.chips // turns, count // turns

    def spread(chunk):
        for n in range(per):
            m = chunk * per + n
            side, r = m * rb // hs, m * rb % hs
            for c in range(2):
                at = slice(c * wide, (c + 1) * wide)
                for k in range(T1):
                    conv_grad[k, n * rb : (n + 1) * rb, at] = summed[k, c, n].astype(F32)
                for u in range(2):
                    v = summed[T1 + u, c, n].astype(F32)
                    if 2 * side + u < plan.T2:
                        dil_grad[2 * side + u, r : r + rb, at] = v
                    else:
                        point_grad[r : r + rb, at] = v

    for chunk in range(turns):
        pl.when(t == chunk * every)(partial(spread, chunk))

    lanes = lanes_of((cs, L))
    for w in range(wg):
        valid = 2 * lens[t * wg + w] - s * L
        v = mm_nt(eye[...], x[w])
        dz = jnp.where(own, gz[w], gz_got[0, w]).astype(F32)
        r = cols[0] * dz + v * cols[1] + cols[2]
        out[w] = jnp.where(lanes < valid, r, 0.0).astype(BF16)


def call(kernel, plan, name, steps, ins, outs, scratch, flops, nbytes, cid=None):
    extra = {} if cid is None else dict(collective_id=cid, has_side_effects=True)
    return pl.pallas_call(
        partial(kernel, plan),
        grid=(steps,),
        in_specs=[SMEM] + [spec for spec, _ in ins],
        out_specs=[spec for spec, _, _ in outs],
        out_shape=[jax.ShapeDtypeStruct(shape, dtype) for _, shape, dtype in outs],
        scratch_shapes=scratch,
        compiler_params=pltpu.CompilerParams(vmem_limit_bytes=VMEM_LIMIT, **extra),
        cost_estimate=pl.CostEstimate(
            flops=int(flops), bytes_accessed=int(nbytes), transcendentals=0
        ),
        name=name,
    )


def per_device(
    inputs,
    lengths,
    input_gain,
    input_shift,
    conv_weight,
    branch_gain,
    branch_shift,
    dilated_tap_weight,
    mixer_gain,
    mixer_shift,
    point_weight,
    point_bias,
    cotangent,
):
    NW, L, C = inputs.shape
    Lp = L // 2
    nz = lax.axis_size("ch")
    R = 2
    plan = Plan(
        ns=lax.axis_size("seq"),
        nz=nz,
        R=R,
        NW=NW,
        L=L,
        C=C,
        H=mixer_gain.shape[0] * nz,
        T1=conv_weight.shape[0],
        T2=dilated_tap_weight.shape[0],
        wb=min(NW * R // nz, max(1, 512 // Lp)),
    )
    g, nw, cs, Ch, H, Hh, wb = plan.g, plan.nw, plan.cs, plan.Ch, plan.H, plan.Hh, plan.wb
    T1, T2, steps = plan.T1, plan.T2, plan.steps
    M = wb * Lp
    hs = H // nz
    lens = lengths.astype(jnp.int32)

    def row(a):
        return a.reshape(1, a.shape[0])

    def grp():
        return lax.rem(lax.axis_index("ch"), g)

    def half():
        return lax.div(lax.axis_index("ch"), g)

    def core():
        return lax.rem(lax.axis_index("seq"), 2)

    def chip4():
        return lax.div(lax.axis_index("seq"), plan.ns // 4)

    def whole(*shape):
        return pl.BlockSpec(shape, lambda t: (0,) * len(shape), pipeline_mode=pl.Buffered(1))

    def const(*shape):
        return pl.BlockSpec(shape, lambda t: (0,) * len(shape))

    def win(*shape):
        return pl.BlockSpec(shape, lambda t: (t,) + (0,) * (len(shape) - 1))

    def arg_win(n, width):
        return pl.BlockSpec((wb, n, width), lambda t: (grp() * steps + t, 0, 0))

    def ins(*pairs):
        return [p for p in pairs]

    share = NW // nz
    nm = max(1, share // wb)

    def edge_spec(n):
        return pl.BlockSpec(
            (nw, 16, C), lambda t: (grp(), n, 0), pipeline_mode=pl.Buffered(1)
        )

    def head_block(t):
        own = lax.div(lax.axis_index("ch") * share, wb) + t
        return jnp.where(t < nm, own, grp() * steps + t - nm), 0, 0

    def after(*shape):
        return pl.BlockSpec(
            shape, lambda t: (jnp.maximum(t - nm, 0),) + (0,) * (len(shape) - 1)
        )

    pairs = ins(
        (pl.BlockSpec((wb, L, C), head_block), inputs),
        (edge_spec(0), inputs),
        (edge_spec(L // 16 - 1), inputs),
        (edge_spec(0), cotangent),
        (edge_spec(Lp // 16 - 1), cotangent),
        (whole(1, cs), row(branch_gain)),
        (whole(1, cs), row(branch_shift)),
        (whole(1, cs), row(point_bias)),
        (whole(1, H // nz), row(mixer_gain)),
        (whole(1, H // nz), row(mixer_shift)),
        (ANY, conv_weight.reshape(T1 * C, C)),
        (whole(C), input_gain),
        (whole(C), input_shift),
        (
            pl.BlockSpec(
                (1, hs, C // 2),
                lambda t: (jnp.minimum(chip4(), T2 - 1), 0, core()),
                pipeline_mode=pl.Buffered(1),
            ),
            jnp.swapaxes(dilated_tap_weight, 1, 2),
        ),
        (
            pl.BlockSpec(
                (hs, C // 2), lambda t: (0, core()), pipeline_mode=pl.Buffered(1)
            ),
            point_weight,
        ),
    )
    plane, line, group = plane_peers(plan), line_peers(plan), group_peers(plan)
    state_shape = (STATE, C)
    edges2, edges3 = (2, nw, EDGE, C), (2, nw, EDGE, H)
    X5, x2, land2, state, beyond, full = call(
        lambda plan, *refs: head_kernel(plan, nm, *refs),
        plan,
        "head",
        nm + steps,
        pairs,
        [
            (after(M, T1 * C), (nw * Lp, T1 * C), BF16),
            (after(wb, Lp, C), (nw, Lp, C), F32),
            (ANY, edges2, BF16),
            (const(*state_shape), state_shape, F32),
            (const(2, 3, nw, C), (2, 3, nw, C), F32),
            (ANY, (2, T2 + 1, nz, hs, C // 2), BF16),
        ],
        [
            pltpu.VMEM((2, 8, C), F32),
            pltpu.VMEM((2, 3, nw, C), F32),
            pltpu.VMEM((2, 3, nw, C), F32),
            pltpu.VMEM((T1 * Lp, L), BF16),
            pltpu.VMEM(edges2, BF16),
            pltpu.VMEM((2, C), F32),
            pltpu.VMEM((T1 * C, C), BF16),
            pltpu.SemaphoreType.DMA,
            pltpu.VMEM((hs, C // 2), BF16),
            pltpu.SemaphoreType.DMA((2, 4)),
            HALO_SEMS,
            HALO_SEMS,
        ]
        + plane.scratch(2, C)
        + line.scratch(3, C)
        + group.scratch(2, C),
        2 * nw * Lp * T1 * C * C,
        nw * Lp * C * 20,
        cid=1,
    )(lens, *[a for _, a in pairs])

    full = full.reshape(2, T2 + 1, H, C // 2)
    taps_spec = whole(2, T2, H, C // 2)
    pw_spec = pl.BlockSpec(
        (2, 1, H, C // 2), lambda t: (0, T2, 0, 0), pipeline_mode=pl.Buffered(1)
    )

    def early(*shape):
        return pl.BlockSpec(
            shape, lambda t: (jnp.minimum(t, steps - 1),) + (0,) * (len(shape) - 1)
        )

    def early_land(width):
        return pl.BlockSpec(
            (2, wb, EDGE, width), lambda t: (0, jnp.minimum(t, steps - 1), 0, 0)
        )

    def late(t):
        return jnp.maximum(t - steps, 0)

    def half_of(n):
        return pl.BlockSpec((n, Ch), lambda t: (0, half()), pipeline_mode=pl.Buffered(1))

    cot_spec = pl.BlockSpec(
        (wb, Lp, C), lambda t: (grp() * steps + jnp.minimum(t, steps - 1), 0, 0)
    )

    pairs = ins(
        (early(wb, Lp, C), x2),
        (early_land(C), land2),
        (taps_spec, full),
        (whole(*state_shape), state),
    )
    Y3, c2, land3, state = call(
        dilated_kernel,
        plan,
        "dilated",
        steps,
        pairs,
        [
            (win(M, T2 * C), (nw * Lp, T2 * C), BF16),
            (win(wb, Lp, H), (nw, Lp, H), F32),
            (ANY, edges3, BF16),
            (const(*state_shape), state_shape, F32),
        ],
        [
            pltpu.VMEM((wb, Lp + 2 * EDGE, C), F32),
            pltpu.VMEM((H, T2 * C), BF16),
            pltpu.VMEM(edges3, BF16),
            pltpu.VMEM((1, 2 * H), F32),
            HALO_SEMS,
        ]
        + group.scratch(1, 2 * H),
        2 * nw * Lp * T2 * C * H,
        nw * Lp * C * 12,
        cid=3,
    )(lens, *[a for _, a in pairs])

    pairs = ins(
        (early(wb, Lp, H), c2),
        (pl.BlockSpec((nw // 2, Lp, Ch), lambda t: (late(t), 0, half())), x2),
        (cot_spec, cotangent),
        (pw_spec, full),
        (whole(*state_shape), state),
        (half_of(STATE), state),
    )
    res, res_other, dz3, pgrad, dland3, state = call(
        point_kernel,
        plan,
        "point",
        steps + 2,
        pairs,
        [
            (pl.BlockSpec((nw // 2, cs, Lp), lambda t: (late(t), 0, 0)), (nw, cs, Lp), BF16),
            (
                pl.BlockSpec((g - 1, nw // 2, cs, Lp), lambda t: (0, late(t), 0, 0)),
                (g - 1, nw, cs, Lp),
                BF16,
            ),
            (early(wb, Lp, H), (nw, Lp, H), F32),
            (const(Hh, C), (Hh, C), BF16),
            (ANY, edges3, BF16),
            (const(*state_shape), state_shape, F32),
        ],
        [
            pltpu.VMEM((H, C), BF16),
            pltpu.VMEM((nw * Lp, H), BF16),
            pltpu.VMEM((H, nw * Lp), BF16),
            pltpu.VMEM((nw * Lp, C), BF16),
            pltpu.VMEM(edges3, BF16),
            pltpu.VMEM((2, C), F32),
            HALO_SEMS,
        ]
        + group.scratch(2, C),
        5 * nw * Lp * C * H,
        nw * Lp * C * 10,
        cid=4,
    )(lens, *[a for _, a in pairs])

    pairs = ins(
        (early(wb, Lp, H), c2),
        (early_land(H), land3),
        (early(wb, Lp, H), dz3),
        (early_land(H), dland3),
        (early(wb, Lp, C), x2),
        (pl.BlockSpec((nw * Lp, C), lambda t: (0, late(t))), Y3),
        (taps_spec, full),
        (whole(*state_shape), state),
    )
    dz2, grads, dland2, state = call(
        dilated_back_kernel,
        plan,
        "dilated_back",
        steps + T2,
        pairs,
        [
            (early(wb, Lp, C), (nw, Lp, C), F32),
            (pl.BlockSpec((Hh, C), lambda t: (0, late(t))), (Hh, T2 * C), BF16),
            (ANY, (2, nw, C), F32),
            (const(*state_shape), state_shape, F32),
        ],
        [
            pltpu.VMEM((wb, Lp + 2 * EDGE, H), F32),
            pltpu.VMEM((M, T2 * H), BF16),
            pltpu.VMEM((T2 * H, C), BF16),
            pltpu.VMEM((H, nw * Lp), BF16),
            pltpu.VMEM((2, nw, C), F32),
            pltpu.VMEM((2, C), F32),
            HALO_SEMS,
        ]
        + group.scratch(2, C),
        4 * nw * Lp * T2 * C * H,
        nw * Lp * C * 20,
        cid=5,
    )(lens, *[a for _, a in pairs])

    def ring(off):
        return [(b * g + j, b * g + (j + off) % g) for b in range(R) for j in range(g)]

    res_other, dz2 = lax.optimization_barrier((res_other, dz2))
    res_got = [lax.ppermute(res_other[off - 1], "ch", ring(off)) for off in range(1, g)]
    res_got = res_got[0][None] if g == 2 else jnp.stack(res_got)

    pairs = ins(
        (win(wb, Lp, C), dz2),
        (whole(2, nw, C), dland2),
        (win(wb, Lp, C), x2),
        (pl.BlockSpec((2, wb, EDGE, C), lambda t: (0, t, 0, 0)), land2),
        (arg_win(Lp, C), cotangent),
        (whole(2, 3, nw, C), beyond),
        (pl.BlockSpec((wb, L, Ch), lambda t: (grp() * steps + t, 0, half())), inputs),
        (
            pl.BlockSpec(
                (T1, Ch, C), lambda t: (0, half(), 0), pipeline_mode=pl.Buffered(1)
            ),
            conv_weight,
        ),
        (whole(*state_shape), state),
        (half_of(STATE), state),
    )
    gz, gz_other, dT, partial_sums = call(
        conv_back_kernel,
        plan,
        "conv_back",
        steps,
        pairs,
        [
            (win(wb, cs, L), (nw, cs, L), BF16),
            (
                pl.BlockSpec((g - 1, wb, cs, L), lambda t: (0, t, 0, 0)),
                (g - 1, nw, cs, L),
                BF16,
            ),
            (const(Ch, nw * Lp), (Ch, nw * Lp), BF16),
            (const(2, Ch), (2, Ch), F32),
        ],
        [
            pltpu.VMEM((wb, Lp + 16, C), F32),
            pltpu.VMEM((M, 3 * C), BF16),
            pltpu.VMEM((2 * Ch, 3 * C), BF16),
            pltpu.VMEM((L, L), BF16),
            pltpu.VMEM((Ch, Ch), BF16),
            pltpu.VMEM((4, Ch, L), F32),
            pltpu.VMEM((2 * Ch, M), F32),
            pltpu.VMEM((2, Ch, L), F32),
        ],
        2 * nw * Lp * 6 * C * Ch,
        nw * Lp * C * 20,
    )(lens, *[a for _, a in pairs])

    chips, rb = plan.chips, plan.rb
    sshape = (T1 + 2, 2, chips, rb, C // 2)
    pairs = ins(
        (pl.BlockSpec((nw * Lp, C), lambda t: (0, t)), X5),
        (whole(Ch, nw * Lp), dT),
        (whole(Hh, T2 * C), grads),
        (whole(Hh, C), pgrad),
        (whole(2, Ch), partial_sums),
        (ANY, gz_other),
    )
    gz_got, sums1, summed = call(
        conv_grad_kernel,
        plan,
        "conv_grad",
        T1,
        pairs,
        [
            (ANY, (g - 1, nw, cs, L), BF16),
            (const(2, Ch), (2, Ch), F32),
            (ANY, sshape, BF16),
        ],
        [pltpu.SemaphoreType.DMA, pltpu.SemaphoreType.DMA((2, g))]
        + Reduction.scratch(plan, grad_batches(plan))
        + group.scratch(2, C),
        2 * nw * Lp * T1 * C * Ch,
        nw * Lp * C * 12,
        cid=6,
    )(lens, *[a for _, a in pairs])

    wg = min(2 * wb, nw)
    count = NW // wg
    turn = nw // wg
    turns = min(count, chips)

    def own_block(t):
        return jnp.where(lax.div(t, turn) == grp(), lax.rem(t, turn), 0)

    def got_slot(t):
        off = lax.rem(grp() - lax.div(t, turn) + g, g)
        return jnp.maximum(off - 1, 0), jnp.where(off > 0, lax.rem(t, turn), 0)

    pairs = ins(
        (pl.BlockSpec((wg, L, Ch), lambda t: (t, 0, half())), inputs),
        (pl.BlockSpec((wg, cs, L), lambda t: (own_block(t), 0, 0)), gz),
        (pl.BlockSpec((1, wg, cs, L), lambda t: got_slot(t) + (0, 0)), gz_got),
        (whole(2, Ch), sums1),
        (pl.BlockSpec((wg, cs, Lp), lambda t: (own_block(t), 0, 0)), res),
        (pl.BlockSpec((1, wg, cs, Lp), lambda t: got_slot(t) + (0, 0)), res_got),
        (
            pl.BlockSpec(
                (T1 + 2, 2, chips // turns, rb, C // 2),
                lambda t: (0, 0, t * turns // count, 0, 0),
            ),
            summed,
        ),
        (whole(*state_shape), state),
        (half_of(STATE), state),
    )
    outs = call(
        lambda plan, *refs: input_grad_kernel(plan, wg, *refs),
        plan,
        "input_grad",
        count,
        pairs,
        [
            (win(wg, cs, L), (NW, cs, L), BF16),
            (win(wg, cs, Lp), (NW, cs, Lp), BF16),
            (
                pl.BlockSpec((T1, cs // turns, C), lambda t: (0, t * turns // count, 0)),
                (T1, cs, C),
                F32,
            ),
            (const(T2, hs, C), (T2, hs, C), F32),
            (const(hs, C), (hs, C), F32),
        ]
        + [(const(1, n), (1, n), F32) for n in (cs, cs, cs, cs, hs, hs, cs)],
        [
            pltpu.VMEM((cs, Ch), BF16),
            pltpu.VMEM((3, cs, L), F32),
            pltpu.VMEM((Ch, L), F32),
        ],
        2 * NW * L * Ch * cs,
        NW * L * cs * 8,
    )(lens, *[a for _, a in pairs])
    grad, result, conv_grad, dil_grad, point_grad = outs[:5]
    g1, b1, g2, b2, g3, b3, pb = [a[0] for a in outs[5:]]
    return (
        jnp.swapaxes(result, 1, 2),
        jnp.swapaxes(grad, 1, 2),
        jnp.swapaxes(conv_grad, 1, 2),
        g1,
        b1,
        g2,
        b2,
        jnp.swapaxes(dil_grad, 1, 2),
        g3,
        b3,
        point_grad,
        pb,
    )


def solution(mesh):
    in_specs = (
        P(None, "seq", None),
        P(),
        P(),
        P(),
        P(),
        P("ch"),
        P("ch"),
        P(None, None, "ch"),
        P("ch"),
        P("ch"),
        P("ch", None),
        P("ch"),
        P(None, "seq", None),
    )
    out_specs = (
        P(None, "seq", "ch"),
        P(None, "seq", "ch"),
        P(None, None, "ch"),
        P("ch"),
        P("ch"),
        P("ch"),
        P("ch"),
        P(None, None, "ch"),
        P("ch"),
        P("ch"),
        P("ch", None),
        P("ch"),
    )
    return jax.shard_map(
        per_device, mesh=mesh, in_specs=in_specs, out_specs=out_specs, check_vma=False
    )
```

```python
from functools import partial
from typing import NamedTuple

import jax
import jax.numpy as jnp
from jax import lax
from jax.experimental import pallas as pl
from jax.experimental.pallas import tpu as pltpu
from jax.sharding import PartitionSpec as P

DIL = 14
EDGE = 16
EPS = 1e-05
GC0 = 0.7978845608028654
GC1 = 0.044715
F32 = jnp.float32
BF16 = jnp.bfloat16
MESH = pl.DeviceIdType.MESH
VMEM_LIMIT = 58 * 1024 * 1024
ANY = pl.BlockSpec(memory_space=pl.ANY)
SMEM = pl.BlockSpec(memory_space=pltpu.SMEM)


ST1, GAIN2, SHIFT2, BIAS, GAIN3, SHIFT3, GAIN1, SHIFT1, ST2, ST3, SU3, BSUM, SU2 = (
    0, 2, 3, 4, 5, 6, 7, 8, 9, 11, 13, 15, 16
)
STATE = 24


class Plan(NamedTuple):
    ns: int
    nz: int
    R: int
    NW: int
    L: int
    C: int
    H: int
    T1: int
    T2: int
    wb: int

    @property
    def g(self):
        return self.nz // self.R

    @property
    def nw(self):
        return self.NW // self.g

    @property
    def Lp(self):
        return self.L // 2

    @property
    def cs(self):
        return self.C // self.nz

    @property
    def Ch(self):
        return self.C // self.R

    @property
    def Hh(self):
        return self.H // self.R

    @property
    def steps(self):
        return self.nw // self.wb

    @property
    def chips(self):
        return self.ns // 2

    @property
    def shares(self):
        if self.steps != 4:
            return self.steps, 0, 0
        return 1, 2, 1

    @property
    def rb(self):
        return self.cs // self.chips

    def place(self):
        s, z = lax.axis_index("seq"), lax.axis_index("ch")
        return s, z, lax.rem(z, self.g), lax.div(z, self.g)


def gelu(z):
    t = jnp.tanh(z * (GC0 + (GC0 * GC1) * (z * z)))
    return z * (0.5 + 0.5 * t)


def gelu_both(z):
    sq = z * z
    t = jnp.tanh(z * (GC0 + (GC0 * GC1) * sq))
    h = 0.5 + 0.5 * t
    v = z * h
    return v, h + v * (1.0 - t) * (GC0 + (3.0 * GC0 * GC1) * sq)


def gelu_slope(z):
    return gelu_both(z)[1]


def fold(v):
    return jnp.sum(v.reshape(v.shape[0] // 8, 8, v.shape[1]), axis=0)


def unfold(v):
    return jnp.sum(v, axis=0, keepdims=True)


def rows_of(shape):
    return lax.broadcasted_iota(jnp.int32, shape, 0)


def lanes_of(shape):
    return lax.broadcasted_iota(jnp.int32, shape, 1)


def total_of(lens):
    n = lens[0]
    for k in range(1, lens.shape[0]):
        n = n + lens[k]
    return n.astype(F32)


def norm_of(stats, total):
    mean = stats[0:1] / total
    square = stats[1:2] / total
    return mean, lax.rsqrt(square - mean * mean + EPS)


def flat(ref):
    return ref[...].reshape(1, ref.shape[0])


def column(row, n):
    return jnp.broadcast_to(row, (n, row.shape[1])).T


def mm(a, b):
    return jnp.dot(a, b, preferred_element_type=F32)


def mm_nt(a, b):
    return lax.dot_general(a, b, (((1,), (1,)), ((), ())), preferred_element_type=F32)


def mm_tn(a, b):
    return lax.dot_general(a, b, (((0,), (0,)), ((), ())), preferred_element_type=F32)


def mm_tt(a, b):
    return lax.dot_general(a, b, (((0,), (1,)), ((), ())), preferred_element_type=F32)


def eye_matrix(n, m, first):
    return jnp.where(lanes_of((n, m)) == rows_of((n, m)) + first, 1.0, 0.0).astype(BF16)


def pick_matrix(L):
    r, n = rows_of((L, L)), lanes_of((L, L))
    bin_of = 2 * r - jnp.where(r >= L // 2, L - 1, 0)
    return jnp.where(n == bin_of, 1.0, 0.0).astype(BF16)


def remote(src, dst, send, recv, device):
    return pltpu.make_async_remote_copy(
        src_ref=src,
        dst_ref=dst,
        send_sem=send,
        recv_sem=recv,
        device_id=device,
        device_id_type=MESH,
    )


def wrap(v, n):
    return jnp.where(v >= n, v - n, v)


def greet(devices):
    barrier = pltpu.get_barrier_semaphore()
    for device in devices:
        pl.semaphore_signal(barrier, inc=1, device_id=device, device_id_type=MESH)


def meet(devices):
    pl.semaphore_wait(pltpu.get_barrier_semaphore(), len(devices))


class Peers:
    def __init__(self, me, others):
        self.me, self.others = me, others
        self.count = len(others) + 1

    def start(self, link):
        packet, buf, sems = link
        for device in self.others:
            remote(packet, buf.at[self.me], sems.at[0], sems.at[1], device).start()

    def finish(self, link):
        packet, buf, sems = link
        buf[self.me] = packet[...]
        rest = buf.at[pl.ds(0, self.count - 1)]
        done = remote(rest, rest, sems.at[0], sems.at[1], self.others[0])
        done.wait_recv()
        acc = buf[0]
        for q in range(1, self.count):
            acc = acc + buf[q]
        done.wait_send()
        return acc

    def scratch(self, rows, width):
        return [
            pltpu.VMEM((rows, width), F32),
            pltpu.VMEM((self.count, rows, width), F32),
            pltpu.SemaphoreType.DMA((2,)),
        ]


def group_peers(plan):
    s, z, i, h = plan.place()
    g = plan.g
    others = [
        (wrap(s + a, plan.ns), h * g + wrap(i + b, g))
        for a in range(plan.ns)
        for b in range(g)
        if a or b
    ]
    return Peers(s * g + i, others)


def plane_peers(plan):
    s, z, i, h = plan.place()
    return Peers(s, [(wrap(s + a, plan.ns), z) for a in range(1, plan.ns)])


def line_peers(plan):
    s, z, i, h = plan.place()
    return Peers(z, [(s, wrap(z + a, plan.nz)) for a in range(1, plan.nz)])


class Halo:
    def __init__(self, plan, edge, land, sems):
        self.edge, self.land, self.sems = edge, land, sems
        s, z, _, _ = plan.place()
        self.to = ((wrap(s + plan.ns - 1, plan.ns), z), (wrap(s + 1, plan.ns), z))

    def copy(self, side, rows):
        return remote(
            self.edge.at[side, rows],
            self.land.at[1 - side, rows],
            self.sems.at[0, side],
            self.sems.at[1, side],
            self.to[side],
        )

    def start(self, first, count):
        for side in range(2):
            self.copy(side, pl.ds(first, count)).start()

    def finish(self):
        for side in range(2):
            done = self.copy(side, pl.ds(0, self.land.shape[1]))
            done.wait_recv()
            done.wait_send()


HALO_SEMS = pltpu.SemaphoreType.DMA((2, 2))


class Gather:
    def __init__(self, plan, part, full, sems):
        self.plan, self.part, self.full, self.sems = plan, part, full, sems
        self.s, self.z, self.i, self.h = plan.place()
        self.c, self.m = lax.rem(self.s, 2), lax.div(self.s, 2)
        self.chips = plan.chips
        self.every = self.chips // 4
        self.tap = lax.div(self.m, self.every)
        self.owner = lax.rem(self.m, self.every) == 0
        self.mine = full.at[self.c, self.tap]

    def others(self):
        g, nz = self.plan.g, self.plan.nz
        return [(self.s, wrap(self.h * g + g + r, nz)) for r in range(nz - g)]

    def far(self, off):
        return (2 * wrap(self.m + off, self.chips) + self.c, self.z)

    def own(self):
        return pltpu.make_async_copy(self.part, self.mine.at[self.z], self.sems.at[0, 0])

    def line(self, off):
        device = (self.s, wrap(self.z + off, self.plan.nz))
        return remote(
            self.part, self.mine.at[self.z], self.sems.at[0, 1], self.sems.at[1, 1], device
        )

    def chip(self, off):
        return remote(self.mine, self.mine, self.sems.at[0, 2], self.sems.at[1, 2], self.far(off))

    def pair(self):
        half = self.full.at[self.c]
        device = (2 * self.m + 1 - self.c, self.z)
        return remote(half, half, self.sems.at[0, 3], self.sems.at[1, 3], device)

    def line_start(self):
        @pl.when(self.owner)
        def _():
            self.own().start()
            for off in range(1, self.plan.nz):
                self.line(off).start()

    def line_finish(self):
        @pl.when(self.owner)
        def _():
            self.own().wait()
            rest = self.mine.at[pl.ds(0, self.plan.nz - 1)]
            device = (self.s, wrap(self.z + 1, self.plan.nz))
            done = remote(rest, rest, self.sems.at[0, 1], self.sems.at[1, 1], device)
            done.wait_recv()
            done.wait_send()

    def chips_start(self):
        @pl.when(self.owner)
        def _():
            for off in range(1, self.chips):
                self.chip(off).start()

    def pair_start(self):
        def taken(count):
            rest = self.full.at[self.c, pl.ds(0, count)]
            return remote(rest, rest, self.sems.at[0, 2], self.sems.at[1, 2], self.far(1))

        @pl.when(self.owner)
        def _():
            taken(3).wait_recv()
            for off in range(1, self.chips):
                self.chip(off).wait_send()

        if self.every > 1:

            @pl.when(jnp.logical_not(self.owner))
            def _():
                taken(4).wait_recv()

        self.pair().start()

    def pair_finish(self):
        done = self.pair()
        done.wait_recv()
        done.wait_send()


def first_step():
    return pl.program_id(0) == 0


def last_step():
    return pl.program_id(0) == pl.num_programs(0) - 1


def keep_state(old, new):
    new[...] = old[...]


def head_kernel(plan, nm, lens, x, xtop, xend, ctop, cend, g2, s2, pb, g3, s3,
                w_hbm, gain, shift, taps, pw,
                X5, x2, land, state, beyond_out, full,
                macc, beyond, xedge, sel, edge, acc, w_ref, w_sem, part,
                gather_sems, xhalo_sems, halo_sems, *links):
    t = pl.program_id(0)
    peers, plane, line = group_peers(plan), plane_peers(plan), line_peers(plan)
    xhalo = Halo(plan, xedge, beyond, xhalo_sems)
    halo = Halo(plan, edge, land, halo_sems)
    gather = Gather(plan, part, full, gather_sems)
    w_copy = pltpu.make_async_copy(w_hbm, w_ref, w_sem)
    plane_link, line_link, link = links[:3], links[3:6], links[6:]
    s, z, i, h = plan.place()
    L, Lp, C, nw, nz, wb = plan.L, plan.Lp, plan.C, plan.nw, plan.nz, plan.wb
    share = plan.NW // nz
    c = t - nm
    everyone = peers.others + gather.others()

    @pl.when(first_step())
    def _():
        w_copy.start()
        greet(everyone)
        part[...] = jnp.where(gather.tap == 3, pw[...], taps[0])
        macc[...] = jnp.zeros_like(macc)
        acc[...] = jnp.zeros_like(acc)
        state[...] = jnp.zeros_like(state)
        state[GAIN1 : GAIN1 + 1] = flat(gain)
        state[SHIFT1 : SHIFT1 + 1] = flat(shift)
        n16 = nw * 16
        for side, (xe, ce, places) in enumerate(
            ((xtop, ctop, (0, 1, 0)), (xend, cend, (14, 15, 15)))
        ):
            for k, at in enumerate(places):
                rows, lanes = rows_of((nw, n16)), lanes_of((nw, n16))
                one = jnp.where(lanes == 16 * rows + at, 1.0, 0.0).astype(BF16)
                block = (xe if k < 2 else ce)[...].reshape(n16, C)
                xedge[side, k] = mm(one, block)
        shape = (Lp, L)
        for k in range(plan.T1):
            at = lanes_of(shape) - (2 * rows_of(shape) + (k - 2))
            sel[k * Lp : (k + 1) * Lp] = jnp.where((at == 0) | (at == 1), 1.0, 0.0).astype(BF16)

    @pl.when(c < 0)
    def _():
        rows = rows_of((L, C))
        for w in range(min(share, wb)):
            at = lax.rem(z * share, wb) + w
            valid = 2 * lens[z * share + t * wb + w] - s * L
            v = jnp.where(rows < valid, x[at].astype(F32), 0.0)
            macc[0] += fold(v)
            macc[1] += fold(v * v)

    @pl.when(c == -1)
    def _():
        packet, more = plane_link[0], line_link[0]
        packet[0:1] = unfold(macc[0])
        packet[1:2] = unfold(macc[1])
        meet(everyone)
        plane.start(plane_link)
        xhalo.start(0, 3)
        at = 0
        spans = []
        more[2:3] = jnp.zeros((1, C), F32)
        for ref in (g2, s2, pb, g3, s3):
            n = ref.shape[1]
            more[2:3, at : at + n] = ref[...]
            spans.append((at, n))
            at += n
        more[0:2] = plane.finish(plane_link)
        line.start(line_link)
        gather.line_start()
        state[ST1 : ST1 + 2] = line.finish(line_link)[0:2]
        for k in range(nz):
            row = line_link[1][k]
            for r, (at, n) in zip((GAIN2, SHIFT2, BIAS, GAIN3, SHIFT3), spans):
                state[r : r + 1, k * n : (k + 1) * n] = row[2:3, at : at + n]
        xhalo.finish()
        beyond_out[...] = beyond[...]
        w_copy.wait()

    @pl.when(c >= 0)
    def _():
        mean, rho = norm_of(state[ST1 : ST1 + 2], 2.0 * total_of(lens))
        scale = state[GAIN1 : GAIN1 + 1] * rho
        offset = state[SHIFT1 : SHIFT1 + 1] - mean * scale
        rows = rows_of((L, C))
        row1 = rows_of((1, C))
        row16 = rows_of((16, C))
        def activate(w):
            at = c * wb + w
            valid = 2 * lens[i * nw + at] - s * L
            a = gelu(x[w].astype(F32) * scale + offset)
            a = jnp.where(rows < valid, a, 0.0).astype(BF16)
            picked = mm(sel[...], a)
            for k in range(5):
                X5[w * Lp : (w + 1) * Lp, k * C : (k + 1) * C] = picked[
                    k * Lp : (k + 1) * Lp
                ].astype(BF16)

            def beside(side, k, bin_at):
                a = gelu(beyond[side, k, pl.ds(at, 1), :] * scale + offset)
                here = (row1 + bin_at < valid) & (row1 + (s * L + bin_at) >= 0)
                return jnp.where(here, a, 0.0).astype(BF16).astype(F32)

            l0, l1 = beside(0, 0, -2), beside(0, 1, -1)
            r0, r1 = beside(1, 0, L), beside(1, 1, L + 1)
            top, end = w * Lp, (w + 1) * Lp
            for k, add in ((0, l0 + l1), (1, l1)):
                X5[top : top + 16, k * C : (k + 1) * C] = (
                    picked[k * Lp : k * Lp + 16] + jnp.where(row16 == 0, add, 0.0)
                ).astype(BF16)
            for k, add in ((3, r0), (4, r0 + r1)):
                X5[end - 16 : end, k * C : (k + 1) * C] = (
                    picked[(k + 1) * Lp - 16 : (k + 1) * Lp] + jnp.where(row16 == 15, add, 0.0)
                ).astype(BF16)

        nc = 256
        rowp = rows_of((Lp, nc))

        def convolve(first, count):
            span = slice(first * Lp, (first + count) * Lp)
            for n in range(C // nc):
                cols = slice(n * nc, (n + 1) * nc)
                y = 0.5 * mm(X5[span], w_ref[:, cols])
                s0 = jnp.zeros((8, nc), F32)
                s1 = jnp.zeros((8, nc), F32)
                for w in range(first, first + count):
                    at = c * wb + w
                    valid = lens[i * nw + at] - s * Lp
                    v = y[(w - first) * Lp : (w - first + 1) * Lp]
                    x2[w, :, cols] = v
                    edge[0, at, :, cols] = v[:EDGE].astype(BF16)
                    edge[1, at, :, cols] = v[Lp - EDGE :].astype(BF16)
                    v = jnp.where(rowp < valid, v, 0.0)
                    s0 = s0 + fold(v)
                    s1 = s1 + fold(v * v)
                acc[0:1, cols] += unfold(s0)
                acc[1:2, cols] += unfold(s1)

        count = max(1, wb // 2)
        for first in range(0, wb, count):
            for w in range(first, first + count):
                activate(w)
            convolve(first, count)
        halo.start(c * wb, wb)

    @pl.when(c == 0)
    def _():
        gather.line_finish()
        gather.chips_start()

    @pl.when(last_step())
    def _():
        link[0][...] = acc[...]
        peers.start(link)
        gather.pair_start()
        state[ST2 : ST2 + 2] = peers.finish(link)
        halo.finish()
        gather.pair_finish()


def dilated_kernel(plan, lens, x2, x2land, w_ref, old,
                   Y3, c2, land, state, ext, wf, edge, acc, halo_sems, *link):
    t = pl.program_id(0)
    peers = group_peers(plan)
    halo = Halo(plan, edge, land, halo_sems)
    s, z, i, h = plan.place()
    Lp, C, H, wb = plan.Lp, plan.C, plan.H, plan.wb

    @pl.when(first_step())
    def _():
        greet(peers.others)
        acc[...] = jnp.zeros_like(acc)
        for k in range(plan.T2):
            for c in range(2):
                at = k * C + c * (C // 2)
                wf[:, at : at + C // 2] = w_ref[c, k]

    mean, rho = norm_of(old[ST2 : ST2 + 2], total_of(lens))
    scale = old[GAIN2 : GAIN2 + 1] * rho
    offset = old[SHIFT2 : SHIFT2 + 1] - mean * scale
    rows = rows_of((Lp, C))
    rowe = rows_of((EDGE, C))

    rowh = rows_of((Lp, H))
    sums0, sums1 = jnp.zeros((8, H), F32), jnp.zeros((8, H), F32)
    nh = min(2, wb)
    for first in range(0, wb, wb // nh):
        span = range(first, first + wb // nh)
        for w in span:
            valid = lens[i * plan.nw + t * wb + w] - s * Lp
            a = jnp.where(rows < valid, gelu(x2[w] * scale + offset), 0.0)
            al = gelu(x2land[0, w].astype(F32) * scale + offset)
            al = jnp.where((rowe - EDGE < valid) & (s > 0), al, 0.0)
            ah = gelu(x2land[1, w].astype(F32) * scale + offset)
            ah = jnp.where(rowe + Lp < valid, ah, 0.0)
            ext[w, 0:EDGE] = al
            ext[w, EDGE : EDGE + Lp] = a
            ext[w, EDGE + Lp :] = ah
            top, end = w * Lp, (w + 1) * Lp
            Y3[top:end, 0:C] = ext[w, EDGE - DIL : EDGE - DIL + Lp].astype(BF16)
            Y3[top:end, C : 2 * C] = a.astype(BF16)
            Y3[top:end, 2 * C : 3 * C] = ext[w, EDGE + DIL : EDGE + DIL + Lp].astype(BF16)
        y = mm_nt(Y3[first * Lp : (first + wb // nh) * Lp], wf[...])
        for w in span:
            at = t * wb + w
            valid = lens[i * plan.nw + at] - s * Lp
            v = y[(w - first) * Lp : (w - first + 1) * Lp]
            c2[w] = v
            edge[0, at] = v[:EDGE].astype(BF16)
            edge[1, at] = v[Lp - EDGE :].astype(BF16)
            v = jnp.where(rowh < valid, v, 0.0)
            sums0 = sums0 + fold(v)
            sums1 = sums1 + fold(v * v)
    acc[0:1, 0:H] += unfold(sums0)
    acc[0:1, H:] += unfold(sums1)

    @pl.when(first_step())
    def _():
        meet(peers.others)

    halo.start(t * wb, wb)

    @pl.when(last_step())
    def _():
        link[0][...] = acc[...]
        peers.start(link)
        keep_state(old, state)
        got = peers.finish(link)
        state[ST3 : ST3 + 1, 0:H] = got[:, 0:H]
        state[ST3 + 1 : ST3 + 2, 0:H] = got[:, H:]
        halo.finish()


def point_kernel(plan, lens, c2, x2, cot, w_ref, old, half_state,
                 res, dz, pgrad, land, state, res_got,
                 pw, a3s, a3T, dos, edge, acc, halo_sems, bulk_sems, *link):
    t = pl.program_id(0)
    peers = group_peers(plan)
    halo = Halo(plan, edge, land, halo_sems)
    s, z, i, h = plan.place()
    Lp, C, H, wb, cs = plan.Lp, plan.C, plan.H, plan.wb, plan.cs
    M = wb * Lp
    g, steps, ahead = plan.g, plan.steps, plan.shares[0]

    def bulk(off, rows):
        to = wrap(i + off, g)
        return remote(
            res.at[to, rows],
            res_got.at[off, rows],
            bulk_sems.at[0, off],
            bulk_sems.at[1, off],
            (s, h * g + to),
        )

    def result_of(block):
        y = mm(a3s[pl.ds(pl.multiple_of(block * M, 128), M)], w_ref[h, 0])
        rowr = rows_of((Lp, y.shape[1]))
        for w in range(wb):
            at = block * wb + w
            valid = lens[i * plan.nw + at] - s * Lp
            r = x2[w] + y[w * Lp : (w + 1) * Lp] + half_state[BIAS : BIAS + 1]
            r = jnp.where(rowr < valid, r, 0.0).astype(BF16).T
            for k in range(g):
                res[k, at] = r[k * cs : (k + 1) * cs]

    @pl.when(first_step())
    def _():
        greet(peers.others)
        acc[...] = jnp.zeros_like(acc)
        for c in range(2):
            pw[:, c * (C // 2) : (c + 1) * (C // 2)] = w_ref[c, 0]

    @pl.when(t < plan.steps)
    def _():
        mean, rho = norm_of(old[ST3 : ST3 + 2, 0:H], total_of(lens))
        scale = old[GAIN3 : GAIN3 + 1, 0:H] * rho
        offset = old[SHIFT3 : SHIFT3 + 1, 0:H] - mean * scale
        shift = -mean * rho
        rowc = rows_of((Lp, C))
        rowh = rows_of((Lp, H))
        block = pl.ds(pl.multiple_of(t * M, 128), M)
        bias = jnp.zeros((8, C), F32)
        parts = []
        for w in range(wb):
            valid = lens[i * plan.nw + t * wb + w] - s * Lp
            d = jnp.where(rowc < valid, cot[w].astype(F32), 0.0)
            bias = bias + fold(d)
            parts.append(d.astype(BF16))
        d = jnp.concatenate(parts, axis=0)
        dos[block] = d
        da = mm_nt(d, pw[...])
        s0, s1 = jnp.zeros((8, H), F32), jnp.zeros((8, H), F32)
        parts = []
        for w in range(wb):
            at = t * wb + w
            valid = lens[i * plan.nw + at] - s * Lp
            top, end = w * Lp, (w + 1) * Lp
            v = c2[w]
            act, slope = gelu_both(v * scale + offset)
            parts.append(jnp.where(rowh < valid, act, 0.0).astype(BF16))
            dzw = da[top:end] * slope
            dz[w] = dzw
            edge[0, at] = dzw[:EDGE].astype(BF16)
            edge[1, at] = dzw[Lp - EDGE :].astype(BF16)
            s0 = s0 + fold(dzw)
            s1 = s1 + fold(dzw * (v * rho + shift))
        a3 = jnp.concatenate(parts, axis=0)
        a3s[block] = a3
        a3T[:, block] = a3.T
        acc[0:1, 0:H] += unfold(s0)
        acc[0:1, H : 2 * H] += unfold(s1)
        acc[1:2] += unfold(bias)

    @pl.when(first_step())
    def _():
        meet(peers.others)

    @pl.when(t < steps)
    def _():
        halo.start(t * wb, wb)

    @pl.when(t < ahead)
    def _():
        result_of(t)
        for off in range(1, g):
            bulk(off, pl.ds(t * wb, wb)).start()

    @pl.when(t == steps - 1)
    def _():
        link[0][...] = acc[...]
        peers.start(link)

    @pl.when(t >= steps)
    def _():
        result_of(t - steps + ahead)

    @pl.when(last_step())
    def _():
        rows = pl.ds(pl.multiple_of(h * plan.Hh, 16), plan.Hh)
        pgrad[...] = mm(a3T[rows], dos[...]).astype(BF16)
        keep_state(old, state)
        got = peers.finish(link)
        state[SU3 : SU3 + 1, 0:H] = got[0:1, 0:H]
        state[SU3 + 1 : SU3 + 2, 0:H] = got[0:1, H : 2 * H]
        state[BSUM : BSUM + 1] = got[1:2]
        halo.finish()
        for off in range(1, g):
            bulk(off, pl.ds(0, ahead * wb)).wait()


def dilated_back_kernel(plan, lens, c2, cland, dz3, dland, x2, Y3, w_ref, old, res,
                        dz2, grads, land, state, res_got,
                        ext, Z3, wt, dcT, edge, acc, bulk_sems, halo_sems, *link):
    t = pl.program_id(0)
    peers = group_peers(plan)
    halo = Halo(plan, edge, land, halo_sems)
    s, z, i, h = plan.place()
    Lp, C, H, wb, nw, g = plan.Lp, plan.C, plan.H, plan.wb, plan.nw, plan.g

    def bulk(off):
        rows = pl.ds(plan.shares[0] * wb, plan.shares[1] * wb)
        to = wrap(i + off, g)
        return remote(
            res.at[to, rows],
            res_got.at[off],
            bulk_sems.at[0, off],
            bulk_sems.at[1, off],
            (s, h * g + to),
        )

    offs = range(1, g) if plan.shares[1] else ()

    @pl.when(first_step())
    def _():
        greet(peers.others)
        acc[...] = jnp.zeros_like(acc)
        for k in range(plan.T2):
            for c in range(2):
                cols = slice(c * (C // 2), (c + 1) * (C // 2))
                wt[k * H : (k + 1) * H, cols] = w_ref[c, k]
        meet(peers.others)
        for off in offs:
            bulk(off).start()

    @pl.when(t < plan.steps)
    def _():
        total = total_of(lens)
        mean3, rho3 = norm_of(old[ST3 : ST3 + 2, 0:H], total)
        gr3 = old[GAIN3 : GAIN3 + 1, 0:H] * rho3
        sg3 = old[SU3 : SU3 + 1, 0:H] / total
        gg3 = old[SU3 + 1 : SU3 + 2, 0:H] / total
        mean2, rho2 = norm_of(old[ST2 : ST2 + 2], total)
        scale2 = old[GAIN2 : GAIN2 + 1] * rho2
        offset2 = old[SHIFT2 : SHIFT2 + 1] - mean2 * scale2
        rowh = rows_of((Lp, H))
        rowe = rows_of((EDGE, H))
        rowc = rows_of((Lp, C))

        by_v = -gr3 * rho3 * gg3
        by_1 = gr3 * (mean3 * rho3 * gg3 - sg3)
        shift2 = -mean2 * rho2

        def back(dz, v):
            return gr3 * dz + by_v * v + by_1

        for w in range(wb):
            valid = lens[i * nw + t * wb + w] - s * Lp
            d = jnp.where(rowh < valid, back(dz3[w], c2[w]), 0.0)
            dl = back(dland[0, w].astype(F32), cland[0, w].astype(F32))
            dl = jnp.where((rowe - EDGE < valid) & (s > 0), dl, 0.0)
            dh = back(dland[1, w].astype(F32), cland[1, w].astype(F32))
            dh = jnp.where(rowe + Lp < valid, dh, 0.0)
            ext[w, 0:EDGE] = dl
            ext[w, EDGE : EDGE + Lp] = d
            ext[w, EDGE + Lp :] = dh
            top, end = w * Lp, (w + 1) * Lp
            Z3[top:end, 0:H] = ext[w, EDGE + DIL : EDGE + DIL + Lp].astype(BF16)
            Z3[top:end, H : 2 * H] = d.astype(BF16)
            Z3[top:end, 2 * H : 3 * H] = ext[w, EDGE - DIL : EDGE - DIL + Lp].astype(BF16)

        y = mm(Z3[...], wt[...])

        M = wb * Lp
        dcT[:, pl.ds(pl.multiple_of(t * M, 128), M)] = Z3[:, H : 2 * H].T
        s0, s1 = jnp.zeros((8, C), F32), jnp.zeros((8, C), F32)
        for w in range(wb):
            at = t * wb + w
            valid = lens[i * nw + at] - s * Lp
            v = x2[w]
            dzw = y[w * Lp : (w + 1) * Lp] * gelu_slope(v * scale2 + offset2)
            dzw = jnp.where(rowc < valid, dzw, 0.0)
            dz2[w] = dzw
            edge[0, pl.ds(at, 1)] = dzw[0:1]
            edge[1, pl.ds(at, 1)] = dzw[Lp - 1 : Lp]
            s0 = s0 + fold(dzw)
            s1 = s1 + fold(dzw * (v * rho2 + shift2))
        acc[0:1] += unfold(s0)
        acc[1:2] += unfold(s1)

    @pl.when(t == plan.steps - 1)
    def _():
        link[0][...] = acc[...]
        peers.start(link)
        halo.start(0, nw)

    @pl.when(t >= plan.steps)
    def _():
        rows = pl.ds(pl.multiple_of(h * plan.Hh, 16), plan.Hh)
        grads[...] = mm(dcT[rows], Y3[...]).astype(BF16)

    @pl.when(last_step())
    def _():
        keep_state(old, state)
        state[SU2 : SU2 + 2] = peers.finish(link)
        halo.finish()
        for off in offs:
            bulk(off).wait()


class Reduction:
    def __init__(self, plan, batches, out, give, mine, got, spread, half, mate, sems):
        self.plan, self.batches, self.out = plan, batches, out
        self.give, self.mine, self.got, self.spread = give, mine, got, spread
        self.half, self.mate = half, mate
        self.sems = sems
        self.s, self.z, self.i, self.h = plan.place()
        self.c = lax.rem(self.s, 2)
        self.m = lax.div(self.s, 2)
        self.chips = plan.chips

    @staticmethod
    def scratch(plan, batches):
        taps, wide = plan.T1 + 2, plan.C // 2
        full = (taps, plan.chips, plan.g, plan.rb, wide)
        part = (taps, plan.g, plan.rb, wide)
        return [
            pltpu.VMEM((taps, 2, plan.chips, plan.rb, wide), BF16),
            *[pltpu.VMEM(full, BF16)] * 4,
            *[pltpu.VMEM(part, BF16)] * 2,
            pltpu.SemaphoreType.DMA((2, len(batches), 5)),
        ]

    def copy(self, b, phase, src, dst, device):
        return remote(src, dst, self.sems.at[0, b, phase], self.sems.at[1, b, phase], device)

    def finish(self, b, phase, ref, device):
        done = self.copy(b, phase, ref, ref, device)
        done.wait_recv()
        done.wait_send()

    def taps(self, b):
        return pl.ds(*self.batches[b])

    def pair(self):
        return (2 * self.m + (1 - self.c), self.z)

    def far(self, off):
        return (2 * wrap(self.m + off, self.chips) + self.c, self.z)

    def member(self, off):
        return (self.s, self.h * self.plan.g + wrap(self.i + off, self.plan.g))

    def put(self, k, rows):
        wide = self.plan.C // 2
        for j in range(self.plan.g):
            for m in range(self.chips):
                v = rows(j, m)
                left, right = v[:, :wide], v[:, wide:]
                self.mine[k, m, j] = jnp.where(self.c == 0, left, right).astype(BF16)
                self.give[k, m, j] = jnp.where(self.c == 0, right, left).astype(BF16)

    def step0(self, b):
        taps = self.taps(b)
        self.copy(b, 0, self.give.at[taps], self.got.at[taps], self.pair()).start()

    def step1(self, b):
        taps = self.taps(b)
        self.finish(b, 0, self.got.at[taps], self.pair())
        first, count = self.batches[b]
        for k in range(first, first + count):
            v = self.mine[k].astype(F32) + self.got[k].astype(F32)
            self.mine[k] = v.astype(BF16)
        for off in range(1, self.chips):
            src = self.mine.at[taps, wrap(self.m + off, self.chips)]
            self.copy(b, 1, src, self.spread.at[taps, self.m], self.far(off)).start()

    def step2(self, b):
        taps = self.taps(b)
        self.finish(b, 1, self.spread.at[taps, pl.ds(0, self.chips - 1)], self.far(1))
        first, count = self.batches[b]
        for k in range(first, first + count):
            self.spread[k, self.m] = self.mine[k, self.m]
            v = self.spread[k, 0].astype(F32)
            for n in range(1, self.chips):
                v = v + self.spread[k, n].astype(F32)
            self.half[k] = v.astype(BF16)
        for off in range(1, self.plan.g):
            src = self.half.at[taps, wrap(self.i + off, self.plan.g)]
            self.copy(b, 2, src, self.mate.at[taps, off], self.member(off)).start()

    def step3(self, b):
        taps = self.taps(b)
        self.finish(b, 2, self.mate.at[taps, pl.ds(1, self.plan.g - 1)], self.member(1))
        first, count = self.batches[b]
        for k in range(first, first + count):
            v = self.half[k, self.i].astype(F32)
            for off in range(1, self.plan.g):
                v = v + self.mate[k, off].astype(F32)
            self.out[k, self.c, self.m] = v.astype(BF16)
        mine = self.out.at[taps, self.c, self.m]
        for off in range(1, self.chips):
            self.copy(b, 3, mine, mine, self.far(off)).start()

    def step4(self, b):
        taps = self.taps(b)
        self.finish(b, 3, self.out.at[taps, self.c, pl.ds(0, self.chips - 1)], self.far(1))
        mine = self.out.at[taps, self.c]
        self.copy(b, 4, mine, mine, self.pair()).start()

    def step5(self, b):
        self.finish(b, 4, self.out.at[self.taps(b), self.c], self.pair())


def tail_turns(plan):
    nD = plan.steps
    first = max(nD - 1, 1)
    turns = [("x", n) for n in range(first)] + [("d", n) for n in range(first, nD)]
    turns += [("w", n) for n in range(plan.T1)]
    return turns + [("x", n) for n in range(first, nD)]


def tail_batches(plan):
    return [(plan.T1, 2), (0, 3), (3, plan.T1 - 3)]


def tail_kernel(plan, lens, dz2, dzland, x2, x2land, cot, beyond, x, X5_hbm, taps, grads, pgrad,
                old, half_state, res,
                gz, gz_got, sums, summed, res_got,
                ext, D3, D0T, wcat, pick, eye, cols, y, part, split, acc, X5, X5_sems,
                bulk_sems, res_sems, *rest):
    t = pl.program_id(0)
    s, z, i, h = plan.place()
    L, Lp, C, wb, g, nw = plan.L, plan.Lp, plan.C, plan.wb, plan.g, plan.nw
    Ch, cs, T1 = plan.Ch, plan.cs, plan.T1
    M = wb * Lp
    nD = plan.steps
    turns = tail_turns(plan)
    last = len(turns) - 1
    peers = group_peers(plan)
    red = Reduction(plan, tail_batches(plan), *rest[:8])
    link = rest[8:]

    def member(off):
        return (s, h * g + wrap(i + off, g))

    def send(first, count):
        rows = pl.ds(first, count)
        for off in range(1, g):
            remote(
                part.at[off - 1, rows],
                gz_got.at[off, rows],
                bulk_sems.at[0, off],
                bulk_sems.at[1, off],
                member(off),
            ).start()

    def res_copy(off):
        rows = pl.ds(nw - wb, wb)
        return remote(
            res.at[wrap(i + off, g), rows],
            res_got.at[off],
            res_sems.at[0, off],
            res_sems.at[1, off],
            member(off),
        )

    res_offs = range(1, g) if plan.shares[2] else ()

    def X5_copy(k):
        cols = pl.ds(pl.multiple_of(k * C, 128), C)
        return pltpu.make_async_copy(X5_hbm.at[:, cols], X5.at[k % 2], X5_sems.at[k % 2])

    def when(at):
        return pl.when(t == min(at, last))

    def turn(kind, k):
        return turns.index((kind, k)) if (kind, k) in turns else last

    def turn_of(kind):
        index = jnp.int32(0)
        here = False
        for n, (what, k) in enumerate(turns):
            if what == kind:
                index = jnp.where(t == n, k, index)
                here = (t == n) | here
        return here, index

    @when(0)
    def _():
        greet(peers.others)
        acc[...] = jnp.zeros_like(acc)
        pick[...] = pick_matrix(L)
        eye[...] = eye_matrix(Ch, Ch, 0)
        mean, rho = norm_of(half_state[ST1 : ST1 + 2], 2.0 * total_of(lens))
        scale = half_state[GAIN1 : GAIN1 + 1] * rho
        offset = half_state[SHIFT1 : SHIFT1 + 1] - mean * scale
        for k, row in enumerate((scale, offset, rho, -mean * rho)):
            cols[k] = column(row, L)
        for first in range(0, Ch, 64):
            rows = slice(first, min(first + 64, Ch))
            for r, parts in enumerate((((0,), (1, 2), (3, 4)), ((0, 1), (2, 3), (4,)))):
                for k, which in enumerate(parts):
                    v = taps[which[0], rows]
                    if len(which) > 1:
                        v = (v.astype(F32) + taps[which[1], rows].astype(F32)).astype(BF16)
                    at = r * Ch
                    wcat[at + rows.start : at + rows.stop, k * C : (k + 1) * C] = v
        meet(peers.others)
        for off in res_offs:
            res_copy(off).start()

    @pl.when(t < nD)
    def _():
        total = total_of(lens)
        mean, rho = norm_of(old[ST2 : ST2 + 2], total)
        gr = old[GAIN2 : GAIN2 + 1] * rho
        sg = old[SU2 : SU2 + 1] / total
        gg = old[SU2 + 1 : SU2 + 2] / total
        rowc = rows_of((Lp, C))
        row1 = rows_of((1, C))

        by_dz = 0.5 * gr
        by_v = -0.5 * gr * rho * gg
        by_1 = 0.5 * gr * (mean * rho * gg - sg)

        def back(dout, dz, v):
            return 0.5 * dout + by_dz * dz + by_v * v + by_1

        def grad_of(w):
            at = t * wb + w
            valid = lens[i * nw + at] - s * Lp
            d = back(cot[w].astype(F32), dz2[w], x2[w])
            d = jnp.where(rowc < valid, d, 0.0)
            one = pl.ds(at, 1)
            dl = back(beyond[0, 2, one, :], dzland[0, one, :], x2land[0, w, EDGE - 1 : EDGE].astype(F32))
            dl = jnp.where((row1 - 1 < valid) & (s > 0), dl, 0.0)
            dh = back(beyond[1, 2, one, :], dzland[1, one, :], x2land[1, w, 0:1].astype(F32))
            dh = jnp.where(row1 + Lp < valid, dh, 0.0)
            ext[w, 7:8] = dl
            ext[w, 8 : 8 + Lp] = d
            ext[w, 8 + Lp : 9 + Lp] = dh
            top, end = w * Lp, (w + 1) * Lp
            D3[t, top:end, 0:C] = ext[w, 9 : 9 + Lp].astype(BF16)
            D3[t, top:end, C : 2 * C] = d.astype(BF16)
            D3[t, top:end, 2 * C : 3 * C] = ext[w, 7 : 7 + Lp].astype(BF16)

        for w in range(wb):
            grad_of(w)
        half = D3[t, :, pl.ds(pl.multiple_of(C + h * Ch, 128), Ch)]
        D0T[:, pl.ds(pl.multiple_of(t * M, 128), M)] = half.T

    here_x, bx = turn_of("x")

    @pl.when(here_x)
    def _():
        lanes = lanes_of((Ch, L))

        def through(w):
            valid = 2 * lens[i * nw + bx * wb + w] - s * L
            top, end = w * Lp, (w + 1) * Lp
            v = mm_nt(eye[...], x[w])
            da = jnp.concatenate([y[0:Ch, top:end], y[Ch:, top:end]], axis=1)
            da = mm(da.astype(BF16), pick[...])
            dzw = da * gelu_slope(v * cols[0] + cols[1])
            dzw = jnp.where(lanes < valid, dzw, 0.0)
            acc[0] += dzw
            acc[1] += dzw * (v * cols[2] + cols[3])
            split[w % 2] = dzw.astype(BF16)
            for off in range(g):
                rows = pl.ds(pl.multiple_of(lax.rem(i + off, g) * cs, 16), cs)
                if off == 0:
                    gz[w] = split[w % 2, rows]
                else:
                    part[off - 1, bx * wb + w] = split[w % 2, rows]

        nh = 2 if wb % 2 == 0 and wb * Lp // 2 % 128 == 0 else 1
        n = wb // nh
        for hf in range(nh):
            rows = slice(hf * n * Lp, (hf + 1) * n * Lp)
            y[:, rows] = mm_nt(wcat[...], D3[bx, rows])
            for w in range(hf * n, (hf + 1) * n):
                through(w)

    @when(0)
    def _():
        hs = plan.H // plan.nz
        rb = plan.rb
        for u in range(2):

            def rows(j, m, u=u):
                side, r = m * rb // hs, m * rb % hs
                n = 2 * side + u
                rows = slice(j * hs + r, j * hs + r + rb)
                v = grads[rows, n * C : (n + 1) * C] if n < plan.T2 else pgrad[rows]
                return v.astype(F32)

            red.put(T1 + u, rows)
        red.step0(0)

    @when(nD - 1)
    def _():
        X5_copy(0).start()

    here_w, k = turn_of("w")

    @pl.when(here_w)
    def _():
        @pl.when(k < T1 - 1)
        def _():
            X5_copy(k + 1).start()

        X5_copy(k).wait()
        y[0:Ch, 0:C] = mm(D0T[...], X5[lax.rem(k, 2)])
        rb = plan.rb
        red.put(k, lambda j, m: y[j * cs + m * rb : j * cs + (m + 1) * rb, 0:C])

    @pl.when(here_x & (bx < nD - 1))
    def _():
        send(bx * wb, wb)

    @when(turn("x", nD - 1))
    def _():
        send((nD - 1) * wb, wb // 2)

    for at, step, batch in (
        (1, red.step1, 0),
        (max(nD - 1, 2), red.step2, 0),
        (turn("w", 2), red.step0, 1),
        (turn("w", 3), red.step1, 1),
        (turn("w", T1 - 1), red.step0, 2),
        (last, red.step1, 2),
        (last, red.step2, 1),
        (last, red.step3, 0),
        (last, red.step2, 2),
    ):

        @when(at)
        def _():
            step(batch)

    @when(last)
    def _():
        send(nw - wb + wb // 2, wb - wb // 2)

    @when(turn("x", nD - 1))
    def _():
        packet = link[0]
        packet[...] = jnp.zeros_like(packet)
        packet[0:1, 0:Ch] = jnp.sum(acc[0].T, axis=0, keepdims=True)
        packet[1:2, 0:Ch] = jnp.sum(acc[1].T, axis=0, keepdims=True)
        peers.start(link)

    @when(last)
    def _():
        red.step3(1)
        red.step4(0)
        red.step3(2)
        red.step4(1)
        sums[...] = peers.finish(link)[:, 0:Ch]
        red.step4(2)
        for b in range(3):
            red.step5(b)
        own = pltpu.make_async_copy(red.out, summed, X5_sems.at[0])
        own.start()
        for off in range(1, g):
            done = remote(
                part.at[off - 1],
                gz_got.at[off],
                bulk_sems.at[0, off],
                bulk_sems.at[1, off],
                member(off),
            )
            done.wait_recv()
            done.wait_send()
        for off in res_offs:
            res_copy(off).wait()
        own.wait()


def input_grad_kernel(plan, wg, lens, x, gz, gz_got, sums, res, res_a, res_b, res_c, summed,
                      state, half_state,
                      out, out_result, conv_grad, dil_grad, point_grad,
                      g1, b1, g2, b2, g3, b3, pb, eye, cols, xt):
    t = pl.program_id(0)
    s, z, i, h = plan.place()
    L, Ch, cs = plan.L, plan.Ch, plan.cs
    turn = plan.nw // wg
    mine = pl.ds(pl.multiple_of(i * cs, 16), cs)

    @pl.when(first_step())
    def _():
        n = 2.0 * total_of(lens)
        mean, rho = norm_of(half_state[ST1 : ST1 + 2], n)
        gr = half_state[GAIN1 : GAIN1 + 1] * rho
        gg = sums[1:2] / n * rho
        for k, row in enumerate((gr, -gr * gg, gr * (mean * gg - sums[0:1] / n))):
            xt[...] = column(row, L)
            cols[k] = xt[mine]
        eye[...] = eye_matrix(cs, Ch, i * cs)

        def mine_of(src, at, which, count, *dsts):
            n = dsts[0].shape[1]
            for k in range(count):

                @pl.when(which == k)
                def _():
                    for dst, r in zip(dsts, at):
                        dst[...] = src[r : r + 1, k * n : (k + 1) * n]

        mine_of(sums, (1, 0), i, plan.g, g1, b1)
        mine_of(state, (SU2 + 1, SU2), z, plan.nz, g2, b2)
        mine_of(state, (SU3 + 1, SU3), z, plan.nz, g3, b3)
        mine_of(state, (BSUM,), z, plan.nz, pb)

    own = lax.div(t, turn) == i
    start = lax.rem(t, turn) == 0

    def columns(w):
        if plan.shares[1] == 0:
            return res_a[0, w]
        if w < plan.wb:
            return jnp.where(start, res_a[0, w], res_b[0, w])
        return jnp.where(start, res_b[0, w - plan.wb], res_c[0, w - plan.wb])

    for w in range(wg):
        out_result[w] = jnp.where(own, res[0, w], columns(w))

    C, T1, hs, rb, wide = plan.C, plan.T1, plan.H // plan.nz, plan.rb, plan.C // 2
    count = plan.NW // wg
    turns = min(count, plan.chips)
    per, every = plan.chips // turns, count // turns

    def spread(chunk):
        for n in range(per):
            m = chunk * per + n
            side, r = m * rb // hs, m * rb % hs
            for c in range(2):
                at = slice(c * wide, (c + 1) * wide)
                for k in range(T1):
                    conv_grad[k, n * rb : (n + 1) * rb, at] = summed[k, c, n].astype(F32)
                for u in range(2):
                    v = summed[T1 + u, c, n].astype(F32)
                    if 2 * side + u < plan.T2:
                        dil_grad[2 * side + u, r : r + rb, at] = v
                    else:
                        point_grad[r : r + rb, at] = v

    for chunk in range(turns):
        pl.when(t == chunk * every)(partial(spread, chunk))

    lanes = lanes_of((cs, L))
    for w in range(wg):
        valid = 2 * lens[t * wg + w] - s * L
        v = mm_nt(eye[...], x[w])
        dz = jnp.where(own, gz[w], gz_got[0, w]).astype(F32)
        r = cols[0] * dz + v * cols[1] + cols[2]
        out[w] = jnp.where(lanes < valid, r, 0.0).astype(BF16)


def call(kernel, plan, name, steps, ins, outs, scratch, flops, nbytes, cid=None):
    extra = {} if cid is None else dict(collective_id=cid, has_side_effects=True)
    return pl.pallas_call(
        partial(kernel, plan),
        grid=(steps,),
        in_specs=[SMEM] + [spec for spec, _ in ins],
        out_specs=[spec for spec, _, _ in outs],
        out_shape=[jax.ShapeDtypeStruct(shape, dtype) for _, shape, dtype in outs],
        scratch_shapes=scratch,
        compiler_params=pltpu.CompilerParams(vmem_limit_bytes=VMEM_LIMIT, **extra),
        cost_estimate=pl.CostEstimate(
            flops=int(flops), bytes_accessed=int(nbytes), transcendentals=0
        ),
        name=name,
    )


def per_device(
    inputs,
    lengths,
    input_gain,
    input_shift,
    conv_weight,
    branch_gain,
    branch_shift,
    dilated_tap_weight,
    mixer_gain,
    mixer_shift,
    point_weight,
    point_bias,
    cotangent,
):
    NW, L, C = inputs.shape
    Lp = L // 2
    nz = lax.axis_size("ch")
    R = 2
    plan = Plan(
        ns=lax.axis_size("seq"),
        nz=nz,
        R=R,
        NW=NW,
        L=L,
        C=C,
        H=mixer_gain.shape[0] * nz,
        T1=conv_weight.shape[0],
        T2=dilated_tap_weight.shape[0],
        wb=min(NW * R // nz, max(1, 512 // Lp)),
    )
    g, nw, cs, Ch, H, Hh, wb = plan.g, plan.nw, plan.cs, plan.Ch, plan.H, plan.Hh, plan.wb
    T1, T2, steps = plan.T1, plan.T2, plan.steps
    M = wb * Lp
    hs = H // nz
    lens = lengths.astype(jnp.int32)

    def row(a):
        return a.reshape(1, a.shape[0])

    def grp():
        return lax.rem(lax.axis_index("ch"), g)

    def half():
        return lax.div(lax.axis_index("ch"), g)

    def core():
        return lax.rem(lax.axis_index("seq"), 2)

    def chip4():
        return lax.div(lax.axis_index("seq"), plan.ns // 4)

    def whole(*shape):
        return pl.BlockSpec(shape, lambda t: (0,) * len(shape), pipeline_mode=pl.Buffered(1))

    def const(*shape):
        return pl.BlockSpec(shape, lambda t: (0,) * len(shape))

    def win(*shape):
        return pl.BlockSpec(shape, lambda t: (t,) + (0,) * (len(shape) - 1))

    def arg_win(n, width):
        return pl.BlockSpec((wb, n, width), lambda t: (grp() * steps + t, 0, 0))

    def ins(*pairs):
        return [p for p in pairs]

    share = NW // nz
    nm = max(1, share // wb)

    def edge_spec(n):
        return pl.BlockSpec(
            (nw, 16, C), lambda t: (grp(), n, 0), pipeline_mode=pl.Buffered(1)
        )

    def head_block(t):
        own = lax.div(lax.axis_index("ch") * share, wb) + t
        return jnp.where(t < nm, own, grp() * steps + t - nm), 0, 0

    def after(*shape):
        return pl.BlockSpec(
            shape, lambda t: (jnp.maximum(t - nm, 0),) + (0,) * (len(shape) - 1)
        )

    pairs = ins(
        (pl.BlockSpec((wb, L, C), head_block), inputs),
        (edge_spec(0), inputs),
        (edge_spec(L // 16 - 1), inputs),
        (edge_spec(0), cotangent),
        (edge_spec(Lp // 16 - 1), cotangent),
        (whole(1, cs), row(branch_gain)),
        (whole(1, cs), row(branch_shift)),
        (whole(1, cs), row(point_bias)),
        (whole(1, H // nz), row(mixer_gain)),
        (whole(1, H // nz), row(mixer_shift)),
        (ANY, conv_weight.reshape(T1 * C, C)),
        (whole(C), input_gain),
        (whole(C), input_shift),
        (
            pl.BlockSpec(
                (1, hs, C // 2),
                lambda t: (jnp.minimum(chip4(), T2 - 1), 0, core()),
                pipeline_mode=pl.Buffered(1),
            ),
            jnp.swapaxes(dilated_tap_weight, 1, 2),
        ),
        (
            pl.BlockSpec(
                (hs, C // 2), lambda t: (0, core()), pipeline_mode=pl.Buffered(1)
            ),
            point_weight,
        ),
    )
    plane, line, group = plane_peers(plan), line_peers(plan), group_peers(plan)
    state_shape = (STATE, C)
    edges2, edges3 = (2, nw, EDGE, C), (2, nw, EDGE, H)
    X5, x2, land2, state, beyond, full = call(
        lambda plan, *refs: head_kernel(plan, nm, *refs),
        plan,
        "head",
        nm + steps,
        pairs,
        [
            (after(M, T1 * C), (nw * Lp, T1 * C), BF16),
            (after(wb, Lp, C), (nw, Lp, C), F32),
            (ANY, edges2, BF16),
            (const(*state_shape), state_shape, F32),
            (const(2, 3, nw, C), (2, 3, nw, C), F32),
            (ANY, (2, T2 + 1, nz, hs, C // 2), BF16),
        ],
        [
            pltpu.VMEM((2, 8, C), F32),
            pltpu.VMEM((2, 3, nw, C), F32),
            pltpu.VMEM((2, 3, nw, C), F32),
            pltpu.VMEM((T1 * Lp, L), BF16),
            pltpu.VMEM(edges2, BF16),
            pltpu.VMEM((2, C), F32),
            pltpu.VMEM((T1 * C, C), BF16),
            pltpu.SemaphoreType.DMA,
            pltpu.VMEM((hs, C // 2), BF16),
            pltpu.SemaphoreType.DMA((2, 4)),
            HALO_SEMS,
            HALO_SEMS,
        ]
        + plane.scratch(2, C)
        + line.scratch(3, C)
        + group.scratch(2, C),
        2 * nw * Lp * T1 * C * C,
        nw * Lp * C * 20,
        cid=1,
    )(lens, *[a for _, a in pairs])

    full = full.reshape(2, T2 + 1, H, C // 2)
    taps_spec = whole(2, T2, H, C // 2)
    pw_spec = pl.BlockSpec(
        (2, 1, H, C // 2), lambda t: (0, T2, 0, 0), pipeline_mode=pl.Buffered(1)
    )

    def early(*shape):
        return pl.BlockSpec(
            shape, lambda t: (jnp.minimum(t, steps - 1),) + (0,) * (len(shape) - 1)
        )

    def early_land(width):
        return pl.BlockSpec(
            (2, wb, EDGE, width), lambda t: (0, jnp.minimum(t, steps - 1), 0, 0)
        )

    ahead = plan.shares[0]

    def late(t):
        return jnp.maximum(t - steps, 0)

    def half_of(n):
        return pl.BlockSpec((n, Ch), lambda t: (0, half()), pipeline_mode=pl.Buffered(1))

    cot_spec = pl.BlockSpec(
        (wb, Lp, C), lambda t: (grp() * steps + jnp.minimum(t, steps - 1), 0, 0)
    )

    pairs = ins(
        (early(wb, Lp, C), x2),
        (early_land(C), land2),
        (taps_spec, full),
        (whole(*state_shape), state),
    )
    Y3, c2, land3, state = call(
        dilated_kernel,
        plan,
        "dilated",
        steps,
        pairs,
        [
            (win(M, T2 * C), (nw * Lp, T2 * C), BF16),
            (win(wb, Lp, H), (nw, Lp, H), F32),
            (ANY, edges3, BF16),
            (const(*state_shape), state_shape, F32),
        ],
        [
            pltpu.VMEM((wb, Lp + 2 * EDGE, C), F32),
            pltpu.VMEM((H, T2 * C), BF16),
            pltpu.VMEM(edges3, BF16),
            pltpu.VMEM((1, 2 * H), F32),
            HALO_SEMS,
        ]
        + group.scratch(1, 2 * H),
        2 * nw * Lp * T2 * C * H,
        nw * Lp * C * 12,
        cid=3,
    )(lens, *[a for _, a in pairs])

    pairs = ins(
        (early(wb, Lp, H), c2),
        (
            pl.BlockSpec(
                (wb, Lp, Ch),
                lambda t: (
                    jnp.where(t < steps, jnp.minimum(t, ahead - 1), late(t) + ahead),
                    0,
                    half(),
                ),
            ),
            x2,
        ),
        (cot_spec, cotangent),
        (pw_spec, full),
        (whole(*state_shape), state),
        (half_of(STATE), state),
    )
    res, dz3, pgrad, dland3, state, res_a = call(
        point_kernel,
        plan,
        "point",
        2 * steps - ahead,
        pairs,
        [
            (const(g, nw, cs, Lp), (g, nw, cs, Lp), BF16),
            (early(wb, Lp, H), (nw, Lp, H), F32),
            (const(Hh, C), (Hh, C), BF16),
            (ANY, edges3, BF16),
            (const(*state_shape), state_shape, F32),
            (ANY, (g, ahead * wb, cs, Lp), BF16),
        ],
        [
            pltpu.VMEM((H, C), BF16),
            pltpu.VMEM((nw * Lp, H), BF16),
            pltpu.VMEM((H, nw * Lp), BF16),
            pltpu.VMEM((nw * Lp, C), BF16),
            pltpu.VMEM(edges3, BF16),
            pltpu.VMEM((2, C), F32),
            HALO_SEMS,
            pltpu.SemaphoreType.DMA((2, g)),
        ]
        + group.scratch(2, C),
        5 * nw * Lp * C * H,
        nw * Lp * C * 10,
        cid=4,
    )(lens, *[a for _, a in pairs])

    pairs = ins(
        (early(wb, Lp, H), c2),
        (early_land(H), land3),
        (early(wb, Lp, H), dz3),
        (early_land(H), dland3),
        (early(wb, Lp, C), x2),
        (pl.BlockSpec((nw * Lp, C), lambda t: (0, late(t))), Y3),
        (taps_spec, full),
        (whole(*state_shape), state),
        (ANY, res),
    )
    dz2, grads, dland2, state, res_b = call(
        dilated_back_kernel,
        plan,
        "dilated_back",
        steps + T2,
        pairs,
        [
            (early(wb, Lp, C), (nw, Lp, C), F32),
            (pl.BlockSpec((Hh, C), lambda t: (0, late(t))), (Hh, T2 * C), BF16),
            (ANY, (2, nw, C), F32),
            (const(*state_shape), state_shape, F32),
            (ANY, (g, max(plan.shares[1], 1) * wb, cs, Lp), BF16),
        ],
        [
            pltpu.VMEM((wb, Lp + 2 * EDGE, H), F32),
            pltpu.VMEM((M, T2 * H), BF16),
            pltpu.VMEM((T2 * H, C), BF16),
            pltpu.VMEM((H, nw * Lp), BF16),
            pltpu.VMEM((2, nw, C), F32),
            pltpu.VMEM((2, C), F32),
            pltpu.SemaphoreType.DMA((2, g)),
            HALO_SEMS,
        ]
        + group.scratch(2, C),
        4 * nw * Lp * T2 * C * H,
        nw * Lp * C * 20,
        cid=5,
    )(lens, *[a for _, a in pairs])

    chips, rb = plan.chips, plan.rb
    turns_t = tail_turns(plan)

    def x_block(t):
        block = jnp.int32(0)
        for n, (what, k) in enumerate(turns_t):
            if what == "x":
                block = jnp.where(t >= n, k, block)
        return block

    sshape = (T1 + 2, 2, chips, rb, C // 2)
    pairs = ins(
        (early(wb, Lp, C), dz2),
        (whole(2, nw, C), dland2),
        (early(wb, Lp, C), x2),
        (early_land(C), land2),
        (cot_spec, cotangent),
        (whole(2, 3, nw, C), beyond),
        (
            pl.BlockSpec(
                (wb, L, Ch), lambda t: (grp() * steps + x_block(t), 0, half())
            ),
            inputs,
        ),
        (ANY, X5),
        (
            pl.BlockSpec(
                (T1, Ch, C), lambda t: (0, half(), 0), pipeline_mode=pl.Buffered(1)
            ),
            conv_weight,
        ),
        (whole(Hh, T2 * C), grads),
        (whole(Hh, C), pgrad),
        (whole(*state_shape), state),
        (half_of(STATE), state),
        (ANY, res),
    )
    gz, gz_got, sums1, summed, res_c = call(
        tail_kernel,
        plan,
        "tail",
        len(turns_t),
        pairs,
        [
            (pl.BlockSpec((wb, cs, L), lambda t: (x_block(t), 0, 0)), (nw, cs, L), BF16),
            (ANY, (g, nw, cs, L), BF16),
            (const(2, Ch), (2, Ch), F32),
            (ANY, sshape, BF16),
            (ANY, (g, wb, cs, Lp), BF16),
        ],
        [
            pltpu.VMEM((wb, Lp + 16, C), F32),
            pltpu.VMEM((steps, M, 3 * C), BF16),
            pltpu.VMEM((Ch, nw * Lp), BF16),
            pltpu.VMEM((2 * Ch, 3 * C), BF16),
            pltpu.VMEM((L, L), BF16),
            pltpu.VMEM((Ch, Ch), BF16),
            pltpu.VMEM((4, Ch, L), F32),
            pltpu.VMEM((2 * Ch, max(M, C)), F32),
            pltpu.VMEM((g - 1, nw, cs, L), BF16),
            pltpu.VMEM((2, Ch, L), BF16),
            pltpu.VMEM((2, Ch, L), F32),
            pltpu.VMEM((2, nw * Lp, C), BF16),
            pltpu.SemaphoreType.DMA((2,)),
            pltpu.SemaphoreType.DMA((2, g)),
            pltpu.SemaphoreType.DMA((2, g)),
        ]
        + Reduction.scratch(plan, tail_batches(plan))
        + group.scratch(2, C),
        2 * nw * Lp * (6 + T1) * C * Ch,
        nw * Lp * C * 40,
        cid=6,
    )(lens, *[a for _, a in pairs])

    wg = 2 * wb if plan.shares[1] else wb
    count = NW // wg
    turn = nw // wg
    turns = min(count, chips)

    def own_block(t):
        return jnp.where(lax.div(t, turn) == grp(), lax.rem(t, turn), 0)

    def got_slot(t):
        off = lax.rem(grp() - lax.div(t, turn) + g, g)
        return jnp.maximum(off, 1), jnp.where(off > 0, lax.rem(t, turn), 0)

    def part_slot(t):
        return got_slot(t) + (0, 0) if plan.shares[1] else got_slot(t)[:1] + (0, 0, 0)

    pairs = ins(
        (pl.BlockSpec((wg, L, Ch), lambda t: (t, 0, half())), inputs),
        (pl.BlockSpec((wg, cs, L), lambda t: (own_block(t), 0, 0)), gz),
        (pl.BlockSpec((1, wg, cs, L), lambda t: got_slot(t) + (0, 0)), gz_got),
        (whole(2, Ch), sums1),
        (pl.BlockSpec((1, wg, cs, Lp), lambda t: (grp(), own_block(t), 0, 0)), res),
        (pl.BlockSpec((1, wb, cs, Lp), lambda t: got_slot(t)[:1] + (0, 0, 0)), res_a),
        (pl.BlockSpec((1, wb, cs, Lp), part_slot), res_b),
        (pl.BlockSpec((1, wb, cs, Lp), lambda t: got_slot(t)[:1] + (0, 0, 0)), res_c),
        (
            pl.BlockSpec(
                (T1 + 2, 2, chips // turns, rb, C // 2),
                lambda t: (0, 0, t * turns // count, 0, 0),
            ),
            summed,
        ),
        (whole(*state_shape), state),
        (half_of(STATE), state),
    )
    outs = call(
        lambda plan, *refs: input_grad_kernel(plan, wg, *refs),
        plan,
        "input_grad",
        count,
        pairs,
        [
            (win(wg, cs, L), (NW, cs, L), BF16),
            (win(wg, cs, Lp), (NW, cs, Lp), BF16),
            (
                pl.BlockSpec((T1, cs // turns, C), lambda t: (0, t * turns // count, 0)),
                (T1, cs, C),
                F32,
            ),
            (const(T2, hs, C), (T2, hs, C), F32),
            (const(hs, C), (hs, C), F32),
        ]
        + [(const(1, n), (1, n), F32) for n in (cs, cs, cs, cs, hs, hs, cs)],
        [
            pltpu.VMEM((cs, Ch), BF16),
            pltpu.VMEM((3, cs, L), F32),
            pltpu.VMEM((Ch, L), F32),
        ],
        2 * NW * L * Ch * cs,
        NW * L * cs * 8,
    )(lens, *[a for _, a in pairs])
    grad, result, conv_grad, dil_grad, point_grad = outs[:5]
    g1, b1, g2, b2, g3, b3, pb = [a[0] for a in outs[5:]]
    return (
        jnp.swapaxes(result, 1, 2),
        jnp.swapaxes(grad, 1, 2),
        jnp.swapaxes(conv_grad, 1, 2),
        g1,
        b1,
        g2,
        b2,
        jnp.swapaxes(dil_grad, 1, 2),
        g3,
        b3,
        point_grad,
        pb,
    )


def solution(mesh):
    in_specs = (
        P(None, "seq", None),
        P(),
        P(),
        P(),
        P(),
        P("ch"),
        P("ch"),
        P(None, None, "ch"),
        P("ch"),
        P("ch"),
        P("ch", None),
        P("ch"),
        P(None, "seq", None),
    )
    out_specs = (
        P(None, "seq", "ch"),
        P(None, "seq", "ch"),
        P(None, None, "ch"),
        P("ch"),
        P("ch"),
        P("ch"),
        P("ch"),
        P(None, None, "ch"),
        P("ch"),
        P("ch"),
        P("ch", None),
        P("ch"),
    )
    return jax.shard_map(
        per_device, mesh=mesh, in_specs=in_specs, out_specs=out_specs, check_vma=False
    )
```

```python
from functools import partial
from typing import NamedTuple

import jax
import jax.numpy as jnp
from jax import lax
from jax.experimental import pallas as pl
from jax.experimental.pallas import tpu as pltpu
from jax.sharding import PartitionSpec as P

DIL = 14
EDGE = 16
EPS = 1e-05
GC0 = 0.7978845608028654
GC1 = 0.044715
F32 = jnp.float32
BF16 = jnp.bfloat16
MESH = pl.DeviceIdType.MESH
VMEM_LIMIT = 58 * 1024 * 1024
ANY = pl.BlockSpec(memory_space=pl.ANY)
SMEM = pl.BlockSpec(memory_space=pltpu.SMEM)


ST1, GAIN2, SHIFT2, BIAS, GAIN3, SHIFT3, GAIN1, SHIFT1, ST2, ST3, SU3, BSUM, SU2 = (
    0, 2, 3, 4, 5, 6, 7, 8, 9, 11, 13, 15, 16
)
STATE = 24


class Plan(NamedTuple):
    ns: int
    nz: int
    R: int
    NW: int
    L: int
    C: int
    H: int
    T1: int
    T2: int
    wb: int

    @property
    def g(self):
        return self.nz // self.R

    @property
    def nw(self):
        return self.NW // self.g

    @property
    def Lp(self):
        return self.L // 2

    @property
    def cs(self):
        return self.C // self.nz

    @property
    def Ch(self):
        return self.C // self.R

    @property
    def Hh(self):
        return self.H // self.R

    @property
    def steps(self):
        return self.nw // self.wb

    @property
    def chips(self):
        return self.ns // 2

    @property
    def rb(self):
        return self.cs // self.chips

    def place(self):
        s, z = lax.axis_index("seq"), lax.axis_index("ch")
        return s, z, lax.rem(z, self.g), lax.div(z, self.g)


def gelu(z):
    t = jnp.tanh(z * (GC0 + (GC0 * GC1) * (z * z)))
    return z * (0.5 + 0.5 * t)


def gelu_both(z):
    sq = z * z
    t = jnp.tanh(z * (GC0 + (GC0 * GC1) * sq))
    h = 0.5 + 0.5 * t
    v = z * h
    return v, h + v * (1.0 - t) * (GC0 + (3.0 * GC0 * GC1) * sq)


def gelu_slope(z):
    return gelu_both(z)[1]


def fold(v):
    return jnp.sum(v.reshape(v.shape[0] // 8, 8, v.shape[1]), axis=0)


def fold_lanes(v):
    out = v[:, 0:128]
    for k in range(128, v.shape[1], 128):
        out = out + v[:, k : k + 128]
    return out


def unfold(v):
    return jnp.sum(v, axis=0, keepdims=True)


def rows_of(shape):
    return lax.broadcasted_iota(jnp.int32, shape, 0)


def lanes_of(shape):
    return lax.broadcasted_iota(jnp.int32, shape, 1)


def total_of(lens):
    n = lens[0]
    for k in range(1, lens.shape[0]):
        n = n + lens[k]
    return n.astype(F32)


def norm_of(stats, total):
    mean = stats[0:1] / total
    square = stats[1:2] / total
    return mean, lax.rsqrt(square - mean * mean + EPS)


def flat(ref):
    return ref[...].reshape(1, ref.shape[0])


def column(row, n):
    return jnp.broadcast_to(row, (n, row.shape[1])).T


def mm(a, b):
    return jnp.dot(a, b, preferred_element_type=F32)


def mm_nt(a, b):
    return lax.dot_general(a, b, (((1,), (1,)), ((), ())), preferred_element_type=F32)


def mm_tn(a, b):
    return lax.dot_general(a, b, (((0,), (0,)), ((), ())), preferred_element_type=F32)


def mm_tt(a, b):
    return lax.dot_general(a, b, (((0,), (1,)), ((), ())), preferred_element_type=F32)


def eye_matrix(n, m, first):
    return jnp.where(lanes_of((n, m)) == rows_of((n, m)) + first, 1.0, 0.0).astype(BF16)


def pick_matrix(L):
    r, n = rows_of((L, L)), lanes_of((L, L))
    bin_of = 2 * r - jnp.where(r >= L // 2, L - 1, 0)
    return jnp.where(n == bin_of, 1.0, 0.0).astype(BF16)


def remote(src, dst, send, recv, device):
    return pltpu.make_async_remote_copy(
        src_ref=src,
        dst_ref=dst,
        send_sem=send,
        recv_sem=recv,
        device_id=device,
        device_id_type=MESH,
    )


def wrap(v, n):
    return jnp.where(v >= n, v - n, v)


def greet(devices):
    barrier = pltpu.get_barrier_semaphore()
    for device in devices:
        pl.semaphore_signal(barrier, inc=1, device_id=device, device_id_type=MESH)


def meet(devices):
    pl.semaphore_wait(pltpu.get_barrier_semaphore(), len(devices))


class Peers:
    def __init__(self, me, others):
        self.me, self.others = me, others
        self.count = len(others) + 1

    def start(self, link):
        packet, buf, sems = link
        for device in self.others:
            remote(packet, buf.at[self.me], sems.at[0], sems.at[1], device).start()

    def finish(self, link):
        packet, buf, sems = link
        buf[self.me] = packet[...]
        rest = buf.at[pl.ds(0, self.count - 1)]
        done = remote(rest, rest, sems.at[0], sems.at[1], self.others[0])
        done.wait_recv()
        acc = buf[0]
        for q in range(1, self.count):
            acc = acc + buf[q]
        done.wait_send()
        return acc

    def scratch(self, rows, width):
        return [
            pltpu.VMEM((rows, width), F32),
            pltpu.VMEM((self.count, rows, width), F32),
            pltpu.SemaphoreType.DMA((2,)),
        ]


def group_peers(plan):
    s, z, i, h = plan.place()
    g = plan.g
    others = [
        (wrap(s + a, plan.ns), h * g + wrap(i + b, g))
        for a in range(plan.ns)
        for b in range(g)
        if a or b
    ]
    return Peers(s * g + i, others)


def plane_peers(plan):
    s, z, i, h = plan.place()
    return Peers(s, [(wrap(s + a, plan.ns), z) for a in range(1, plan.ns)])


def line_peers(plan):
    s, z, i, h = plan.place()
    return Peers(z, [(s, wrap(z + a, plan.nz)) for a in range(1, plan.nz)])


class Halo:
    def __init__(self, plan, edge, land, sems):
        self.edge, self.land, self.sems = edge, land, sems
        s, z, _, _ = plan.place()
        self.to = ((wrap(s + plan.ns - 1, plan.ns), z), (wrap(s + 1, plan.ns), z))

    def copy(self, side, rows):
        return remote(
            self.edge.at[side, rows],
            self.land.at[1 - side, rows],
            self.sems.at[0, side],
            self.sems.at[1, side],
            self.to[side],
        )

    def start(self, first, count):
        for side in range(2):
            self.copy(side, pl.ds(first, count)).start()

    def finish(self):
        for side in range(2):
            done = self.copy(side, pl.ds(0, self.land.shape[1]))
            done.wait_recv()
            done.wait_send()


HALO_SEMS = pltpu.SemaphoreType.DMA((2, 2))


class Gather:
    def __init__(self, plan, part, full, sems):
        self.plan, self.part, self.full, self.sems = plan, part, full, sems
        self.s, self.z, self.i, self.h = plan.place()
        self.c, self.m = lax.rem(self.s, 2), lax.div(self.s, 2)
        self.chips = plan.chips
        self.every = self.chips // 4
        self.tap = lax.div(self.m, self.every)
        self.owner = lax.rem(self.m, self.every) == 0
        self.mine = full.at[self.c, self.tap]

    def others(self):
        g, nz = self.plan.g, self.plan.nz
        return [(self.s, wrap(self.h * g + g + r, nz)) for r in range(nz - g)]

    def far(self, off):
        return (2 * wrap(self.m + off, self.chips) + self.c, self.z)

    def own(self):
        return pltpu.make_async_copy(self.part, self.mine.at[self.z], self.sems.at[0, 0])

    def line(self, off):
        device = (self.s, wrap(self.z + off, self.plan.nz))
        return remote(
            self.part, self.mine.at[self.z], self.sems.at[0, 1], self.sems.at[1, 1], device
        )

    def chip(self, off):
        return remote(self.mine, self.mine, self.sems.at[0, 2], self.sems.at[1, 2], self.far(off))

    def pair(self):
        half = self.full.at[self.c]
        device = (2 * self.m + 1 - self.c, self.z)
        return remote(half, half, self.sems.at[0, 3], self.sems.at[1, 3], device)

    def line_start(self):
        @pl.when(self.owner)
        def _():
            self.own().start()
            for off in range(1, self.plan.nz):
                self.line(off).start()

    def line_finish(self):
        @pl.when(self.owner)
        def _():
            self.own().wait()
            rest = self.mine.at[pl.ds(0, self.plan.nz - 1)]
            device = (self.s, wrap(self.z + 1, self.plan.nz))
            done = remote(rest, rest, self.sems.at[0, 1], self.sems.at[1, 1], device)
            done.wait_recv()
            done.wait_send()

    def chips_start(self):
        @pl.when(self.owner)
        def _():
            for off in range(1, self.chips):
                self.chip(off).start()

    def pair_start(self):
        def taken(count):
            rest = self.full.at[self.c, pl.ds(0, count)]
            return remote(rest, rest, self.sems.at[0, 2], self.sems.at[1, 2], self.far(1))

        @pl.when(self.owner)
        def _():
            taken(3).wait_recv()
            for off in range(1, self.chips):
                self.chip(off).wait_send()

        if self.every > 1:

            @pl.when(jnp.logical_not(self.owner))
            def _():
                taken(4).wait_recv()

        self.pair().start()

    def pair_finish(self):
        done = self.pair()
        done.wait_recv()
        done.wait_send()


def first_step():
    return pl.program_id(0) == 0


def last_step():
    return pl.program_id(0) == pl.num_programs(0) - 1


def head_kernel(plan, nm, lens, x, xtop, xend, ctop, cend, g2, s2, pb, g3, s3,
                w_hbm, gain, shift, taps, pw,
                X5, x2, land, state, beyond_out, full,
                macc, beyond, xedge, sel, edge, acc, w_ref, w_sem, part,
                gather_sems, xhalo_sems, halo_sems, *links):
    t = pl.program_id(0)
    peers, plane, line = group_peers(plan), plane_peers(plan), line_peers(plan)
    xhalo = Halo(plan, xedge, beyond, xhalo_sems)
    halo = Halo(plan, edge, land, halo_sems)
    gather = Gather(plan, part, full, gather_sems)
    w_copy = pltpu.make_async_copy(w_hbm, w_ref, w_sem)
    plane_link, line_link, link = links[:3], links[3:6], links[6:]
    s, z, i, h = plan.place()
    L, Lp, C, nw, nz, wb = plan.L, plan.Lp, plan.C, plan.nw, plan.nz, plan.wb
    share = plan.NW // nz
    c = t - nm
    everyone = peers.others + gather.others()

    @pl.when(first_step())
    def _():
        w_copy.start()
        greet(everyone)
        part[...] = jnp.where(gather.tap == 3, pw[...], taps[0])
        macc[...] = jnp.zeros_like(macc)
        acc[...] = jnp.zeros_like(acc)
        state[...] = jnp.zeros_like(state)
        state[GAIN1 : GAIN1 + 1] = flat(gain)
        state[SHIFT1 : SHIFT1 + 1] = flat(shift)
        n16 = nw * 16
        for side, (xe, ce, places) in enumerate(
            ((xtop, ctop, (0, 1, 0)), (xend, cend, (14, 15, 15)))
        ):
            for k, at in enumerate(places):
                rows, lanes = rows_of((nw, n16)), lanes_of((nw, n16))
                one = jnp.where(lanes == 16 * rows + at, 1.0, 0.0).astype(BF16)
                block = (xe if k < 2 else ce)[...].reshape(n16, C)
                xedge[side, k] = mm(one, block)
        shape = (Lp, L)
        for k in range(plan.T1):
            at = lanes_of(shape) - (2 * rows_of(shape) + (k - 2))
            sel[k * Lp : (k + 1) * Lp] = jnp.where((at == 0) | (at == 1), 1.0, 0.0).astype(BF16)

    @pl.when(c < 0)
    def _():
        rows = rows_of((L, C))
        for w in range(min(share, wb)):
            at = lax.rem(z * share, wb) + w
            valid = 2 * lens[z * share + t * wb + w] - s * L
            v = jnp.where(rows < valid, x[at].astype(F32), 0.0)
            macc[0] += fold(v)
            macc[1] += fold(v * v)

    @pl.when(c == -1)
    def _():
        packet, more = plane_link[0], line_link[0]
        packet[0:1] = unfold(macc[0])
        packet[1:2] = unfold(macc[1])
        meet(everyone)
        plane.start(plane_link)
        xhalo.start(0, 3)
        at = 0
        spans = []
        more[2:3] = jnp.zeros((1, C), F32)
        for ref in (g2, s2, pb, g3, s3):
            n = ref.shape[1]
            more[2:3, at : at + n] = ref[...]
            spans.append((at, n))
            at += n
        more[0:2] = plane.finish(plane_link)
        line.start(line_link)
        gather.line_start()
        state[ST1 : ST1 + 2] = line.finish(line_link)[0:2]
        for k in range(nz):
            row = line_link[1][k]
            for r, (at, n) in zip((GAIN2, SHIFT2, BIAS, GAIN3, SHIFT3), spans):
                state[r : r + 1, k * n : (k + 1) * n] = row[2:3, at : at + n]
        xhalo.finish()
        beyond_out[...] = beyond[...]
        w_copy.wait()

    @pl.when(c >= 0)
    def _():
        mean, rho = norm_of(state[ST1 : ST1 + 2], 2.0 * total_of(lens))
        scale = state[GAIN1 : GAIN1 + 1] * rho
        offset = state[SHIFT1 : SHIFT1 + 1] - mean * scale
        rows = rows_of((L, C))
        row1 = rows_of((1, C))
        row16 = rows_of((16, C))
        def activate(w):
            at = c * wb + w
            valid = 2 * lens[i * nw + at] - s * L
            a = gelu(x[w].astype(F32) * scale + offset)
            a = jnp.where(rows < valid, a, 0.0).astype(BF16)
            picked = mm(sel[...], a)
            for k in range(5):
                X5[w * Lp : (w + 1) * Lp, k * C : (k + 1) * C] = picked[
                    k * Lp : (k + 1) * Lp
                ].astype(BF16)

            def beside(side, k, bin_at):
                a = gelu(beyond[side, k, pl.ds(at, 1), :] * scale + offset)
                here = (row1 + bin_at < valid) & (row1 + (s * L + bin_at) >= 0)
                return jnp.where(here, a, 0.0).astype(BF16).astype(F32)

            l0, l1 = beside(0, 0, -2), beside(0, 1, -1)
            r0, r1 = beside(1, 0, L), beside(1, 1, L + 1)
            top, end = w * Lp, (w + 1) * Lp
            for k, add in ((0, l0 + l1), (1, l1)):
                X5[top : top + 16, k * C : (k + 1) * C] = (
                    picked[k * Lp : k * Lp + 16] + jnp.where(row16 == 0, add, 0.0)
                ).astype(BF16)
            for k, add in ((3, r0), (4, r0 + r1)):
                X5[end - 16 : end, k * C : (k + 1) * C] = (
                    picked[(k + 1) * Lp - 16 : (k + 1) * Lp] + jnp.where(row16 == 15, add, 0.0)
                ).astype(BF16)

        nc = 256
        rowp = rows_of((Lp, nc))

        def convolve(first, count):
            span = slice(first * Lp, (first + count) * Lp)
            for n in range(C // nc):
                cols = slice(n * nc, (n + 1) * nc)
                y = 0.5 * mm(X5[span], w_ref[:, cols])
                s0 = jnp.zeros((8, nc), F32)
                s1 = jnp.zeros((8, nc), F32)
                for w in range(first, first + count):
                    at = c * wb + w
                    valid = lens[i * nw + at] - s * Lp
                    v = y[(w - first) * Lp : (w - first + 1) * Lp]
                    x2[w, :, cols] = v
                    edge[0, at, :, cols] = v[:EDGE].astype(BF16)
                    edge[1, at, :, cols] = v[Lp - EDGE :].astype(BF16)
                    v = jnp.where(rowp < valid, v, 0.0)
                    s0 = s0 + fold(v)
                    s1 = s1 + fold(v * v)
                acc[0:1, cols] += unfold(s0)
                acc[1:2, cols] += unfold(s1)

        count = max(1, wb // 2)
        for first in range(0, wb, count):
            for w in range(first, first + count):
                activate(w)
            convolve(first, count)
        halo.start(c * wb, wb)

    @pl.when(c == 0)
    def _():
        gather.line_finish()
        gather.chips_start()

    @pl.when(last_step())
    def _():
        link[0][...] = acc[...]
        peers.start(link)
        gather.pair_start()
        state[ST2 : ST2 + 2] = peers.finish(link)
        halo.finish()
        gather.pair_finish()


def block_kernel(plan, lens, x2, x2half, x2land, cot, w_ref, pw_ref, old, half_state,
                 dz2, grads, pgrad, res, land, state, res_got,
                 ext, wf, wt, pw, Y3, c2, dz3, das, a3s, a3T, dos, Z3, dcT,
                 cedge, cland, cacc, dedge, dland, dacc, bedge, bacc, halo_sems, bulk_sems,
                 *links):
    t = pl.program_id(0)
    peers = group_peers(plan)
    s, z, i, h = plan.place()
    Lp, C, H, wb, nw, cs, g = plan.Lp, plan.C, plan.H, plan.wb, plan.nw, plan.cs, plan.g
    M = wb * Lp
    steps = plan.steps
    p0, r0, b0, g0 = block_phases(plan)[:4]
    c_link, d_link, b_link = links[:3], links[3:6], links[6:]
    c_halo = Halo(plan, cedge, cland, halo_sems.at[0])
    d_halo = Halo(plan, dedge, dland, halo_sems.at[1])
    b_halo = Halo(plan, bedge, land, halo_sems.at[2])

    def bulk(off, rows):
        to = wrap(i + off, g)
        return remote(
            res.at[to, rows],
            res_got.at[off, rows],
            bulk_sems.at[0, off],
            bulk_sems.at[1, off],
            (s, h * g + to),
        )

    def result_of(block):
        y = mm(a3s[pl.ds(pl.multiple_of(block * M, 128), M)], pw_ref[h, 0])
        rowr = rows_of((Lp, y.shape[1]))
        for w in range(wb):
            at = block * wb + w
            valid = lens[i * plan.nw + at] - s * Lp
            r = x2half[w] + y[w * Lp : (w + 1) * Lp] + half_state[BIAS : BIAS + 1]
            r = jnp.where(rowr < valid, r, 0.0).astype(BF16).T
            for k in range(g):
                res[k, at] = r[k * cs : (k + 1) * cs]

    def send_result(block):
        result_of(block)
        for off in range(1, g):
            bulk(off, pl.ds(block * wb, wb)).start()

    @pl.when(first_step())
    def _():
        greet(peers.others)
        state[...] = old[...]
        cacc[...] = jnp.zeros_like(cacc)
        dacc[...] = jnp.zeros_like(dacc)
        bacc[...] = jnp.zeros_like(bacc)
        for c in range(2):
            cols = slice(c * (C // 2), (c + 1) * (C // 2))
            pw[:, cols] = pw_ref[c, 0]
            for k in range(plan.T2):
                at = k * C + c * (C // 2)
                wf[:, at : at + C // 2] = w_ref[c, k]
                wt[k * H : (k + 1) * H, cols] = w_ref[c, k]

    @pl.when(t < p0)
    def _():
        base = pl.multiple_of(t * M, 128)
        mean, rho = norm_of(state[ST2 : ST2 + 2], total_of(lens))
        scale = state[GAIN2 : GAIN2 + 1] * rho
        offset = state[SHIFT2 : SHIFT2 + 1] - mean * scale
        rows = rows_of((Lp, C))
        rowe = rows_of((EDGE, C))

        rowh = rows_of((Lp, H))
        sums0, sums1 = jnp.zeros((8, H), F32), jnp.zeros((8, H), F32)
        nh = min(2, wb)
        for first in range(0, wb, wb // nh):
            span = range(first, first + wb // nh)
            for w in span:
                valid = lens[i * plan.nw + t * wb + w] - s * Lp
                a = jnp.where(rows < valid, gelu(x2[w] * scale + offset), 0.0)
                al = gelu(x2land[0, w].astype(F32) * scale + offset)
                al = jnp.where((rowe - EDGE < valid) & (s > 0), al, 0.0)
                ah = gelu(x2land[1, w].astype(F32) * scale + offset)
                ah = jnp.where(rowe + Lp < valid, ah, 0.0)
                ext[w, 0:EDGE] = al
                ext[w, EDGE : EDGE + Lp] = a
                ext[w, EDGE + Lp :] = ah
                top, end = w * Lp, (w + 1) * Lp
                Y3[pl.ds(base + top, Lp), 0:C] = ext[w, EDGE - DIL : EDGE - DIL + Lp].astype(BF16)
                Y3[pl.ds(base + top, Lp), C : 2 * C] = a.astype(BF16)
                Y3[pl.ds(base + top, Lp), 2 * C : 3 * C] = ext[w, EDGE + DIL : EDGE + DIL + Lp].astype(BF16)
            y = mm_nt(Y3[pl.ds(base + first * Lp, wb // nh * Lp)], wf[...])
            for w in span:
                at = t * wb + w
                valid = lens[i * plan.nw + at] - s * Lp
                v = y[(w - first) * Lp : (w - first + 1) * Lp]
                c2[at] = v
                cedge[0, at] = v[:EDGE].astype(BF16)
                cedge[1, at] = v[Lp - EDGE :].astype(BF16)
                v = jnp.where(rowh < valid, v, 0.0)
                sums0 = sums0 + fold(v)
                sums1 = sums1 + fold(v * v)
        cacc[0:1, 0:H] += unfold(sums0)
        cacc[0:1, H:] += unfold(sums1)

    @pl.when(first_step())
    def _():
        meet(peers.others)

    @pl.when(t < p0)
    def _():
        c_halo.start(t * wb, wb)

    @pl.when(t == p0 - 1)
    def _():
        c_link[0][...] = cacc[...]
        peers.start(c_link)

    here_p = (t >= p0) & (t < p0 + steps)

    @pl.when(here_p)
    def _():
        u = t - p0
        rowc = rows_of((Lp, C))
        block = pl.ds(pl.multiple_of(u * M, 128), M)
        bias = jnp.zeros((8, C), F32)
        parts = []
        for w in range(wb):
            valid = lens[i * plan.nw + u * wb + w] - s * Lp
            d = jnp.where(rowc < valid, cot[w].astype(F32), 0.0)
            bias = bias + fold(d)
            parts.append(d.astype(BF16))
        d = jnp.concatenate(parts, axis=0)
        dos[block] = d
        das[...] = mm_nt(d, pw[...])
        dacc[1:2] += unfold(bias)

    @pl.when(t == p0)
    def _():
        got = peers.finish(c_link)
        state[ST3 : ST3 + 1, 0:H] = got[:, 0:H]
        state[ST3 + 1 : ST3 + 2, 0:H] = got[:, H:]

    @pl.when(here_p)
    def _():
        u = t - p0
        block = pl.ds(pl.multiple_of(u * M, 128), M)
        rowh = rows_of((Lp, H))
        mean, rho = norm_of(state[ST3 : ST3 + 2, 0:H], total_of(lens))
        scale = state[GAIN3 : GAIN3 + 1, 0:H] * rho
        offset = state[SHIFT3 : SHIFT3 + 1, 0:H] - mean * scale
        s0, s1 = jnp.zeros((8, H), F32), jnp.zeros((8, H), F32)
        parts = []
        for w in range(wb):
            at = u * wb + w
            valid = lens[i * plan.nw + at] - s * Lp
            top, end = w * Lp, (w + 1) * Lp
            v = c2[at]
            zv = v * scale + offset
            act, slope = gelu_both(zv)
            parts.append(jnp.where(rowh < valid, act, 0.0).astype(BF16))
            dzw = das[top:end] * slope
            dz3[at] = dzw
            dedge[0, at] = dzw[:EDGE].astype(BF16)
            dedge[1, at] = dzw[Lp - EDGE :].astype(BF16)
            s0 = s0 + fold(dzw)
            s1 = s1 + fold(dzw * zv)
        a3 = jnp.concatenate(parts, axis=0)
        a3s[block] = a3
        a3T[:, block] = a3.T
        dacc[0:1, 0:H] += unfold(s0)
        dacc[0:1, H : 2 * H] += unfold(s1)
        d_halo.start(u * wb, wb)

    @pl.when(t == p0)
    def _():
        send_result(0)

    @pl.when(t == p0 + steps - 1)
    def _():
        d_link[0][...] = dacc[...]
        peers.start(d_link)

    @pl.when((t >= r0) & (t < b0))
    def _():
        send_result(t - r0 + 1)

    @pl.when(t == b0 - 1)
    def _():
        rows = pl.ds(pl.multiple_of(h * plan.Hh, 16), plan.Hh)
        pgrad[...] = mm(a3T[rows], dos[...]).astype(BF16)

    @pl.when(t == b0)
    def _():
        got = peers.finish(d_link)
        shift = state[SHIFT3 : SHIFT3 + 1, 0:H]
        gain = state[GAIN3 : GAIN3 + 1, 0:H]
        state[SU3 : SU3 + 1, 0:H] = got[0:1, 0:H]
        state[SU3 + 1 : SU3 + 2, 0:H] = (got[0:1, H : 2 * H] - shift * got[0:1, 0:H]) / gain
        state[BSUM : BSUM + 1] = got[1:2]
        c_halo.finish()
        d_halo.finish()

    @pl.when((t >= b0) & (t < g0))
    def _():
        u = t - b0
        total = total_of(lens)
        mean3, rho3 = norm_of(state[ST3 : ST3 + 2, 0:H], total)
        gr3 = state[GAIN3 : GAIN3 + 1, 0:H] * rho3
        sg3 = state[SU3 : SU3 + 1, 0:H] / total
        gg3 = state[SU3 + 1 : SU3 + 2, 0:H] / total
        mean2, rho2 = norm_of(state[ST2 : ST2 + 2], total)
        scale2 = state[GAIN2 : GAIN2 + 1] * rho2
        offset2 = state[SHIFT2 : SHIFT2 + 1] - mean2 * scale2
        rowh = rows_of((Lp, H))
        rowe = rows_of((EDGE, H))
        rowc = rows_of((Lp, C))

        by_v = -gr3 * rho3 * gg3
        by_1 = gr3 * (mean3 * rho3 * gg3 - sg3)

        def back(dz, v):
            return gr3 * dz + by_v * v + by_1

        for w in range(wb):
            valid = lens[i * nw + u * wb + w] - s * Lp
            d = jnp.where(rowh < valid, back(dz3[u * wb + w], c2[u * wb + w]), 0.0)
            dl = back(dland[0, u * wb + w].astype(F32), cland[0, u * wb + w].astype(F32))
            dl = jnp.where((rowe - EDGE < valid) & (s > 0), dl, 0.0)
            dh = back(dland[1, u * wb + w].astype(F32), cland[1, u * wb + w].astype(F32))
            dh = jnp.where(rowe + Lp < valid, dh, 0.0)
            ext[w, 0:EDGE, 0:H] = dl
            ext[w, EDGE : EDGE + Lp, 0:H] = d
            ext[w, EDGE + Lp :, 0:H] = dh
            top, end = w * Lp, (w + 1) * Lp
            Z3[top:end, 0:H] = ext[w, EDGE + DIL : EDGE + DIL + Lp, 0:H].astype(BF16)
            Z3[top:end, H : 2 * H] = d.astype(BF16)
            Z3[top:end, 2 * H : 3 * H] = ext[w, EDGE - DIL : EDGE - DIL + Lp, 0:H].astype(BF16)

        y = mm(Z3[...], wt[...])

        M = wb * Lp
        dcT[:, pl.ds(pl.multiple_of(u * M, 128), M)] = Z3[:, H : 2 * H].T
        s0, s1 = jnp.zeros((8, C), F32), jnp.zeros((8, C), F32)
        for w in range(wb):
            at = u * wb + w
            valid = lens[i * nw + at] - s * Lp
            v = x2[w]
            zv = v * scale2 + offset2
            dzw = y[w * Lp : (w + 1) * Lp] * gelu_slope(zv)
            dzw = jnp.where(rowc < valid, dzw, 0.0)
            dz2[w] = dzw
            bedge[0, pl.ds(at, 1)] = dzw[0:1]
            bedge[1, pl.ds(at, 1)] = dzw[Lp - 1 : Lp]
            s0 = s0 + fold(dzw)
            s1 = s1 + fold(dzw * zv)
        bacc[0:1] += unfold(s0)
        bacc[1:2] += unfold(s1)

    @pl.when(t == g0 - 1)
    def _():
        b_link[0][...] = bacc[...]
        peers.start(b_link)
        b_halo.start(0, nw)

    @pl.when(t >= g0)
    def _():
        rows = pl.ds(pl.multiple_of(h * plan.Hh, 16), plan.Hh)
        cols = pl.ds(pl.multiple_of((t - g0) * C, 128), C)
        grads[...] = mm(dcT[rows], Y3[:, cols]).astype(BF16)

    @pl.when(last_step())
    def _():
        got = peers.finish(b_link)
        shift, gain = state[SHIFT2 : SHIFT2 + 1], state[GAIN2 : GAIN2 + 1]
        state[SU2 : SU2 + 1] = got[0:1]
        state[SU2 + 1 : SU2 + 2] = (got[1:2] - shift * got[0:1]) / gain
        b_halo.finish()
        for off in range(1, g):
            bulk(off, pl.ds(0, nw)).wait()


def block_phases(plan):
    n = plan.steps
    return n, 2 * n, 3 * n - 1, 4 * n - 1, 4 * n - 1 + plan.T2


class Reduction:
    def __init__(self, plan, batches, out, give, mine, got, spread, half, mate, sems):
        self.plan, self.batches, self.out = plan, batches, out
        self.give, self.mine, self.got, self.spread = give, mine, got, spread
        self.half, self.mate = half, mate
        self.sems = sems
        self.s, self.z, self.i, self.h = plan.place()
        self.c = lax.rem(self.s, 2)
        self.m = lax.div(self.s, 2)
        self.chips = plan.chips

    @staticmethod
    def scratch(plan, batches):
        taps, wide = plan.T1 + 2, plan.C // 2
        full = (taps, plan.chips, plan.g, plan.rb, wide)
        part = (taps, plan.g, plan.rb, wide)
        return [
            pltpu.VMEM((taps, 2, plan.chips, plan.rb, wide), BF16),
            *[pltpu.VMEM(full, BF16)] * 4,
            *[pltpu.VMEM(part, BF16)] * 2,
            pltpu.SemaphoreType.DMA((2, len(batches), 5)),
        ]

    def copy(self, b, phase, src, dst, device):
        return remote(src, dst, self.sems.at[0, b, phase], self.sems.at[1, b, phase], device)

    def finish(self, b, phase, ref, device):
        done = self.copy(b, phase, ref, ref, device)
        done.wait_recv()
        done.wait_send()

    def taps(self, b):
        return pl.ds(*self.batches[b])

    def pair(self):
        return (2 * self.m + (1 - self.c), self.z)

    def far(self, off):
        return (2 * wrap(self.m + off, self.chips) + self.c, self.z)

    def member(self, off):
        return (self.s, self.h * self.plan.g + wrap(self.i + off, self.plan.g))

    def put(self, k, rows):
        wide = self.plan.C // 2
        for j in range(self.plan.g):
            for m in range(self.chips):
                v = rows(j, m)
                left, right = v[:, :wide], v[:, wide:]
                self.mine[k, m, j] = jnp.where(self.c == 0, left, right).astype(BF16)
                self.give[k, m, j] = jnp.where(self.c == 0, right, left).astype(BF16)

    def step0(self, b):
        taps = self.taps(b)
        self.copy(b, 0, self.give.at[taps], self.got.at[taps], self.pair()).start()

    def step1(self, b):
        taps = self.taps(b)
        self.finish(b, 0, self.got.at[taps], self.pair())
        first, count = self.batches[b]
        for k in range(first, first + count):
            v = self.mine[k].astype(F32) + self.got[k].astype(F32)
            self.mine[k] = v.astype(BF16)
        for off in range(1, self.chips):
            src = self.mine.at[taps, wrap(self.m + off, self.chips)]
            self.copy(b, 1, src, self.spread.at[taps, self.m], self.far(off)).start()

    def step2(self, b):
        taps = self.taps(b)
        self.finish(b, 1, self.spread.at[taps, pl.ds(0, self.chips - 1)], self.far(1))
        first, count = self.batches[b]
        for k in range(first, first + count):
            self.spread[k, self.m] = self.mine[k, self.m]
            v = self.spread[k, 0].astype(F32)
            for n in range(1, self.chips):
                v = v + self.spread[k, n].astype(F32)
            self.half[k] = v.astype(BF16)
        for off in range(1, self.plan.g):
            src = self.half.at[taps, wrap(self.i + off, self.plan.g)]
            self.copy(b, 2, src, self.mate.at[taps, off], self.member(off)).start()

    def step3(self, b):
        taps = self.taps(b)
        self.finish(b, 2, self.mate.at[taps, pl.ds(1, self.plan.g - 1)], self.member(1))
        first, count = self.batches[b]
        for k in range(first, first + count):
            v = self.half[k, self.i].astype(F32)
            for off in range(1, self.plan.g):
                v = v + self.mate[k, off].astype(F32)
            self.out[k, self.c, self.m] = v.astype(BF16)
        mine = self.out.at[taps, self.c, self.m]
        for off in range(1, self.chips):
            self.copy(b, 3, mine, mine, self.far(off)).start()

    def step4(self, b):
        taps = self.taps(b)
        self.finish(b, 3, self.out.at[taps, self.c, pl.ds(0, self.chips - 1)], self.far(1))
        mine = self.out.at[taps, self.c]
        self.copy(b, 4, mine, mine, self.pair()).start()

    def step5(self, b):
        self.finish(b, 4, self.out.at[self.taps(b), self.c], self.pair())


def tail_turns(plan):
    nD = plan.steps
    first = max(nD - 1, 1)
    turns = [("x", n) for n in range(first)] + [("d", n) for n in range(first, nD)]
    turns += [("w", n) for n in range(plan.T1)]
    return turns + [("x", n) for n in range(first, nD)]


def tail_batches(plan):
    return [(plan.T1, 2), (0, 3), (3, plan.T1 - 3)]


def tail_kernel(plan, lens, dz2, dzland, x2, x2land, cot, beyond, x, X5_hbm, taps, grads, pgrad,
                old, half_state,
                gz, gz_got, sums, summed,
                ext, D3, D0T, wcat, pick, eye, cols, y, part, split, acc, X5, X5_sems,
                bulk_sems, *rest):
    t = pl.program_id(0)
    s, z, i, h = plan.place()
    L, Lp, C, wb, g, nw = plan.L, plan.Lp, plan.C, plan.wb, plan.g, plan.nw
    Ch, cs, T1 = plan.Ch, plan.cs, plan.T1
    M = wb * Lp
    nD = plan.steps
    turns = tail_turns(plan)
    last = len(turns) - 1
    peers = group_peers(plan)
    red = Reduction(plan, tail_batches(plan), *rest[:8])
    link = rest[8:]

    def member(off):
        return (s, h * g + wrap(i + off, g))

    def send(first, count):
        rows = pl.ds(first, count)
        for off in range(1, g):
            remote(
                part.at[off - 1, rows],
                gz_got.at[off, rows],
                bulk_sems.at[0, off],
                bulk_sems.at[1, off],
                member(off),
            ).start()

    def X5_copy(k):
        cols = pl.ds(pl.multiple_of(k * C, 128), C)
        return pltpu.make_async_copy(X5_hbm.at[:, cols], X5.at[k % 2], X5_sems.at[k % 2])

    def when(at):
        return pl.when(t == min(at, last))

    def turn(kind, k):
        return turns.index((kind, k)) if (kind, k) in turns else last

    def turn_of(kind):
        index = jnp.int32(0)
        here = False
        for n, (what, k) in enumerate(turns):
            if what == kind:
                index = jnp.where(t == n, k, index)
                here = (t == n) | here
        return here, index

    @when(0)
    def _():
        greet(peers.others)
        acc[...] = jnp.zeros_like(acc)
        pick[...] = pick_matrix(L)
        eye[...] = eye_matrix(Ch, Ch, 0)
        mean, rho = norm_of(half_state[ST1 : ST1 + 2], 2.0 * total_of(lens))
        scale = half_state[GAIN1 : GAIN1 + 1] * rho
        offset = half_state[SHIFT1 : SHIFT1 + 1] - mean * scale
        for k, row in enumerate((scale, offset)):
            cols[k] = column(row, L)
        for first in range(0, Ch, 64):
            rows = slice(first, min(first + 64, Ch))
            for r, parts in enumerate((((0,), (1, 2), (3, 4)), ((0, 1), (2, 3), (4,)))):
                for k, which in enumerate(parts):
                    v = taps[which[0], rows]
                    if len(which) > 1:
                        v = (v.astype(F32) + taps[which[1], rows].astype(F32)).astype(BF16)
                    at = r * Ch
                    wcat[at + rows.start : at + rows.stop, k * C : (k + 1) * C] = v
        meet(peers.others)

    @pl.when(t < nD)
    def _():
        total = total_of(lens)
        mean, rho = norm_of(old[ST2 : ST2 + 2], total)
        gr = old[GAIN2 : GAIN2 + 1] * rho
        sg = old[SU2 : SU2 + 1] / total
        gg = old[SU2 + 1 : SU2 + 2] / total
        rowc = rows_of((Lp, C))
        row1 = rows_of((1, C))

        by_dz = 0.5 * gr
        by_v = -0.5 * gr * rho * gg
        by_1 = 0.5 * gr * (mean * rho * gg - sg)

        def back(dout, dz, v):
            return 0.5 * dout + by_dz * dz + by_v * v + by_1

        def grad_of(w):
            at = t * wb + w
            valid = lens[i * nw + at] - s * Lp
            d = back(cot[w].astype(F32), dz2[w], x2[w])
            d = jnp.where(rowc < valid, d, 0.0)
            one = pl.ds(at, 1)
            dl = back(beyond[0, 2, one, :], dzland[0, one, :], x2land[0, w, EDGE - 1 : EDGE].astype(F32))
            dl = jnp.where((row1 - 1 < valid) & (s > 0), dl, 0.0)
            dh = back(beyond[1, 2, one, :], dzland[1, one, :], x2land[1, w, 0:1].astype(F32))
            dh = jnp.where(row1 + Lp < valid, dh, 0.0)
            ext[w, 7:8] = dl
            ext[w, 8 : 8 + Lp] = d
            ext[w, 8 + Lp : 9 + Lp] = dh
            top, end = w * Lp, (w + 1) * Lp
            D3[t, top:end, 0:C] = ext[w, 9 : 9 + Lp].astype(BF16)
            D3[t, top:end, C : 2 * C] = d.astype(BF16)
            D3[t, top:end, 2 * C : 3 * C] = ext[w, 7 : 7 + Lp].astype(BF16)

        for w in range(wb):
            grad_of(w)
        half = D3[t, :, pl.ds(pl.multiple_of(C + h * Ch, 128), Ch)]
        D0T[:, pl.ds(pl.multiple_of(t * M, 128), M)] = half.T

    here_x, bx = turn_of("x")

    @pl.when(here_x)
    def _():
        lanes = lanes_of((Ch, L))

        def through(w):
            valid = 2 * lens[i * nw + bx * wb + w] - s * L
            top, end = w * Lp, (w + 1) * Lp
            v = mm_nt(eye[...], x[w])
            da = jnp.concatenate([y[0:Ch, top:end], y[Ch:, top:end]], axis=1)
            da = mm(da.astype(BF16), pick[...])
            zv = v * cols[0] + cols[1]
            dzw = da * gelu_slope(zv)
            dzw = jnp.where(lanes < valid, dzw, 0.0)
            acc[0] += fold_lanes(dzw)
            acc[1] += fold_lanes(dzw * zv)
            split[w % 2] = dzw.astype(BF16)
            for off in range(g):
                rows = pl.ds(pl.multiple_of(lax.rem(i + off, g) * cs, 16), cs)
                if off == 0:
                    gz[w] = split[w % 2, rows]
                else:
                    part[off - 1, bx * wb + w] = split[w % 2, rows]

        nh = 2 if wb % 2 == 0 and wb * Lp // 2 % 128 == 0 else 1
        n = wb // nh
        for hf in range(nh):
            rows = slice(hf * n * Lp, (hf + 1) * n * Lp)
            y[:, rows] = mm_nt(wcat[...], D3[bx, rows])
            for w in range(hf * n, (hf + 1) * n):
                through(w)

    @when(0)
    def _():
        hs = plan.H // plan.nz
        rb = plan.rb
        for u in range(2):

            def rows(j, m, u=u):
                side, r = m * rb // hs, m * rb % hs
                n = 2 * side + u
                rows = slice(j * hs + r, j * hs + r + rb)
                v = grads[rows, n * C : (n + 1) * C] if n < plan.T2 else pgrad[rows]
                return v.astype(F32)

            red.put(T1 + u, rows)
        red.step0(0)

    @when(nD - 1)
    def _():
        X5_copy(0).start()

    here_w, k = turn_of("w")

    @pl.when(here_w)
    def _():
        @pl.when(k < T1 - 1)
        def _():
            X5_copy(k + 1).start()

        X5_copy(k).wait()
        y[0:Ch, 0:C] = mm(D0T[...], X5[lax.rem(k, 2)])
        rb = plan.rb
        red.put(k, lambda j, m: y[j * cs + m * rb : j * cs + (m + 1) * rb, 0:C])

    @pl.when(here_x & (bx < nD - 1))
    def _():
        send(bx * wb, wb)

    @when(turn("x", nD - 1))
    def _():
        send((nD - 1) * wb, wb // 2)

    for at, step, batch in (
        (1, red.step1, 0),
        (max(nD - 1, 2), red.step2, 0),
        (turn("w", 2), red.step0, 1),
        (turn("w", 3), red.step1, 1),
        (turn("w", T1 - 1), red.step0, 2),
        (last, red.step1, 2),
        (last, red.step2, 1),
        (last, red.step3, 0),
        (last, red.step2, 2),
    ):

        @when(at)
        def _():
            step(batch)

    @when(last)
    def _():
        send(nw - wb + wb // 2, wb - wb // 2)

    @when(turn("x", nD - 1))
    def _():
        packet = link[0]
        packet[...] = jnp.zeros_like(packet)
        packet[0:1, 0:Ch] = jnp.sum(acc[0].T, axis=0, keepdims=True)
        packet[1:2, 0:Ch] = jnp.sum(acc[1].T, axis=0, keepdims=True)
        peers.start(link)

    @when(last)
    def _():
        red.step3(1)
        red.step4(0)
        red.step3(2)
        red.step4(1)
        got = peers.finish(link)[:, 0:Ch]
        shift, gain = half_state[SHIFT1 : SHIFT1 + 1], half_state[GAIN1 : GAIN1 + 1]
        sums[0:1] = got[0:1]
        sums[1:2] = (got[1:2] - shift * got[0:1]) / gain
        red.step4(2)
        for b in range(3):
            red.step5(b)
        own = pltpu.make_async_copy(red.out, summed, X5_sems.at[0])
        own.start()
        for off in range(1, g):
            done = remote(
                part.at[off - 1],
                gz_got.at[off],
                bulk_sems.at[0, off],
                bulk_sems.at[1, off],
                member(off),
            )
            done.wait_recv()
            done.wait_send()
        own.wait()


def input_grad_kernel(plan, wg, lens, x, gz, gz_got, sums, res, res_got, summed,
                      state, half_state,
                      out, out_result, conv_grad, dil_grad, point_grad,
                      g1, b1, g2, b2, g3, b3, pb, eye, cols, xt):
    t = pl.program_id(0)
    s, z, i, h = plan.place()
    L, Ch, cs = plan.L, plan.Ch, plan.cs
    turn = plan.nw // wg
    mine = pl.ds(pl.multiple_of(i * cs, 16), cs)

    @pl.when(first_step())
    def _():
        n = 2.0 * total_of(lens)
        mean, rho = norm_of(half_state[ST1 : ST1 + 2], n)
        gr = half_state[GAIN1 : GAIN1 + 1] * rho
        gg = sums[1:2] / n * rho
        for k, row in enumerate((gr, -gr * gg, gr * (mean * gg - sums[0:1] / n))):
            xt[...] = column(row, L)
            cols[k] = xt[mine]
        eye[...] = eye_matrix(cs, Ch, i * cs)

        def mine_of(src, at, which, count, *dsts):
            n = dsts[0].shape[1]
            for k in range(count):

                @pl.when(which == k)
                def _():
                    for dst, r in zip(dsts, at):
                        dst[...] = src[r : r + 1, k * n : (k + 1) * n]

        mine_of(sums, (1, 0), i, plan.g, g1, b1)
        mine_of(state, (SU2 + 1, SU2), z, plan.nz, g2, b2)
        mine_of(state, (SU3 + 1, SU3), z, plan.nz, g3, b3)
        mine_of(state, (BSUM,), z, plan.nz, pb)

    own = lax.div(t, turn) == i
    for w in range(wg):
        out_result[w] = jnp.where(own, res[0, w], res_got[0, w])

    C, T1, hs, rb, wide = plan.C, plan.T1, plan.H // plan.nz, plan.rb, plan.C // 2
    count = plan.NW // wg
    turns = min(count, plan.chips)
    per, every = plan.chips // turns, count // turns

    def spread(chunk):
        for n in range(per):
            m = chunk * per + n
            side, r = m * rb // hs, m * rb % hs
            for c in range(2):
                at = slice(c * wide, (c + 1) * wide)
                for k in range(T1):
                    conv_grad[k, n * rb : (n + 1) * rb, at] = summed[k, c, n].astype(F32)
                for u in range(2):
                    v = summed[T1 + u, c, n].astype(F32)
                    if 2 * side + u < plan.T2:
                        dil_grad[2 * side + u, r : r + rb, at] = v
                    else:
                        point_grad[r : r + rb, at] = v

    for chunk in range(turns):
        pl.when(t == chunk * every)(partial(spread, chunk))

    lanes = lanes_of((cs, L))
    for w in range(wg):
        valid = 2 * lens[t * wg + w] - s * L
        v = mm_nt(eye[...], x[w])
        dz = jnp.where(own, gz[w], gz_got[0, w]).astype(F32)
        r = cols[0] * dz + v * cols[1] + cols[2]
        out[w] = jnp.where(lanes < valid, r, 0.0).astype(BF16)


def call(kernel, plan, name, steps, ins, outs, scratch, flops, nbytes, cid=None):
    extra = {} if cid is None else dict(collective_id=cid, has_side_effects=True)
    return pl.pallas_call(
        partial(kernel, plan),
        grid=(steps,),
        in_specs=[SMEM] + [spec for spec, _ in ins],
        out_specs=[spec for spec, _, _ in outs],
        out_shape=[jax.ShapeDtypeStruct(shape, dtype) for _, shape, dtype in outs],
        scratch_shapes=scratch,
        compiler_params=pltpu.CompilerParams(vmem_limit_bytes=VMEM_LIMIT, **extra),
        cost_estimate=pl.CostEstimate(
            flops=int(flops), bytes_accessed=int(nbytes), transcendentals=0
        ),
        name=name,
    )


def per_device(
    inputs,
    lengths,
    input_gain,
    input_shift,
    conv_weight,
    branch_gain,
    branch_shift,
    dilated_tap_weight,
    mixer_gain,
    mixer_shift,
    point_weight,
    point_bias,
    cotangent,
):
    NW, L, C = inputs.shape
    Lp = L // 2
    nz = lax.axis_size("ch")
    R = 2
    plan = Plan(
        ns=lax.axis_size("seq"),
        nz=nz,
        R=R,
        NW=NW,
        L=L,
        C=C,
        H=mixer_gain.shape[0] * nz,
        T1=conv_weight.shape[0],
        T2=dilated_tap_weight.shape[0],
        wb=min(NW * R // nz, max(1, 512 // Lp)),
    )
    g, nw, cs, Ch, H, Hh, wb = plan.g, plan.nw, plan.cs, plan.Ch, plan.H, plan.Hh, plan.wb
    T1, T2, steps = plan.T1, plan.T2, plan.steps
    M = wb * Lp
    hs = H // nz
    lens = lengths.astype(jnp.int32)

    def row(a):
        return a.reshape(1, a.shape[0])

    def grp():
        return lax.rem(lax.axis_index("ch"), g)

    def half():
        return lax.div(lax.axis_index("ch"), g)

    def core():
        return lax.rem(lax.axis_index("seq"), 2)

    def chip4():
        return lax.div(lax.axis_index("seq"), plan.ns // 4)

    def whole(*shape):
        return pl.BlockSpec(shape, lambda t: (0,) * len(shape), pipeline_mode=pl.Buffered(1))

    def const(*shape):
        return pl.BlockSpec(shape, lambda t: (0,) * len(shape))

    def win(*shape):
        return pl.BlockSpec(shape, lambda t: (t,) + (0,) * (len(shape) - 1))

    def arg_win(n, width):
        return pl.BlockSpec((wb, n, width), lambda t: (grp() * steps + t, 0, 0))

    def ins(*pairs):
        return [p for p in pairs]

    share = NW // nz
    nm = max(1, share // wb)

    def edge_spec(n):
        return pl.BlockSpec(
            (nw, 16, C), lambda t: (grp(), n, 0), pipeline_mode=pl.Buffered(1)
        )

    def head_block(t):
        own = lax.div(lax.axis_index("ch") * share, wb) + t
        return jnp.where(t < nm, own, grp() * steps + t - nm), 0, 0

    def after(*shape):
        return pl.BlockSpec(
            shape, lambda t: (jnp.maximum(t - nm, 0),) + (0,) * (len(shape) - 1)
        )

    pairs = ins(
        (pl.BlockSpec((wb, L, C), head_block), inputs),
        (edge_spec(0), inputs),
        (edge_spec(L // 16 - 1), inputs),
        (edge_spec(0), cotangent),
        (edge_spec(Lp // 16 - 1), cotangent),
        (whole(1, cs), row(branch_gain)),
        (whole(1, cs), row(branch_shift)),
        (whole(1, cs), row(point_bias)),
        (whole(1, H // nz), row(mixer_gain)),
        (whole(1, H // nz), row(mixer_shift)),
        (ANY, conv_weight.reshape(T1 * C, C)),
        (whole(C), input_gain),
        (whole(C), input_shift),
        (
            pl.BlockSpec(
                (1, hs, C // 2),
                lambda t: (jnp.minimum(chip4(), T2 - 1), 0, core()),
                pipeline_mode=pl.Buffered(1),
            ),
            jnp.swapaxes(dilated_tap_weight, 1, 2),
        ),
        (
            pl.BlockSpec(
                (hs, C // 2), lambda t: (0, core()), pipeline_mode=pl.Buffered(1)
            ),
            point_weight,
        ),
    )
    plane, line, group = plane_peers(plan), line_peers(plan), group_peers(plan)
    state_shape = (STATE, C)
    edges2, edges3 = (2, nw, EDGE, C), (2, nw, EDGE, H)
    X5, x2, land2, state, beyond, full = call(
        lambda plan, *refs: head_kernel(plan, nm, *refs),
        plan,
        "head",
        nm + steps,
        pairs,
        [
            (after(M, T1 * C), (nw * Lp, T1 * C), BF16),
            (after(wb, Lp, C), (nw, Lp, C), F32),
            (ANY, edges2, BF16),
            (const(*state_shape), state_shape, F32),
            (const(2, 3, nw, C), (2, 3, nw, C), F32),
            (ANY, (2, T2 + 1, nz, hs, C // 2), BF16),
        ],
        [
            pltpu.VMEM((2, 8, C), F32),
            pltpu.VMEM((2, 3, nw, C), F32),
            pltpu.VMEM((2, 3, nw, C), F32),
            pltpu.VMEM((T1 * Lp, L), BF16),
            pltpu.VMEM(edges2, BF16),
            pltpu.VMEM((2, C), F32),
            pltpu.VMEM((T1 * C, C), BF16),
            pltpu.SemaphoreType.DMA,
            pltpu.VMEM((hs, C // 2), BF16),
            pltpu.SemaphoreType.DMA((2, 4)),
            HALO_SEMS,
            HALO_SEMS,
        ]
        + plane.scratch(2, C)
        + line.scratch(3, C)
        + group.scratch(2, C),
        2 * nw * Lp * T1 * C * C,
        nw * Lp * C * 20,
        cid=1,
    )(lens, *[a for _, a in pairs])

    full = full.reshape(2, T2 + 1, H, C // 2)
    taps_spec = whole(2, T2, H, C // 2)
    pw_spec = pl.BlockSpec(
        (2, 1, H, C // 2), lambda t: (0, T2, 0, 0), pipeline_mode=pl.Buffered(1)
    )

    def early(*shape):
        return pl.BlockSpec(
            shape, lambda t: (jnp.minimum(t, steps - 1),) + (0,) * (len(shape) - 1)
        )

    def early_land(width):
        return pl.BlockSpec(
            (2, wb, EDGE, width), lambda t: (0, jnp.minimum(t, steps - 1), 0, 0)
        )

    def half_of(n):
        return pl.BlockSpec((n, Ch), lambda t: (0, half()), pipeline_mode=pl.Buffered(1))

    cot_spec = pl.BlockSpec(
        (wb, Lp, C), lambda t: (grp() * steps + jnp.minimum(t, steps - 1), 0, 0)
    )

    p0, r0, b0, g0, block_steps = block_phases(plan)

    def at_phase(first):
        return lambda t: jnp.clip(t - first, 0, steps - 1)

    in_p, in_b = at_phase(p0), at_phase(b0)
    pairs = ins(
        (
            pl.BlockSpec(
                (wb, Lp, C),
                lambda t: (jnp.where(t < p0 + steps, jnp.minimum(t, steps - 1), in_b(t)), 0, 0),
            ),
            x2,
        ),
        (
            pl.BlockSpec(
                (wb, Lp, Ch),
                lambda t: (jnp.clip(t - r0 + 1, 0, steps - 1), 0, half()),
            ),
            x2,
        ),
        (early_land(C), land2),
        (pl.BlockSpec((wb, Lp, C), lambda t: (grp() * steps + in_p(t), 0, 0)), cotangent),
        (taps_spec, full),
        (pw_spec, full),
        (whole(*state_shape), state),
        (half_of(STATE), state),
    )
    dz2, grads, pgrad, res, dland2, state, res_got = call(
        block_kernel,
        plan,
        "block",
        block_steps,
        pairs,
        [
            (pl.BlockSpec((wb, Lp, C), lambda t: (in_b(t), 0, 0)), (nw, Lp, C), F32),
            (
                pl.BlockSpec((Hh, C), lambda t: (0, jnp.maximum(t - g0, 0))),
                (Hh, T2 * C),
                BF16,
            ),
            (const(Hh, C), (Hh, C), BF16),
            (const(g, nw, cs, Lp), (g, nw, cs, Lp), BF16),
            (ANY, (2, nw, C), F32),
            (const(*state_shape), state_shape, F32),
            (ANY, (g, nw, cs, Lp), BF16),
        ],
        [
            pltpu.VMEM((wb, Lp + 2 * EDGE, C), F32),
            pltpu.VMEM((H, T2 * C), BF16),
            pltpu.VMEM((T2 * H, C), BF16),
            pltpu.VMEM((H, C), BF16),
            pltpu.VMEM((nw * Lp, T2 * C), BF16),
            pltpu.VMEM((nw, Lp, H), F32),
            pltpu.VMEM((nw, Lp, H), F32),
            pltpu.VMEM((M, H), F32),
            pltpu.VMEM((nw * Lp, H), BF16),
            pltpu.VMEM((H, nw * Lp), BF16),
            pltpu.VMEM((nw * Lp, C), BF16),
            pltpu.VMEM((M, T2 * H), BF16),
            pltpu.VMEM((H, nw * Lp), BF16),
            pltpu.VMEM(edges3, BF16),
            pltpu.VMEM(edges3, BF16),
            pltpu.VMEM((1, 2 * H), F32),
            pltpu.VMEM(edges3, BF16),
            pltpu.VMEM(edges3, BF16),
            pltpu.VMEM((2, C), F32),
            pltpu.VMEM((2, nw, C), F32),
            pltpu.VMEM((2, C), F32),
            pltpu.SemaphoreType.DMA((3, 2, 2)),
            pltpu.SemaphoreType.DMA((2, g)),
        ]
        + group.scratch(1, 2 * H)
        + group.scratch(2, C)
        + group.scratch(2, C),
        nw * Lp * C * H * (6 * T2 + 6),
        nw * Lp * C * 30,
        cid=3,
    )(lens, *[a for _, a in pairs])

    chips, rb = plan.chips, plan.rb
    turns_t = tail_turns(plan)

    def x_block(t):
        block = jnp.int32(0)
        for n, (what, k) in enumerate(turns_t):
            if what == "x":
                block = jnp.where(t >= n, k, block)
        return block

    sshape = (T1 + 2, 2, chips, rb, C // 2)
    pairs = ins(
        (early(wb, Lp, C), dz2),
        (whole(2, nw, C), dland2),
        (early(wb, Lp, C), x2),
        (early_land(C), land2),
        (cot_spec, cotangent),
        (whole(2, 3, nw, C), beyond),
        (
            pl.BlockSpec(
                (wb, L, Ch), lambda t: (grp() * steps + x_block(t), 0, half())
            ),
            inputs,
        ),
        (ANY, X5),
        (
            pl.BlockSpec(
                (T1, Ch, C), lambda t: (0, half(), 0), pipeline_mode=pl.Buffered(1)
            ),
            conv_weight,
        ),
        (whole(Hh, T2 * C), grads),
        (whole(Hh, C), pgrad),
        (whole(*state_shape), state),
        (half_of(STATE), state),
    )
    gz, gz_got, sums1, summed = call(
        tail_kernel,
        plan,
        "tail",
        len(turns_t),
        pairs,
        [
            (pl.BlockSpec((wb, cs, L), lambda t: (x_block(t), 0, 0)), (nw, cs, L), BF16),
            (ANY, (g, nw, cs, L), BF16),
            (const(2, Ch), (2, Ch), F32),
            (ANY, sshape, BF16),
        ],
        [
            pltpu.VMEM((wb, Lp + 16, C), F32),
            pltpu.VMEM((steps, M, 3 * C), BF16),
            pltpu.VMEM((Ch, nw * Lp), BF16),
            pltpu.VMEM((2 * Ch, 3 * C), BF16),
            pltpu.VMEM((L, L), BF16),
            pltpu.VMEM((Ch, Ch), BF16),
            pltpu.VMEM((2, Ch, L), F32),
            pltpu.VMEM((2 * Ch, max(M, C)), F32),
            pltpu.VMEM((g - 1, nw, cs, L), BF16),
            pltpu.VMEM((2, Ch, L), BF16),
            pltpu.VMEM((2, Ch, min(L, 128)), F32),
            pltpu.VMEM((2, nw * Lp, C), BF16),
            pltpu.SemaphoreType.DMA((2,)),
            pltpu.SemaphoreType.DMA((2, g)),
        ]
        + Reduction.scratch(plan, tail_batches(plan))
        + group.scratch(2, C),
        2 * nw * Lp * (6 + T1) * C * Ch,
        nw * Lp * C * 40,
        cid=6,
    )(lens, *[a for _, a in pairs])

    wg = min(2 * wb, nw)
    count = NW // wg
    turn = nw // wg
    turns = min(count, chips)

    def own_block(t):
        return jnp.where(lax.div(t, turn) == grp(), lax.rem(t, turn), 0)

    def got_slot(t):
        off = lax.rem(grp() - lax.div(t, turn) + g, g)
        return jnp.maximum(off, 1), jnp.where(off > 0, lax.rem(t, turn), 0)

    pairs = ins(
        (pl.BlockSpec((wg, L, Ch), lambda t: (t, 0, half())), inputs),
        (pl.BlockSpec((wg, cs, L), lambda t: (own_block(t), 0, 0)), gz),
        (pl.BlockSpec((1, wg, cs, L), lambda t: got_slot(t) + (0, 0)), gz_got),
        (whole(2, Ch), sums1),
        (pl.BlockSpec((1, wg, cs, Lp), lambda t: (grp(), own_block(t), 0, 0)), res),
        (pl.BlockSpec((1, wg, cs, Lp), lambda t: got_slot(t) + (0, 0)), res_got),
        (
            pl.BlockSpec(
                (T1 + 2, 2, chips // turns, rb, C // 2),
                lambda t: (0, 0, t * turns // count, 0, 0),
            ),
            summed,
        ),
        (whole(*state_shape), state),
        (half_of(STATE), state),
    )
    outs = call(
        lambda plan, *refs: input_grad_kernel(plan, wg, *refs),
        plan,
        "input_grad",
        count,
        pairs,
        [
            (win(wg, cs, L), (NW, cs, L), BF16),
            (win(wg, cs, Lp), (NW, cs, Lp), BF16),
            (
                pl.BlockSpec((T1, cs // turns, C), lambda t: (0, t * turns // count, 0)),
                (T1, cs, C),
                F32,
            ),
            (const(T2, hs, C), (T2, hs, C), F32),
            (const(hs, C), (hs, C), F32),
        ]
        + [(const(1, n), (1, n), F32) for n in (cs, cs, cs, cs, hs, hs, cs)],
        [
            pltpu.VMEM((cs, Ch), BF16),
            pltpu.VMEM((3, cs, L), F32),
            pltpu.VMEM((Ch, L), F32),
        ],
        2 * NW * L * Ch * cs,
        NW * L * cs * 8,
    )(lens, *[a for _, a in pairs])
    grad, result, conv_grad, dil_grad, point_grad = outs[:5]
    g1, b1, g2, b2, g3, b3, pb = [a[0] for a in outs[5:]]
    return (
        jnp.swapaxes(result, 1, 2),
        jnp.swapaxes(grad, 1, 2),
        jnp.swapaxes(conv_grad, 1, 2),
        g1,
        b1,
        g2,
        b2,
        jnp.swapaxes(dil_grad, 1, 2),
        g3,
        b3,
        point_grad,
        pb,
    )


def solution(mesh):
    in_specs = (
        P(None, "seq", None),
        P(),
        P(),
        P(),
        P(),
        P("ch"),
        P("ch"),
        P(None, None, "ch"),
        P("ch"),
        P("ch"),
        P("ch", None),
        P("ch"),
        P(None, "seq", None),
    )
    out_specs = (
        P(None, "seq", "ch"),
        P(None, "seq", "ch"),
        P(None, None, "ch"),
        P("ch"),
        P("ch"),
        P("ch"),
        P("ch"),
        P(None, None, "ch"),
        P("ch"),
        P("ch"),
        P("ch", None),
        P("ch"),
    )
    return jax.shard_map(
        per_device, mesh=mesh, in_specs=in_specs, out_specs=out_specs, check_vma=False
    )
```

```python
from functools import partial
from typing import NamedTuple

import jax
import jax.numpy as jnp
from jax import lax
from jax.experimental import pallas as pl
from jax.experimental.pallas import tpu as pltpu
from jax.sharding import PartitionSpec as P

DIL = 14
EDGE = 16
EPS = 1e-05
GC0 = 0.7978845608028654
GC1 = 0.044715
F32 = jnp.float32
BF16 = jnp.bfloat16
MESH = pl.DeviceIdType.MESH
VMEM_LIMIT = 58 * 1024 * 1024
ANY = pl.BlockSpec(memory_space=pl.ANY)
SMEM = pl.BlockSpec(memory_space=pltpu.SMEM)


ST1, GAIN2, SHIFT2, BIAS, GAIN3, SHIFT3, GAIN1, SHIFT1, ST2, ST3, SU3, BSUM, SU2 = (
    0, 2, 3, 4, 5, 6, 7, 8, 9, 11, 13, 15, 16
)
STATE = 24


class Plan(NamedTuple):
    ns: int
    nz: int
    R: int
    NW: int
    L: int
    C: int
    H: int
    T1: int
    T2: int
    wb: int

    @property
    def g(self):
        return self.nz // self.R

    @property
    def nw(self):
        return self.NW // self.g

    @property
    def Lp(self):
        return self.L // 2

    @property
    def cs(self):
        return self.C // self.nz

    @property
    def Ch(self):
        return self.C // self.R

    @property
    def Hh(self):
        return self.H // self.R

    @property
    def steps(self):
        return self.nw // self.wb

    @property
    def chips(self):
        return self.ns // 2

    @property
    def rb(self):
        return self.cs // self.chips

    def place(self):
        s, z = lax.axis_index("seq"), lax.axis_index("ch")
        return s, z, lax.rem(z, self.g), lax.div(z, self.g)


def gelu(z):
    t = jnp.tanh(z * (GC0 + (GC0 * GC1) * (z * z)))
    return z * (0.5 + 0.5 * t)


def gelu_both(z):
    sq = z * z
    t = jnp.tanh(z * (GC0 + (GC0 * GC1) * sq))
    h = 0.5 + 0.5 * t
    v = z * h
    return v, h + v * (1.0 - t) * (GC0 + (3.0 * GC0 * GC1) * sq)


def gelu_slope(z):
    return gelu_both(z)[1]


def fold(v):
    return jnp.sum(v.reshape(v.shape[0] // 8, 8, v.shape[1]), axis=0)


def fold_lanes(v):
    out = v[:, 0:128]
    for k in range(128, v.shape[1], 128):
        out = out + v[:, k : k + 128]
    return out


def unfold(v):
    return jnp.sum(v, axis=0, keepdims=True)


def rows_of(shape):
    return lax.broadcasted_iota(jnp.int32, shape, 0)


def lanes_of(shape):
    return lax.broadcasted_iota(jnp.int32, shape, 1)


def total_of(lens):
    n = lens[0]
    for k in range(1, lens.shape[0]):
        n = n + lens[k]
    return n.astype(F32)


def norm_of(stats, total):
    mean = stats[0:1] / total
    square = stats[1:2] / total
    return mean, lax.rsqrt(square - mean * mean + EPS)


def flat(ref):
    return ref[...].reshape(1, ref.shape[0])


def column(row, n):
    return jnp.broadcast_to(row, (n, row.shape[1])).T


def mm(a, b):
    return jnp.dot(a, b, preferred_element_type=F32)


def mm_nt(a, b):
    return lax.dot_general(a, b, (((1,), (1,)), ((), ())), preferred_element_type=F32)


def mm_tn(a, b):
    return lax.dot_general(a, b, (((0,), (0,)), ((), ())), preferred_element_type=F32)


def mm_tt(a, b):
    return lax.dot_general(a, b, (((0,), (1,)), ((), ())), preferred_element_type=F32)


def eye_matrix(n, m, first):
    return jnp.where(lanes_of((n, m)) == rows_of((n, m)) + first, 1.0, 0.0).astype(BF16)


def pick_matrix(L):
    r, n = rows_of((L, L)), lanes_of((L, L))
    bin_of = 2 * r - jnp.where(r >= L // 2, L - 1, 0)
    return jnp.where(n == bin_of, 1.0, 0.0).astype(BF16)


def remote(src, dst, send, recv, device):
    return pltpu.make_async_remote_copy(
        src_ref=src,
        dst_ref=dst,
        send_sem=send,
        recv_sem=recv,
        device_id=device,
        device_id_type=MESH,
    )


def wrap(v, n):
    return jnp.where(v >= n, v - n, v)


def greet(devices):
    barrier = pltpu.get_barrier_semaphore()
    for device in devices:
        pl.semaphore_signal(barrier, inc=1, device_id=device, device_id_type=MESH)


def meet(devices):
    pl.semaphore_wait(pltpu.get_barrier_semaphore(), len(devices))


class Peers:
    def __init__(self, me, others):
        self.me, self.others = me, others
        self.count = len(others) + 1

    def start(self, link):
        packet, buf, sems = link
        for device in self.others:
            remote(packet, buf.at[self.me], sems.at[0], sems.at[1], device).start()

    def finish(self, link):
        packet, buf, sems = link
        buf[self.me] = packet[...]
        rest = buf.at[pl.ds(0, self.count - 1)]
        done = remote(rest, rest, sems.at[0], sems.at[1], self.others[0])
        done.wait_recv()
        acc = buf[0]
        for q in range(1, self.count):
            acc = acc + buf[q]
        done.wait_send()
        return acc

    def scratch(self, rows, width):
        return [
            pltpu.VMEM((rows, width), F32),
            pltpu.VMEM((self.count, rows, width), F32),
            pltpu.SemaphoreType.DMA((2,)),
        ]


def group_peers(plan):
    s, z, i, h = plan.place()
    g = plan.g
    others = [
        (wrap(s + a, plan.ns), h * g + wrap(i + b, g))
        for a in range(plan.ns)
        for b in range(g)
        if a or b
    ]
    return Peers(s * g + i, others)


def plane_peers(plan):
    s, z, i, h = plan.place()
    return Peers(s, [(wrap(s + a, plan.ns), z) for a in range(1, plan.ns)])


def line_peers(plan):
    s, z, i, h = plan.place()
    return Peers(z, [(s, wrap(z + a, plan.nz)) for a in range(1, plan.nz)])


class Halo:
    def __init__(self, plan, edge, land, sems):
        self.edge, self.land, self.sems = edge, land, sems
        s, z, _, _ = plan.place()
        self.to = ((wrap(s + plan.ns - 1, plan.ns), z), (wrap(s + 1, plan.ns), z))

    def copy(self, side, rows):
        return remote(
            self.edge.at[side, rows],
            self.land.at[1 - side, rows],
            self.sems.at[0, side],
            self.sems.at[1, side],
            self.to[side],
        )

    def start(self, first, count):
        for side in range(2):
            self.copy(side, pl.ds(first, count)).start()

    def finish(self):
        for side in range(2):
            done = self.copy(side, pl.ds(0, self.land.shape[1]))
            done.wait_recv()
            done.wait_send()


HALO_SEMS = pltpu.SemaphoreType.DMA((2, 2))


class Gather:
    def __init__(self, plan, part, full, sems):
        self.plan, self.part, self.full, self.sems = plan, part, full, sems
        self.s, self.z, self.i, self.h = plan.place()
        self.c, self.m = lax.rem(self.s, 2), lax.div(self.s, 2)
        self.chips = plan.chips
        self.every = self.chips // 4
        self.tap = lax.div(self.m, self.every)
        self.owner = lax.rem(self.m, self.every) == 0
        self.mine = full.at[self.c, self.tap]

    def others(self):
        g, nz = self.plan.g, self.plan.nz
        return [(self.s, wrap(self.h * g + g + r, nz)) for r in range(nz - g)]

    def far(self, off):
        return (2 * wrap(self.m + off, self.chips) + self.c, self.z)

    def own(self):
        return pltpu.make_async_copy(self.part, self.mine.at[self.z], self.sems.at[0, 0])

    def line(self, off):
        device = (self.s, wrap(self.z + off, self.plan.nz))
        return remote(
            self.part, self.mine.at[self.z], self.sems.at[0, 1], self.sems.at[1, 1], device
        )

    def chip(self, off):
        return remote(self.mine, self.mine, self.sems.at[0, 2], self.sems.at[1, 2], self.far(off))

    def pair(self):
        half = self.full.at[self.c]
        device = (2 * self.m + 1 - self.c, self.z)
        return remote(half, half, self.sems.at[0, 3], self.sems.at[1, 3], device)

    def line_start(self):
        @pl.when(self.owner)
        def _():
            self.own().start()
            for off in range(1, self.plan.nz):
                self.line(off).start()

    def line_finish(self):
        @pl.when(self.owner)
        def _():
            self.own().wait()
            rest = self.mine.at[pl.ds(0, self.plan.nz - 1)]
            device = (self.s, wrap(self.z + 1, self.plan.nz))
            done = remote(rest, rest, self.sems.at[0, 1], self.sems.at[1, 1], device)
            done.wait_recv()
            done.wait_send()

    def chips_start(self):
        @pl.when(self.owner)
        def _():
            for off in range(1, self.chips):
                self.chip(off).start()

    def pair_start(self):
        def taken(count):
            rest = self.full.at[self.c, pl.ds(0, count)]
            return remote(rest, rest, self.sems.at[0, 2], self.sems.at[1, 2], self.far(1))

        @pl.when(self.owner)
        def _():
            taken(3).wait_recv()
            for off in range(1, self.chips):
                self.chip(off).wait_send()

        if self.every > 1:

            @pl.when(jnp.logical_not(self.owner))
            def _():
                taken(4).wait_recv()

        self.pair().start()

    def pair_finish(self):
        done = self.pair()
        done.wait_recv()
        done.wait_send()


def first_step():
    return pl.program_id(0) == 0


def last_step():
    return pl.program_id(0) == pl.num_programs(0) - 1


def head_kernel(plan, nm, lens, x, xtop, xend, ctop, cend, g2, s2, pb, g3, s3,
                w_hbm, gain, shift, taps, pw,
                X5, x2, land, state, beyond_out, full,
                macc, beyond, xedge, sel, edge, acc, w_ref, w_sem, part,
                gather_sems, xhalo_sems, halo_sems, *links):
    t = pl.program_id(0)
    peers, plane, line = group_peers(plan), plane_peers(plan), line_peers(plan)
    xhalo = Halo(plan, xedge, beyond, xhalo_sems)
    halo = Halo(plan, edge, land, halo_sems)
    gather = Gather(plan, part, full, gather_sems)
    w_copy = pltpu.make_async_copy(w_hbm, w_ref, w_sem)
    plane_link, line_link, link = links[:3], links[3:6], links[6:]
    s, z, i, h = plan.place()
    L, Lp, C, nw, nz, wb = plan.L, plan.Lp, plan.C, plan.nw, plan.nz, plan.wb
    share = plan.NW // nz
    c = t - nm
    everyone = peers.others + gather.others()

    @pl.when(first_step())
    def _():
        w_copy.start()
        greet(everyone)
        part[...] = jnp.where(gather.tap == 3, pw[...], taps[0])
        macc[...] = jnp.zeros_like(macc)
        acc[...] = jnp.zeros_like(acc)
        state[...] = jnp.zeros_like(state)
        state[GAIN1 : GAIN1 + 1] = flat(gain)
        state[SHIFT1 : SHIFT1 + 1] = flat(shift)
        n16 = nw * 16
        for side, (xe, ce, places) in enumerate(
            ((xtop, ctop, (0, 1, 0)), (xend, cend, (14, 15, 15)))
        ):
            for k, at in enumerate(places):
                rows, lanes = rows_of((nw, n16)), lanes_of((nw, n16))
                one = jnp.where(lanes == 16 * rows + at, 1.0, 0.0).astype(BF16)
                block = (xe if k < 2 else ce)[...].reshape(n16, C)
                xedge[side, k] = mm(one, block)
        shape = (Lp, L)
        for k in range(plan.T1):
            at = lanes_of(shape) - (2 * rows_of(shape) + (k - 2))
            sel[k * Lp : (k + 1) * Lp] = jnp.where((at == 0) | (at == 1), 1.0, 0.0).astype(BF16)

    @pl.when(c < 0)
    def _():
        rows = rows_of((L, C))
        for w in range(min(share, wb)):
            at = lax.rem(z * share, wb) + w
            valid = 2 * lens[z * share + t * wb + w] - s * L
            v = jnp.where(rows < valid, x[at].astype(F32), 0.0)
            macc[0] += fold(v)
            macc[1] += fold(v * v)

    @pl.when(c == -1)
    def _():
        packet, more = plane_link[0], line_link[0]
        packet[0:1] = unfold(macc[0])
        packet[1:2] = unfold(macc[1])
        meet(everyone)
        plane.start(plane_link)
        xhalo.start(0, 3)
        at = 0
        spans = []
        more[2:3] = jnp.zeros((1, C), F32)
        for ref in (g2, s2, pb, g3, s3):
            n = ref.shape[1]
            more[2:3, at : at + n] = ref[...]
            spans.append((at, n))
            at += n
        more[0:2] = plane.finish(plane_link)
        line.start(line_link)
        gather.line_start()
        state[ST1 : ST1 + 2] = line.finish(line_link)[0:2]
        for k in range(nz):
            row = line_link[1][k]
            for r, (at, n) in zip((GAIN2, SHIFT2, BIAS, GAIN3, SHIFT3), spans):
                state[r : r + 1, k * n : (k + 1) * n] = row[2:3, at : at + n]
        xhalo.finish()
        beyond_out[...] = beyond[...]
        w_copy.wait()

    @pl.when(c >= 0)
    def _():
        mean, rho = norm_of(state[ST1 : ST1 + 2], 2.0 * total_of(lens))
        scale = state[GAIN1 : GAIN1 + 1] * rho
        offset = state[SHIFT1 : SHIFT1 + 1] - mean * scale
        rows = rows_of((L, C))
        row1 = rows_of((1, C))
        row16 = rows_of((16, C))
        def activate(w):
            at = c * wb + w
            valid = 2 * lens[i * nw + at] - s * L
            a = gelu(x[w].astype(F32) * scale + offset)
            a = jnp.where(rows < valid, a, 0.0).astype(BF16)
            picked = mm(sel[...], a)
            for k in range(5):
                X5[k, w * Lp : (w + 1) * Lp] = picked[k * Lp : (k + 1) * Lp].astype(BF16)

            def beside(side, k, bin_at):
                a = gelu(beyond[side, k, pl.ds(at, 1), :] * scale + offset)
                here = (row1 + bin_at < valid) & (row1 + (s * L + bin_at) >= 0)
                return jnp.where(here, a, 0.0).astype(BF16).astype(F32)

            l0, l1 = beside(0, 0, -2), beside(0, 1, -1)
            r0, r1 = beside(1, 0, L), beside(1, 1, L + 1)
            top, end = w * Lp, (w + 1) * Lp
            for k, add in ((0, l0 + l1), (1, l1)):
                X5[k, top : top + 16] = (
                    picked[k * Lp : k * Lp + 16] + jnp.where(row16 == 0, add, 0.0)
                ).astype(BF16)
            for k, add in ((3, r0), (4, r0 + r1)):
                X5[k, end - 16 : end] = (
                    picked[(k + 1) * Lp - 16 : (k + 1) * Lp] + jnp.where(row16 == 15, add, 0.0)
                ).astype(BF16)

        nc = 256
        rowp = rows_of((Lp, nc))

        def convolve(first, count):
            span = slice(first * Lp, (first + count) * Lp)
            for n in range(C // nc):
                cols = slice(n * nc, (n + 1) * nc)
                taps = [X5[k, span] for k in range(plan.T1)]
                y = 0.5 * mm(jnp.concatenate(taps, axis=1), w_ref[:, cols])
                s0 = jnp.zeros((8, nc), F32)
                s1 = jnp.zeros((8, nc), F32)
                for w in range(first, first + count):
                    at = c * wb + w
                    valid = lens[i * nw + at] - s * Lp
                    v = y[(w - first) * Lp : (w - first + 1) * Lp]
                    x2[w, :, cols] = v
                    edge[0, at, :, cols] = v[:EDGE].astype(BF16)
                    edge[1, at, :, cols] = v[Lp - EDGE :].astype(BF16)
                    v = jnp.where(rowp < valid, v, 0.0)
                    s0 = s0 + fold(v)
                    s1 = s1 + fold(v * v)
                acc[0:1, cols] += unfold(s0)
                acc[1:2, cols] += unfold(s1)

        count = max(1, wb // 2)
        for first in range(0, wb, count):
            for w in range(first, first + count):
                activate(w)
            convolve(first, count)
        halo.start(c * wb, wb)

    @pl.when(c == 0)
    def _():
        gather.line_finish()
        gather.chips_start()

    @pl.when(last_step())
    def _():
        link[0][...] = acc[...]
        peers.start(link)
        gather.pair_start()
        state[ST2 : ST2 + 2] = peers.finish(link)
        halo.finish()
        gather.pair_finish()


def block_kernel(plan, lens, x2, x2half, x2land, cot, w_ref, pw_ref, old, half_state,
                 dz2, grads, pgrad, res, land, state, res_got,
                 ext, wf, wt, pw, Y3, c2, dz3, das, a3s, a3T, dos, Z3, dcT,
                 cedge, cland, cacc, dedge, dland, dacc, bedge, bacc, halo_sems, bulk_sems,
                 *links):
    t = pl.program_id(0)
    peers = group_peers(plan)
    s, z, i, h = plan.place()
    Lp, C, H, wb, nw, cs, g = plan.Lp, plan.C, plan.H, plan.wb, plan.nw, plan.cs, plan.g
    M = wb * Lp
    steps = plan.steps
    p0, r0, b0, g0 = block_phases(plan)[:4]
    c_link, d_link, b_link = links[:3], links[3:6], links[6:]
    c_halo = Halo(plan, cedge, cland, halo_sems.at[0])
    d_halo = Halo(plan, dedge, dland, halo_sems.at[1])
    b_halo = Halo(plan, bedge, land, halo_sems.at[2])

    def bulk(off, rows):
        to = wrap(i + off, g)
        return remote(
            res.at[to, rows],
            res_got.at[off, rows],
            bulk_sems.at[0, off],
            bulk_sems.at[1, off],
            (s, h * g + to),
        )

    def result_of(block):
        y = mm(a3s[pl.ds(pl.multiple_of(block * M, 128), M)], pw_ref[h, 0])
        rowr = rows_of((Lp, y.shape[1]))
        for w in range(wb):
            at = block * wb + w
            valid = lens[i * plan.nw + at] - s * Lp
            r = x2half[w] + y[w * Lp : (w + 1) * Lp] + half_state[BIAS : BIAS + 1]
            r = jnp.where(rowr < valid, r, 0.0).astype(BF16).T
            for k in range(g):
                res[k, at] = r[k * cs : (k + 1) * cs]

    def send_result(block):
        result_of(block)
        for off in range(1, g):
            bulk(off, pl.ds(block * wb, wb)).start()

    @pl.when(first_step())
    def _():
        greet(peers.others)
        state[...] = old[...]
        cacc[...] = jnp.zeros_like(cacc)
        dacc[...] = jnp.zeros_like(dacc)
        bacc[...] = jnp.zeros_like(bacc)
        for c in range(2):
            cols = slice(c * (C // 2), (c + 1) * (C // 2))
            pw[:, cols] = pw_ref[c, 0]
            for k in range(plan.T2):
                at = k * C + c * (C // 2)
                wf[:, at : at + C // 2] = w_ref[c, k]
                wt[k * H : (k + 1) * H, cols] = w_ref[c, k]

    @pl.when(t < p0)
    def _():
        base = pl.multiple_of(t * M, 128)
        mean, rho = norm_of(state[ST2 : ST2 + 2], total_of(lens))
        scale = state[GAIN2 : GAIN2 + 1] * rho
        offset = state[SHIFT2 : SHIFT2 + 1] - mean * scale
        rows = rows_of((Lp, C))
        rowe = rows_of((EDGE, C))

        rowh = rows_of((Lp, H))
        sums0, sums1 = jnp.zeros((8, H), F32), jnp.zeros((8, H), F32)
        nh = min(2, wb)
        for first in range(0, wb, wb // nh):
            span = range(first, first + wb // nh)
            for w in span:
                valid = lens[i * plan.nw + t * wb + w] - s * Lp
                a = jnp.where(rows < valid, gelu(x2[w] * scale + offset), 0.0)
                al = gelu(x2land[0, w].astype(F32) * scale + offset)
                al = jnp.where((rowe - EDGE < valid) & (s > 0), al, 0.0)
                ah = gelu(x2land[1, w].astype(F32) * scale + offset)
                ah = jnp.where(rowe + Lp < valid, ah, 0.0)
                ext[w, 0:EDGE] = al
                ext[w, EDGE : EDGE + Lp] = a
                ext[w, EDGE + Lp :] = ah
                top, end = w * Lp, (w + 1) * Lp
                Y3[pl.ds(base + top, Lp), 0:C] = ext[w, EDGE - DIL : EDGE - DIL + Lp].astype(BF16)
                Y3[pl.ds(base + top, Lp), C : 2 * C] = a.astype(BF16)
                Y3[pl.ds(base + top, Lp), 2 * C : 3 * C] = ext[w, EDGE + DIL : EDGE + DIL + Lp].astype(BF16)
            y = mm_nt(Y3[pl.ds(base + first * Lp, wb // nh * Lp)], wf[...])
            for w in span:
                at = t * wb + w
                valid = lens[i * plan.nw + at] - s * Lp
                v = y[(w - first) * Lp : (w - first + 1) * Lp]
                c2[at] = v
                cedge[0, at] = v[:EDGE].astype(BF16)
                cedge[1, at] = v[Lp - EDGE :].astype(BF16)
                v = jnp.where(rowh < valid, v, 0.0)
                sums0 = sums0 + fold(v)
                sums1 = sums1 + fold(v * v)
        cacc[0:1, 0:H] += unfold(sums0)
        cacc[0:1, H:] += unfold(sums1)

    @pl.when(first_step())
    def _():
        meet(peers.others)

    @pl.when(t < p0)
    def _():
        c_halo.start(t * wb, wb)

    @pl.when(t == p0 - 1)
    def _():
        c_link[0][...] = cacc[...]
        peers.start(c_link)

    here_p = (t >= p0) & (t < p0 + steps)

    @pl.when(here_p)
    def _():
        u = t - p0
        rowc = rows_of((Lp, C))
        block = pl.ds(pl.multiple_of(u * M, 128), M)
        bias = jnp.zeros((8, C), F32)
        parts = []
        for w in range(wb):
            valid = lens[i * plan.nw + u * wb + w] - s * Lp
            d = jnp.where(rowc < valid, cot[w].astype(F32), 0.0)
            bias = bias + fold(d)
            parts.append(d.astype(BF16))
        d = jnp.concatenate(parts, axis=0)
        dos[block] = d
        das[...] = mm_nt(d, pw[...])
        dacc[1:2] += unfold(bias)

    @pl.when(t == p0)
    def _():
        got = peers.finish(c_link)
        state[ST3 : ST3 + 1, 0:H] = got[:, 0:H]
        state[ST3 + 1 : ST3 + 2, 0:H] = got[:, H:]

    @pl.when(here_p)
    def _():
        u = t - p0
        block = pl.ds(pl.multiple_of(u * M, 128), M)
        rowh = rows_of((Lp, H))
        mean, rho = norm_of(state[ST3 : ST3 + 2, 0:H], total_of(lens))
        scale = state[GAIN3 : GAIN3 + 1, 0:H] * rho
        offset = state[SHIFT3 : SHIFT3 + 1, 0:H] - mean * scale
        s0, s1 = jnp.zeros((8, H), F32), jnp.zeros((8, H), F32)
        parts = []
        for w in range(wb):
            at = u * wb + w
            valid = lens[i * plan.nw + at] - s * Lp
            top, end = w * Lp, (w + 1) * Lp
            v = c2[at]
            zv = v * scale + offset
            act, slope = gelu_both(zv)
            parts.append(jnp.where(rowh < valid, act, 0.0).astype(BF16))
            dzw = das[top:end] * slope
            dz3[at] = dzw
            dedge[0, at] = dzw[:EDGE].astype(BF16)
            dedge[1, at] = dzw[Lp - EDGE :].astype(BF16)
            s0 = s0 + fold(dzw)
            s1 = s1 + fold(dzw * zv)
        a3 = jnp.concatenate(parts, axis=0)
        a3s[block] = a3
        a3T[:, block] = a3.T
        dacc[0:1, 0:H] += unfold(s0)
        dacc[0:1, H : 2 * H] += unfold(s1)
        d_halo.start(u * wb, wb)

    @pl.when(t == p0)
    def _():
        send_result(0)

    @pl.when(t == p0 + steps - 1)
    def _():
        d_link[0][...] = dacc[...]
        peers.start(d_link)

    @pl.when((t >= r0) & (t < b0))
    def _():
        send_result(t - r0 + 1)

    @pl.when(t == b0 - 1)
    def _():
        rows = pl.ds(pl.multiple_of(h * plan.Hh, 16), plan.Hh)
        pgrad[...] = mm(a3T[rows], dos[...]).astype(BF16)

    @pl.when(t == b0)
    def _():
        got = peers.finish(d_link)
        shift = state[SHIFT3 : SHIFT3 + 1, 0:H]
        gain = state[GAIN3 : GAIN3 + 1, 0:H]
        state[SU3 : SU3 + 1, 0:H] = got[0:1, 0:H]
        state[SU3 + 1 : SU3 + 2, 0:H] = (got[0:1, H : 2 * H] - shift * got[0:1, 0:H]) / gain
        state[BSUM : BSUM + 1] = got[1:2]
        c_halo.finish()
        d_halo.finish()

    @pl.when((t >= b0) & (t < g0))
    def _():
        u = t - b0
        total = total_of(lens)
        mean3, rho3 = norm_of(state[ST3 : ST3 + 2, 0:H], total)
        gr3 = state[GAIN3 : GAIN3 + 1, 0:H] * rho3
        sg3 = state[SU3 : SU3 + 1, 0:H] / total
        gg3 = state[SU3 + 1 : SU3 + 2, 0:H] / total
        mean2, rho2 = norm_of(state[ST2 : ST2 + 2], total)
        scale2 = state[GAIN2 : GAIN2 + 1] * rho2
        offset2 = state[SHIFT2 : SHIFT2 + 1] - mean2 * scale2
        rowh = rows_of((Lp, H))
        rowe = rows_of((EDGE, H))
        rowc = rows_of((Lp, C))

        by_v = -gr3 * rho3 * gg3
        by_1 = gr3 * (mean3 * rho3 * gg3 - sg3)

        def back(dz, v):
            return gr3 * dz + by_v * v + by_1

        for w in range(wb):
            valid = lens[i * nw + u * wb + w] - s * Lp
            d = jnp.where(rowh < valid, back(dz3[u * wb + w], c2[u * wb + w]), 0.0)
            dl = back(dland[0, u * wb + w].astype(F32), cland[0, u * wb + w].astype(F32))
            dl = jnp.where((rowe - EDGE < valid) & (s > 0), dl, 0.0)
            dh = back(dland[1, u * wb + w].astype(F32), cland[1, u * wb + w].astype(F32))
            dh = jnp.where(rowe + Lp < valid, dh, 0.0)
            ext[w, 0:EDGE, 0:H] = dl
            ext[w, EDGE : EDGE + Lp, 0:H] = d
            ext[w, EDGE + Lp :, 0:H] = dh
            top, end = w * Lp, (w + 1) * Lp
            Z3[top:end, 0:H] = ext[w, EDGE + DIL : EDGE + DIL + Lp, 0:H].astype(BF16)
            Z3[top:end, H : 2 * H] = d.astype(BF16)
            Z3[top:end, 2 * H : 3 * H] = ext[w, EDGE - DIL : EDGE - DIL + Lp, 0:H].astype(BF16)

        y = mm(Z3[...], wt[...])

        M = wb * Lp
        dcT[:, pl.ds(pl.multiple_of(u * M, 128), M)] = Z3[:, H : 2 * H].T
        s0, s1 = jnp.zeros((8, C), F32), jnp.zeros((8, C), F32)
        for w in range(wb):
            at = u * wb + w
            valid = lens[i * nw + at] - s * Lp
            v = x2[w]
            zv = v * scale2 + offset2
            dzw = y[w * Lp : (w + 1) * Lp] * gelu_slope(zv)
            dzw = jnp.where(rowc < valid, dzw, 0.0)
            dz2[w] = dzw
            bedge[0, pl.ds(at, 1)] = dzw[0:1]
            bedge[1, pl.ds(at, 1)] = dzw[Lp - 1 : Lp]
            s0 = s0 + fold(dzw)
            s1 = s1 + fold(dzw * zv)
        bacc[0:1] += unfold(s0)
        bacc[1:2] += unfold(s1)

    @pl.when(t == g0 - 1)
    def _():
        b_link[0][...] = bacc[...]
        peers.start(b_link)
        b_halo.start(0, nw)

    @pl.when(t >= g0)
    def _():
        rows = pl.ds(pl.multiple_of(h * plan.Hh, 16), plan.Hh)
        cols = pl.ds(pl.multiple_of((t - g0) * C, 128), C)
        grads[...] = mm(dcT[rows], Y3[:, cols]).astype(BF16)

    @pl.when(last_step())
    def _():
        got = peers.finish(b_link)
        shift, gain = state[SHIFT2 : SHIFT2 + 1], state[GAIN2 : GAIN2 + 1]
        state[SU2 : SU2 + 1] = got[0:1]
        state[SU2 + 1 : SU2 + 2] = (got[1:2] - shift * got[0:1]) / gain
        b_halo.finish()
        for off in range(1, g):
            bulk(off, pl.ds(0, nw)).wait()


def block_phases(plan):
    n = plan.steps
    return n, 2 * n, 3 * n - 1, 4 * n - 1, 4 * n - 1 + plan.T2


class Reduction:
    def __init__(self, plan, batches, out, give, mine, got, spread, half, mate, sems):
        self.plan, self.batches, self.out = plan, batches, out
        self.give, self.mine, self.got, self.spread = give, mine, got, spread
        self.half, self.mate = half, mate
        self.sems = sems
        self.s, self.z, self.i, self.h = plan.place()
        self.c = lax.rem(self.s, 2)
        self.m = lax.div(self.s, 2)
        self.chips = plan.chips

    @staticmethod
    def scratch(plan, batches):
        taps, wide = plan.T1 + 2, plan.C // 2
        full = (taps, plan.chips, plan.g, plan.rb, wide)
        part = (taps, plan.g, plan.rb, wide)
        return [
            pltpu.VMEM((taps, 2, plan.chips, plan.rb, wide), BF16),
            *[pltpu.VMEM(full, BF16)] * 4,
            *[pltpu.VMEM(part, BF16)] * 2,
            pltpu.SemaphoreType.DMA((2, len(batches), 5)),
        ]

    def copy(self, b, phase, src, dst, device):
        return remote(src, dst, self.sems.at[0, b, phase], self.sems.at[1, b, phase], device)

    def finish(self, b, phase, ref, device):
        done = self.copy(b, phase, ref, ref, device)
        done.wait_recv()
        done.wait_send()

    def taps(self, b):
        return pl.ds(*self.batches[b])

    def pair(self):
        return (2 * self.m + (1 - self.c), self.z)

    def far(self, off):
        return (2 * wrap(self.m + off, self.chips) + self.c, self.z)

    def member(self, off):
        return (self.s, self.h * self.plan.g + wrap(self.i + off, self.plan.g))

    def put(self, k, rows):
        wide = self.plan.C // 2
        for j in range(self.plan.g):
            for m in range(self.chips):
                v = rows(j, m)
                left, right = v[:, :wide], v[:, wide:]
                self.mine[k, m, j] = jnp.where(self.c == 0, left, right).astype(BF16)
                self.give[k, m, j] = jnp.where(self.c == 0, right, left).astype(BF16)

    def step0(self, b):
        taps = self.taps(b)
        self.copy(b, 0, self.give.at[taps], self.got.at[taps], self.pair()).start()

    def step1(self, b):
        taps = self.taps(b)
        self.finish(b, 0, self.got.at[taps], self.pair())
        first, count = self.batches[b]
        for k in range(first, first + count):
            v = self.mine[k].astype(F32) + self.got[k].astype(F32)
            self.mine[k] = v.astype(BF16)
        for off in range(1, self.chips):
            src = self.mine.at[taps, wrap(self.m + off, self.chips)]
            self.copy(b, 1, src, self.spread.at[taps, self.m], self.far(off)).start()

    def step2(self, b):
        taps = self.taps(b)
        self.finish(b, 1, self.spread.at[taps, pl.ds(0, self.chips - 1)], self.far(1))
        first, count = self.batches[b]
        for k in range(first, first + count):
            self.spread[k, self.m] = self.mine[k, self.m]
            v = self.spread[k, 0].astype(F32)
            for n in range(1, self.chips):
                v = v + self.spread[k, n].astype(F32)
            self.half[k] = v.astype(BF16)
        for off in range(1, self.plan.g):
            src = self.half.at[taps, wrap(self.i + off, self.plan.g)]
            self.copy(b, 2, src, self.mate.at[taps, off], self.member(off)).start()

    def step3(self, b):
        taps = self.taps(b)
        self.finish(b, 2, self.mate.at[taps, pl.ds(1, self.plan.g - 1)], self.member(1))
        first, count = self.batches[b]
        for k in range(first, first + count):
            v = self.half[k, self.i].astype(F32)
            for off in range(1, self.plan.g):
                v = v + self.mate[k, off].astype(F32)
            self.out[k, self.c, self.m] = v.astype(BF16)
        mine = self.out.at[taps, self.c, self.m]
        for off in range(1, self.chips):
            self.copy(b, 3, mine, mine, self.far(off)).start()

    def step4(self, b):
        taps = self.taps(b)
        self.finish(b, 3, self.out.at[taps, self.c, pl.ds(0, self.chips - 1)], self.far(1))
        mine = self.out.at[taps, self.c]
        self.copy(b, 4, mine, mine, self.pair()).start()

    def step5(self, b):
        self.finish(b, 4, self.out.at[self.taps(b), self.c], self.pair())


def tail_turns(plan):
    nD = plan.steps
    first = max(nD - 1, 1)
    turns = [("x", n) for n in range(first)] + [("d", n) for n in range(first, nD)]
    turns += [("w", n) for n in range(plan.T1)]
    return turns + [("x", n) for n in range(first, nD)]


def tail_batches(plan):
    return [(plan.T1, 2), (0, 2), (2, 2), (4, plan.T1 - 4)]


def tail_kernel(plan, lens, dz2, dzland, x2, x2land, cot, beyond, x, X5_hbm, taps, grads, pgrad,
                old, half_state,
                gz, gz_got, sums, summed,
                ext, D3, D0T, wcat, pick, eye, cols, y, part, split, acc, X5, X5_sems,
                bulk_sems, *rest):
    t = pl.program_id(0)
    s, z, i, h = plan.place()
    L, Lp, C, wb, g, nw = plan.L, plan.Lp, plan.C, plan.wb, plan.g, plan.nw
    Ch, cs, T1 = plan.Ch, plan.cs, plan.T1
    M = wb * Lp
    nD = plan.steps
    turns = tail_turns(plan)
    last = len(turns) - 1
    peers = group_peers(plan)
    red = Reduction(plan, tail_batches(plan), *rest[:8])
    link = rest[8:]

    def member(off):
        return (s, h * g + wrap(i + off, g))

    def send(first, count):
        rows = pl.ds(first, count)
        for off in range(1, g):
            remote(
                part.at[off - 1, rows],
                gz_got.at[off, rows],
                bulk_sems.at[0, off],
                bulk_sems.at[1, off],
                member(off),
            ).start()

    def X5_copy(k):
        return pltpu.make_async_copy(X5_hbm.at[k], X5.at[k % 2], X5_sems.at[k % 2])

    def when(at):
        return pl.when(t == min(at, last))

    def turn(kind, k):
        return turns.index((kind, k)) if (kind, k) in turns else last

    def turn_of(kind):
        index = jnp.int32(0)
        here = False
        for n, (what, k) in enumerate(turns):
            if what == kind:
                index = jnp.where(t == n, k, index)
                here = (t == n) | here
        return here, index

    @when(0)
    def _():
        greet(peers.others)
        acc[...] = jnp.zeros_like(acc)
        pick[...] = pick_matrix(L)
        eye[...] = eye_matrix(Ch, Ch, 0)
        mean, rho = norm_of(half_state[ST1 : ST1 + 2], 2.0 * total_of(lens))
        scale = half_state[GAIN1 : GAIN1 + 1] * rho
        offset = half_state[SHIFT1 : SHIFT1 + 1] - mean * scale
        for k, row in enumerate((scale, offset)):
            cols[k] = column(row, L)
        for first in range(0, Ch, 64):
            rows = slice(first, min(first + 64, Ch))
            for r, parts in enumerate((((0,), (1, 2), (3, 4)), ((0, 1), (2, 3), (4,)))):
                for k, which in enumerate(parts):
                    v = taps[which[0], rows]
                    if len(which) > 1:
                        v = (v.astype(F32) + taps[which[1], rows].astype(F32)).astype(BF16)
                    at = r * Ch
                    wcat[at + rows.start : at + rows.stop, k * C : (k + 1) * C] = v
        meet(peers.others)

    @pl.when(t < nD)
    def _():
        total = total_of(lens)
        mean, rho = norm_of(old[ST2 : ST2 + 2], total)
        gr = old[GAIN2 : GAIN2 + 1] * rho
        sg = old[SU2 : SU2 + 1] / total
        gg = old[SU2 + 1 : SU2 + 2] / total
        rowc = rows_of((Lp, C))
        row1 = rows_of((1, C))

        by_dz = 0.5 * gr
        by_v = -0.5 * gr * rho * gg
        by_1 = 0.5 * gr * (mean * rho * gg - sg)

        def back(dout, dz, v):
            return 0.5 * dout + by_dz * dz + by_v * v + by_1

        def grad_of(w):
            at = t * wb + w
            valid = lens[i * nw + at] - s * Lp
            d = back(cot[w].astype(F32), dz2[w], x2[w])
            d = jnp.where(rowc < valid, d, 0.0)
            one = pl.ds(at, 1)
            dl = back(beyond[0, 2, one, :], dzland[0, one, :], x2land[0, w, EDGE - 1 : EDGE].astype(F32))
            dl = jnp.where((row1 - 1 < valid) & (s > 0), dl, 0.0)
            dh = back(beyond[1, 2, one, :], dzland[1, one, :], x2land[1, w, 0:1].astype(F32))
            dh = jnp.where(row1 + Lp < valid, dh, 0.0)
            ext[w, 7:8] = dl
            ext[w, 8 : 8 + Lp] = d
            ext[w, 8 + Lp : 9 + Lp] = dh
            top, end = w * Lp, (w + 1) * Lp
            D3[t, top:end, 0:C] = ext[w, 9 : 9 + Lp].astype(BF16)
            D3[t, top:end, C : 2 * C] = d.astype(BF16)
            D3[t, top:end, 2 * C : 3 * C] = ext[w, 7 : 7 + Lp].astype(BF16)

        for w in range(wb):
            grad_of(w)
        half = D3[t, :, pl.ds(pl.multiple_of(C + h * Ch, 128), Ch)]
        D0T[:, pl.ds(pl.multiple_of(t * M, 128), M)] = half.T

    here_x, bx = turn_of("x")

    @pl.when(here_x)
    def _():
        lanes = lanes_of((Ch, L))

        def through(w):
            valid = 2 * lens[i * nw + bx * wb + w] - s * L
            top, end = w * Lp, (w + 1) * Lp
            v = mm_nt(eye[...], x[w])
            da = jnp.concatenate([y[0:Ch, top:end], y[Ch:, top:end]], axis=1)
            da = mm(da.astype(BF16), pick[...])
            zv = v * cols[0] + cols[1]
            dzw = da * gelu_slope(zv)
            dzw = jnp.where(lanes < valid, dzw, 0.0)
            acc[0] += fold_lanes(dzw)
            acc[1] += fold_lanes(dzw * zv)
            split[w % 2] = dzw.astype(BF16)
            for off in range(g):
                rows = pl.ds(pl.multiple_of(lax.rem(i + off, g) * cs, 16), cs)
                if off == 0:
                    gz[w] = split[w % 2, rows]
                else:
                    part[off - 1, bx * wb + w] = split[w % 2, rows]

        nh = 2 if wb % 2 == 0 and wb * Lp // 2 % 128 == 0 else 1
        n = wb // nh
        for hf in range(nh):
            rows = slice(hf * n * Lp, (hf + 1) * n * Lp)
            y[:, rows] = mm_nt(wcat[...], D3[bx, rows])
            for w in range(hf * n, (hf + 1) * n):
                through(w)

    @when(0)
    def _():
        hs = plan.H // plan.nz
        rb = plan.rb
        for u in range(2):

            def rows(j, m, u=u):
                side, r = m * rb // hs, m * rb % hs
                n = 2 * side + u
                rows = slice(j * hs + r, j * hs + r + rb)
                v = grads[rows, n * C : (n + 1) * C] if n < plan.T2 else pgrad[rows]
                return v.astype(F32)

            red.put(T1 + u, rows)
        red.step0(0)

    @when(1)
    def _():
        X5_copy(0).start()
        X5_copy(1).start()

    here_w, k = turn_of("w")

    @pl.when(here_w)
    def _():
        X5_copy(k).wait()
        y[0:Ch, 0:C] = mm(D0T[...], X5[lax.rem(k, 2)])

        @pl.when(k < T1 - 2)
        def _():
            X5_copy(k + 2).start()

        rb = plan.rb
        red.put(k, lambda j, m: y[j * cs + m * rb : j * cs + (m + 1) * rb, 0:C])

    @pl.when(here_x & (bx < nD - 1))
    def _():
        send(bx * wb, wb)

    @when(turn("x", nD - 1))
    def _():
        send((nD - 1) * wb, wb // 2)

    @when(turn("x", nD - 1))
    def _():
        packet = link[0]
        packet[...] = jnp.zeros_like(packet)
        packet[0:1, 0:Ch] = jnp.sum(acc[0].T, axis=0, keepdims=True)
        packet[1:2, 0:Ch] = jnp.sum(acc[1].T, axis=0, keepdims=True)
        peers.start(link)

    for at, step, batch in (
        (1, red.step1, 0),
        (max(nD - 1, 2), red.step2, 0),
        (turn("w", 1), red.step0, 1),
        (turn("w", 2), red.step1, 1),
        (turn("w", 3), red.step0, 2),
        (turn("w", 4), red.step1, 2),
        (turn("w", 4), red.step0, 3),
        (turn("w", 4), red.step2, 1),
        (last, red.step1, 3),
        (last, red.step2, 2),
        (last, red.step3, 0),
        (last, red.step3, 1),
        (last, red.step2, 3),
    ):

        @when(at)
        def _():
            step(batch)

    @when(last)
    def _():
        send(nw - wb + wb // 2, wb - wb // 2)

    @when(last)
    def _():
        red.step3(2)
        red.step4(0)
        red.step4(1)
        red.step3(3)
        red.step4(2)
        got = peers.finish(link)[:, 0:Ch]
        shift, gain = half_state[SHIFT1 : SHIFT1 + 1], half_state[GAIN1 : GAIN1 + 1]
        sums[0:1] = got[0:1]
        sums[1:2] = (got[1:2] - shift * got[0:1]) / gain
        red.step4(3)
        for b in range(4):
            red.step5(b)
        own = pltpu.make_async_copy(red.out, summed, X5_sems.at[0])
        own.start()
        for off in range(1, g):
            done = remote(
                part.at[off - 1],
                gz_got.at[off],
                bulk_sems.at[0, off],
                bulk_sems.at[1, off],
                member(off),
            )
            done.wait_recv()
            done.wait_send()
        own.wait()


def input_grad_kernel(plan, wg, lens, x, gz, gz_got, sums, res, res_got, summed,
                      state, half_state,
                      out, out_result, conv_grad, dil_grad, point_grad,
                      g1, b1, g2, b2, g3, b3, pb, eye, cols, xt):
    t = pl.program_id(0)
    s, z, i, h = plan.place()
    L, Ch, cs = plan.L, plan.Ch, plan.cs
    turn = plan.nw // wg
    mine = pl.ds(pl.multiple_of(i * cs, 16), cs)

    @pl.when(first_step())
    def _():
        n = 2.0 * total_of(lens)
        mean, rho = norm_of(half_state[ST1 : ST1 + 2], n)
        gr = half_state[GAIN1 : GAIN1 + 1] * rho
        gg = sums[1:2] / n * rho
        for k, row in enumerate((gr, -gr * gg, gr * (mean * gg - sums[0:1] / n))):
            xt[...] = column(row, L)
            cols[k] = xt[mine]
        eye[...] = eye_matrix(cs, Ch, i * cs)

        def mine_of(src, at, which, count, *dsts):
            n = dsts[0].shape[1]
            for k in range(count):

                @pl.when(which == k)
                def _():
                    for dst, r in zip(dsts, at):
                        dst[...] = src[r : r + 1, k * n : (k + 1) * n]

        mine_of(sums, (1, 0), i, plan.g, g1, b1)
        mine_of(state, (SU2 + 1, SU2), z, plan.nz, g2, b2)
        mine_of(state, (SU3 + 1, SU3), z, plan.nz, g3, b3)
        mine_of(state, (BSUM,), z, plan.nz, pb)

    own = lax.div(t, turn) == i
    for w in range(wg):
        out_result[w] = jnp.where(own, res[0, w], res_got[0, w])

    C, T1, hs, rb, wide = plan.C, plan.T1, plan.H // plan.nz, plan.rb, plan.C // 2
    count = plan.NW // wg
    turns = min(count, plan.chips)
    per, every = plan.chips // turns, count // turns

    def spread(chunk):
        for n in range(per):
            m = chunk * per + n
            side, r = m * rb // hs, m * rb % hs
            for c in range(2):
                at = slice(c * wide, (c + 1) * wide)
                for k in range(T1):
                    conv_grad[k, n * rb : (n + 1) * rb, at] = summed[k, c, n].astype(F32)
                for u in range(2):
                    v = summed[T1 + u, c, n].astype(F32)
                    if 2 * side + u < plan.T2:
                        dil_grad[2 * side + u, r : r + rb, at] = v
                    else:
                        point_grad[r : r + rb, at] = v

    for chunk in range(turns):
        pl.when(t == chunk * every)(partial(spread, chunk))

    lanes = lanes_of((cs, L))
    for w in range(wg):
        valid = 2 * lens[t * wg + w] - s * L
        v = mm_nt(eye[...], x[w])
        dz = jnp.where(own, gz[w], gz_got[0, w]).astype(F32)
        r = cols[0] * dz + v * cols[1] + cols[2]
        out[w] = jnp.where(lanes < valid, r, 0.0).astype(BF16)


def call(kernel, plan, name, steps, ins, outs, scratch, flops, nbytes, cid=None):
    extra = {} if cid is None else dict(collective_id=cid, has_side_effects=True)
    return pl.pallas_call(
        partial(kernel, plan),
        grid=(steps,),
        in_specs=[SMEM] + [spec for spec, _ in ins],
        out_specs=[spec for spec, _, _ in outs],
        out_shape=[jax.ShapeDtypeStruct(shape, dtype) for _, shape, dtype in outs],
        scratch_shapes=scratch,
        compiler_params=pltpu.CompilerParams(vmem_limit_bytes=VMEM_LIMIT, **extra),
        cost_estimate=pl.CostEstimate(
            flops=int(flops), bytes_accessed=int(nbytes), transcendentals=0
        ),
        name=name,
    )


def per_device(
    inputs,
    lengths,
    input_gain,
    input_shift,
    conv_weight,
    branch_gain,
    branch_shift,
    dilated_tap_weight,
    mixer_gain,
    mixer_shift,
    point_weight,
    point_bias,
    cotangent,
):
    NW, L, C = inputs.shape
    Lp = L // 2
    nz = lax.axis_size("ch")
    R = 2
    plan = Plan(
        ns=lax.axis_size("seq"),
        nz=nz,
        R=R,
        NW=NW,
        L=L,
        C=C,
        H=mixer_gain.shape[0] * nz,
        T1=conv_weight.shape[0],
        T2=dilated_tap_weight.shape[0],
        wb=min(NW * R // nz, max(1, 512 // Lp)),
    )
    g, nw, cs, Ch, H, Hh, wb = plan.g, plan.nw, plan.cs, plan.Ch, plan.H, plan.Hh, plan.wb
    T1, T2, steps = plan.T1, plan.T2, plan.steps
    M = wb * Lp
    hs = H // nz
    lens = lengths.astype(jnp.int32)

    def row(a):
        return a.reshape(1, a.shape[0])

    def grp():
        return lax.rem(lax.axis_index("ch"), g)

    def half():
        return lax.div(lax.axis_index("ch"), g)

    def core():
        return lax.rem(lax.axis_index("seq"), 2)

    def chip4():
        return lax.div(lax.axis_index("seq"), plan.ns // 4)

    def whole(*shape):
        return pl.BlockSpec(shape, lambda t: (0,) * len(shape), pipeline_mode=pl.Buffered(1))

    def const(*shape):
        return pl.BlockSpec(shape, lambda t: (0,) * len(shape))

    def win(*shape):
        return pl.BlockSpec(shape, lambda t: (t,) + (0,) * (len(shape) - 1))

    def arg_win(n, width):
        return pl.BlockSpec((wb, n, width), lambda t: (grp() * steps + t, 0, 0))

    def ins(*pairs):
        return [p for p in pairs]

    share = NW // nz
    nm = max(1, share // wb)

    def edge_spec(n):
        return pl.BlockSpec(
            (nw, 16, C), lambda t: (grp(), n, 0), pipeline_mode=pl.Buffered(1)
        )

    def head_block(t):
        own = lax.div(lax.axis_index("ch") * share, wb) + t
        return jnp.where(t < nm, own, grp() * steps + t - nm), 0, 0

    def after(*shape):
        return pl.BlockSpec(
            shape, lambda t: (jnp.maximum(t - nm, 0),) + (0,) * (len(shape) - 1)
        )

    pairs = ins(
        (pl.BlockSpec((wb, L, C), head_block), inputs),
        (edge_spec(0), inputs),
        (edge_spec(L // 16 - 1), inputs),
        (edge_spec(0), cotangent),
        (edge_spec(Lp // 16 - 1), cotangent),
        (whole(1, cs), row(branch_gain)),
        (whole(1, cs), row(branch_shift)),
        (whole(1, cs), row(point_bias)),
        (whole(1, H // nz), row(mixer_gain)),
        (whole(1, H // nz), row(mixer_shift)),
        (ANY, conv_weight.reshape(T1 * C, C)),
        (whole(C), input_gain),
        (whole(C), input_shift),
        (
            pl.BlockSpec(
                (1, hs, C // 2),
                lambda t: (jnp.minimum(chip4(), T2 - 1), 0, core()),
                pipeline_mode=pl.Buffered(1),
            ),
            jnp.swapaxes(dilated_tap_weight, 1, 2),
        ),
        (
            pl.BlockSpec(
                (hs, C // 2), lambda t: (0, core()), pipeline_mode=pl.Buffered(1)
            ),
            point_weight,
        ),
    )
    plane, line, group = plane_peers(plan), line_peers(plan), group_peers(plan)
    state_shape = (STATE, C)
    edges2, edges3 = (2, nw, EDGE, C), (2, nw, EDGE, H)
    X5, x2, land2, state, beyond, full = call(
        lambda plan, *refs: head_kernel(plan, nm, *refs),
        plan,
        "head",
        nm + steps,
        pairs,
        [
            (
                pl.BlockSpec((T1, M, C), lambda t: (0, jnp.maximum(t - nm, 0), 0)),
                (T1, nw * Lp, C),
                BF16,
            ),
            (after(wb, Lp, C), (nw, Lp, C), F32),
            (ANY, edges2, BF16),
            (const(*state_shape), state_shape, F32),
            (const(2, 3, nw, C), (2, 3, nw, C), F32),
            (ANY, (2, T2 + 1, nz, hs, C // 2), BF16),
        ],
        [
            pltpu.VMEM((2, 8, C), F32),
            pltpu.VMEM((2, 3, nw, C), F32),
            pltpu.VMEM((2, 3, nw, C), F32),
            pltpu.VMEM((T1 * Lp, L), BF16),
            pltpu.VMEM(edges2, BF16),
            pltpu.VMEM((2, C), F32),
            pltpu.VMEM((T1 * C, C), BF16),
            pltpu.SemaphoreType.DMA,
            pltpu.VMEM((hs, C // 2), BF16),
            pltpu.SemaphoreType.DMA((2, 4)),
            HALO_SEMS,
            HALO_SEMS,
        ]
        + plane.scratch(2, C)
        + line.scratch(3, C)
        + group.scratch(2, C),
        2 * nw * Lp * T1 * C * C,
        nw * Lp * C * 20,
        cid=1,
    )(lens, *[a for _, a in pairs])

    full = full.reshape(2, T2 + 1, H, C // 2)
    taps_spec = whole(2, T2, H, C // 2)
    pw_spec = pl.BlockSpec(
        (2, 1, H, C // 2), lambda t: (0, T2, 0, 0), pipeline_mode=pl.Buffered(1)
    )

    def early(*shape):
        return pl.BlockSpec(
            shape, lambda t: (jnp.minimum(t, steps - 1),) + (0,) * (len(shape) - 1)
        )

    def early_land(width):
        return pl.BlockSpec(
            (2, wb, EDGE, width), lambda t: (0, jnp.minimum(t, steps - 1), 0, 0)
        )

    def half_of(n):
        return pl.BlockSpec((n, Ch), lambda t: (0, half()), pipeline_mode=pl.Buffered(1))

    cot_spec = pl.BlockSpec(
        (wb, Lp, C), lambda t: (grp() * steps + jnp.minimum(t, steps - 1), 0, 0)
    )

    p0, r0, b0, g0, block_steps = block_phases(plan)

    def at_phase(first):
        return lambda t: jnp.clip(t - first, 0, steps - 1)

    in_p, in_b = at_phase(p0), at_phase(b0)
    pairs = ins(
        (
            pl.BlockSpec(
                (wb, Lp, C),
                lambda t: (jnp.where(t < p0 + steps, jnp.minimum(t, steps - 1), in_b(t)), 0, 0),
            ),
            x2,
        ),
        (
            pl.BlockSpec(
                (wb, Lp, Ch),
                lambda t: (jnp.clip(t - r0 + 1, 0, steps - 1), 0, half()),
            ),
            x2,
        ),
        (early_land(C), land2),
        (pl.BlockSpec((wb, Lp, C), lambda t: (grp() * steps + in_p(t), 0, 0)), cotangent),
        (taps_spec, full),
        (pw_spec, full),
        (whole(*state_shape), state),
        (half_of(STATE), state),
    )
    dz2, grads, pgrad, res, dland2, state, res_got = call(
        block_kernel,
        plan,
        "block",
        block_steps,
        pairs,
        [
            (pl.BlockSpec((wb, Lp, C), lambda t: (in_b(t), 0, 0)), (nw, Lp, C), F32),
            (
                pl.BlockSpec((Hh, C), lambda t: (0, jnp.maximum(t - g0, 0))),
                (Hh, T2 * C),
                BF16,
            ),
            (const(Hh, C), (Hh, C), BF16),
            (const(g, nw, cs, Lp), (g, nw, cs, Lp), BF16),
            (ANY, (2, nw, C), F32),
            (const(*state_shape), state_shape, F32),
            (ANY, (g, nw, cs, Lp), BF16),
        ],
        [
            pltpu.VMEM((wb, Lp + 2 * EDGE, C), F32),
            pltpu.VMEM((H, T2 * C), BF16),
            pltpu.VMEM((T2 * H, C), BF16),
            pltpu.VMEM((H, C), BF16),
            pltpu.VMEM((nw * Lp, T2 * C), BF16),
            pltpu.VMEM((nw, Lp, H), F32),
            pltpu.VMEM((nw, Lp, H), F32),
            pltpu.VMEM((M, H), F32),
            pltpu.VMEM((nw * Lp, H), BF16),
            pltpu.VMEM((H, nw * Lp), BF16),
            pltpu.VMEM((nw * Lp, C), BF16),
            pltpu.VMEM((M, T2 * H), BF16),
            pltpu.VMEM((H, nw * Lp), BF16),
            pltpu.VMEM(edges3, BF16),
            pltpu.VMEM(edges3, BF16),
            pltpu.VMEM((1, 2 * H), F32),
            pltpu.VMEM(edges3, BF16),
            pltpu.VMEM(edges3, BF16),
            pltpu.VMEM((2, C), F32),
            pltpu.VMEM((2, nw, C), F32),
            pltpu.VMEM((2, C), F32),
            pltpu.SemaphoreType.DMA((3, 2, 2)),
            pltpu.SemaphoreType.DMA((2, g)),
        ]
        + group.scratch(1, 2 * H)
        + group.scratch(2, C)
        + group.scratch(2, C),
        nw * Lp * C * H * (6 * T2 + 6),
        nw * Lp * C * 30,
        cid=3,
    )(lens, *[a for _, a in pairs])

    chips, rb = plan.chips, plan.rb
    turns_t = tail_turns(plan)

    def x_block(t):
        block = jnp.int32(0)
        for n, (what, k) in enumerate(turns_t):
            if what == "x":
                block = jnp.where(t >= n, k, block)
        return block

    sshape = (T1 + 2, 2, chips, rb, C // 2)
    pairs = ins(
        (early(wb, Lp, C), dz2),
        (whole(2, nw, C), dland2),
        (early(wb, Lp, C), x2),
        (early_land(C), land2),
        (cot_spec, cotangent),
        (whole(2, 3, nw, C), beyond),
        (
            pl.BlockSpec(
                (wb, L, Ch), lambda t: (grp() * steps + x_block(t), 0, half())
            ),
            inputs,
        ),
        (ANY, X5),
        (
            pl.BlockSpec(
                (T1, Ch, C), lambda t: (0, half(), 0), pipeline_mode=pl.Buffered(1)
            ),
            conv_weight,
        ),
        (whole(Hh, T2 * C), grads),
        (whole(Hh, C), pgrad),
        (whole(*state_shape), state),
        (half_of(STATE), state),
    )
    gz, gz_got, sums1, summed = call(
        tail_kernel,
        plan,
        "tail",
        len(turns_t),
        pairs,
        [
            (pl.BlockSpec((wb, cs, L), lambda t: (x_block(t), 0, 0)), (nw, cs, L), BF16),
            (ANY, (g, nw, cs, L), BF16),
            (const(2, Ch), (2, Ch), F32),
            (ANY, sshape, BF16),
        ],
        [
            pltpu.VMEM((wb, Lp + 16, C), F32),
            pltpu.VMEM((steps, M, 3 * C), BF16),
            pltpu.VMEM((Ch, nw * Lp), BF16),
            pltpu.VMEM((2 * Ch, 3 * C), BF16),
            pltpu.VMEM((L, L), BF16),
            pltpu.VMEM((Ch, Ch), BF16),
            pltpu.VMEM((2, Ch, L), F32),
            pltpu.VMEM((2 * Ch, max(M, C)), F32),
            pltpu.VMEM((g - 1, nw, cs, L), BF16),
            pltpu.VMEM((2, Ch, L), BF16),
            pltpu.VMEM((2, Ch, min(L, 128)), F32),
            pltpu.VMEM((2, nw * Lp, C), BF16),
            pltpu.SemaphoreType.DMA((2,)),
            pltpu.SemaphoreType.DMA((2, g)),
        ]
        + Reduction.scratch(plan, tail_batches(plan))
        + group.scratch(2, C),
        2 * nw * Lp * (6 + T1) * C * Ch,
        nw * Lp * C * 40,
        cid=6,
    )(lens, *[a for _, a in pairs])

    wg = min(2 * wb, nw)
    count = NW // wg
    turn = nw // wg
    turns = min(count, chips)

    def own_block(t):
        return jnp.where(lax.div(t, turn) == grp(), lax.rem(t, turn), 0)

    def got_slot(t):
        off = lax.rem(grp() - lax.div(t, turn) + g, g)
        return jnp.maximum(off, 1), jnp.where(off > 0, lax.rem(t, turn), 0)

    pairs = ins(
        (pl.BlockSpec((wg, L, Ch), lambda t: (t, 0, half())), inputs),
        (pl.BlockSpec((wg, cs, L), lambda t: (own_block(t), 0, 0)), gz),
        (pl.BlockSpec((1, wg, cs, L), lambda t: got_slot(t) + (0, 0)), gz_got),
        (whole(2, Ch), sums1),
        (pl.BlockSpec((1, wg, cs, Lp), lambda t: (grp(), own_block(t), 0, 0)), res),
        (pl.BlockSpec((1, wg, cs, Lp), lambda t: got_slot(t) + (0, 0)), res_got),
        (
            pl.BlockSpec(
                (T1 + 2, 2, chips // turns, rb, C // 2),
                lambda t: (0, 0, t * turns // count, 0, 0),
            ),
            summed,
        ),
        (whole(*state_shape), state),
        (half_of(STATE), state),
    )
    outs = call(
        lambda plan, *refs: input_grad_kernel(plan, wg, *refs),
        plan,
        "input_grad",
        count,
        pairs,
        [
            (win(wg, cs, L), (NW, cs, L), BF16),
            (win(wg, cs, Lp), (NW, cs, Lp), BF16),
            (
                pl.BlockSpec((T1, cs // turns, C), lambda t: (0, t * turns // count, 0)),
                (T1, cs, C),
                F32,
            ),
            (const(T2, hs, C), (T2, hs, C), F32),
            (const(hs, C), (hs, C), F32),
        ]
        + [(const(1, n), (1, n), F32) for n in (cs, cs, cs, cs, hs, hs, cs)],
        [
            pltpu.VMEM((cs, Ch), BF16),
            pltpu.VMEM((3, cs, L), F32),
            pltpu.VMEM((Ch, L), F32),
        ],
        2 * NW * L * Ch * cs,
        NW * L * cs * 8,
    )(lens, *[a for _, a in pairs])
    grad, result, conv_grad, dil_grad, point_grad = outs[:5]
    g1, b1, g2, b2, g3, b3, pb = [a[0] for a in outs[5:]]
    return (
        jnp.swapaxes(result, 1, 2),
        jnp.swapaxes(grad, 1, 2),
        jnp.swapaxes(conv_grad, 1, 2),
        g1,
        b1,
        g2,
        b2,
        jnp.swapaxes(dil_grad, 1, 2),
        g3,
        b3,
        point_grad,
        pb,
    )


def solution(mesh):
    in_specs = (
        P(None, "seq", None),
        P(),
        P(),
        P(),
        P(),
        P("ch"),
        P("ch"),
        P(None, None, "ch"),
        P("ch"),
        P("ch"),
        P("ch", None),
        P("ch"),
        P(None, "seq", None),
    )
    out_specs = (
        P(None, "seq", "ch"),
        P(None, "seq", "ch"),
        P(None, None, "ch"),
        P("ch"),
        P("ch"),
        P("ch"),
        P("ch"),
        P(None, None, "ch"),
        P("ch"),
        P("ch"),
        P("ch", None),
        P("ch"),
    )
    return jax.shard_map(
        per_device, mesh=mesh, in_specs=in_specs, out_specs=out_specs, check_vma=False
    )
```

```python
from functools import partial
from typing import NamedTuple

import jax
import jax.numpy as jnp
from jax import lax
from jax.experimental import pallas as pl
from jax.experimental.pallas import tpu as pltpu
from jax.sharding import PartitionSpec as P

DIL = 14
EDGE = 16
EPS = 1e-05
GC0 = 0.7978845608028654
GC1 = 0.044715
F32 = jnp.float32
BF16 = jnp.bfloat16
MESH = pl.DeviceIdType.MESH
VMEM_LIMIT = 58 * 1024 * 1024
ANY = pl.BlockSpec(memory_space=pl.ANY)
SMEM = pl.BlockSpec(memory_space=pltpu.SMEM)


ST1, GAIN2, SHIFT2, BIAS, GAIN3, SHIFT3, GAIN1, SHIFT1, ST2, ST3, SU3, BSUM, SU2 = (
    0, 2, 3, 4, 5, 6, 7, 8, 9, 11, 13, 15, 16
)
STATE = 24


class Plan(NamedTuple):
    ns: int
    nz: int
    R: int
    NW: int
    L: int
    C: int
    H: int
    T1: int
    T2: int
    wb: int

    @property
    def g(self):
        return self.nz // self.R

    @property
    def nw(self):
        return self.NW // self.g

    @property
    def Lp(self):
        return self.L // 2

    @property
    def cs(self):
        return self.C // self.nz

    @property
    def Ch(self):
        return self.C // self.R

    @property
    def Hh(self):
        return self.H // self.R

    @property
    def steps(self):
        return self.nw // self.wb

    @property
    def chips(self):
        return self.ns // 2

    @property
    def rb(self):
        return self.cs // self.chips

    def place(self):
        s, z = lax.axis_index("seq"), lax.axis_index("ch")
        return s, z, lax.rem(z, self.g), lax.div(z, self.g)


def gelu(z):
    t = jnp.tanh(z * (GC0 + (GC0 * GC1) * (z * z)))
    return z * (0.5 + 0.5 * t)


def gelu_both(z):
    sq = z * z
    t = jnp.tanh(z * (GC0 + (GC0 * GC1) * sq))
    h = 0.5 + 0.5 * t
    v = z * h
    return v, h + v * (1.0 - t) * (GC0 + (3.0 * GC0 * GC1) * sq)


def gelu_slope(z):
    return gelu_both(z)[1]


def fold(v):
    return jnp.sum(v.reshape(v.shape[0] // 8, 8, v.shape[1]), axis=0)


def fold_lanes(v):
    out = v[:, 0:128]
    for k in range(128, v.shape[1], 128):
        out = out + v[:, k : k + 128]
    return out


def unfold(v):
    return jnp.sum(v, axis=0, keepdims=True)


def rows_of(shape):
    return lax.broadcasted_iota(jnp.int32, shape, 0)


def lanes_of(shape):
    return lax.broadcasted_iota(jnp.int32, shape, 1)


def total_of(lens):
    n = lens[0]
    for k in range(1, lens.shape[0]):
        n = n + lens[k]
    return n.astype(F32)


def norm_of(stats, total):
    mean = stats[0:1] / total
    square = stats[1:2] / total
    return mean, lax.rsqrt(square - mean * mean + EPS)


def flat(ref):
    return ref[...].reshape(1, ref.shape[0])


def column(row, n):
    return jnp.broadcast_to(row, (n, row.shape[1])).T


def mm(a, b):
    return jnp.dot(a, b, preferred_element_type=F32)


def mm_nt(a, b):
    return lax.dot_general(a, b, (((1,), (1,)), ((), ())), preferred_element_type=F32)


def mm_tn(a, b):
    return lax.dot_general(a, b, (((0,), (0,)), ((), ())), preferred_element_type=F32)


def mm_tt(a, b):
    return lax.dot_general(a, b, (((0,), (1,)), ((), ())), preferred_element_type=F32)


def eye_matrix(n, m, first):
    return jnp.where(lanes_of((n, m)) == rows_of((n, m)) + first, 1.0, 0.0).astype(BF16)


def pick_matrix(L):
    r, n = rows_of((L, L)), lanes_of((L, L))
    bin_of = 2 * r - jnp.where(r >= L // 2, L - 1, 0)
    return jnp.where(n == bin_of, 1.0, 0.0).astype(BF16)


def remote(src, dst, send, recv, device):
    return pltpu.make_async_remote_copy(
        src_ref=src,
        dst_ref=dst,
        send_sem=send,
        recv_sem=recv,
        device_id=device,
        device_id_type=MESH,
    )


def wrap(v, n):
    return jnp.where(v >= n, v - n, v)


def greet(devices):
    barrier = pltpu.get_barrier_semaphore()
    for device in devices:
        pl.semaphore_signal(barrier, inc=1, device_id=device, device_id_type=MESH)


def meet(devices):
    pl.semaphore_wait(pltpu.get_barrier_semaphore(), len(devices))


class Peers:
    def __init__(self, me, others):
        self.me, self.others = me, others
        self.count = len(others) + 1

    def start(self, link):
        packet, buf, sems = link
        for device in self.others:
            remote(packet, buf.at[self.me], sems.at[0], sems.at[1], device).start()

    def finish(self, link):
        packet, buf, sems = link
        buf[self.me] = packet[...]
        rest = buf.at[pl.ds(0, self.count - 1)]
        done = remote(rest, rest, sems.at[0], sems.at[1], self.others[0])
        done.wait_recv()
        acc = buf[0]
        for q in range(1, self.count):
            acc = acc + buf[q]
        done.wait_send()
        return acc

    def scratch(self, rows, width):
        return [
            pltpu.VMEM((rows, width), F32),
            pltpu.VMEM((self.count, rows, width), F32),
            pltpu.SemaphoreType.DMA((2,)),
        ]


def group_peers(plan):
    s, z, i, h = plan.place()
    g = plan.g
    others = [
        (wrap(s + a, plan.ns), h * g + wrap(i + b, g))
        for a in range(plan.ns)
        for b in range(g)
        if a or b
    ]
    return Peers(s * g + i, others)


def plane_peers(plan):
    s, z, i, h = plan.place()
    return Peers(s, [(wrap(s + a, plan.ns), z) for a in range(1, plan.ns)])


def line_peers(plan):
    s, z, i, h = plan.place()
    return Peers(z, [(s, wrap(z + a, plan.nz)) for a in range(1, plan.nz)])


class Halo:
    def __init__(self, plan, edge, land, sems):
        self.edge, self.land, self.sems = edge, land, sems
        s, z, _, _ = plan.place()
        self.to = ((wrap(s + plan.ns - 1, plan.ns), z), (wrap(s + 1, plan.ns), z))

    def copy(self, side, rows):
        return remote(
            self.edge.at[side, rows],
            self.land.at[1 - side, rows],
            self.sems.at[0, side],
            self.sems.at[1, side],
            self.to[side],
        )

    def start(self, first, count):
        for side in range(2):
            self.copy(side, pl.ds(first, count)).start()

    def finish(self):
        for side in range(2):
            done = self.copy(side, pl.ds(0, self.land.shape[1]))
            done.wait_recv()
            done.wait_send()


HALO_SEMS = pltpu.SemaphoreType.DMA((2, 2))


class Gather:
    def __init__(self, plan, part, full, sems):
        self.plan, self.part, self.full, self.sems = plan, part, full, sems
        self.s, self.z, self.i, self.h = plan.place()
        self.c, self.m = lax.rem(self.s, 2), lax.div(self.s, 2)
        self.chips = plan.chips
        self.every = self.chips // 4
        self.tap = lax.div(self.m, self.every)
        self.owner = lax.rem(self.m, self.every) == 0
        self.mine = full.at[self.c, self.tap]

    def others(self):
        g, nz = self.plan.g, self.plan.nz
        return [(self.s, wrap(self.h * g + g + r, nz)) for r in range(nz - g)]

    def far(self, off):
        return (2 * wrap(self.m + off, self.chips) + self.c, self.z)

    def own(self):
        return pltpu.make_async_copy(self.part, self.mine.at[self.z], self.sems.at[0, 0])

    def line(self, off):
        device = (self.s, wrap(self.z + off, self.plan.nz))
        return remote(
            self.part, self.mine.at[self.z], self.sems.at[0, 1], self.sems.at[1, 1], device
        )

    def chip(self, off):
        return remote(self.mine, self.mine, self.sems.at[0, 2], self.sems.at[1, 2], self.far(off))

    def pair(self):
        half = self.full.at[self.c]
        device = (2 * self.m + 1 - self.c, self.z)
        return remote(half, half, self.sems.at[0, 3], self.sems.at[1, 3], device)

    def line_start(self):
        @pl.when(self.owner)
        def _():
            self.own().start()
            for off in range(1, self.plan.nz):
                self.line(off).start()

    def line_finish(self):
        @pl.when(self.owner)
        def _():
            self.own().wait()
            rest = self.mine.at[pl.ds(0, self.plan.nz - 1)]
            device = (self.s, wrap(self.z + 1, self.plan.nz))
            done = remote(rest, rest, self.sems.at[0, 1], self.sems.at[1, 1], device)
            done.wait_recv()
            done.wait_send()

    def chips_start(self):
        @pl.when(self.owner)
        def _():
            for off in range(1, self.chips):
                self.chip(off).start()

    def pair_start(self):
        def taken(count):
            rest = self.full.at[self.c, pl.ds(0, count)]
            return remote(rest, rest, self.sems.at[0, 2], self.sems.at[1, 2], self.far(1))

        @pl.when(self.owner)
        def _():
            taken(3).wait_recv()
            for off in range(1, self.chips):
                self.chip(off).wait_send()

        if self.every > 1:

            @pl.when(jnp.logical_not(self.owner))
            def _():
                taken(4).wait_recv()

        self.pair().start()

    def pair_finish(self):
        done = self.pair()
        done.wait_recv()
        done.wait_send()


def first_step():
    return pl.program_id(0) == 0


def last_step():
    return pl.program_id(0) == pl.num_programs(0) - 1


def head_kernel(plan, nm, lens, x, xtop, xend, ctop, cend, g2, s2, pb, g3, s3,
                w_hbm, gain, shift, taps, pw,
                X5, x2, land, state, beyond_out, full,
                macc, beyond, xedge, sel, edge, acc, w_ref, w_sem, part,
                gather_sems, xhalo_sems, halo_sems, *links):
    t = pl.program_id(0)
    peers, plane, line = group_peers(plan), plane_peers(plan), line_peers(plan)
    xhalo = Halo(plan, xedge, beyond, xhalo_sems)
    halo = Halo(plan, edge, land, halo_sems)
    gather = Gather(plan, part, full, gather_sems)
    w_copy = pltpu.make_async_copy(w_hbm, w_ref, w_sem)
    plane_link, line_link, link = links[:3], links[3:6], links[6:]
    s, z, i, h = plan.place()
    L, Lp, C, nw, nz, wb = plan.L, plan.Lp, plan.C, plan.nw, plan.nz, plan.wb
    share = plan.NW // nz
    c = t - nm
    everyone = peers.others + gather.others()

    @pl.when(first_step())
    def _():
        w_copy.start()
        greet(everyone)
        part[...] = jnp.where(gather.tap == 3, pw[...], taps[0])
        macc[...] = jnp.zeros_like(macc)
        acc[...] = jnp.zeros_like(acc)
        state[...] = jnp.zeros_like(state)
        state[GAIN1 : GAIN1 + 1] = flat(gain)
        state[SHIFT1 : SHIFT1 + 1] = flat(shift)
        n16 = nw * 16
        for side, (xe, ce, places) in enumerate(
            ((xtop, ctop, (0, 1, 0)), (xend, cend, (14, 15, 15)))
        ):
            for k, at in enumerate(places):
                rows, lanes = rows_of((nw, n16)), lanes_of((nw, n16))
                one = jnp.where(lanes == 16 * rows + at, 1.0, 0.0).astype(BF16)
                block = (xe if k < 2 else ce)[...].reshape(n16, C)
                xedge[side, k] = mm(one, block)
        shape = (Lp, L)
        for k in range(plan.T1):
            at = lanes_of(shape) - (2 * rows_of(shape) + (k - 2))
            sel[k * Lp : (k + 1) * Lp] = jnp.where((at == 0) | (at == 1), 1.0, 0.0).astype(BF16)

    @pl.when(c < 0)
    def _():
        rows = rows_of((L, C))
        for w in range(min(share, wb)):
            at = lax.rem(z * share, wb) + w
            valid = 2 * lens[z * share + t * wb + w] - s * L
            v = jnp.where(rows < valid, x[at].astype(F32), 0.0)
            macc[0] += fold(v)
            macc[1] += fold(v * v)

    @pl.when(c == -1)
    def _():
        packet, more = plane_link[0], line_link[0]
        packet[0:1] = unfold(macc[0])
        packet[1:2] = unfold(macc[1])
        meet(everyone)
        plane.start(plane_link)
        xhalo.start(0, 3)
        at = 0
        spans = []
        more[2:3] = jnp.zeros((1, C), F32)
        for ref in (g2, s2, pb, g3, s3):
            n = ref.shape[1]
            more[2:3, at : at + n] = ref[...]
            spans.append((at, n))
            at += n
        more[0:2] = plane.finish(plane_link)
        line.start(line_link)
        gather.line_start()
        state[ST1 : ST1 + 2] = line.finish(line_link)[0:2]
        for k in range(nz):
            row = line_link[1][k]
            for r, (at, n) in zip((GAIN2, SHIFT2, BIAS, GAIN3, SHIFT3), spans):
                state[r : r + 1, k * n : (k + 1) * n] = row[2:3, at : at + n]
        xhalo.finish()
        beyond_out[...] = beyond[...]
        w_copy.wait()

    @pl.when(c >= 0)
    def _():
        mean, rho = norm_of(state[ST1 : ST1 + 2], 2.0 * total_of(lens))
        scale = state[GAIN1 : GAIN1 + 1] * rho
        offset = state[SHIFT1 : SHIFT1 + 1] - mean * scale
        rows = rows_of((L, C))
        row1 = rows_of((1, C))
        row16 = rows_of((16, C))
        def activate(w):
            at = c * wb + w
            valid = 2 * lens[i * nw + at] - s * L
            a = gelu(x[w].astype(F32) * scale + offset)
            a = jnp.where(rows < valid, a, 0.0).astype(BF16)
            picked = mm(sel[...], a)
            for k in range(5):
                X5[k, w * Lp : (w + 1) * Lp] = picked[k * Lp : (k + 1) * Lp].astype(BF16)

            def beside(side, k, bin_at):
                a = gelu(beyond[side, k, pl.ds(at, 1), :] * scale + offset)
                here = (row1 + bin_at < valid) & (row1 + (s * L + bin_at) >= 0)
                return jnp.where(here, a, 0.0).astype(BF16).astype(F32)

            l0, l1 = beside(0, 0, -2), beside(0, 1, -1)
            r0, r1 = beside(1, 0, L), beside(1, 1, L + 1)
            top, end = w * Lp, (w + 1) * Lp
            for k, add in ((0, l0 + l1), (1, l1)):
                X5[k, top : top + 16] = (
                    picked[k * Lp : k * Lp + 16] + jnp.where(row16 == 0, add, 0.0)
                ).astype(BF16)
            for k, add in ((3, r0), (4, r0 + r1)):
                X5[k, end - 16 : end] = (
                    picked[(k + 1) * Lp - 16 : (k + 1) * Lp] + jnp.where(row16 == 15, add, 0.0)
                ).astype(BF16)

        nc = 256
        rowp = rows_of((Lp, nc))

        def convolve(first, count):
            span = slice(first * Lp, (first + count) * Lp)
            for n in range(C // nc):
                cols = slice(n * nc, (n + 1) * nc)
                taps = [X5[k, span] for k in range(plan.T1)]
                y = 0.5 * mm(jnp.concatenate(taps, axis=1), w_ref[:, cols])
                s0 = jnp.zeros((8, nc), F32)
                s1 = jnp.zeros((8, nc), F32)
                for w in range(first, first + count):
                    at = c * wb + w
                    valid = lens[i * nw + at] - s * Lp
                    v = y[(w - first) * Lp : (w - first + 1) * Lp]
                    x2[w, :, cols] = v
                    edge[0, at, :, cols] = v[:EDGE].astype(BF16)
                    edge[1, at, :, cols] = v[Lp - EDGE :].astype(BF16)
                    v = jnp.where(rowp < valid, v, 0.0)
                    s0 = s0 + fold(v)
                    s1 = s1 + fold(v * v)
                acc[0:1, cols] += unfold(s0)
                acc[1:2, cols] += unfold(s1)

        count = max(1, wb // 2)
        for first in range(0, wb, count):
            for w in range(first, first + count):
                activate(w)
            convolve(first, count)
        halo.start(c * wb, wb)

    @pl.when(c == 0)
    def _():
        gather.line_finish()
        gather.chips_start()

    @pl.when(last_step())
    def _():
        link[0][...] = acc[...]
        peers.start(link)
        gather.pair_start()
        state[ST2 : ST2 + 2] = peers.finish(link)
        halo.finish()
        gather.pair_finish()


def block_kernel(plan, lens, x2, x2half, x2land, cot, w_ref, pw_ref, old, half_state,
                 dz2, grads, pgrad, res, land, state, res_got,
                 ext, wf, wt, pw, Y3, c2, dz3, das, a3s, a3T, dos, Z3, dcT,
                 cedge, cland, cacc, dedge, dland, dacc, bedge, bacc, halo_sems, bulk_sems,
                 *links):
    t = pl.program_id(0)
    peers = group_peers(plan)
    s, z, i, h = plan.place()
    Lp, C, H, wb, nw, cs, g = plan.Lp, plan.C, plan.H, plan.wb, plan.nw, plan.cs, plan.g
    M = wb * Lp
    steps = plan.steps
    p0, r0, b0, g0 = block_phases(plan)[:4]
    c_link, d_link, b_link = links[:3], links[3:6], links[6:]
    c_halo = Halo(plan, cedge, cland, halo_sems.at[0])
    d_halo = Halo(plan, dedge, dland, halo_sems.at[1])
    b_halo = Halo(plan, bedge, land, halo_sems.at[2])

    def bulk(off, rows):
        to = wrap(i + off, g)
        return remote(
            res.at[to, rows],
            res_got.at[off, rows],
            bulk_sems.at[0, off],
            bulk_sems.at[1, off],
            (s, h * g + to),
        )

    def result_of(block):
        y = mm(a3s[pl.ds(pl.multiple_of(block * M, 128), M)], pw_ref[h, 0])
        rowr = rows_of((Lp, y.shape[1]))
        for w in range(wb):
            at = block * wb + w
            valid = lens[i * plan.nw + at] - s * Lp
            r = x2half[w] + y[w * Lp : (w + 1) * Lp] + half_state[BIAS : BIAS + 1]
            r = jnp.where(rowr < valid, r, 0.0).astype(BF16).T
            for k in range(g):
                res[k, at] = r[k * cs : (k + 1) * cs]

    def send_result(block):
        result_of(block)
        for off in range(1, g):
            bulk(off, pl.ds(block * wb, wb)).start()

    @pl.when(first_step())
    def _():
        greet(peers.others)
        state[...] = old[...]
        cacc[...] = jnp.zeros_like(cacc)
        dacc[...] = jnp.zeros_like(dacc)
        bacc[...] = jnp.zeros_like(bacc)
        for c in range(2):
            cols = slice(c * (C // 2), (c + 1) * (C // 2))
            pw[:, cols] = pw_ref[c, 0]
            for k in range(plan.T2):
                at = k * C + c * (C // 2)
                wf[:, at : at + C // 2] = w_ref[c, k]
                wt[k * H : (k + 1) * H, cols] = w_ref[c, k]

    @pl.when(t < p0)
    def _():
        base = pl.multiple_of(t * M, 128)
        mean, rho = norm_of(state[ST2 : ST2 + 2], total_of(lens))
        scale = state[GAIN2 : GAIN2 + 1] * rho
        offset = state[SHIFT2 : SHIFT2 + 1] - mean * scale
        rows = rows_of((Lp, C))
        rowe = rows_of((EDGE, C))

        rowh = rows_of((Lp, H))
        sums0, sums1 = jnp.zeros((8, H), F32), jnp.zeros((8, H), F32)
        nh = min(2, wb)
        for first in range(0, wb, wb // nh):
            span = range(first, first + wb // nh)
            for w in span:
                valid = lens[i * plan.nw + t * wb + w] - s * Lp
                a = jnp.where(rows < valid, gelu(x2[w] * scale + offset), 0.0)
                al = gelu(x2land[0, w].astype(F32) * scale + offset)
                al = jnp.where((rowe - EDGE < valid) & (s > 0), al, 0.0)
                ah = gelu(x2land[1, w].astype(F32) * scale + offset)
                ah = jnp.where(rowe + Lp < valid, ah, 0.0)
                ext[w, 0:EDGE] = al
                ext[w, EDGE : EDGE + Lp] = a
                ext[w, EDGE + Lp :] = ah
                top, end = w * Lp, (w + 1) * Lp
                Y3[pl.ds(base + top, Lp), 0:C] = ext[w, EDGE - DIL : EDGE - DIL + Lp].astype(BF16)
                Y3[pl.ds(base + top, Lp), C : 2 * C] = a.astype(BF16)
                Y3[pl.ds(base + top, Lp), 2 * C : 3 * C] = ext[w, EDGE + DIL : EDGE + DIL + Lp].astype(BF16)
            y = mm_nt(Y3[pl.ds(base + first * Lp, wb // nh * Lp)], wf[...])
            for w in span:
                at = t * wb + w
                valid = lens[i * plan.nw + at] - s * Lp
                v = y[(w - first) * Lp : (w - first + 1) * Lp]
                c2[at] = v
                cedge[0, at] = v[:EDGE].astype(BF16)
                cedge[1, at] = v[Lp - EDGE :].astype(BF16)
                v = jnp.where(rowh < valid, v, 0.0)
                sums0 = sums0 + fold(v)
                sums1 = sums1 + fold(v * v)
        cacc[0:1, 0:H] += unfold(sums0)
        cacc[0:1, H:] += unfold(sums1)

    @pl.when(first_step())
    def _():
        meet(peers.others)

    @pl.when(t < p0)
    def _():
        c_halo.start(t * wb, wb)

    @pl.when(t == p0 - 1)
    def _():
        c_link[0][...] = cacc[...]
        peers.start(c_link)

    here_p = (t >= p0) & (t < p0 + steps)

    @pl.when(here_p)
    def _():
        u = t - p0
        rowc = rows_of((Lp, C))
        block = pl.ds(pl.multiple_of(u * M, 128), M)
        bias = jnp.zeros((8, C), F32)
        parts = []
        for w in range(wb):
            valid = lens[i * plan.nw + u * wb + w] - s * Lp
            d = jnp.where(rowc < valid, cot[w].astype(F32), 0.0)
            bias = bias + fold(d)
            parts.append(d.astype(BF16))
        d = jnp.concatenate(parts, axis=0)
        dos[block] = d
        das[...] = mm_nt(d, pw[...])
        dacc[1:2] += unfold(bias)

    @pl.when(t == p0)
    def _():
        got = peers.finish(c_link)
        state[ST3 : ST3 + 1, 0:H] = got[:, 0:H]
        state[ST3 + 1 : ST3 + 2, 0:H] = got[:, H:]

    @pl.when(here_p)
    def _():
        u = t - p0
        block = pl.ds(pl.multiple_of(u * M, 128), M)
        rowh = rows_of((Lp, H))
        mean, rho = norm_of(state[ST3 : ST3 + 2, 0:H], total_of(lens))
        scale = state[GAIN3 : GAIN3 + 1, 0:H] * rho
        offset = state[SHIFT3 : SHIFT3 + 1, 0:H] - mean * scale
        s0, s1 = jnp.zeros((8, H), F32), jnp.zeros((8, H), F32)
        parts = []
        for w in range(wb):
            at = u * wb + w
            valid = lens[i * plan.nw + at] - s * Lp
            top, end = w * Lp, (w + 1) * Lp
            v = c2[at]
            zv = v * scale + offset
            act, slope = gelu_both(zv)
            parts.append(jnp.where(rowh < valid, act, 0.0).astype(BF16))
            dzw = das[top:end] * slope
            dz3[at] = dzw
            dedge[0, at] = dzw[:EDGE].astype(BF16)
            dedge[1, at] = dzw[Lp - EDGE :].astype(BF16)
            s0 = s0 + fold(dzw)
            s1 = s1 + fold(dzw * zv)
        a3 = jnp.concatenate(parts, axis=0)
        a3s[block] = a3
        a3T[:, block] = a3.T
        dacc[0:1, 0:H] += unfold(s0)
        dacc[0:1, H : 2 * H] += unfold(s1)
        d_halo.start(u * wb, wb)

    @pl.when(t == p0)
    def _():
        send_result(0)

    @pl.when(t == p0 + steps - 1)
    def _():
        d_link[0][...] = dacc[...]
        peers.start(d_link)

    @pl.when((t >= r0) & (t < b0))
    def _():
        send_result(t - r0 + 1)

    @pl.when(t == b0 - 1)
    def _():
        rows = pl.ds(pl.multiple_of(h * plan.Hh, 16), plan.Hh)
        pgrad[...] = mm(a3T[rows], dos[...]).astype(BF16)

    @pl.when(t == b0)
    def _():
        got = peers.finish(d_link)
        shift = state[SHIFT3 : SHIFT3 + 1, 0:H]
        gain = state[GAIN3 : GAIN3 + 1, 0:H]
        state[SU3 : SU3 + 1, 0:H] = got[0:1, 0:H]
        state[SU3 + 1 : SU3 + 2, 0:H] = (got[0:1, H : 2 * H] - shift * got[0:1, 0:H]) / gain
        state[BSUM : BSUM + 1] = got[1:2]
        c_halo.finish()
        d_halo.finish()

    @pl.when((t >= b0) & (t < g0))
    def _():
        u = t - b0
        total = total_of(lens)
        mean3, rho3 = norm_of(state[ST3 : ST3 + 2, 0:H], total)
        gr3 = state[GAIN3 : GAIN3 + 1, 0:H] * rho3
        sg3 = state[SU3 : SU3 + 1, 0:H] / total
        gg3 = state[SU3 + 1 : SU3 + 2, 0:H] / total
        mean2, rho2 = norm_of(state[ST2 : ST2 + 2], total)
        scale2 = state[GAIN2 : GAIN2 + 1] * rho2
        offset2 = state[SHIFT2 : SHIFT2 + 1] - mean2 * scale2
        rowh = rows_of((Lp, H))
        rowe = rows_of((EDGE, H))
        rowc = rows_of((Lp, C))

        by_v = -gr3 * rho3 * gg3
        by_1 = gr3 * (mean3 * rho3 * gg3 - sg3)

        def back(dz, v):
            return gr3 * dz + by_v * v + by_1

        for w in range(wb):
            valid = lens[i * nw + u * wb + w] - s * Lp
            d = jnp.where(rowh < valid, back(dz3[u * wb + w], c2[u * wb + w]), 0.0)
            dl = back(dland[0, u * wb + w].astype(F32), cland[0, u * wb + w].astype(F32))
            dl = jnp.where((rowe - EDGE < valid) & (s > 0), dl, 0.0)
            dh = back(dland[1, u * wb + w].astype(F32), cland[1, u * wb + w].astype(F32))
            dh = jnp.where(rowe + Lp < valid, dh, 0.0)
            ext[w, 0:EDGE, 0:H] = dl
            ext[w, EDGE : EDGE + Lp, 0:H] = d
            ext[w, EDGE + Lp :, 0:H] = dh
            top, end = w * Lp, (w + 1) * Lp
            Z3[top:end, 0:H] = ext[w, EDGE + DIL : EDGE + DIL + Lp, 0:H].astype(BF16)
            Z3[top:end, H : 2 * H] = d.astype(BF16)
            Z3[top:end, 2 * H : 3 * H] = ext[w, EDGE - DIL : EDGE - DIL + Lp, 0:H].astype(BF16)

        y = mm(Z3[...], wt[...])

        M = wb * Lp
        dcT[:, pl.ds(pl.multiple_of(u * M, 128), M)] = Z3[:, H : 2 * H].T
        s0, s1 = jnp.zeros((8, C), F32), jnp.zeros((8, C), F32)
        for w in range(wb):
            at = u * wb + w
            valid = lens[i * nw + at] - s * Lp
            v = x2[w]
            zv = v * scale2 + offset2
            dzw = y[w * Lp : (w + 1) * Lp] * gelu_slope(zv)
            dzw = jnp.where(rowc < valid, dzw, 0.0)
            dz2[w] = dzw
            bedge[0, pl.ds(at, 1)] = dzw[0:1]
            bedge[1, pl.ds(at, 1)] = dzw[Lp - 1 : Lp]
            s0 = s0 + fold(dzw)
            s1 = s1 + fold(dzw * zv)
        bacc[0:1] += unfold(s0)
        bacc[1:2] += unfold(s1)

    @pl.when(t == g0 - 1)
    def _():
        b_link[0][...] = bacc[...]
        peers.start(b_link)
        b_halo.start(0, nw)

    @pl.when(t >= g0)
    def _():
        rows = pl.ds(pl.multiple_of(h * plan.Hh, 16), plan.Hh)
        cols = pl.ds(pl.multiple_of((t - g0) * C, 128), C)
        grads[...] = mm(dcT[rows], Y3[:, cols]).astype(BF16)

    @pl.when(last_step())
    def _():
        got = peers.finish(b_link)
        shift, gain = state[SHIFT2 : SHIFT2 + 1], state[GAIN2 : GAIN2 + 1]
        state[SU2 : SU2 + 1] = got[0:1]
        state[SU2 + 1 : SU2 + 2] = (got[1:2] - shift * got[0:1]) / gain
        b_halo.finish()
        for off in range(1, g):
            bulk(off, pl.ds(0, nw)).wait()


def block_phases(plan):
    n = plan.steps
    return n, 2 * n, 3 * n - 1, 4 * n - 1, 4 * n - 1 + plan.T2


class Reduction:
    def __init__(self, plan, batches, out, give, mine, got, spread, half, mate, sems):
        self.plan, self.batches, self.out = plan, batches, out
        self.give, self.mine, self.got, self.spread = give, mine, got, spread
        self.half, self.mate = half, mate
        self.sems = sems
        self.s, self.z, self.i, self.h = plan.place()
        self.c = lax.rem(self.s, 2)
        self.m = lax.div(self.s, 2)
        self.chips = plan.chips

    @staticmethod
    def scratch(plan, batches):
        taps, wide = plan.T1 + 2, plan.C // 2
        full = (taps, plan.chips, plan.g, plan.rb, wide)
        part = (taps, plan.g, plan.rb, wide)
        return [
            pltpu.VMEM((taps, 2, plan.chips, plan.rb, wide), BF16),
            *[pltpu.VMEM(full, BF16)] * 4,
            *[pltpu.VMEM(part, BF16)] * 2,
            pltpu.SemaphoreType.DMA((2, len(batches), 5)),
        ]

    def copy(self, b, phase, src, dst, device):
        return remote(src, dst, self.sems.at[0, b, phase], self.sems.at[1, b, phase], device)

    def finish(self, b, phase, ref, device):
        done = self.copy(b, phase, ref, ref, device)
        done.wait_recv()
        done.wait_send()

    def taps(self, b):
        return pl.ds(*self.batches[b])

    def pair(self):
        return (2 * self.m + (1 - self.c), self.z)

    def far(self, off):
        return (2 * wrap(self.m + off, self.chips) + self.c, self.z)

    def member(self, off):
        return (self.s, self.h * self.plan.g + wrap(self.i + off, self.plan.g))

    def put(self, k, rows):
        wide = self.plan.C // 2
        for j in range(self.plan.g):
            for m in range(self.chips):
                v = rows(j, m)
                left, right = v[:, :wide], v[:, wide:]
                self.mine[k, m, j] = jnp.where(self.c == 0, left, right).astype(BF16)
                self.give[k, m, j] = jnp.where(self.c == 0, right, left).astype(BF16)

    def step0(self, b):
        taps = self.taps(b)
        self.copy(b, 0, self.give.at[taps], self.got.at[taps], self.pair()).start()

    def step1(self, b):
        taps = self.taps(b)
        self.finish(b, 0, self.got.at[taps], self.pair())
        first, count = self.batches[b]
        for k in range(first, first + count):
            v = self.mine[k].astype(F32) + self.got[k].astype(F32)
            self.mine[k] = v.astype(BF16)
        for off in range(1, self.chips):
            src = self.mine.at[taps, wrap(self.m + off, self.chips)]
            self.copy(b, 1, src, self.spread.at[taps, self.m], self.far(off)).start()

    def step2(self, b):
        taps = self.taps(b)
        self.finish(b, 1, self.spread.at[taps, pl.ds(0, self.chips - 1)], self.far(1))
        first, count = self.batches[b]
        for k in range(first, first + count):
            self.spread[k, self.m] = self.mine[k, self.m]
            v = self.spread[k, 0].astype(F32)
            for n in range(1, self.chips):
                v = v + self.spread[k, n].astype(F32)
            self.half[k] = v.astype(BF16)
        for off in range(1, self.plan.g):
            src = self.half.at[taps, wrap(self.i + off, self.plan.g)]
            self.copy(b, 2, src, self.mate.at[taps, off], self.member(off)).start()

    def step3(self, b):
        taps = self.taps(b)
        self.finish(b, 2, self.mate.at[taps, pl.ds(1, self.plan.g - 1)], self.member(1))
        first, count = self.batches[b]
        for k in range(first, first + count):
            v = self.half[k, self.i].astype(F32)
            for off in range(1, self.plan.g):
                v = v + self.mate[k, off].astype(F32)
            self.out[k, self.c, self.m] = v.astype(BF16)
        mine = self.out.at[taps, self.c, self.m]
        for off in range(1, self.chips):
            self.copy(b, 3, mine, mine, self.far(off)).start()

    def step4(self, b):
        taps = self.taps(b)
        self.finish(b, 3, self.out.at[taps, self.c, pl.ds(0, self.chips - 1)], self.far(1))
        mine = self.out.at[taps, self.c]
        self.copy(b, 4, mine, mine, self.pair()).start()

    def step5(self, b):
        self.finish(b, 4, self.out.at[self.taps(b), self.c], self.pair())


def tail_turns(plan):
    nD = plan.steps
    first = max(nD - 1, 1)
    turns = [("x", n) for n in range(first)] + [("d", n) for n in range(first, nD)]
    turns += [("w", n) for n in range(plan.T1)]
    return turns + [("x", n) for n in range(first, nD)]


def tail_batches(plan):
    return [(plan.T1, 2), (0, 2), (2, 2), (4, plan.T1 - 4)]


def tail_kernel(plan, lens, dz2, dzland, x2, x2land, cot, beyond, x, X5_hbm, taps, grads, pgrad,
                old, half_state,
                gz, gz_got, sums, summed, gz_mine,
                ext, D3, D0T, wcat, pick, eye, cols, y, part, split, acc, X5, X5_sems,
                bulk_sems, store_sem, *rest):
    t = pl.program_id(0)
    s, z, i, h = plan.place()
    L, Lp, C, wb, g, nw = plan.L, plan.Lp, plan.C, plan.wb, plan.g, plan.nw
    Ch, cs, T1 = plan.Ch, plan.cs, plan.T1
    M = wb * Lp
    nD = plan.steps
    turns = tail_turns(plan)
    last = len(turns) - 1
    peers = group_peers(plan)
    red = Reduction(plan, tail_batches(plan), *rest[:8])
    link = rest[8:]

    def member(off):
        return (s, h * g + wrap(i + off, g))

    def send(first, count):
        rows = pl.ds(first, count)
        for off in range(1, g):
            remote(
                gz_mine.at[off - 1, rows],
                gz_got.at[off, rows],
                bulk_sems.at[0, off],
                bulk_sems.at[1, off],
                member(off),
            ).start()

    def X5_copy(k):
        return pltpu.make_async_copy(X5_hbm.at[k], X5.at[k % 2], X5_sems.at[k % 2])

    def when(at):
        return pl.when(t == min(at, last))

    def turn(kind, k):
        return turns.index((kind, k)) if (kind, k) in turns else last

    def turn_of(kind):
        index = jnp.int32(0)
        here = False
        for n, (what, k) in enumerate(turns):
            if what == kind:
                index = jnp.where(t == n, k, index)
                here = (t == n) | here
        return here, index

    @when(0)
    def _():
        greet(peers.others)
        acc[...] = jnp.zeros_like(acc)
        pick[...] = pick_matrix(L)
        eye[...] = eye_matrix(Ch, Ch, 0)
        mean, rho = norm_of(half_state[ST1 : ST1 + 2], 2.0 * total_of(lens))
        scale = half_state[GAIN1 : GAIN1 + 1] * rho
        offset = half_state[SHIFT1 : SHIFT1 + 1] - mean * scale
        for k, row in enumerate((scale, offset)):
            cols[k] = column(row, L)
        for first in range(0, Ch, 64):
            rows = slice(first, min(first + 64, Ch))
            for r, parts in enumerate((((0,), (1, 2), (3, 4)), ((0, 1), (2, 3), (4,)))):
                for k, which in enumerate(parts):
                    v = taps[which[0], rows]
                    if len(which) > 1:
                        v = (v.astype(F32) + taps[which[1], rows].astype(F32)).astype(BF16)
                    at = r * Ch
                    wcat[at + rows.start : at + rows.stop, k * C : (k + 1) * C] = v
        meet(peers.others)

    @pl.when(t < nD)
    def _():
        total = total_of(lens)
        mean, rho = norm_of(old[ST2 : ST2 + 2], total)
        gr = old[GAIN2 : GAIN2 + 1] * rho
        sg = old[SU2 : SU2 + 1] / total
        gg = old[SU2 + 1 : SU2 + 2] / total
        rowc = rows_of((Lp, C))
        row1 = rows_of((1, C))

        by_dz = 0.5 * gr
        by_v = -0.5 * gr * rho * gg
        by_1 = 0.5 * gr * (mean * rho * gg - sg)

        def back(dout, dz, v):
            return 0.5 * dout + by_dz * dz + by_v * v + by_1

        def grad_of(w):
            at = t * wb + w
            valid = lens[i * nw + at] - s * Lp
            d = back(cot[w].astype(F32), dz2[w], x2[w])
            d = jnp.where(rowc < valid, d, 0.0)
            one = pl.ds(at, 1)
            dl = back(beyond[0, 2, one, :], dzland[0, one, :], x2land[0, w, EDGE - 1 : EDGE].astype(F32))
            dl = jnp.where((row1 - 1 < valid) & (s > 0), dl, 0.0)
            dh = back(beyond[1, 2, one, :], dzland[1, one, :], x2land[1, w, 0:1].astype(F32))
            dh = jnp.where(row1 + Lp < valid, dh, 0.0)
            ext[w, 7:8] = dl
            ext[w, 8 : 8 + Lp] = d
            ext[w, 8 + Lp : 9 + Lp] = dh
            top, end = w * Lp, (w + 1) * Lp
            D3[t, top:end, 0:C] = ext[w, 9 : 9 + Lp].astype(BF16)
            D3[t, top:end, C : 2 * C] = d.astype(BF16)
            D3[t, top:end, 2 * C : 3 * C] = ext[w, 7 : 7 + Lp].astype(BF16)

        for w in range(wb):
            grad_of(w)
        half = D3[t, :, pl.ds(pl.multiple_of(C + h * Ch, 128), Ch)]
        D0T[:, pl.ds(pl.multiple_of(t * M, 128), M)] = half.T

    here_x, bx = turn_of("x")

    @pl.when(here_x)
    def _():
        lanes = lanes_of((Ch, L))

        def through(w):
            valid = 2 * lens[i * nw + bx * wb + w] - s * L
            top, end = w * Lp, (w + 1) * Lp
            v = mm_nt(eye[...], x[w])
            da = jnp.concatenate([y[0:Ch, top:end], y[Ch:, top:end]], axis=1)
            da = mm(da.astype(BF16), pick[...])
            zv = v * cols[0] + cols[1]
            dzw = da * gelu_slope(zv)
            dzw = jnp.where(lanes < valid, dzw, 0.0)
            acc[0] += fold_lanes(dzw)
            acc[1] += fold_lanes(dzw * zv)
            split[w % 2] = dzw.astype(BF16)
            for off in range(g):
                rows = pl.ds(pl.multiple_of(lax.rem(i + off, g) * cs, 16), cs)
                if off == 0:
                    gz[w] = split[w % 2, rows]
                else:
                    part[off - 1, bx * wb + w] = split[w % 2, rows]

        nh = 2 if wb % 2 == 0 and wb * Lp // 2 % 128 == 0 else 1
        n = wb // nh
        for hf in range(nh):
            rows = slice(hf * n * Lp, (hf + 1) * n * Lp)
            y[:, rows] = mm_nt(wcat[...], D3[bx, rows])
            for w in range(hf * n, (hf + 1) * n):
                through(w)

    @when(0)
    def _():
        hs = plan.H // plan.nz
        rb = plan.rb
        for u in range(2):

            def rows(j, m, u=u):
                side, r = m * rb // hs, m * rb % hs
                n = 2 * side + u
                rows = slice(j * hs + r, j * hs + r + rb)
                v = grads[rows, n * C : (n + 1) * C] if n < plan.T2 else pgrad[rows]
                return v.astype(F32)

            red.put(T1 + u, rows)
        red.step0(0)

    @when(1)
    def _():
        X5_copy(0).start()
        X5_copy(1).start()

    here_w, k = turn_of("w")

    @pl.when(here_w)
    def _():
        X5_copy(k).wait()
        y[0:Ch, 0:C] = mm(D0T[...], X5[lax.rem(k, 2)])

        @pl.when(k < T1 - 2)
        def _():
            X5_copy(k + 2).start()

        rb = plan.rb
        red.put(k, lambda j, m: y[j * cs + m * rb : j * cs + (m + 1) * rb, 0:C])

    @pl.when(here_x)
    def _():
        rows = pl.ds(bx * wb, wb)
        stored = pltpu.make_async_copy(part.at[:, rows], gz_mine.at[:, rows], store_sem)
        stored.start()
        stored.wait()

    @pl.when(here_x & (bx < nD - 1))
    def _():
        send(bx * wb, wb)

    @when(turn("x", nD - 1))
    def _():
        send((nD - 1) * wb, wb // 2)

    @when(turn("x", nD - 1))
    def _():
        packet = link[0]
        packet[...] = jnp.zeros_like(packet)
        packet[0:1, 0:Ch] = jnp.sum(acc[0].T, axis=0, keepdims=True)
        packet[1:2, 0:Ch] = jnp.sum(acc[1].T, axis=0, keepdims=True)
        peers.start(link)

    for at, step, batch in (
        (1, red.step1, 0),
        (max(nD - 1, 2), red.step2, 0),
        (turn("w", 1), red.step0, 1),
        (turn("w", 2), red.step1, 1),
        (turn("w", 3), red.step0, 2),
        (turn("w", 4), red.step1, 2),
        (turn("w", 4), red.step0, 3),
        (turn("w", 4), red.step2, 1),
        (last, red.step1, 3),
        (last, red.step2, 2),
        (last, red.step3, 0),
        (last, red.step3, 1),
        (last, red.step2, 3),
    ):

        @when(at)
        def _():
            step(batch)

    @when(last)
    def _():
        send(nw - wb + wb // 2, wb - wb // 2)

    @when(last)
    def _():
        red.step3(2)
        red.step4(0)
        red.step4(1)
        red.step3(3)
        red.step4(2)
        got = peers.finish(link)[:, 0:Ch]
        shift, gain = half_state[SHIFT1 : SHIFT1 + 1], half_state[GAIN1 : GAIN1 + 1]
        sums[0:1] = got[0:1]
        sums[1:2] = (got[1:2] - shift * got[0:1]) / gain
        red.step4(3)
        for b in range(4):
            red.step5(b)
        own = pltpu.make_async_copy(red.out, summed, X5_sems.at[0])
        own.start()
        for off in range(1, g):
            done = remote(
                gz_mine.at[off - 1],
                gz_got.at[off],
                bulk_sems.at[0, off],
                bulk_sems.at[1, off],
                member(off),
            )
            done.wait_recv()
            done.wait_send()
        own.wait()


def input_grad_kernel(plan, wg, lens, x, gz, gz_got, sums, res, res_got, summed,
                      state, half_state,
                      out, out_result, conv_grad, dil_grad, point_grad,
                      g1, b1, g2, b2, g3, b3, pb, eye, cols, xt):
    t = pl.program_id(0)
    s, z, i, h = plan.place()
    L, Ch, cs = plan.L, plan.Ch, plan.cs
    turn = plan.nw // wg
    mine = pl.ds(pl.multiple_of(i * cs, 16), cs)

    @pl.when(first_step())
    def _():
        n = 2.0 * total_of(lens)
        mean, rho = norm_of(half_state[ST1 : ST1 + 2], n)
        gr = half_state[GAIN1 : GAIN1 + 1] * rho
        gg = sums[1:2] / n * rho
        for k, row in enumerate((gr, -gr * gg, gr * (mean * gg - sums[0:1] / n))):
            xt[...] = column(row, L)
            cols[k] = xt[mine]
        eye[...] = eye_matrix(cs, Ch, i * cs)

        def mine_of(src, at, which, count, *dsts):
            n = dsts[0].shape[1]
            for k in range(count):

                @pl.when(which == k)
                def _():
                    for dst, r in zip(dsts, at):
                        dst[...] = src[r : r + 1, k * n : (k + 1) * n]

        mine_of(sums, (1, 0), i, plan.g, g1, b1)
        mine_of(state, (SU2 + 1, SU2), z, plan.nz, g2, b2)
        mine_of(state, (SU3 + 1, SU3), z, plan.nz, g3, b3)
        mine_of(state, (BSUM,), z, plan.nz, pb)

    own = lax.div(t, turn) == i
    for w in range(wg):
        out_result[w] = jnp.where(own, res[0, w], res_got[0, w])

    C, T1, hs, rb, wide = plan.C, plan.T1, plan.H // plan.nz, plan.rb, plan.C // 2
    count = plan.NW // wg
    turns = min(count, plan.chips)
    per, every = plan.chips // turns, count // turns

    def spread(chunk):
        for n in range(per):
            m = chunk * per + n
            side, r = m * rb // hs, m * rb % hs
            for c in range(2):
                at = slice(c * wide, (c + 1) * wide)
                for k in range(T1):
                    conv_grad[k, n * rb : (n + 1) * rb, at] = summed[k, c, n].astype(F32)
                for u in range(2):
                    v = summed[T1 + u, c, n].astype(F32)
                    if 2 * side + u < plan.T2:
                        dil_grad[2 * side + u, r : r + rb, at] = v
                    else:
                        point_grad[r : r + rb, at] = v

    for chunk in range(turns):
        pl.when(t == chunk * every)(partial(spread, chunk))

    lanes = lanes_of((cs, L))
    for w in range(wg):
        valid = 2 * lens[t * wg + w] - s * L
        v = mm_nt(eye[...], x[w])
        dz = jnp.where(own, gz[w], gz_got[0, w]).astype(F32)
        r = cols[0] * dz + v * cols[1] + cols[2]
        out[w] = jnp.where(lanes < valid, r, 0.0).astype(BF16)


def call(kernel, plan, name, steps, ins, outs, scratch, flops, nbytes, cid=None):
    extra = {} if cid is None else dict(collective_id=cid, has_side_effects=True)
    return pl.pallas_call(
        partial(kernel, plan),
        grid=(steps,),
        in_specs=[SMEM] + [spec for spec, _ in ins],
        out_specs=[spec for spec, _, _ in outs],
        out_shape=[jax.ShapeDtypeStruct(shape, dtype) for _, shape, dtype in outs],
        scratch_shapes=scratch,
        compiler_params=pltpu.CompilerParams(vmem_limit_bytes=VMEM_LIMIT, **extra),
        cost_estimate=pl.CostEstimate(
            flops=int(flops), bytes_accessed=int(nbytes), transcendentals=0
        ),
        name=name,
    )


def per_device(
    inputs,
    lengths,
    input_gain,
    input_shift,
    conv_weight,
    branch_gain,
    branch_shift,
    dilated_tap_weight,
    mixer_gain,
    mixer_shift,
    point_weight,
    point_bias,
    cotangent,
):
    NW, L, C = inputs.shape
    Lp = L // 2
    nz = lax.axis_size("ch")
    R = 2
    plan = Plan(
        ns=lax.axis_size("seq"),
        nz=nz,
        R=R,
        NW=NW,
        L=L,
        C=C,
        H=mixer_gain.shape[0] * nz,
        T1=conv_weight.shape[0],
        T2=dilated_tap_weight.shape[0],
        wb=min(NW * R // nz, max(1, 512 // Lp)),
    )
    g, nw, cs, Ch, H, Hh, wb = plan.g, plan.nw, plan.cs, plan.Ch, plan.H, plan.Hh, plan.wb
    T1, T2, steps = plan.T1, plan.T2, plan.steps
    M = wb * Lp
    hs = H // nz
    lens = lengths.astype(jnp.int32)

    def row(a):
        return a.reshape(1, a.shape[0])

    def grp():
        return lax.rem(lax.axis_index("ch"), g)

    def half():
        return lax.div(lax.axis_index("ch"), g)

    def core():
        return lax.rem(lax.axis_index("seq"), 2)

    def chip4():
        return lax.div(lax.axis_index("seq"), plan.ns // 4)

    def whole(*shape):
        return pl.BlockSpec(shape, lambda t: (0,) * len(shape), pipeline_mode=pl.Buffered(1))

    def const(*shape):
        return pl.BlockSpec(shape, lambda t: (0,) * len(shape))

    def win(*shape):
        return pl.BlockSpec(shape, lambda t: (t,) + (0,) * (len(shape) - 1))

    def arg_win(n, width):
        return pl.BlockSpec((wb, n, width), lambda t: (grp() * steps + t, 0, 0))

    def ins(*pairs):
        return [p for p in pairs]

    share = NW // nz
    nm = max(1, share // wb)

    def edge_spec(n):
        return pl.BlockSpec(
            (nw, 16, C), lambda t: (grp(), n, 0), pipeline_mode=pl.Buffered(1)
        )

    def head_block(t):
        own = lax.div(lax.axis_index("ch") * share, wb) + t
        return jnp.where(t < nm, own, grp() * steps + t - nm), 0, 0

    def after(*shape):
        return pl.BlockSpec(
            shape, lambda t: (jnp.maximum(t - nm, 0),) + (0,) * (len(shape) - 1)
        )

    pairs = ins(
        (pl.BlockSpec((wb, L, C), head_block), inputs),
        (edge_spec(0), inputs),
        (edge_spec(L // 16 - 1), inputs),
        (edge_spec(0), cotangent),
        (edge_spec(Lp // 16 - 1), cotangent),
        (whole(1, cs), row(branch_gain)),
        (whole(1, cs), row(branch_shift)),
        (whole(1, cs), row(point_bias)),
        (whole(1, H // nz), row(mixer_gain)),
        (whole(1, H // nz), row(mixer_shift)),
        (ANY, conv_weight.reshape(T1 * C, C)),
        (whole(C), input_gain),
        (whole(C), input_shift),
        (
            pl.BlockSpec(
                (1, hs, C // 2),
                lambda t: (jnp.minimum(chip4(), T2 - 1), 0, core()),
                pipeline_mode=pl.Buffered(1),
            ),
            jnp.swapaxes(dilated_tap_weight, 1, 2),
        ),
        (
            pl.BlockSpec(
                (hs, C // 2), lambda t: (0, core()), pipeline_mode=pl.Buffered(1)
            ),
            point_weight,
        ),
    )
    plane, line, group = plane_peers(plan), line_peers(plan), group_peers(plan)
    state_shape = (STATE, C)
    edges2, edges3 = (2, nw, EDGE, C), (2, nw, EDGE, H)
    X5, x2, land2, state, beyond, full = call(
        lambda plan, *refs: head_kernel(plan, nm, *refs),
        plan,
        "head",
        nm + steps,
        pairs,
        [
            (
                pl.BlockSpec((T1, M, C), lambda t: (0, jnp.maximum(t - nm, 0), 0)),
                (T1, nw * Lp, C),
                BF16,
            ),
            (after(wb, Lp, C), (nw, Lp, C), F32),
            (ANY, edges2, BF16),
            (const(*state_shape), state_shape, F32),
            (const(2, 3, nw, C), (2, 3, nw, C), F32),
            (ANY, (2, T2 + 1, nz, hs, C // 2), BF16),
        ],
        [
            pltpu.VMEM((2, 8, C), F32),
            pltpu.VMEM((2, 3, nw, C), F32),
            pltpu.VMEM((2, 3, nw, C), F32),
            pltpu.VMEM((T1 * Lp, L), BF16),
            pltpu.VMEM(edges2, BF16),
            pltpu.VMEM((2, C), F32),
            pltpu.VMEM((T1 * C, C), BF16),
            pltpu.SemaphoreType.DMA,
            pltpu.VMEM((hs, C // 2), BF16),
            pltpu.SemaphoreType.DMA((2, 4)),
            HALO_SEMS,
            HALO_SEMS,
        ]
        + plane.scratch(2, C)
        + line.scratch(3, C)
        + group.scratch(2, C),
        2 * nw * Lp * T1 * C * C,
        nw * Lp * C * 20,
        cid=1,
    )(lens, *[a for _, a in pairs])

    full = full.reshape(2, T2 + 1, H, C // 2)
    taps_spec = whole(2, T2, H, C // 2)
    pw_spec = pl.BlockSpec(
        (2, 1, H, C // 2), lambda t: (0, T2, 0, 0), pipeline_mode=pl.Buffered(1)
    )

    def early(*shape):
        return pl.BlockSpec(
            shape, lambda t: (jnp.minimum(t, steps - 1),) + (0,) * (len(shape) - 1)
        )

    def early_land(width):
        return pl.BlockSpec(
            (2, wb, EDGE, width), lambda t: (0, jnp.minimum(t, steps - 1), 0, 0)
        )

    def half_of(n):
        return pl.BlockSpec((n, Ch), lambda t: (0, half()), pipeline_mode=pl.Buffered(1))

    cot_spec = pl.BlockSpec(
        (wb, Lp, C), lambda t: (grp() * steps + jnp.minimum(t, steps - 1), 0, 0)
    )

    p0, r0, b0, g0, block_steps = block_phases(plan)

    def at_phase(first):
        return lambda t: jnp.clip(t - first, 0, steps - 1)

    in_p, in_b = at_phase(p0), at_phase(b0)
    pairs = ins(
        (
            pl.BlockSpec(
                (wb, Lp, C),
                lambda t: (jnp.where(t < p0 + steps, jnp.minimum(t, steps - 1), in_b(t)), 0, 0),
            ),
            x2,
        ),
        (
            pl.BlockSpec(
                (wb, Lp, Ch),
                lambda t: (jnp.clip(t - r0 + 1, 0, steps - 1), 0, half()),
            ),
            x2,
        ),
        (early_land(C), land2),
        (pl.BlockSpec((wb, Lp, C), lambda t: (grp() * steps + in_p(t), 0, 0)), cotangent),
        (taps_spec, full),
        (pw_spec, full),
        (whole(*state_shape), state),
        (half_of(STATE), state),
    )
    dz2, grads, pgrad, res, dland2, state, res_got = call(
        block_kernel,
        plan,
        "block",
        block_steps,
        pairs,
        [
            (pl.BlockSpec((wb, Lp, C), lambda t: (in_b(t), 0, 0)), (nw, Lp, C), F32),
            (
                pl.BlockSpec((Hh, C), lambda t: (0, jnp.maximum(t - g0, 0))),
                (Hh, T2 * C),
                BF16,
            ),
            (const(Hh, C), (Hh, C), BF16),
            (const(g, nw, cs, Lp), (g, nw, cs, Lp), BF16),
            (ANY, (2, nw, C), F32),
            (const(*state_shape), state_shape, F32),
            (ANY, (g, nw, cs, Lp), BF16),
        ],
        [
            pltpu.VMEM((wb, Lp + 2 * EDGE, C), F32),
            pltpu.VMEM((H, T2 * C), BF16),
            pltpu.VMEM((T2 * H, C), BF16),
            pltpu.VMEM((H, C), BF16),
            pltpu.VMEM((nw * Lp, T2 * C), BF16),
            pltpu.VMEM((nw, Lp, H), F32),
            pltpu.VMEM((nw, Lp, H), F32),
            pltpu.VMEM((M, H), F32),
            pltpu.VMEM((nw * Lp, H), BF16),
            pltpu.VMEM((H, nw * Lp), BF16),
            pltpu.VMEM((nw * Lp, C), BF16),
            pltpu.VMEM((M, T2 * H), BF16),
            pltpu.VMEM((H, nw * Lp), BF16),
            pltpu.VMEM(edges3, BF16),
            pltpu.VMEM(edges3, BF16),
            pltpu.VMEM((1, 2 * H), F32),
            pltpu.VMEM(edges3, BF16),
            pltpu.VMEM(edges3, BF16),
            pltpu.VMEM((2, C), F32),
            pltpu.VMEM((2, nw, C), F32),
            pltpu.VMEM((2, C), F32),
            pltpu.SemaphoreType.DMA((3, 2, 2)),
            pltpu.SemaphoreType.DMA((2, g)),
        ]
        + group.scratch(1, 2 * H)
        + group.scratch(2, C)
        + group.scratch(2, C),
        nw * Lp * C * H * (6 * T2 + 6),
        nw * Lp * C * 30,
        cid=3,
    )(lens, *[a for _, a in pairs])

    chips, rb = plan.chips, plan.rb
    turns_t = tail_turns(plan)

    def x_block(t):
        block = jnp.int32(0)
        for n, (what, k) in enumerate(turns_t):
            if what == "x":
                block = jnp.where(t >= n, k, block)
        return block

    sshape = (T1 + 2, 2, chips, rb, C // 2)
    pairs = ins(
        (early(wb, Lp, C), dz2),
        (whole(2, nw, C), dland2),
        (early(wb, Lp, C), x2),
        (early_land(C), land2),
        (cot_spec, cotangent),
        (whole(2, 3, nw, C), beyond),
        (
            pl.BlockSpec(
                (wb, L, Ch), lambda t: (grp() * steps + x_block(t), 0, half())
            ),
            inputs,
        ),
        (ANY, X5),
        (
            pl.BlockSpec(
                (T1, Ch, C), lambda t: (0, half(), 0), pipeline_mode=pl.Buffered(1)
            ),
            conv_weight,
        ),
        (whole(Hh, T2 * C), grads),
        (whole(Hh, C), pgrad),
        (whole(*state_shape), state),
        (half_of(STATE), state),
    )
    gz, gz_got, sums1, summed, _ = call(
        tail_kernel,
        plan,
        "tail",
        len(turns_t),
        pairs,
        [
            (pl.BlockSpec((wb, cs, L), lambda t: (x_block(t), 0, 0)), (nw, cs, L), BF16),
            (ANY, (g, nw, cs, L), BF16),
            (const(2, Ch), (2, Ch), F32),
            (ANY, sshape, BF16),
            (ANY, (g - 1, nw, cs, L), BF16),
        ],
        [
            pltpu.VMEM((wb, Lp + 16, C), F32),
            pltpu.VMEM((steps, M, 3 * C), BF16),
            pltpu.VMEM((Ch, nw * Lp), BF16),
            pltpu.VMEM((2 * Ch, 3 * C), BF16),
            pltpu.VMEM((L, L), BF16),
            pltpu.VMEM((Ch, Ch), BF16),
            pltpu.VMEM((2, Ch, L), F32),
            pltpu.VMEM((2 * Ch, max(M, C)), F32),
            pltpu.VMEM((g - 1, nw, cs, L), BF16),
            pltpu.VMEM((2, Ch, L), BF16),
            pltpu.VMEM((2, Ch, min(L, 128)), F32),
            pltpu.VMEM((2, nw * Lp, C), BF16),
            pltpu.SemaphoreType.DMA((2,)),
            pltpu.SemaphoreType.DMA((2, g)),
            pltpu.SemaphoreType.DMA,
        ]
        + Reduction.scratch(plan, tail_batches(plan))
        + group.scratch(2, C),
        2 * nw * Lp * (6 + T1) * C * Ch,
        nw * Lp * C * 40,
        cid=6,
    )(lens, *[a for _, a in pairs])

    wg = min(2 * wb, nw)
    count = NW // wg
    turn = nw // wg
    turns = min(count, chips)

    def own_block(t):
        return jnp.where(lax.div(t, turn) == grp(), lax.rem(t, turn), 0)

    def got_slot(t):
        off = lax.rem(grp() - lax.div(t, turn) + g, g)
        return jnp.maximum(off, 1), jnp.where(off > 0, lax.rem(t, turn), 0)

    pairs = ins(
        (pl.BlockSpec((wg, L, Ch), lambda t: (t, 0, half())), inputs),
        (pl.BlockSpec((wg, cs, L), lambda t: (own_block(t), 0, 0)), gz),
        (pl.BlockSpec((1, wg, cs, L), lambda t: got_slot(t) + (0, 0)), gz_got),
        (whole(2, Ch), sums1),
        (pl.BlockSpec((1, wg, cs, Lp), lambda t: (grp(), own_block(t), 0, 0)), res),
        (pl.BlockSpec((1, wg, cs, Lp), lambda t: got_slot(t) + (0, 0)), res_got),
        (
            pl.BlockSpec(
                (T1 + 2, 2, chips // turns, rb, C // 2),
                lambda t: (0, 0, t * turns // count, 0, 0),
            ),
            summed,
        ),
        (whole(*state_shape), state),
        (half_of(STATE), state),
    )
    outs = call(
        lambda plan, *refs: input_grad_kernel(plan, wg, *refs),
        plan,
        "input_grad",
        count,
        pairs,
        [
            (win(wg, cs, L), (NW, cs, L), BF16),
            (win(wg, cs, Lp), (NW, cs, Lp), BF16),
            (
                pl.BlockSpec((T1, cs // turns, C), lambda t: (0, t * turns // count, 0)),
                (T1, cs, C),
                F32,
            ),
            (const(T2, hs, C), (T2, hs, C), F32),
            (const(hs, C), (hs, C), F32),
        ]
        + [(const(1, n), (1, n), F32) for n in (cs, cs, cs, cs, hs, hs, cs)],
        [
            pltpu.VMEM((cs, Ch), BF16),
            pltpu.VMEM((3, cs, L), F32),
            pltpu.VMEM((Ch, L), F32),
        ],
        2 * NW * L * Ch * cs,
        NW * L * cs * 8,
    )(lens, *[a for _, a in pairs])
    grad, result, conv_grad, dil_grad, point_grad = outs[:5]
    g1, b1, g2, b2, g3, b3, pb = [a[0] for a in outs[5:]]
    return (
        jnp.swapaxes(result, 1, 2),
        jnp.swapaxes(grad, 1, 2),
        jnp.swapaxes(conv_grad, 1, 2),
        g1,
        b1,
        g2,
        b2,
        jnp.swapaxes(dil_grad, 1, 2),
        g3,
        b3,
        point_grad,
        pb,
    )


def solution(mesh):
    in_specs = (
        P(None, "seq", None),
        P(),
        P(),
        P(),
        P(),
        P("ch"),
        P("ch"),
        P(None, None, "ch"),
        P("ch"),
        P("ch"),
        P("ch", None),
        P("ch"),
        P(None, "seq", None),
    )
    out_specs = (
        P(None, "seq", "ch"),
        P(None, "seq", "ch"),
        P(None, None, "ch"),
        P("ch"),
        P("ch"),
        P("ch"),
        P("ch"),
        P(None, None, "ch"),
        P("ch"),
        P("ch"),
        P("ch", None),
        P("ch"),
    )
    return jax.shard_map(
        per_device, mesh=mesh, in_specs=in_specs, out_specs=out_specs, check_vma=False
    )
```

```python
from functools import partial
from typing import NamedTuple

import jax
import jax.numpy as jnp
from jax import lax
from jax.experimental import pallas as pl
from jax.experimental.pallas import tpu as pltpu
from jax.sharding import PartitionSpec as P

DIL = 14
EDGE = 16
EPS = 1e-05
GC0 = 0.7978845608028654
GC1 = 0.044715
F32 = jnp.float32
BF16 = jnp.bfloat16
MESH = pl.DeviceIdType.MESH
VMEM_LIMIT = 58 * 1024 * 1024
ANY = pl.BlockSpec(memory_space=pl.ANY)
SMEM = pl.BlockSpec(memory_space=pltpu.SMEM)


ST1, GAIN2, SHIFT2, BIAS, GAIN3, SHIFT3, GAIN1, SHIFT1, ST2, ST3, SU3, BSUM, SU2 = (
    0, 2, 3, 4, 5, 6, 7, 8, 9, 11, 13, 15, 16
)
STATE = 24


class Plan(NamedTuple):
    ns: int
    nz: int
    R: int
    NW: int
    L: int
    C: int
    H: int
    T1: int
    T2: int
    wb: int

    @property
    def g(self):
        return self.nz // self.R

    @property
    def nw(self):
        return self.NW // self.g

    @property
    def Lp(self):
        return self.L // 2

    @property
    def cs(self):
        return self.C // self.nz

    @property
    def Ch(self):
        return self.C // self.R

    @property
    def Hh(self):
        return self.H // self.R

    @property
    def steps(self):
        return self.nw // self.wb

    @property
    def chips(self):
        return self.ns // 2

    @property
    def rb(self):
        return self.cs // self.chips

    def place(self):
        s, z = lax.axis_index("seq"), lax.axis_index("ch")
        return s, z, lax.rem(z, self.g), lax.div(z, self.g)


def gelu(z):
    t = jnp.tanh(z * (GC0 + (GC0 * GC1) * (z * z)))
    return z * (0.5 + 0.5 * t)


def gelu_both(z):
    sq = z * z
    t = jnp.tanh(z * (GC0 + (GC0 * GC1) * sq))
    h = 0.5 + 0.5 * t
    v = z * h
    return v, h + v * (1.0 - t) * (GC0 + (3.0 * GC0 * GC1) * sq)


def gelu_slope(z):
    return gelu_both(z)[1]


def fold(v):
    return jnp.sum(v.reshape(v.shape[0] // 8, 8, v.shape[1]), axis=0)


def fold_lanes(v):
    out = v[:, 0:128]
    for k in range(128, v.shape[1], 128):
        out = out + v[:, k : k + 128]
    return out


def unfold(v):
    return jnp.sum(v, axis=0, keepdims=True)


def rows_of(shape):
    return lax.broadcasted_iota(jnp.int32, shape, 0)


def lanes_of(shape):
    return lax.broadcasted_iota(jnp.int32, shape, 1)


def total_of(lens):
    n = lens[0]
    for k in range(1, lens.shape[0]):
        n = n + lens[k]
    return n.astype(F32)


def norm_of(stats, total):
    mean = stats[0:1] / total
    square = stats[1:2] / total
    return mean, lax.rsqrt(square - mean * mean + EPS)


def flat(ref):
    return ref[...].reshape(1, ref.shape[0])


def column(row, n):
    return jnp.broadcast_to(row, (n, row.shape[1])).T


def mm(a, b):
    return jnp.dot(a, b, preferred_element_type=F32)


def mm_nt(a, b):
    return lax.dot_general(a, b, (((1,), (1,)), ((), ())), preferred_element_type=F32)


def mm_tn(a, b):
    return lax.dot_general(a, b, (((0,), (0,)), ((), ())), preferred_element_type=F32)


def mm_tt(a, b):
    return lax.dot_general(a, b, (((0,), (1,)), ((), ())), preferred_element_type=F32)


def eye_matrix(n, m, first):
    return jnp.where(lanes_of((n, m)) == rows_of((n, m)) + first, 1.0, 0.0).astype(BF16)


def pick_matrix(L):
    r, n = rows_of((L, L)), lanes_of((L, L))
    bin_of = 2 * r - jnp.where(r >= L // 2, L - 1, 0)
    return jnp.where(n == bin_of, 1.0, 0.0).astype(BF16)


def remote(src, dst, send, recv, device):
    return pltpu.make_async_remote_copy(
        src_ref=src,
        dst_ref=dst,
        send_sem=send,
        recv_sem=recv,
        device_id=device,
        device_id_type=MESH,
    )


def wrap(v, n):
    return jnp.where(v >= n, v - n, v)


def greet(devices):
    barrier = pltpu.get_barrier_semaphore()
    for device in devices:
        pl.semaphore_signal(barrier, inc=1, device_id=device, device_id_type=MESH)


def meet(devices):
    pl.semaphore_wait(pltpu.get_barrier_semaphore(), len(devices))


class Peers:
    def __init__(self, me, others):
        self.me, self.others = me, others
        self.count = len(others) + 1

    def start(self, link):
        packet, buf, sems = link
        for device in self.others:
            remote(packet, buf.at[self.me], sems.at[0], sems.at[1], device).start()

    def finish(self, link):
        packet, buf, sems = link
        buf[self.me] = packet[...]
        rest = buf.at[pl.ds(0, self.count - 1)]
        done = remote(rest, rest, sems.at[0], sems.at[1], self.others[0])
        done.wait_recv()
        acc = buf[0]
        for q in range(1, self.count):
            acc = acc + buf[q]
        done.wait_send()
        return acc

    def scratch(self, rows, width):
        return [
            pltpu.VMEM((rows, width), F32),
            pltpu.VMEM((self.count, rows, width), F32),
            pltpu.SemaphoreType.DMA((2,)),
        ]


def group_peers(plan):
    s, z, i, h = plan.place()
    g = plan.g
    others = [
        (wrap(s + a, plan.ns), h * g + wrap(i + b, g))
        for a in range(plan.ns)
        for b in range(g)
        if a or b
    ]
    return Peers(s * g + i, others)


def plane_peers(plan):
    s, z, i, h = plan.place()
    return Peers(s, [(wrap(s + a, plan.ns), z) for a in range(1, plan.ns)])


def line_peers(plan):
    s, z, i, h = plan.place()
    return Peers(z, [(s, wrap(z + a, plan.nz)) for a in range(1, plan.nz)])


class Halo:
    def __init__(self, plan, edge, land, sems):
        self.edge, self.land, self.sems = edge, land, sems
        s, z, _, _ = plan.place()
        self.to = ((wrap(s + plan.ns - 1, plan.ns), z), (wrap(s + 1, plan.ns), z))

    def copy(self, side, rows):
        return remote(
            self.edge.at[side, rows],
            self.land.at[1 - side, rows],
            self.sems.at[0, side],
            self.sems.at[1, side],
            self.to[side],
        )

    def start(self, first, count):
        for side in range(2):
            self.copy(side, pl.ds(first, count)).start()

    def finish(self):
        for side in range(2):
            done = self.copy(side, pl.ds(0, self.land.shape[1]))
            done.wait_recv()
            done.wait_send()


HALO_SEMS = pltpu.SemaphoreType.DMA((2, 2))


class Gather:
    def __init__(self, plan, part, full, sems):
        self.plan, self.part, self.full, self.sems = plan, part, full, sems
        self.s, self.z, self.i, self.h = plan.place()
        self.c, self.m = lax.rem(self.s, 2), lax.div(self.s, 2)
        self.chips = plan.chips
        self.every = self.chips // 4
        self.tap = lax.div(self.m, self.every)
        self.owner = lax.rem(self.m, self.every) == 0
        self.mine = full.at[self.c, self.tap]

    def others(self):
        g, nz = self.plan.g, self.plan.nz
        return [(self.s, wrap(self.h * g + g + r, nz)) for r in range(nz - g)]

    def far(self, off):
        return (2 * wrap(self.m + off, self.chips) + self.c, self.z)

    def own(self):
        return pltpu.make_async_copy(self.part, self.mine.at[self.z], self.sems.at[0, 0])

    def line(self, off):
        device = (self.s, wrap(self.z + off, self.plan.nz))
        return remote(
            self.part, self.mine.at[self.z], self.sems.at[0, 1], self.sems.at[1, 1], device
        )

    def chip(self, off):
        return remote(self.mine, self.mine, self.sems.at[0, 2], self.sems.at[1, 2], self.far(off))

    def pair(self):
        half = self.full.at[self.c]
        device = (2 * self.m + 1 - self.c, self.z)
        return remote(half, half, self.sems.at[0, 3], self.sems.at[1, 3], device)

    def line_start(self):
        @pl.when(self.owner)
        def _():
            self.own().start()
            for off in range(1, self.plan.nz):
                self.line(off).start()

    def line_finish(self):
        @pl.when(self.owner)
        def _():
            self.own().wait()
            rest = self.mine.at[pl.ds(0, self.plan.nz - 1)]
            device = (self.s, wrap(self.z + 1, self.plan.nz))
            done = remote(rest, rest, self.sems.at[0, 1], self.sems.at[1, 1], device)
            done.wait_recv()
            done.wait_send()

    def chips_start(self):
        @pl.when(self.owner)
        def _():
            for off in range(1, self.chips):
                self.chip(off).start()

    def pair_start(self):
        def taken(count):
            rest = self.full.at[self.c, pl.ds(0, count)]
            return remote(rest, rest, self.sems.at[0, 2], self.sems.at[1, 2], self.far(1))

        @pl.when(self.owner)
        def _():
            taken(3).wait_recv()
            for off in range(1, self.chips):
                self.chip(off).wait_send()

        if self.every > 1:

            @pl.when(jnp.logical_not(self.owner))
            def _():
                taken(4).wait_recv()

        self.pair().start()

    def pair_finish(self):
        done = self.pair()
        done.wait_recv()
        done.wait_send()


def first_step():
    return pl.program_id(0) == 0


def last_step():
    return pl.program_id(0) == pl.num_programs(0) - 1


def head_kernel(plan, nm, lens, x, xtop, xend, ctop, cend, g2, s2, pb, g3, s3,
                w_hbm, gain, shift, taps, pw,
                X5, x2, land, state, beyond_out, full,
                macc, beyond, xedge, sel, edge, acc, w_ref, w_sem, part,
                gather_sems, xhalo_sems, halo_sems, *links):
    t = pl.program_id(0)
    peers, plane, line = group_peers(plan), plane_peers(plan), line_peers(plan)
    xhalo = Halo(plan, xedge, beyond, xhalo_sems)
    halo = Halo(plan, edge, land, halo_sems)
    gather = Gather(plan, part, full, gather_sems)
    w_copy = pltpu.make_async_copy(w_hbm, w_ref, w_sem)
    plane_link, line_link, link = links[:3], links[3:6], links[6:]
    s, z, i, h = plan.place()
    L, Lp, C, nw, nz, wb = plan.L, plan.Lp, plan.C, plan.nw, plan.nz, plan.wb
    share = plan.NW // nz
    c = t - nm
    everyone = peers.others + gather.others()

    @pl.when(first_step())
    def _():
        w_copy.start()
        greet(everyone)
        part[...] = jnp.where(gather.tap == 3, pw[...], taps[0])
        macc[...] = jnp.zeros_like(macc)
        acc[...] = jnp.zeros_like(acc)
        state[...] = jnp.zeros_like(state)
        state[GAIN1 : GAIN1 + 1] = flat(gain)
        state[SHIFT1 : SHIFT1 + 1] = flat(shift)
        n16 = nw * 16
        for side, (xe, ce, places) in enumerate(
            ((xtop, ctop, (0, 1, 0)), (xend, cend, (14, 15, 15)))
        ):
            for k, at in enumerate(places):
                rows, lanes = rows_of((nw, n16)), lanes_of((nw, n16))
                one = jnp.where(lanes == 16 * rows + at, 1.0, 0.0).astype(BF16)
                block = (xe if k < 2 else ce)[...].reshape(n16, C)
                xedge[side, k] = mm(one, block)
        shape = (Lp, L)
        for k in range(plan.T1):
            at = lanes_of(shape) - (2 * rows_of(shape) + (k - 2))
            sel[k * Lp : (k + 1) * Lp] = jnp.where((at == 0) | (at == 1), 1.0, 0.0).astype(BF16)

    @pl.when(c < 0)
    def _():
        rows = rows_of((L, C))
        for w in range(min(share, wb)):
            at = lax.rem(z * share, wb) + w
            valid = 2 * lens[z * share + t * wb + w] - s * L
            v = jnp.where(rows < valid, x[at].astype(F32), 0.0)
            macc[0] += fold(v)
            macc[1] += fold(v * v)

    @pl.when(c == -1)
    def _():
        packet, more = plane_link[0], line_link[0]
        packet[0:1] = unfold(macc[0])
        packet[1:2] = unfold(macc[1])
        meet(everyone)
        plane.start(plane_link)
        xhalo.start(0, 3)
        at = 0
        spans = []
        more[2:3] = jnp.zeros((1, C), F32)
        for ref in (g2, s2, pb, g3, s3):
            n = ref.shape[1]
            more[2:3, at : at + n] = ref[...]
            spans.append((at, n))
            at += n
        more[0:2] = plane.finish(plane_link)
        line.start(line_link)
        gather.line_start()
        state[ST1 : ST1 + 2] = line.finish(line_link)[0:2]
        for k in range(nz):
            row = line_link[1][k]
            for r, (at, n) in zip((GAIN2, SHIFT2, BIAS, GAIN3, SHIFT3), spans):
                state[r : r + 1, k * n : (k + 1) * n] = row[2:3, at : at + n]
        xhalo.finish()
        beyond_out[...] = beyond[...]
        w_copy.wait()

    @pl.when(c >= 0)
    def _():
        mean, rho = norm_of(state[ST1 : ST1 + 2], 2.0 * total_of(lens))
        scale = state[GAIN1 : GAIN1 + 1] * rho
        offset = state[SHIFT1 : SHIFT1 + 1] - mean * scale
        rows = rows_of((L, C))
        row1 = rows_of((1, C))
        row16 = rows_of((16, C))
        def activate(w):
            at = c * wb + w
            valid = 2 * lens[i * nw + at] - s * L
            a = gelu(x[w].astype(F32) * scale + offset)
            a = jnp.where(rows < valid, a, 0.0).astype(BF16)
            picked = mm(sel[...], a)
            for k in range(5):
                X5[k, w * Lp : (w + 1) * Lp] = picked[k * Lp : (k + 1) * Lp].astype(BF16)

            def beside(side, k, bin_at):
                a = gelu(beyond[side, k, pl.ds(at, 1), :] * scale + offset)
                here = (row1 + bin_at < valid) & (row1 + (s * L + bin_at) >= 0)
                return jnp.where(here, a, 0.0).astype(BF16).astype(F32)

            l0, l1 = beside(0, 0, -2), beside(0, 1, -1)
            r0, r1 = beside(1, 0, L), beside(1, 1, L + 1)
            top, end = w * Lp, (w + 1) * Lp
            for k, add in ((0, l0 + l1), (1, l1)):
                X5[k, top : top + 16] = (
                    picked[k * Lp : k * Lp + 16] + jnp.where(row16 == 0, add, 0.0)
                ).astype(BF16)
            for k, add in ((3, r0), (4, r0 + r1)):
                X5[k, end - 16 : end] = (
                    picked[(k + 1) * Lp - 16 : (k + 1) * Lp] + jnp.where(row16 == 15, add, 0.0)
                ).astype(BF16)

        nc = 256
        rowp = rows_of((Lp, nc))

        def convolve(first, count):
            span = slice(first * Lp, (first + count) * Lp)
            for n in range(C // nc):
                cols = slice(n * nc, (n + 1) * nc)
                taps = [X5[k, span] for k in range(plan.T1)]
                y = 0.5 * mm(jnp.concatenate(taps, axis=1), w_ref[:, cols])
                s0 = jnp.zeros((8, nc), F32)
                s1 = jnp.zeros((8, nc), F32)
                for w in range(first, first + count):
                    at = c * wb + w
                    valid = lens[i * nw + at] - s * Lp
                    v = y[(w - first) * Lp : (w - first + 1) * Lp]
                    x2[w, :, cols] = v
                    edge[0, at, :, cols] = v[:EDGE].astype(BF16)
                    edge[1, at, :, cols] = v[Lp - EDGE :].astype(BF16)
                    v = jnp.where(rowp < valid, v, 0.0)
                    s0 = s0 + fold(v)
                    s1 = s1 + fold(v * v)
                acc[0:1, cols] += unfold(s0)
                acc[1:2, cols] += unfold(s1)

        count = max(1, wb // 2)
        for first in range(0, wb, count):
            for w in range(first, first + count):
                activate(w)
            convolve(first, count)
        halo.start(c * wb, wb)

    @pl.when(c == 0)
    def _():
        gather.line_finish()
        gather.chips_start()

    @pl.when(last_step())
    def _():
        link[0][...] = acc[...]
        peers.start(link)
        gather.pair_start()
        state[ST2 : ST2 + 2] = peers.finish(link)
        halo.finish()
        gather.pair_finish()


def block_kernel(plan, lens, x2, x2half, x2land, cot, w_ref, pw_ref, old, half_state,
                 dz2, grads, pgrad, res, land, state, res_got,
                 ext, wf, wt, pw, Y3, c2, dz3, das, a3s, a3T, dos, Z3, dcT,
                 cedge, cland, cacc, dedge, dland, dacc, bedge, bacc, halo_sems, bulk_sems,
                 *links):
    t = pl.program_id(0)
    peers = group_peers(plan)
    s, z, i, h = plan.place()
    Lp, C, H, wb, nw, cs, g = plan.Lp, plan.C, plan.H, plan.wb, plan.nw, plan.cs, plan.g
    M = wb * Lp
    steps = plan.steps
    p0, r0, b0, g0 = block_phases(plan)[:4]
    c_link, d_link, b_link = links[:3], links[3:6], links[6:]
    c_halo = Halo(plan, cedge, cland, halo_sems.at[0])
    d_halo = Halo(plan, dedge, dland, halo_sems.at[1])
    b_halo = Halo(plan, bedge, land, halo_sems.at[2])

    def bulk(off, rows):
        to = wrap(i + off, g)
        return remote(
            res.at[to, rows],
            res_got.at[off, rows],
            bulk_sems.at[0, off],
            bulk_sems.at[1, off],
            (s, h * g + to),
        )

    def result_of(block):
        y = mm(a3s[pl.ds(pl.multiple_of(block * M, 128), M)], pw_ref[h, 0])
        rowr = rows_of((Lp, y.shape[1]))
        for w in range(wb):
            at = block * wb + w
            valid = lens[i * plan.nw + at] - s * Lp
            r = x2half[w] + y[w * Lp : (w + 1) * Lp] + half_state[BIAS : BIAS + 1]
            r = jnp.where(rowr < valid, r, 0.0).astype(BF16).T
            for k in range(g):
                res[k, at] = r[k * cs : (k + 1) * cs]

    def send_result(block):
        result_of(block)
        for off in range(1, g):
            bulk(off, pl.ds(block * wb, wb)).start()

    @pl.when(first_step())
    def _():
        greet(peers.others)
        state[...] = old[...]
        cacc[...] = jnp.zeros_like(cacc)
        dacc[...] = jnp.zeros_like(dacc)
        bacc[...] = jnp.zeros_like(bacc)
        for c in range(2):
            cols = slice(c * (C // 2), (c + 1) * (C // 2))
            pw[:, cols] = pw_ref[c, 0]
            for k in range(plan.T2):
                at = k * C + c * (C // 2)
                wf[:, at : at + C // 2] = w_ref[c, k]
                wt[k * H : (k + 1) * H, cols] = w_ref[c, k]

    @pl.when(t < p0)
    def _():
        base = pl.multiple_of(t * M, 128)
        mean, rho = norm_of(state[ST2 : ST2 + 2], total_of(lens))
        scale = state[GAIN2 : GAIN2 + 1] * rho
        offset = state[SHIFT2 : SHIFT2 + 1] - mean * scale
        rows = rows_of((Lp, C))
        rowe = rows_of((EDGE, C))

        rowh = rows_of((Lp, H))
        sums0, sums1 = jnp.zeros((8, H), F32), jnp.zeros((8, H), F32)
        nh = min(2, wb)
        for first in range(0, wb, wb // nh):
            span = range(first, first + wb // nh)
            for w in span:
                valid = lens[i * plan.nw + t * wb + w] - s * Lp
                a = jnp.where(rows < valid, gelu(x2[w] * scale + offset), 0.0)
                al = gelu(x2land[0, w].astype(F32) * scale + offset)
                al = jnp.where((rowe - EDGE < valid) & (s > 0), al, 0.0)
                ah = gelu(x2land[1, w].astype(F32) * scale + offset)
                ah = jnp.where(rowe + Lp < valid, ah, 0.0)
                ext[w, 0:EDGE] = al
                ext[w, EDGE : EDGE + Lp] = a
                ext[w, EDGE + Lp :] = ah
                top, end = w * Lp, (w + 1) * Lp
                Y3[pl.ds(base + top, Lp), 0:C] = ext[w, EDGE - DIL : EDGE - DIL + Lp].astype(BF16)
                Y3[pl.ds(base + top, Lp), C : 2 * C] = a.astype(BF16)
                Y3[pl.ds(base + top, Lp), 2 * C : 3 * C] = ext[w, EDGE + DIL : EDGE + DIL + Lp].astype(BF16)
            y = mm_nt(Y3[pl.ds(base + first * Lp, wb // nh * Lp)], wf[...])
            for w in span:
                at = t * wb + w
                valid = lens[i * plan.nw + at] - s * Lp
                v = y[(w - first) * Lp : (w - first + 1) * Lp]
                c2[at] = v
                cedge[0, at] = v[:EDGE].astype(BF16)
                cedge[1, at] = v[Lp - EDGE :].astype(BF16)
                v = jnp.where(rowh < valid, v, 0.0)
                sums0 = sums0 + fold(v)
                sums1 = sums1 + fold(v * v)
        cacc[0:1, 0:H] += unfold(sums0)
        cacc[0:1, H:] += unfold(sums1)

    @pl.when(first_step())
    def _():
        meet(peers.others)

    @pl.when(t < p0)
    def _():
        c_halo.start(t * wb, wb)

    @pl.when(t == p0 - 1)
    def _():
        c_link[0][...] = cacc[...]
        peers.start(c_link)

    here_p = (t >= p0) & (t < p0 + steps)

    @pl.when(here_p)
    def _():
        u = t - p0
        rowc = rows_of((Lp, C))
        block = pl.ds(pl.multiple_of(u * M, 128), M)
        bias = jnp.zeros((8, C), F32)
        parts = []
        for w in range(wb):
            valid = lens[i * plan.nw + u * wb + w] - s * Lp
            d = jnp.where(rowc < valid, cot[w].astype(F32), 0.0)
            bias = bias + fold(d)
            parts.append(d.astype(BF16))
        d = jnp.concatenate(parts, axis=0)
        dos[block] = d
        das[...] = mm_nt(d, pw[...])
        dacc[1:2] += unfold(bias)

    @pl.when(t == p0)
    def _():
        got = peers.finish(c_link)
        state[ST3 : ST3 + 1, 0:H] = got[:, 0:H]
        state[ST3 + 1 : ST3 + 2, 0:H] = got[:, H:]

    @pl.when(here_p)
    def _():
        u = t - p0
        block = pl.ds(pl.multiple_of(u * M, 128), M)
        rowh = rows_of((Lp, H))
        mean, rho = norm_of(state[ST3 : ST3 + 2, 0:H], total_of(lens))
        scale = state[GAIN3 : GAIN3 + 1, 0:H] * rho
        offset = state[SHIFT3 : SHIFT3 + 1, 0:H] - mean * scale
        s0, s1 = jnp.zeros((8, H), F32), jnp.zeros((8, H), F32)
        parts = []
        for w in range(wb):
            at = u * wb + w
            valid = lens[i * plan.nw + at] - s * Lp
            top, end = w * Lp, (w + 1) * Lp
            v = c2[at]
            zv = v * scale + offset
            act, slope = gelu_both(zv)
            parts.append(jnp.where(rowh < valid, act, 0.0).astype(BF16))
            dzw = das[top:end] * slope
            dz3[at] = dzw
            dedge[0, at] = dzw[:EDGE].astype(BF16)
            dedge[1, at] = dzw[Lp - EDGE :].astype(BF16)
            s0 = s0 + fold(dzw)
            s1 = s1 + fold(dzw * zv)
        a3 = jnp.concatenate(parts, axis=0)
        a3s[block] = a3
        a3T[:, block] = a3.T
        dacc[0:1, 0:H] += unfold(s0)
        dacc[0:1, H : 2 * H] += unfold(s1)
        d_halo.start(u * wb, wb)

    @pl.when(t == p0)
    def _():
        send_result(0)

    @pl.when(t == p0 + steps - 1)
    def _():
        d_link[0][...] = dacc[...]
        peers.start(d_link)

    @pl.when((t >= r0) & (t < b0))
    def _():
        send_result(t - r0 + 1)

    @pl.when(t == b0 - 1)
    def _():
        rows = pl.ds(pl.multiple_of(h * plan.Hh, 16), plan.Hh)
        pgrad[...] = mm(a3T[rows], dos[...]).astype(BF16)

    @pl.when(t == b0)
    def _():
        got = peers.finish(d_link)
        shift = state[SHIFT3 : SHIFT3 + 1, 0:H]
        gain = state[GAIN3 : GAIN3 + 1, 0:H]
        state[SU3 : SU3 + 1, 0:H] = got[0:1, 0:H]
        state[SU3 + 1 : SU3 + 2, 0:H] = (got[0:1, H : 2 * H] - shift * got[0:1, 0:H]) / gain
        state[BSUM : BSUM + 1] = got[1:2]
        c_halo.finish()
        d_halo.finish()

    @pl.when((t >= b0) & (t < g0))
    def _():
        u = t - b0
        total = total_of(lens)
        mean3, rho3 = norm_of(state[ST3 : ST3 + 2, 0:H], total)
        gr3 = state[GAIN3 : GAIN3 + 1, 0:H] * rho3
        sg3 = state[SU3 : SU3 + 1, 0:H] / total
        gg3 = state[SU3 + 1 : SU3 + 2, 0:H] / total
        mean2, rho2 = norm_of(state[ST2 : ST2 + 2], total)
        scale2 = state[GAIN2 : GAIN2 + 1] * rho2
        offset2 = state[SHIFT2 : SHIFT2 + 1] - mean2 * scale2
        rowh = rows_of((Lp, H))
        rowe = rows_of((EDGE, H))
        rowc = rows_of((Lp, C))

        by_v = -gr3 * rho3 * gg3
        by_1 = gr3 * (mean3 * rho3 * gg3 - sg3)

        def back(dz, v):
            return gr3 * dz + by_v * v + by_1

        for w in range(wb):
            valid = lens[i * nw + u * wb + w] - s * Lp
            d = jnp.where(rowh < valid, back(dz3[u * wb + w], c2[u * wb + w]), 0.0)
            dl = back(dland[0, u * wb + w].astype(F32), cland[0, u * wb + w].astype(F32))
            dl = jnp.where((rowe - EDGE < valid) & (s > 0), dl, 0.0)
            dh = back(dland[1, u * wb + w].astype(F32), cland[1, u * wb + w].astype(F32))
            dh = jnp.where(rowe + Lp < valid, dh, 0.0)
            ext[w, 0:EDGE, 0:H] = dl
            ext[w, EDGE : EDGE + Lp, 0:H] = d
            ext[w, EDGE + Lp :, 0:H] = dh
            top, end = w * Lp, (w + 1) * Lp
            Z3[top:end, 0:H] = ext[w, EDGE + DIL : EDGE + DIL + Lp, 0:H].astype(BF16)
            Z3[top:end, H : 2 * H] = d.astype(BF16)
            Z3[top:end, 2 * H : 3 * H] = ext[w, EDGE - DIL : EDGE - DIL + Lp, 0:H].astype(BF16)

        y = mm(Z3[...], wt[...])

        M = wb * Lp
        dcT[:, pl.ds(pl.multiple_of(u * M, 128), M)] = Z3[:, H : 2 * H].T
        s0, s1 = jnp.zeros((8, C), F32), jnp.zeros((8, C), F32)
        for w in range(wb):
            at = u * wb + w
            valid = lens[i * nw + at] - s * Lp
            v = x2[w]
            zv = v * scale2 + offset2
            dzw = y[w * Lp : (w + 1) * Lp] * gelu_slope(zv)
            dzw = jnp.where(rowc < valid, dzw, 0.0)
            dz2[w] = dzw
            bedge[0, pl.ds(at, 1)] = dzw[0:1]
            bedge[1, pl.ds(at, 1)] = dzw[Lp - 1 : Lp]
            s0 = s0 + fold(dzw)
            s1 = s1 + fold(dzw * zv)
        bacc[0:1] += unfold(s0)
        bacc[1:2] += unfold(s1)

    @pl.when(t == g0 - 1)
    def _():
        b_link[0][...] = bacc[...]
        peers.start(b_link)
        b_halo.start(0, nw)

    @pl.when(t >= g0)
    def _():
        rows = pl.ds(pl.multiple_of(h * plan.Hh, 16), plan.Hh)
        cols = pl.ds(pl.multiple_of((t - g0) * C, 128), C)
        grads[...] = mm(dcT[rows], Y3[:, cols]).astype(BF16)

    @pl.when(last_step())
    def _():
        got = peers.finish(b_link)
        shift, gain = state[SHIFT2 : SHIFT2 + 1], state[GAIN2 : GAIN2 + 1]
        state[SU2 : SU2 + 1] = got[0:1]
        state[SU2 + 1 : SU2 + 2] = (got[1:2] - shift * got[0:1]) / gain
        b_halo.finish()
        for off in range(1, g):
            bulk(off, pl.ds(0, nw)).wait()


def block_phases(plan):
    n = plan.steps
    return n, 2 * n, 3 * n - 1, 4 * n - 1, 4 * n - 1 + plan.T2


class Reduction:
    def __init__(self, plan, batches, out, give, mine, got, spread, half, mate, sems):
        self.plan, self.batches, self.out = plan, batches, out
        self.give, self.mine, self.got, self.spread = give, mine, got, spread
        self.half, self.mate = half, mate
        self.sems = sems
        self.s, self.z, self.i, self.h = plan.place()
        self.c = lax.rem(self.s, 2)
        self.m = lax.div(self.s, 2)
        self.chips = plan.chips

    @staticmethod
    def scratch(plan, batches):
        taps, wide = plan.T1 + 2, plan.C // 2
        full = (taps, plan.chips, plan.g, plan.rb, wide)
        part = (taps, plan.g, plan.rb, wide)
        return [
            pltpu.VMEM((taps, 2, plan.chips, plan.rb, wide), BF16),
            *[pltpu.VMEM(full, BF16)] * 4,
            *[pltpu.VMEM(part, BF16)] * 2,
            pltpu.SemaphoreType.DMA((2, len(batches), 5)),
        ]

    def copy(self, b, phase, src, dst, device):
        return remote(src, dst, self.sems.at[0, b, phase], self.sems.at[1, b, phase], device)

    def finish(self, b, phase, ref, device):
        done = self.copy(b, phase, ref, ref, device)
        done.wait_recv()
        done.wait_send()

    def taps(self, b):
        return pl.ds(*self.batches[b])

    def pair(self):
        return (2 * self.m + (1 - self.c), self.z)

    def far(self, off):
        return (2 * wrap(self.m + off, self.chips) + self.c, self.z)

    def member(self, off):
        return (self.s, self.h * self.plan.g + wrap(self.i + off, self.plan.g))

    def put(self, k, rows):
        wide = self.plan.C // 2
        for j in range(self.plan.g):
            for m in range(self.chips):
                v = rows(j, m)
                left, right = v[:, :wide], v[:, wide:]
                self.mine[k, m, j] = jnp.where(self.c == 0, left, right).astype(BF16)
                self.give[k, m, j] = jnp.where(self.c == 0, right, left).astype(BF16)

    def step0(self, b):
        taps = self.taps(b)
        self.copy(b, 0, self.give.at[taps], self.got.at[taps], self.pair()).start()

    def step1(self, b):
        taps = self.taps(b)
        self.finish(b, 0, self.got.at[taps], self.pair())
        first, count = self.batches[b]
        for k in range(first, first + count):
            v = self.mine[k].astype(F32) + self.got[k].astype(F32)
            self.mine[k] = v.astype(BF16)
        for off in range(1, self.chips):
            src = self.mine.at[taps, wrap(self.m + off, self.chips)]
            self.copy(b, 1, src, self.spread.at[taps, self.m], self.far(off)).start()

    def step2(self, b):
        taps = self.taps(b)
        self.finish(b, 1, self.spread.at[taps, pl.ds(0, self.chips - 1)], self.far(1))
        first, count = self.batches[b]
        for k in range(first, first + count):
            self.spread[k, self.m] = self.mine[k, self.m]
            v = self.spread[k, 0].astype(F32)
            for n in range(1, self.chips):
                v = v + self.spread[k, n].astype(F32)
            self.half[k] = v.astype(BF16)
        for off in range(1, self.plan.g):
            src = self.half.at[taps, wrap(self.i + off, self.plan.g)]
            self.copy(b, 2, src, self.mate.at[taps, off], self.member(off)).start()

    def step3(self, b):
        taps = self.taps(b)
        self.finish(b, 2, self.mate.at[taps, pl.ds(1, self.plan.g - 1)], self.member(1))
        first, count = self.batches[b]
        for k in range(first, first + count):
            v = self.half[k, self.i].astype(F32)
            for off in range(1, self.plan.g):
                v = v + self.mate[k, off].astype(F32)
            self.out[k, self.c, self.m] = v.astype(BF16)
        mine = self.out.at[taps, self.c, self.m]
        for off in range(1, self.chips):
            self.copy(b, 3, mine, mine, self.far(off)).start()

    def step4(self, b):
        taps = self.taps(b)
        self.finish(b, 3, self.out.at[taps, self.c, pl.ds(0, self.chips - 1)], self.far(1))
        mine = self.out.at[taps, self.c]
        self.copy(b, 4, mine, mine, self.pair()).start()

    def step5(self, b):
        self.finish(b, 4, self.out.at[self.taps(b), self.c], self.pair())


def tail_turns(plan):
    nD = plan.steps
    first = max(nD - 1, 1)
    turns = [("x", n) for n in range(first)] + [("d", n) for n in range(first, nD)]
    turns += [("w", n) for n in range(plan.T1)]
    return turns + [("x", n) for n in range(first, nD)]


def tail_batches(plan):
    return [(plan.T1, 2), (0, 2), (2, 2), (4, plan.T1 - 4)]


def tail_kernel(plan, lens, dz2, dzland, x2, x2land, cot, beyond, x, X5_hbm, taps_hbm, grads, pgrad,
                old, half_state,
                gz, gz_got, sums, summed,
                ext, D3, D0T, wcat, pick, eye, cols, y, part, split, acc, X5, X5_sems,
                taps, bulk_sems, *rest):
    t = pl.program_id(0)
    s, z, i, h = plan.place()
    L, Lp, C, wb, g, nw = plan.L, plan.Lp, plan.C, plan.wb, plan.g, plan.nw
    Ch, cs, T1 = plan.Ch, plan.cs, plan.T1
    M = wb * Lp
    nD = plan.steps
    turns = tail_turns(plan)
    last = len(turns) - 1
    peers = group_peers(plan)
    red = Reduction(plan, tail_batches(plan), *rest[:8])
    link = rest[8:]

    def member(off):
        return (s, h * g + wrap(i + off, g))

    def send(first, count):
        rows = pl.ds(first, count)
        for off in range(1, g):
            remote(
                part.at[off - 1, rows],
                gz_got.at[off, rows],
                bulk_sems.at[0, off],
                bulk_sems.at[1, off],
                member(off),
            ).start()

    def X5_copy(k):
        return pltpu.make_async_copy(X5_hbm.at[k], X5.at[k % 2], X5_sems.at[k % 2])

    def when(at):
        return pl.when(t == min(at, last))

    def turn(kind, k):
        return turns.index((kind, k)) if (kind, k) in turns else last

    def turn_of(kind):
        index = jnp.int32(0)
        here = False
        for n, (what, k) in enumerate(turns):
            if what == kind:
                index = jnp.where(t == n, k, index)
                here = (t == n) | here
        return here, index

    taps_copy = pltpu.make_async_copy(
        taps_hbm.at[:, pl.ds(pl.multiple_of(h * Ch, 128), Ch)], taps, X5_sems.at[2]
    )

    @when(0)
    def _():
        taps_copy.start()
        greet(peers.others)
        acc[...] = jnp.zeros_like(acc)
        pick[...] = pick_matrix(L)
        eye[...] = eye_matrix(Ch, Ch, 0)
        mean, rho = norm_of(half_state[ST1 : ST1 + 2], 2.0 * total_of(lens))
        scale = half_state[GAIN1 : GAIN1 + 1] * rho
        offset = half_state[SHIFT1 : SHIFT1 + 1] - mean * scale
        for k, row in enumerate((scale, offset)):
            cols[k] = column(row, L)

    @pl.when(t < nD)
    def _():
        total = total_of(lens)
        mean, rho = norm_of(old[ST2 : ST2 + 2], total)
        gr = old[GAIN2 : GAIN2 + 1] * rho
        sg = old[SU2 : SU2 + 1] / total
        gg = old[SU2 + 1 : SU2 + 2] / total
        rowc = rows_of((Lp, C))
        row1 = rows_of((1, C))

        by_dz = 0.5 * gr
        by_v = -0.5 * gr * rho * gg
        by_1 = 0.5 * gr * (mean * rho * gg - sg)

        def back(dout, dz, v):
            return 0.5 * dout + by_dz * dz + by_v * v + by_1

        def grad_of(w):
            at = t * wb + w
            valid = lens[i * nw + at] - s * Lp
            d = back(cot[w].astype(F32), dz2[w], x2[w])
            d = jnp.where(rowc < valid, d, 0.0)
            one = pl.ds(at, 1)
            dl = back(beyond[0, 2, one, :], dzland[0, one, :], x2land[0, w, EDGE - 1 : EDGE].astype(F32))
            dl = jnp.where((row1 - 1 < valid) & (s > 0), dl, 0.0)
            dh = back(beyond[1, 2, one, :], dzland[1, one, :], x2land[1, w, 0:1].astype(F32))
            dh = jnp.where(row1 + Lp < valid, dh, 0.0)
            ext[w, 7:8] = dl
            ext[w, 8 : 8 + Lp] = d
            ext[w, 8 + Lp : 9 + Lp] = dh
            top, end = w * Lp, (w + 1) * Lp
            D3[t, top:end, 0:C] = ext[w, 9 : 9 + Lp].astype(BF16)
            D3[t, top:end, C : 2 * C] = d.astype(BF16)
            D3[t, top:end, 2 * C : 3 * C] = ext[w, 7 : 7 + Lp].astype(BF16)

        for w in range(wb):
            grad_of(w)
        half = D3[t, :, pl.ds(pl.multiple_of(C + h * Ch, 128), Ch)]
        D0T[:, pl.ds(pl.multiple_of(t * M, 128), M)] = half.T

    @when(0)
    def _():
        taps_copy.wait()
        for first in range(0, Ch, 64):
            rows = slice(first, min(first + 64, Ch))
            for r, parts in enumerate((((0,), (1, 2), (3, 4)), ((0, 1), (2, 3), (4,)))):
                for k, which in enumerate(parts):
                    v = taps[which[0], rows]
                    if len(which) > 1:
                        v = (v.astype(F32) + taps[which[1], rows].astype(F32)).astype(BF16)
                    at = r * Ch
                    wcat[at + rows.start : at + rows.stop, k * C : (k + 1) * C] = v
        meet(peers.others)

    here_x, bx = turn_of("x")

    def gradient(hf, nh):
        lanes = lanes_of((Ch, L))

        def through(w):
            valid = 2 * lens[i * nw + bx * wb + w] - s * L
            top, end = w * Lp, (w + 1) * Lp
            v = mm_nt(eye[...], x[w])
            da = jnp.concatenate([y[0:Ch, top:end], y[Ch:, top:end]], axis=1)
            da = mm(da.astype(BF16), pick[...])
            zv = v * cols[0] + cols[1]
            dzw = da * gelu_slope(zv)
            dzw = jnp.where(lanes < valid, dzw, 0.0)
            acc[0] += fold_lanes(dzw)
            acc[1] += fold_lanes(dzw * zv)
            split[w % 2] = dzw.astype(BF16)
            for off in range(g):
                rows = pl.ds(pl.multiple_of(lax.rem(i + off, g) * cs, 16), cs)
                if off == 0:
                    gz[w] = split[w % 2, rows]
                else:
                    part[off - 1, bx * wb + w] = split[w % 2, rows]

        n = wb // nh
        rows = slice(hf * n * Lp, (hf + 1) * n * Lp)
        y[:, rows] = mm_nt(wcat[...], D3[bx, rows])
        for w in range(hf * n, (hf + 1) * n):
            through(w)

    nh = 2 if wb % 2 == 0 and wb * Lp // 2 % 128 == 0 else 1

    @pl.when(here_x)
    def _():
        gradient(0, nh)
        send(bx * wb, wb // nh)

    for step, batch in ((red.step1, 3), (red.step2, 1)):

        @when(last)
        def _():
            if nh == 2 and turns[last][0] == "x":
                step(batch)

    if nh == 2:

        @pl.when(here_x)
        def _():
            gradient(1, nh)

    @pl.when(here_x & (bx < nD - 1))
    def _():
        if nh == 2:
            send(bx * wb + wb // nh, wb // nh)

    @when(0)
    def _():
        hs = plan.H // plan.nz
        rb = plan.rb
        for u in range(2):

            def rows(j, m, u=u):
                side, r = m * rb // hs, m * rb % hs
                n = 2 * side + u
                rows = slice(j * hs + r, j * hs + r + rb)
                v = grads[rows, n * C : (n + 1) * C] if n < plan.T2 else pgrad[rows]
                return v.astype(F32)

            red.put(T1 + u, rows)
        red.step0(0)

    @when(1)
    def _():
        X5_copy(0).start()
        X5_copy(1).start()

    here_w, k = turn_of("w")

    @pl.when(here_w)
    def _():
        X5_copy(k).wait()
        y[0:Ch, 0:C] = mm(D0T[...], X5[lax.rem(k, 2)])

        @pl.when(k < T1 - 2)
        def _():
            X5_copy(k + 2).start()

        rb = plan.rb
        red.put(k, lambda j, m: y[j * cs + m * rb : j * cs + (m + 1) * rb, 0:C])

    @when(turn("x", nD - 1))
    def _():
        packet = link[0]
        packet[...] = jnp.zeros_like(packet)
        packet[0:1, 0:Ch] = jnp.sum(acc[0].T, axis=0, keepdims=True)
        packet[1:2, 0:Ch] = jnp.sum(acc[1].T, axis=0, keepdims=True)
        peers.start(link)

    for at, step, batch in (
        (1, red.step1, 0),
        (max(nD - 1, 2), red.step2, 0),
        (turn("w", 1), red.step0, 1),
        (turn("w", 3), red.step1, 1),
        (turn("w", 3), red.step0, 2),
        (turn("w", 4), red.step0, 3),
        (turn("w", 4), red.step1, 2),
        *(() if nh == 2 and turns[last][0] == "x" else ((last, red.step1, 3), (last, red.step2, 1))),
        (last, red.step2, 2),
        (last, red.step3, 0),
        (last, red.step3, 1),
        (last, red.step2, 3),
    ):

        @when(at)
        def _():
            step(batch)

    @when(last)
    def _():
        if nh == 2:
            send(nw - wb // 2, wb // 2)

    @when(last)
    def _():
        red.step3(2)
        red.step4(0)
        red.step4(1)
        red.step3(3)
        red.step4(2)
        got = peers.finish(link)[:, 0:Ch]
        shift, gain = half_state[SHIFT1 : SHIFT1 + 1], half_state[GAIN1 : GAIN1 + 1]
        sums[0:1] = got[0:1]
        sums[1:2] = (got[1:2] - shift * got[0:1]) / gain
        red.step4(3)
        for b in range(4):
            red.step5(b)
        own = pltpu.make_async_copy(red.out, summed, X5_sems.at[0])
        own.start()
        for off in range(1, g):
            done = remote(
                part.at[off - 1],
                gz_got.at[off],
                bulk_sems.at[0, off],
                bulk_sems.at[1, off],
                member(off),
            )
            done.wait_recv()
            done.wait_send()
        own.wait()


def input_grad_kernel(plan, wg, lens, x, gz, gz_got, sums, res, res_got, summed,
                      state, half_state,
                      out, out_result, conv_grad, dil_grad, point_grad,
                      g1, b1, g2, b2, g3, b3, pb, eye, cols, xt):
    t = pl.program_id(0)
    s, z, i, h = plan.place()
    L, Ch, cs = plan.L, plan.Ch, plan.cs
    turn = plan.nw // wg
    mine = pl.ds(pl.multiple_of(i * cs, 16), cs)

    @pl.when(first_step())
    def _():
        n = 2.0 * total_of(lens)
        mean, rho = norm_of(half_state[ST1 : ST1 + 2], n)
        gr = half_state[GAIN1 : GAIN1 + 1] * rho
        gg = sums[1:2] / n * rho
        for k, row in enumerate((gr, -gr * gg, gr * (mean * gg - sums[0:1] / n))):
            xt[...] = column(row, L)
            cols[k] = xt[mine]
        eye[...] = eye_matrix(cs, Ch, i * cs)

        def mine_of(src, at, which, count, *dsts):
            n = dsts[0].shape[1]
            for k in range(count):

                @pl.when(which == k)
                def _():
                    for dst, r in zip(dsts, at):
                        dst[...] = src[r : r + 1, k * n : (k + 1) * n]

        mine_of(sums, (1, 0), i, plan.g, g1, b1)
        mine_of(state, (SU2 + 1, SU2), z, plan.nz, g2, b2)
        mine_of(state, (SU3 + 1, SU3), z, plan.nz, g3, b3)
        mine_of(state, (BSUM,), z, plan.nz, pb)

    own = lax.div(t, turn) == i
    for w in range(wg):
        out_result[w] = jnp.where(own, res[0, w], res_got[0, w])

    C, T1, hs, rb, wide = plan.C, plan.T1, plan.H // plan.nz, plan.rb, plan.C // 2
    count = plan.NW // wg
    turns = min(count, plan.chips)
    per, every = plan.chips // turns, count // turns

    def spread(chunk):
        for n in range(per):
            m = chunk * per + n
            side, r = m * rb // hs, m * rb % hs
            for c in range(2):
                at = slice(c * wide, (c + 1) * wide)
                for k in range(T1):
                    conv_grad[k, n * rb : (n + 1) * rb, at] = summed[k, c, n].astype(F32)
                for u in range(2):
                    v = summed[T1 + u, c, n].astype(F32)
                    if 2 * side + u < plan.T2:
                        dil_grad[2 * side + u, r : r + rb, at] = v
                    else:
                        point_grad[r : r + rb, at] = v

    for chunk in range(turns):
        pl.when(t == chunk * every)(partial(spread, chunk))

    lanes = lanes_of((cs, L))
    for w in range(wg):
        valid = 2 * lens[t * wg + w] - s * L
        v = mm_nt(eye[...], x[w])
        dz = jnp.where(own, gz[w], gz_got[0, w]).astype(F32)
        r = cols[0] * dz + v * cols[1] + cols[2]
        out[w] = jnp.where(lanes < valid, r, 0.0).astype(BF16)


def call(kernel, plan, name, steps, ins, outs, scratch, flops, nbytes, cid=None):
    extra = {} if cid is None else dict(collective_id=cid, has_side_effects=True)
    return pl.pallas_call(
        partial(kernel, plan),
        grid=(steps,),
        in_specs=[SMEM] + [spec for spec, _ in ins],
        out_specs=[spec for spec, _, _ in outs],
        out_shape=[jax.ShapeDtypeStruct(shape, dtype) for _, shape, dtype in outs],
        scratch_shapes=scratch,
        compiler_params=pltpu.CompilerParams(vmem_limit_bytes=VMEM_LIMIT, **extra),
        cost_estimate=pl.CostEstimate(
            flops=int(flops), bytes_accessed=int(nbytes), transcendentals=0
        ),
        name=name,
    )


def per_device(
    inputs,
    lengths,
    input_gain,
    input_shift,
    conv_weight,
    branch_gain,
    branch_shift,
    dilated_tap_weight,
    mixer_gain,
    mixer_shift,
    point_weight,
    point_bias,
    cotangent,
):
    NW, L, C = inputs.shape
    Lp = L // 2
    nz = lax.axis_size("ch")
    R = 2
    plan = Plan(
        ns=lax.axis_size("seq"),
        nz=nz,
        R=R,
        NW=NW,
        L=L,
        C=C,
        H=mixer_gain.shape[0] * nz,
        T1=conv_weight.shape[0],
        T2=dilated_tap_weight.shape[0],
        wb=min(NW * R // nz, max(1, 512 // Lp)),
    )
    g, nw, cs, Ch, H, Hh, wb = plan.g, plan.nw, plan.cs, plan.Ch, plan.H, plan.Hh, plan.wb
    T1, T2, steps = plan.T1, plan.T2, plan.steps
    M = wb * Lp
    hs = H // nz
    lens = lengths.astype(jnp.int32)

    def row(a):
        return a.reshape(1, a.shape[0])

    def grp():
        return lax.rem(lax.axis_index("ch"), g)

    def half():
        return lax.div(lax.axis_index("ch"), g)

    def core():
        return lax.rem(lax.axis_index("seq"), 2)

    def chip4():
        return lax.div(lax.axis_index("seq"), plan.ns // 4)

    def whole(*shape):
        return pl.BlockSpec(shape, lambda t: (0,) * len(shape), pipeline_mode=pl.Buffered(1))

    def const(*shape):
        return pl.BlockSpec(shape, lambda t: (0,) * len(shape))

    def win(*shape):
        return pl.BlockSpec(shape, lambda t: (t,) + (0,) * (len(shape) - 1))

    def arg_win(n, width):
        return pl.BlockSpec((wb, n, width), lambda t: (grp() * steps + t, 0, 0))

    def ins(*pairs):
        return [p for p in pairs]

    share = NW // nz
    nm = max(1, share // wb)

    def edge_spec(n):
        return pl.BlockSpec(
            (nw, 16, C), lambda t: (grp(), n, 0), pipeline_mode=pl.Buffered(1)
        )

    def head_block(t):
        own = lax.div(lax.axis_index("ch") * share, wb) + t
        return jnp.where(t < nm, own, grp() * steps + t - nm), 0, 0

    def after(*shape):
        return pl.BlockSpec(
            shape, lambda t: (jnp.maximum(t - nm, 0),) + (0,) * (len(shape) - 1)
        )

    pairs = ins(
        (pl.BlockSpec((wb, L, C), head_block), inputs),
        (edge_spec(0), inputs),
        (edge_spec(L // 16 - 1), inputs),
        (edge_spec(0), cotangent),
        (edge_spec(Lp // 16 - 1), cotangent),
        (whole(1, cs), row(branch_gain)),
        (whole(1, cs), row(branch_shift)),
        (whole(1, cs), row(point_bias)),
        (whole(1, H // nz), row(mixer_gain)),
        (whole(1, H // nz), row(mixer_shift)),
        (ANY, conv_weight.reshape(T1 * C, C)),
        (whole(C), input_gain),
        (whole(C), input_shift),
        (
            pl.BlockSpec(
                (1, hs, C // 2),
                lambda t: (jnp.minimum(chip4(), T2 - 1), 0, core()),
                pipeline_mode=pl.Buffered(1),
            ),
            jnp.swapaxes(dilated_tap_weight, 1, 2),
        ),
        (
            pl.BlockSpec(
                (hs, C // 2), lambda t: (0, core()), pipeline_mode=pl.Buffered(1)
            ),
            point_weight,
        ),
    )
    plane, line, group = plane_peers(plan), line_peers(plan), group_peers(plan)
    state_shape = (STATE, C)
    edges2, edges3 = (2, nw, EDGE, C), (2, nw, EDGE, H)
    X5, x2, land2, state, beyond, full = call(
        lambda plan, *refs: head_kernel(plan, nm, *refs),
        plan,
        "head",
        nm + steps,
        pairs,
        [
            (
                pl.BlockSpec((T1, M, C), lambda t: (0, jnp.maximum(t - nm, 0), 0)),
                (T1, nw * Lp, C),
                BF16,
            ),
            (after(wb, Lp, C), (nw, Lp, C), F32),
            (ANY, edges2, BF16),
            (const(*state_shape), state_shape, F32),
            (const(2, 3, nw, C), (2, 3, nw, C), F32),
            (ANY, (2, T2 + 1, nz, hs, C // 2), BF16),
        ],
        [
            pltpu.VMEM((2, 8, C), F32),
            pltpu.VMEM((2, 3, nw, C), F32),
            pltpu.VMEM((2, 3, nw, C), F32),
            pltpu.VMEM((T1 * Lp, L), BF16),
            pltpu.VMEM(edges2, BF16),
            pltpu.VMEM((2, C), F32),
            pltpu.VMEM((T1 * C, C), BF16),
            pltpu.SemaphoreType.DMA,
            pltpu.VMEM((hs, C // 2), BF16),
            pltpu.SemaphoreType.DMA((2, 4)),
            HALO_SEMS,
            HALO_SEMS,
        ]
        + plane.scratch(2, C)
        + line.scratch(3, C)
        + group.scratch(2, C),
        2 * nw * Lp * T1 * C * C,
        nw * Lp * C * 20,
        cid=1,
    )(lens, *[a for _, a in pairs])

    full = full.reshape(2, T2 + 1, H, C // 2)
    taps_spec = whole(2, T2, H, C // 2)
    pw_spec = pl.BlockSpec(
        (2, 1, H, C // 2), lambda t: (0, T2, 0, 0), pipeline_mode=pl.Buffered(1)
    )

    def early(*shape):
        return pl.BlockSpec(
            shape, lambda t: (jnp.minimum(t, steps - 1),) + (0,) * (len(shape) - 1)
        )

    def early_land(width):
        return pl.BlockSpec(
            (2, wb, EDGE, width), lambda t: (0, jnp.minimum(t, steps - 1), 0, 0)
        )

    def half_of(n):
        return pl.BlockSpec((n, Ch), lambda t: (0, half()), pipeline_mode=pl.Buffered(1))

    cot_spec = pl.BlockSpec(
        (wb, Lp, C), lambda t: (grp() * steps + jnp.minimum(t, steps - 1), 0, 0)
    )

    p0, r0, b0, g0, block_steps = block_phases(plan)

    def at_phase(first):
        return lambda t: jnp.clip(t - first, 0, steps - 1)

    in_p, in_b = at_phase(p0), at_phase(b0)
    pairs = ins(
        (
            pl.BlockSpec(
                (wb, Lp, C),
                lambda t: (jnp.where(t < p0 + steps, jnp.minimum(t, steps - 1), in_b(t)), 0, 0),
            ),
            x2,
        ),
        (
            pl.BlockSpec(
                (wb, Lp, Ch),
                lambda t: (jnp.clip(t - r0 + 1, 0, steps - 1), 0, half()),
            ),
            x2,
        ),
        (early_land(C), land2),
        (pl.BlockSpec((wb, Lp, C), lambda t: (grp() * steps + in_p(t), 0, 0)), cotangent),
        (taps_spec, full),
        (pw_spec, full),
        (whole(*state_shape), state),
        (half_of(STATE), state),
    )
    dz2, grads, pgrad, res, dland2, state, res_got = call(
        block_kernel,
        plan,
        "block",
        block_steps,
        pairs,
        [
            (pl.BlockSpec((wb, Lp, C), lambda t: (in_b(t), 0, 0)), (nw, Lp, C), F32),
            (
                pl.BlockSpec((Hh, C), lambda t: (0, jnp.maximum(t - g0, 0))),
                (Hh, T2 * C),
                BF16,
            ),
            (const(Hh, C), (Hh, C), BF16),
            (const(g, nw, cs, Lp), (g, nw, cs, Lp), BF16),
            (ANY, (2, nw, C), F32),
            (const(*state_shape), state_shape, F32),
            (ANY, (g, nw, cs, Lp), BF16),
        ],
        [
            pltpu.VMEM((wb, Lp + 2 * EDGE, C), F32),
            pltpu.VMEM((H, T2 * C), BF16),
            pltpu.VMEM((T2 * H, C), BF16),
            pltpu.VMEM((H, C), BF16),
            pltpu.VMEM((nw * Lp, T2 * C), BF16),
            pltpu.VMEM((nw, Lp, H), F32),
            pltpu.VMEM((nw, Lp, H), F32),
            pltpu.VMEM((M, H), F32),
            pltpu.VMEM((nw * Lp, H), BF16),
            pltpu.VMEM((H, nw * Lp), BF16),
            pltpu.VMEM((nw * Lp, C), BF16),
            pltpu.VMEM((M, T2 * H), BF16),
            pltpu.VMEM((H, nw * Lp), BF16),
            pltpu.VMEM(edges3, BF16),
            pltpu.VMEM(edges3, BF16),
            pltpu.VMEM((1, 2 * H), F32),
            pltpu.VMEM(edges3, BF16),
            pltpu.VMEM(edges3, BF16),
            pltpu.VMEM((2, C), F32),
            pltpu.VMEM((2, nw, C), F32),
            pltpu.VMEM((2, C), F32),
            pltpu.SemaphoreType.DMA((3, 2, 2)),
            pltpu.SemaphoreType.DMA((2, g)),
        ]
        + group.scratch(1, 2 * H)
        + group.scratch(2, C)
        + group.scratch(2, C),
        nw * Lp * C * H * (6 * T2 + 6),
        nw * Lp * C * 30,
        cid=3,
    )(lens, *[a for _, a in pairs])

    chips, rb = plan.chips, plan.rb
    turns_t = tail_turns(plan)

    def x_block(t):
        block = jnp.int32(0)
        for n, (what, k) in enumerate(turns_t):
            if what == "x":
                block = jnp.where(t >= n, k, block)
        return block

    sshape = (T1 + 2, 2, chips, rb, C // 2)
    pairs = ins(
        (early(wb, Lp, C), dz2),
        (whole(2, nw, C), dland2),
        (early(wb, Lp, C), x2),
        (early_land(C), land2),
        (cot_spec, cotangent),
        (whole(2, 3, nw, C), beyond),
        (
            pl.BlockSpec(
                (wb, L, Ch), lambda t: (grp() * steps + x_block(t), 0, half())
            ),
            inputs,
        ),
        (ANY, X5),
        (ANY, conv_weight),
        (whole(Hh, T2 * C), grads),
        (whole(Hh, C), pgrad),
        (whole(*state_shape), state),
        (half_of(STATE), state),
    )
    gz, gz_got, sums1, summed = call(
        tail_kernel,
        plan,
        "tail",
        len(turns_t),
        pairs,
        [
            (pl.BlockSpec((wb, cs, L), lambda t: (x_block(t), 0, 0)), (nw, cs, L), BF16),
            (ANY, (g, nw, cs, L), BF16),
            (const(2, Ch), (2, Ch), F32),
            (ANY, sshape, BF16),
        ],
        [
            pltpu.VMEM((wb, Lp + 16, C), F32),
            pltpu.VMEM((steps, M, 3 * C), BF16),
            pltpu.VMEM((Ch, nw * Lp), BF16),
            pltpu.VMEM((2 * Ch, 3 * C), BF16),
            pltpu.VMEM((L, L), BF16),
            pltpu.VMEM((Ch, Ch), BF16),
            pltpu.VMEM((2, Ch, L), F32),
            pltpu.VMEM((2 * Ch, max(M, C)), F32),
            pltpu.VMEM((g - 1, nw, cs, L), BF16),
            pltpu.VMEM((2, Ch, L), BF16),
            pltpu.VMEM((2, Ch, min(L, 128)), F32),
            pltpu.VMEM((2, nw * Lp, C), BF16),
            pltpu.SemaphoreType.DMA((3,)),
            pltpu.VMEM((T1, Ch, C), BF16),
            pltpu.SemaphoreType.DMA((2, g)),
        ]
        + Reduction.scratch(plan, tail_batches(plan))
        + group.scratch(2, C),
        2 * nw * Lp * (6 + T1) * C * Ch,
        nw * Lp * C * 40,
        cid=6,
    )(lens, *[a for _, a in pairs])

    wg = min(2 * wb, nw)
    count = NW // wg
    turn = nw // wg
    turns = min(count, chips)

    def own_block(t):
        return jnp.where(lax.div(t, turn) == grp(), lax.rem(t, turn), 0)

    def got_slot(t):
        off = lax.rem(grp() - lax.div(t, turn) + g, g)
        return jnp.maximum(off, 1), jnp.where(off > 0, lax.rem(t, turn), 0)

    pairs = ins(
        (pl.BlockSpec((wg, L, Ch), lambda t: (t, 0, half())), inputs),
        (pl.BlockSpec((wg, cs, L), lambda t: (own_block(t), 0, 0)), gz),
        (pl.BlockSpec((1, wg, cs, L), lambda t: got_slot(t) + (0, 0)), gz_got),
        (whole(2, Ch), sums1),
        (pl.BlockSpec((1, wg, cs, Lp), lambda t: (grp(), own_block(t), 0, 0)), res),
        (pl.BlockSpec((1, wg, cs, Lp), lambda t: got_slot(t) + (0, 0)), res_got),
        (
            pl.BlockSpec(
                (T1 + 2, 2, chips // turns, rb, C // 2),
                lambda t: (0, 0, t * turns // count, 0, 0),
            ),
            summed,
        ),
        (whole(*state_shape), state),
        (half_of(STATE), state),
    )
    outs = call(
        lambda plan, *refs: input_grad_kernel(plan, wg, *refs),
        plan,
        "input_grad",
        count,
        pairs,
        [
            (win(wg, cs, L), (NW, cs, L), BF16),
            (win(wg, cs, Lp), (NW, cs, Lp), BF16),
            (
                pl.BlockSpec((T1, cs // turns, C), lambda t: (0, t * turns // count, 0)),
                (T1, cs, C),
                F32,
            ),
            (const(T2, hs, C), (T2, hs, C), F32),
            (const(hs, C), (hs, C), F32),
        ]
        + [(const(1, n), (1, n), F32) for n in (cs, cs, cs, cs, hs, hs, cs)],
        [
            pltpu.VMEM((cs, Ch), BF16),
            pltpu.VMEM((3, cs, L), F32),
            pltpu.VMEM((Ch, L), F32),
        ],
        2 * NW * L * Ch * cs,
        NW * L * cs * 8,
    )(lens, *[a for _, a in pairs])
    grad, result, conv_grad, dil_grad, point_grad = outs[:5]
    g1, b1, g2, b2, g3, b3, pb = [a[0] for a in outs[5:]]
    return (
        jnp.swapaxes(result, 1, 2),
        jnp.swapaxes(grad, 1, 2),
        jnp.swapaxes(conv_grad, 1, 2),
        g1,
        b1,
        g2,
        b2,
        jnp.swapaxes(dil_grad, 1, 2),
        g3,
        b3,
        point_grad,
        pb,
    )


def solution(mesh):
    in_specs = (
        P(None, "seq", None),
        P(),
        P(),
        P(),
        P(),
        P("ch"),
        P("ch"),
        P(None, None, "ch"),
        P("ch"),
        P("ch"),
        P("ch", None),
        P("ch"),
        P(None, "seq", None),
    )
    out_specs = (
        P(None, "seq", "ch"),
        P(None, "seq", "ch"),
        P(None, None, "ch"),
        P("ch"),
        P("ch"),
        P("ch"),
        P("ch"),
        P(None, None, "ch"),
        P("ch"),
        P("ch"),
        P("ch", None),
        P("ch"),
    )
    return jax.shard_map(
        per_device, mesh=mesh, in_specs=in_specs, out_specs=out_specs, check_vma=False
    )
```

```python
from functools import partial
from typing import NamedTuple

import jax
import jax.numpy as jnp
from jax import lax
from jax.experimental import pallas as pl
from jax.experimental.pallas import tpu as pltpu
from jax.sharding import PartitionSpec as P

DIL = 14
EDGE = 16
EPS = 1e-05
GC0 = 0.7978845608028654
GC1 = 0.044715
F32 = jnp.float32
BF16 = jnp.bfloat16
MESH = pl.DeviceIdType.MESH
VMEM_LIMIT = 58 * 1024 * 1024
ANY = pl.BlockSpec(memory_space=pl.ANY)
SMEM = pl.BlockSpec(memory_space=pltpu.SMEM)


ST1, GAIN2, SHIFT2, BIAS, GAIN3, SHIFT3, GAIN1, SHIFT1, ST2, ST3, SU3, BSUM, SU2 = (
    0, 2, 3, 4, 5, 6, 7, 8, 9, 11, 13, 15, 16
)
STATE = 24


class Plan(NamedTuple):
    ns: int
    nz: int
    R: int
    NW: int
    L: int
    C: int
    H: int
    T1: int
    T2: int
    wb: int

    @property
    def g(self):
        return self.nz // self.R

    @property
    def nw(self):
        return self.NW // self.g

    @property
    def Lp(self):
        return self.L // 2

    @property
    def cs(self):
        return self.C // self.nz

    @property
    def Ch(self):
        return self.C // self.R

    @property
    def Hh(self):
        return self.H // self.R

    @property
    def steps(self):
        return self.nw // self.wb

    @property
    def chips(self):
        return self.ns // 2

    @property
    def rb(self):
        return self.cs // self.chips

    def place(self):
        s, z = lax.axis_index("seq"), lax.axis_index("ch")
        return s, z, lax.rem(z, self.g), lax.div(z, self.g)


def gelu(z):
    t = jnp.tanh(z * (GC0 + (GC0 * GC1) * (z * z)))
    return z * (0.5 + 0.5 * t)


def gelu_both(z):
    sq = z * z
    t = jnp.tanh(z * (GC0 + (GC0 * GC1) * sq))
    h = 0.5 + 0.5 * t
    v = z * h
    return v, h + v * (1.0 - t) * (GC0 + (3.0 * GC0 * GC1) * sq)


def gelu_slope(z):
    return gelu_both(z)[1]


def fold(v):
    return jnp.sum(v.reshape(v.shape[0] // 8, 8, v.shape[1]), axis=0)


def fold_lanes(v):
    out = v[:, 0:128]
    for k in range(128, v.shape[1], 128):
        out = out + v[:, k : k + 128]
    return out


def unfold(v):
    return jnp.sum(v, axis=0, keepdims=True)


def rows_of(shape):
    return lax.broadcasted_iota(jnp.int32, shape, 0)


def lanes_of(shape):
    return lax.broadcasted_iota(jnp.int32, shape, 1)


def total_of(lens):
    n = lens[0]
    for k in range(1, lens.shape[0]):
        n = n + lens[k]
    return n.astype(F32)


def norm_of(stats, total):
    mean = stats[0:1] / total
    square = stats[1:2] / total
    return mean, lax.rsqrt(square - mean * mean + EPS)


def flat(ref):
    return ref[...].reshape(1, ref.shape[0])


def column(row, n):
    return jnp.broadcast_to(row, (n, row.shape[1])).T


def mm(a, b):
    return jnp.dot(a, b, preferred_element_type=F32)


def mm_nt(a, b):
    return lax.dot_general(a, b, (((1,), (1,)), ((), ())), preferred_element_type=F32)


def mm_tn(a, b):
    return lax.dot_general(a, b, (((0,), (0,)), ((), ())), preferred_element_type=F32)


def mm_tt(a, b):
    return lax.dot_general(a, b, (((0,), (1,)), ((), ())), preferred_element_type=F32)


def eye_matrix(n, m, first):
    return jnp.where(lanes_of((n, m)) == rows_of((n, m)) + first, 1.0, 0.0).astype(BF16)


def pick_matrix(L):
    r, n = rows_of((L, L)), lanes_of((L, L))
    bin_of = 2 * r - jnp.where(r >= L // 2, L - 1, 0)
    return jnp.where(n == bin_of, 1.0, 0.0).astype(BF16)


def remote(src, dst, send, recv, device):
    return pltpu.make_async_remote_copy(
        src_ref=src,
        dst_ref=dst,
        send_sem=send,
        recv_sem=recv,
        device_id=device,
        device_id_type=MESH,
    )


def wrap(v, n):
    return jnp.where(v >= n, v - n, v)


def greet(devices):
    barrier = pltpu.get_barrier_semaphore()
    for device in devices:
        pl.semaphore_signal(barrier, inc=1, device_id=device, device_id_type=MESH)


def meet(devices):
    pl.semaphore_wait(pltpu.get_barrier_semaphore(), len(devices))


class Peers:
    def __init__(self, me, others):
        self.me, self.others = me, others
        self.count = len(others) + 1

    def start(self, link):
        packet, buf, sems = link
        for device in self.others:
            remote(packet, buf.at[self.me], sems.at[0], sems.at[1], device).start()

    def finish(self, link):
        packet, buf, sems = link
        buf[self.me] = packet[...]
        rest = buf.at[pl.ds(0, self.count - 1)]
        done = remote(rest, rest, sems.at[0], sems.at[1], self.others[0])
        done.wait_recv()
        acc = buf[0]
        for q in range(1, self.count):
            acc = acc + buf[q]
        done.wait_send()
        return acc

    def scratch(self, rows, width):
        return [
            pltpu.VMEM((rows, width), F32),
            pltpu.VMEM((self.count, rows, width), F32),
            pltpu.SemaphoreType.DMA((2,)),
        ]


def group_peers(plan):
    s, z, i, h = plan.place()
    g = plan.g
    others = [
        (wrap(s + a, plan.ns), h * g + wrap(i + b, g))
        for a in range(plan.ns)
        for b in range(g)
        if a or b
    ]
    return Peers(s * g + i, others)


def plane_peers(plan):
    s, z, i, h = plan.place()
    return Peers(s, [(wrap(s + a, plan.ns), z) for a in range(1, plan.ns)])


def line_peers(plan):
    s, z, i, h = plan.place()
    return Peers(z, [(s, wrap(z + a, plan.nz)) for a in range(1, plan.nz)])


class Halo:
    def __init__(self, plan, edge, land, sems):
        self.edge, self.land, self.sems = edge, land, sems
        s, z, _, _ = plan.place()
        self.to = ((wrap(s + plan.ns - 1, plan.ns), z), (wrap(s + 1, plan.ns), z))

    def copy(self, side, rows):
        return remote(
            self.edge.at[side, rows],
            self.land.at[1 - side, rows],
            self.sems.at[0, side],
            self.sems.at[1, side],
            self.to[side],
        )

    def start(self, first, count):
        for side in range(2):
            self.copy(side, pl.ds(first, count)).start()

    def finish(self):
        for side in range(2):
            done = self.copy(side, pl.ds(0, self.land.shape[1]))
            done.wait_recv()
            done.wait_send()


HALO_SEMS = pltpu.SemaphoreType.DMA((2, 2))


class Gather:
    def __init__(self, plan, part, full, sems):
        self.plan, self.part, self.full, self.sems = plan, part, full, sems
        self.s, self.z, self.i, self.h = plan.place()
        self.c, self.m = lax.rem(self.s, 2), lax.div(self.s, 2)
        self.chips = plan.chips
        self.every = self.chips // 4
        self.tap = lax.div(self.m, self.every)
        self.owner = lax.rem(self.m, self.every) == 0
        self.mine = full.at[self.c, self.tap]

    def others(self):
        g, nz = self.plan.g, self.plan.nz
        return [(self.s, wrap(self.h * g + g + r, nz)) for r in range(nz - g)]

    def far(self, off):
        return (2 * wrap(self.m + off, self.chips) + self.c, self.z)

    def own(self):
        return pltpu.make_async_copy(self.part, self.mine.at[self.z], self.sems.at[0, 0])

    def line(self, off):
        device = (self.s, wrap(self.z + off, self.plan.nz))
        return remote(
            self.part, self.mine.at[self.z], self.sems.at[0, 1], self.sems.at[1, 1], device
        )

    def chip(self, off):
        return remote(self.mine, self.mine, self.sems.at[0, 2], self.sems.at[1, 2], self.far(off))

    def pair(self):
        half = self.full.at[self.c]
        device = (2 * self.m + 1 - self.c, self.z)
        return remote(half, half, self.sems.at[0, 3], self.sems.at[1, 3], device)

    def line_start(self):
        @pl.when(self.owner)
        def _():
            self.own().start()
            for off in range(1, self.plan.nz):
                self.line(off).start()

    def line_finish(self):
        @pl.when(self.owner)
        def _():
            self.own().wait()
            rest = self.mine.at[pl.ds(0, self.plan.nz - 1)]
            device = (self.s, wrap(self.z + 1, self.plan.nz))
            done = remote(rest, rest, self.sems.at[0, 1], self.sems.at[1, 1], device)
            done.wait_recv()
            done.wait_send()

    def chips_start(self):
        @pl.when(self.owner)
        def _():
            for off in range(1, self.chips):
                self.chip(off).start()

    def pair_start(self):
        def taken(count):
            rest = self.full.at[self.c, pl.ds(0, count)]
            return remote(rest, rest, self.sems.at[0, 2], self.sems.at[1, 2], self.far(1))

        @pl.when(self.owner)
        def _():
            taken(3).wait_recv()
            for off in range(1, self.chips):
                self.chip(off).wait_send()

        if self.every > 1:

            @pl.when(jnp.logical_not(self.owner))
            def _():
                taken(4).wait_recv()

        self.pair().start()

    def pair_finish(self):
        done = self.pair()
        done.wait_recv()
        done.wait_send()


def first_step():
    return pl.program_id(0) == 0


def last_step():
    return pl.program_id(0) == pl.num_programs(0) - 1


def head_kernel(plan, nm, lens, x, xtop, xend, ctop, cend, g2, s2, pb, g3, s3,
                w_hbm, gain, shift, taps, pw,
                X5, x2, land, state, beyond_out, full,
                macc, beyond, xedge, sel, act, edge, acc, w_ref, w_sem, part,
                gather_sems, xhalo_sems, halo_sems, *links):
    t = pl.program_id(0)
    peers, plane, line = group_peers(plan), plane_peers(plan), line_peers(plan)
    xhalo = Halo(plan, xedge, beyond, xhalo_sems)
    halo = Halo(plan, edge, land, halo_sems)
    gather = Gather(plan, part, full, gather_sems)
    w_copy = pltpu.make_async_copy(w_hbm, w_ref, w_sem)
    plane_link, line_link, link = links[:3], links[3:6], links[6:]
    s, z, i, h = plan.place()
    L, Lp, C, nw, nz, wb = plan.L, plan.Lp, plan.C, plan.nw, plan.nz, plan.wb
    share = plan.NW // nz
    c = t - nm - 1
    everyone = peers.others + gather.others()

    @pl.when(first_step())
    def _():
        w_copy.start()
        greet(everyone)
        part[...] = jnp.where(gather.tap == 3, pw[...], taps[0])
        macc[...] = jnp.zeros_like(macc)
        acc[...] = jnp.zeros_like(acc)
        state[...] = jnp.zeros_like(state)
        state[GAIN1 : GAIN1 + 1] = flat(gain)
        state[SHIFT1 : SHIFT1 + 1] = flat(shift)
        n16 = nw * 16
        for side, (xe, ce, places) in enumerate(
            ((xtop, ctop, (0, 1, 0)), (xend, cend, (14, 15, 15)))
        ):
            for k, at in enumerate(places):
                rows, lanes = rows_of((nw, n16)), lanes_of((nw, n16))
                one = jnp.where(lanes == 16 * rows + at, 1.0, 0.0).astype(BF16)
                block = (xe if k < 2 else ce)[...].reshape(n16, C)
                xedge[side, k] = mm(one, block)
        shape = (Lp, L)
        for k in range(plan.T1):
            at = lanes_of(shape) - (2 * rows_of(shape) + (k - 2))
            sel[k * Lp : (k + 1) * Lp] = jnp.where((at == 0) | (at == 1), 1.0, 0.0).astype(BF16)

    @pl.when(t < nm)
    def _():
        rows = rows_of((L, C))
        for w in range(min(share, wb)):
            at = lax.rem(z * share, wb) + w
            valid = 2 * lens[z * share + t * wb + w] - s * L
            v = jnp.where(rows < valid, x[at].astype(F32), 0.0)
            macc[0] += fold(v)
            macc[1] += fold(v * v)

    @pl.when(t == nm - 1)
    def _():
        packet = plane_link[0]
        packet[0:1] = unfold(macc[0])
        packet[1:2] = unfold(macc[1])
        meet(everyone)
        plane.start(plane_link)
        xhalo.start(0, 3)
    def activation():
        mean, rho = norm_of(state[ST1 : ST1 + 2], 2.0 * total_of(lens))
        scale = state[GAIN1 : GAIN1 + 1] * rho
        offset = state[SHIFT1 : SHIFT1 + 1] - mean * scale
        rows = rows_of((L, C))

        def activate(n, w):
            valid = 2 * lens[i * nw + n * wb + w] - s * L
            a = gelu(x[w].astype(F32) * scale + offset)
            act[w] = jnp.where(rows < valid, a, 0.0).astype(BF16)

        return scale, offset, activate

    @pl.when(c == -1)
    def _():
        more = line_link[0]
        at = 0
        spans = []
        more[2:3] = jnp.zeros((1, C), F32)
        for ref in (g2, s2, pb, g3, s3):
            n = ref.shape[1]
            more[2:3, at : at + n] = ref[...]
            spans.append((at, n))
            at += n
        more[0:2] = plane.finish(plane_link)
        line.start(line_link)
        gather.line_start()
        state[ST1 : ST1 + 2] = line.finish(line_link)[0:2]
        for k in range(nz):
            row = line_link[1][k]
            for r, (at, n) in zip((GAIN2, SHIFT2, BIAS, GAIN3, SHIFT3), spans):
                state[r : r + 1, k * n : (k + 1) * n] = row[2:3, at : at + n]
        xhalo.finish()
        beyond_out[...] = beyond[...]
        w_copy.wait()

        _, _, activate = activation()
        for w in range(wb):
            activate(0, w)

    @pl.when(c >= 0)
    def _():
        scale, offset, activate = activation()
        row1 = rows_of((1, C))
        row16 = rows_of((16, C))

        def pairs(w):
            at = c * wb + w
            valid = 2 * lens[i * nw + at] - s * L
            picked = mm(sel[...], act[w])
            for k in range(5):
                X5[k, w * Lp : (w + 1) * Lp] = picked[k * Lp : (k + 1) * Lp].astype(BF16)

            def beside(side, k, bin_at):
                a = gelu(beyond[side, k, pl.ds(at, 1), :] * scale + offset)
                here = (row1 + bin_at < valid) & (row1 + (s * L + bin_at) >= 0)
                return jnp.where(here, a, 0.0).astype(BF16).astype(F32)

            l0, l1 = beside(0, 0, -2), beside(0, 1, -1)
            r0, r1 = beside(1, 0, L), beside(1, 1, L + 1)
            top, end = w * Lp, (w + 1) * Lp
            for k, add in ((0, l0 + l1), (1, l1)):
                X5[k, top : top + 16] = (
                    picked[k * Lp : k * Lp + 16] + jnp.where(row16 == 0, add, 0.0)
                ).astype(BF16)
            for k, add in ((3, r0), (4, r0 + r1)):
                X5[k, end - 16 : end] = (
                    picked[(k + 1) * Lp - 16 : (k + 1) * Lp] + jnp.where(row16 == 15, add, 0.0)
                ).astype(BF16)

        nc = 256
        rowp = rows_of((Lp, nc))

        def convolve(n):
            cols = slice(n * nc, (n + 1) * nc)
            taps = [X5[k] for k in range(plan.T1)]
            y = 0.5 * mm(jnp.concatenate(taps, axis=1), w_ref[:, cols])
            s0 = jnp.zeros((8, nc), F32)
            s1 = jnp.zeros((8, nc), F32)
            for w in range(wb):
                at = c * wb + w
                valid = lens[i * nw + at] - s * Lp
                v = y[w * Lp : (w + 1) * Lp]
                x2[w, :, cols] = v
                edge[0, at, :, cols] = v[:EDGE].astype(BF16)
                edge[1, at, :, cols] = v[Lp - EDGE :].astype(BF16)
                v = jnp.where(rowp < valid, v, 0.0)
                s0 = s0 + fold(v)
                s1 = s1 + fold(v * v)
            acc[0:1, cols] += unfold(s0)
            acc[1:2, cols] += unfold(s1)

        for w in range(wb):
            pairs(w)
        chunks = C // nc
        after = jnp.minimum(c + 1, plan.steps - 1)
        for n in range(chunks):
            convolve(n)
            for w in range(n * wb // chunks, (n + 1) * wb // chunks):
                activate(after, w)
        halo.start(c * wb, wb)

    @pl.when(c == 0)
    def _():
        gather.line_finish()
        gather.chips_start()

    @pl.when(last_step())
    def _():
        link[0][...] = acc[...]
        peers.start(link)
        gather.pair_start()
        state[ST2 : ST2 + 2] = peers.finish(link)
        halo.finish()
        gather.pair_finish()


def block_kernel(plan, lens, x2, x2half, x2land, cot, w_ref, pw_ref, old, half_state,
                 dz2, grads, pgrad, res, land, state, res_got,
                 ext, wf, wt, pw, Y3, c2, dz3, das, a3s, a3T, dos, Z3, dcT,
                 cedge, cland, cacc, dedge, dland, dacc, bedge, bacc, halo_sems, bulk_sems,
                 *links):
    t = pl.program_id(0)
    peers = group_peers(plan)
    s, z, i, h = plan.place()
    Lp, C, H, wb, nw, cs, g = plan.Lp, plan.C, plan.H, plan.wb, plan.nw, plan.cs, plan.g
    M = wb * Lp
    steps = plan.steps
    p0, r0, b0, g0 = block_phases(plan)[:4]
    c_link, d_link, b_link = links[:3], links[3:6], links[6:]
    c_halo = Halo(plan, cedge, cland, halo_sems.at[0])
    d_halo = Halo(plan, dedge, dland, halo_sems.at[1])
    b_halo = Halo(plan, bedge, land, halo_sems.at[2])

    def bulk(off, rows):
        to = wrap(i + off, g)
        return remote(
            res.at[to, rows],
            res_got.at[off, rows],
            bulk_sems.at[0, off],
            bulk_sems.at[1, off],
            (s, h * g + to),
        )

    def result_of(block):
        y = mm(a3s[pl.ds(pl.multiple_of(block * M, 128), M)], pw_ref[h, 0])
        rowr = rows_of((Lp, y.shape[1]))
        for w in range(wb):
            at = block * wb + w
            valid = lens[i * plan.nw + at] - s * Lp
            r = x2half[w] + y[w * Lp : (w + 1) * Lp] + half_state[BIAS : BIAS + 1]
            r = jnp.where(rowr < valid, r, 0.0).astype(BF16).T
            for k in range(g):
                res[k, at] = r[k * cs : (k + 1) * cs]

    def send_result(block):
        result_of(block)
        for off in range(1, g):
            bulk(off, pl.ds(block * wb, wb)).start()

    @pl.when(first_step())
    def _():
        greet(peers.others)
        state[...] = old[...]
        cacc[...] = jnp.zeros_like(cacc)
        dacc[...] = jnp.zeros_like(dacc)
        bacc[...] = jnp.zeros_like(bacc)
        for c in range(2):
            cols = slice(c * (C // 2), (c + 1) * (C // 2))
            pw[:, cols] = pw_ref[c, 0]
            for k in range(plan.T2):
                at = k * C + c * (C // 2)
                wf[:, at : at + C // 2] = w_ref[c, k]
                wt[k * H : (k + 1) * H, cols] = w_ref[c, k]

    @pl.when(t < p0)
    def _():
        base = pl.multiple_of(t * M, 128)
        mean, rho = norm_of(state[ST2 : ST2 + 2], total_of(lens))
        scale = state[GAIN2 : GAIN2 + 1] * rho
        offset = state[SHIFT2 : SHIFT2 + 1] - mean * scale
        rows = rows_of((Lp, C))
        rowe = rows_of((EDGE, C))

        rowh = rows_of((Lp, H))
        sums0, sums1 = jnp.zeros((8, H), F32), jnp.zeros((8, H), F32)
        nh = min(2, wb)
        for first in range(0, wb, wb // nh):
            span = range(first, first + wb // nh)
            for w in span:
                valid = lens[i * plan.nw + t * wb + w] - s * Lp
                a = jnp.where(rows < valid, gelu(x2[w] * scale + offset), 0.0)
                al = gelu(x2land[0, w].astype(F32) * scale + offset)
                al = jnp.where((rowe - EDGE < valid) & (s > 0), al, 0.0)
                ah = gelu(x2land[1, w].astype(F32) * scale + offset)
                ah = jnp.where(rowe + Lp < valid, ah, 0.0)
                ext[w, 0:EDGE] = al
                ext[w, EDGE : EDGE + Lp] = a
                ext[w, EDGE + Lp :] = ah
                top, end = w * Lp, (w + 1) * Lp
                Y3[pl.ds(base + top, Lp), 0:C] = ext[w, EDGE - DIL : EDGE - DIL + Lp].astype(BF16)
                Y3[pl.ds(base + top, Lp), C : 2 * C] = a.astype(BF16)
                Y3[pl.ds(base + top, Lp), 2 * C : 3 * C] = ext[w, EDGE + DIL : EDGE + DIL + Lp].astype(BF16)
            y = mm_nt(Y3[pl.ds(base + first * Lp, wb // nh * Lp)], wf[...])
            for w in span:
                at = t * wb + w
                valid = lens[i * plan.nw + at] - s * Lp
                v = y[(w - first) * Lp : (w - first + 1) * Lp]
                c2[at] = v
                cedge[0, at] = v[:EDGE].astype(BF16)
                cedge[1, at] = v[Lp - EDGE :].astype(BF16)
                v = jnp.where(rowh < valid, v, 0.0)
                sums0 = sums0 + fold(v)
                sums1 = sums1 + fold(v * v)
        cacc[0:1, 0:H] += unfold(sums0)
        cacc[0:1, H:] += unfold(sums1)

    @pl.when(first_step())
    def _():
        meet(peers.others)

    @pl.when(t < p0)
    def _():
        c_halo.start(t * wb, wb)

    @pl.when(t == p0 - 1)
    def _():
        c_link[0][...] = cacc[...]
        peers.start(c_link)

    here_p = (t >= p0) & (t < p0 + steps)

    @pl.when(here_p)
    def _():
        u = t - p0
        rowc = rows_of((Lp, C))
        block = pl.ds(pl.multiple_of(u * M, 128), M)
        bias = jnp.zeros((8, C), F32)
        parts = []
        for w in range(wb):
            valid = lens[i * plan.nw + u * wb + w] - s * Lp
            d = jnp.where(rowc < valid, cot[w].astype(F32), 0.0)
            bias = bias + fold(d)
            parts.append(d.astype(BF16))
        d = jnp.concatenate(parts, axis=0)
        dos[block] = d
        das[...] = mm_nt(d, pw[...])
        dacc[1:2] += unfold(bias)

    @pl.when(t == p0)
    def _():
        got = peers.finish(c_link)
        state[ST3 : ST3 + 1, 0:H] = got[:, 0:H]
        state[ST3 + 1 : ST3 + 2, 0:H] = got[:, H:]

    @pl.when(here_p)
    def _():
        u = t - p0
        block = pl.ds(pl.multiple_of(u * M, 128), M)
        rowh = rows_of((Lp, H))
        mean, rho = norm_of(state[ST3 : ST3 + 2, 0:H], total_of(lens))
        scale = state[GAIN3 : GAIN3 + 1, 0:H] * rho
        offset = state[SHIFT3 : SHIFT3 + 1, 0:H] - mean * scale
        s0, s1 = jnp.zeros((8, H), F32), jnp.zeros((8, H), F32)
        parts = []
        for w in range(wb):
            at = u * wb + w
            valid = lens[i * plan.nw + at] - s * Lp
            top, end = w * Lp, (w + 1) * Lp
            v = c2[at]
            zv = v * scale + offset
            act, slope = gelu_both(zv)
            parts.append(jnp.where(rowh < valid, act, 0.0).astype(BF16))
            dzw = das[top:end] * slope
            dz3[at] = dzw
            dedge[0, at] = dzw[:EDGE].astype(BF16)
            dedge[1, at] = dzw[Lp - EDGE :].astype(BF16)
            s0 = s0 + fold(dzw)
            s1 = s1 + fold(dzw * zv)
        a3 = jnp.concatenate(parts, axis=0)
        a3s[block] = a3
        a3T[:, block] = a3.T
        dacc[0:1, 0:H] += unfold(s0)
        dacc[0:1, H : 2 * H] += unfold(s1)
        d_halo.start(u * wb, wb)

    @pl.when(t == p0)
    def _():
        send_result(0)

    @pl.when(t == p0 + steps - 1)
    def _():
        d_link[0][...] = dacc[...]
        peers.start(d_link)

    @pl.when((t >= r0) & (t < b0))
    def _():
        send_result(t - r0 + 1)

    @pl.when(t == b0 - 1)
    def _():
        rows = pl.ds(pl.multiple_of(h * plan.Hh, 16), plan.Hh)
        pgrad[...] = mm(a3T[rows], dos[...]).astype(BF16)

    @pl.when(t == b0)
    def _():
        got = peers.finish(d_link)
        shift = state[SHIFT3 : SHIFT3 + 1, 0:H]
        gain = state[GAIN3 : GAIN3 + 1, 0:H]
        state[SU3 : SU3 + 1, 0:H] = got[0:1, 0:H]
        state[SU3 + 1 : SU3 + 2, 0:H] = (got[0:1, H : 2 * H] - shift * got[0:1, 0:H]) / gain
        state[BSUM : BSUM + 1] = got[1:2]
        c_halo.finish()
        d_halo.finish()

    @pl.when((t >= b0) & (t < g0))
    def _():
        u = t - b0
        total = total_of(lens)
        mean3, rho3 = norm_of(state[ST3 : ST3 + 2, 0:H], total)
        gr3 = state[GAIN3 : GAIN3 + 1, 0:H] * rho3
        sg3 = state[SU3 : SU3 + 1, 0:H] / total
        gg3 = state[SU3 + 1 : SU3 + 2, 0:H] / total
        mean2, rho2 = norm_of(state[ST2 : ST2 + 2], total)
        scale2 = state[GAIN2 : GAIN2 + 1] * rho2
        offset2 = state[SHIFT2 : SHIFT2 + 1] - mean2 * scale2
        rowh = rows_of((Lp, H))
        rowe = rows_of((EDGE, H))
        rowc = rows_of((Lp, C))

        by_v = -gr3 * rho3 * gg3
        by_1 = gr3 * (mean3 * rho3 * gg3 - sg3)

        def back(dz, v):
            return gr3 * dz + by_v * v + by_1

        for w in range(wb):
            valid = lens[i * nw + u * wb + w] - s * Lp
            d = jnp.where(rowh < valid, back(dz3[u * wb + w], c2[u * wb + w]), 0.0)
            dl = back(dland[0, u * wb + w].astype(F32), cland[0, u * wb + w].astype(F32))
            dl = jnp.where((rowe - EDGE < valid) & (s > 0), dl, 0.0)
            dh = back(dland[1, u * wb + w].astype(F32), cland[1, u * wb + w].astype(F32))
            dh = jnp.where(rowe + Lp < valid, dh, 0.0)
            ext[w, 0:EDGE, 0:H] = dl
            ext[w, EDGE : EDGE + Lp, 0:H] = d
            ext[w, EDGE + Lp :, 0:H] = dh
            top, end = w * Lp, (w + 1) * Lp
            Z3[top:end, 0:H] = ext[w, EDGE + DIL : EDGE + DIL + Lp, 0:H].astype(BF16)
            Z3[top:end, H : 2 * H] = d.astype(BF16)
            Z3[top:end, 2 * H : 3 * H] = ext[w, EDGE - DIL : EDGE - DIL + Lp, 0:H].astype(BF16)

        y = mm(Z3[...], wt[...])

        M = wb * Lp
        dcT[:, pl.ds(pl.multiple_of(u * M, 128), M)] = Z3[:, H : 2 * H].T
        s0, s1 = jnp.zeros((8, C), F32), jnp.zeros((8, C), F32)
        for w in range(wb):
            at = u * wb + w
            valid = lens[i * nw + at] - s * Lp
            v = x2[w]
            zv = v * scale2 + offset2
            dzw = y[w * Lp : (w + 1) * Lp] * gelu_slope(zv)
            dzw = jnp.where(rowc < valid, dzw, 0.0)
            dz2[w] = dzw
            bedge[0, pl.ds(at, 1)] = dzw[0:1]
            bedge[1, pl.ds(at, 1)] = dzw[Lp - 1 : Lp]
            s0 = s0 + fold(dzw)
            s1 = s1 + fold(dzw * zv)
        bacc[0:1] += unfold(s0)
        bacc[1:2] += unfold(s1)

    @pl.when(t == g0 - 1)
    def _():
        b_link[0][...] = bacc[...]
        peers.start(b_link)
        b_halo.start(0, nw)

    @pl.when(t >= g0)
    def _():
        rows = pl.ds(pl.multiple_of(h * plan.Hh, 16), plan.Hh)
        cols = pl.ds(pl.multiple_of((t - g0) * C, 128), C)
        grads[...] = mm(dcT[rows], Y3[:, cols]).astype(BF16)

    @pl.when(last_step())
    def _():
        got = peers.finish(b_link)
        shift, gain = state[SHIFT2 : SHIFT2 + 1], state[GAIN2 : GAIN2 + 1]
        state[SU2 : SU2 + 1] = got[0:1]
        state[SU2 + 1 : SU2 + 2] = (got[1:2] - shift * got[0:1]) / gain
        b_halo.finish()
        for off in range(1, g):
            bulk(off, pl.ds(0, nw)).wait()


def block_phases(plan):
    n = plan.steps
    return n, 2 * n, 3 * n - 1, 4 * n - 1, 4 * n - 1 + plan.T2


class Reduction:
    def __init__(self, plan, batches, out, give, mine, got, spread, half, mate, sems):
        self.plan, self.batches, self.out = plan, batches, out
        self.give, self.mine, self.got, self.spread = give, mine, got, spread
        self.half, self.mate = half, mate
        self.sems = sems
        self.s, self.z, self.i, self.h = plan.place()
        self.c = lax.rem(self.s, 2)
        self.m = lax.div(self.s, 2)
        self.chips = plan.chips

    @staticmethod
    def scratch(plan, batches):
        taps, wide = plan.T1 + 2, plan.C // 2
        full = (taps, plan.chips, plan.g, plan.rb, wide)
        part = (taps, plan.g, plan.rb, wide)
        return [
            pltpu.VMEM((taps, 2, plan.chips, plan.rb, wide), BF16),
            *[pltpu.VMEM(full, BF16)] * 4,
            *[pltpu.VMEM(part, BF16)] * 2,
            pltpu.SemaphoreType.DMA((2, len(batches), 5)),
        ]

    def copy(self, b, phase, src, dst, device):
        return remote(src, dst, self.sems.at[0, b, phase], self.sems.at[1, b, phase], device)

    def finish(self, b, phase, ref, device):
        done = self.copy(b, phase, ref, ref, device)
        done.wait_recv()
        done.wait_send()

    def taps(self, b):
        return pl.ds(*self.batches[b])

    def pair(self):
        return (2 * self.m + (1 - self.c), self.z)

    def far(self, off):
        return (2 * wrap(self.m + off, self.chips) + self.c, self.z)

    def member(self, off):
        return (self.s, self.h * self.plan.g + wrap(self.i + off, self.plan.g))

    def put(self, k, rows):
        wide = self.plan.C // 2
        for j in range(self.plan.g):
            for m in range(self.chips):
                v = rows(j, m)
                left, right = v[:, :wide], v[:, wide:]
                self.mine[k, m, j] = jnp.where(self.c == 0, left, right).astype(BF16)
                self.give[k, m, j] = jnp.where(self.c == 0, right, left).astype(BF16)

    def step0(self, b):
        taps = self.taps(b)
        self.copy(b, 0, self.give.at[taps], self.got.at[taps], self.pair()).start()

    def step1(self, b):
        taps = self.taps(b)
        self.finish(b, 0, self.got.at[taps], self.pair())
        first, count = self.batches[b]
        for k in range(first, first + count):
            v = self.mine[k].astype(F32) + self.got[k].astype(F32)
            self.mine[k] = v.astype(BF16)
        for off in range(1, self.chips):
            src = self.mine.at[taps, wrap(self.m + off, self.chips)]
            self.copy(b, 1, src, self.spread.at[taps, self.m], self.far(off)).start()

    def step2(self, b):
        taps = self.taps(b)
        self.finish(b, 1, self.spread.at[taps, pl.ds(0, self.chips - 1)], self.far(1))
        first, count = self.batches[b]
        for k in range(first, first + count):
            self.spread[k, self.m] = self.mine[k, self.m]
            v = self.spread[k, 0].astype(F32)
            for n in range(1, self.chips):
                v = v + self.spread[k, n].astype(F32)
            self.half[k] = v.astype(BF16)
        for off in range(1, self.plan.g):
            src = self.half.at[taps, wrap(self.i + off, self.plan.g)]
            self.copy(b, 2, src, self.mate.at[taps, off], self.member(off)).start()

    def step3(self, b):
        taps = self.taps(b)
        self.finish(b, 2, self.mate.at[taps, pl.ds(1, self.plan.g - 1)], self.member(1))
        first, count = self.batches[b]
        for k in range(first, first + count):
            v = self.half[k, self.i].astype(F32)
            for off in range(1, self.plan.g):
                v = v + self.mate[k, off].astype(F32)
            self.out[k, self.c, self.m] = v.astype(BF16)
        mine = self.out.at[taps, self.c, self.m]
        for off in range(1, self.chips):
            self.copy(b, 3, mine, mine, self.far(off)).start()

    def step4(self, b):
        taps = self.taps(b)
        self.finish(b, 3, self.out.at[taps, self.c, pl.ds(0, self.chips - 1)], self.far(1))
        mine = self.out.at[taps, self.c]
        self.copy(b, 4, mine, mine, self.pair()).start()

    def step5(self, b):
        self.finish(b, 4, self.out.at[self.taps(b), self.c], self.pair())


def tail_turns(plan):
    nD = plan.steps
    first = max(nD - 1, 1)
    turns = [("x", n) for n in range(first)] + [("d", n) for n in range(first, nD)]
    turns += [("w", n) for n in range(plan.T1)]
    return turns + [("x", n) for n in range(first, nD)]


def tail_batches(plan):
    return [(plan.T1, 2), (0, 2), (2, 2), (4, plan.T1 - 4)]


def tail_kernel(plan, lens, dz2, dzland, x2, x2land, cot, beyond, x, X5_hbm, taps_hbm, grads, pgrad,
                old, half_state,
                gz, gz_got, sums, summed,
                ext, D3, D0T, wcat, pick, eye, cols, y, part, split, acc, X5, X5_sems,
                taps, bulk_sems, *rest):
    t = pl.program_id(0)
    s, z, i, h = plan.place()
    L, Lp, C, wb, g, nw = plan.L, plan.Lp, plan.C, plan.wb, plan.g, plan.nw
    Ch, cs, T1 = plan.Ch, plan.cs, plan.T1
    M = wb * Lp
    nD = plan.steps
    turns = tail_turns(plan)
    last = len(turns) - 1
    peers = group_peers(plan)
    red = Reduction(plan, tail_batches(plan), *rest[:8])
    link = rest[8:]

    def member(off):
        return (s, h * g + wrap(i + off, g))

    def send(first, count):
        rows = pl.ds(first, count)
        for off in range(1, g):
            remote(
                part.at[off - 1, rows],
                gz_got.at[off, rows],
                bulk_sems.at[0, off],
                bulk_sems.at[1, off],
                member(off),
            ).start()

    def X5_copy(k):
        return pltpu.make_async_copy(X5_hbm.at[k], X5.at[k % 2], X5_sems.at[k % 2])

    def when(at):
        return pl.when(t == min(at, last))

    def turn(kind, k):
        return turns.index((kind, k)) if (kind, k) in turns else last

    def turn_of(kind):
        index = jnp.int32(0)
        here = False
        for n, (what, k) in enumerate(turns):
            if what == kind:
                index = jnp.where(t == n, k, index)
                here = (t == n) | here
        return here, index

    taps_copy = pltpu.make_async_copy(
        taps_hbm.at[:, pl.ds(pl.multiple_of(h * Ch, 128), Ch)], taps, X5_sems.at[2]
    )

    @when(0)
    def _():
        taps_copy.start()
        greet(peers.others)
        acc[...] = jnp.zeros_like(acc)
        pick[...] = pick_matrix(L)
        eye[...] = eye_matrix(Ch, Ch, 0)
        mean, rho = norm_of(half_state[ST1 : ST1 + 2], 2.0 * total_of(lens))
        scale = half_state[GAIN1 : GAIN1 + 1] * rho
        offset = half_state[SHIFT1 : SHIFT1 + 1] - mean * scale
        for k, row in enumerate((scale, offset)):
            cols[k] = column(row, L)

    @pl.when(t < nD)
    def _():
        total = total_of(lens)
        mean, rho = norm_of(old[ST2 : ST2 + 2], total)
        gr = old[GAIN2 : GAIN2 + 1] * rho
        sg = old[SU2 : SU2 + 1] / total
        gg = old[SU2 + 1 : SU2 + 2] / total
        rowc = rows_of((Lp, C))
        row1 = rows_of((1, C))

        by_dz = 0.5 * gr
        by_v = -0.5 * gr * rho * gg
        by_1 = 0.5 * gr * (mean * rho * gg - sg)

        def back(dout, dz, v):
            return 0.5 * dout + by_dz * dz + by_v * v + by_1

        def grad_of(w):
            at = t * wb + w
            valid = lens[i * nw + at] - s * Lp
            d = back(cot[w].astype(F32), dz2[w], x2[w])
            d = jnp.where(rowc < valid, d, 0.0)
            one = pl.ds(at, 1)
            dl = back(beyond[0, 2, one, :], dzland[0, one, :], x2land[0, w, EDGE - 1 : EDGE].astype(F32))
            dl = jnp.where((row1 - 1 < valid) & (s > 0), dl, 0.0)
            dh = back(beyond[1, 2, one, :], dzland[1, one, :], x2land[1, w, 0:1].astype(F32))
            dh = jnp.where(row1 + Lp < valid, dh, 0.0)
            ext[w, 7:8] = dl
            ext[w, 8 : 8 + Lp] = d
            ext[w, 8 + Lp : 9 + Lp] = dh
            top, end = w * Lp, (w + 1) * Lp
            D3[t, top:end, 0:C] = ext[w, 9 : 9 + Lp].astype(BF16)
            D3[t, top:end, C : 2 * C] = d.astype(BF16)
            D3[t, top:end, 2 * C : 3 * C] = ext[w, 7 : 7 + Lp].astype(BF16)

        for w in range(wb):
            grad_of(w)
        half = D3[t, :, pl.ds(pl.multiple_of(C + h * Ch, 128), Ch)]
        D0T[:, pl.ds(pl.multiple_of(t * M, 128), M)] = half.T

    @when(0)
    def _():
        taps_copy.wait()
        for first in range(0, Ch, 64):
            rows = slice(first, min(first + 64, Ch))
            for r, parts in enumerate((((0,), (1, 2), (3, 4)), ((0, 1), (2, 3), (4,)))):
                for k, which in enumerate(parts):
                    v = taps[which[0], rows]
                    if len(which) > 1:
                        v = (v.astype(F32) + taps[which[1], rows].astype(F32)).astype(BF16)
                    at = r * Ch
                    wcat[at + rows.start : at + rows.stop, k * C : (k + 1) * C] = v
        meet(peers.others)

    here_x, bx = turn_of("x")

    def gradient(hf, nh):
        lanes = lanes_of((Ch, L))

        def through(w):
            valid = 2 * lens[i * nw + bx * wb + w] - s * L
            top, end = w * Lp, (w + 1) * Lp
            v = mm_nt(eye[...], x[w])
            da = jnp.concatenate([y[0:Ch, top:end], y[Ch:, top:end]], axis=1)
            da = mm(da.astype(BF16), pick[...])
            zv = v * cols[0] + cols[1]
            dzw = da * gelu_slope(zv)
            dzw = jnp.where(lanes < valid, dzw, 0.0)
            acc[0] += fold_lanes(dzw)
            acc[1] += fold_lanes(dzw * zv)
            split[w % 2] = dzw.astype(BF16)
            for off in range(g):
                rows = pl.ds(pl.multiple_of(lax.rem(i + off, g) * cs, 16), cs)
                if off == 0:
                    gz[w] = split[w % 2, rows]
                else:
                    part[off - 1, bx * wb + w] = split[w % 2, rows]

        n = wb // nh
        rows = slice(hf * n * Lp, (hf + 1) * n * Lp)
        y[:, rows] = mm_nt(wcat[...], D3[bx, rows])
        for w in range(hf * n, (hf + 1) * n):
            through(w)

    nh = 2 if wb % 2 == 0 and wb * Lp // 2 % 128 == 0 else 1

    @pl.when(here_x)
    def _():
        gradient(0, nh)
        send(bx * wb, wb // nh)

    for step, batch in ((red.step1, 3), (red.step2, 1)):

        @when(last)
        def _():
            if nh == 2 and turns[last][0] == "x":
                step(batch)

    if nh == 2:

        @pl.when(here_x)
        def _():
            gradient(1, nh)

    @pl.when(here_x & (bx < nD - 1))
    def _():
        if nh == 2:
            send(bx * wb + wb // nh, wb // nh)

    @when(0)
    def _():
        hs = plan.H // plan.nz
        rb = plan.rb
        for u in range(2):

            def rows(j, m, u=u):
                side, r = m * rb // hs, m * rb % hs
                n = 2 * side + u
                rows = slice(j * hs + r, j * hs + r + rb)
                v = grads[rows, n * C : (n + 1) * C] if n < plan.T2 else pgrad[rows]
                return v.astype(F32)

            red.put(T1 + u, rows)
        red.step0(0)

    @when(1)
    def _():
        X5_copy(0).start()
        X5_copy(1).start()

    here_w, k = turn_of("w")

    @pl.when(here_w)
    def _():
        X5_copy(k).wait()
        y[0:Ch, 0:C] = mm(D0T[...], X5[lax.rem(k, 2)])

        @pl.when(k < T1 - 2)
        def _():
            X5_copy(k + 2).start()

        rb = plan.rb
        red.put(k, lambda j, m: y[j * cs + m * rb : j * cs + (m + 1) * rb, 0:C])

    @when(turn("x", nD - 1))
    def _():
        packet = link[0]
        packet[...] = jnp.zeros_like(packet)
        packet[0:1, 0:Ch] = jnp.sum(acc[0].T, axis=0, keepdims=True)
        packet[1:2, 0:Ch] = jnp.sum(acc[1].T, axis=0, keepdims=True)
        peers.start(link)

    for at, step, batch in (
        (1, red.step1, 0),
        (max(nD - 1, 2), red.step2, 0),
        (turn("w", 1), red.step0, 1),
        (turn("w", 3), red.step1, 1),
        (turn("w", 3), red.step0, 2),
        (turn("w", 4), red.step0, 3),
        (turn("w", 4), red.step1, 2),
        *(() if nh == 2 and turns[last][0] == "x" else ((last, red.step1, 3), (last, red.step2, 1))),
        (last, red.step2, 2),
        (last, red.step3, 0),
        (last, red.step3, 1),
        (last, red.step2, 3),
    ):

        @when(at)
        def _():
            step(batch)

    @when(last)
    def _():
        if nh == 2:
            send(nw - wb // 2, wb // 2)

    @when(last)
    def _():
        red.step3(2)
        red.step4(0)
        red.step4(1)
        red.step3(3)
        red.step4(2)
        got = peers.finish(link)[:, 0:Ch]
        shift, gain = half_state[SHIFT1 : SHIFT1 + 1], half_state[GAIN1 : GAIN1 + 1]
        sums[0:1] = got[0:1]
        sums[1:2] = (got[1:2] - shift * got[0:1]) / gain
        red.step4(3)
        for b in range(4):
            red.step5(b)
        own = pltpu.make_async_copy(red.out, summed, X5_sems.at[0])
        own.start()
        for off in range(1, g):
            done = remote(
                part.at[off - 1],
                gz_got.at[off],
                bulk_sems.at[0, off],
                bulk_sems.at[1, off],
                member(off),
            )
            done.wait_recv()
            done.wait_send()
        own.wait()


def input_grad_kernel(plan, wg, lens, x, gz, gz_got, sums, res, res_got, summed,
                      state, half_state,
                      out, out_result, conv_grad, dil_grad, point_grad,
                      g1, b1, g2, b2, g3, b3, pb, eye, cols, xt):
    t = pl.program_id(0)
    s, z, i, h = plan.place()
    L, Ch, cs = plan.L, plan.Ch, plan.cs
    turn = plan.nw // wg
    mine = pl.ds(pl.multiple_of(i * cs, 16), cs)

    @pl.when(first_step())
    def _():
        n = 2.0 * total_of(lens)
        mean, rho = norm_of(half_state[ST1 : ST1 + 2], n)
        gr = half_state[GAIN1 : GAIN1 + 1] * rho
        gg = sums[1:2] / n * rho
        for k, row in enumerate((gr, -gr * gg, gr * (mean * gg - sums[0:1] / n))):
            xt[...] = column(row, L)
            cols[k] = xt[mine]
        eye[...] = eye_matrix(cs, Ch, i * cs)

        def mine_of(src, at, which, count, *dsts):
            n = dsts[0].shape[1]
            for k in range(count):

                @pl.when(which == k)
                def _():
                    for dst, r in zip(dsts, at):
                        dst[...] = src[r : r + 1, k * n : (k + 1) * n]

        mine_of(sums, (1, 0), i, plan.g, g1, b1)
        mine_of(state, (SU2 + 1, SU2), z, plan.nz, g2, b2)
        mine_of(state, (SU3 + 1, SU3), z, plan.nz, g3, b3)
        mine_of(state, (BSUM,), z, plan.nz, pb)

    own = lax.div(t, turn) == i
    for w in range(wg):
        out_result[w] = jnp.where(own, res[0, w], res_got[0, w])

    C, T1, hs, rb, wide = plan.C, plan.T1, plan.H // plan.nz, plan.rb, plan.C // 2
    count = plan.NW // wg
    turns = min(count, plan.chips)
    per, every = plan.chips // turns, count // turns

    def spread(chunk):
        for n in range(per):
            m = chunk * per + n
            side, r = m * rb // hs, m * rb % hs
            for c in range(2):
                at = slice(c * wide, (c + 1) * wide)
                for k in range(T1):
                    conv_grad[k, n * rb : (n + 1) * rb, at] = summed[k, c, n].astype(F32)
                for u in range(2):
                    v = summed[T1 + u, c, n].astype(F32)
                    if 2 * side + u < plan.T2:
                        dil_grad[2 * side + u, r : r + rb, at] = v
                    else:
                        point_grad[r : r + rb, at] = v

    for chunk in range(turns):
        pl.when(t == chunk * every)(partial(spread, chunk))

    lanes = lanes_of((cs, L))
    for w in range(wg):
        valid = 2 * lens[t * wg + w] - s * L
        v = mm_nt(eye[...], x[w])
        dz = jnp.where(own, gz[w], gz_got[0, w]).astype(F32)
        r = cols[0] * dz + v * cols[1] + cols[2]
        out[w] = jnp.where(lanes < valid, r, 0.0).astype(BF16)


def call(kernel, plan, name, steps, ins, outs, scratch, flops, nbytes, cid=None):
    extra = {} if cid is None else dict(collective_id=cid, has_side_effects=True)
    return pl.pallas_call(
        partial(kernel, plan),
        grid=(steps,),
        in_specs=[SMEM] + [spec for spec, _ in ins],
        out_specs=[spec for spec, _, _ in outs],
        out_shape=[jax.ShapeDtypeStruct(shape, dtype) for _, shape, dtype in outs],
        scratch_shapes=scratch,
        compiler_params=pltpu.CompilerParams(vmem_limit_bytes=VMEM_LIMIT, **extra),
        cost_estimate=pl.CostEstimate(
            flops=int(flops), bytes_accessed=int(nbytes), transcendentals=0
        ),
        name=name,
    )


def per_device(
    inputs,
    lengths,
    input_gain,
    input_shift,
    conv_weight,
    branch_gain,
    branch_shift,
    dilated_tap_weight,
    mixer_gain,
    mixer_shift,
    point_weight,
    point_bias,
    cotangent,
):
    NW, L, C = inputs.shape
    Lp = L // 2
    nz = lax.axis_size("ch")
    R = 2
    plan = Plan(
        ns=lax.axis_size("seq"),
        nz=nz,
        R=R,
        NW=NW,
        L=L,
        C=C,
        H=mixer_gain.shape[0] * nz,
        T1=conv_weight.shape[0],
        T2=dilated_tap_weight.shape[0],
        wb=min(NW * R // nz, max(1, 512 // Lp)),
    )
    g, nw, cs, Ch, H, Hh, wb = plan.g, plan.nw, plan.cs, plan.Ch, plan.H, plan.Hh, plan.wb
    T1, T2, steps = plan.T1, plan.T2, plan.steps
    M = wb * Lp
    hs = H // nz
    lens = lengths.astype(jnp.int32)

    def row(a):
        return a.reshape(1, a.shape[0])

    def grp():
        return lax.rem(lax.axis_index("ch"), g)

    def half():
        return lax.div(lax.axis_index("ch"), g)

    def core():
        return lax.rem(lax.axis_index("seq"), 2)

    def chip4():
        return lax.div(lax.axis_index("seq"), plan.ns // 4)

    def whole(*shape):
        return pl.BlockSpec(shape, lambda t: (0,) * len(shape), pipeline_mode=pl.Buffered(1))

    def const(*shape):
        return pl.BlockSpec(shape, lambda t: (0,) * len(shape))

    def win(*shape):
        return pl.BlockSpec(shape, lambda t: (t,) + (0,) * (len(shape) - 1))

    def arg_win(n, width):
        return pl.BlockSpec((wb, n, width), lambda t: (grp() * steps + t, 0, 0))

    def ins(*pairs):
        return [p for p in pairs]

    share = NW // nz
    nm = max(1, share // wb)

    def edge_spec(n):
        return pl.BlockSpec(
            (nw, 16, C), lambda t: (grp(), n, 0), pipeline_mode=pl.Buffered(1)
        )

    def head_block(t):
        own = lax.div(lax.axis_index("ch") * share, wb) + t
        return jnp.where(t < nm, own, grp() * steps + jnp.clip(t - nm, 0, steps - 1)), 0, 0

    def after(*shape):
        return pl.BlockSpec(
            shape, lambda t: (jnp.maximum(t - nm - 1, 0),) + (0,) * (len(shape) - 1)
        )

    pairs = ins(
        (pl.BlockSpec((wb, L, C), head_block), inputs),
        (edge_spec(0), inputs),
        (edge_spec(L // 16 - 1), inputs),
        (edge_spec(0), cotangent),
        (edge_spec(Lp // 16 - 1), cotangent),
        (whole(1, cs), row(branch_gain)),
        (whole(1, cs), row(branch_shift)),
        (whole(1, cs), row(point_bias)),
        (whole(1, H // nz), row(mixer_gain)),
        (whole(1, H // nz), row(mixer_shift)),
        (ANY, conv_weight.reshape(T1 * C, C)),
        (whole(C), input_gain),
        (whole(C), input_shift),
        (
            pl.BlockSpec(
                (1, hs, C // 2),
                lambda t: (jnp.minimum(chip4(), T2 - 1), 0, core()),
                pipeline_mode=pl.Buffered(1),
            ),
            jnp.swapaxes(dilated_tap_weight, 1, 2),
        ),
        (
            pl.BlockSpec(
                (hs, C // 2), lambda t: (0, core()), pipeline_mode=pl.Buffered(1)
            ),
            point_weight,
        ),
    )
    plane, line, group = plane_peers(plan), line_peers(plan), group_peers(plan)
    state_shape = (STATE, C)
    edges2, edges3 = (2, nw, EDGE, C), (2, nw, EDGE, H)
    X5, x2, land2, state, beyond, full = call(
        lambda plan, *refs: head_kernel(plan, nm, *refs),
        plan,
        "head",
        nm + 1 + steps,
        pairs,
        [
            (
                pl.BlockSpec((T1, M, C), lambda t: (0, jnp.maximum(t - nm - 1, 0), 0)),
                (T1, nw * Lp, C),
                BF16,
            ),
            (after(wb, Lp, C), (nw, Lp, C), F32),
            (ANY, edges2, BF16),
            (const(*state_shape), state_shape, F32),
            (const(2, 3, nw, C), (2, 3, nw, C), F32),
            (ANY, (2, T2 + 1, nz, hs, C // 2), BF16),
        ],
        [
            pltpu.VMEM((2, 8, C), F32),
            pltpu.VMEM((2, 3, nw, C), F32),
            pltpu.VMEM((2, 3, nw, C), F32),
            pltpu.VMEM((T1 * Lp, L), BF16),
            pltpu.VMEM((wb, L, C), BF16),
            pltpu.VMEM(edges2, BF16),
            pltpu.VMEM((2, C), F32),
            pltpu.VMEM((T1 * C, C), BF16),
            pltpu.SemaphoreType.DMA,
            pltpu.VMEM((hs, C // 2), BF16),
            pltpu.SemaphoreType.DMA((2, 4)),
            HALO_SEMS,
            HALO_SEMS,
        ]
        + plane.scratch(2, C)
        + line.scratch(3, C)
        + group.scratch(2, C),
        2 * nw * Lp * T1 * C * C,
        nw * Lp * C * 20,
        cid=1,
    )(lens, *[a for _, a in pairs])

    full = full.reshape(2, T2 + 1, H, C // 2)
    taps_spec = whole(2, T2, H, C // 2)
    pw_spec = pl.BlockSpec(
        (2, 1, H, C // 2), lambda t: (0, T2, 0, 0), pipeline_mode=pl.Buffered(1)
    )

    def early(*shape):
        return pl.BlockSpec(
            shape, lambda t: (jnp.minimum(t, steps - 1),) + (0,) * (len(shape) - 1)
        )

    def early_land(width):
        return pl.BlockSpec(
            (2, wb, EDGE, width), lambda t: (0, jnp.minimum(t, steps - 1), 0, 0)
        )

    def half_of(n):
        return pl.BlockSpec((n, Ch), lambda t: (0, half()), pipeline_mode=pl.Buffered(1))

    cot_spec = pl.BlockSpec(
        (wb, Lp, C), lambda t: (grp() * steps + jnp.minimum(t, steps - 1), 0, 0)
    )

    p0, r0, b0, g0, block_steps = block_phases(plan)

    def at_phase(first):
        return lambda t: jnp.clip(t - first, 0, steps - 1)

    in_p, in_b = at_phase(p0), at_phase(b0)
    pairs = ins(
        (
            pl.BlockSpec(
                (wb, Lp, C),
                lambda t: (jnp.where(t < p0 + steps, jnp.minimum(t, steps - 1), in_b(t)), 0, 0),
            ),
            x2,
        ),
        (
            pl.BlockSpec(
                (wb, Lp, Ch),
                lambda t: (jnp.clip(t - r0 + 1, 0, steps - 1), 0, half()),
            ),
            x2,
        ),
        (early_land(C), land2),
        (pl.BlockSpec((wb, Lp, C), lambda t: (grp() * steps + in_p(t), 0, 0)), cotangent),
        (taps_spec, full),
        (pw_spec, full),
        (whole(*state_shape), state),
        (half_of(STATE), state),
    )
    dz2, grads, pgrad, res, dland2, state, res_got = call(
        block_kernel,
        plan,
        "block",
        block_steps,
        pairs,
        [
            (pl.BlockSpec((wb, Lp, C), lambda t: (in_b(t), 0, 0)), (nw, Lp, C), F32),
            (
                pl.BlockSpec((Hh, C), lambda t: (0, jnp.maximum(t - g0, 0))),
                (Hh, T2 * C),
                BF16,
            ),
            (const(Hh, C), (Hh, C), BF16),
            (const(g, nw, cs, Lp), (g, nw, cs, Lp), BF16),
            (ANY, (2, nw, C), F32),
            (const(*state_shape), state_shape, F32),
            (ANY, (g, nw, cs, Lp), BF16),
        ],
        [
            pltpu.VMEM((wb, Lp + 2 * EDGE, C), F32),
            pltpu.VMEM((H, T2 * C), BF16),
            pltpu.VMEM((T2 * H, C), BF16),
            pltpu.VMEM((H, C), BF16),
            pltpu.VMEM((nw * Lp, T2 * C), BF16),
            pltpu.VMEM((nw, Lp, H), F32),
            pltpu.VMEM((nw, Lp, H), F32),
            pltpu.VMEM((M, H), F32),
            pltpu.VMEM((nw * Lp, H), BF16),
            pltpu.VMEM((H, nw * Lp), BF16),
            pltpu.VMEM((nw * Lp, C), BF16),
            pltpu.VMEM((M, T2 * H), BF16),
            pltpu.VMEM((H, nw * Lp), BF16),
            pltpu.VMEM(edges3, BF16),
            pltpu.VMEM(edges3, BF16),
            pltpu.VMEM((1, 2 * H), F32),
            pltpu.VMEM(edges3, BF16),
            pltpu.VMEM(edges3, BF16),
            pltpu.VMEM((2, C), F32),
            pltpu.VMEM((2, nw, C), F32),
            pltpu.VMEM((2, C), F32),
            pltpu.SemaphoreType.DMA((3, 2, 2)),
            pltpu.SemaphoreType.DMA((2, g)),
        ]
        + group.scratch(1, 2 * H)
        + group.scratch(2, C)
        + group.scratch(2, C),
        nw * Lp * C * H * (6 * T2 + 6),
        nw * Lp * C * 30,
        cid=3,
    )(lens, *[a for _, a in pairs])

    chips, rb = plan.chips, plan.rb
    turns_t = tail_turns(plan)

    def x_block(t):
        block = jnp.int32(0)
        for n, (what, k) in enumerate(turns_t):
            if what == "x":
                block = jnp.where(t >= n, k, block)
        return block

    sshape = (T1 + 2, 2, chips, rb, C // 2)
    pairs = ins(
        (early(wb, Lp, C), dz2),
        (whole(2, nw, C), dland2),
        (early(wb, Lp, C), x2),
        (early_land(C), land2),
        (cot_spec, cotangent),
        (whole(2, 3, nw, C), beyond),
        (
            pl.BlockSpec(
                (wb, L, Ch), lambda t: (grp() * steps + x_block(t), 0, half())
            ),
            inputs,
        ),
        (ANY, X5),
        (ANY, conv_weight),
        (whole(Hh, T2 * C), grads),
        (whole(Hh, C), pgrad),
        (whole(*state_shape), state),
        (half_of(STATE), state),
    )
    gz, gz_got, sums1, summed = call(
        tail_kernel,
        plan,
        "tail",
        len(turns_t),
        pairs,
        [
            (pl.BlockSpec((wb, cs, L), lambda t: (x_block(t), 0, 0)), (nw, cs, L), BF16),
            (ANY, (g, nw, cs, L), BF16),
            (const(2, Ch), (2, Ch), F32),
            (ANY, sshape, BF16),
        ],
        [
            pltpu.VMEM((wb, Lp + 16, C), F32),
            pltpu.VMEM((steps, M, 3 * C), BF16),
            pltpu.VMEM((Ch, nw * Lp), BF16),
            pltpu.VMEM((2 * Ch, 3 * C), BF16),
            pltpu.VMEM((L, L), BF16),
            pltpu.VMEM((Ch, Ch), BF16),
            pltpu.VMEM((2, Ch, L), F32),
            pltpu.VMEM((2 * Ch, max(M, C)), F32),
            pltpu.VMEM((g - 1, nw, cs, L), BF16),
            pltpu.VMEM((2, Ch, L), BF16),
            pltpu.VMEM((2, Ch, min(L, 128)), F32),
            pltpu.VMEM((2, nw * Lp, C), BF16),
            pltpu.SemaphoreType.DMA((3,)),
            pltpu.VMEM((T1, Ch, C), BF16),
            pltpu.SemaphoreType.DMA((2, g)),
        ]
        + Reduction.scratch(plan, tail_batches(plan))
        + group.scratch(2, C),
        2 * nw * Lp * (6 + T1) * C * Ch,
        nw * Lp * C * 40,
        cid=6,
    )(lens, *[a for _, a in pairs])

    wg = min(2 * wb, nw)
    count = NW // wg
    turn = nw // wg
    turns = min(count, chips)

    def own_block(t):
        return jnp.where(lax.div(t, turn) == grp(), lax.rem(t, turn), 0)

    def got_slot(t):
        off = lax.rem(grp() - lax.div(t, turn) + g, g)
        return jnp.maximum(off, 1), jnp.where(off > 0, lax.rem(t, turn), 0)

    pairs = ins(
        (pl.BlockSpec((wg, L, Ch), lambda t: (t, 0, half())), inputs),
        (pl.BlockSpec((wg, cs, L), lambda t: (own_block(t), 0, 0)), gz),
        (pl.BlockSpec((1, wg, cs, L), lambda t: got_slot(t) + (0, 0)), gz_got),
        (whole(2, Ch), sums1),
        (pl.BlockSpec((1, wg, cs, Lp), lambda t: (grp(), own_block(t), 0, 0)), res),
        (pl.BlockSpec((1, wg, cs, Lp), lambda t: got_slot(t) + (0, 0)), res_got),
        (
            pl.BlockSpec(
                (T1 + 2, 2, chips // turns, rb, C // 2),
                lambda t: (0, 0, t * turns // count, 0, 0),
            ),
            summed,
        ),
        (whole(*state_shape), state),
        (half_of(STATE), state),
    )
    outs = call(
        lambda plan, *refs: input_grad_kernel(plan, wg, *refs),
        plan,
        "input_grad",
        count,
        pairs,
        [
            (win(wg, cs, L), (NW, cs, L), BF16),
            (win(wg, cs, Lp), (NW, cs, Lp), BF16),
            (
                pl.BlockSpec((T1, cs // turns, C), lambda t: (0, t * turns // count, 0)),
                (T1, cs, C),
                F32,
            ),
            (const(T2, hs, C), (T2, hs, C), F32),
            (const(hs, C), (hs, C), F32),
        ]
        + [(const(1, n), (1, n), F32) for n in (cs, cs, cs, cs, hs, hs, cs)],
        [
            pltpu.VMEM((cs, Ch), BF16),
            pltpu.VMEM((3, cs, L), F32),
            pltpu.VMEM((Ch, L), F32),
        ],
        2 * NW * L * Ch * cs,
        NW * L * cs * 8,
    )(lens, *[a for _, a in pairs])
    grad, result, conv_grad, dil_grad, point_grad = outs[:5]
    g1, b1, g2, b2, g3, b3, pb = [a[0] for a in outs[5:]]
    return (
        jnp.swapaxes(result, 1, 2),
        jnp.swapaxes(grad, 1, 2),
        jnp.swapaxes(conv_grad, 1, 2),
        g1,
        b1,
        g2,
        b2,
        jnp.swapaxes(dil_grad, 1, 2),
        g3,
        b3,
        point_grad,
        pb,
    )


def solution(mesh):
    in_specs = (
        P(None, "seq", None),
        P(),
        P(),
        P(),
        P(),
        P("ch"),
        P("ch"),
        P(None, None, "ch"),
        P("ch"),
        P("ch"),
        P("ch", None),
        P("ch"),
        P(None, "seq", None),
    )
    out_specs = (
        P(None, "seq", "ch"),
        P(None, "seq", "ch"),
        P(None, None, "ch"),
        P("ch"),
        P("ch"),
        P("ch"),
        P("ch"),
        P(None, None, "ch"),
        P("ch"),
        P("ch"),
        P("ch", None),
        P("ch"),
    )
    return jax.shard_map(
        per_device, mesh=mesh, in_specs=in_specs, out_specs=out_specs, check_vma=False
    )
```

```python
from functools import partial
from typing import NamedTuple

import jax
import jax.numpy as jnp
from jax import lax
from jax.experimental import pallas as pl
from jax.experimental.pallas import tpu as pltpu
from jax.sharding import PartitionSpec as P

DIL = 14
EDGE = 16
EPS = 1e-05
GC0 = 0.7978845608028654
GC1 = 0.044715
F32 = jnp.float32
BF16 = jnp.bfloat16
MESH = pl.DeviceIdType.MESH
VMEM_LIMIT = 58 * 1024 * 1024
ANY = pl.BlockSpec(memory_space=pl.ANY)
SMEM = pl.BlockSpec(memory_space=pltpu.SMEM)


ST1, GAIN2, SHIFT2, BIAS, GAIN3, SHIFT3, GAIN1, SHIFT1, ST2, ST3, SU3, BSUM, SU2 = (
    0, 2, 3, 4, 5, 6, 7, 8, 9, 11, 13, 15, 16
)
STATE = 24


class Plan(NamedTuple):
    ns: int
    nz: int
    R: int
    NW: int
    L: int
    C: int
    H: int
    T1: int
    T2: int
    wb: int

    @property
    def g(self):
        return self.nz // self.R

    @property
    def nw(self):
        return self.NW // self.g

    @property
    def Lp(self):
        return self.L // 2

    @property
    def cs(self):
        return self.C // self.nz

    @property
    def Ch(self):
        return self.C // self.R

    @property
    def Hh(self):
        return self.H // self.R

    @property
    def steps(self):
        return self.nw // self.wb

    @property
    def chips(self):
        return self.ns // 2

    @property
    def rb(self):
        return self.cs // self.chips

    def place(self):
        s, z = lax.axis_index("seq"), lax.axis_index("ch")
        return s, z, lax.rem(z, self.g), lax.div(z, self.g)


def gelu(z):
    t = jnp.tanh(z * (GC0 + (GC0 * GC1) * (z * z)))
    return z * (0.5 + 0.5 * t)


def gelu_both(z):
    sq = z * z
    t = jnp.tanh(z * (GC0 + (GC0 * GC1) * sq))
    h = 0.5 + 0.5 * t
    v = z * h
    return v, h + v * (1.0 - t) * (GC0 + (3.0 * GC0 * GC1) * sq)


def gelu_slope(z):
    return gelu_both(z)[1]


def fold(v):
    return jnp.sum(v.reshape(v.shape[0] // 8, 8, v.shape[1]), axis=0)


def fold_lanes(v):
    out = v[:, 0:128]
    for k in range(128, v.shape[1], 128):
        out = out + v[:, k : k + 128]
    return out


def unfold(v):
    return jnp.sum(v, axis=0, keepdims=True)


def rows_of(shape):
    return lax.broadcasted_iota(jnp.int32, shape, 0)


def lanes_of(shape):
    return lax.broadcasted_iota(jnp.int32, shape, 1)


def total_of(lens):
    n = lens[0]
    for k in range(1, lens.shape[0]):
        n = n + lens[k]
    return n.astype(F32)


def norm_of(stats, total):
    mean = stats[0:1] / total
    square = stats[1:2] / total
    return mean, lax.rsqrt(square - mean * mean + EPS)


def flat(ref):
    return ref[...].reshape(1, ref.shape[0])


def column(row, n):
    return jnp.broadcast_to(row, (n, row.shape[1])).T


def mm(a, b):
    return jnp.dot(a, b, preferred_element_type=F32)


def mm_nt(a, b):
    return lax.dot_general(a, b, (((1,), (1,)), ((), ())), preferred_element_type=F32)


def mm_tn(a, b):
    return lax.dot_general(a, b, (((0,), (0,)), ((), ())), preferred_element_type=F32)


def mm_tt(a, b):
    return lax.dot_general(a, b, (((0,), (1,)), ((), ())), preferred_element_type=F32)


def eye_matrix(n, m, first):
    return jnp.where(lanes_of((n, m)) == rows_of((n, m)) + first, 1.0, 0.0).astype(BF16)


def pick_matrix(L):
    r, n = rows_of((L, L)), lanes_of((L, L))
    bin_of = 2 * r - jnp.where(r >= L // 2, L - 1, 0)
    return jnp.where(n == bin_of, 1.0, 0.0).astype(BF16)


def remote(src, dst, send, recv, device):
    return pltpu.make_async_remote_copy(
        src_ref=src,
        dst_ref=dst,
        send_sem=send,
        recv_sem=recv,
        device_id=device,
        device_id_type=MESH,
    )


def wrap(v, n):
    return jnp.where(v >= n, v - n, v)


def greet(devices):
    barrier = pltpu.get_barrier_semaphore()
    for device in devices:
        pl.semaphore_signal(barrier, inc=1, device_id=device, device_id_type=MESH)


def meet(devices):
    pl.semaphore_wait(pltpu.get_barrier_semaphore(), len(devices))


class Peers:
    def __init__(self, me, others):
        self.me, self.others = me, others
        self.count = len(others) + 1

    def start(self, link):
        packet, buf, sems = link
        for device in self.others:
            remote(packet, buf.at[self.me], sems.at[0], sems.at[1], device).start()

    def finish(self, link):
        packet, buf, sems = link
        buf[self.me] = packet[...]
        rest = buf.at[pl.ds(0, self.count - 1)]
        done = remote(rest, rest, sems.at[0], sems.at[1], self.others[0])
        done.wait_recv()
        acc = buf[0]
        for q in range(1, self.count):
            acc = acc + buf[q]
        done.wait_send()
        return acc

    def scratch(self, rows, width):
        return [
            pltpu.VMEM((rows, width), F32),
            pltpu.VMEM((self.count, rows, width), F32),
            pltpu.SemaphoreType.DMA((2,)),
        ]


def group_peers(plan):
    s, z, i, h = plan.place()
    g = plan.g
    others = [
        (wrap(s + a, plan.ns), h * g + wrap(i + b, g))
        for a in range(plan.ns)
        for b in range(g)
        if a or b
    ]
    return Peers(s * g + i, others)


def plane_peers(plan):
    s, z, i, h = plan.place()
    return Peers(s, [(wrap(s + a, plan.ns), z) for a in range(1, plan.ns)])


def line_peers(plan):
    s, z, i, h = plan.place()
    return Peers(z, [(s, wrap(z + a, plan.nz)) for a in range(1, plan.nz)])


class Halo:
    def __init__(self, plan, edge, land, sems):
        self.edge, self.land, self.sems = edge, land, sems
        s, z, _, _ = plan.place()
        self.to = ((wrap(s + plan.ns - 1, plan.ns), z), (wrap(s + 1, plan.ns), z))

    def copy(self, side, rows):
        return remote(
            self.edge.at[side, rows],
            self.land.at[1 - side, rows],
            self.sems.at[0, side],
            self.sems.at[1, side],
            self.to[side],
        )

    def start(self, first, count):
        for side in range(2):
            self.copy(side, pl.ds(first, count)).start()

    def finish(self):
        for side in range(2):
            done = self.copy(side, pl.ds(0, self.land.shape[1]))
            done.wait_recv()
            done.wait_send()


HALO_SEMS = pltpu.SemaphoreType.DMA((2, 2))


class Gather:
    def __init__(self, plan, part, full, sems):
        self.plan, self.part, self.full, self.sems = plan, part, full, sems
        self.s, self.z, self.i, self.h = plan.place()
        self.c, self.m = lax.rem(self.s, 2), lax.div(self.s, 2)
        self.chips = plan.chips
        self.every = self.chips // 4
        self.tap = lax.div(self.m, self.every)
        self.owner = lax.rem(self.m, self.every) == 0
        self.mine = full.at[self.c, self.tap]

    def others(self):
        g, nz = self.plan.g, self.plan.nz
        return [(self.s, wrap(self.h * g + g + r, nz)) for r in range(nz - g)]

    def far(self, off):
        return (2 * wrap(self.m + off, self.chips) + self.c, self.z)

    def own(self):
        return pltpu.make_async_copy(self.part, self.mine.at[self.z], self.sems.at[0, 0])

    def line(self, off):
        device = (self.s, wrap(self.z + off, self.plan.nz))
        return remote(
            self.part, self.mine.at[self.z], self.sems.at[0, 1], self.sems.at[1, 1], device
        )

    def chip(self, off):
        return remote(self.mine, self.mine, self.sems.at[0, 2], self.sems.at[1, 2], self.far(off))

    def pair(self):
        half = self.full.at[self.c]
        device = (2 * self.m + 1 - self.c, self.z)
        return remote(half, half, self.sems.at[0, 3], self.sems.at[1, 3], device)

    def line_start(self):
        @pl.when(self.owner)
        def _():
            self.own().start()
            for off in range(1, self.plan.nz):
                self.line(off).start()

    def line_finish(self):
        @pl.when(self.owner)
        def _():
            self.own().wait()
            rest = self.mine.at[pl.ds(0, self.plan.nz - 1)]
            device = (self.s, wrap(self.z + 1, self.plan.nz))
            done = remote(rest, rest, self.sems.at[0, 1], self.sems.at[1, 1], device)
            done.wait_recv()
            done.wait_send()

    def chips_start(self):
        @pl.when(self.owner)
        def _():
            for off in range(1, self.chips):
                self.chip(off).start()

    def pair_start(self):
        def taken(count):
            rest = self.full.at[self.c, pl.ds(0, count)]
            return remote(rest, rest, self.sems.at[0, 2], self.sems.at[1, 2], self.far(1))

        @pl.when(self.owner)
        def _():
            taken(3).wait_recv()
            for off in range(1, self.chips):
                self.chip(off).wait_send()

        if self.every > 1:

            @pl.when(jnp.logical_not(self.owner))
            def _():
                taken(4).wait_recv()

        self.pair().start()

    def pair_finish(self):
        done = self.pair()
        done.wait_recv()
        done.wait_send()


def first_step():
    return pl.program_id(0) == 0


def last_step():
    return pl.program_id(0) == pl.num_programs(0) - 1


def head_kernel(plan, nm, lens, x, xtop, xend, ctop, cend, g2, s2, pb, g3, s3,
                w_hbm, gain, shift, taps, pw,
                X5, x2, land, state, beyond_out, full,
                macc, beyond, xedge, sel, edge, acc, w_ref, w_sem, part,
                gather_sems, xhalo_sems, halo_sems, *links):
    t = pl.program_id(0)
    peers, plane, line = group_peers(plan), plane_peers(plan), line_peers(plan)
    xhalo = Halo(plan, xedge, beyond, xhalo_sems)
    halo = Halo(plan, edge, land, halo_sems)
    gather = Gather(plan, part, full, gather_sems)
    w_copy = pltpu.make_async_copy(w_hbm, w_ref, w_sem)
    plane_link, line_link, link = links[:3], links[3:6], links[6:]
    s, z, i, h = plan.place()
    L, Lp, C, nw, nz, wb = plan.L, plan.Lp, plan.C, plan.nw, plan.nz, plan.wb
    share = plan.NW // nz
    c = t - nm
    everyone = peers.others + gather.others()

    @pl.when(first_step())
    def _():
        w_copy.start()
        greet(everyone)
        part[...] = jnp.where(gather.tap == 3, pw[...], taps[0])
        macc[...] = jnp.zeros_like(macc)
        acc[...] = jnp.zeros_like(acc)
        state[...] = jnp.zeros_like(state)
        state[GAIN1 : GAIN1 + 1] = flat(gain)
        state[SHIFT1 : SHIFT1 + 1] = flat(shift)
        n16 = nw * 16
        for side, (xe, ce, places) in enumerate(
            ((xtop, ctop, (0, 1, 0)), (xend, cend, (14, 15, 15)))
        ):
            for k, at in enumerate(places):
                rows, lanes = rows_of((nw, n16)), lanes_of((nw, n16))
                one = jnp.where(lanes == 16 * rows + at, 1.0, 0.0).astype(BF16)
                block = (xe if k < 2 else ce)[...].reshape(n16, C)
                xedge[side, k] = mm(one, block)
        shape = (Lp, L)
        for k in range(plan.T1):
            at = lanes_of(shape) - (2 * rows_of(shape) + (k - 2))
            sel[k * Lp : (k + 1) * Lp] = jnp.where((at == 0) | (at == 1), 1.0, 0.0).astype(BF16)

    @pl.when(c < 0)
    def _():
        rows = rows_of((L, C))
        for w in range(min(share, wb)):
            at = lax.rem(z * share, wb) + w
            valid = 2 * lens[z * share + t * wb + w] - s * L
            v = jnp.where(rows < valid, x[at].astype(F32), 0.0)
            macc[0] += fold(v)
            macc[1] += fold(v * v)

    @pl.when(c == -1)
    def _():
        packet, more = plane_link[0], line_link[0]
        packet[0:1] = unfold(macc[0])
        packet[1:2] = unfold(macc[1])
        meet(everyone)
        plane.start(plane_link)
        xhalo.start(0, 3)
        at = 0
        spans = []
        more[2:3] = jnp.zeros((1, C), F32)
        for ref in (g2, s2, pb, g3, s3):
            n = ref.shape[1]
            more[2:3, at : at + n] = ref[...]
            spans.append((at, n))
            at += n
        more[0:2] = plane.finish(plane_link)
        line.start(line_link)
        gather.line_start()
        state[ST1 : ST1 + 2] = line.finish(line_link)[0:2]
        for k in range(nz):
            row = line_link[1][k]
            for r, (at, n) in zip((GAIN2, SHIFT2, BIAS, GAIN3, SHIFT3), spans):
                state[r : r + 1, k * n : (k + 1) * n] = row[2:3, at : at + n]
        xhalo.finish()
        beyond_out[...] = beyond[...]
        w_copy.wait()

    @pl.when(c >= 0)
    def _():
        mean, rho = norm_of(state[ST1 : ST1 + 2], 2.0 * total_of(lens))
        scale = state[GAIN1 : GAIN1 + 1] * rho
        offset = state[SHIFT1 : SHIFT1 + 1] - mean * scale
        rows = rows_of((L, C))
        row1 = rows_of((1, C))
        row16 = rows_of((16, C))
        def activate(w):
            at = c * wb + w
            valid = 2 * lens[i * nw + at] - s * L
            a = gelu(x[w].astype(F32) * scale + offset)
            a = jnp.where(rows < valid, a, 0.0).astype(BF16)
            picked = mm(sel[...], a)
            for k in range(5):
                X5[k, w * Lp : (w + 1) * Lp] = picked[k * Lp : (k + 1) * Lp].astype(BF16)

            def beside(side, k, bin_at):
                a = gelu(beyond[side, k, pl.ds(at, 1), :] * scale + offset)
                here = (row1 + bin_at < valid) & (row1 + (s * L + bin_at) >= 0)
                return jnp.where(here, a, 0.0).astype(BF16).astype(F32)

            l0, l1 = beside(0, 0, -2), beside(0, 1, -1)
            r0, r1 = beside(1, 0, L), beside(1, 1, L + 1)
            top, end = w * Lp, (w + 1) * Lp
            for k, add in ((0, l0 + l1), (1, l1)):
                X5[k, top : top + 16] = (
                    picked[k * Lp : k * Lp + 16] + jnp.where(row16 == 0, add, 0.0)
                ).astype(BF16)
            for k, add in ((3, r0), (4, r0 + r1)):
                X5[k, end - 16 : end] = (
                    picked[(k + 1) * Lp - 16 : (k + 1) * Lp] + jnp.where(row16 == 15, add, 0.0)
                ).astype(BF16)

        nc = 256
        rowp = rows_of((Lp, nc))

        def convolve(first, count):
            span = slice(first * Lp, (first + count) * Lp)
            for n in range(C // nc):
                cols = slice(n * nc, (n + 1) * nc)
                taps = [X5[k, span] for k in range(plan.T1)]
                y = 0.5 * mm(jnp.concatenate(taps, axis=1), w_ref[:, cols])
                s0 = jnp.zeros((8, nc), F32)
                s1 = jnp.zeros((8, nc), F32)
                for w in range(first, first + count):
                    at = c * wb + w
                    valid = lens[i * nw + at] - s * Lp
                    v = y[(w - first) * Lp : (w - first + 1) * Lp]
                    x2[w, :, cols] = v
                    edge[0, at, :, cols] = v[:EDGE].astype(BF16)
                    edge[1, at, :, cols] = v[Lp - EDGE :].astype(BF16)
                    v = jnp.where(rowp < valid, v, 0.0)
                    s0 = s0 + fold(v)
                    s1 = s1 + fold(v * v)
                acc[0:1, cols] += unfold(s0)
                acc[1:2, cols] += unfold(s1)

        count = max(1, wb // 2)
        for first in range(0, wb, count):
            for w in range(first, first + count):
                activate(w)
            convolve(first, count)
        halo.start(c * wb, wb)

    @pl.when(c == 0)
    def _():
        gather.line_finish()
        gather.chips_start()

    @pl.when(last_step())
    def _():
        link[0][...] = acc[...]
        peers.start(link)
        gather.pair_start()
        state[ST2 : ST2 + 2] = peers.finish(link)
        halo.finish()
        gather.pair_finish()


def block_kernel(plan, lens, x2, x2_hbm, x2land, cot, w_ref, pw_ref, old, half_state,
                 dz2, grads, pgrad, res, land, state, res_got,
                 ext, wf, wt, pw, Y3, c2, dz3, das, a3s, a3T, dos, Z3, dcT,
                 cedge, cland, cacc, dedge, dland, dacc, bedge, bacc, halo_sems, bulk_sems,
                 x2half, x2_sem, *links):
    t = pl.program_id(0)
    peers = group_peers(plan)
    s, z, i, h = plan.place()
    Lp, C, H, wb, nw, cs, g = plan.Lp, plan.C, plan.H, plan.wb, plan.nw, plan.cs, plan.g
    M = wb * Lp
    steps = plan.steps
    p0, r0, b0, g0 = block_phases(plan)[:4]
    c_link, d_link, b_link = links[:3], links[3:6], links[6:]
    c_halo = Halo(plan, cedge, cland, halo_sems.at[0])
    d_halo = Halo(plan, dedge, dland, halo_sems.at[1])
    b_halo = Halo(plan, bedge, land, halo_sems.at[2])

    def bulk(off, rows):
        to = wrap(i + off, g)
        return remote(
            res.at[to, rows],
            res_got.at[off, rows],
            bulk_sems.at[0, off],
            bulk_sems.at[1, off],
            (s, h * g + to),
        )

    def result_of(block):
        y = mm(a3s[pl.ds(pl.multiple_of(block * M, 128), M)], pw_ref[h, 0])
        rowr = rows_of((Lp, y.shape[1]))
        for w in range(wb):
            at = block * wb + w
            valid = lens[i * plan.nw + at] - s * Lp
            r = x2half[at] + y[w * Lp : (w + 1) * Lp] + half_state[BIAS : BIAS + 1]
            r = jnp.where(rowr < valid, r, 0.0).astype(BF16).T
            for k in range(g):
                res[k, at] = r[k * cs : (k + 1) * cs]

    def send_result(block):
        result_of(block)
        for off in range(1, g):
            bulk(off, pl.ds(block * wb, wb)).start()

    half_copy = pltpu.make_async_copy(
        x2_hbm.at[:, :, pl.ds(pl.multiple_of(h * plan.Ch, 128), plan.Ch)], x2half, x2_sem
    )

    @pl.when(first_step())
    def _():
        half_copy.start()
        greet(peers.others)
        state[...] = old[...]
        cacc[...] = jnp.zeros_like(cacc)
        dacc[...] = jnp.zeros_like(dacc)
        bacc[...] = jnp.zeros_like(bacc)
        for c in range(2):
            cols = slice(c * (C // 2), (c + 1) * (C // 2))
            pw[:, cols] = pw_ref[c, 0]
            for k in range(plan.T2):
                at = k * C + c * (C // 2)
                wf[:, at : at + C // 2] = w_ref[c, k]
                wt[k * H : (k + 1) * H, cols] = w_ref[c, k]

    @pl.when(t < p0)
    def _():
        base = pl.multiple_of(t * M, 128)
        mean, rho = norm_of(state[ST2 : ST2 + 2], total_of(lens))
        scale = state[GAIN2 : GAIN2 + 1] * rho
        offset = state[SHIFT2 : SHIFT2 + 1] - mean * scale
        rows = rows_of((Lp, C))
        rowe = rows_of((EDGE, C))

        rowh = rows_of((Lp, H))
        sums0, sums1 = jnp.zeros((8, H), F32), jnp.zeros((8, H), F32)
        nh = min(2, wb)
        for first in range(0, wb, wb // nh):
            span = range(first, first + wb // nh)
            for w in span:
                valid = lens[i * plan.nw + t * wb + w] - s * Lp
                a = jnp.where(rows < valid, gelu(x2[w] * scale + offset), 0.0)
                al = gelu(x2land[0, w].astype(F32) * scale + offset)
                al = jnp.where((rowe - EDGE < valid) & (s > 0), al, 0.0)
                ah = gelu(x2land[1, w].astype(F32) * scale + offset)
                ah = jnp.where(rowe + Lp < valid, ah, 0.0)
                ext[w, 0:EDGE] = al
                ext[w, EDGE : EDGE + Lp] = a
                ext[w, EDGE + Lp :] = ah
                top, end = w * Lp, (w + 1) * Lp
                Y3[pl.ds(base + top, Lp), 0:C] = ext[w, EDGE - DIL : EDGE - DIL + Lp].astype(BF16)
                Y3[pl.ds(base + top, Lp), C : 2 * C] = a.astype(BF16)
                Y3[pl.ds(base + top, Lp), 2 * C : 3 * C] = ext[w, EDGE + DIL : EDGE + DIL + Lp].astype(BF16)
            y = mm_nt(Y3[pl.ds(base + first * Lp, wb // nh * Lp)], wf[...])
            for w in span:
                at = t * wb + w
                valid = lens[i * plan.nw + at] - s * Lp
                v = y[(w - first) * Lp : (w - first + 1) * Lp]
                c2[at] = v
                cedge[0, at] = v[:EDGE].astype(BF16)
                cedge[1, at] = v[Lp - EDGE :].astype(BF16)
                v = jnp.where(rowh < valid, v, 0.0)
                sums0 = sums0 + fold(v)
                sums1 = sums1 + fold(v * v)
        cacc[0:1, 0:H] += unfold(sums0)
        cacc[0:1, H:] += unfold(sums1)

    @pl.when(first_step())
    def _():
        meet(peers.others)

    @pl.when(t < p0)
    def _():
        c_halo.start(t * wb, wb)

    @pl.when(t == p0 - 1)
    def _():
        c_link[0][...] = cacc[...]
        peers.start(c_link)

    here_p = (t >= p0) & (t < p0 + steps)

    @pl.when(here_p)
    def _():
        u = t - p0
        rowc = rows_of((Lp, C))
        block = pl.ds(pl.multiple_of(u * M, 128), M)
        bias = jnp.zeros((8, C), F32)
        parts = []
        for w in range(wb):
            valid = lens[i * plan.nw + u * wb + w] - s * Lp
            d = jnp.where(rowc < valid, cot[w].astype(F32), 0.0)
            bias = bias + fold(d)
            parts.append(d.astype(BF16))
        d = jnp.concatenate(parts, axis=0)
        dos[block] = d
        das[...] = mm_nt(d, pw[...])
        dacc[1:2] += unfold(bias)

    @pl.when(t == p0)
    def _():
        got = peers.finish(c_link)
        state[ST3 : ST3 + 1, 0:H] = got[:, 0:H]
        state[ST3 + 1 : ST3 + 2, 0:H] = got[:, H:]

    @pl.when(here_p)
    def _():
        u = t - p0
        block = pl.ds(pl.multiple_of(u * M, 128), M)
        rowh = rows_of((Lp, H))
        mean, rho = norm_of(state[ST3 : ST3 + 2, 0:H], total_of(lens))
        scale = state[GAIN3 : GAIN3 + 1, 0:H] * rho
        offset = state[SHIFT3 : SHIFT3 + 1, 0:H] - mean * scale
        s0, s1 = jnp.zeros((8, H), F32), jnp.zeros((8, H), F32)
        parts = []
        for w in range(wb):
            at = u * wb + w
            valid = lens[i * plan.nw + at] - s * Lp
            top, end = w * Lp, (w + 1) * Lp
            v = c2[at]
            zv = v * scale + offset
            act, slope = gelu_both(zv)
            parts.append(jnp.where(rowh < valid, act, 0.0).astype(BF16))
            dzw = das[top:end] * slope
            dz3[at] = dzw
            dedge[0, at] = dzw[:EDGE].astype(BF16)
            dedge[1, at] = dzw[Lp - EDGE :].astype(BF16)
            s0 = s0 + fold(dzw)
            s1 = s1 + fold(dzw * zv)
        a3 = jnp.concatenate(parts, axis=0)
        a3s[block] = a3
        a3T[:, block] = a3.T
        dacc[0:1, 0:H] += unfold(s0)
        dacc[0:1, H : 2 * H] += unfold(s1)
        d_halo.start(u * wb, wb)

    @pl.when(t == p0)
    def _():
        half_copy.wait()
        send_result(0)

    @pl.when(t == p0 + steps - 1)
    def _():
        d_link[0][...] = dacc[...]
        peers.start(d_link)

    @pl.when(t == r0)
    def _():
        for block in range(1, steps):
            send_result(block)
        rows = pl.ds(pl.multiple_of(h * plan.Hh, 16), plan.Hh)
        pgrad[...] = mm(a3T[rows], dos[...]).astype(BF16)

    @pl.when(t == b0)
    def _():
        got = peers.finish(d_link)
        shift = state[SHIFT3 : SHIFT3 + 1, 0:H]
        gain = state[GAIN3 : GAIN3 + 1, 0:H]
        state[SU3 : SU3 + 1, 0:H] = got[0:1, 0:H]
        state[SU3 + 1 : SU3 + 2, 0:H] = (got[0:1, H : 2 * H] - shift * got[0:1, 0:H]) / gain
        state[BSUM : BSUM + 1] = got[1:2]
        c_halo.finish()
        d_halo.finish()

    @pl.when((t >= b0) & (t < g0))
    def _():
        u = t - b0
        total = total_of(lens)
        mean3, rho3 = norm_of(state[ST3 : ST3 + 2, 0:H], total)
        gr3 = state[GAIN3 : GAIN3 + 1, 0:H] * rho3
        sg3 = state[SU3 : SU3 + 1, 0:H] / total
        gg3 = state[SU3 + 1 : SU3 + 2, 0:H] / total
        mean2, rho2 = norm_of(state[ST2 : ST2 + 2], total)
        scale2 = state[GAIN2 : GAIN2 + 1] * rho2
        offset2 = state[SHIFT2 : SHIFT2 + 1] - mean2 * scale2
        rowh = rows_of((Lp, H))
        rowe = rows_of((EDGE, H))
        rowc = rows_of((Lp, C))

        by_v = -gr3 * rho3 * gg3
        by_1 = gr3 * (mean3 * rho3 * gg3 - sg3)

        def back(dz, v):
            return gr3 * dz + by_v * v + by_1

        for w in range(wb):
            valid = lens[i * nw + u * wb + w] - s * Lp
            d = jnp.where(rowh < valid, back(dz3[u * wb + w], c2[u * wb + w]), 0.0)
            dl = back(dland[0, u * wb + w].astype(F32), cland[0, u * wb + w].astype(F32))
            dl = jnp.where((rowe - EDGE < valid) & (s > 0), dl, 0.0)
            dh = back(dland[1, u * wb + w].astype(F32), cland[1, u * wb + w].astype(F32))
            dh = jnp.where(rowe + Lp < valid, dh, 0.0)
            ext[w, 0:EDGE, 0:H] = dl
            ext[w, EDGE : EDGE + Lp, 0:H] = d
            ext[w, EDGE + Lp :, 0:H] = dh
            top, end = w * Lp, (w + 1) * Lp
            Z3[top:end, 0:H] = ext[w, EDGE + DIL : EDGE + DIL + Lp, 0:H].astype(BF16)
            Z3[top:end, H : 2 * H] = d.astype(BF16)
            Z3[top:end, 2 * H : 3 * H] = ext[w, EDGE - DIL : EDGE - DIL + Lp, 0:H].astype(BF16)

        y = mm(Z3[...], wt[...])

        M = wb * Lp
        dcT[:, pl.ds(pl.multiple_of(u * M, 128), M)] = Z3[:, H : 2 * H].T
        s0, s1 = jnp.zeros((8, C), F32), jnp.zeros((8, C), F32)
        for w in range(wb):
            at = u * wb + w
            valid = lens[i * nw + at] - s * Lp
            v = x2[w]
            zv = v * scale2 + offset2
            dzw = y[w * Lp : (w + 1) * Lp] * gelu_slope(zv)
            dzw = jnp.where(rowc < valid, dzw, 0.0)
            dz2[w] = dzw
            bedge[0, pl.ds(at, 1)] = dzw[0:1]
            bedge[1, pl.ds(at, 1)] = dzw[Lp - 1 : Lp]
            s0 = s0 + fold(dzw)
            s1 = s1 + fold(dzw * zv)
        bacc[0:1] += unfold(s0)
        bacc[1:2] += unfold(s1)

    @pl.when(t == g0 - 1)
    def _():
        b_link[0][...] = bacc[...]
        peers.start(b_link)
        b_halo.start(0, nw)

    @pl.when(last_step())
    def _():
        rows = pl.ds(pl.multiple_of(h * plan.Hh, 16), plan.Hh)
        for n in range(plan.T2):
            cols = slice(n * C, (n + 1) * C)
            grads[:, cols] = mm(dcT[rows], Y3[:, cols]).astype(BF16)

    @pl.when(last_step())
    def _():
        got = peers.finish(b_link)
        shift, gain = state[SHIFT2 : SHIFT2 + 1], state[GAIN2 : GAIN2 + 1]
        state[SU2 : SU2 + 1] = got[0:1]
        state[SU2 + 1 : SU2 + 2] = (got[1:2] - shift * got[0:1]) / gain
        b_halo.finish()
        for off in range(1, g):
            bulk(off, pl.ds(0, nw)).wait()


def block_phases(plan):
    n = plan.steps
    return n, 2 * n, 2 * n + 1, 3 * n + 1, 3 * n + 2


class Reduction:
    def __init__(self, plan, batches, out, give, mine, got, spread, half, mate, sems):
        self.plan, self.batches, self.out = plan, batches, out
        self.give, self.mine, self.got, self.spread = give, mine, got, spread
        self.half, self.mate = half, mate
        self.sems = sems
        self.s, self.z, self.i, self.h = plan.place()
        self.c = lax.rem(self.s, 2)
        self.m = lax.div(self.s, 2)
        self.chips = plan.chips

    @staticmethod
    def scratch(plan, batches):
        taps, wide = plan.T1 + 2, plan.C // 2
        full = (taps, plan.chips, plan.g, plan.rb, wide)
        part = (taps, plan.g, plan.rb, wide)
        return [
            pltpu.VMEM((taps, 2, plan.chips, plan.rb, wide), BF16),
            *[pltpu.VMEM(full, BF16)] * 4,
            *[pltpu.VMEM(part, BF16)] * 2,
            pltpu.SemaphoreType.DMA((2, len(batches), 5)),
        ]

    def copy(self, b, phase, src, dst, device):
        return remote(src, dst, self.sems.at[0, b, phase], self.sems.at[1, b, phase], device)

    def finish(self, b, phase, ref, device):
        done = self.copy(b, phase, ref, ref, device)
        done.wait_recv()
        done.wait_send()

    def taps(self, b):
        return pl.ds(*self.batches[b])

    def pair(self):
        return (2 * self.m + (1 - self.c), self.z)

    def far(self, off):
        return (2 * wrap(self.m + off, self.chips) + self.c, self.z)

    def member(self, off):
        return (self.s, self.h * self.plan.g + wrap(self.i + off, self.plan.g))

    def put(self, k, rows):
        wide = self.plan.C // 2
        for j in range(self.plan.g):
            for m in range(self.chips):
                v = rows(j, m)
                left, right = v[:, :wide], v[:, wide:]
                self.mine[k, m, j] = jnp.where(self.c == 0, left, right).astype(BF16)
                self.give[k, m, j] = jnp.where(self.c == 0, right, left).astype(BF16)

    def step0(self, b):
        taps = self.taps(b)
        self.copy(b, 0, self.give.at[taps], self.got.at[taps], self.pair()).start()

    def step1(self, b):
        taps = self.taps(b)
        self.finish(b, 0, self.got.at[taps], self.pair())
        first, count = self.batches[b]
        for k in range(first, first + count):
            v = self.mine[k].astype(F32) + self.got[k].astype(F32)
            self.mine[k] = v.astype(BF16)
        for off in range(1, self.chips):
            src = self.mine.at[taps, wrap(self.m + off, self.chips)]
            self.copy(b, 1, src, self.spread.at[taps, self.m], self.far(off)).start()

    def step2(self, b):
        taps = self.taps(b)
        self.finish(b, 1, self.spread.at[taps, pl.ds(0, self.chips - 1)], self.far(1))
        first, count = self.batches[b]
        for k in range(first, first + count):
            self.spread[k, self.m] = self.mine[k, self.m]
            v = self.spread[k, 0].astype(F32)
            for n in range(1, self.chips):
                v = v + self.spread[k, n].astype(F32)
            self.half[k] = v.astype(BF16)
        for off in range(1, self.plan.g):
            src = self.half.at[taps, wrap(self.i + off, self.plan.g)]
            self.copy(b, 2, src, self.mate.at[taps, off], self.member(off)).start()

    def step3(self, b):
        taps = self.taps(b)
        self.finish(b, 2, self.mate.at[taps, pl.ds(1, self.plan.g - 1)], self.member(1))
        first, count = self.batches[b]
        for k in range(first, first + count):
            v = self.half[k, self.i].astype(F32)
            for off in range(1, self.plan.g):
                v = v + self.mate[k, off].astype(F32)
            self.out[k, self.c, self.m] = v.astype(BF16)
        mine = self.out.at[taps, self.c, self.m]
        for off in range(1, self.chips):
            self.copy(b, 3, mine, mine, self.far(off)).start()

    def step4(self, b):
        taps = self.taps(b)
        self.finish(b, 3, self.out.at[taps, self.c, pl.ds(0, self.chips - 1)], self.far(1))
        mine = self.out.at[taps, self.c]
        self.copy(b, 4, mine, mine, self.pair()).start()

    def step5(self, b):
        self.finish(b, 4, self.out.at[self.taps(b), self.c], self.pair())


def tail_turns(plan):
    nD = plan.steps
    first = max(nD - 1, 1)
    turns = [("x", n) for n in range(first)] + [("d", n) for n in range(first, nD)]
    turns += [("w", 0)]
    return turns + [("x", n) for n in range(first, nD)]


def tail_batches(plan):
    return [(plan.T1, 2), (0, 2), (2, 2), (4, plan.T1 - 4)]


def tail_kernel(plan, lens, dz2, dzland, x2, x2land, cot, beyond, x, X5_hbm, taps_hbm, grads, pgrad,
                old, half_state,
                gz, gz_got, sums, summed,
                ext, D3, D0T, wcat, pick, eye, cols, y, part, split, acc, X5, X5_sems,
                taps, bulk_sems, *rest):
    t = pl.program_id(0)
    s, z, i, h = plan.place()
    L, Lp, C, wb, g, nw = plan.L, plan.Lp, plan.C, plan.wb, plan.g, plan.nw
    Ch, cs, T1 = plan.Ch, plan.cs, plan.T1
    M = wb * Lp
    nD = plan.steps
    turns = tail_turns(plan)
    last = len(turns) - 1
    peers = group_peers(plan)
    red = Reduction(plan, tail_batches(plan), *rest[:8])
    link = rest[8:]

    def member(off):
        return (s, h * g + wrap(i + off, g))

    def send(first, count):
        rows = pl.ds(first, count)
        for off in range(1, g):
            remote(
                part.at[off - 1, rows],
                gz_got.at[off, rows],
                bulk_sems.at[0, off],
                bulk_sems.at[1, off],
                member(off),
            ).start()

    def X5_copy(k):
        return pltpu.make_async_copy(X5_hbm.at[k], X5.at[k % 2], X5_sems.at[k % 2])

    def when(at):
        return pl.when(t == min(at, last))

    def turn(kind, k):
        return turns.index((kind, k)) if (kind, k) in turns else last

    def turn_of(kind):
        index = jnp.int32(0)
        here = False
        for n, (what, k) in enumerate(turns):
            if what == kind:
                index = jnp.where(t == n, k, index)
                here = (t == n) | here
        return here, index

    taps_copy = pltpu.make_async_copy(
        taps_hbm.at[:, pl.ds(pl.multiple_of(h * Ch, 128), Ch)], taps, X5_sems.at[2]
    )

    @when(0)
    def _():
        taps_copy.start()
        greet(peers.others)
        acc[...] = jnp.zeros_like(acc)
        pick[...] = pick_matrix(L)
        eye[...] = eye_matrix(Ch, Ch, 0)
        mean, rho = norm_of(half_state[ST1 : ST1 + 2], 2.0 * total_of(lens))
        scale = half_state[GAIN1 : GAIN1 + 1] * rho
        offset = half_state[SHIFT1 : SHIFT1 + 1] - mean * scale
        for k, row in enumerate((scale, offset)):
            cols[k] = column(row, L)

    @pl.when(t < nD)
    def _():
        total = total_of(lens)
        mean, rho = norm_of(old[ST2 : ST2 + 2], total)
        gr = old[GAIN2 : GAIN2 + 1] * rho
        sg = old[SU2 : SU2 + 1] / total
        gg = old[SU2 + 1 : SU2 + 2] / total
        rowc = rows_of((Lp, C))
        row1 = rows_of((1, C))

        by_dz = 0.5 * gr
        by_v = -0.5 * gr * rho * gg
        by_1 = 0.5 * gr * (mean * rho * gg - sg)

        def back(dout, dz, v):
            return 0.5 * dout + by_dz * dz + by_v * v + by_1

        def grad_of(w):
            at = t * wb + w
            valid = lens[i * nw + at] - s * Lp
            d = back(cot[w].astype(F32), dz2[w], x2[w])
            d = jnp.where(rowc < valid, d, 0.0)
            one = pl.ds(at, 1)
            dl = back(beyond[0, 2, one, :], dzland[0, one, :], x2land[0, w, EDGE - 1 : EDGE].astype(F32))
            dl = jnp.where((row1 - 1 < valid) & (s > 0), dl, 0.0)
            dh = back(beyond[1, 2, one, :], dzland[1, one, :], x2land[1, w, 0:1].astype(F32))
            dh = jnp.where(row1 + Lp < valid, dh, 0.0)
            ext[w, 7:8] = dl
            ext[w, 8 : 8 + Lp] = d
            ext[w, 8 + Lp : 9 + Lp] = dh
            top, end = w * Lp, (w + 1) * Lp
            D3[t, top:end, 0:C] = ext[w, 9 : 9 + Lp].astype(BF16)
            D3[t, top:end, C : 2 * C] = d.astype(BF16)
            D3[t, top:end, 2 * C : 3 * C] = ext[w, 7 : 7 + Lp].astype(BF16)

        for w in range(wb):
            grad_of(w)
        half = D3[t, :, pl.ds(pl.multiple_of(C + h * Ch, 128), Ch)]
        D0T[:, pl.ds(pl.multiple_of(t * M, 128), M)] = half.T

    @when(0)
    def _():
        taps_copy.wait()
        for first in range(0, Ch, 64):
            rows = slice(first, min(first + 64, Ch))
            for r, parts in enumerate((((0,), (1, 2), (3, 4)), ((0, 1), (2, 3), (4,)))):
                for k, which in enumerate(parts):
                    v = taps[which[0], rows]
                    if len(which) > 1:
                        v = (v.astype(F32) + taps[which[1], rows].astype(F32)).astype(BF16)
                    at = r * Ch
                    wcat[at + rows.start : at + rows.stop, k * C : (k + 1) * C] = v
        meet(peers.others)

    here_x, bx = turn_of("x")

    def gradient(hf, nh):
        lanes = lanes_of((Ch, L))

        def through(w):
            valid = 2 * lens[i * nw + bx * wb + w] - s * L
            top, end = w * Lp, (w + 1) * Lp
            v = mm_nt(eye[...], x[w])
            da = jnp.concatenate([y[0:Ch, top:end], y[Ch:, top:end]], axis=1)
            da = mm(da.astype(BF16), pick[...])
            zv = v * cols[0] + cols[1]
            dzw = da * gelu_slope(zv)
            dzw = jnp.where(lanes < valid, dzw, 0.0)
            acc[0] += fold_lanes(dzw)
            acc[1] += fold_lanes(dzw * zv)
            split[w % 2] = dzw.astype(BF16)
            for off in range(g):
                rows = pl.ds(pl.multiple_of(lax.rem(i + off, g) * cs, 16), cs)
                if off == 0:
                    gz[w] = split[w % 2, rows]
                else:
                    part[off - 1, bx * wb + w] = split[w % 2, rows]

        n = wb // nh
        rows = slice(hf * n * Lp, (hf + 1) * n * Lp)
        y[:, rows] = mm_nt(wcat[...], D3[bx, rows])
        for w in range(hf * n, (hf + 1) * n):
            through(w)

    nh = 2 if wb % 2 == 0 and wb * Lp // 2 % 128 == 0 else 1

    @pl.when(here_x)
    def _():
        gradient(0, nh)
        send(bx * wb, wb // nh)

    for step, batch in ((red.step1, 3), (red.step2, 1)):

        @when(last)
        def _():
            if nh == 2 and turns[last][0] == "x":
                step(batch)

    if nh == 2:

        @pl.when(here_x)
        def _():
            gradient(1, nh)

    @pl.when(here_x & (bx < nD - 1))
    def _():
        if nh == 2:
            send(bx * wb + wb // nh, wb // nh)

    @when(0)
    def _():
        hs = plan.H // plan.nz
        rb = plan.rb
        for u in range(2):

            def rows(j, m, u=u):
                side, r = m * rb // hs, m * rb % hs
                n = 2 * side + u
                rows = slice(j * hs + r, j * hs + r + rb)
                v = grads[rows, n * C : (n + 1) * C] if n < plan.T2 else pgrad[rows]
                return v.astype(F32)

            red.put(T1 + u, rows)
        red.step0(0)

    @when(0)
    def _():
        X5_copy(0).start()
        X5_copy(1).start()

    @when(turn("w", 0))
    def _():
        rb = plan.rb
        for k in range(T1):
            X5_copy(k).wait()
            tap = mm(D0T[...], X5[k % 2])
            if k + 2 < T1:
                X5_copy(k + 2).start()
            red.put(k, lambda j, m: tap[j * cs + m * rb : j * cs + (m + 1) * rb])
            if k == 1:
                red.step0(1)
            if k == 3:
                red.step1(1)
                red.step0(2)
        red.step0(3)
        red.step1(2)

    @when(turn("x", nD - 1))
    def _():
        packet = link[0]
        packet[...] = jnp.zeros_like(packet)
        packet[0:1, 0:Ch] = jnp.sum(acc[0].T, axis=0, keepdims=True)
        packet[1:2, 0:Ch] = jnp.sum(acc[1].T, axis=0, keepdims=True)
        peers.start(link)

    ends = nh == 2 and turns[last][0] == "x"
    for at, step, batch in (
        (1, red.step1, 0),
        (max(nD - 1, 2), red.step2, 0),
        *(() if ends else ((last, red.step1, 3), (last, red.step2, 1))),
        (last, red.step2, 2),
        (last, red.step3, 0),
        (last, red.step3, 1),
        (last, red.step2, 3),
    ):

        @when(at)
        def _():
            step(batch)

    @when(last)
    def _():
        if nh == 2:
            send(nw - wb // 2, wb // 2)

    @when(last)
    def _():
        red.step3(2)
        red.step4(0)
        red.step4(1)
        red.step3(3)
        red.step4(2)
        got = peers.finish(link)[:, 0:Ch]
        shift, gain = half_state[SHIFT1 : SHIFT1 + 1], half_state[GAIN1 : GAIN1 + 1]
        sums[0:1] = got[0:1]
        sums[1:2] = (got[1:2] - shift * got[0:1]) / gain
        red.step4(3)
        for b in range(4):
            red.step5(b)
        own = pltpu.make_async_copy(red.out, summed, X5_sems.at[0])
        own.start()
        for off in range(1, g):
            done = remote(
                part.at[off - 1],
                gz_got.at[off],
                bulk_sems.at[0, off],
                bulk_sems.at[1, off],
                member(off),
            )
            done.wait_recv()
            done.wait_send()
        own.wait()


def input_grad_kernel(plan, wg, lens, x, gz, gz_got, sums, res, res_got, summed,
                      state, half_state,
                      out, out_result, conv_grad, dil_grad, point_grad,
                      g1, b1, g2, b2, g3, b3, pb, eye, cols, xt):
    t = pl.program_id(0)
    s, z, i, h = plan.place()
    L, Ch, cs = plan.L, plan.Ch, plan.cs
    turn = plan.nw // wg
    mine = pl.ds(pl.multiple_of(i * cs, 16), cs)

    @pl.when(first_step())
    def _():
        n = 2.0 * total_of(lens)
        mean, rho = norm_of(half_state[ST1 : ST1 + 2], n)
        gr = half_state[GAIN1 : GAIN1 + 1] * rho
        gg = sums[1:2] / n * rho
        for k, row in enumerate((gr, -gr * gg, gr * (mean * gg - sums[0:1] / n))):
            xt[...] = column(row, L)
            cols[k] = xt[mine]
        eye[...] = eye_matrix(cs, Ch, i * cs)

        def mine_of(src, at, which, count, *dsts):
            n = dsts[0].shape[1]
            for k in range(count):

                @pl.when(which == k)
                def _():
                    for dst, r in zip(dsts, at):
                        dst[...] = src[r : r + 1, k * n : (k + 1) * n]

        mine_of(sums, (1, 0), i, plan.g, g1, b1)
        mine_of(state, (SU2 + 1, SU2), z, plan.nz, g2, b2)
        mine_of(state, (SU3 + 1, SU3), z, plan.nz, g3, b3)
        mine_of(state, (BSUM,), z, plan.nz, pb)

    own = lax.div(t, turn) == i
    for w in range(wg):
        out_result[w] = jnp.where(own, res[0, w], res_got[0, w])

    C, T1, hs, rb, wide = plan.C, plan.T1, plan.H // plan.nz, plan.rb, plan.C // 2
    count = plan.NW // wg
    turns = min(count, plan.chips)
    per, every = plan.chips // turns, count // turns

    def spread(chunk):
        for n in range(per):
            m = chunk * per + n
            side, r = m * rb // hs, m * rb % hs
            for c in range(2):
                at = slice(c * wide, (c + 1) * wide)
                for k in range(T1):
                    conv_grad[k, n * rb : (n + 1) * rb, at] = summed[k, c, n].astype(F32)
                for u in range(2):
                    v = summed[T1 + u, c, n].astype(F32)
                    if 2 * side + u < plan.T2:
                        dil_grad[2 * side + u, r : r + rb, at] = v
                    else:
                        point_grad[r : r + rb, at] = v

    for chunk in range(turns):
        pl.when(t == chunk * every)(partial(spread, chunk))

    lanes = lanes_of((cs, L))
    for w in range(wg):
        valid = 2 * lens[t * wg + w] - s * L
        v = mm_nt(eye[...], x[w])
        dz = jnp.where(own, gz[w], gz_got[0, w]).astype(F32)
        r = cols[0] * dz + v * cols[1] + cols[2]
        out[w] = jnp.where(lanes < valid, r, 0.0).astype(BF16)


def call(kernel, plan, name, steps, ins, outs, scratch, flops, nbytes, cid=None):
    extra = {} if cid is None else dict(collective_id=cid, has_side_effects=True)
    return pl.pallas_call(
        partial(kernel, plan),
        grid=(steps,),
        in_specs=[SMEM] + [spec for spec, _ in ins],
        out_specs=[spec for spec, _, _ in outs],
        out_shape=[jax.ShapeDtypeStruct(shape, dtype) for _, shape, dtype in outs],
        scratch_shapes=scratch,
        compiler_params=pltpu.CompilerParams(vmem_limit_bytes=VMEM_LIMIT, **extra),
        cost_estimate=pl.CostEstimate(
            flops=int(flops), bytes_accessed=int(nbytes), transcendentals=0
        ),
        name=name,
    )


def per_device(
    inputs,
    lengths,
    input_gain,
    input_shift,
    conv_weight,
    branch_gain,
    branch_shift,
    dilated_tap_weight,
    mixer_gain,
    mixer_shift,
    point_weight,
    point_bias,
    cotangent,
):
    NW, L, C = inputs.shape
    Lp = L // 2
    nz = lax.axis_size("ch")
    R = 2
    plan = Plan(
        ns=lax.axis_size("seq"),
        nz=nz,
        R=R,
        NW=NW,
        L=L,
        C=C,
        H=mixer_gain.shape[0] * nz,
        T1=conv_weight.shape[0],
        T2=dilated_tap_weight.shape[0],
        wb=min(NW * R // nz, max(1, 512 // Lp)),
    )
    g, nw, cs, Ch, H, Hh, wb = plan.g, plan.nw, plan.cs, plan.Ch, plan.H, plan.Hh, plan.wb
    T1, T2, steps = plan.T1, plan.T2, plan.steps
    M = wb * Lp
    hs = H // nz
    lens = lengths.astype(jnp.int32)

    def row(a):
        return a.reshape(1, a.shape[0])

    def grp():
        return lax.rem(lax.axis_index("ch"), g)

    def half():
        return lax.div(lax.axis_index("ch"), g)

    def core():
        return lax.rem(lax.axis_index("seq"), 2)

    def chip4():
        return lax.div(lax.axis_index("seq"), plan.ns // 4)

    def whole(*shape):
        return pl.BlockSpec(shape, lambda t: (0,) * len(shape), pipeline_mode=pl.Buffered(1))

    def const(*shape):
        return pl.BlockSpec(shape, lambda t: (0,) * len(shape))

    def win(*shape):
        return pl.BlockSpec(shape, lambda t: (t,) + (0,) * (len(shape) - 1))

    def arg_win(n, width):
        return pl.BlockSpec((wb, n, width), lambda t: (grp() * steps + t, 0, 0))

    def ins(*pairs):
        return [p for p in pairs]

    share = NW // nz
    nm = max(1, share // wb)

    def edge_spec(n):
        return pl.BlockSpec(
            (nw, 16, C), lambda t: (grp(), n, 0), pipeline_mode=pl.Buffered(1)
        )

    def head_block(t):
        own = lax.div(lax.axis_index("ch") * share, wb) + t
        return jnp.where(t < nm, own, grp() * steps + t - nm), 0, 0

    def after(*shape):
        return pl.BlockSpec(
            shape, lambda t: (jnp.maximum(t - nm, 0),) + (0,) * (len(shape) - 1)
        )

    pairs = ins(
        (pl.BlockSpec((wb, L, C), head_block), inputs),
        (edge_spec(0), inputs),
        (edge_spec(L // 16 - 1), inputs),
        (edge_spec(0), cotangent),
        (edge_spec(Lp // 16 - 1), cotangent),
        (whole(1, cs), row(branch_gain)),
        (whole(1, cs), row(branch_shift)),
        (whole(1, cs), row(point_bias)),
        (whole(1, H // nz), row(mixer_gain)),
        (whole(1, H // nz), row(mixer_shift)),
        (ANY, conv_weight.reshape(T1 * C, C)),
        (whole(C), input_gain),
        (whole(C), input_shift),
        (
            pl.BlockSpec(
                (1, hs, C // 2),
                lambda t: (jnp.minimum(chip4(), T2 - 1), 0, core()),
                pipeline_mode=pl.Buffered(1),
            ),
            jnp.swapaxes(dilated_tap_weight, 1, 2),
        ),
        (
            pl.BlockSpec(
                (hs, C // 2), lambda t: (0, core()), pipeline_mode=pl.Buffered(1)
            ),
            point_weight,
        ),
    )
    plane, line, group = plane_peers(plan), line_peers(plan), group_peers(plan)
    state_shape = (STATE, C)
    edges2, edges3 = (2, nw, EDGE, C), (2, nw, EDGE, H)
    X5, x2, land2, state, beyond, full = call(
        lambda plan, *refs: head_kernel(plan, nm, *refs),
        plan,
        "head",
        nm + steps,
        pairs,
        [
            (
                pl.BlockSpec((T1, M, C), lambda t: (0, jnp.maximum(t - nm, 0), 0)),
                (T1, nw * Lp, C),
                BF16,
            ),
            (after(wb, Lp, C), (nw, Lp, C), F32),
            (ANY, edges2, BF16),
            (const(*state_shape), state_shape, F32),
            (const(2, 3, nw, C), (2, 3, nw, C), F32),
            (ANY, (2, T2 + 1, nz, hs, C // 2), BF16),
        ],
        [
            pltpu.VMEM((2, 8, C), F32),
            pltpu.VMEM((2, 3, nw, C), F32),
            pltpu.VMEM((2, 3, nw, C), F32),
            pltpu.VMEM((T1 * Lp, L), BF16),
            pltpu.VMEM(edges2, BF16),
            pltpu.VMEM((2, C), F32),
            pltpu.VMEM((T1 * C, C), BF16),
            pltpu.SemaphoreType.DMA,
            pltpu.VMEM((hs, C // 2), BF16),
            pltpu.SemaphoreType.DMA((2, 4)),
            HALO_SEMS,
            HALO_SEMS,
        ]
        + plane.scratch(2, C)
        + line.scratch(3, C)
        + group.scratch(2, C),
        2 * nw * Lp * T1 * C * C,
        nw * Lp * C * 20,
        cid=1,
    )(lens, *[a for _, a in pairs])

    full = full.reshape(2, T2 + 1, H, C // 2)
    taps_spec = whole(2, T2, H, C // 2)
    pw_spec = pl.BlockSpec(
        (2, 1, H, C // 2), lambda t: (0, T2, 0, 0), pipeline_mode=pl.Buffered(1)
    )

    def early(*shape):
        return pl.BlockSpec(
            shape, lambda t: (jnp.minimum(t, steps - 1),) + (0,) * (len(shape) - 1)
        )

    def early_land(width):
        return pl.BlockSpec(
            (2, wb, EDGE, width), lambda t: (0, jnp.minimum(t, steps - 1), 0, 0)
        )

    def half_of(n):
        return pl.BlockSpec((n, Ch), lambda t: (0, half()), pipeline_mode=pl.Buffered(1))

    cot_spec = pl.BlockSpec(
        (wb, Lp, C), lambda t: (grp() * steps + jnp.minimum(t, steps - 1), 0, 0)
    )

    p0, r0, b0, g0, block_steps = block_phases(plan)

    def at_phase(first):
        return lambda t: jnp.clip(t - first, 0, steps - 1)

    in_p, in_b = at_phase(p0), at_phase(b0)
    pairs = ins(
        (
            pl.BlockSpec(
                (wb, Lp, C),
                lambda t: (jnp.where(t < p0 + steps, jnp.minimum(t, steps - 1), in_b(t)), 0, 0),
            ),
            x2,
        ),
        (ANY, x2),
        (early_land(C), land2),
        (pl.BlockSpec((wb, Lp, C), lambda t: (grp() * steps + in_p(t), 0, 0)), cotangent),
        (taps_spec, full),
        (pw_spec, full),
        (whole(*state_shape), state),
        (half_of(STATE), state),
    )
    dz2, grads, pgrad, res, dland2, state, res_got = call(
        block_kernel,
        plan,
        "block",
        block_steps,
        pairs,
        [
            (pl.BlockSpec((wb, Lp, C), lambda t: (in_b(t), 0, 0)), (nw, Lp, C), F32),
            (const(Hh, T2 * C), (Hh, T2 * C), BF16),
            (const(Hh, C), (Hh, C), BF16),
            (const(g, nw, cs, Lp), (g, nw, cs, Lp), BF16),
            (ANY, (2, nw, C), F32),
            (const(*state_shape), state_shape, F32),
            (ANY, (g, nw, cs, Lp), BF16),
        ],
        [
            pltpu.VMEM((wb, Lp + 2 * EDGE, C), F32),
            pltpu.VMEM((H, T2 * C), BF16),
            pltpu.VMEM((T2 * H, C), BF16),
            pltpu.VMEM((H, C), BF16),
            pltpu.VMEM((nw * Lp, T2 * C), BF16),
            pltpu.VMEM((nw, Lp, H), F32),
            pltpu.VMEM((nw, Lp, H), F32),
            pltpu.VMEM((M, H), F32),
            pltpu.VMEM((nw * Lp, H), BF16),
            pltpu.VMEM((H, nw * Lp), BF16),
            pltpu.VMEM((nw * Lp, C), BF16),
            pltpu.VMEM((M, T2 * H), BF16),
            pltpu.VMEM((H, nw * Lp), BF16),
            pltpu.VMEM(edges3, BF16),
            pltpu.VMEM(edges3, BF16),
            pltpu.VMEM((1, 2 * H), F32),
            pltpu.VMEM(edges3, BF16),
            pltpu.VMEM(edges3, BF16),
            pltpu.VMEM((2, C), F32),
            pltpu.VMEM((2, nw, C), F32),
            pltpu.VMEM((2, C), F32),
            pltpu.SemaphoreType.DMA((3, 2, 2)),
            pltpu.SemaphoreType.DMA((2, g)),
            pltpu.VMEM((nw, Lp, Ch), F32),
            pltpu.SemaphoreType.DMA,
        ]
        + group.scratch(1, 2 * H)
        + group.scratch(2, C)
        + group.scratch(2, C),
        nw * Lp * C * H * (6 * T2 + 6),
        nw * Lp * C * 30,
        cid=3,
    )(lens, *[a for _, a in pairs])

    chips, rb = plan.chips, plan.rb
    turns_t = tail_turns(plan)

    def x_block(t):
        block = jnp.int32(0)
        for n, (what, k) in enumerate(turns_t):
            if what == "x":
                block = jnp.where(t >= n, k, block)
        return block

    sshape = (T1 + 2, 2, chips, rb, C // 2)
    pairs = ins(
        (early(wb, Lp, C), dz2),
        (whole(2, nw, C), dland2),
        (early(wb, Lp, C), x2),
        (early_land(C), land2),
        (cot_spec, cotangent),
        (whole(2, 3, nw, C), beyond),
        (
            pl.BlockSpec(
                (wb, L, Ch), lambda t: (grp() * steps + x_block(t), 0, half())
            ),
            inputs,
        ),
        (ANY, X5),
        (ANY, conv_weight),
        (whole(Hh, T2 * C), grads),
        (whole(Hh, C), pgrad),
        (whole(*state_shape), state),
        (half_of(STATE), state),
    )
    gz, gz_got, sums1, summed = call(
        tail_kernel,
        plan,
        "tail",
        len(turns_t),
        pairs,
        [
            (pl.BlockSpec((wb, cs, L), lambda t: (x_block(t), 0, 0)), (nw, cs, L), BF16),
            (ANY, (g, nw, cs, L), BF16),
            (const(2, Ch), (2, Ch), F32),
            (ANY, sshape, BF16),
        ],
        [
            pltpu.VMEM((wb, Lp + 16, C), F32),
            pltpu.VMEM((steps, M, 3 * C), BF16),
            pltpu.VMEM((Ch, nw * Lp), BF16),
            pltpu.VMEM((2 * Ch, 3 * C), BF16),
            pltpu.VMEM((L, L), BF16),
            pltpu.VMEM((Ch, Ch), BF16),
            pltpu.VMEM((2, Ch, L), F32),
            pltpu.VMEM((2 * Ch, max(M, C)), F32),
            pltpu.VMEM((g - 1, nw, cs, L), BF16),
            pltpu.VMEM((2, Ch, L), BF16),
            pltpu.VMEM((2, Ch, min(L, 128)), F32),
            pltpu.VMEM((2, nw * Lp, C), BF16),
            pltpu.SemaphoreType.DMA((3,)),
            pltpu.VMEM((T1, Ch, C), BF16),
            pltpu.SemaphoreType.DMA((2, g)),
        ]
        + Reduction.scratch(plan, tail_batches(plan))
        + group.scratch(2, C),
        2 * nw * Lp * (6 + T1) * C * Ch,
        nw * Lp * C * 40,
        cid=6,
    )(lens, *[a for _, a in pairs])

    wg = min(2 * wb, nw)
    count = NW // wg
    turn = nw // wg
    turns = min(count, chips)

    def own_block(t):
        return jnp.where(lax.div(t, turn) == grp(), lax.rem(t, turn), 0)

    def got_slot(t):
        off = lax.rem(grp() - lax.div(t, turn) + g, g)
        return jnp.maximum(off, 1), jnp.where(off > 0, lax.rem(t, turn), 0)

    pairs = ins(
        (pl.BlockSpec((wg, L, Ch), lambda t: (t, 0, half())), inputs),
        (pl.BlockSpec((wg, cs, L), lambda t: (own_block(t), 0, 0)), gz),
        (pl.BlockSpec((1, wg, cs, L), lambda t: got_slot(t) + (0, 0)), gz_got),
        (whole(2, Ch), sums1),
        (pl.BlockSpec((1, wg, cs, Lp), lambda t: (grp(), own_block(t), 0, 0)), res),
        (pl.BlockSpec((1, wg, cs, Lp), lambda t: got_slot(t) + (0, 0)), res_got),
        (
            pl.BlockSpec(
                (T1 + 2, 2, chips // turns, rb, C // 2),
                lambda t: (0, 0, t * turns // count, 0, 0),
            ),
            summed,
        ),
        (whole(*state_shape), state),
        (half_of(STATE), state),
    )
    outs = call(
        lambda plan, *refs: input_grad_kernel(plan, wg, *refs),
        plan,
        "input_grad",
        count,
        pairs,
        [
            (win(wg, cs, L), (NW, cs, L), BF16),
            (win(wg, cs, Lp), (NW, cs, Lp), BF16),
            (
                pl.BlockSpec((T1, cs // turns, C), lambda t: (0, t * turns // count, 0)),
                (T1, cs, C),
                F32,
            ),
            (const(T2, hs, C), (T2, hs, C), F32),
            (const(hs, C), (hs, C), F32),
        ]
        + [(const(1, n), (1, n), F32) for n in (cs, cs, cs, cs, hs, hs, cs)],
        [
            pltpu.VMEM((cs, Ch), BF16),
            pltpu.VMEM((3, cs, L), F32),
            pltpu.VMEM((Ch, L), F32),
        ],
        2 * NW * L * Ch * cs,
        NW * L * cs * 8,
    )(lens, *[a for _, a in pairs])
    grad, result, conv_grad, dil_grad, point_grad = outs[:5]
    g1, b1, g2, b2, g3, b3, pb = [a[0] for a in outs[5:]]
    return (
        jnp.swapaxes(result, 1, 2),
        jnp.swapaxes(grad, 1, 2),
        jnp.swapaxes(conv_grad, 1, 2),
        g1,
        b1,
        g2,
        b2,
        jnp.swapaxes(dil_grad, 1, 2),
        g3,
        b3,
        point_grad,
        pb,
    )


def solution(mesh):
    in_specs = (
        P(None, "seq", None),
        P(),
        P(),
        P(),
        P(),
        P("ch"),
        P("ch"),
        P(None, None, "ch"),
        P("ch"),
        P("ch"),
        P("ch", None),
        P("ch"),
        P(None, "seq", None),
    )
    out_specs = (
        P(None, "seq", "ch"),
        P(None, "seq", "ch"),
        P(None, None, "ch"),
        P("ch"),
        P("ch"),
        P("ch"),
        P("ch"),
        P(None, None, "ch"),
        P("ch"),
        P("ch"),
        P("ch", None),
        P("ch"),
    )
    return jax.shard_map(
        per_device, mesh=mesh, in_specs=in_specs, out_specs=out_specs, check_vma=False
    )
```

```python
from functools import partial
from typing import NamedTuple

import jax
import jax.numpy as jnp
from jax import lax
from jax.experimental import pallas as pl
from jax.experimental.pallas import tpu as pltpu
from jax.sharding import PartitionSpec as P

DIL = 14
EDGE = 16
EPS = 1e-05
GC0 = 0.7978845608028654
GC1 = 0.044715
F32 = jnp.float32
BF16 = jnp.bfloat16
MESH = pl.DeviceIdType.MESH
VMEM_LIMIT = 58 * 1024 * 1024
ANY = pl.BlockSpec(memory_space=pl.ANY)
SMEM = pl.BlockSpec(memory_space=pltpu.SMEM)


ST1, GAIN2, SHIFT2, BIAS, GAIN3, SHIFT3, GAIN1, SHIFT1, ST2, ST3, SU3, BSUM, SU2 = (
    0, 2, 3, 4, 5, 6, 7, 8, 9, 11, 13, 15, 16
)
STATE = 24


class Plan(NamedTuple):
    ns: int
    nz: int
    R: int
    NW: int
    L: int
    C: int
    H: int
    T1: int
    T2: int
    wb: int

    @property
    def g(self):
        return self.nz // self.R

    @property
    def nw(self):
        return self.NW // self.g

    @property
    def Lp(self):
        return self.L // 2

    @property
    def cs(self):
        return self.C // self.nz

    @property
    def Ch(self):
        return self.C // self.R

    @property
    def Hh(self):
        return self.H // self.R

    @property
    def steps(self):
        return self.nw // self.wb

    @property
    def chips(self):
        return self.ns // 2

    @property
    def rb(self):
        return self.cs // self.chips

    def place(self):
        s, z = lax.axis_index("seq"), lax.axis_index("ch")
        return s, z, lax.rem(z, self.g), lax.div(z, self.g)


def gelu(z):
    t = jnp.tanh(z * (GC0 + (GC0 * GC1) * (z * z)))
    return z * (0.5 + 0.5 * t)


def gelu_both(z):
    sq = z * z
    t = jnp.tanh(z * (GC0 + (GC0 * GC1) * sq))
    h = 0.5 + 0.5 * t
    v = z * h
    return v, h + v * (1.0 - t) * (GC0 + (3.0 * GC0 * GC1) * sq)


def gelu_slope(z):
    return gelu_both(z)[1]


def fold(v):
    return jnp.sum(v.reshape(v.shape[0] // 8, 8, v.shape[1]), axis=0)


def fold_lanes(v):
    out = v[:, 0:128]
    for k in range(128, v.shape[1], 128):
        out = out + v[:, k : k + 128]
    return out


def unfold(v):
    return jnp.sum(v, axis=0, keepdims=True)


def rows_of(shape):
    return lax.broadcasted_iota(jnp.int32, shape, 0)


def lanes_of(shape):
    return lax.broadcasted_iota(jnp.int32, shape, 1)


def total_of(lens):
    n = lens[0]
    for k in range(1, lens.shape[0]):
        n = n + lens[k]
    return n.astype(F32)


def norm_of(stats, total):
    mean = stats[0:1] / total
    square = stats[1:2] / total
    return mean, lax.rsqrt(square - mean * mean + EPS)


def flat(ref):
    return ref[...].reshape(1, ref.shape[0])


def column(row, n):
    return jnp.broadcast_to(row, (n, row.shape[1])).T


def mm(a, b):
    return jnp.dot(a, b, preferred_element_type=F32)


def mm_nt(a, b):
    return lax.dot_general(a, b, (((1,), (1,)), ((), ())), preferred_element_type=F32)


def mm_tn(a, b):
    return lax.dot_general(a, b, (((0,), (0,)), ((), ())), preferred_element_type=F32)


def mm_tt(a, b):
    return lax.dot_general(a, b, (((0,), (1,)), ((), ())), preferred_element_type=F32)


def eye_matrix(n, m, first):
    return jnp.where(lanes_of((n, m)) == rows_of((n, m)) + first, 1.0, 0.0).astype(BF16)


def pick_matrix(L):
    r, n = rows_of((L, L)), lanes_of((L, L))
    bin_of = 2 * r - jnp.where(r >= L // 2, L - 1, 0)
    return jnp.where(n == bin_of, 1.0, 0.0).astype(BF16)


def remote(src, dst, send, recv, device):
    return pltpu.make_async_remote_copy(
        src_ref=src,
        dst_ref=dst,
        send_sem=send,
        recv_sem=recv,
        device_id=device,
        device_id_type=MESH,
    )


def wrap(v, n):
    return jnp.where(v >= n, v - n, v)


def greet(devices):
    barrier = pltpu.get_barrier_semaphore()
    for device in devices:
        pl.semaphore_signal(barrier, inc=1, device_id=device, device_id_type=MESH)


def meet(devices):
    pl.semaphore_wait(pltpu.get_barrier_semaphore(), len(devices))


class Peers:
    def __init__(self, me, others):
        self.me, self.others = me, others
        self.count = len(others) + 1

    def start(self, link):
        packet, buf, sems = link
        for device in self.others:
            remote(packet, buf.at[self.me], sems.at[0], sems.at[1], device).start()

    def finish(self, link):
        packet, buf, sems = link
        buf[self.me] = packet[...]
        rest = buf.at[pl.ds(0, self.count - 1)]
        done = remote(rest, rest, sems.at[0], sems.at[1], self.others[0])
        done.wait_recv()
        acc = buf[0]
        for q in range(1, self.count):
            acc = acc + buf[q]
        done.wait_send()
        return acc

    def scratch(self, rows, width):
        return [
            pltpu.VMEM((rows, width), F32),
            pltpu.VMEM((self.count, rows, width), F32),
            pltpu.SemaphoreType.DMA((2,)),
        ]


def group_peers(plan):
    s, z, i, h = plan.place()
    g = plan.g
    others = [
        (wrap(s + a, plan.ns), h * g + wrap(i + b, g))
        for a in range(plan.ns)
        for b in range(g)
        if a or b
    ]
    return Peers(s * g + i, others)


def plane_peers(plan):
    s, z, i, h = plan.place()
    return Peers(s, [(wrap(s + a, plan.ns), z) for a in range(1, plan.ns)])


def line_peers(plan):
    s, z, i, h = plan.place()
    return Peers(z, [(s, wrap(z + a, plan.nz)) for a in range(1, plan.nz)])


class Halo:
    def __init__(self, plan, edge, land, sems):
        self.edge, self.land, self.sems = edge, land, sems
        s, z, _, _ = plan.place()
        self.to = ((wrap(s + plan.ns - 1, plan.ns), z), (wrap(s + 1, plan.ns), z))

    def copy(self, side, rows):
        return remote(
            self.edge.at[side, rows],
            self.land.at[1 - side, rows],
            self.sems.at[0, side],
            self.sems.at[1, side],
            self.to[side],
        )

    def start(self, first, count):
        for side in range(2):
            self.copy(side, pl.ds(first, count)).start()

    def finish(self):
        for side in range(2):
            done = self.copy(side, pl.ds(0, self.land.shape[1]))
            done.wait_recv()
            done.wait_send()


HALO_SEMS = pltpu.SemaphoreType.DMA((2, 2))


class Gather:
    def __init__(self, plan, part, full, sems):
        self.plan, self.part, self.full, self.sems = plan, part, full, sems
        self.s, self.z, self.i, self.h = plan.place()
        self.c, self.m = lax.rem(self.s, 2), lax.div(self.s, 2)
        self.chips = plan.chips
        self.every = self.chips // 4
        self.tap = lax.div(self.m, self.every)
        self.owner = lax.rem(self.m, self.every) == 0
        self.mine = full.at[self.c, self.tap]

    def others(self):
        g, nz = self.plan.g, self.plan.nz
        return [(self.s, wrap(self.h * g + g + r, nz)) for r in range(nz - g)]

    def far(self, off):
        return (2 * wrap(self.m + off, self.chips) + self.c, self.z)

    def own(self):
        return pltpu.make_async_copy(self.part, self.mine.at[self.z], self.sems.at[0, 0])

    def line(self, off):
        device = (self.s, wrap(self.z + off, self.plan.nz))
        return remote(
            self.part, self.mine.at[self.z], self.sems.at[0, 1], self.sems.at[1, 1], device
        )

    def chip(self, off):
        return remote(self.mine, self.mine, self.sems.at[0, 2], self.sems.at[1, 2], self.far(off))

    def pair(self):
        half = self.full.at[self.c]
        device = (2 * self.m + 1 - self.c, self.z)
        return remote(half, half, self.sems.at[0, 3], self.sems.at[1, 3], device)

    def line_start(self):
        @pl.when(self.owner)
        def _():
            self.own().start()
            for off in range(1, self.plan.nz):
                self.line(off).start()

    def line_finish(self):
        @pl.when(self.owner)
        def _():
            self.own().wait()
            rest = self.mine.at[pl.ds(0, self.plan.nz - 1)]
            device = (self.s, wrap(self.z + 1, self.plan.nz))
            done = remote(rest, rest, self.sems.at[0, 1], self.sems.at[1, 1], device)
            done.wait_recv()
            done.wait_send()

    def chips_start(self):
        @pl.when(self.owner)
        def _():
            for off in range(1, self.chips):
                self.chip(off).start()

    def pair_start(self):
        def taken(count):
            rest = self.full.at[self.c, pl.ds(0, count)]
            return remote(rest, rest, self.sems.at[0, 2], self.sems.at[1, 2], self.far(1))

        @pl.when(self.owner)
        def _():
            taken(3).wait_recv()
            for off in range(1, self.chips):
                self.chip(off).wait_send()

        if self.every > 1:

            @pl.when(jnp.logical_not(self.owner))
            def _():
                taken(4).wait_recv()

        self.pair().start()

    def pair_finish(self):
        done = self.pair()
        done.wait_recv()
        done.wait_send()


def first_step():
    return pl.program_id(0) == 0


def last_step():
    return pl.program_id(0) == pl.num_programs(0) - 1


def head_kernel(plan, nm, lens, x, xtop, xend, ctop, cend, g2, s2, pb, g3, s3,
                w_hbm, gain, shift, taps, pw,
                X5, x2, land, state, beyond_out, full,
                macc, beyond, xedge, sel, edge, acc, w_ref, w_sem, part,
                gather_sems, xhalo_sems, halo_sems, *links):
    t = pl.program_id(0)
    peers, plane, line = group_peers(plan), plane_peers(plan), line_peers(plan)
    xhalo = Halo(plan, xedge, beyond, xhalo_sems)
    halo = Halo(plan, edge, land, halo_sems)
    gather = Gather(plan, part, full, gather_sems)
    w_copy = pltpu.make_async_copy(w_hbm, w_ref, w_sem)
    plane_link, line_link, link = links[:3], links[3:6], links[6:]
    s, z, i, h = plan.place()
    L, Lp, C, nw, nz, wb = plan.L, plan.Lp, plan.C, plan.nw, plan.nz, plan.wb
    share = plan.NW // nz
    c = t - nm
    everyone = peers.others + gather.others()

    @pl.when(first_step())
    def _():
        w_copy.start()
        greet(everyone)
        part[...] = jnp.where(gather.tap == 3, pw[...], taps[0])
        macc[...] = jnp.zeros_like(macc)
        acc[...] = jnp.zeros_like(acc)
        state[...] = jnp.zeros_like(state)
        state[GAIN1 : GAIN1 + 1] = flat(gain)
        state[SHIFT1 : SHIFT1 + 1] = flat(shift)
        n16 = nw * 16
        for side, (xe, ce, places) in enumerate(
            ((xtop, ctop, (0, 1, 0)), (xend, cend, (14, 15, 15)))
        ):
            for k, at in enumerate(places):
                rows, lanes = rows_of((nw, n16)), lanes_of((nw, n16))
                one = jnp.where(lanes == 16 * rows + at, 1.0, 0.0).astype(BF16)
                block = (xe if k < 2 else ce)[...].reshape(n16, C)
                xedge[side, k] = mm(one, block)
        shape = (Lp, L)
        for k in range(plan.T1):
            at = lanes_of(shape) - (2 * rows_of(shape) + (k - 2))
            sel[k * Lp : (k + 1) * Lp] = jnp.where((at == 0) | (at == 1), 1.0, 0.0).astype(BF16)

    @pl.when(c < 0)
    def _():
        rows = rows_of((L, C))
        for w in range(min(share, wb)):
            at = lax.rem(z * share, wb) + w
            valid = 2 * lens[z * share + t * wb + w] - s * L
            v = jnp.where(rows < valid, x[at].astype(F32), 0.0)
            macc[0] += fold(v)
            macc[1] += fold(v * v)

    @pl.when(c == -1)
    def _():
        packet, more = plane_link[0], line_link[0]
        packet[0:1] = unfold(macc[0])
        packet[1:2] = unfold(macc[1])
        meet(everyone)
        plane.start(plane_link)
        xhalo.start(0, 3)
        at = 0
        spans = []
        more[2:3] = jnp.zeros((1, C), F32)
        for ref in (g2, s2, pb, g3, s3):
            n = ref.shape[1]
            more[2:3, at : at + n] = ref[...]
            spans.append((at, n))
            at += n
        more[0:2] = plane.finish(plane_link)
        line.start(line_link)
        gather.line_start()
        state[ST1 : ST1 + 2] = line.finish(line_link)[0:2]
        for k in range(nz):
            row = line_link[1][k]
            for r, (at, n) in zip((GAIN2, SHIFT2, BIAS, GAIN3, SHIFT3), spans):
                state[r : r + 1, k * n : (k + 1) * n] = row[2:3, at : at + n]
        xhalo.finish()
        beyond_out[...] = beyond[...]
        w_copy.wait()

    @pl.when(c >= 0)
    def _():
        mean, rho = norm_of(state[ST1 : ST1 + 2], 2.0 * total_of(lens))
        scale = state[GAIN1 : GAIN1 + 1] * rho
        offset = state[SHIFT1 : SHIFT1 + 1] - mean * scale
        rows = rows_of((L, C))
        row1 = rows_of((1, C))
        row16 = rows_of((16, C))
        def activate(w):
            at = c * wb + w
            valid = 2 * lens[i * nw + at] - s * L
            a = gelu(x[w].astype(F32) * scale + offset)
            a = jnp.where(rows < valid, a, 0.0).astype(BF16)
            picked = mm(sel[...], a)
            for k in range(5):
                X5[k, w * Lp : (w + 1) * Lp] = picked[k * Lp : (k + 1) * Lp].astype(BF16)

            def beside(side, k, bin_at):
                a = gelu(beyond[side, k, pl.ds(at, 1), :] * scale + offset)
                here = (row1 + bin_at < valid) & (row1 + (s * L + bin_at) >= 0)
                return jnp.where(here, a, 0.0).astype(BF16).astype(F32)

            l0, l1 = beside(0, 0, -2), beside(0, 1, -1)
            r0, r1 = beside(1, 0, L), beside(1, 1, L + 1)
            top, end = w * Lp, (w + 1) * Lp
            for k, add in ((0, l0 + l1), (1, l1)):
                X5[k, top : top + 16] = (
                    picked[k * Lp : k * Lp + 16] + jnp.where(row16 == 0, add, 0.0)
                ).astype(BF16)
            for k, add in ((3, r0), (4, r0 + r1)):
                X5[k, end - 16 : end] = (
                    picked[(k + 1) * Lp - 16 : (k + 1) * Lp] + jnp.where(row16 == 15, add, 0.0)
                ).astype(BF16)

        nc = 256
        rowp = rows_of((Lp, nc))

        def convolve(first, count):
            span = slice(first * Lp, (first + count) * Lp)
            for n in range(C // nc):
                cols = slice(n * nc, (n + 1) * nc)
                taps = [X5[k, span] for k in range(plan.T1)]
                y = 0.5 * mm(jnp.concatenate(taps, axis=1), w_ref[:, cols])
                s0 = jnp.zeros((8, nc), F32)
                s1 = jnp.zeros((8, nc), F32)
                for w in range(first, first + count):
                    at = c * wb + w
                    valid = lens[i * nw + at] - s * Lp
                    v = y[(w - first) * Lp : (w - first + 1) * Lp]
                    x2[w, :, cols] = v
                    edge[0, at, :, cols] = v[:EDGE].astype(BF16)
                    edge[1, at, :, cols] = v[Lp - EDGE :].astype(BF16)
                    v = jnp.where(rowp < valid, v, 0.0)
                    s0 = s0 + fold(v)
                    s1 = s1 + fold(v * v)
                acc[0:1, cols] += unfold(s0)
                acc[1:2, cols] += unfold(s1)

        count = max(1, wb // 2)
        for first in range(0, wb, count):
            for w in range(first, first + count):
                activate(w)
            convolve(first, count)
        halo.start(c * wb, wb)

    @pl.when(c == 0)
    def _():
        gather.line_finish()
        gather.chips_start()

    @pl.when(last_step())
    def _():
        link[0][...] = acc[...]
        peers.start(link)
        gather.pair_start()
        state[ST2 : ST2 + 2] = peers.finish(link)
        halo.finish()
        gather.pair_finish()


def block_kernel(plan, lens, x2, x2_hbm, x2land, cot, w_ref, pw_ref, old, half_state,
                 dz2, grads, pgrad, res, land, state, res_got,
                 ext, wf, wt, pw, Y3, c2, dz3, das, a3s, a3T, dos, Z3, dcT,
                 cedge, cland, cacc, dedge, dland, dacc, bedge, bacc, halo_sems, bulk_sems,
                 x2half, x2_sem, *links):
    t = pl.program_id(0)
    peers = group_peers(plan)
    s, z, i, h = plan.place()
    Lp, C, H, wb, nw, cs, g = plan.Lp, plan.C, plan.H, plan.wb, plan.nw, plan.cs, plan.g
    M = wb * Lp
    steps = plan.steps
    p0, r0, b0, g0 = block_phases(plan)[:4]
    c_link, d_link, b_link = links[:3], links[3:6], links[6:]
    c_halo = Halo(plan, cedge, cland, halo_sems.at[0])
    d_halo = Halo(plan, dedge, dland, halo_sems.at[1])
    b_halo = Halo(plan, bedge, land, halo_sems.at[2])

    def bulk(off, rows):
        to = wrap(i + off, g)
        return remote(
            res.at[to, rows],
            res_got.at[off, rows],
            bulk_sems.at[0, off],
            bulk_sems.at[1, off],
            (s, h * g + to),
        )

    def result_of(block):
        y = mm(a3s[pl.ds(pl.multiple_of(block * M, 128), M)], pw_ref[h, 0])
        rowr = rows_of((Lp, y.shape[1]))
        for w in range(wb):
            at = block * wb + w
            valid = lens[i * plan.nw + at] - s * Lp
            r = x2half[at] + y[w * Lp : (w + 1) * Lp] + half_state[BIAS : BIAS + 1]
            r = jnp.where(rowr < valid, r, 0.0).astype(BF16).T
            for k in range(g):
                res[k, at] = r[k * cs : (k + 1) * cs]

    def send_result(block):
        result_of(block)
        for off in range(1, g):
            bulk(off, pl.ds(block * wb, wb)).start()

    half_copy = pltpu.make_async_copy(
        x2_hbm.at[:, :, pl.ds(pl.multiple_of(h * plan.Ch, 128), plan.Ch)], x2half, x2_sem
    )

    @pl.when(first_step())
    def _():
        half_copy.start()
        greet(peers.others)
        state[...] = old[...]
        cacc[...] = jnp.zeros_like(cacc)
        dacc[...] = jnp.zeros_like(dacc)
        bacc[...] = jnp.zeros_like(bacc)
        for c in range(2):
            cols = slice(c * (C // 2), (c + 1) * (C // 2))
            pw[:, cols] = pw_ref[c, 0]
            for k in range(plan.T2):
                at = k * C + c * (C // 2)
                wf[:, at : at + C // 2] = w_ref[c, k]
                wt[k * H : (k + 1) * H, cols] = w_ref[c, k]

    @pl.when(t < p0)
    def _():
        base = pl.multiple_of(t * M, 128)
        mean, rho = norm_of(state[ST2 : ST2 + 2], total_of(lens))
        scale = state[GAIN2 : GAIN2 + 1] * rho
        offset = state[SHIFT2 : SHIFT2 + 1] - mean * scale
        rows = rows_of((Lp, C))
        rowe = rows_of((EDGE, C))

        rowh = rows_of((Lp, H))
        sums0, sums1 = jnp.zeros((8, H), F32), jnp.zeros((8, H), F32)
        nh = min(2, wb)
        for first in range(0, wb, wb // nh):
            span = range(first, first + wb // nh)
            for w in span:
                valid = lens[i * plan.nw + t * wb + w] - s * Lp
                a = jnp.where(rows < valid, gelu(x2[w] * scale + offset), 0.0)
                al = gelu(x2land[0, w].astype(F32) * scale + offset)
                al = jnp.where((rowe - EDGE < valid) & (s > 0), al, 0.0)
                ah = gelu(x2land[1, w].astype(F32) * scale + offset)
                ah = jnp.where(rowe + Lp < valid, ah, 0.0)
                ext[w, 0:EDGE] = al
                ext[w, EDGE : EDGE + Lp] = a
                ext[w, EDGE + Lp :] = ah
                top, end = w * Lp, (w + 1) * Lp
                Y3[pl.ds(base + top, Lp), 0:C] = ext[w, EDGE - DIL : EDGE - DIL + Lp].astype(BF16)
                Y3[pl.ds(base + top, Lp), C : 2 * C] = a.astype(BF16)
                Y3[pl.ds(base + top, Lp), 2 * C : 3 * C] = ext[w, EDGE + DIL : EDGE + DIL + Lp].astype(BF16)
            y = mm_nt(Y3[pl.ds(base + first * Lp, wb // nh * Lp)], wf[...])
            for w in span:
                at = t * wb + w
                valid = lens[i * plan.nw + at] - s * Lp
                v = y[(w - first) * Lp : (w - first + 1) * Lp]
                c2[at] = v
                cedge[0, at] = v[:EDGE].astype(BF16)
                cedge[1, at] = v[Lp - EDGE :].astype(BF16)
                v = jnp.where(rowh < valid, v, 0.0)
                sums0 = sums0 + fold(v)
                sums1 = sums1 + fold(v * v)
        cacc[0:1, 0:H] += unfold(sums0)
        cacc[0:1, H:] += unfold(sums1)

    @pl.when(first_step())
    def _():
        meet(peers.others)

    @pl.when(t < p0)
    def _():
        c_halo.start(t * wb, wb)

    @pl.when(t == p0 - 1)
    def _():
        c_link[0][...] = cacc[...]
        peers.start(c_link)

    here_p = (t >= p0) & (t < p0 + steps)

    @pl.when(here_p)
    def _():
        u = t - p0
        rowc = rows_of((Lp, C))
        block = pl.ds(pl.multiple_of(u * M, 128), M)
        bias = jnp.zeros((8, C), F32)
        parts = []
        for w in range(wb):
            valid = lens[i * plan.nw + u * wb + w] - s * Lp
            d = jnp.where(rowc < valid, cot[w].astype(F32), 0.0)
            bias = bias + fold(d)
            parts.append(d.astype(BF16))
        d = jnp.concatenate(parts, axis=0)
        dos[block] = d
        das[...] = mm_nt(d, pw[...])
        dacc[1:2] += unfold(bias)

    @pl.when(t == p0)
    def _():
        got = peers.finish(c_link)
        state[ST3 : ST3 + 1, 0:H] = got[:, 0:H]
        state[ST3 + 1 : ST3 + 2, 0:H] = got[:, H:]

    @pl.when(here_p)
    def _():
        u = t - p0
        block = pl.ds(pl.multiple_of(u * M, 128), M)
        rowh = rows_of((Lp, H))
        mean, rho = norm_of(state[ST3 : ST3 + 2, 0:H], total_of(lens))
        scale = state[GAIN3 : GAIN3 + 1, 0:H] * rho
        offset = state[SHIFT3 : SHIFT3 + 1, 0:H] - mean * scale
        s0, s1 = jnp.zeros((8, H), F32), jnp.zeros((8, H), F32)
        parts = []
        for w in range(wb):
            at = u * wb + w
            valid = lens[i * plan.nw + at] - s * Lp
            top, end = w * Lp, (w + 1) * Lp
            v = c2[at]
            zv = v * scale + offset
            act, slope = gelu_both(zv)
            parts.append(jnp.where(rowh < valid, act, 0.0).astype(BF16))
            dzw = das[top:end] * slope
            dz3[at] = dzw
            dedge[0, at] = dzw[:EDGE].astype(BF16)
            dedge[1, at] = dzw[Lp - EDGE :].astype(BF16)
            s0 = s0 + fold(dzw)
            s1 = s1 + fold(dzw * zv)
        a3 = jnp.concatenate(parts, axis=0)
        a3s[block] = a3
        a3T[:, block] = a3.T
        dacc[0:1, 0:H] += unfold(s0)
        dacc[0:1, H : 2 * H] += unfold(s1)
        d_halo.start(u * wb, wb)

    @pl.when(t == p0)
    def _():
        half_copy.wait()
        send_result(0)

    @pl.when(t == p0 + steps - 1)
    def _():
        d_link[0][...] = dacc[...]
        peers.start(d_link)

    @pl.when(t == r0)
    def _():
        for block in range(1, steps):
            send_result(block)
        rows = pl.ds(pl.multiple_of(h * plan.Hh, 16), plan.Hh)
        pgrad[...] = mm(a3T[rows], dos[...]).astype(BF16)

    @pl.when(t == b0)
    def _():
        got = peers.finish(d_link)
        shift = state[SHIFT3 : SHIFT3 + 1, 0:H]
        gain = state[GAIN3 : GAIN3 + 1, 0:H]
        state[SU3 : SU3 + 1, 0:H] = got[0:1, 0:H]
        state[SU3 + 1 : SU3 + 2, 0:H] = (got[0:1, H : 2 * H] - shift * got[0:1, 0:H]) / gain
        state[BSUM : BSUM + 1] = got[1:2]
        c_halo.finish()
        d_halo.finish()

    @pl.when((t >= b0) & (t < g0))
    def _():
        u = t - b0
        total = total_of(lens)
        mean3, rho3 = norm_of(state[ST3 : ST3 + 2, 0:H], total)
        gr3 = state[GAIN3 : GAIN3 + 1, 0:H] * rho3
        sg3 = state[SU3 : SU3 + 1, 0:H] / total
        gg3 = state[SU3 + 1 : SU3 + 2, 0:H] / total
        mean2, rho2 = norm_of(state[ST2 : ST2 + 2], total)
        scale2 = state[GAIN2 : GAIN2 + 1] * rho2
        offset2 = state[SHIFT2 : SHIFT2 + 1] - mean2 * scale2
        rowh = rows_of((Lp, H))
        rowe = rows_of((EDGE, H))
        rowc = rows_of((Lp, C))

        by_v = -gr3 * rho3 * gg3
        by_1 = gr3 * (mean3 * rho3 * gg3 - sg3)

        def back(dz, v):
            return gr3 * dz + by_v * v + by_1

        for w in range(wb):
            valid = lens[i * nw + u * wb + w] - s * Lp
            d = jnp.where(rowh < valid, back(dz3[u * wb + w], c2[u * wb + w]), 0.0)
            dl = back(dland[0, u * wb + w].astype(F32), cland[0, u * wb + w].astype(F32))
            dl = jnp.where((rowe - EDGE < valid) & (s > 0), dl, 0.0)
            dh = back(dland[1, u * wb + w].astype(F32), cland[1, u * wb + w].astype(F32))
            dh = jnp.where(rowe + Lp < valid, dh, 0.0)
            ext[w, 0:EDGE, 0:H] = dl
            ext[w, EDGE : EDGE + Lp, 0:H] = d
            ext[w, EDGE + Lp :, 0:H] = dh
            top, end = w * Lp, (w + 1) * Lp
            Z3[top:end, 0:H] = ext[w, EDGE + DIL : EDGE + DIL + Lp, 0:H].astype(BF16)
            Z3[top:end, H : 2 * H] = d.astype(BF16)
            Z3[top:end, 2 * H : 3 * H] = ext[w, EDGE - DIL : EDGE - DIL + Lp, 0:H].astype(BF16)

        y = mm(Z3[...], wt[...])

        M = wb * Lp
        dcT[:, pl.ds(pl.multiple_of(u * M, 128), M)] = Z3[:, H : 2 * H].T
        s0, s1 = jnp.zeros((8, C), F32), jnp.zeros((8, C), F32)
        for w in range(wb):
            at = u * wb + w
            valid = lens[i * nw + at] - s * Lp
            v = x2[w]
            zv = v * scale2 + offset2
            dzw = y[w * Lp : (w + 1) * Lp] * gelu_slope(zv)
            dzw = jnp.where(rowc < valid, dzw, 0.0)
            dz2[w] = dzw
            bedge[0, pl.ds(at, 1)] = dzw[0:1]
            bedge[1, pl.ds(at, 1)] = dzw[Lp - 1 : Lp]
            s0 = s0 + fold(dzw)
            s1 = s1 + fold(dzw * zv)
        bacc[0:1] += unfold(s0)
        bacc[1:2] += unfold(s1)

    @pl.when(t == g0 - 1)
    def _():
        b_link[0][...] = bacc[...]
        peers.start(b_link)
        b_halo.start(0, nw)

    @pl.when(last_step())
    def _():
        rows = pl.ds(pl.multiple_of(h * plan.Hh, 16), plan.Hh)
        for n in range(plan.T2):
            cols = slice(n * C, (n + 1) * C)
            grads[:, cols] = mm(dcT[rows], Y3[:, cols]).astype(BF16)

    @pl.when(last_step())
    def _():
        got = peers.finish(b_link)
        shift, gain = state[SHIFT2 : SHIFT2 + 1], state[GAIN2 : GAIN2 + 1]
        state[SU2 : SU2 + 1] = got[0:1]
        state[SU2 + 1 : SU2 + 2] = (got[1:2] - shift * got[0:1]) / gain
        b_halo.finish()
        for off in range(1, g):
            bulk(off, pl.ds(0, nw)).wait()


def block_phases(plan):
    n = plan.steps
    return n, 2 * n, 2 * n + 1, 3 * n + 1, 3 * n + 2


class Reduction:
    def __init__(self, plan, batches, out, give, mine, got, spread, half, mate, sems):
        self.plan, self.batches, self.out = plan, batches, out
        self.give, self.mine, self.got, self.spread = give, mine, got, spread
        self.half, self.mate = half, mate
        self.sems = sems
        self.s, self.z, self.i, self.h = plan.place()
        self.c = lax.rem(self.s, 2)
        self.m = lax.div(self.s, 2)
        self.chips = plan.chips

    @staticmethod
    def scratch(plan, batches):
        taps, wide = plan.T1 + 2, plan.C // 2
        full = (taps, plan.chips, plan.g, plan.rb, wide)
        part = (taps, plan.g, plan.rb, wide)
        return [
            pltpu.VMEM((taps, 2, plan.chips, plan.rb, wide), BF16),
            *[pltpu.VMEM(full, BF16)] * 4,
            *[pltpu.VMEM(part, BF16)] * 2,
            pltpu.SemaphoreType.DMA((2, len(batches), 5)),
        ]

    def copy(self, b, phase, src, dst, device):
        return remote(src, dst, self.sems.at[0, b, phase], self.sems.at[1, b, phase], device)

    def finish(self, b, phase, ref, device):
        done = self.copy(b, phase, ref, ref, device)
        done.wait_recv()
        done.wait_send()

    def taps(self, b):
        return pl.ds(*self.batches[b])

    def pair(self):
        return (2 * self.m + (1 - self.c), self.z)

    def far(self, off):
        return (2 * wrap(self.m + off, self.chips) + self.c, self.z)

    def member(self, off):
        return (self.s, self.h * self.plan.g + wrap(self.i + off, self.plan.g))

    def put(self, k, rows):
        wide = self.plan.C // 2
        for j in range(self.plan.g):
            for m in range(self.chips):
                v = rows(j, m)
                left, right = v[:, :wide], v[:, wide:]
                self.mine[k, m, j] = jnp.where(self.c == 0, left, right).astype(BF16)
                self.give[k, m, j] = jnp.where(self.c == 0, right, left).astype(BF16)

    def step0(self, b):
        taps = self.taps(b)
        self.copy(b, 0, self.give.at[taps], self.got.at[taps], self.pair()).start()

    def step1(self, b):
        taps = self.taps(b)
        self.finish(b, 0, self.got.at[taps], self.pair())
        first, count = self.batches[b]
        for k in range(first, first + count):
            v = self.mine[k].astype(F32) + self.got[k].astype(F32)
            self.mine[k] = v.astype(BF16)
        for off in range(1, self.chips):
            src = self.mine.at[taps, wrap(self.m + off, self.chips)]
            self.copy(b, 1, src, self.spread.at[taps, self.m], self.far(off)).start()

    def step2(self, b):
        taps = self.taps(b)
        self.finish(b, 1, self.spread.at[taps, pl.ds(0, self.chips - 1)], self.far(1))
        first, count = self.batches[b]
        for k in range(first, first + count):
            self.spread[k, self.m] = self.mine[k, self.m]
            v = self.spread[k, 0].astype(F32)
            for n in range(1, self.chips):
                v = v + self.spread[k, n].astype(F32)
            self.half[k] = v.astype(BF16)
        for off in range(1, self.plan.g):
            src = self.half.at[taps, wrap(self.i + off, self.plan.g)]
            self.copy(b, 2, src, self.mate.at[taps, off], self.member(off)).start()

    def step3(self, b):
        taps = self.taps(b)
        self.finish(b, 2, self.mate.at[taps, pl.ds(1, self.plan.g - 1)], self.member(1))
        first, count = self.batches[b]
        for k in range(first, first + count):
            v = self.half[k, self.i].astype(F32)
            for off in range(1, self.plan.g):
                v = v + self.mate[k, off].astype(F32)
            self.out[k, self.c, self.m] = v.astype(BF16)
        mine = self.out.at[taps, self.c, self.m]
        for off in range(1, self.chips):
            self.copy(b, 3, mine, mine, self.far(off)).start()

    def step4(self, b):
        taps = self.taps(b)
        self.finish(b, 3, self.out.at[taps, self.c, pl.ds(0, self.chips - 1)], self.far(1))
        mine = self.out.at[taps, self.c]
        self.copy(b, 4, mine, mine, self.pair()).start()

    def step5(self, b):
        self.finish(b, 4, self.out.at[self.taps(b), self.c], self.pair())


def tail_turns(plan):
    nD, T1 = plan.steps, plan.T1
    turns = [("x", 0)] + [("d", n) for n in range(1, nD)]
    xs, ws = [("x", n) for n in range(1, nD)], [("w", n) for n in range(T1)]
    for count in (2, 1, T1):
        turns += ws[:count] + xs[:1]
        xs, ws = xs[1:], ws[count:]
    return turns + xs


def tail_batches(plan):
    return [(plan.T1, 2), (0, 2)] + [(k, 1) for k in range(2, plan.T1)]


def tail_kernel(plan, lens, dz2, dzland, x2, x2land, cot, beyond, x, X5_hbm, taps_hbm, grads, pgrad,
                old, half_state,
                gz, gz_got, sums, summed,
                ext, D3, D0T, wcat, pick, eye, cols, y, part, split, acc, X5, X5_sems,
                taps, bulk_sems, *rest):
    t = pl.program_id(0)
    s, z, i, h = plan.place()
    L, Lp, C, wb, g, nw = plan.L, plan.Lp, plan.C, plan.wb, plan.g, plan.nw
    Ch, cs, T1 = plan.Ch, plan.cs, plan.T1
    M = wb * Lp
    nD = plan.steps
    turns = tail_turns(plan)
    last = len(turns) - 1
    peers = group_peers(plan)
    red = Reduction(plan, tail_batches(plan), *rest[:8])
    link = rest[8:]

    def member(off):
        return (s, h * g + wrap(i + off, g))

    def send(first, count):
        rows = pl.ds(first, count)
        for off in range(1, g):
            remote(
                part.at[off - 1, rows],
                gz_got.at[off, rows],
                bulk_sems.at[0, off],
                bulk_sems.at[1, off],
                member(off),
            ).start()

    def X5_copy(k):
        return pltpu.make_async_copy(X5_hbm.at[k], X5.at[k % 2], X5_sems.at[k % 2])

    def when(at):
        return pl.when(t == min(at, last))

    def turn(kind, k):
        return turns.index((kind, k)) if (kind, k) in turns else last

    def turn_of(kind):
        index = jnp.int32(0)
        here = False
        for n, (what, k) in enumerate(turns):
            if what == kind:
                index = jnp.where(t == n, k, index)
                here = (t == n) | here
        return here, index

    taps_copy = pltpu.make_async_copy(
        taps_hbm.at[:, pl.ds(pl.multiple_of(h * Ch, 128), Ch)], taps, X5_sems.at[2]
    )

    @when(0)
    def _():
        taps_copy.start()
        greet(peers.others)
        acc[...] = jnp.zeros_like(acc)
        pick[...] = pick_matrix(L)
        eye[...] = eye_matrix(Ch, Ch, 0)
        mean, rho = norm_of(half_state[ST1 : ST1 + 2], 2.0 * total_of(lens))
        scale = half_state[GAIN1 : GAIN1 + 1] * rho
        offset = half_state[SHIFT1 : SHIFT1 + 1] - mean * scale
        for k, row in enumerate((scale, offset)):
            cols[k] = column(row, L)

    @pl.when(t < nD)
    def _():
        total = total_of(lens)
        mean, rho = norm_of(old[ST2 : ST2 + 2], total)
        gr = old[GAIN2 : GAIN2 + 1] * rho
        sg = old[SU2 : SU2 + 1] / total
        gg = old[SU2 + 1 : SU2 + 2] / total
        rowc = rows_of((Lp, C))
        row1 = rows_of((1, C))

        by_dz = 0.5 * gr
        by_v = -0.5 * gr * rho * gg
        by_1 = 0.5 * gr * (mean * rho * gg - sg)

        def back(dout, dz, v):
            return 0.5 * dout + by_dz * dz + by_v * v + by_1

        def grad_of(w):
            at = t * wb + w
            valid = lens[i * nw + at] - s * Lp
            d = back(cot[w].astype(F32), dz2[w], x2[w])
            d = jnp.where(rowc < valid, d, 0.0)
            one = pl.ds(at, 1)
            dl = back(beyond[0, 2, one, :], dzland[0, one, :], x2land[0, w, EDGE - 1 : EDGE].astype(F32))
            dl = jnp.where((row1 - 1 < valid) & (s > 0), dl, 0.0)
            dh = back(beyond[1, 2, one, :], dzland[1, one, :], x2land[1, w, 0:1].astype(F32))
            dh = jnp.where(row1 + Lp < valid, dh, 0.0)
            ext[w, 7:8] = dl
            ext[w, 8 : 8 + Lp] = d
            ext[w, 8 + Lp : 9 + Lp] = dh
            top, end = w * Lp, (w + 1) * Lp
            D3[t, top:end, 0:C] = ext[w, 9 : 9 + Lp].astype(BF16)
            D3[t, top:end, C : 2 * C] = d.astype(BF16)
            D3[t, top:end, 2 * C : 3 * C] = ext[w, 7 : 7 + Lp].astype(BF16)

        for w in range(wb):
            grad_of(w)
        half = D3[t, :, pl.ds(pl.multiple_of(C + h * Ch, 128), Ch)]
        D0T[:, pl.ds(pl.multiple_of(t * M, 128), M)] = half.T

    @when(0)
    def _():
        taps_copy.wait()
        for first in range(0, Ch, 64):
            rows = slice(first, min(first + 64, Ch))
            for r, parts in enumerate((((0,), (1, 2), (3, 4)), ((0, 1), (2, 3), (4,)))):
                for k, which in enumerate(parts):
                    v = taps[which[0], rows]
                    if len(which) > 1:
                        v = (v.astype(F32) + taps[which[1], rows].astype(F32)).astype(BF16)
                    at = r * Ch
                    wcat[at + rows.start : at + rows.stop, k * C : (k + 1) * C] = v
        meet(peers.others)

    here_x, bx = turn_of("x")

    def gradient(hf, nh):
        lanes = lanes_of((Ch, L))

        def through(w):
            valid = 2 * lens[i * nw + bx * wb + w] - s * L
            top, end = w * Lp, (w + 1) * Lp
            v = mm_nt(eye[...], x[w])
            da = jnp.concatenate([y[0:Ch, top:end], y[Ch:, top:end]], axis=1)
            da = mm(da.astype(BF16), pick[...])
            zv = v * cols[0] + cols[1]
            dzw = da * gelu_slope(zv)
            dzw = jnp.where(lanes < valid, dzw, 0.0)
            acc[0] += fold_lanes(dzw)
            acc[1] += fold_lanes(dzw * zv)
            split[w % 2] = dzw.astype(BF16)
            for off in range(g):
                rows = pl.ds(pl.multiple_of(lax.rem(i + off, g) * cs, 16), cs)
                if off == 0:
                    gz[w] = split[w % 2, rows]
                else:
                    part[off - 1, bx * wb + w] = split[w % 2, rows]

        n = wb // nh
        rows = slice(hf * n * Lp, (hf + 1) * n * Lp)
        y[:, rows] = mm_nt(wcat[...], D3[bx, rows])
        for w in range(hf * n, (hf + 1) * n):
            through(w)

    nh = 2 if wb % 2 == 0 and wb * Lp // 2 % 128 == 0 else 1

    @pl.when(here_x)
    def _():
        gradient(0, nh)
        send(bx * wb, wb // nh)

    first = min(1, last)
    table = (
        (first, 1, red.step1, 0),
        (max(turn("w", 1), first + 1), 1, red.step2, 0),
        (turn("w", 1), 1, red.step0, 1),
        (turn("x", 1), 0, red.step1, 1),
        (turn("w", 2), 1, red.step0, 2),
        (turn("x", 2), 0, red.step1, 2),
        (turn("x", 2), 1, red.step3, 0),
        (turn("x", 2), 1, red.step2, 1),
        (turn("w", 3), 1, red.step0, 3),
        (turn("w", 4), 1, red.step0, 4),
        (turn("w", 4), 1, red.step1, 3),
        (turn("w", 4), 1, red.step2, 2),
        (turn("x", 3), 0, red.step1, 4),
        (turn("x", 3), 0, red.step4, 0),
        (turn("x", 3), 0, red.step3, 1),
        (last, 1, red.step2, 3),
        (last, 1, red.step3, 2),
        (last, 1, red.step2, 4),
    )

    def between(at, end):
        return end == 0 and nh == 2 and turns[at][0] == "x"

    def go_on(entries):
        for at, _, step, batch in entries:

            @when(at)
            def _():
                step(batch)

    go_on([e for e in table if between(*e[:2])])

    if nh == 2:

        @pl.when(here_x)
        def _():
            gradient(1, nh)

    @when(0)
    def _():
        hs = plan.H // plan.nz
        rb = plan.rb
        for u in range(2):

            def rows(j, m, u=u):
                side, r = m * rb // hs, m * rb % hs
                n = 2 * side + u
                rows = slice(j * hs + r, j * hs + r + rb)
                v = grads[rows, n * C : (n + 1) * C] if n < plan.T2 else pgrad[rows]
                return v.astype(F32)

            red.put(T1 + u, rows)
        red.step0(0)

    @when(1)
    def _():
        X5_copy(0).start()
        X5_copy(1).start()

    here_w, k = turn_of("w")

    @pl.when(here_w)
    def _():
        X5_copy(k).wait()
        y[0:Ch, 0:C] = mm(D0T[...], X5[lax.rem(k, 2)])

        @pl.when(k < T1 - 2)
        def _():
            X5_copy(k + 2).start()

        rb = plan.rb
        red.put(k, lambda j, m: y[j * cs + m * rb : j * cs + (m + 1) * rb, 0:C])

    @when(turn("x", nD - 1))
    def _():
        packet = link[0]
        packet[...] = jnp.zeros_like(packet)
        packet[0:1, 0:Ch] = jnp.sum(acc[0].T, axis=0, keepdims=True)
        packet[1:2, 0:Ch] = jnp.sum(acc[1].T, axis=0, keepdims=True)
        peers.start(link)

    go_on([e for e in table if not between(*e[:2])])

    @pl.when(here_x & (bx < nD - 1))
    def _():
        if nh == 2:
            send(bx * wb + wb // nh, wb // nh)

    @when(last)
    def _():
        if nh == 2:
            send(nw - wb // 2, wb // 2)

    @when(last)
    def _():
        red.step3(3)
        red.step4(1)
        red.step4(2)
        red.step3(4)
        red.step4(3)
        got = peers.finish(link)[:, 0:Ch]
        shift, gain = half_state[SHIFT1 : SHIFT1 + 1], half_state[GAIN1 : GAIN1 + 1]
        sums[0:1] = got[0:1]
        sums[1:2] = (got[1:2] - shift * got[0:1]) / gain
        red.step4(4)
        for b in range(5):
            red.step5(b)
        own = pltpu.make_async_copy(red.out, summed, X5_sems.at[0])
        own.start()
        for off in range(1, g):
            done = remote(
                part.at[off - 1],
                gz_got.at[off],
                bulk_sems.at[0, off],
                bulk_sems.at[1, off],
                member(off),
            )
            done.wait_recv()
            done.wait_send()
        own.wait()


def input_grad_kernel(plan, wg, lens, x, gz, gz_got, sums, res, res_got, summed,
                      state, half_state,
                      out, out_result, conv_grad, dil_grad, point_grad,
                      g1, b1, g2, b2, g3, b3, pb, eye, cols, xt):
    t = pl.program_id(0)
    s, z, i, h = plan.place()
    L, Ch, cs = plan.L, plan.Ch, plan.cs
    turn = plan.nw // wg
    mine = pl.ds(pl.multiple_of(i * cs, 16), cs)

    @pl.when(first_step())
    def _():
        n = 2.0 * total_of(lens)
        mean, rho = norm_of(half_state[ST1 : ST1 + 2], n)
        gr = half_state[GAIN1 : GAIN1 + 1] * rho
        gg = sums[1:2] / n * rho
        for k, row in enumerate((gr, -gr * gg, gr * (mean * gg - sums[0:1] / n))):
            xt[...] = column(row, L)
            cols[k] = xt[mine]
        eye[...] = eye_matrix(cs, Ch, i * cs)

        def mine_of(src, at, which, count, *dsts):
            n = dsts[0].shape[1]
            for k in range(count):

                @pl.when(which == k)
                def _():
                    for dst, r in zip(dsts, at):
                        dst[...] = src[r : r + 1, k * n : (k + 1) * n]

        mine_of(sums, (1, 0), i, plan.g, g1, b1)
        mine_of(state, (SU2 + 1, SU2), z, plan.nz, g2, b2)
        mine_of(state, (SU3 + 1, SU3), z, plan.nz, g3, b3)
        mine_of(state, (BSUM,), z, plan.nz, pb)

    own = lax.div(t, turn) == i
    for w in range(wg):
        out_result[w] = jnp.where(own, res[0, w], res_got[0, w])

    C, T1, hs, rb, wide = plan.C, plan.T1, plan.H // plan.nz, plan.rb, plan.C // 2
    count = plan.NW // wg
    turns = min(count, plan.chips)
    per, every = plan.chips // turns, count // turns

    def spread(chunk):
        for n in range(per):
            m = chunk * per + n
            side, r = m * rb // hs, m * rb % hs
            for c in range(2):
                at = slice(c * wide, (c + 1) * wide)
                for k in range(T1):
                    conv_grad[k, n * rb : (n + 1) * rb, at] = summed[k, c, n].astype(F32)
                for u in range(2):
                    v = summed[T1 + u, c, n].astype(F32)
                    if 2 * side + u < plan.T2:
                        dil_grad[2 * side + u, r : r + rb, at] = v
                    else:
                        point_grad[r : r + rb, at] = v

    for chunk in range(turns):
        pl.when(t == chunk * every)(partial(spread, chunk))

    lanes = lanes_of((cs, L))
    for w in range(wg):
        valid = 2 * lens[t * wg + w] - s * L
        v = mm_nt(eye[...], x[w])
        dz = jnp.where(own, gz[w], gz_got[0, w]).astype(F32)
        r = cols[0] * dz + v * cols[1] + cols[2]
        out[w] = jnp.where(lanes < valid, r, 0.0).astype(BF16)


def call(kernel, plan, name, steps, ins, outs, scratch, flops, nbytes, cid=None):
    extra = {} if cid is None else dict(collective_id=cid, has_side_effects=True)
    return pl.pallas_call(
        partial(kernel, plan),
        grid=(steps,),
        in_specs=[SMEM] + [spec for spec, _ in ins],
        out_specs=[spec for spec, _, _ in outs],
        out_shape=[jax.ShapeDtypeStruct(shape, dtype) for _, shape, dtype in outs],
        scratch_shapes=scratch,
        compiler_params=pltpu.CompilerParams(vmem_limit_bytes=VMEM_LIMIT, **extra),
        cost_estimate=pl.CostEstimate(
            flops=int(flops), bytes_accessed=int(nbytes), transcendentals=0
        ),
        name=name,
    )


def per_device(
    inputs,
    lengths,
    input_gain,
    input_shift,
    conv_weight,
    branch_gain,
    branch_shift,
    dilated_tap_weight,
    mixer_gain,
    mixer_shift,
    point_weight,
    point_bias,
    cotangent,
):
    NW, L, C = inputs.shape
    Lp = L // 2
    nz = lax.axis_size("ch")
    R = 2
    plan = Plan(
        ns=lax.axis_size("seq"),
        nz=nz,
        R=R,
        NW=NW,
        L=L,
        C=C,
        H=mixer_gain.shape[0] * nz,
        T1=conv_weight.shape[0],
        T2=dilated_tap_weight.shape[0],
        wb=min(NW * R // nz, max(1, 512 // Lp)),
    )
    g, nw, cs, Ch, H, Hh, wb = plan.g, plan.nw, plan.cs, plan.Ch, plan.H, plan.Hh, plan.wb
    T1, T2, steps = plan.T1, plan.T2, plan.steps
    M = wb * Lp
    hs = H // nz
    lens = lengths.astype(jnp.int32)

    def row(a):
        return a.reshape(1, a.shape[0])

    def grp():
        return lax.rem(lax.axis_index("ch"), g)

    def half():
        return lax.div(lax.axis_index("ch"), g)

    def core():
        return lax.rem(lax.axis_index("seq"), 2)

    def chip4():
        return lax.div(lax.axis_index("seq"), plan.ns // 4)

    def whole(*shape):
        return pl.BlockSpec(shape, lambda t: (0,) * len(shape), pipeline_mode=pl.Buffered(1))

    def const(*shape):
        return pl.BlockSpec(shape, lambda t: (0,) * len(shape))

    def win(*shape):
        return pl.BlockSpec(shape, lambda t: (t,) + (0,) * (len(shape) - 1))

    def arg_win(n, width):
        return pl.BlockSpec((wb, n, width), lambda t: (grp() * steps + t, 0, 0))

    def ins(*pairs):
        return [p for p in pairs]

    share = NW // nz
    nm = max(1, share // wb)

    def edge_spec(n):
        return pl.BlockSpec(
            (nw, 16, C), lambda t: (grp(), n, 0), pipeline_mode=pl.Buffered(1)
        )

    def head_block(t):
        own = lax.div(lax.axis_index("ch") * share, wb) + t
        return jnp.where(t < nm, own, grp() * steps + t - nm), 0, 0

    def after(*shape):
        return pl.BlockSpec(
            shape, lambda t: (jnp.maximum(t - nm, 0),) + (0,) * (len(shape) - 1)
        )

    pairs = ins(
        (pl.BlockSpec((wb, L, C), head_block), inputs),
        (edge_spec(0), inputs),
        (edge_spec(L // 16 - 1), inputs),
        (edge_spec(0), cotangent),
        (edge_spec(Lp // 16 - 1), cotangent),
        (whole(1, cs), row(branch_gain)),
        (whole(1, cs), row(branch_shift)),
        (whole(1, cs), row(point_bias)),
        (whole(1, H // nz), row(mixer_gain)),
        (whole(1, H // nz), row(mixer_shift)),
        (ANY, conv_weight.reshape(T1 * C, C)),
        (whole(C), input_gain),
        (whole(C), input_shift),
        (
            pl.BlockSpec(
                (1, hs, C // 2),
                lambda t: (jnp.minimum(chip4(), T2 - 1), 0, core()),
                pipeline_mode=pl.Buffered(1),
            ),
            jnp.swapaxes(dilated_tap_weight, 1, 2),
        ),
        (
            pl.BlockSpec(
                (hs, C // 2), lambda t: (0, core()), pipeline_mode=pl.Buffered(1)
            ),
            point_weight,
        ),
    )
    plane, line, group = plane_peers(plan), line_peers(plan), group_peers(plan)
    state_shape = (STATE, C)
    edges2, edges3 = (2, nw, EDGE, C), (2, nw, EDGE, H)
    X5, x2, land2, state, beyond, full = call(
        lambda plan, *refs: head_kernel(plan, nm, *refs),
        plan,
        "head",
        nm + steps,
        pairs,
        [
            (
                pl.BlockSpec((T1, M, C), lambda t: (0, jnp.maximum(t - nm, 0), 0)),
                (T1, nw * Lp, C),
                BF16,
            ),
            (after(wb, Lp, C), (nw, Lp, C), F32),
            (ANY, edges2, BF16),
            (const(*state_shape), state_shape, F32),
            (const(2, 3, nw, C), (2, 3, nw, C), F32),
            (ANY, (2, T2 + 1, nz, hs, C // 2), BF16),
        ],
        [
            pltpu.VMEM((2, 8, C), F32),
            pltpu.VMEM((2, 3, nw, C), F32),
            pltpu.VMEM((2, 3, nw, C), F32),
            pltpu.VMEM((T1 * Lp, L), BF16),
            pltpu.VMEM(edges2, BF16),
            pltpu.VMEM((2, C), F32),
            pltpu.VMEM((T1 * C, C), BF16),
            pltpu.SemaphoreType.DMA,
            pltpu.VMEM((hs, C // 2), BF16),
            pltpu.SemaphoreType.DMA((2, 4)),
            HALO_SEMS,
            HALO_SEMS,
        ]
        + plane.scratch(2, C)
        + line.scratch(3, C)
        + group.scratch(2, C),
        2 * nw * Lp * T1 * C * C,
        nw * Lp * C * 20,
        cid=1,
    )(lens, *[a for _, a in pairs])

    full = full.reshape(2, T2 + 1, H, C // 2)
    taps_spec = whole(2, T2, H, C // 2)
    pw_spec = pl.BlockSpec(
        (2, 1, H, C // 2), lambda t: (0, T2, 0, 0), pipeline_mode=pl.Buffered(1)
    )

    def early(*shape):
        return pl.BlockSpec(
            shape, lambda t: (jnp.minimum(t, steps - 1),) + (0,) * (len(shape) - 1)
        )

    def early_land(width):
        return pl.BlockSpec(
            (2, wb, EDGE, width), lambda t: (0, jnp.minimum(t, steps - 1), 0, 0)
        )

    def half_of(n):
        return pl.BlockSpec((n, Ch), lambda t: (0, half()), pipeline_mode=pl.Buffered(1))

    cot_spec = pl.BlockSpec(
        (wb, Lp, C), lambda t: (grp() * steps + jnp.minimum(t, steps - 1), 0, 0)
    )

    p0, r0, b0, g0, block_steps = block_phases(plan)

    def at_phase(first):
        return lambda t: jnp.clip(t - first, 0, steps - 1)

    in_p, in_b = at_phase(p0), at_phase(b0)
    pairs = ins(
        (
            pl.BlockSpec(
                (wb, Lp, C),
                lambda t: (jnp.where(t < p0 + steps, jnp.minimum(t, steps - 1), in_b(t)), 0, 0),
            ),
            x2,
        ),
        (ANY, x2),
        (early_land(C), land2),
        (pl.BlockSpec((wb, Lp, C), lambda t: (grp() * steps + in_p(t), 0, 0)), cotangent),
        (taps_spec, full),
        (pw_spec, full),
        (whole(*state_shape), state),
        (half_of(STATE), state),
    )
    dz2, grads, pgrad, res, dland2, state, res_got = call(
        block_kernel,
        plan,
        "block",
        block_steps,
        pairs,
        [
            (pl.BlockSpec((wb, Lp, C), lambda t: (in_b(t), 0, 0)), (nw, Lp, C), F32),
            (const(Hh, T2 * C), (Hh, T2 * C), BF16),
            (const(Hh, C), (Hh, C), BF16),
            (const(g, nw, cs, Lp), (g, nw, cs, Lp), BF16),
            (ANY, (2, nw, C), F32),
            (const(*state_shape), state_shape, F32),
            (ANY, (g, nw, cs, Lp), BF16),
        ],
        [
            pltpu.VMEM((wb, Lp + 2 * EDGE, C), F32),
            pltpu.VMEM((H, T2 * C), BF16),
            pltpu.VMEM((T2 * H, C), BF16),
            pltpu.VMEM((H, C), BF16),
            pltpu.VMEM((nw * Lp, T2 * C), BF16),
            pltpu.VMEM((nw, Lp, H), F32),
            pltpu.VMEM((nw, Lp, H), F32),
            pltpu.VMEM((M, H), F32),
            pltpu.VMEM((nw * Lp, H), BF16),
            pltpu.VMEM((H, nw * Lp), BF16),
            pltpu.VMEM((nw * Lp, C), BF16),
            pltpu.VMEM((M, T2 * H), BF16),
            pltpu.VMEM((H, nw * Lp), BF16),
            pltpu.VMEM(edges3, BF16),
            pltpu.VMEM(edges3, BF16),
            pltpu.VMEM((1, 2 * H), F32),
            pltpu.VMEM(edges3, BF16),
            pltpu.VMEM(edges3, BF16),
            pltpu.VMEM((2, C), F32),
            pltpu.VMEM((2, nw, C), F32),
            pltpu.VMEM((2, C), F32),
            pltpu.SemaphoreType.DMA((3, 2, 2)),
            pltpu.SemaphoreType.DMA((2, g)),
            pltpu.VMEM((nw, Lp, Ch), F32),
            pltpu.SemaphoreType.DMA,
        ]
        + group.scratch(1, 2 * H)
        + group.scratch(2, C)
        + group.scratch(2, C),
        nw * Lp * C * H * (6 * T2 + 6),
        nw * Lp * C * 30,
        cid=3,
    )(lens, *[a for _, a in pairs])

    chips, rb = plan.chips, plan.rb
    turns_t = tail_turns(plan)

    def x_block(t):
        block = jnp.int32(0)
        for n, (what, k) in enumerate(turns_t):
            if what == "x":
                block = jnp.where(t >= n, k, block)
        return block

    sshape = (T1 + 2, 2, chips, rb, C // 2)
    pairs = ins(
        (early(wb, Lp, C), dz2),
        (whole(2, nw, C), dland2),
        (early(wb, Lp, C), x2),
        (early_land(C), land2),
        (cot_spec, cotangent),
        (whole(2, 3, nw, C), beyond),
        (
            pl.BlockSpec(
                (wb, L, Ch), lambda t: (grp() * steps + x_block(t), 0, half())
            ),
            inputs,
        ),
        (ANY, X5),
        (ANY, conv_weight),
        (whole(Hh, T2 * C), grads),
        (whole(Hh, C), pgrad),
        (whole(*state_shape), state),
        (half_of(STATE), state),
    )
    gz, gz_got, sums1, summed = call(
        tail_kernel,
        plan,
        "tail",
        len(turns_t),
        pairs,
        [
            (pl.BlockSpec((wb, cs, L), lambda t: (x_block(t), 0, 0)), (nw, cs, L), BF16),
            (ANY, (g, nw, cs, L), BF16),
            (const(2, Ch), (2, Ch), F32),
            (ANY, sshape, BF16),
        ],
        [
            pltpu.VMEM((wb, Lp + 16, C), F32),
            pltpu.VMEM((steps, M, 3 * C), BF16),
            pltpu.VMEM((Ch, nw * Lp), BF16),
            pltpu.VMEM((2 * Ch, 3 * C), BF16),
            pltpu.VMEM((L, L), BF16),
            pltpu.VMEM((Ch, Ch), BF16),
            pltpu.VMEM((2, Ch, L), F32),
            pltpu.VMEM((2 * Ch, max(M, C)), F32),
            pltpu.VMEM((g - 1, nw, cs, L), BF16),
            pltpu.VMEM((2, Ch, L), BF16),
            pltpu.VMEM((2, Ch, min(L, 128)), F32),
            pltpu.VMEM((2, nw * Lp, C), BF16),
            pltpu.SemaphoreType.DMA((3,)),
            pltpu.VMEM((T1, Ch, C), BF16),
            pltpu.SemaphoreType.DMA((2, g)),
        ]
        + Reduction.scratch(plan, tail_batches(plan))
        + group.scratch(2, C),
        2 * nw * Lp * (6 + T1) * C * Ch,
        nw * Lp * C * 40,
        cid=6,
    )(lens, *[a for _, a in pairs])

    wg = min(2 * wb, nw)
    count = NW // wg
    turn = nw // wg
    turns = min(count, chips)

    def own_block(t):
        return jnp.where(lax.div(t, turn) == grp(), lax.rem(t, turn), 0)

    def got_slot(t):
        off = lax.rem(grp() - lax.div(t, turn) + g, g)
        return jnp.maximum(off, 1), jnp.where(off > 0, lax.rem(t, turn), 0)

    pairs = ins(
        (pl.BlockSpec((wg, L, Ch), lambda t: (t, 0, half())), inputs),
        (pl.BlockSpec((wg, cs, L), lambda t: (own_block(t), 0, 0)), gz),
        (pl.BlockSpec((1, wg, cs, L), lambda t: got_slot(t) + (0, 0)), gz_got),
        (whole(2, Ch), sums1),
        (pl.BlockSpec((1, wg, cs, Lp), lambda t: (grp(), own_block(t), 0, 0)), res),
        (pl.BlockSpec((1, wg, cs, Lp), lambda t: got_slot(t) + (0, 0)), res_got),
        (
            pl.BlockSpec(
                (T1 + 2, 2, chips // turns, rb, C // 2),
                lambda t: (0, 0, t * turns // count, 0, 0),
            ),
            summed,
        ),
        (whole(*state_shape), state),
        (half_of(STATE), state),
    )
    outs = call(
        lambda plan, *refs: input_grad_kernel(plan, wg, *refs),
        plan,
        "input_grad",
        count,
        pairs,
        [
            (win(wg, cs, L), (NW, cs, L), BF16),
            (win(wg, cs, Lp), (NW, cs, Lp), BF16),
            (
                pl.BlockSpec((T1, cs // turns, C), lambda t: (0, t * turns // count, 0)),
                (T1, cs, C),
                F32,
            ),
            (const(T2, hs, C), (T2, hs, C), F32),
            (const(hs, C), (hs, C), F32),
        ]
        + [(const(1, n), (1, n), F32) for n in (cs, cs, cs, cs, hs, hs, cs)],
        [
            pltpu.VMEM((cs, Ch), BF16),
            pltpu.VMEM((3, cs, L), F32),
            pltpu.VMEM((Ch, L), F32),
        ],
        2 * NW * L * Ch * cs,
        NW * L * cs * 8,
    )(lens, *[a for _, a in pairs])
    grad, result, conv_grad, dil_grad, point_grad = outs[:5]
    g1, b1, g2, b2, g3, b3, pb = [a[0] for a in outs[5:]]
    return (
        jnp.swapaxes(result, 1, 2),
        jnp.swapaxes(grad, 1, 2),
        jnp.swapaxes(conv_grad, 1, 2),
        g1,
        b1,
        g2,
        b2,
        jnp.swapaxes(dil_grad, 1, 2),
        g3,
        b3,
        point_grad,
        pb,
    )


def solution(mesh):
    in_specs = (
        P(None, "seq", None),
        P(),
        P(),
        P(),
        P(),
        P("ch"),
        P("ch"),
        P(None, None, "ch"),
        P("ch"),
        P("ch"),
        P("ch", None),
        P("ch"),
        P(None, "seq", None),
    )
    out_specs = (
        P(None, "seq", "ch"),
        P(None, "seq", "ch"),
        P(None, None, "ch"),
        P("ch"),
        P("ch"),
        P("ch"),
        P("ch"),
        P(None, None, "ch"),
        P("ch"),
        P("ch"),
        P("ch", None),
        P("ch"),
    )
    return jax.shard_map(
        per_device, mesh=mesh, in_specs=in_specs, out_specs=out_specs, check_vma=False
    )
```

```python
from functools import partial
from typing import NamedTuple

import jax
import jax.numpy as jnp
from jax import lax
from jax.experimental import pallas as pl
from jax.experimental.pallas import tpu as pltpu
from jax.sharding import PartitionSpec as P

DIL = 14
EDGE = 16
EPS = 1e-05
GC0 = 0.7978845608028654
GC1 = 0.044715
F32 = jnp.float32
BF16 = jnp.bfloat16
MESH = pl.DeviceIdType.MESH
VMEM_LIMIT = 58 * 1024 * 1024
ANY = pl.BlockSpec(memory_space=pl.ANY)
SMEM = pl.BlockSpec(memory_space=pltpu.SMEM)


ST1, GAIN2, SHIFT2, BIAS, GAIN3, SHIFT3, GAIN1, SHIFT1, ST2, ST3, SU3, BSUM, SU2 = (
    0, 2, 3, 4, 5, 6, 7, 8, 9, 11, 13, 15, 16
)
STATE = 24


class Plan(NamedTuple):
    ns: int
    nz: int
    R: int
    NW: int
    L: int
    C: int
    H: int
    T1: int
    T2: int
    wb: int

    @property
    def g(self):
        return self.nz // self.R

    @property
    def nw(self):
        return self.NW // self.g

    @property
    def Lp(self):
        return self.L // 2

    @property
    def cs(self):
        return self.C // self.nz

    @property
    def Ch(self):
        return self.C // self.R

    @property
    def Hh(self):
        return self.H // self.R

    @property
    def steps(self):
        return self.nw // self.wb

    @property
    def chips(self):
        return self.ns // 2

    @property
    def rb(self):
        return self.cs // self.chips

    def place(self):
        s, z = lax.axis_index("seq"), lax.axis_index("ch")
        return s, z, lax.rem(z, self.g), lax.div(z, self.g)


def gelu(z):
    t = jnp.tanh(z * (GC0 + (GC0 * GC1) * (z * z)))
    return z * (0.5 + 0.5 * t)


def gelu_both(z):
    sq = z * z
    t = jnp.tanh(z * (GC0 + (GC0 * GC1) * sq))
    h = 0.5 + 0.5 * t
    v = z * h
    return v, h + v * (1.0 - t) * (GC0 + (3.0 * GC0 * GC1) * sq)


def gelu_slope(z):
    return gelu_both(z)[1]


def fold(v):
    return jnp.sum(v.reshape(v.shape[0] // 8, 8, v.shape[1]), axis=0)


def fold_lanes(v):
    out = v[:, 0:128]
    for k in range(128, v.shape[1], 128):
        out = out + v[:, k : k + 128]
    return out


def unfold(v):
    return jnp.sum(v, axis=0, keepdims=True)


def rows_of(shape):
    return lax.broadcasted_iota(jnp.int32, shape, 0)


def lanes_of(shape):
    return lax.broadcasted_iota(jnp.int32, shape, 1)


def total_of(lens):
    n = lens[0]
    for k in range(1, lens.shape[0]):
        n = n + lens[k]
    return n.astype(F32)


def norm_of(stats, total):
    mean = stats[0:1] / total
    square = stats[1:2] / total
    return mean, lax.rsqrt(square - mean * mean + EPS)


def flat(ref):
    return ref[...].reshape(1, ref.shape[0])


def column(row, n):
    return jnp.broadcast_to(row, (n, row.shape[1])).T


def mm(a, b):
    return jnp.dot(a, b, preferred_element_type=F32)


def mm_nt(a, b):
    return lax.dot_general(a, b, (((1,), (1,)), ((), ())), preferred_element_type=F32)


def mm_tn(a, b):
    return lax.dot_general(a, b, (((0,), (0,)), ((), ())), preferred_element_type=F32)


def mm_tt(a, b):
    return lax.dot_general(a, b, (((0,), (1,)), ((), ())), preferred_element_type=F32)


def eye_matrix(n, m, first):
    return jnp.where(lanes_of((n, m)) == rows_of((n, m)) + first, 1.0, 0.0).astype(BF16)


def pick_matrix(L):
    r, n = rows_of((L, L)), lanes_of((L, L))
    bin_of = 2 * r - jnp.where(r >= L // 2, L - 1, 0)
    return jnp.where(n == bin_of, 1.0, 0.0).astype(BF16)


def remote(src, dst, send, recv, device):
    return pltpu.make_async_remote_copy(
        src_ref=src,
        dst_ref=dst,
        send_sem=send,
        recv_sem=recv,
        device_id=device,
        device_id_type=MESH,
    )


def wrap(v, n):
    return jnp.where(v >= n, v - n, v)


def greet(devices):
    barrier = pltpu.get_barrier_semaphore()
    for device in devices:
        pl.semaphore_signal(barrier, inc=1, device_id=device, device_id_type=MESH)


def meet(devices):
    pl.semaphore_wait(pltpu.get_barrier_semaphore(), len(devices))


class Peers:
    def __init__(self, me, others):
        self.me, self.others = me, others
        self.count = len(others) + 1

    def start(self, link):
        packet, buf, sems = link
        for device in self.others:
            remote(packet, buf.at[self.me], sems.at[0], sems.at[1], device).start()

    def finish(self, link):
        packet, buf, sems = link
        buf[self.me] = packet[...]
        rest = buf.at[pl.ds(0, self.count - 1)]
        done = remote(rest, rest, sems.at[0], sems.at[1], self.others[0])
        done.wait_recv()
        acc = buf[0]
        for q in range(1, self.count):
            acc = acc + buf[q]
        done.wait_send()
        return acc

    def scratch(self, rows, width):
        return [
            pltpu.VMEM((rows, width), F32),
            pltpu.VMEM((self.count, rows, width), F32),
            pltpu.SemaphoreType.DMA((2,)),
        ]


def group_peers(plan):
    s, z, i, h = plan.place()
    g = plan.g
    others = [
        (wrap(s + a, plan.ns), h * g + wrap(i + b, g))
        for a in range(plan.ns)
        for b in range(g)
        if a or b
    ]
    return Peers(s * g + i, others)


def plane_peers(plan):
    s, z, i, h = plan.place()
    return Peers(s, [(wrap(s + a, plan.ns), z) for a in range(1, plan.ns)])


def line_peers(plan):
    s, z, i, h = plan.place()
    return Peers(z, [(s, wrap(z + a, plan.nz)) for a in range(1, plan.nz)])


class Halo:
    def __init__(self, plan, edge, land, sems):
        self.edge, self.land, self.sems = edge, land, sems
        s, z, _, _ = plan.place()
        self.to = ((wrap(s + plan.ns - 1, plan.ns), z), (wrap(s + 1, plan.ns), z))

    def copy(self, side, rows):
        return remote(
            self.edge.at[side, rows],
            self.land.at[1 - side, rows],
            self.sems.at[0, side],
            self.sems.at[1, side],
            self.to[side],
        )

    def start(self, first, count):
        for side in range(2):
            self.copy(side, pl.ds(first, count)).start()

    def finish(self):
        for side in range(2):
            done = self.copy(side, pl.ds(0, self.land.shape[1]))
            done.wait_recv()
            done.wait_send()


HALO_SEMS = pltpu.SemaphoreType.DMA((2, 2))


class Gather:
    def __init__(self, plan, part, full, sems):
        self.plan, self.part, self.full, self.sems = plan, part, full, sems
        self.s, self.z, self.i, self.h = plan.place()
        self.c, self.m = lax.rem(self.s, 2), lax.div(self.s, 2)
        self.chips = plan.chips
        self.every = self.chips // 4
        self.tap = lax.div(self.m, self.every)
        self.owner = lax.rem(self.m, self.every) == 0
        self.mine = full.at[self.c, self.tap]

    def others(self):
        g, nz = self.plan.g, self.plan.nz
        return [(self.s, wrap(self.h * g + g + r, nz)) for r in range(nz - g)]

    def far(self, off):
        return (2 * wrap(self.m + off, self.chips) + self.c, self.z)

    def line(self, off):
        nz = self.plan.nz
        device = (self.s, wrap(self.z + off, nz))
        dst = self.mine.at[nz - off]
        return remote(self.part, dst, self.sems.at[0, 1], self.sems.at[1, 1], device)

    def far_rows(self, taps):
        return self.full.at[self.c, taps, pl.ds(1, self.plan.nz - 1)]

    def chip(self, off):
        rows = self.far_rows(self.tap)
        return remote(rows, rows, self.sems.at[0, 2], self.sems.at[1, 2], self.far(off))

    def pair(self):
        half = self.far_rows(pl.ds(0, 4))
        device = (2 * self.m + 1 - self.c, self.z)
        return remote(half, half, self.sems.at[0, 3], self.sems.at[1, 3], device)

    def line_start(self):
        @pl.when(self.owner)
        def _():
            for off in range(1, self.plan.nz):
                self.line(off).start()

    def line_finish(self):
        @pl.when(self.owner)
        def _():
            rest = self.far_rows(self.tap)
            device = (self.s, wrap(self.z + 1, self.plan.nz))
            done = remote(rest, rest, self.sems.at[0, 1], self.sems.at[1, 1], device)
            done.wait_recv()
            done.wait_send()

    def chips_start(self):
        @pl.when(self.owner)
        def _():
            for off in range(1, self.chips):
                self.chip(off).start()

    def pair_start(self):
        def taken(count):
            rest = self.far_rows(pl.ds(0, count))
            return remote(rest, rest, self.sems.at[0, 2], self.sems.at[1, 2], self.far(1))

        @pl.when(self.owner)
        def _():
            taken(3).wait_recv()
            for off in range(1, self.chips):
                self.chip(off).wait_send()

        if self.every > 1:

            @pl.when(jnp.logical_not(self.owner))
            def _():
                taken(4).wait_recv()

        self.pair().start()

    def pair_finish(self):
        done = self.pair()
        done.wait_recv()
        done.wait_send()


def first_step():
    return pl.program_id(0) == 0


def last_step():
    return pl.program_id(0) == pl.num_programs(0) - 1


def head_kernel(plan, nm, lens, x, xtop, xend, ctop, cend, g2, s2, pb, g3, s3,
                w_hbm, gain, shift, taps, pw,
                X5, x2, land, state, beyond_out, full,
                macc, beyond, xedge, sel, edge, acc, w_ref, w_sem, part,
                gather_sems, xhalo_sems, halo_sems, *links):
    t = pl.program_id(0)
    peers, plane, line = group_peers(plan), plane_peers(plan), line_peers(plan)
    xhalo = Halo(plan, xedge, beyond, xhalo_sems)
    halo = Halo(plan, edge, land, halo_sems)
    gather = Gather(plan, part, full, gather_sems)
    w_copy = pltpu.make_async_copy(w_hbm, w_ref, w_sem)
    plane_link, line_link, link = links[:3], links[3:6], links[6:]
    s, z, i, h = plan.place()
    L, Lp, C, nw, nz, wb = plan.L, plan.Lp, plan.C, plan.nw, plan.nz, plan.wb
    share = plan.NW // nz
    c = t - nm
    everyone = peers.others + gather.others()

    @pl.when(first_step())
    def _():
        w_copy.start()
        greet(everyone)
        part[...] = jnp.where(gather.tap == 3, pw[...], taps[0])
        macc[...] = jnp.zeros_like(macc)
        acc[...] = jnp.zeros_like(acc)
        state[...] = jnp.zeros_like(state)
        state[GAIN1 : GAIN1 + 1] = flat(gain)
        state[SHIFT1 : SHIFT1 + 1] = flat(shift)
        n16 = nw * 16
        for side, (xe, ce, places) in enumerate(
            ((xtop, ctop, (0, 1, 0)), (xend, cend, (14, 15, 15)))
        ):
            for k, at in enumerate(places):
                rows, lanes = rows_of((nw, n16)), lanes_of((nw, n16))
                one = jnp.where(lanes == 16 * rows + at, 1.0, 0.0).astype(BF16)
                block = (xe if k < 2 else ce)[...].reshape(n16, C)
                xedge[side, k] = mm(one, block)
        shape = (Lp, L)
        for odd in range(2):
            at = lanes_of(shape) - (2 * rows_of(shape) + odd)
            one = jnp.where((at == 0) | (at == 1), 1.0, 0.0)
            sel[odd * Lp : (odd + 1) * Lp] = one.astype(BF16)

    @pl.when(c < 0)
    def _():
        rows = rows_of((L, C))
        for w in range(min(share, wb)):
            at = lax.rem(z * share, wb) + w
            valid = 2 * lens[z * share + t * wb + w] - s * L
            v = jnp.where(rows < valid, x[at].astype(F32), 0.0)
            macc[0] += fold(v)
            macc[1] += fold(v * v)

    @pl.when(c == -1)
    def _():
        packet, more = plane_link[0], line_link[0]
        packet[0:1] = unfold(macc[0])
        packet[1:2] = unfold(macc[1])
        meet(everyone)
        plane.start(plane_link)
        xhalo.start(0, 3)
        at = 0
        spans = []
        more[2:3] = jnp.zeros((1, C), F32)
        for ref in (g2, s2, pb, g3, s3):
            n = ref.shape[1]
            more[2:3, at : at + n] = ref[...]
            spans.append((at, n))
            at += n
        more[0:2] = plane.finish(plane_link)
        line.start(line_link)
        gather.line_start()
        state[ST1 : ST1 + 2] = line.finish(line_link)[0:2]
        for k in range(nz):
            row = line_link[1][k]
            for r, (at, n) in zip((GAIN2, SHIFT2, BIAS, GAIN3, SHIFT3), spans):
                state[r : r + 1, k * n : (k + 1) * n] = row[2:3, at : at + n]
        xhalo.finish()
        beyond_out[...] = beyond[...]
        w_copy.wait()

    @pl.when(c >= 0)
    def _():
        mean, rho = norm_of(state[ST1 : ST1 + 2], 2.0 * total_of(lens))
        scale = state[GAIN1 : GAIN1 + 1] * rho
        offset = state[SHIFT1 : SHIFT1 + 1] - mean * scale
        rows = rows_of((L, C))
        row1 = rows_of((1, C))
        row16 = rows_of((16, C))
        def activate(w):
            at = c * wb + w
            valid = 2 * lens[i * nw + at] - s * L
            a = gelu(x[w].astype(F32) * scale + offset)
            a = jnp.where(rows < valid, a, 0.0).astype(BF16)
            picked = mm(sel[...], a)
            even, odd = picked[0:Lp], picked[Lp:]
            top, end = w * Lp, (w + 1) * Lp
            before = [pltpu.roll(v, 1, 0) for v in (even, odd)]
            behind = pltpu.roll(even, Lp - 1, 0)
            for k, v in enumerate((*before, even, odd, behind)):
                X5[k, top:end] = v.astype(BF16)

            def beside(side, k, bin_at):
                a = gelu(beyond[side, k, pl.ds(at, 1), :] * scale + offset)
                here = (row1 + bin_at < valid) & (row1 + (s * L + bin_at) >= 0)
                return jnp.where(here, a, 0.0).astype(BF16).astype(F32)

            l0, l1 = beside(0, 0, -2), beside(0, 1, -1)
            r0, r1 = beside(1, 0, L), beside(1, 1, L + 1)
            start = a[0:1].astype(F32)
            for k, row in ((0, l0 + l1), (1, l1 + start)):
                X5[k, top : top + 16] = jnp.where(row16 == 0, row, before[k][0:16]).astype(BF16)
            X5[3, end - 16 : end] = (
                odd[Lp - 16 :] + jnp.where(row16 == 15, r0, 0.0)
            ).astype(BF16)
            X5[4, end - 16 : end] = jnp.where(row16 == 15, r0 + r1, behind[Lp - 16 :]).astype(BF16)

        nc = 256
        rowp = rows_of((Lp, nc))

        def convolve(first, count):
            span = slice(first * Lp, (first + count) * Lp)
            for n in range(C // nc):
                cols = slice(n * nc, (n + 1) * nc)
                taps = [X5[k, span] for k in range(plan.T1)]
                y = 0.5 * mm(jnp.concatenate(taps, axis=1), w_ref[:, cols])
                s0 = jnp.zeros((8, nc), F32)
                s1 = jnp.zeros((8, nc), F32)
                for w in range(first, first + count):
                    at = c * wb + w
                    valid = lens[i * nw + at] - s * Lp
                    v = y[(w - first) * Lp : (w - first + 1) * Lp]
                    x2[w, :, cols] = v
                    edge[0, at, :, cols] = v[:EDGE].astype(BF16)
                    edge[1, at, :, cols] = v[Lp - EDGE :].astype(BF16)
                    v = jnp.where(rowp < valid, v, 0.0)
                    s0 = s0 + fold(v)
                    s1 = s1 + fold(v * v)
                acc[0:1, cols] += unfold(s0)
                acc[1:2, cols] += unfold(s1)

        count = max(1, wb // 2)
        for first in range(0, wb, count):
            for w in range(first, first + count):
                activate(w)
            convolve(first, count)
        halo.start(c * wb, wb)

    @pl.when(c == 0)
    def _():
        gather.line_finish()
        gather.chips_start()

    @pl.when(last_step())
    def _():
        link[0][...] = acc[...]
        peers.start(link)
        gather.pair_start()
        state[ST2 : ST2 + 2] = peers.finish(link)
        halo.finish()
        gather.pair_finish()


def block_kernel(plan, lens, x2, x2_hbm, x2land, cot, w_ref, pw_ref, own_w, own_pw, old, half_state,
                 dz2, grads, pgrad, res, land, state, res_got,
                 ext, wf, wt, pw, Y3, c2, dz3, das, a3s, a3T, dos, Z3, dcT,
                 cedge, cland, cacc, dedge, dland, dacc, bedge, bacc, halo_sems, bulk_sems,
                 x2half, x2_sem, *links):
    t = pl.program_id(0)
    peers = group_peers(plan)
    s, z, i, h = plan.place()
    Lp, C, H, wb, nw, cs, g = plan.Lp, plan.C, plan.H, plan.wb, plan.nw, plan.cs, plan.g
    M = wb * Lp
    steps = plan.steps
    p0, r0, b0, g0 = block_phases(plan)[:4]
    c_link, d_link, b_link = links[:3], links[3:6], links[6:]
    c_halo = Halo(plan, cedge, cland, halo_sems.at[0])
    d_halo = Halo(plan, dedge, dland, halo_sems.at[1])
    b_halo = Halo(plan, bedge, land, halo_sems.at[2])

    def bulk(off, rows):
        to = wrap(i + off, g)
        return remote(
            res.at[to, rows],
            res_got.at[off, rows],
            bulk_sems.at[0, off],
            bulk_sems.at[1, off],
            (s, h * g + to),
        )

    def result_of(block):
        y = mm(a3s[pl.ds(pl.multiple_of(block * M, 128), M)], pw[:, pl.ds(pl.multiple_of(h * plan.Ch, 128), plan.Ch)])
        rowr = rows_of((Lp, y.shape[1]))
        for w in range(wb):
            at = block * wb + w
            valid = lens[i * plan.nw + at] - s * Lp
            r = x2half[at] + y[w * Lp : (w + 1) * Lp] + half_state[BIAS : BIAS + 1]
            r = jnp.where(rowr < valid, r, 0.0).astype(BF16).T
            for k in range(g):
                res[k, at] = r[k * cs : (k + 1) * cs]

    def send_result(block):
        result_of(block)
        for off in range(1, g):
            bulk(off, pl.ds(block * wb, wb)).start()

    half_copy = pltpu.make_async_copy(
        x2_hbm.at[:, :, pl.ds(pl.multiple_of(h * plan.Ch, 128), plan.Ch)], x2half, x2_sem
    )

    @pl.when(first_step())
    def _():
        half_copy.start()
        greet(peers.others)
        state[...] = old[...]
        cacc[...] = jnp.zeros_like(cacc)
        dacc[...] = jnp.zeros_like(dacc)
        bacc[...] = jnp.zeros_like(bacc)
        hs = H // plan.nz

        def rows_at(which, first=0):
            return pl.ds(pl.multiple_of(first + which * hs, 16), hs)

        for r in range(plan.nz):
            at = wrap(z + r, plan.nz)
            for c in range(2):
                cols = slice(c * (C // 2), (c + 1) * (C // 2))
                pw[rows_at(at), cols] = own_pw[:, cols] if r == 0 else pw_ref[c, 0, r]
                for k in range(plan.T2):
                    v = own_w[k, :, cols] if r == 0 else w_ref[c, k, r]
                    wf[rows_at(at), k * C + cols.start : k * C + cols.stop] = v
                    wt[rows_at(at, k * H), cols] = v

    @pl.when(t < p0)
    def _():
        base = pl.multiple_of(t * M, 128)
        mean, rho = norm_of(state[ST2 : ST2 + 2], total_of(lens))
        scale = state[GAIN2 : GAIN2 + 1] * rho
        offset = state[SHIFT2 : SHIFT2 + 1] - mean * scale
        rows = rows_of((Lp, C))
        rowe = rows_of((EDGE, C))

        rowh = rows_of((Lp, H))
        sums0, sums1 = jnp.zeros((8, H), F32), jnp.zeros((8, H), F32)
        nh = min(2, wb)
        for first in range(0, wb, wb // nh):
            span = range(first, first + wb // nh)
            for w in span:
                valid = lens[i * plan.nw + t * wb + w] - s * Lp
                a = jnp.where(rows < valid, gelu(x2[w] * scale + offset), 0.0)
                al = gelu(x2land[0, w].astype(F32) * scale + offset)
                al = jnp.where((rowe - EDGE < valid) & (s > 0), al, 0.0)
                ah = gelu(x2land[1, w].astype(F32) * scale + offset)
                ah = jnp.where(rowe + Lp < valid, ah, 0.0)
                ext[w, 0:EDGE] = al
                ext[w, EDGE : EDGE + Lp] = a
                ext[w, EDGE + Lp :] = ah
                top, end = w * Lp, (w + 1) * Lp
                Y3[pl.ds(base + top, Lp), 0:C] = ext[w, EDGE - DIL : EDGE - DIL + Lp].astype(BF16)
                Y3[pl.ds(base + top, Lp), C : 2 * C] = a.astype(BF16)
                Y3[pl.ds(base + top, Lp), 2 * C : 3 * C] = ext[w, EDGE + DIL : EDGE + DIL + Lp].astype(BF16)
            y = mm_nt(Y3[pl.ds(base + first * Lp, wb // nh * Lp)], wf[...])
            for w in span:
                at = t * wb + w
                valid = lens[i * plan.nw + at] - s * Lp
                v = y[(w - first) * Lp : (w - first + 1) * Lp]
                c2[at] = v
                cedge[0, at] = v[:EDGE].astype(BF16)
                cedge[1, at] = v[Lp - EDGE :].astype(BF16)
                v = jnp.where(rowh < valid, v, 0.0)
                sums0 = sums0 + fold(v)
                sums1 = sums1 + fold(v * v)
        cacc[0:1, 0:H] += unfold(sums0)
        cacc[0:1, H:] += unfold(sums1)

    @pl.when(first_step())
    def _():
        meet(peers.others)

    @pl.when(t < p0)
    def _():
        c_halo.start(t * wb, wb)

    @pl.when(t == p0 - 1)
    def _():
        c_link[0][...] = cacc[...]
        peers.start(c_link)

    here_p = (t >= p0) & (t < p0 + steps)

    @pl.when(here_p)
    def _():
        u = t - p0
        rowc = rows_of((Lp, C))
        block = pl.ds(pl.multiple_of(u * M, 128), M)
        bias = jnp.zeros((8, C), F32)
        parts = []
        for w in range(wb):
            valid = lens[i * plan.nw + u * wb + w] - s * Lp
            d = jnp.where(rowc < valid, cot[w].astype(F32), 0.0)
            bias = bias + fold(d)
            parts.append(d.astype(BF16))
        d = jnp.concatenate(parts, axis=0)
        dos[block] = d
        das[...] = mm_nt(d, pw[...])
        dacc[1:2] += unfold(bias)

    @pl.when(t == p0)
    def _():
        got = peers.finish(c_link)
        state[ST3 : ST3 + 1, 0:H] = got[:, 0:H]
        state[ST3 + 1 : ST3 + 2, 0:H] = got[:, H:]

    @pl.when(here_p)
    def _():
        u = t - p0
        block = pl.ds(pl.multiple_of(u * M, 128), M)
        rowh = rows_of((Lp, H))
        mean, rho = norm_of(state[ST3 : ST3 + 2, 0:H], total_of(lens))
        scale = state[GAIN3 : GAIN3 + 1, 0:H] * rho
        offset = state[SHIFT3 : SHIFT3 + 1, 0:H] - mean * scale
        s0, s1 = jnp.zeros((8, H), F32), jnp.zeros((8, H), F32)
        parts = []
        for w in range(wb):
            at = u * wb + w
            valid = lens[i * plan.nw + at] - s * Lp
            top, end = w * Lp, (w + 1) * Lp
            v = c2[at]
            zv = v * scale + offset
            act, slope = gelu_both(zv)
            parts.append(jnp.where(rowh < valid, act, 0.0).astype(BF16))
            dzw = das[top:end] * slope
            dz3[at] = dzw
            dedge[0, at] = dzw[:EDGE].astype(BF16)
            dedge[1, at] = dzw[Lp - EDGE :].astype(BF16)
            s0 = s0 + fold(dzw)
            s1 = s1 + fold(dzw * zv)
        a3 = jnp.concatenate(parts, axis=0)
        a3s[block] = a3
        a3T[:, block] = a3.T
        dacc[0:1, 0:H] += unfold(s0)
        dacc[0:1, H : 2 * H] += unfold(s1)
        d_halo.start(u * wb, wb)

    @pl.when(t == p0)
    def _():
        half_copy.wait()
        send_result(0)

    @pl.when(t == p0 + steps - 1)
    def _():
        d_link[0][...] = dacc[...]
        peers.start(d_link)

    @pl.when(t == r0)
    def _():
        for block in range(1, steps):
            send_result(block)
        rows = pl.ds(pl.multiple_of(h * plan.Hh, 16), plan.Hh)
        pgrad[...] = mm(a3T[rows], dos[...]).astype(BF16)

    @pl.when(t == b0)
    def _():
        got = peers.finish(d_link)
        shift = state[SHIFT3 : SHIFT3 + 1, 0:H]
        gain = state[GAIN3 : GAIN3 + 1, 0:H]
        state[SU3 : SU3 + 1, 0:H] = got[0:1, 0:H]
        state[SU3 + 1 : SU3 + 2, 0:H] = (got[0:1, H : 2 * H] - shift * got[0:1, 0:H]) / gain
        state[BSUM : BSUM + 1] = got[1:2]
        c_halo.finish()
        d_halo.finish()

    @pl.when((t >= b0) & (t < g0))
    def _():
        u = t - b0
        total = total_of(lens)
        mean3, rho3 = norm_of(state[ST3 : ST3 + 2, 0:H], total)
        gr3 = state[GAIN3 : GAIN3 + 1, 0:H] * rho3
        sg3 = state[SU3 : SU3 + 1, 0:H] / total
        gg3 = state[SU3 + 1 : SU3 + 2, 0:H] / total
        mean2, rho2 = norm_of(state[ST2 : ST2 + 2], total)
        scale2 = state[GAIN2 : GAIN2 + 1] * rho2
        offset2 = state[SHIFT2 : SHIFT2 + 1] - mean2 * scale2
        rowh = rows_of((Lp, H))
        rowe = rows_of((EDGE, H))
        rowc = rows_of((Lp, C))

        by_v = -gr3 * rho3 * gg3
        by_1 = gr3 * (mean3 * rho3 * gg3 - sg3)

        def back(dz, v):
            return gr3 * dz + by_v * v + by_1

        for w in range(wb):
            valid = lens[i * nw + u * wb + w] - s * Lp
            d = jnp.where(rowh < valid, back(dz3[u * wb + w], c2[u * wb + w]), 0.0)
            dl = back(dland[0, u * wb + w].astype(F32), cland[0, u * wb + w].astype(F32))
            dl = jnp.where((rowe - EDGE < valid) & (s > 0), dl, 0.0)
            dh = back(dland[1, u * wb + w].astype(F32), cland[1, u * wb + w].astype(F32))
            dh = jnp.where(rowe + Lp < valid, dh, 0.0)
            ext[w, 0:EDGE, 0:H] = dl
            ext[w, EDGE : EDGE + Lp, 0:H] = d
            ext[w, EDGE + Lp :, 0:H] = dh
            top, end = w * Lp, (w + 1) * Lp
            Z3[top:end, 0:H] = ext[w, EDGE + DIL : EDGE + DIL + Lp, 0:H].astype(BF16)
            Z3[top:end, H : 2 * H] = d.astype(BF16)
            Z3[top:end, 2 * H : 3 * H] = ext[w, EDGE - DIL : EDGE - DIL + Lp, 0:H].astype(BF16)

        y = mm(Z3[...], wt[...])

        M = wb * Lp
        dcT[:, pl.ds(pl.multiple_of(u * M, 128), M)] = Z3[:, H : 2 * H].T
        s0, s1 = jnp.zeros((8, C), F32), jnp.zeros((8, C), F32)
        for w in range(wb):
            at = u * wb + w
            valid = lens[i * nw + at] - s * Lp
            v = x2[w]
            zv = v * scale2 + offset2
            dzw = y[w * Lp : (w + 1) * Lp] * gelu_slope(zv)
            dzw = jnp.where(rowc < valid, dzw, 0.0)
            dz2[w] = dzw
            bedge[0, pl.ds(at, 1)] = dzw[0:1]
            bedge[1, pl.ds(at, 1)] = dzw[Lp - 1 : Lp]
            s0 = s0 + fold(dzw)
            s1 = s1 + fold(dzw * zv)
        bacc[0:1] += unfold(s0)
        bacc[1:2] += unfold(s1)

    @pl.when(t == g0 - 1)
    def _():
        b_link[0][...] = bacc[...]
        peers.start(b_link)
        b_halo.start(0, nw)

    @pl.when(last_step())
    def _():
        rows = pl.ds(pl.multiple_of(h * plan.Hh, 16), plan.Hh)
        for n in range(plan.T2):
            cols = slice(n * C, (n + 1) * C)
            grads[:, cols] = mm(dcT[rows], Y3[:, cols]).astype(BF16)

    @pl.when(last_step())
    def _():
        got = peers.finish(b_link)
        shift, gain = state[SHIFT2 : SHIFT2 + 1], state[GAIN2 : GAIN2 + 1]
        state[SU2 : SU2 + 1] = got[0:1]
        state[SU2 + 1 : SU2 + 2] = (got[1:2] - shift * got[0:1]) / gain
        b_halo.finish()
        for off in range(1, g):
            bulk(off, pl.ds(0, nw)).wait()


def block_phases(plan):
    n = plan.steps
    return n, 2 * n, 2 * n + 1, 3 * n + 1, 3 * n + 2


class Reduction:
    def __init__(self, plan, batches, out, give, mine, got, spread, half, mate, sems):
        self.plan, self.batches, self.out = plan, batches, out
        self.give, self.mine, self.got, self.spread = give, mine, got, spread
        self.half, self.mate = half, mate
        self.sems = sems
        self.s, self.z, self.i, self.h = plan.place()
        self.c = lax.rem(self.s, 2)
        self.m = lax.div(self.s, 2)
        self.chips = plan.chips

    @staticmethod
    def scratch(plan, batches):
        taps, wide = plan.T1 + 2, plan.C // 2
        full = (taps, plan.chips, plan.g, plan.rb, wide)
        part = (taps, plan.g, plan.rb, wide)
        return [
            pltpu.VMEM((taps, 2, plan.chips, plan.rb, wide), BF16),
            *[pltpu.VMEM(full, BF16)] * 4,
            *[pltpu.VMEM(part, BF16)] * 2,
            pltpu.SemaphoreType.DMA((2, len(batches), 5)),
        ]

    def copy(self, b, phase, src, dst, device):
        return remote(src, dst, self.sems.at[0, b, phase], self.sems.at[1, b, phase], device)

    def finish(self, b, phase, ref, device):
        done = self.copy(b, phase, ref, ref, device)
        done.wait_recv()
        done.wait_send()

    def taps(self, b):
        return pl.ds(*self.batches[b])

    def pair(self):
        return (2 * self.m + (1 - self.c), self.z)

    def far(self, off):
        return (2 * wrap(self.m + off, self.chips) + self.c, self.z)

    def member(self, off):
        return (self.s, self.h * self.plan.g + wrap(self.i + off, self.plan.g))

    def put(self, k, rows):
        wide = self.plan.C // 2
        for j in range(self.plan.g):
            for m in range(self.chips):
                v = rows(j, m)
                left, right = v[:, :wide], v[:, wide:]
                self.mine[k, m, j] = jnp.where(self.c == 0, left, right).astype(BF16)
                self.give[k, m, j] = jnp.where(self.c == 0, right, left).astype(BF16)

    def step0(self, b):
        taps = self.taps(b)
        self.copy(b, 0, self.give.at[taps], self.got.at[taps], self.pair()).start()

    def step1(self, b):
        taps = self.taps(b)
        self.finish(b, 0, self.got.at[taps], self.pair())
        first, count = self.batches[b]
        for k in range(first, first + count):
            v = self.mine[k].astype(F32) + self.got[k].astype(F32)
            self.mine[k] = v.astype(BF16)
        for off in range(1, self.chips):
            src = self.mine.at[taps, wrap(self.m + off, self.chips)]
            self.copy(b, 1, src, self.spread.at[taps, self.m], self.far(off)).start()

    def step2(self, b):
        taps = self.taps(b)
        self.finish(b, 1, self.spread.at[taps, pl.ds(0, self.chips - 1)], self.far(1))
        first, count = self.batches[b]
        for k in range(first, first + count):
            self.spread[k, self.m] = self.mine[k, self.m]
            v = self.spread[k, 0].astype(F32)
            for n in range(1, self.chips):
                v = v + self.spread[k, n].astype(F32)
            self.half[k] = v.astype(BF16)
        for off in range(1, self.plan.g):
            src = self.half.at[taps, wrap(self.i + off, self.plan.g)]
            self.copy(b, 2, src, self.mate.at[taps, off], self.member(off)).start()

    def step3(self, b):
        taps = self.taps(b)
        self.finish(b, 2, self.mate.at[taps, pl.ds(1, self.plan.g - 1)], self.member(1))
        first, count = self.batches[b]
        for k in range(first, first + count):
            v = self.half[k, self.i].astype(F32)
            for off in range(1, self.plan.g):
                v = v + self.mate[k, off].astype(F32)
            self.out[k, self.c, self.m] = v.astype(BF16)
        mine = self.out.at[taps, self.c, self.m]
        for off in range(1, self.chips):
            self.copy(b, 3, mine, mine, self.far(off)).start()

    def step4(self, b):
        taps = self.taps(b)
        self.finish(b, 3, self.out.at[taps, self.c, pl.ds(0, self.chips - 1)], self.far(1))
        mine = self.out.at[taps, self.c]
        self.copy(b, 4, mine, mine, self.pair()).start()

    def step5(self, b):
        self.finish(b, 4, self.out.at[self.taps(b), self.c], self.pair())


def tail_turns(plan):
    nD, T1 = plan.steps, plan.T1
    turns = [("x", 0)] + [("d", n) for n in range(1, nD)]
    xs, ws = [("x", n) for n in range(1, nD)], [("w", n) for n in range(T1)]
    for count in (2, 1, T1):
        turns += ws[:count] + xs[:1]
        xs, ws = xs[1:], ws[count:]
    return turns + xs


def tail_batches(plan):
    return [(plan.T1, 2), (0, 2)] + [(k, 1) for k in range(2, plan.T1)]


def tail_kernel(plan, lens, dz2, dzland, x2, x2land, cot, beyond, x, X5_hbm, taps_hbm, grads, pgrad,
                old, half_state,
                gz, gz_got, sums, summed,
                ext, D3, D0T, wcat, pick, eye, cols, y, part, split, acc, X5, X5_sems,
                taps, bulk_sems, *rest):
    t = pl.program_id(0)
    s, z, i, h = plan.place()
    L, Lp, C, wb, g, nw = plan.L, plan.Lp, plan.C, plan.wb, plan.g, plan.nw
    Ch, cs, T1 = plan.Ch, plan.cs, plan.T1
    M = wb * Lp
    nD = plan.steps
    turns = tail_turns(plan)
    last = len(turns) - 1
    peers = group_peers(plan)
    red = Reduction(plan, tail_batches(plan), *rest[:8])
    link = rest[8:]

    def member(off):
        return (s, h * g + wrap(i + off, g))

    def send(first, count):
        rows = pl.ds(first, count)
        for off in range(1, g):
            remote(
                part.at[off - 1, rows],
                gz_got.at[off, rows],
                bulk_sems.at[0, off],
                bulk_sems.at[1, off],
                member(off),
            ).start()

    def X5_copy(k):
        return pltpu.make_async_copy(X5_hbm.at[k], X5.at[k % 2], X5_sems.at[k % 2])

    def when(at):
        return pl.when(t == min(at, last))

    def turn(kind, k):
        return turns.index((kind, k)) if (kind, k) in turns else last

    def turn_of(kind):
        index = jnp.int32(0)
        here = False
        for n, (what, k) in enumerate(turns):
            if what == kind:
                index = jnp.where(t == n, k, index)
                here = (t == n) | here
        return here, index

    taps_copy = pltpu.make_async_copy(
        taps_hbm.at[:, pl.ds(pl.multiple_of(h * Ch, 128), Ch)], taps, X5_sems.at[2]
    )

    @when(0)
    def _():
        taps_copy.start()
        greet(peers.others)
        acc[...] = jnp.zeros_like(acc)
        pick[...] = pick_matrix(L)
        eye[...] = eye_matrix(Ch, Ch, 0)
        mean, rho = norm_of(half_state[ST1 : ST1 + 2], 2.0 * total_of(lens))
        scale = half_state[GAIN1 : GAIN1 + 1] * rho
        offset = half_state[SHIFT1 : SHIFT1 + 1] - mean * scale
        for k, row in enumerate((scale, offset)):
            cols[k] = column(row, L)

    @pl.when(t < nD)
    def _():
        total = total_of(lens)
        mean, rho = norm_of(old[ST2 : ST2 + 2], total)
        gr = old[GAIN2 : GAIN2 + 1] * rho
        sg = old[SU2 : SU2 + 1] / total
        gg = old[SU2 + 1 : SU2 + 2] / total
        rowc = rows_of((Lp, C))
        row1 = rows_of((1, C))

        by_dz = 0.5 * gr
        by_v = -0.5 * gr * rho * gg
        by_1 = 0.5 * gr * (mean * rho * gg - sg)

        def back(dout, dz, v):
            return 0.5 * dout + by_dz * dz + by_v * v + by_1

        def grad_of(w):
            at = t * wb + w
            valid = lens[i * nw + at] - s * Lp
            d = back(cot[w].astype(F32), dz2[w], x2[w])
            d = jnp.where(rowc < valid, d, 0.0)
            one = pl.ds(at, 1)
            dl = back(beyond[0, 2, one, :], dzland[0, one, :], x2land[0, w, EDGE - 1 : EDGE].astype(F32))
            dl = jnp.where((row1 - 1 < valid) & (s > 0), dl, 0.0)
            dh = back(beyond[1, 2, one, :], dzland[1, one, :], x2land[1, w, 0:1].astype(F32))
            dh = jnp.where(row1 + Lp < valid, dh, 0.0)
            ext[w, 7:8] = dl
            ext[w, 8 : 8 + Lp] = d
            ext[w, 8 + Lp : 9 + Lp] = dh
            top, end = w * Lp, (w + 1) * Lp
            D3[t, top:end, 0:C] = ext[w, 9 : 9 + Lp].astype(BF16)
            D3[t, top:end, C : 2 * C] = d.astype(BF16)
            D3[t, top:end, 2 * C : 3 * C] = ext[w, 7 : 7 + Lp].astype(BF16)

        for w in range(wb):
            grad_of(w)
        half = D3[t, :, pl.ds(pl.multiple_of(C + h * Ch, 128), Ch)]
        D0T[:, pl.ds(pl.multiple_of(t * M, 128), M)] = half.T

    @when(0)
    def _():
        taps_copy.wait()
        for first in range(0, Ch, 64):
            rows = slice(first, min(first + 64, Ch))
            for r, parts in enumerate((((0,), (1, 2), (3, 4)), ((0, 1), (2, 3), (4,)))):
                for k, which in enumerate(parts):
                    v = taps[which[0], rows]
                    if len(which) > 1:
                        v = (v.astype(F32) + taps[which[1], rows].astype(F32)).astype(BF16)
                    at = r * Ch
                    wcat[at + rows.start : at + rows.stop, k * C : (k + 1) * C] = v
        meet(peers.others)

    here_x, bx = turn_of("x")

    def gradient(hf, nh):
        lanes = lanes_of((Ch, L))

        def through(w):
            valid = 2 * lens[i * nw + bx * wb + w] - s * L
            top, end = w * Lp, (w + 1) * Lp
            v = mm_nt(eye[...], x[w])
            da = jnp.concatenate([y[0:Ch, top:end], y[Ch:, top:end]], axis=1)
            da = mm(da.astype(BF16), pick[...])
            zv = v * cols[0] + cols[1]
            dzw = da * gelu_slope(zv)
            dzw = jnp.where(lanes < valid, dzw, 0.0)
            acc[0] += fold_lanes(dzw)
            acc[1] += fold_lanes(dzw * zv)
            split[w % 2] = dzw.astype(BF16)
            for off in range(g):
                rows = pl.ds(pl.multiple_of(lax.rem(i + off, g) * cs, 16), cs)
                if off == 0:
                    gz[w] = split[w % 2, rows]
                else:
                    part[off - 1, bx * wb + w] = split[w % 2, rows]

        n = wb // nh
        rows = slice(hf * n * Lp, (hf + 1) * n * Lp)
        y[:, rows] = mm_nt(wcat[...], D3[bx, rows])
        for w in range(hf * n, (hf + 1) * n):
            through(w)

    nh = 2 if wb % 2 == 0 and wb * Lp // 2 % 128 == 0 else 1

    @pl.when(here_x)
    def _():
        gradient(0, nh)
        send(bx * wb, wb // nh)

    first = min(1, last)
    table = (
        (first, 1, red.step1, 0),
        (max(turn("w", 1), first + 1), 1, red.step2, 0),
        (turn("w", 1), 1, red.step0, 1),
        (turn("x", 1), 0, red.step1, 1),
        (turn("w", 2), 1, red.step0, 2),
        (turn("x", 2), 0, red.step1, 2),
        (turn("x", 2), 1, red.step3, 0),
        (turn("x", 2), 1, red.step2, 1),
        (turn("w", 3), 1, red.step0, 3),
        (turn("w", 4), 1, red.step0, 4),
        (turn("w", 4), 1, red.step1, 3),
        (turn("w", 4), 1, red.step2, 2),
        (turn("x", 3), 0, red.step1, 4),
        (turn("x", 3), 0, red.step4, 0),
        (turn("x", 3), 0, red.step3, 1),
        (last, 1, red.step2, 3),
        (last, 1, red.step3, 2),
        (last, 1, red.step2, 4),
    )

    def between(at, end):
        return end == 0 and nh == 2 and turns[at][0] == "x"

    def go_on(entries):
        for at, _, step, batch in entries:

            @when(at)
            def _():
                step(batch)

    go_on([e for e in table if between(*e[:2])])

    if nh == 2:

        @pl.when(here_x)
        def _():
            gradient(1, nh)

    @when(0)
    def _():
        hs = plan.H // plan.nz
        rb = plan.rb
        for u in range(2):

            def rows(j, m, u=u):
                side, r = m * rb // hs, m * rb % hs
                n = 2 * side + u
                rows = slice(j * hs + r, j * hs + r + rb)
                v = grads[rows, n * C : (n + 1) * C] if n < plan.T2 else pgrad[rows]
                return v.astype(F32)

            red.put(T1 + u, rows)
        red.step0(0)

    @when(1)
    def _():
        X5_copy(0).start()
        X5_copy(1).start()

    here_w, k = turn_of("w")

    @pl.when(here_w)
    def _():
        X5_copy(k).wait()
        y[0:Ch, 0:C] = mm(D0T[...], X5[lax.rem(k, 2)])

        @pl.when(k < T1 - 2)
        def _():
            X5_copy(k + 2).start()

        rb = plan.rb
        red.put(k, lambda j, m: y[j * cs + m * rb : j * cs + (m + 1) * rb, 0:C])

    @when(turn("x", nD - 1))
    def _():
        packet = link[0]
        packet[...] = jnp.zeros_like(packet)
        packet[0:1, 0:Ch] = jnp.sum(acc[0].T, axis=0, keepdims=True)
        packet[1:2, 0:Ch] = jnp.sum(acc[1].T, axis=0, keepdims=True)
        peers.start(link)

    go_on([e for e in table if not between(*e[:2])])

    @pl.when(here_x & (bx < nD - 1))
    def _():
        if nh == 2:
            send(bx * wb + wb // nh, wb // nh)

    @when(last)
    def _():
        if nh == 2:
            send(nw - wb // 2, wb // 2)

    @when(last)
    def _():
        red.step3(3)
        red.step4(1)
        red.step4(2)
        red.step3(4)
        red.step4(3)
        got = peers.finish(link)[:, 0:Ch]
        shift, gain = half_state[SHIFT1 : SHIFT1 + 1], half_state[GAIN1 : GAIN1 + 1]
        sums[0:1] = got[0:1]
        sums[1:2] = (got[1:2] - shift * got[0:1]) / gain
        red.step4(4)
        for b in range(5):
            red.step5(b)
        own = pltpu.make_async_copy(red.out, summed, X5_sems.at[0])
        own.start()
        for off in range(1, g):
            done = remote(
                part.at[off - 1],
                gz_got.at[off],
                bulk_sems.at[0, off],
                bulk_sems.at[1, off],
                member(off),
            )
            done.wait_recv()
            done.wait_send()
        own.wait()


def input_grad_kernel(plan, wg, lens, x, gz, gz_got, sums, res, res_got, summed,
                      state, half_state,
                      out, out_result, conv_grad, dil_grad, point_grad,
                      g1, b1, g2, b2, g3, b3, pb, eye, cols, xt):
    t = pl.program_id(0)
    s, z, i, h = plan.place()
    L, Ch, cs = plan.L, plan.Ch, plan.cs
    turn = plan.nw // wg
    mine = pl.ds(pl.multiple_of(i * cs, 16), cs)

    @pl.when(first_step())
    def _():
        n = 2.0 * total_of(lens)
        mean, rho = norm_of(half_state[ST1 : ST1 + 2], n)
        gr = half_state[GAIN1 : GAIN1 + 1] * rho
        gg = sums[1:2] / n * rho
        for k, row in enumerate((gr, -gr * gg, gr * (mean * gg - sums[0:1] / n))):
            xt[...] = column(row, L)
            cols[k] = xt[mine]
        eye[...] = eye_matrix(cs, Ch, i * cs)

        def mine_of(src, at, which, count, *dsts):
            n = dsts[0].shape[1]
            for k in range(count):

                @pl.when(which == k)
                def _():
                    for dst, r in zip(dsts, at):
                        dst[...] = src[r : r + 1, k * n : (k + 1) * n]

        mine_of(sums, (1, 0), i, plan.g, g1, b1)
        mine_of(state, (SU2 + 1, SU2), z, plan.nz, g2, b2)
        mine_of(state, (SU3 + 1, SU3), z, plan.nz, g3, b3)
        mine_of(state, (BSUM,), z, plan.nz, pb)

    own = lax.div(t, turn) == i
    for w in range(wg):
        out_result[w] = jnp.where(own, res[0, w], res_got[0, w])

    C, T1, hs, rb, wide = plan.C, plan.T1, plan.H // plan.nz, plan.rb, plan.C // 2
    count = plan.NW // wg
    turns = min(count, plan.chips)
    per, every = plan.chips // turns, count // turns

    def spread(chunk):
        for n in range(per):
            m = chunk * per + n
            side, r = m * rb // hs, m * rb % hs
            for c in range(2):
                at = slice(c * wide, (c + 1) * wide)
                for k in range(T1):
                    conv_grad[k, n * rb : (n + 1) * rb, at] = summed[k, c, n].astype(F32)
                for u in range(2):
                    v = summed[T1 + u, c, n].astype(F32)
                    if 2 * side + u < plan.T2:
                        dil_grad[2 * side + u, r : r + rb, at] = v
                    else:
                        point_grad[r : r + rb, at] = v

    for chunk in range(turns):
        pl.when(t == chunk * every)(partial(spread, chunk))

    lanes = lanes_of((cs, L))
    for w in range(wg):
        valid = 2 * lens[t * wg + w] - s * L
        v = mm_nt(eye[...], x[w])
        dz = jnp.where(own, gz[w], gz_got[0, w]).astype(F32)
        r = cols[0] * dz + v * cols[1] + cols[2]
        out[w] = jnp.where(lanes < valid, r, 0.0).astype(BF16)


def call(kernel, plan, name, steps, ins, outs, scratch, flops, nbytes, cid=None):
    extra = {} if cid is None else dict(collective_id=cid, has_side_effects=True)
    return pl.pallas_call(
        partial(kernel, plan),
        grid=(steps,),
        in_specs=[SMEM] + [spec for spec, _ in ins],
        out_specs=[spec for spec, _, _ in outs],
        out_shape=[jax.ShapeDtypeStruct(shape, dtype) for _, shape, dtype in outs],
        scratch_shapes=scratch,
        compiler_params=pltpu.CompilerParams(vmem_limit_bytes=VMEM_LIMIT, **extra),
        cost_estimate=pl.CostEstimate(
            flops=int(flops), bytes_accessed=int(nbytes), transcendentals=0
        ),
        name=name,
    )


def per_device(
    inputs,
    lengths,
    input_gain,
    input_shift,
    conv_weight,
    branch_gain,
    branch_shift,
    dilated_tap_weight,
    mixer_gain,
    mixer_shift,
    point_weight,
    point_bias,
    cotangent,
):
    NW, L, C = inputs.shape
    Lp = L // 2
    nz = lax.axis_size("ch")
    R = 2
    plan = Plan(
        ns=lax.axis_size("seq"),
        nz=nz,
        R=R,
        NW=NW,
        L=L,
        C=C,
        H=mixer_gain.shape[0] * nz,
        T1=conv_weight.shape[0],
        T2=dilated_tap_weight.shape[0],
        wb=min(NW * R // nz, max(1, 512 // Lp)),
    )
    g, nw, cs, Ch, H, Hh, wb = plan.g, plan.nw, plan.cs, plan.Ch, plan.H, plan.Hh, plan.wb
    T1, T2, steps = plan.T1, plan.T2, plan.steps
    M = wb * Lp
    hs = H // nz
    lens = lengths.astype(jnp.int32)

    def row(a):
        return a.reshape(1, a.shape[0])

    def grp():
        return lax.rem(lax.axis_index("ch"), g)

    def half():
        return lax.div(lax.axis_index("ch"), g)

    def core():
        return lax.rem(lax.axis_index("seq"), 2)

    def chip4():
        return lax.div(lax.axis_index("seq"), plan.ns // 4)

    def whole(*shape):
        return pl.BlockSpec(shape, lambda t: (0,) * len(shape), pipeline_mode=pl.Buffered(1))

    def const(*shape):
        return pl.BlockSpec(shape, lambda t: (0,) * len(shape))

    def win(*shape):
        return pl.BlockSpec(shape, lambda t: (t,) + (0,) * (len(shape) - 1))

    def arg_win(n, width):
        return pl.BlockSpec((wb, n, width), lambda t: (grp() * steps + t, 0, 0))

    def ins(*pairs):
        return [p for p in pairs]

    share = NW // nz
    nm = max(1, share // wb)

    def edge_spec(n):
        return pl.BlockSpec(
            (nw, 16, C), lambda t: (grp(), n, 0), pipeline_mode=pl.Buffered(1)
        )

    def head_block(t):
        own = lax.div(lax.axis_index("ch") * share, wb) + t
        return jnp.where(t < nm, own, grp() * steps + t - nm), 0, 0

    def after(*shape):
        return pl.BlockSpec(
            shape, lambda t: (jnp.maximum(t - nm, 0),) + (0,) * (len(shape) - 1)
        )

    pairs = ins(
        (pl.BlockSpec((wb, L, C), head_block), inputs),
        (edge_spec(0), inputs),
        (edge_spec(L // 16 - 1), inputs),
        (edge_spec(0), cotangent),
        (edge_spec(Lp // 16 - 1), cotangent),
        (whole(1, cs), row(branch_gain)),
        (whole(1, cs), row(branch_shift)),
        (whole(1, cs), row(point_bias)),
        (whole(1, H // nz), row(mixer_gain)),
        (whole(1, H // nz), row(mixer_shift)),
        (ANY, conv_weight.reshape(T1 * C, C)),
        (whole(C), input_gain),
        (whole(C), input_shift),
        (
            pl.BlockSpec(
                (1, hs, C // 2),
                lambda t: (jnp.minimum(chip4(), T2 - 1), 0, core()),
                pipeline_mode=pl.Buffered(1),
            ),
            jnp.swapaxes(dilated_tap_weight, 1, 2),
        ),
        (
            pl.BlockSpec(
                (hs, C // 2), lambda t: (0, core()), pipeline_mode=pl.Buffered(1)
            ),
            point_weight,
        ),
    )
    plane, line, group = plane_peers(plan), line_peers(plan), group_peers(plan)
    state_shape = (STATE, C)
    edges2, edges3 = (2, nw, EDGE, C), (2, nw, EDGE, H)
    X5, x2, land2, state, beyond, full = call(
        lambda plan, *refs: head_kernel(plan, nm, *refs),
        plan,
        "head",
        nm + steps,
        pairs,
        [
            (
                pl.BlockSpec((T1, M, C), lambda t: (0, jnp.maximum(t - nm, 0), 0)),
                (T1, nw * Lp, C),
                BF16,
            ),
            (after(wb, Lp, C), (nw, Lp, C), F32),
            (ANY, edges2, BF16),
            (const(*state_shape), state_shape, F32),
            (const(2, 3, nw, C), (2, 3, nw, C), F32),
            (ANY, (2, T2 + 1, nz, hs, C // 2), BF16),
        ],
        [
            pltpu.VMEM((2, 8, C), F32),
            pltpu.VMEM((2, 3, nw, C), F32),
            pltpu.VMEM((2, 3, nw, C), F32),
            pltpu.VMEM((L, L), BF16),
            pltpu.VMEM(edges2, BF16),
            pltpu.VMEM((2, C), F32),
            pltpu.VMEM((T1 * C, C), BF16),
            pltpu.SemaphoreType.DMA,
            pltpu.VMEM((hs, C // 2), BF16),
            pltpu.SemaphoreType.DMA((2, 4)),
            HALO_SEMS,
            HALO_SEMS,
        ]
        + plane.scratch(2, C)
        + line.scratch(3, C)
        + group.scratch(2, C),
        2 * nw * Lp * T1 * C * C,
        nw * Lp * C * 20,
        cid=1,
    )(lens, *[a for _, a in pairs])

    taps_spec = whole(2, T2, nz, hs, C // 2)
    pw_spec = pl.BlockSpec(
        (2, 1, nz, hs, C // 2), lambda t: (0, T2, 0, 0, 0), pipeline_mode=pl.Buffered(1)
    )

    def early(*shape):
        return pl.BlockSpec(
            shape, lambda t: (jnp.minimum(t, steps - 1),) + (0,) * (len(shape) - 1)
        )

    def early_land(width):
        return pl.BlockSpec(
            (2, wb, EDGE, width), lambda t: (0, jnp.minimum(t, steps - 1), 0, 0)
        )

    def half_of(n):
        return pl.BlockSpec((n, Ch), lambda t: (0, half()), pipeline_mode=pl.Buffered(1))

    cot_spec = pl.BlockSpec(
        (wb, Lp, C), lambda t: (grp() * steps + jnp.minimum(t, steps - 1), 0, 0)
    )

    p0, r0, b0, g0, block_steps = block_phases(plan)

    def at_phase(first):
        return lambda t: jnp.clip(t - first, 0, steps - 1)

    in_p, in_b = at_phase(p0), at_phase(b0)
    pairs = ins(
        (
            pl.BlockSpec(
                (wb, Lp, C),
                lambda t: (jnp.where(t < p0 + steps, jnp.minimum(t, steps - 1), in_b(t)), 0, 0),
            ),
            x2,
        ),
        (ANY, x2),
        (early_land(C), land2),
        (pl.BlockSpec((wb, Lp, C), lambda t: (grp() * steps + in_p(t), 0, 0)), cotangent),
        (taps_spec, full),
        (pw_spec, full),
        (whole(T2, hs, C), jnp.swapaxes(dilated_tap_weight, 1, 2)),
        (whole(hs, C), point_weight),
        (whole(*state_shape), state),
        (half_of(STATE), state),
    )
    dz2, grads, pgrad, res, dland2, state, res_got = call(
        block_kernel,
        plan,
        "block",
        block_steps,
        pairs,
        [
            (pl.BlockSpec((wb, Lp, C), lambda t: (in_b(t), 0, 0)), (nw, Lp, C), F32),
            (const(Hh, T2 * C), (Hh, T2 * C), BF16),
            (const(Hh, C), (Hh, C), BF16),
            (const(g, nw, cs, Lp), (g, nw, cs, Lp), BF16),
            (ANY, (2, nw, C), F32),
            (const(*state_shape), state_shape, F32),
            (ANY, (g, nw, cs, Lp), BF16),
        ],
        [
            pltpu.VMEM((wb, Lp + 2 * EDGE, C), F32),
            pltpu.VMEM((H, T2 * C), BF16),
            pltpu.VMEM((T2 * H, C), BF16),
            pltpu.VMEM((H, C), BF16),
            pltpu.VMEM((nw * Lp, T2 * C), BF16),
            pltpu.VMEM((nw, Lp, H), F32),
            pltpu.VMEM((nw, Lp, H), F32),
            pltpu.VMEM((M, H), F32),
            pltpu.VMEM((nw * Lp, H), BF16),
            pltpu.VMEM((H, nw * Lp), BF16),
            pltpu.VMEM((nw * Lp, C), BF16),
            pltpu.VMEM((M, T2 * H), BF16),
            pltpu.VMEM((H, nw * Lp), BF16),
            pltpu.VMEM(edges3, BF16),
            pltpu.VMEM(edges3, BF16),
            pltpu.VMEM((1, 2 * H), F32),
            pltpu.VMEM(edges3, BF16),
            pltpu.VMEM(edges3, BF16),
            pltpu.VMEM((2, C), F32),
            pltpu.VMEM((2, nw, C), F32),
            pltpu.VMEM((2, C), F32),
            pltpu.SemaphoreType.DMA((3, 2, 2)),
            pltpu.SemaphoreType.DMA((2, g)),
            pltpu.VMEM((nw, Lp, Ch), F32),
            pltpu.SemaphoreType.DMA,
        ]
        + group.scratch(1, 2 * H)
        + group.scratch(2, C)
        + group.scratch(2, C),
        nw * Lp * C * H * (6 * T2 + 6),
        nw * Lp * C * 30,
        cid=3,
    )(lens, *[a for _, a in pairs])

    chips, rb = plan.chips, plan.rb
    turns_t = tail_turns(plan)

    def x_block(t):
        block = jnp.int32(0)
        for n, (what, k) in enumerate(turns_t):
            if what == "x":
                block = jnp.where(t >= n, k, block)
        return block

    sshape = (T1 + 2, 2, chips, rb, C // 2)
    pairs = ins(
        (early(wb, Lp, C), dz2),
        (whole(2, nw, C), dland2),
        (early(wb, Lp, C), x2),
        (early_land(C), land2),
        (cot_spec, cotangent),
        (whole(2, 3, nw, C), beyond),
        (
            pl.BlockSpec(
                (wb, L, Ch), lambda t: (grp() * steps + x_block(t), 0, half())
            ),
            inputs,
        ),
        (ANY, X5),
        (ANY, conv_weight),
        (whole(Hh, T2 * C), grads),
        (whole(Hh, C), pgrad),
        (whole(*state_shape), state),
        (half_of(STATE), state),
    )
    gz, gz_got, sums1, summed = call(
        tail_kernel,
        plan,
        "tail",
        len(turns_t),
        pairs,
        [
            (pl.BlockSpec((wb, cs, L), lambda t: (x_block(t), 0, 0)), (nw, cs, L), BF16),
            (ANY, (g, nw, cs, L), BF16),
            (const(2, Ch), (2, Ch), F32),
            (ANY, sshape, BF16),
        ],
        [
            pltpu.VMEM((wb, Lp + 16, C), F32),
            pltpu.VMEM((steps, M, 3 * C), BF16),
            pltpu.VMEM((Ch, nw * Lp), BF16),
            pltpu.VMEM((2 * Ch, 3 * C), BF16),
            pltpu.VMEM((L, L), BF16),
            pltpu.VMEM((Ch, Ch), BF16),
            pltpu.VMEM((2, Ch, L), F32),
            pltpu.VMEM((2 * Ch, max(M, C)), F32),
            pltpu.VMEM((g - 1, nw, cs, L), BF16),
            pltpu.VMEM((2, Ch, L), BF16),
            pltpu.VMEM((2, Ch, min(L, 128)), F32),
            pltpu.VMEM((2, nw * Lp, C), BF16),
            pltpu.SemaphoreType.DMA((3,)),
            pltpu.VMEM((T1, Ch, C), BF16),
            pltpu.SemaphoreType.DMA((2, g)),
        ]
        + Reduction.scratch(plan, tail_batches(plan))
        + group.scratch(2, C),
        2 * nw * Lp * (6 + T1) * C * Ch,
        nw * Lp * C * 40,
        cid=6,
    )(lens, *[a for _, a in pairs])

    wg = min(2 * wb, nw)
    count = NW // wg
    turn = nw // wg
    turns = min(count, chips)

    def own_block(t):
        return jnp.where(lax.div(t, turn) == grp(), lax.rem(t, turn), 0)

    def got_slot(t):
        off = lax.rem(grp() - lax.div(t, turn) + g, g)
        return jnp.maximum(off, 1), jnp.where(off > 0, lax.rem(t, turn), 0)

    pairs = ins(
        (pl.BlockSpec((wg, L, Ch), lambda t: (t, 0, half())), inputs),
        (pl.BlockSpec((wg, cs, L), lambda t: (own_block(t), 0, 0)), gz),
        (pl.BlockSpec((1, wg, cs, L), lambda t: got_slot(t) + (0, 0)), gz_got),
        (whole(2, Ch), sums1),
        (pl.BlockSpec((1, wg, cs, Lp), lambda t: (grp(), own_block(t), 0, 0)), res),
        (pl.BlockSpec((1, wg, cs, Lp), lambda t: got_slot(t) + (0, 0)), res_got),
        (
            pl.BlockSpec(
                (T1 + 2, 2, chips // turns, rb, C // 2),
                lambda t: (0, 0, t * turns // count, 0, 0),
            ),
            summed,
        ),
        (whole(*state_shape), state),
        (half_of(STATE), state),
    )
    outs = call(
        lambda plan, *refs: input_grad_kernel(plan, wg, *refs),
        plan,
        "input_grad",
        count,
        pairs,
        [
            (win(wg, cs, L), (NW, cs, L), BF16),
            (win(wg, cs, Lp), (NW, cs, Lp), BF16),
            (
                pl.BlockSpec((T1, cs // turns, C), lambda t: (0, t * turns // count, 0)),
                (T1, cs, C),
                F32,
            ),
            (const(T2, hs, C), (T2, hs, C), F32),
            (const(hs, C), (hs, C), F32),
        ]
        + [(const(1, n), (1, n), F32) for n in (cs, cs, cs, cs, hs, hs, cs)],
        [
            pltpu.VMEM((cs, Ch), BF16),
            pltpu.VMEM((3, cs, L), F32),
            pltpu.VMEM((Ch, L), F32),
        ],
        2 * NW * L * Ch * cs,
        NW * L * cs * 8,
    )(lens, *[a for _, a in pairs])
    grad, result, conv_grad, dil_grad, point_grad = outs[:5]
    g1, b1, g2, b2, g3, b3, pb = [a[0] for a in outs[5:]]
    return (
        jnp.swapaxes(result, 1, 2),
        jnp.swapaxes(grad, 1, 2),
        jnp.swapaxes(conv_grad, 1, 2),
        g1,
        b1,
        g2,
        b2,
        jnp.swapaxes(dil_grad, 1, 2),
        g3,
        b3,
        point_grad,
        pb,
    )


def solution(mesh):
    in_specs = (
        P(None, "seq", None),
        P(),
        P(),
        P(),
        P(),
        P("ch"),
        P("ch"),
        P(None, None, "ch"),
        P("ch"),
        P("ch"),
        P("ch", None),
        P("ch"),
        P(None, "seq", None),
    )
    out_specs = (
        P(None, "seq", "ch"),
        P(None, "seq", "ch"),
        P(None, None, "ch"),
        P("ch"),
        P("ch"),
        P("ch"),
        P("ch"),
        P(None, None, "ch"),
        P("ch"),
        P("ch"),
        P("ch", None),
        P("ch"),
    )
    return jax.shard_map(
        per_device, mesh=mesh, in_specs=in_specs, out_specs=out_specs, check_vma=False
    )
```

```python
from functools import partial
from typing import NamedTuple

import jax
import jax.numpy as jnp
from jax import lax
from jax.experimental import pallas as pl
from jax.experimental.pallas import tpu as pltpu
from jax.sharding import PartitionSpec as P

DIL = 14
EDGE = 16
EPS = 1e-05
GC0 = 0.7978845608028654
GC1 = 0.044715
F32 = jnp.float32
BF16 = jnp.bfloat16
MESH = pl.DeviceIdType.MESH
VMEM_LIMIT = 58 * 1024 * 1024
ANY = pl.BlockSpec(memory_space=pl.ANY)
SMEM = pl.BlockSpec(memory_space=pltpu.SMEM)


ST1, GAIN2, SHIFT2, BIAS, GAIN3, SHIFT3, GAIN1, SHIFT1, ST2, ST3, SU3, BSUM, SU2 = (
    0, 2, 3, 4, 5, 6, 7, 8, 9, 11, 13, 15, 16
)
STATE = 24


class Plan(NamedTuple):
    ns: int
    nz: int
    R: int
    NW: int
    L: int
    C: int
    H: int
    T1: int
    T2: int
    wb: int

    @property
    def g(self):
        return self.nz // self.R

    @property
    def nw(self):
        return self.NW // self.g

    @property
    def Lp(self):
        return self.L // 2

    @property
    def cs(self):
        return self.C // self.nz

    @property
    def Ch(self):
        return self.C // self.R

    @property
    def Hh(self):
        return self.H // self.R

    @property
    def steps(self):
        return self.nw // self.wb

    @property
    def chips(self):
        return self.ns // 2

    @property
    def rb(self):
        return self.cs // self.chips

    def place(self):
        s, z = lax.axis_index("seq"), lax.axis_index("ch")
        return s, z, lax.rem(z, self.g), lax.div(z, self.g)


def gelu(z):
    t = jnp.tanh(z * (GC0 + (GC0 * GC1) * (z * z)))
    return z * (0.5 + 0.5 * t)


def gelu_both(z):
    sq = z * z
    t = jnp.tanh(z * (GC0 + (GC0 * GC1) * sq))
    h = 0.5 + 0.5 * t
    v = z * h
    return v, h + v * (1.0 - t) * (GC0 + (3.0 * GC0 * GC1) * sq)


def gelu_slope(z):
    return gelu_both(z)[1]


def fold(v):
    return jnp.sum(v.reshape(v.shape[0] // 8, 8, v.shape[1]), axis=0)


def fold_lanes(v):
    out = v[:, 0:128]
    for k in range(128, v.shape[1], 128):
        out = out + v[:, k : k + 128]
    return out


def unfold(v):
    return jnp.sum(v, axis=0, keepdims=True)


def rows_of(shape):
    return lax.broadcasted_iota(jnp.int32, shape, 0)


def lanes_of(shape):
    return lax.broadcasted_iota(jnp.int32, shape, 1)


def total_of(lens):
    n = lens[0]
    for k in range(1, lens.shape[0]):
        n = n + lens[k]
    return n.astype(F32)


def norm_of(stats, total):
    mean = stats[0:1] / total
    square = stats[1:2] / total
    return mean, lax.rsqrt(square - mean * mean + EPS)


def flat(ref):
    return ref[...].reshape(1, ref.shape[0])


def column(row, n):
    return jnp.broadcast_to(row, (n, row.shape[1])).T


def mm(a, b):
    return jnp.dot(a, b, preferred_element_type=F32)


def mm_nt(a, b):
    return lax.dot_general(a, b, (((1,), (1,)), ((), ())), preferred_element_type=F32)


def mm_tn(a, b):
    return lax.dot_general(a, b, (((0,), (0,)), ((), ())), preferred_element_type=F32)


def mm_tt(a, b):
    return lax.dot_general(a, b, (((0,), (1,)), ((), ())), preferred_element_type=F32)


def eye_matrix(n, m, first):
    return jnp.where(lanes_of((n, m)) == rows_of((n, m)) + first, 1.0, 0.0).astype(BF16)


def pick_matrix(L):
    r, n = rows_of((L, L)), lanes_of((L, L))
    bin_of = 2 * r - jnp.where(r >= L // 2, L - 1, 0)
    return jnp.where(n == bin_of, 1.0, 0.0).astype(BF16)


def remote(src, dst, send, recv, device):
    return pltpu.make_async_remote_copy(
        src_ref=src,
        dst_ref=dst,
        send_sem=send,
        recv_sem=recv,
        device_id=device,
        device_id_type=MESH,
    )


def wrap(v, n):
    return jnp.where(v >= n, v - n, v)


def greet(devices):
    barrier = pltpu.get_barrier_semaphore()
    for device in devices:
        pl.semaphore_signal(barrier, inc=1, device_id=device, device_id_type=MESH)


def meet(devices):
    pl.semaphore_wait(pltpu.get_barrier_semaphore(), len(devices))


class Peers:
    def __init__(self, me, others):
        self.me, self.others = me, others
        self.count = len(others) + 1

    def start(self, link):
        packet, buf, sems = link
        for device in self.others:
            remote(packet, buf.at[self.me], sems.at[0], sems.at[1], device).start()

    def finish(self, link):
        packet, buf, sems = link
        buf[self.me] = packet[...]
        rest = buf.at[pl.ds(0, self.count - 1)]
        done = remote(rest, rest, sems.at[0], sems.at[1], self.others[0])
        done.wait_recv()
        acc = buf[0]
        for q in range(1, self.count):
            acc = acc + buf[q]
        done.wait_send()
        return acc

    def scratch(self, rows, width):
        return [
            pltpu.VMEM((rows, width), F32),
            pltpu.VMEM((self.count, rows, width), F32),
            pltpu.SemaphoreType.DMA((2,)),
        ]


def group_peers(plan):
    s, z, i, h = plan.place()
    g = plan.g
    others = [
        (wrap(s + a, plan.ns), h * g + wrap(i + b, g))
        for a in range(plan.ns)
        for b in range(g)
        if a or b
    ]
    return Peers(s * g + i, others)


def plane_peers(plan):
    s, z, i, h = plan.place()
    return Peers(s, [(wrap(s + a, plan.ns), z) for a in range(1, plan.ns)])


def line_peers(plan):
    s, z, i, h = plan.place()
    return Peers(z, [(s, wrap(z + a, plan.nz)) for a in range(1, plan.nz)])


class Halo:
    def __init__(self, plan, edge, land, sems):
        self.edge, self.land, self.sems = edge, land, sems
        s, z, _, _ = plan.place()
        self.to = ((wrap(s + plan.ns - 1, plan.ns), z), (wrap(s + 1, plan.ns), z))

    def copy(self, side, rows):
        return remote(
            self.edge.at[side, rows],
            self.land.at[1 - side, rows],
            self.sems.at[0, side],
            self.sems.at[1, side],
            self.to[side],
        )

    def start(self, first, count):
        for side in range(2):
            self.copy(side, pl.ds(first, count)).start()

    def finish(self):
        for side in range(2):
            done = self.copy(side, pl.ds(0, self.land.shape[1]))
            done.wait_recv()
            done.wait_send()


HALO_SEMS = pltpu.SemaphoreType.DMA((2, 2))


class Gather:
    def __init__(self, plan, part, full, sems):
        self.plan, self.part, self.full, self.sems = plan, part, full, sems
        self.s, self.z, self.i, self.h = plan.place()
        self.c, self.m = lax.rem(self.s, 2), lax.div(self.s, 2)
        self.chips = plan.chips
        self.every = self.chips // 4
        self.tap = lax.div(self.m, self.every)
        self.owner = lax.rem(self.m, self.every) == 0
        self.mine = full.at[self.c, self.tap]

    def others(self):
        g, nz = self.plan.g, self.plan.nz
        return [(self.s, wrap(self.h * g + g + r, nz)) for r in range(nz - g)]

    def far(self, off):
        return (2 * wrap(self.m + off, self.chips) + self.c, self.z)

    def line(self, off):
        nz = self.plan.nz
        device = (self.s, wrap(self.z + off, nz))
        dst = self.mine.at[nz - off]
        return remote(self.part, dst, self.sems.at[0, 1], self.sems.at[1, 1], device)

    def far_rows(self, taps):
        return self.full.at[self.c, taps, pl.ds(1, self.plan.nz - 1)]

    def chip(self, off):
        rows = self.far_rows(self.tap)
        return remote(rows, rows, self.sems.at[0, 2], self.sems.at[1, 2], self.far(off))

    def pair(self):
        half = self.far_rows(pl.ds(0, 4))
        device = (2 * self.m + 1 - self.c, self.z)
        return remote(half, half, self.sems.at[0, 3], self.sems.at[1, 3], device)

    def line_start(self):
        @pl.when(self.owner)
        def _():
            for off in range(1, self.plan.nz):
                self.line(off).start()

    def line_finish(self):
        @pl.when(self.owner)
        def _():
            rest = self.far_rows(self.tap)
            device = (self.s, wrap(self.z + 1, self.plan.nz))
            done = remote(rest, rest, self.sems.at[0, 1], self.sems.at[1, 1], device)
            done.wait_recv()
            done.wait_send()

    def chips_start(self):
        @pl.when(self.owner)
        def _():
            for off in range(1, self.chips):
                self.chip(off).start()

    def pair_start(self):
        def taken(count):
            rest = self.far_rows(pl.ds(0, count))
            return remote(rest, rest, self.sems.at[0, 2], self.sems.at[1, 2], self.far(1))

        @pl.when(self.owner)
        def _():
            taken(3).wait_recv()
            for off in range(1, self.chips):
                self.chip(off).wait_send()

        if self.every > 1:

            @pl.when(jnp.logical_not(self.owner))
            def _():
                taken(4).wait_recv()

        self.pair().start()

    def pair_finish(self):
        done = self.pair()
        done.wait_recv()
        done.wait_send()


def first_step():
    return pl.program_id(0) == 0


def last_step():
    return pl.program_id(0) == pl.num_programs(0) - 1


def head_kernel(plan, nm, lens, x, xtop, xend, ctop, cend, g2, s2, pb, g3, s3,
                w_hbm, gain, shift, taps, pw,
                X5, x2, land, state, beyond_out, full,
                macc, beyond, xedge, sel, edge, acc, w_ref, w_sem, part,
                gather_sems, xhalo_sems, halo_sems, *links):
    t = pl.program_id(0)
    peers, plane, line = group_peers(plan), plane_peers(plan), line_peers(plan)
    xhalo = Halo(plan, xedge, beyond, xhalo_sems)
    halo = Halo(plan, edge, land, halo_sems)
    gather = Gather(plan, part, full, gather_sems)
    w_copy = pltpu.make_async_copy(w_hbm, w_ref, w_sem)
    plane_link, line_link, link = links[:3], links[3:6], links[6:]
    s, z, i, h = plan.place()
    L, Lp, C, nw, nz, wb = plan.L, plan.Lp, plan.C, plan.nw, plan.nz, plan.wb
    share = plan.NW // nz
    c = t - nm
    everyone = peers.others + gather.others()

    @pl.when(first_step())
    def _():
        w_copy.start()
        greet(everyone)
        part[...] = jnp.where(gather.tap == 3, pw[...], taps[0])
        macc[...] = jnp.zeros_like(macc)
        acc[...] = jnp.zeros_like(acc)
        state[...] = jnp.zeros_like(state)
        state[GAIN1 : GAIN1 + 1] = flat(gain)
        state[SHIFT1 : SHIFT1 + 1] = flat(shift)
        n16 = nw * 16
        for side, (xe, ce, places) in enumerate(
            ((xtop, ctop, (0, 1, 0)), (xend, cend, (14, 15, 15)))
        ):
            for k, at in enumerate(places):
                rows, lanes = rows_of((nw, n16)), lanes_of((nw, n16))
                one = jnp.where(lanes == 16 * rows + at, 1.0, 0.0).astype(BF16)
                block = (xe if k < 2 else ce)[...].reshape(n16, C)
                xedge[side, k] = mm(one, block)
        shape = (Lp, L)
        for odd in range(2):
            at = lanes_of(shape) - (2 * rows_of(shape) + odd)
            one = jnp.where((at == 0) | (at == 1), 1.0, 0.0)
            sel[odd * Lp : (odd + 1) * Lp] = one.astype(BF16)

    @pl.when(c < 0)
    def _():
        rows = rows_of((L, C))
        for w in range(min(share, wb)):
            at = lax.rem(z * share, wb) + w
            valid = 2 * lens[z * share + t * wb + w] - s * L
            v = jnp.where(rows < valid, x[at].astype(F32), 0.0)
            macc[0] += fold(v)
            macc[1] += fold(v * v)

    @pl.when(c == -1)
    def _():
        packet, more = plane_link[0], line_link[0]
        packet[0:1] = unfold(macc[0])
        packet[1:2] = unfold(macc[1])
        meet(everyone)
        plane.start(plane_link)
        xhalo.start(0, 3)
        at = 0
        spans = []
        more[2:3] = jnp.zeros((1, C), F32)
        for ref in (g2, s2, pb, g3, s3):
            n = ref.shape[1]
            more[2:3, at : at + n] = ref[...]
            spans.append((at, n))
            at += n
        more[0:2] = plane.finish(plane_link)
        line.start(line_link)
        gather.line_start()
        state[ST1 : ST1 + 2] = line.finish(line_link)[0:2]
        for k in range(nz):
            row = line_link[1][k]
            for r, (at, n) in zip((GAIN2, SHIFT2, BIAS, GAIN3, SHIFT3), spans):
                state[r : r + 1, k * n : (k + 1) * n] = row[2:3, at : at + n]
        xhalo.finish()
        beyond_out[...] = beyond[...]
        w_copy.wait()

    @pl.when(c >= 0)
    def _():
        mean, rho = norm_of(state[ST1 : ST1 + 2], 2.0 * total_of(lens))
        scale = state[GAIN1 : GAIN1 + 1] * rho
        offset = state[SHIFT1 : SHIFT1 + 1] - mean * scale
        rows = rows_of((L, C))
        row1 = rows_of((1, C))
        row16 = rows_of((16, C))
        def activate(w):
            at = c * wb + w
            valid = 2 * lens[i * nw + at] - s * L
            a = gelu(x[w].astype(F32) * scale + offset)
            a = jnp.where(rows < valid, a, 0.0).astype(BF16)
            picked = mm(sel[...], a)
            even, odd = picked[0:Lp], picked[Lp:]
            top, end = w * Lp, (w + 1) * Lp
            before = [pltpu.roll(v, 1, 0) for v in (even, odd)]
            behind = pltpu.roll(even, Lp - 1, 0)
            for k, v in enumerate((*before, even, odd, behind)):
                X5[k, top:end] = v.astype(BF16)

            def beside(side, k, bin_at):
                a = gelu(beyond[side, k, pl.ds(at, 1), :] * scale + offset)
                here = (row1 + bin_at < valid) & (row1 + (s * L + bin_at) >= 0)
                return jnp.where(here, a, 0.0).astype(BF16).astype(F32)

            l0, l1 = beside(0, 0, -2), beside(0, 1, -1)
            r0, r1 = beside(1, 0, L), beside(1, 1, L + 1)
            start = a[0:1].astype(F32)
            for k, row in ((0, l0 + l1), (1, l1 + start)):
                X5[k, top : top + 16] = jnp.where(row16 == 0, row, before[k][0:16]).astype(BF16)
            X5[3, end - 16 : end] = (
                odd[Lp - 16 :] + jnp.where(row16 == 15, r0, 0.0)
            ).astype(BF16)
            X5[4, end - 16 : end] = jnp.where(row16 == 15, r0 + r1, behind[Lp - 16 :]).astype(BF16)

        nc = 256
        rowp = rows_of((Lp, nc))

        def convolve(first, count):
            span = slice(first * Lp, (first + count) * Lp)
            for n in range(C // nc):
                cols = slice(n * nc, (n + 1) * nc)
                taps = [X5[k, span] for k in range(plan.T1)]
                y = 0.5 * mm(jnp.concatenate(taps, axis=1), w_ref[:, cols])
                s0 = jnp.zeros((8, nc), F32)
                s1 = jnp.zeros((8, nc), F32)
                for w in range(first, first + count):
                    at = c * wb + w
                    valid = lens[i * nw + at] - s * Lp
                    v = y[(w - first) * Lp : (w - first + 1) * Lp]
                    x2[w, :, cols] = v
                    edge[0, at, :, cols] = v[:EDGE].astype(BF16)
                    edge[1, at, :, cols] = v[Lp - EDGE :].astype(BF16)
                    v = jnp.where(rowp < valid, v, 0.0)
                    s0 = s0 + fold(v)
                    s1 = s1 + fold(v * v)
                acc[0:1, cols] += unfold(s0)
                acc[1:2, cols] += unfold(s1)

        count = max(1, wb // 2)
        for first in range(0, wb, count):
            for w in range(first, first + count):
                activate(w)
            convolve(first, count)
        halo.start(c * wb, wb)

    @pl.when(c == 0)
    def _():
        gather.line_finish()
        gather.chips_start()

    @pl.when(last_step())
    def _():
        link[0][...] = acc[...]
        peers.start(link)
        gather.pair_start()
        state[ST2 : ST2 + 2] = peers.finish(link)
        halo.finish()
        gather.pair_finish()


def block_kernel(plan, lens, x2, x2_hbm, x2land, cot, w_ref, pw_ref, own_w, own_pw, old, half_state,
                 dz2, grads, pgrad, res, land, state, res_got,
                 ext, wf, wt, pw, Y3, c2, dz3, das, a3s, a3T, dos, Z3, dcT,
                 cedge, cland, cacc, dedge, dland, dacc, bedge, bacc, halo_sems, bulk_sems,
                 x2half, x2_sem, *links):
    t = pl.program_id(0)
    peers = group_peers(plan)
    s, z, i, h = plan.place()
    Lp, C, H, wb, nw, cs, g = plan.Lp, plan.C, plan.H, plan.wb, plan.nw, plan.cs, plan.g
    M = wb * Lp
    steps = plan.steps
    p0, r0, b0, g0 = block_phases(plan)[:4]
    c_link, d_link, b_link = links[:3], links[3:6], links[6:]
    c_halo = Halo(plan, cedge, cland, halo_sems.at[0])
    d_halo = Halo(plan, dedge, dland, halo_sems.at[1])
    b_halo = Halo(plan, bedge, land, halo_sems.at[2])

    def bulk(off, rows):
        to = wrap(i + off, g)
        return remote(
            res.at[to, rows],
            res_got.at[off, rows],
            bulk_sems.at[0, off],
            bulk_sems.at[1, off],
            (s, h * g + to),
        )

    def result_of(block):
        y = mm(a3s[pl.ds(pl.multiple_of(block * M, 128), M)], pw[:, pl.ds(pl.multiple_of(h * plan.Ch, 128), plan.Ch)])
        rowr = rows_of((Lp, y.shape[1]))
        for w in range(wb):
            at = block * wb + w
            valid = lens[i * plan.nw + at] - s * Lp
            r = x2half[at] + y[w * Lp : (w + 1) * Lp] + half_state[BIAS : BIAS + 1]
            r = jnp.where(rowr < valid, r, 0.0).astype(BF16).T
            for k in range(g):
                res[k, at] = r[k * cs : (k + 1) * cs]

    def send_result(block):
        result_of(block)
        for off in range(1, g):
            bulk(off, pl.ds(block * wb, wb)).start()

    half_copy = pltpu.make_async_copy(
        x2_hbm.at[:, :, pl.ds(pl.multiple_of(h * plan.Ch, 128), plan.Ch)], x2half, x2_sem
    )

    @pl.when(first_step())
    def _():
        half_copy.start()
        greet(peers.others)
        state[...] = old[...]
        cacc[...] = jnp.zeros_like(cacc)
        dacc[...] = jnp.zeros_like(dacc)
        bacc[...] = jnp.zeros_like(bacc)
        hs = H // plan.nz

        def rows_at(which, first=0):
            return pl.ds(pl.multiple_of(first + which * hs, 16), hs)

        for r in range(plan.nz):
            at = wrap(z + r, plan.nz)
            for c in range(2):
                cols = slice(c * (C // 2), (c + 1) * (C // 2))
                pw[rows_at(at), cols] = own_pw[:, cols] if r == 0 else pw_ref[c, 0, r]
                for k in range(plan.T2):
                    v = own_w[k, :, cols] if r == 0 else w_ref[c, k, r]
                    wf[rows_at(at), k * C + cols.start : k * C + cols.stop] = v
                    wt[rows_at(at, k * H), cols] = v

    @pl.when(t < p0)
    def _():
        base = pl.multiple_of(t * M, 128)
        mean, rho = norm_of(state[ST2 : ST2 + 2], total_of(lens))
        scale = state[GAIN2 : GAIN2 + 1] * rho
        offset = state[SHIFT2 : SHIFT2 + 1] - mean * scale
        rows = rows_of((Lp, C))
        rowe = rows_of((EDGE, C))

        rowh = rows_of((Lp, H))
        sums0, sums1 = jnp.zeros((8, H), F32), jnp.zeros((8, H), F32)
        nh = 1
        for first in range(0, wb, wb // nh):
            span = range(first, first + wb // nh)
            for w in span:
                valid = lens[i * plan.nw + t * wb + w] - s * Lp
                a = jnp.where(rows < valid, gelu(x2[w] * scale + offset), 0.0)
                al = gelu(x2land[0, w].astype(F32) * scale + offset)
                al = jnp.where((rowe - EDGE < valid) & (s > 0), al, 0.0)
                ah = gelu(x2land[1, w].astype(F32) * scale + offset)
                ah = jnp.where(rowe + Lp < valid, ah, 0.0)
                ext[w, 0:EDGE] = al
                ext[w, EDGE : EDGE + Lp] = a
                ext[w, EDGE + Lp :] = ah
                top, end = w * Lp, (w + 1) * Lp
                Y3[pl.ds(base + top, Lp), 0:C] = ext[w, EDGE - DIL : EDGE - DIL + Lp].astype(BF16)
                Y3[pl.ds(base + top, Lp), C : 2 * C] = a.astype(BF16)
                Y3[pl.ds(base + top, Lp), 2 * C : 3 * C] = ext[w, EDGE + DIL : EDGE + DIL + Lp].astype(BF16)
            y = mm_nt(Y3[pl.ds(base + first * Lp, wb // nh * Lp)], wf[...])
            for w in span:
                at = t * wb + w
                valid = lens[i * plan.nw + at] - s * Lp
                v = y[(w - first) * Lp : (w - first + 1) * Lp]
                c2[at] = v
                cedge[0, at] = v[:EDGE].astype(BF16)
                cedge[1, at] = v[Lp - EDGE :].astype(BF16)
                v = jnp.where(rowh < valid, v, 0.0)
                sums0 = sums0 + fold(v)
                sums1 = sums1 + fold(v * v)
        cacc[0:1, 0:H] += unfold(sums0)
        cacc[0:1, H:] += unfold(sums1)

    @pl.when(first_step())
    def _():
        meet(peers.others)

    @pl.when(t < p0)
    def _():
        c_halo.start(t * wb, wb)

    @pl.when(t == p0 - 1)
    def _():
        c_link[0][...] = cacc[...]
        peers.start(c_link)

    here_p = (t >= p0) & (t < p0 + steps)

    @pl.when(here_p)
    def _():
        u = t - p0
        rowc = rows_of((Lp, C))
        block = pl.ds(pl.multiple_of(u * M, 128), M)
        bias = jnp.zeros((8, C), F32)
        parts = []
        for w in range(wb):
            valid = lens[i * plan.nw + u * wb + w] - s * Lp
            d = jnp.where(rowc < valid, cot[w].astype(F32), 0.0)
            bias = bias + fold(d)
            parts.append(d.astype(BF16))
        d = jnp.concatenate(parts, axis=0)
        dos[block] = d
        das[...] = mm_nt(d, pw[...])
        dacc[1:2] += unfold(bias)

    @pl.when(t == p0)
    def _():
        got = peers.finish(c_link)
        state[ST3 : ST3 + 1, 0:H] = got[:, 0:H]
        state[ST3 + 1 : ST3 + 2, 0:H] = got[:, H:]

    @pl.when(here_p)
    def _():
        u = t - p0
        block = pl.ds(pl.multiple_of(u * M, 128), M)
        rowh = rows_of((Lp, H))
        mean, rho = norm_of(state[ST3 : ST3 + 2, 0:H], total_of(lens))
        scale = state[GAIN3 : GAIN3 + 1, 0:H] * rho
        offset = state[SHIFT3 : SHIFT3 + 1, 0:H] - mean * scale
        s0, s1 = jnp.zeros((8, H), F32), jnp.zeros((8, H), F32)
        parts = []
        for w in range(wb):
            at = u * wb + w
            valid = lens[i * plan.nw + at] - s * Lp
            top, end = w * Lp, (w + 1) * Lp
            v = c2[at]
            zv = v * scale + offset
            act, slope = gelu_both(zv)
            parts.append(jnp.where(rowh < valid, act, 0.0).astype(BF16))
            dzw = das[top:end] * slope
            dz3[at] = dzw
            dedge[0, at] = dzw[:EDGE].astype(BF16)
            dedge[1, at] = dzw[Lp - EDGE :].astype(BF16)
            s0 = s0 + fold(dzw)
            s1 = s1 + fold(dzw * zv)
        a3 = jnp.concatenate(parts, axis=0)
        a3s[block] = a3
        a3T[:, block] = a3.T
        dacc[0:1, 0:H] += unfold(s0)
        dacc[0:1, H : 2 * H] += unfold(s1)
        d_halo.start(u * wb, wb)

    @pl.when(t == p0)
    def _():
        half_copy.wait()
        send_result(0)

    @pl.when(t == p0 + steps - 1)
    def _():
        d_link[0][...] = dacc[...]
        peers.start(d_link)

    @pl.when(t == r0)
    def _():
        for block in range(1, steps):
            send_result(block)
        rows = pl.ds(pl.multiple_of(h * plan.Hh, 16), plan.Hh)
        pgrad[...] = mm(a3T[rows], dos[...]).astype(BF16)

    @pl.when(t == b0)
    def _():
        got = peers.finish(d_link)
        shift = state[SHIFT3 : SHIFT3 + 1, 0:H]
        gain = state[GAIN3 : GAIN3 + 1, 0:H]
        state[SU3 : SU3 + 1, 0:H] = got[0:1, 0:H]
        state[SU3 + 1 : SU3 + 2, 0:H] = (got[0:1, H : 2 * H] - shift * got[0:1, 0:H]) / gain
        state[BSUM : BSUM + 1] = got[1:2]
        c_halo.finish()
        d_halo.finish()

    @pl.when((t >= b0) & (t < g0))
    def _():
        u = t - b0
        total = total_of(lens)
        mean3, rho3 = norm_of(state[ST3 : ST3 + 2, 0:H], total)
        gr3 = state[GAIN3 : GAIN3 + 1, 0:H] * rho3
        sg3 = state[SU3 : SU3 + 1, 0:H] / total
        gg3 = state[SU3 + 1 : SU3 + 2, 0:H] / total
        mean2, rho2 = norm_of(state[ST2 : ST2 + 2], total)
        scale2 = state[GAIN2 : GAIN2 + 1] * rho2
        offset2 = state[SHIFT2 : SHIFT2 + 1] - mean2 * scale2
        rowh = rows_of((Lp, H))
        rowe = rows_of((EDGE, H))
        rowc = rows_of((Lp, C))

        by_v = -gr3 * rho3 * gg3
        by_1 = gr3 * (mean3 * rho3 * gg3 - sg3)

        def back(dz, v):
            return gr3 * dz + by_v * v + by_1

        for w in range(wb):
            valid = lens[i * nw + u * wb + w] - s * Lp
            d = jnp.where(rowh < valid, back(dz3[u * wb + w], c2[u * wb + w]), 0.0)
            dl = back(dland[0, u * wb + w].astype(F32), cland[0, u * wb + w].astype(F32))
            dl = jnp.where((rowe - EDGE < valid) & (s > 0), dl, 0.0)
            dh = back(dland[1, u * wb + w].astype(F32), cland[1, u * wb + w].astype(F32))
            dh = jnp.where(rowe + Lp < valid, dh, 0.0)
            ext[w, 0:EDGE, 0:H] = dl
            ext[w, EDGE : EDGE + Lp, 0:H] = d
            ext[w, EDGE + Lp :, 0:H] = dh
            top, end = w * Lp, (w + 1) * Lp
            Z3[top:end, 0:H] = ext[w, EDGE + DIL : EDGE + DIL + Lp, 0:H].astype(BF16)
            Z3[top:end, H : 2 * H] = d.astype(BF16)
            Z3[top:end, 2 * H : 3 * H] = ext[w, EDGE - DIL : EDGE - DIL + Lp, 0:H].astype(BF16)

        y = mm(Z3[...], wt[...])

        M = wb * Lp
        dcT[:, pl.ds(pl.multiple_of(u * M, 128), M)] = Z3[:, H : 2 * H].T
        s0, s1 = jnp.zeros((8, C), F32), jnp.zeros((8, C), F32)
        for w in range(wb):
            at = u * wb + w
            valid = lens[i * nw + at] - s * Lp
            v = x2[w]
            zv = v * scale2 + offset2
            dzw = y[w * Lp : (w + 1) * Lp] * gelu_slope(zv)
            dzw = jnp.where(rowc < valid, dzw, 0.0)
            dz2[w] = dzw
            bedge[0, pl.ds(at, 1)] = dzw[0:1]
            bedge[1, pl.ds(at, 1)] = dzw[Lp - 1 : Lp]
            s0 = s0 + fold(dzw)
            s1 = s1 + fold(dzw * zv)
        bacc[0:1] += unfold(s0)
        bacc[1:2] += unfold(s1)

    @pl.when(t == g0 - 1)
    def _():
        b_link[0][...] = bacc[...]
        peers.start(b_link)
        b_halo.start(0, nw)

    @pl.when(last_step())
    def _():
        rows = pl.ds(pl.multiple_of(h * plan.Hh, 16), plan.Hh)
        for n in range(plan.T2):
            cols = slice(n * C, (n + 1) * C)
            grads[:, cols] = mm(dcT[rows], Y3[:, cols]).astype(BF16)

    @pl.when(last_step())
    def _():
        got = peers.finish(b_link)
        shift, gain = state[SHIFT2 : SHIFT2 + 1], state[GAIN2 : GAIN2 + 1]
        state[SU2 : SU2 + 1] = got[0:1]
        state[SU2 + 1 : SU2 + 2] = (got[1:2] - shift * got[0:1]) / gain
        b_halo.finish()
        for off in range(1, g):
            bulk(off, pl.ds(0, nw)).wait()


def block_phases(plan):
    n = plan.steps
    return n, 2 * n, 2 * n + 1, 3 * n + 1, 3 * n + 2


class Reduction:
    def __init__(self, plan, batches, out, give, mine, got, spread, half, mate, sems):
        self.plan, self.batches, self.out = plan, batches, out
        self.give, self.mine, self.got, self.spread = give, mine, got, spread
        self.half, self.mate = half, mate
        self.sems = sems
        self.s, self.z, self.i, self.h = plan.place()
        self.c = lax.rem(self.s, 2)
        self.m = lax.div(self.s, 2)
        self.chips = plan.chips

    @staticmethod
    def scratch(plan, batches):
        taps, wide = plan.T1 + 2, plan.C // 2
        full = (taps, plan.chips, plan.g, plan.rb, wide)
        part = (taps, plan.g, plan.rb, wide)
        return [
            pltpu.VMEM((taps, 2, plan.chips, plan.rb, wide), BF16),
            *[pltpu.VMEM(full, BF16)] * 4,
            *[pltpu.VMEM(part, BF16)] * 2,
            pltpu.SemaphoreType.DMA((2, len(batches), 5)),
        ]

    def copy(self, b, phase, src, dst, device):
        return remote(src, dst, self.sems.at[0, b, phase], self.sems.at[1, b, phase], device)

    def finish(self, b, phase, ref, device):
        done = self.copy(b, phase, ref, ref, device)
        done.wait_recv()
        done.wait_send()

    def taps(self, b):
        return pl.ds(*self.batches[b])

    def pair(self):
        return (2 * self.m + (1 - self.c), self.z)

    def far(self, off):
        return (2 * wrap(self.m + off, self.chips) + self.c, self.z)

    def member(self, off):
        return (self.s, self.h * self.plan.g + wrap(self.i + off, self.plan.g))

    def put(self, k, rows):
        wide = self.plan.C // 2
        for j in range(self.plan.g):
            for m in range(self.chips):
                v = rows(j, m)
                left, right = v[:, :wide], v[:, wide:]
                self.mine[k, m, j] = jnp.where(self.c == 0, left, right).astype(BF16)
                self.give[k, m, j] = jnp.where(self.c == 0, right, left).astype(BF16)

    def step0(self, b):
        taps = self.taps(b)
        self.copy(b, 0, self.give.at[taps], self.got.at[taps], self.pair()).start()

    def step1(self, b):
        taps = self.taps(b)
        self.finish(b, 0, self.got.at[taps], self.pair())
        first, count = self.batches[b]
        for k in range(first, first + count):
            v = self.mine[k].astype(F32) + self.got[k].astype(F32)
            self.mine[k] = v.astype(BF16)
        for off in range(1, self.chips):
            src = self.mine.at[taps, wrap(self.m + off, self.chips)]
            self.copy(b, 1, src, self.spread.at[taps, self.m], self.far(off)).start()

    def step2(self, b):
        taps = self.taps(b)
        self.finish(b, 1, self.spread.at[taps, pl.ds(0, self.chips - 1)], self.far(1))
        first, count = self.batches[b]
        for k in range(first, first + count):
            self.spread[k, self.m] = self.mine[k, self.m]
            v = self.spread[k, 0].astype(F32)
            for n in range(1, self.chips):
                v = v + self.spread[k, n].astype(F32)
            self.half[k] = v.astype(BF16)
        for off in range(1, self.plan.g):
            src = self.half.at[taps, wrap(self.i + off, self.plan.g)]
            self.copy(b, 2, src, self.mate.at[taps, off], self.member(off)).start()

    def step3(self, b):
        taps = self.taps(b)
        self.finish(b, 2, self.mate.at[taps, pl.ds(1, self.plan.g - 1)], self.member(1))
        first, count = self.batches[b]
        for k in range(first, first + count):
            v = self.half[k, self.i].astype(F32)
            for off in range(1, self.plan.g):
                v = v + self.mate[k, off].astype(F32)
            self.out[k, self.c, self.m] = v.astype(BF16)
        mine = self.out.at[taps, self.c, self.m]
        for off in range(1, self.chips):
            self.copy(b, 3, mine, mine, self.far(off)).start()

    def step4(self, b):
        taps = self.taps(b)
        self.finish(b, 3, self.out.at[taps, self.c, pl.ds(0, self.chips - 1)], self.far(1))
        mine = self.out.at[taps, self.c]
        self.copy(b, 4, mine, mine, self.pair()).start()

    def step5(self, b):
        self.finish(b, 4, self.out.at[self.taps(b), self.c], self.pair())


def tail_turns(plan):
    nD, T1 = plan.steps, plan.T1
    turns = [("x", 0)] + [("d", n) for n in range(1, nD)]
    xs, ws = [("x", n) for n in range(1, nD)], [("w", n) for n in range(T1)]
    for count in (1, 1, T1):
        turns += ws[:count] + xs[:1]
        xs, ws = xs[1:], ws[count:]
    return turns + xs


def tail_batches(plan):
    return [(plan.T1, 2), (0, 2)] + [(k, 1) for k in range(2, plan.T1)]


def tail_kernel(plan, lens, dz2, dzland, x2, x2land, cot, beyond, x, X5_hbm, taps_hbm, grads, pgrad,
                old, half_state,
                gz, gz_got, sums, summed,
                ext, D3, D0T, wcat, pick, eye, cols, y, part, split, acc, X5, X5_sems,
                taps, bulk_sems, *rest):
    t = pl.program_id(0)
    s, z, i, h = plan.place()
    L, Lp, C, wb, g, nw = plan.L, plan.Lp, plan.C, plan.wb, plan.g, plan.nw
    Ch, cs, T1 = plan.Ch, plan.cs, plan.T1
    M = wb * Lp
    nD = plan.steps
    turns = tail_turns(plan)
    last = len(turns) - 1
    peers = group_peers(plan)
    red = Reduction(plan, tail_batches(plan), *rest[:8])
    link = rest[8:]

    def member(off):
        return (s, h * g + wrap(i + off, g))

    def send(first, count):
        rows = pl.ds(first, count)
        for off in range(1, g):
            remote(
                part.at[off - 1, rows],
                gz_got.at[off, rows],
                bulk_sems.at[0, off],
                bulk_sems.at[1, off],
                member(off),
            ).start()

    def X5_copy(k):
        return pltpu.make_async_copy(X5_hbm.at[k], X5.at[k % 2], X5_sems.at[k % 2])

    def when(at):
        return pl.when(t == min(at, last))

    def turn(kind, k):
        return turns.index((kind, k)) if (kind, k) in turns else last

    def turn_of(kind):
        index = jnp.int32(0)
        here = False
        for n, (what, k) in enumerate(turns):
            if what == kind:
                index = jnp.where(t == n, k, index)
                here = (t == n) | here
        return here, index

    taps_copy = pltpu.make_async_copy(
        taps_hbm.at[:, pl.ds(pl.multiple_of(h * Ch, 128), Ch)], taps, X5_sems.at[2]
    )

    @when(0)
    def _():
        taps_copy.start()
        greet(peers.others)
        acc[...] = jnp.zeros_like(acc)
        pick[...] = pick_matrix(L)
        eye[...] = eye_matrix(Ch, Ch, 0)
        mean, rho = norm_of(half_state[ST1 : ST1 + 2], 2.0 * total_of(lens))
        scale = half_state[GAIN1 : GAIN1 + 1] * rho
        offset = half_state[SHIFT1 : SHIFT1 + 1] - mean * scale
        for k, row in enumerate((scale, offset)):
            cols[k] = column(row, L)

    @pl.when(t < nD)
    def _():
        total = total_of(lens)
        mean, rho = norm_of(old[ST2 : ST2 + 2], total)
        gr = old[GAIN2 : GAIN2 + 1] * rho
        sg = old[SU2 : SU2 + 1] / total
        gg = old[SU2 + 1 : SU2 + 2] / total
        rowc = rows_of((Lp, C))
        row1 = rows_of((1, C))

        by_dz = 0.5 * gr
        by_v = -0.5 * gr * rho * gg
        by_1 = 0.5 * gr * (mean * rho * gg - sg)

        def back(dout, dz, v):
            return 0.5 * dout + by_dz * dz + by_v * v + by_1

        def grad_of(w):
            at = t * wb + w
            valid = lens[i * nw + at] - s * Lp
            d = back(cot[w].astype(F32), dz2[w], x2[w])
            d = jnp.where(rowc < valid, d, 0.0)
            one = pl.ds(at, 1)
            dl = back(beyond[0, 2, one, :], dzland[0, one, :], x2land[0, w, EDGE - 1 : EDGE].astype(F32))
            dl = jnp.where((row1 - 1 < valid) & (s > 0), dl, 0.0)
            dh = back(beyond[1, 2, one, :], dzland[1, one, :], x2land[1, w, 0:1].astype(F32))
            dh = jnp.where(row1 + Lp < valid, dh, 0.0)
            ext[w, 7:8] = dl
            ext[w, 8 : 8 + Lp] = d
            ext[w, 8 + Lp : 9 + Lp] = dh
            top, end = w * Lp, (w + 1) * Lp
            D3[t, top:end, 0:C] = ext[w, 9 : 9 + Lp].astype(BF16)
            D3[t, top:end, C : 2 * C] = d.astype(BF16)
            D3[t, top:end, 2 * C : 3 * C] = ext[w, 7 : 7 + Lp].astype(BF16)

        for w in range(wb):
            grad_of(w)
        half = D3[t, :, pl.ds(pl.multiple_of(C + h * Ch, 128), Ch)]
        D0T[:, pl.ds(pl.multiple_of(t * M, 128), M)] = half.T

    @when(0)
    def _():
        taps_copy.wait()
        for first in range(0, Ch, 64):
            rows = slice(first, min(first + 64, Ch))
            for r, parts in enumerate((((0,), (1, 2), (3, 4)), ((0, 1), (2, 3), (4,)))):
                for k, which in enumerate(parts):
                    v = taps[which[0], rows]
                    if len(which) > 1:
                        v = (v.astype(F32) + taps[which[1], rows].astype(F32)).astype(BF16)
                    at = r * Ch
                    wcat[at + rows.start : at + rows.stop, k * C : (k + 1) * C] = v
        meet(peers.others)

    here_x, bx = turn_of("x")

    def gradient(hf, nh):
        lanes = lanes_of((Ch, L))

        def through(w):
            valid = 2 * lens[i * nw + bx * wb + w] - s * L
            top, end = w * Lp, (w + 1) * Lp
            v = mm_nt(eye[...], x[w])
            da = jnp.concatenate([y[0:Ch, top:end], y[Ch:, top:end]], axis=1)
            da = mm(da.astype(BF16), pick[...])
            zv = v * cols[0] + cols[1]
            dzw = da * gelu_slope(zv)
            dzw = jnp.where(lanes < valid, dzw, 0.0)
            acc[0] += fold_lanes(dzw)
            acc[1] += fold_lanes(dzw * zv)
            split[w % 2] = dzw.astype(BF16)
            for off in range(g):
                rows = pl.ds(pl.multiple_of(lax.rem(i + off, g) * cs, 16), cs)
                if off == 0:
                    gz[w] = split[w % 2, rows]
                else:
                    part[off - 1, bx * wb + w] = split[w % 2, rows]

        n = wb // nh
        rows = slice(hf * n * Lp, (hf + 1) * n * Lp)
        y[:, rows] = mm_nt(wcat[...], D3[bx, rows])
        for w in range(hf * n, (hf + 1) * n):
            through(w)

    nh = 2 if wb % 2 == 0 and wb * Lp // 2 % 128 == 0 else 1

    @pl.when(here_x)
    def _():
        gradient(0, nh)
        send(bx * wb, wb // nh)

    first = min(1, last)
    w2 = max(turn("w", 2), turn("x", 1))
    w3 = max(turn("w", 3), turn("x", 2))
    w4 = max(turn("w", 4), turn("x", 2))
    table = (
        (first, 1, red.step1, 0),
        (turn("x", 1), 0, red.step2, 0),
        (turn("w", 1), 1, red.step0, 1),
        (turn("x", 2), 0, red.step1, 1),
        (turn("w", 2), 1, red.step0, 2),
        (w2, 1, red.step3, 0),
        (turn("w", 3), 1, red.step0, 3),
        (w3, 1, red.step1, 2),
        (w3, 1, red.step2, 1),
        (turn("w", 4), 1, red.step0, 4),
        (w4, 1, red.step1, 3),
        (w4, 1, red.step4, 0),
        (turn("x", 3), 0, red.step1, 4),
        (turn("x", 3), 0, red.step2, 2),
        (last, 1, red.step2, 3),
        (last, 1, red.step3, 1),
        (last, 1, red.step3, 2),
        (last, 1, red.step2, 4),
    )

    def between(at, end):
        return end == 0 and nh == 2 and turns[at][0] == "x"

    def go_on(entries):
        for at, _, step, batch in entries:

            @when(at)
            def _():
                step(batch)

    go_on([e for e in table if between(*e[:2])])

    if nh == 2:

        @pl.when(here_x)
        def _():
            gradient(1, nh)

    @when(0)
    def _():
        hs = plan.H // plan.nz
        rb = plan.rb
        for u in range(2):

            def rows(j, m, u=u):
                side, r = m * rb // hs, m * rb % hs
                n = 2 * side + u
                rows = slice(j * hs + r, j * hs + r + rb)
                v = grads[rows, n * C : (n + 1) * C] if n < plan.T2 else pgrad[rows]
                return v.astype(F32)

            red.put(T1 + u, rows)
        red.step0(0)

    @when(1)
    def _():
        X5_copy(0).start()
        X5_copy(1).start()

    here_w, k = turn_of("w")

    @pl.when(here_w)
    def _():
        X5_copy(k).wait()
        y[0:Ch, 0:C] = mm(D0T[...], X5[lax.rem(k, 2)])

        @pl.when(k < T1 - 2)
        def _():
            X5_copy(k + 2).start()

        rb = plan.rb
        red.put(k, lambda j, m: y[j * cs + m * rb : j * cs + (m + 1) * rb, 0:C])

    @when(turn("x", nD - 1))
    def _():
        packet = link[0]
        packet[...] = jnp.zeros_like(packet)
        packet[0:1, 0:Ch] = jnp.sum(acc[0].T, axis=0, keepdims=True)
        packet[1:2, 0:Ch] = jnp.sum(acc[1].T, axis=0, keepdims=True)
        peers.start(link)

    go_on([e for e in table if not between(*e[:2])])

    @pl.when(here_x & (bx < nD - 1))
    def _():
        if nh == 2:
            send(bx * wb + wb // nh, wb // nh)

    @when(last)
    def _():
        if nh == 2:
            send(nw - wb // 2, wb // 2)

    @when(last)
    def _():
        red.step3(3)
        red.step4(1)
        red.step4(2)
        red.step3(4)
        red.step4(3)
        got = peers.finish(link)[:, 0:Ch]
        shift, gain = half_state[SHIFT1 : SHIFT1 + 1], half_state[GAIN1 : GAIN1 + 1]
        sums[0:1] = got[0:1]
        sums[1:2] = (got[1:2] - shift * got[0:1]) / gain
        red.step4(4)
        for b in range(5):
            red.step5(b)
        own = pltpu.make_async_copy(red.out, summed, X5_sems.at[0])
        own.start()
        for off in range(1, g):
            done = remote(
                part.at[off - 1],
                gz_got.at[off],
                bulk_sems.at[0, off],
                bulk_sems.at[1, off],
                member(off),
            )
            done.wait_recv()
            done.wait_send()
        own.wait()


def input_grad_kernel(plan, wg, lens, x, gz, gz_got, sums, res, res_got, summed,
                      state, half_state,
                      out, out_result, conv_grad, dil_grad, point_grad,
                      g1, b1, g2, b2, g3, b3, pb, eye, cols, xt):
    t = pl.program_id(0)
    s, z, i, h = plan.place()
    L, Ch, cs = plan.L, plan.Ch, plan.cs
    turn = plan.nw // wg
    mine = pl.ds(pl.multiple_of(i * cs, 16), cs)

    @pl.when(first_step())
    def _():
        n = 2.0 * total_of(lens)
        mean, rho = norm_of(half_state[ST1 : ST1 + 2], n)
        gr = half_state[GAIN1 : GAIN1 + 1] * rho
        gg = sums[1:2] / n * rho
        for k, row in enumerate((gr, -gr * gg, gr * (mean * gg - sums[0:1] / n))):
            xt[...] = column(row, L)
            cols[k] = xt[mine]
        eye[...] = eye_matrix(cs, Ch, i * cs)

        def mine_of(src, at, which, count, *dsts):
            n = dsts[0].shape[1]
            for k in range(count):

                @pl.when(which == k)
                def _():
                    for dst, r in zip(dsts, at):
                        dst[...] = src[r : r + 1, k * n : (k + 1) * n]

        mine_of(sums, (1, 0), i, plan.g, g1, b1)
        mine_of(state, (SU2 + 1, SU2), z, plan.nz, g2, b2)
        mine_of(state, (SU3 + 1, SU3), z, plan.nz, g3, b3)
        mine_of(state, (BSUM,), z, plan.nz, pb)

    own = lax.div(t, turn) == i
    for w in range(wg):
        out_result[w] = jnp.where(own, res[0, w], res_got[0, w])

    C, T1, hs, rb, wide = plan.C, plan.T1, plan.H // plan.nz, plan.rb, plan.C // 2
    count = plan.NW // wg
    turns = min(count, plan.chips)
    per, every = plan.chips // turns, count // turns

    def spread(chunk):
        for n in range(per):
            m = chunk * per + n
            side, r = m * rb // hs, m * rb % hs
            for c in range(2):
                at = slice(c * wide, (c + 1) * wide)
                for k in range(T1):
                    conv_grad[k, n * rb : (n + 1) * rb, at] = summed[k, c, n].astype(F32)
                for u in range(2):
                    v = summed[T1 + u, c, n].astype(F32)
                    if 2 * side + u < plan.T2:
                        dil_grad[2 * side + u, r : r + rb, at] = v
                    else:
                        point_grad[r : r + rb, at] = v

    for chunk in range(turns):
        pl.when(t == chunk * every)(partial(spread, chunk))

    lanes = lanes_of((cs, L))
    for w in range(wg):
        valid = 2 * lens[t * wg + w] - s * L
        v = mm_nt(eye[...], x[w])
        dz = jnp.where(own, gz[w], gz_got[0, w]).astype(F32)
        r = cols[0] * dz + v * cols[1] + cols[2]
        out[w] = jnp.where(lanes < valid, r, 0.0).astype(BF16)


def call(kernel, plan, name, steps, ins, outs, scratch, flops, nbytes, cid=None):
    extra = {} if cid is None else dict(collective_id=cid, has_side_effects=True)
    return pl.pallas_call(
        partial(kernel, plan),
        grid=(steps,),
        in_specs=[SMEM] + [spec for spec, _ in ins],
        out_specs=[spec for spec, _, _ in outs],
        out_shape=[jax.ShapeDtypeStruct(shape, dtype) for _, shape, dtype in outs],
        scratch_shapes=scratch,
        compiler_params=pltpu.CompilerParams(vmem_limit_bytes=VMEM_LIMIT, **extra),
        cost_estimate=pl.CostEstimate(
            flops=int(flops), bytes_accessed=int(nbytes), transcendentals=0
        ),
        name=name,
    )


def per_device(
    inputs,
    lengths,
    input_gain,
    input_shift,
    conv_weight,
    branch_gain,
    branch_shift,
    dilated_tap_weight,
    mixer_gain,
    mixer_shift,
    point_weight,
    point_bias,
    cotangent,
):
    NW, L, C = inputs.shape
    Lp = L // 2
    nz = lax.axis_size("ch")
    R = 2
    plan = Plan(
        ns=lax.axis_size("seq"),
        nz=nz,
        R=R,
        NW=NW,
        L=L,
        C=C,
        H=mixer_gain.shape[0] * nz,
        T1=conv_weight.shape[0],
        T2=dilated_tap_weight.shape[0],
        wb=min(NW * R // nz, max(1, 512 // Lp)),
    )
    g, nw, cs, Ch, H, Hh, wb = plan.g, plan.nw, plan.cs, plan.Ch, plan.H, plan.Hh, plan.wb
    T1, T2, steps = plan.T1, plan.T2, plan.steps
    M = wb * Lp
    hs = H // nz
    lens = lengths.astype(jnp.int32)

    def row(a):
        return a.reshape(1, a.shape[0])

    def grp():
        return lax.rem(lax.axis_index("ch"), g)

    def half():
        return lax.div(lax.axis_index("ch"), g)

    def core():
        return lax.rem(lax.axis_index("seq"), 2)

    def chip4():
        return lax.div(lax.axis_index("seq"), plan.ns // 4)

    def whole(*shape):
        return pl.BlockSpec(shape, lambda t: (0,) * len(shape), pipeline_mode=pl.Buffered(1))

    def const(*shape):
        return pl.BlockSpec(shape, lambda t: (0,) * len(shape))

    def win(*shape):
        return pl.BlockSpec(shape, lambda t: (t,) + (0,) * (len(shape) - 1))

    def arg_win(n, width):
        return pl.BlockSpec((wb, n, width), lambda t: (grp() * steps + t, 0, 0))

    def ins(*pairs):
        return [p for p in pairs]

    share = NW // nz
    nm = max(1, share // wb)

    def edge_spec(n):
        return pl.BlockSpec(
            (nw, 16, C), lambda t: (grp(), n, 0), pipeline_mode=pl.Buffered(1)
        )

    def head_block(t):
        own = lax.div(lax.axis_index("ch") * share, wb) + t
        return jnp.where(t < nm, own, grp() * steps + t - nm), 0, 0

    def after(*shape):
        return pl.BlockSpec(
            shape, lambda t: (jnp.maximum(t - nm, 0),) + (0,) * (len(shape) - 1)
        )

    pairs = ins(
        (pl.BlockSpec((wb, L, C), head_block), inputs),
        (edge_spec(0), inputs),
        (edge_spec(L // 16 - 1), inputs),
        (edge_spec(0), cotangent),
        (edge_spec(Lp // 16 - 1), cotangent),
        (whole(1, cs), row(branch_gain)),
        (whole(1, cs), row(branch_shift)),
        (whole(1, cs), row(point_bias)),
        (whole(1, H // nz), row(mixer_gain)),
        (whole(1, H // nz), row(mixer_shift)),
        (ANY, conv_weight.reshape(T1 * C, C)),
        (whole(C), input_gain),
        (whole(C), input_shift),
        (
            pl.BlockSpec(
                (1, hs, C // 2),
                lambda t: (jnp.minimum(chip4(), T2 - 1), 0, core()),
                pipeline_mode=pl.Buffered(1),
            ),
            jnp.swapaxes(dilated_tap_weight, 1, 2),
        ),
        (
            pl.BlockSpec(
                (hs, C // 2), lambda t: (0, core()), pipeline_mode=pl.Buffered(1)
            ),
            point_weight,
        ),
    )
    plane, line, group = plane_peers(plan), line_peers(plan), group_peers(plan)
    state_shape = (STATE, C)
    edges2, edges3 = (2, nw, EDGE, C), (2, nw, EDGE, H)
    X5, x2, land2, state, beyond, full = call(
        lambda plan, *refs: head_kernel(plan, nm, *refs),
        plan,
        "head",
        nm + steps,
        pairs,
        [
            (
                pl.BlockSpec((T1, M, C), lambda t: (0, jnp.maximum(t - nm, 0), 0)),
                (T1, nw * Lp, C),
                BF16,
            ),
            (after(wb, Lp, C), (nw, Lp, C), F32),
            (ANY, edges2, BF16),
            (const(*state_shape), state_shape, F32),
            (const(2, 3, nw, C), (2, 3, nw, C), F32),
            (ANY, (2, T2 + 1, nz, hs, C // 2), BF16),
        ],
        [
            pltpu.VMEM((2, 8, C), F32),
            pltpu.VMEM((2, 3, nw, C), F32),
            pltpu.VMEM((2, 3, nw, C), F32),
            pltpu.VMEM((L, L), BF16),
            pltpu.VMEM(edges2, BF16),
            pltpu.VMEM((2, C), F32),
            pltpu.VMEM((T1 * C, C), BF16),
            pltpu.SemaphoreType.DMA,
            pltpu.VMEM((hs, C // 2), BF16),
            pltpu.SemaphoreType.DMA((2, 4)),
            HALO_SEMS,
            HALO_SEMS,
        ]
        + plane.scratch(2, C)
        + line.scratch(3, C)
        + group.scratch(2, C),
        2 * nw * Lp * T1 * C * C,
        nw * Lp * C * 20,
        cid=1,
    )(lens, *[a for _, a in pairs])

    taps_spec = whole(2, T2, nz, hs, C // 2)
    pw_spec = pl.BlockSpec(
        (2, 1, nz, hs, C // 2), lambda t: (0, T2, 0, 0, 0), pipeline_mode=pl.Buffered(1)
    )

    def early(*shape):
        return pl.BlockSpec(
            shape, lambda t: (jnp.minimum(t, steps - 1),) + (0,) * (len(shape) - 1)
        )

    def early_land(width):
        return pl.BlockSpec(
            (2, wb, EDGE, width), lambda t: (0, jnp.minimum(t, steps - 1), 0, 0)
        )

    def half_of(n):
        return pl.BlockSpec((n, Ch), lambda t: (0, half()), pipeline_mode=pl.Buffered(1))

    cot_spec = pl.BlockSpec(
        (wb, Lp, C), lambda t: (grp() * steps + jnp.minimum(t, steps - 1), 0, 0)
    )

    p0, r0, b0, g0, block_steps = block_phases(plan)

    def at_phase(first):
        return lambda t: jnp.clip(t - first, 0, steps - 1)

    in_p, in_b = at_phase(p0), at_phase(b0)
    pairs = ins(
        (
            pl.BlockSpec(
                (wb, Lp, C),
                lambda t: (jnp.where(t < p0 + steps, jnp.minimum(t, steps - 1), in_b(t)), 0, 0),
            ),
            x2,
        ),
        (ANY, x2),
        (early_land(C), land2),
        (pl.BlockSpec((wb, Lp, C), lambda t: (grp() * steps + in_p(t), 0, 0)), cotangent),
        (taps_spec, full),
        (pw_spec, full),
        (whole(T2, hs, C), jnp.swapaxes(dilated_tap_weight, 1, 2)),
        (whole(hs, C), point_weight),
        (whole(*state_shape), state),
        (half_of(STATE), state),
    )
    dz2, grads, pgrad, res, dland2, state, res_got = call(
        block_kernel,
        plan,
        "block",
        block_steps,
        pairs,
        [
            (pl.BlockSpec((wb, Lp, C), lambda t: (in_b(t), 0, 0)), (nw, Lp, C), F32),
            (const(Hh, T2 * C), (Hh, T2 * C), BF16),
            (const(Hh, C), (Hh, C), BF16),
            (const(g, nw, cs, Lp), (g, nw, cs, Lp), BF16),
            (ANY, (2, nw, C), F32),
            (const(*state_shape), state_shape, F32),
            (ANY, (g, nw, cs, Lp), BF16),
        ],
        [
            pltpu.VMEM((wb, Lp + 2 * EDGE, C), F32),
            pltpu.VMEM((H, T2 * C), BF16),
            pltpu.VMEM((T2 * H, C), BF16),
            pltpu.VMEM((H, C), BF16),
            pltpu.VMEM((nw * Lp, T2 * C), BF16),
            pltpu.VMEM((nw, Lp, H), F32),
            pltpu.VMEM((nw, Lp, H), F32),
            pltpu.VMEM((M, H), F32),
            pltpu.VMEM((nw * Lp, H), BF16),
            pltpu.VMEM((H, nw * Lp), BF16),
            pltpu.VMEM((nw * Lp, C), BF16),
            pltpu.VMEM((M, T2 * H), BF16),
            pltpu.VMEM((H, nw * Lp), BF16),
            pltpu.VMEM(edges3, BF16),
            pltpu.VMEM(edges3, BF16),
            pltpu.VMEM((1, 2 * H), F32),
            pltpu.VMEM(edges3, BF16),
            pltpu.VMEM(edges3, BF16),
            pltpu.VMEM((2, C), F32),
            pltpu.VMEM((2, nw, C), F32),
            pltpu.VMEM((2, C), F32),
            pltpu.SemaphoreType.DMA((3, 2, 2)),
            pltpu.SemaphoreType.DMA((2, g)),
            pltpu.VMEM((nw, Lp, Ch), F32),
            pltpu.SemaphoreType.DMA,
        ]
        + group.scratch(1, 2 * H)
        + group.scratch(2, C)
        + group.scratch(2, C),
        nw * Lp * C * H * (6 * T2 + 6),
        nw * Lp * C * 30,
        cid=3,
    )(lens, *[a for _, a in pairs])

    chips, rb = plan.chips, plan.rb
    turns_t = tail_turns(plan)

    def x_block(t):
        block = jnp.int32(0)
        for n, (what, k) in enumerate(turns_t):
            if what == "x":
                block = jnp.where(t >= n, k, block)
        return block

    sshape = (T1 + 2, 2, chips, rb, C // 2)
    pairs = ins(
        (early(wb, Lp, C), dz2),
        (whole(2, nw, C), dland2),
        (early(wb, Lp, C), x2),
        (early_land(C), land2),
        (cot_spec, cotangent),
        (whole(2, 3, nw, C), beyond),
        (
            pl.BlockSpec(
                (wb, L, Ch), lambda t: (grp() * steps + x_block(t), 0, half())
            ),
            inputs,
        ),
        (ANY, X5),
        (ANY, conv_weight),
        (whole(Hh, T2 * C), grads),
        (whole(Hh, C), pgrad),
        (whole(*state_shape), state),
        (half_of(STATE), state),
    )
    gz, gz_got, sums1, summed = call(
        tail_kernel,
        plan,
        "tail",
        len(turns_t),
        pairs,
        [
            (pl.BlockSpec((wb, cs, L), lambda t: (x_block(t), 0, 0)), (nw, cs, L), BF16),
            (ANY, (g, nw, cs, L), BF16),
            (const(2, Ch), (2, Ch), F32),
            (ANY, sshape, BF16),
        ],
        [
            pltpu.VMEM((wb, Lp + 16, C), F32),
            pltpu.VMEM((steps, M, 3 * C), BF16),
            pltpu.VMEM((Ch, nw * Lp), BF16),
            pltpu.VMEM((2 * Ch, 3 * C), BF16),
            pltpu.VMEM((L, L), BF16),
            pltpu.VMEM((Ch, Ch), BF16),
            pltpu.VMEM((2, Ch, L), F32),
            pltpu.VMEM((2 * Ch, max(M, C)), F32),
            pltpu.VMEM((g - 1, nw, cs, L), BF16),
            pltpu.VMEM((2, Ch, L), BF16),
            pltpu.VMEM((2, Ch, min(L, 128)), F32),
            pltpu.VMEM((2, nw * Lp, C), BF16),
            pltpu.SemaphoreType.DMA((3,)),
            pltpu.VMEM((T1, Ch, C), BF16),
            pltpu.SemaphoreType.DMA((2, g)),
        ]
        + Reduction.scratch(plan, tail_batches(plan))
        + group.scratch(2, C),
        2 * nw * Lp * (6 + T1) * C * Ch,
        nw * Lp * C * 40,
        cid=6,
    )(lens, *[a for _, a in pairs])

    wg = min(2 * wb, nw)
    count = NW // wg
    turn = nw // wg
    turns = min(count, chips)

    def own_block(t):
        return jnp.where(lax.div(t, turn) == grp(), lax.rem(t, turn), 0)

    def got_slot(t):
        off = lax.rem(grp() - lax.div(t, turn) + g, g)
        return jnp.maximum(off, 1), jnp.where(off > 0, lax.rem(t, turn), 0)

    pairs = ins(
        (pl.BlockSpec((wg, L, Ch), lambda t: (t, 0, half())), inputs),
        (pl.BlockSpec((wg, cs, L), lambda t: (own_block(t), 0, 0)), gz),
        (pl.BlockSpec((1, wg, cs, L), lambda t: got_slot(t) + (0, 0)), gz_got),
        (whole(2, Ch), sums1),
        (pl.BlockSpec((1, wg, cs, Lp), lambda t: (grp(), own_block(t), 0, 0)), res),
        (pl.BlockSpec((1, wg, cs, Lp), lambda t: got_slot(t) + (0, 0)), res_got),
        (
            pl.BlockSpec(
                (T1 + 2, 2, chips // turns, rb, C // 2),
                lambda t: (0, 0, t * turns // count, 0, 0),
            ),
            summed,
        ),
        (whole(*state_shape), state),
        (half_of(STATE), state),
    )
    outs = call(
        lambda plan, *refs: input_grad_kernel(plan, wg, *refs),
        plan,
        "input_grad",
        count,
        pairs,
        [
            (win(wg, cs, L), (NW, cs, L), BF16),
            (win(wg, cs, Lp), (NW, cs, Lp), BF16),
            (
                pl.BlockSpec((T1, cs // turns, C), lambda t: (0, t * turns // count, 0)),
                (T1, cs, C),
                F32,
            ),
            (const(T2, hs, C), (T2, hs, C), F32),
            (const(hs, C), (hs, C), F32),
        ]
        + [(const(1, n), (1, n), F32) for n in (cs, cs, cs, cs, hs, hs, cs)],
        [
            pltpu.VMEM((cs, Ch), BF16),
            pltpu.VMEM((3, cs, L), F32),
            pltpu.VMEM((Ch, L), F32),
        ],
        2 * NW * L * Ch * cs,
        NW * L * cs * 8,
    )(lens, *[a for _, a in pairs])
    grad, result, conv_grad, dil_grad, point_grad = outs[:5]
    g1, b1, g2, b2, g3, b3, pb = [a[0] for a in outs[5:]]
    return (
        jnp.swapaxes(result, 1, 2),
        jnp.swapaxes(grad, 1, 2),
        jnp.swapaxes(conv_grad, 1, 2),
        g1,
        b1,
        g2,
        b2,
        jnp.swapaxes(dil_grad, 1, 2),
        g3,
        b3,
        point_grad,
        pb,
    )


def solution(mesh):
    in_specs = (
        P(None, "seq", None),
        P(),
        P(),
        P(),
        P(),
        P("ch"),
        P("ch"),
        P(None, None, "ch"),
        P("ch"),
        P("ch"),
        P("ch", None),
        P("ch"),
        P(None, "seq", None),
    )
    out_specs = (
        P(None, "seq", "ch"),
        P(None, "seq", "ch"),
        P(None, None, "ch"),
        P("ch"),
        P("ch"),
        P("ch"),
        P("ch"),
        P(None, None, "ch"),
        P("ch"),
        P("ch"),
        P("ch", None),
        P("ch"),
    )
    return jax.shard_map(
        per_device, mesh=mesh, in_specs=in_specs, out_specs=out_specs, check_vma=False
    )
```

```python
from functools import partial
from typing import NamedTuple

import jax
import jax.numpy as jnp
from jax import lax
from jax.experimental import pallas as pl
from jax.experimental.pallas import tpu as pltpu
from jax.sharding import PartitionSpec as P

DIL = 14
EDGE = 16
EPS = 1e-05
GC0 = 0.7978845608028654
GC1 = 0.044715
F32 = jnp.float32
BF16 = jnp.bfloat16
MESH = pl.DeviceIdType.MESH
VMEM_LIMIT = 58 * 1024 * 1024
ANY = pl.BlockSpec(memory_space=pl.ANY)
SMEM = pl.BlockSpec(memory_space=pltpu.SMEM)


ST1, GAIN2, SHIFT2, BIAS, GAIN3, SHIFT3, GAIN1, SHIFT1, ST2, ST3, SU3, BSUM, SU2 = (
    0, 2, 3, 4, 5, 6, 7, 8, 9, 11, 13, 15, 16
)
STATE = 24


class Plan(NamedTuple):
    ns: int
    nz: int
    R: int
    NW: int
    L: int
    C: int
    H: int
    T1: int
    T2: int
    wb: int

    @property
    def g(self):
        return self.nz // self.R

    @property
    def nw(self):
        return self.NW // self.g

    @property
    def Lp(self):
        return self.L // 2

    @property
    def cs(self):
        return self.C // self.nz

    @property
    def Ch(self):
        return self.C // self.R

    @property
    def Hh(self):
        return self.H // self.R

    @property
    def steps(self):
        return self.nw // self.wb

    @property
    def chips(self):
        return self.ns // 2

    @property
    def rb(self):
        return self.cs // self.chips

    def place(self):
        s, z = lax.axis_index("seq"), lax.axis_index("ch")
        return s, z, lax.rem(z, self.g), lax.div(z, self.g)


def gelu(z):
    t = jnp.tanh(z * (GC0 + (GC0 * GC1) * (z * z)))
    return z * (0.5 + 0.5 * t)


def gelu_both(z):
    sq = z * z
    t = jnp.tanh(z * (GC0 + (GC0 * GC1) * sq))
    h = 0.5 + 0.5 * t
    v = z * h
    return v, h + v * (1.0 - t) * (GC0 + (3.0 * GC0 * GC1) * sq)


def gelu_slope(z):
    return gelu_both(z)[1]


def fold(v):
    return jnp.sum(v.reshape(v.shape[0] // 8, 8, v.shape[1]), axis=0)


def fold_lanes(v):
    out = v[:, 0:128]
    for k in range(128, v.shape[1], 128):
        out = out + v[:, k : k + 128]
    return out


def unfold(v):
    return jnp.sum(v, axis=0, keepdims=True)


def rows_of(shape):
    return lax.broadcasted_iota(jnp.int32, shape, 0)


def lanes_of(shape):
    return lax.broadcasted_iota(jnp.int32, shape, 1)


def total_of(lens):
    n = lens[0]
    for k in range(1, lens.shape[0]):
        n = n + lens[k]
    return n.astype(F32)


def norm_of(stats, total):
    mean = stats[0:1] / total
    square = stats[1:2] / total
    return mean, lax.rsqrt(square - mean * mean + EPS)


def flat(ref):
    return ref[...].reshape(1, ref.shape[0])


def column(row, n):
    return jnp.broadcast_to(row, (n, row.shape[1])).T


def mm(a, b):
    return jnp.dot(a, b, preferred_element_type=F32)


def mm_nt(a, b):
    return lax.dot_general(a, b, (((1,), (1,)), ((), ())), preferred_element_type=F32)


def mm_tn(a, b):
    return lax.dot_general(a, b, (((0,), (0,)), ((), ())), preferred_element_type=F32)


def mm_tt(a, b):
    return lax.dot_general(a, b, (((0,), (1,)), ((), ())), preferred_element_type=F32)


def eye_matrix(n, m, first):
    return jnp.where(lanes_of((n, m)) == rows_of((n, m)) + first, 1.0, 0.0).astype(BF16)


def pick_matrix(L):
    r, n = rows_of((L, L)), lanes_of((L, L))
    bin_of = 2 * r - jnp.where(r >= L // 2, L - 1, 0)
    return jnp.where(n == bin_of, 1.0, 0.0).astype(BF16)


def remote(src, dst, send, recv, device):
    return pltpu.make_async_remote_copy(
        src_ref=src,
        dst_ref=dst,
        send_sem=send,
        recv_sem=recv,
        device_id=device,
        device_id_type=MESH,
    )


def wrap(v, n):
    return jnp.where(v >= n, v - n, v)


def greet(devices):
    barrier = pltpu.get_barrier_semaphore()
    for device in devices:
        pl.semaphore_signal(barrier, inc=1, device_id=device, device_id_type=MESH)


def meet(devices):
    pl.semaphore_wait(pltpu.get_barrier_semaphore(), len(devices))


class Peers:
    def __init__(self, me, others):
        self.me, self.others = me, others
        self.count = len(others) + 1

    def start(self, link):
        packet, buf, sems = link
        for device in self.others:
            remote(packet, buf.at[self.me], sems.at[0], sems.at[1], device).start()

    def finish(self, link):
        packet, buf, sems = link
        buf[self.me] = packet[...]
        rest = buf.at[pl.ds(0, self.count - 1)]
        done = remote(rest, rest, sems.at[0], sems.at[1], self.others[0])
        done.wait_recv()
        acc = buf[0]
        for q in range(1, self.count):
            acc = acc + buf[q]
        done.wait_send()
        return acc

    def scratch(self, rows, width):
        return [
            pltpu.VMEM((rows, width), F32),
            pltpu.VMEM((self.count, rows, width), F32),
            pltpu.SemaphoreType.DMA((2,)),
        ]


def group_peers(plan):
    s, z, i, h = plan.place()
    g = plan.g
    others = [
        (wrap(s + a, plan.ns), h * g + wrap(i + b, g))
        for a in range(plan.ns)
        for b in range(g)
        if a or b
    ]
    return Peers(s * g + i, others)


def plane_peers(plan):
    s, z, i, h = plan.place()
    return Peers(s, [(wrap(s + a, plan.ns), z) for a in range(1, plan.ns)])


def line_peers(plan):
    s, z, i, h = plan.place()
    return Peers(z, [(s, wrap(z + a, plan.nz)) for a in range(1, plan.nz)])


class Halo:
    def __init__(self, plan, edge, land, sems):
        self.edge, self.land, self.sems = edge, land, sems
        s, z, _, _ = plan.place()
        self.to = ((wrap(s + plan.ns - 1, plan.ns), z), (wrap(s + 1, plan.ns), z))

    def copy(self, side, rows):
        return remote(
            self.edge.at[side, rows],
            self.land.at[1 - side, rows],
            self.sems.at[0, side],
            self.sems.at[1, side],
            self.to[side],
        )

    def start(self, first, count):
        for side in range(2):
            self.copy(side, pl.ds(first, count)).start()

    def finish(self):
        for side in range(2):
            done = self.copy(side, pl.ds(0, self.land.shape[1]))
            done.wait_recv()
            done.wait_send()


HALO_SEMS = pltpu.SemaphoreType.DMA((2, 2))


class Gather:
    def __init__(self, plan, part, full, sems):
        self.plan, self.part, self.full, self.sems = plan, part, full, sems
        self.s, self.z, self.i, self.h = plan.place()
        self.c, self.m = lax.rem(self.s, 2), lax.div(self.s, 2)
        self.chips = plan.chips
        self.every = self.chips // 4
        self.tap = lax.div(self.m, self.every)
        self.owner = lax.rem(self.m, self.every) == 0
        self.mine = full.at[self.c, self.tap]

    def others(self):
        g, nz = self.plan.g, self.plan.nz
        return [(self.s, wrap(self.h * g + g + r, nz)) for r in range(nz - g)]

    def far(self, off):
        return (2 * wrap(self.m + off, self.chips) + self.c, self.z)

    def line(self, off):
        nz = self.plan.nz
        device = (self.s, wrap(self.z + off, nz))
        dst = self.mine.at[nz - off]
        return remote(self.part, dst, self.sems.at[0, 1], self.sems.at[1, 1], device)

    def far_rows(self, taps):
        return self.full.at[self.c, taps, pl.ds(1, self.plan.nz - 1)]

    def chip(self, off):
        rows = self.far_rows(self.tap)
        return remote(rows, rows, self.sems.at[0, 2], self.sems.at[1, 2], self.far(off))

    def pair(self):
        half = self.far_rows(pl.ds(0, 4))
        device = (2 * self.m + 1 - self.c, self.z)
        return remote(half, half, self.sems.at[0, 3], self.sems.at[1, 3], device)

    def line_start(self):
        @pl.when(self.owner)
        def _():
            for off in range(1, self.plan.nz):
                self.line(off).start()

    def line_finish(self):
        @pl.when(self.owner)
        def _():
            rest = self.far_rows(self.tap)
            device = (self.s, wrap(self.z + 1, self.plan.nz))
            done = remote(rest, rest, self.sems.at[0, 1], self.sems.at[1, 1], device)
            done.wait_recv()
            done.wait_send()

    def chips_start(self):
        @pl.when(self.owner)
        def _():
            for off in range(1, self.chips):
                self.chip(off).start()

    def pair_start(self):
        def taken(count):
            rest = self.far_rows(pl.ds(0, count))
            return remote(rest, rest, self.sems.at[0, 2], self.sems.at[1, 2], self.far(1))

        @pl.when(self.owner)
        def _():
            taken(3).wait_recv()
            for off in range(1, self.chips):
                self.chip(off).wait_send()

        if self.every > 1:

            @pl.when(jnp.logical_not(self.owner))
            def _():
                taken(4).wait_recv()

        self.pair().start()

    def pair_finish(self):
        done = self.pair()
        done.wait_recv()
        done.wait_send()


def first_step():
    return pl.program_id(0) == 0


def last_step():
    return pl.program_id(0) == pl.num_programs(0) - 1


def head_kernel(plan, nm, lens, x, xtop, xend, ctop, cend, g2, s2, pb, g3, s3,
                w_hbm, gain, shift, taps, pw,
                X5, x2, land, state, beyond_out, full,
                macc, beyond, xedge, sel, edge, acc, w_ref, w_sem, part,
                gather_sems, xhalo_sems, halo_sems, *links):
    t = pl.program_id(0)
    peers, plane, line = group_peers(plan), plane_peers(plan), line_peers(plan)
    xhalo = Halo(plan, xedge, beyond, xhalo_sems)
    halo = Halo(plan, edge, land, halo_sems)
    gather = Gather(plan, part, full, gather_sems)
    w_copy = pltpu.make_async_copy(w_hbm, w_ref, w_sem)
    plane_link, line_link, link = links[:3], links[3:6], links[6:]
    s, z, i, h = plan.place()
    L, Lp, C, nw, nz, wb = plan.L, plan.Lp, plan.C, plan.nw, plan.nz, plan.wb
    share = plan.NW // nz
    c = t - nm
    everyone = peers.others + gather.others()

    @pl.when(first_step())
    def _():
        w_copy.start()
        greet(everyone)
        part[...] = jnp.where(gather.tap == 3, pw[...], taps[0])
        macc[...] = jnp.zeros_like(macc)
        acc[...] = jnp.zeros_like(acc)
        state[...] = jnp.zeros_like(state)
        state[GAIN1 : GAIN1 + 1] = flat(gain)
        state[SHIFT1 : SHIFT1 + 1] = flat(shift)
        n16 = nw * 16
        for side, (xe, ce, places) in enumerate(
            ((xtop, ctop, (0, 1, 0)), (xend, cend, (14, 15, 15)))
        ):
            for k, at in enumerate(places):
                rows, lanes = rows_of((nw, n16)), lanes_of((nw, n16))
                one = jnp.where(lanes == 16 * rows + at, 1.0, 0.0).astype(BF16)
                block = (xe if k < 2 else ce)[...].reshape(n16, C)
                xedge[side, k] = mm(one, block)
        shape = (Lp, L)
        for odd in range(2):
            at = lanes_of(shape) - (2 * rows_of(shape) + odd)
            one = jnp.where((at == 0) | (at == 1), 1.0, 0.0)
            sel[odd * Lp : (odd + 1) * Lp] = one.astype(BF16)

    @pl.when(c < 0)
    def _():
        rows = rows_of((L, C))
        for w in range(min(share, wb)):
            at = lax.rem(z * share, wb) + w
            valid = 2 * lens[z * share + t * wb + w] - s * L
            v = jnp.where(rows < valid, x[at].astype(F32), 0.0)
            macc[0] += fold(v)
            macc[1] += fold(v * v)

    @pl.when(c == -1)
    def _():
        packet, more = plane_link[0], line_link[0]
        packet[0:1] = unfold(macc[0])
        packet[1:2] = unfold(macc[1])
        meet(everyone)
        plane.start(plane_link)
        xhalo.start(0, 3)
        at = 0
        spans = []
        more[2:3] = jnp.zeros((1, C), F32)
        for ref in (g2, s2, pb, g3, s3):
            n = ref.shape[1]
            more[2:3, at : at + n] = ref[...]
            spans.append((at, n))
            at += n
        more[0:2] = plane.finish(plane_link)
        line.start(line_link)
        gather.line_start()
        state[ST1 : ST1 + 2] = line.finish(line_link)[0:2]
        for k in range(nz):
            row = line_link[1][k]
            for r, (at, n) in zip((GAIN2, SHIFT2, BIAS, GAIN3, SHIFT3), spans):
                state[r : r + 1, k * n : (k + 1) * n] = row[2:3, at : at + n]
        xhalo.finish()
        beyond_out[...] = beyond[...]
        w_copy.wait()

    @pl.when(c >= 0)
    def _():
        mean, rho = norm_of(state[ST1 : ST1 + 2], 2.0 * total_of(lens))
        scale = state[GAIN1 : GAIN1 + 1] * rho
        offset = state[SHIFT1 : SHIFT1 + 1] - mean * scale
        rows = rows_of((L, C))
        row1 = rows_of((1, C))
        row16 = rows_of((16, C))
        def activate(w):
            at = c * wb + w
            valid = 2 * lens[i * nw + at] - s * L
            a = gelu(x[w].astype(F32) * scale + offset)
            a = jnp.where(rows < valid, a, 0.0).astype(BF16)
            picked = mm(sel[...], a)
            even, odd = picked[0:Lp], picked[Lp:]
            top, end = w * Lp, (w + 1) * Lp
            before = [pltpu.roll(v, 1, 0) for v in (even, odd)]
            behind = pltpu.roll(even, Lp - 1, 0)
            for k, v in enumerate((*before, even, odd, behind)):
                X5[k, top:end] = v.astype(BF16)

            def beside(side, k, bin_at):
                a = gelu(beyond[side, k, pl.ds(at, 1), :] * scale + offset)
                here = (row1 + bin_at < valid) & (row1 + (s * L + bin_at) >= 0)
                return jnp.where(here, a, 0.0).astype(BF16).astype(F32)

            l0, l1 = beside(0, 0, -2), beside(0, 1, -1)
            r0, r1 = beside(1, 0, L), beside(1, 1, L + 1)
            start = a[0:1].astype(F32)
            for k, row in ((0, l0 + l1), (1, l1 + start)):
                X5[k, top : top + 16] = jnp.where(row16 == 0, row, before[k][0:16]).astype(BF16)
            X5[3, end - 16 : end] = (
                odd[Lp - 16 :] + jnp.where(row16 == 15, r0, 0.0)
            ).astype(BF16)
            X5[4, end - 16 : end] = jnp.where(row16 == 15, r0 + r1, behind[Lp - 16 :]).astype(BF16)

        nc = 256
        rowp = rows_of((Lp, nc))

        def convolve(first, count):
            span = slice(first * Lp, (first + count) * Lp)
            for n in range(C // nc):
                cols = slice(n * nc, (n + 1) * nc)
                taps = [X5[k, span] for k in range(plan.T1)]
                y = 0.5 * mm(jnp.concatenate(taps, axis=1), w_ref[:, cols])
                s0 = jnp.zeros((8, nc), F32)
                s1 = jnp.zeros((8, nc), F32)
                for w in range(first, first + count):
                    at = c * wb + w
                    valid = lens[i * nw + at] - s * Lp
                    v = y[(w - first) * Lp : (w - first + 1) * Lp]
                    x2[w, :, cols] = v
                    edge[0, at, :, cols] = v[:EDGE].astype(BF16)
                    edge[1, at, :, cols] = v[Lp - EDGE :].astype(BF16)
                    v = jnp.where(rowp < valid, v, 0.0)
                    s0 = s0 + fold(v)
                    s1 = s1 + fold(v * v)
                acc[0:1, cols] += unfold(s0)
                acc[1:2, cols] += unfold(s1)

        count = max(1, wb // 2)
        for first in range(0, wb, count):
            for w in range(first, first + count):
                activate(w)
            convolve(first, count)
        halo.start(c * wb, wb)

    @pl.when(c == 0)
    def _():
        gather.line_finish()
        gather.chips_start()

    @pl.when(last_step())
    def _():
        link[0][...] = acc[...]
        peers.start(link)
        gather.pair_start()
        state[ST2 : ST2 + 2] = peers.finish(link)
        halo.finish()
        gather.pair_finish()


def block_kernel(plan, lens, x2, x2_hbm, x2land, cot, w_ref, pw_ref, own_w, own_pw, old, half_state,
                 dz2, grads, pgrad, res, land, state, res_got,
                 ext, wf, wt, pw, Y3, c2, dz3, das, a3s, a3T, dos, Z3, dcT,
                 cedge, cland, cacc, dedge, dland, dacc, bedge, bacc, halo_sems, bulk_sems,
                 x2half, x2_sem, *links):
    t = pl.program_id(0)
    peers = group_peers(plan)
    s, z, i, h = plan.place()
    Lp, C, H, wb, nw, cs, g = plan.Lp, plan.C, plan.H, plan.wb, plan.nw, plan.cs, plan.g
    M = wb * Lp
    steps = plan.steps
    p0, r0, b0, g0 = block_phases(plan)[:4]
    c_link, d_link, b_link = links[:3], links[3:6], links[6:]
    c_halo = Halo(plan, cedge, cland, halo_sems.at[0])
    d_halo = Halo(plan, dedge, dland, halo_sems.at[1])
    b_halo = Halo(plan, bedge, land, halo_sems.at[2])

    def bulk(off, rows):
        to = wrap(i + off, g)
        return remote(
            res.at[to, rows],
            res_got.at[off, rows],
            bulk_sems.at[0, off],
            bulk_sems.at[1, off],
            (s, h * g + to),
        )

    def result_of(block):
        y = mm(a3s[pl.ds(pl.multiple_of(block * M, 128), M)], pw[:, pl.ds(pl.multiple_of(h * plan.Ch, 128), plan.Ch)])
        rowr = rows_of((Lp, y.shape[1]))
        for w in range(wb):
            at = block * wb + w
            valid = lens[i * plan.nw + at] - s * Lp
            r = x2half[at] + y[w * Lp : (w + 1) * Lp] + half_state[BIAS : BIAS + 1]
            r = jnp.where(rowr < valid, r, 0.0).astype(BF16).T
            for k in range(g):
                res[k, at] = r[k * cs : (k + 1) * cs]

    def send_result(block):
        result_of(block)
        for off in range(1, g):
            bulk(off, pl.ds(block * wb, wb)).start()

    half_copy = pltpu.make_async_copy(
        x2_hbm.at[:, :, pl.ds(pl.multiple_of(h * plan.Ch, 128), plan.Ch)], x2half, x2_sem
    )

    @pl.when(first_step())
    def _():
        half_copy.start()
        greet(peers.others)
        state[...] = old[...]
        cacc[...] = jnp.zeros_like(cacc)
        dacc[...] = jnp.zeros_like(dacc)
        bacc[...] = jnp.zeros_like(bacc)
        hs = H // plan.nz

        def rows_at(which, first=0):
            return pl.ds(pl.multiple_of(first + which * hs, 16), hs)

        for r in range(plan.nz):
            at = wrap(z + r, plan.nz)
            for c in range(2):
                cols = slice(c * (C // 2), (c + 1) * (C // 2))
                pw[rows_at(at), cols] = own_pw[:, cols] if r == 0 else pw_ref[c, 0, r]
                for k in range(plan.T2):
                    v = own_w[k, :, cols] if r == 0 else w_ref[c, k, r]
                    wf[rows_at(at), k * C + cols.start : k * C + cols.stop] = v
                    wt[rows_at(at, k * H), cols] = v

    @pl.when(t < p0)
    def _():
        base = pl.multiple_of(t * M, 128)
        mean, rho = norm_of(state[ST2 : ST2 + 2], total_of(lens))
        scale = state[GAIN2 : GAIN2 + 1] * rho
        offset = state[SHIFT2 : SHIFT2 + 1] - mean * scale
        rows = rows_of((Lp, C))
        rowe = rows_of((EDGE, C))

        rowh = rows_of((Lp, H))
        sums0, sums1 = jnp.zeros((8, H), F32), jnp.zeros((8, H), F32)
        nh = min(2, wb)
        for first in range(0, wb, wb // nh):
            span = range(first, first + wb // nh)
            for w in span:
                valid = lens[i * plan.nw + t * wb + w] - s * Lp
                a = jnp.where(rows < valid, gelu(x2[w] * scale + offset), 0.0)
                al = gelu(x2land[0, w].astype(F32) * scale + offset)
                al = jnp.where((rowe - EDGE < valid) & (s > 0), al, 0.0)
                ah = gelu(x2land[1, w].astype(F32) * scale + offset)
                ah = jnp.where(rowe + Lp < valid, ah, 0.0)
                ext[w, 0:EDGE] = al
                ext[w, EDGE : EDGE + Lp] = a
                ext[w, EDGE + Lp :] = ah
                top, end = w * Lp, (w + 1) * Lp
                Y3[pl.ds(base + top, Lp), 0:C] = ext[w, EDGE - DIL : EDGE - DIL + Lp].astype(BF16)
                Y3[pl.ds(base + top, Lp), C : 2 * C] = a.astype(BF16)
                Y3[pl.ds(base + top, Lp), 2 * C : 3 * C] = ext[w, EDGE + DIL : EDGE + DIL + Lp].astype(BF16)
            y = mm_nt(Y3[pl.ds(base + first * Lp, wb // nh * Lp)], wf[...])
            for w in span:
                at = t * wb + w
                valid = lens[i * plan.nw + at] - s * Lp
                v = y[(w - first) * Lp : (w - first + 1) * Lp]
                c2[at] = v
                cedge[0, at] = v[:EDGE].astype(BF16)
                cedge[1, at] = v[Lp - EDGE :].astype(BF16)
                v = jnp.where(rowh < valid, v, 0.0)
                sums0 = sums0 + fold(v)
                sums1 = sums1 + fold(v * v)
        cacc[0:1, 0:H] += unfold(sums0)
        cacc[0:1, H:] += unfold(sums1)

    @pl.when(first_step())
    def _():
        meet(peers.others)

    @pl.when(t < p0)
    def _():
        c_halo.start(t * wb, wb)

    @pl.when(t == p0 - 1)
    def _():
        c_link[0][...] = cacc[...]
        peers.start(c_link)

    here_p = (t >= p0) & (t < p0 + steps)

    @pl.when(here_p)
    def _():
        u = t - p0
        rowc = rows_of((Lp, C))
        block = pl.ds(pl.multiple_of(u * M, 128), M)
        bias = jnp.zeros((8, C), F32)
        parts = []
        for w in range(wb):
            valid = lens[i * plan.nw + u * wb + w] - s * Lp
            d = jnp.where(rowc < valid, cot[w].astype(F32), 0.0)
            bias = bias + fold(d)
            parts.append(d.astype(BF16))
        d = jnp.concatenate(parts, axis=0)
        dos[block] = d
        das[...] = mm_nt(d, pw[...])
        dacc[1:2] += unfold(bias)

    @pl.when(t == p0)
    def _():
        got = peers.finish(c_link)
        state[ST3 : ST3 + 1, 0:H] = got[:, 0:H]
        state[ST3 + 1 : ST3 + 2, 0:H] = got[:, H:]

    @pl.when(here_p)
    def _():
        u = t - p0
        block = pl.ds(pl.multiple_of(u * M, 128), M)
        rowh = rows_of((Lp, H))
        mean, rho = norm_of(state[ST3 : ST3 + 2, 0:H], total_of(lens))
        scale = state[GAIN3 : GAIN3 + 1, 0:H] * rho
        offset = state[SHIFT3 : SHIFT3 + 1, 0:H] - mean * scale
        s0, s1 = jnp.zeros((8, H), F32), jnp.zeros((8, H), F32)
        parts = []
        for w in range(wb):
            at = u * wb + w
            valid = lens[i * plan.nw + at] - s * Lp
            top, end = w * Lp, (w + 1) * Lp
            v = c2[at]
            zv = v * scale + offset
            act, slope = gelu_both(zv)
            parts.append(jnp.where(rowh < valid, act, 0.0).astype(BF16))
            dzw = das[top:end] * slope
            dz3[at] = dzw
            dedge[0, at] = dzw[:EDGE].astype(BF16)
            dedge[1, at] = dzw[Lp - EDGE :].astype(BF16)
            s0 = s0 + fold(dzw)
            s1 = s1 + fold(dzw * zv)
        a3 = jnp.concatenate(parts, axis=0)
        a3s[block] = a3
        a3T[:, block] = a3.T
        dacc[0:1, 0:H] += unfold(s0)
        dacc[0:1, H : 2 * H] += unfold(s1)
        d_halo.start(u * wb, wb)

    @pl.when(t == p0)
    def _():
        half_copy.wait()
        send_result(0)

    @pl.when(t == p0 + steps - 1)
    def _():
        d_link[0][...] = dacc[...]
        peers.start(d_link)

    @pl.when(t == r0)
    def _():
        for block in range(1, steps):
            send_result(block)
        rows = pl.ds(pl.multiple_of(h * plan.Hh, 16), plan.Hh)
        pgrad[...] = mm(a3T[rows], dos[...]).astype(BF16)

    @pl.when(t == b0)
    def _():
        got = peers.finish(d_link)
        shift = state[SHIFT3 : SHIFT3 + 1, 0:H]
        gain = state[GAIN3 : GAIN3 + 1, 0:H]
        state[SU3 : SU3 + 1, 0:H] = got[0:1, 0:H]
        state[SU3 + 1 : SU3 + 2, 0:H] = (got[0:1, H : 2 * H] - shift * got[0:1, 0:H]) / gain
        state[BSUM : BSUM + 1] = got[1:2]
        c_halo.finish()
        d_halo.finish()

    @pl.when((t >= b0) & (t < g0))
    def _():
        u = t - b0
        total = total_of(lens)
        mean3, rho3 = norm_of(state[ST3 : ST3 + 2, 0:H], total)
        gr3 = state[GAIN3 : GAIN3 + 1, 0:H] * rho3
        sg3 = state[SU3 : SU3 + 1, 0:H] / total
        gg3 = state[SU3 + 1 : SU3 + 2, 0:H] / total
        mean2, rho2 = norm_of(state[ST2 : ST2 + 2], total)
        scale2 = state[GAIN2 : GAIN2 + 1] * rho2
        offset2 = state[SHIFT2 : SHIFT2 + 1] - mean2 * scale2
        rowh = rows_of((Lp, H))
        rowe = rows_of((EDGE, H))
        rowc = rows_of((Lp, C))

        by_v = -gr3 * rho3 * gg3
        by_1 = gr3 * (mean3 * rho3 * gg3 - sg3)

        def back(dz, v):
            return gr3 * dz + by_v * v + by_1

        for w in range(wb):
            valid = lens[i * nw + u * wb + w] - s * Lp
            d = jnp.where(rowh < valid, back(dz3[u * wb + w], c2[u * wb + w]), 0.0)
            dl = back(dland[0, u * wb + w].astype(F32), cland[0, u * wb + w].astype(F32))
            dl = jnp.where((rowe - EDGE < valid) & (s > 0), dl, 0.0)
            dh = back(dland[1, u * wb + w].astype(F32), cland[1, u * wb + w].astype(F32))
            dh = jnp.where(rowe + Lp < valid, dh, 0.0)
            ext[w, 0:EDGE, 0:H] = dl
            ext[w, EDGE : EDGE + Lp, 0:H] = d
            ext[w, EDGE + Lp :, 0:H] = dh
            top, end = w * Lp, (w + 1) * Lp
            Z3[top:end, 0:H] = ext[w, EDGE + DIL : EDGE + DIL + Lp, 0:H].astype(BF16)
            Z3[top:end, H : 2 * H] = d.astype(BF16)
            Z3[top:end, 2 * H : 3 * H] = ext[w, EDGE - DIL : EDGE - DIL + Lp, 0:H].astype(BF16)

        y = mm(Z3[...], wt[...])

        M = wb * Lp
        dcT[:, pl.ds(pl.multiple_of(u * M, 128), M)] = Z3[:, H : 2 * H].T
        s0, s1 = jnp.zeros((8, C), F32), jnp.zeros((8, C), F32)
        for w in range(wb):
            at = u * wb + w
            valid = lens[i * nw + at] - s * Lp
            v = x2[w]
            zv = v * scale2 + offset2
            dzw = y[w * Lp : (w + 1) * Lp] * gelu_slope(zv)
            dzw = jnp.where(rowc < valid, dzw, 0.0)
            dz2[w] = dzw
            bedge[0, pl.ds(at, 1)] = dzw[0:1]
            bedge[1, pl.ds(at, 1)] = dzw[Lp - 1 : Lp]
            s0 = s0 + fold(dzw)
            s1 = s1 + fold(dzw * zv)
        bacc[0:1] += unfold(s0)
        bacc[1:2] += unfold(s1)

    @pl.when(t == g0 - 1)
    def _():
        b_link[0][...] = bacc[...]
        peers.start(b_link)
        b_halo.start(0, nw)

    @pl.when(last_step())
    def _():
        rows = pl.ds(pl.multiple_of(h * plan.Hh, 16), plan.Hh)
        for n in range(plan.T2):
            cols = slice(n * C, (n + 1) * C)
            grads[:, cols] = mm(dcT[rows], Y3[:, cols]).astype(BF16)

    @pl.when(last_step())
    def _():
        got = peers.finish(b_link)
        shift, gain = state[SHIFT2 : SHIFT2 + 1], state[GAIN2 : GAIN2 + 1]
        state[SU2 : SU2 + 1] = got[0:1]
        state[SU2 + 1 : SU2 + 2] = (got[1:2] - shift * got[0:1]) / gain
        b_halo.finish()
        for off in range(1, g):
            bulk(off, pl.ds(0, nw)).wait()


def block_phases(plan):
    n = plan.steps
    return n, 2 * n, 2 * n + 1, 3 * n + 1, 3 * n + 2


class Reduction:
    def __init__(self, plan, batches, out, give, mine, got, spread, half, mate, sems):
        self.plan, self.batches, self.out = plan, batches, out
        self.give, self.mine, self.got, self.spread = give, mine, got, spread
        self.half, self.mate = half, mate
        self.sems = sems
        self.s, self.z, self.i, self.h = plan.place()
        self.c = lax.rem(self.s, 2)
        self.m = lax.div(self.s, 2)
        self.chips = plan.chips

    @staticmethod
    def scratch(plan, batches):
        taps, wide = plan.T1 + 2, plan.C // 2
        full = (taps, plan.chips, plan.g, plan.rb, wide)
        part = (taps, plan.g, plan.rb, wide)
        return [
            pltpu.VMEM((taps, 2, plan.chips, plan.rb, wide), BF16),
            *[pltpu.VMEM(full, BF16)] * 4,
            *[pltpu.VMEM(part, BF16)] * 2,
            pltpu.SemaphoreType.DMA((2, len(batches), 5)),
        ]

    def copy(self, b, phase, src, dst, device):
        return remote(src, dst, self.sems.at[0, b, phase], self.sems.at[1, b, phase], device)

    def finish(self, b, phase, ref, device):
        done = self.copy(b, phase, ref, ref, device)
        done.wait_recv()
        done.wait_send()

    def taps(self, b):
        return pl.ds(*self.batches[b])

    def pair(self):
        return (2 * self.m + (1 - self.c), self.z)

    def far(self, off):
        return (2 * wrap(self.m + off, self.chips) + self.c, self.z)

    def member(self, off):
        return (self.s, self.h * self.plan.g + wrap(self.i + off, self.plan.g))

    def put(self, k, rows):
        wide = self.plan.C // 2
        for j in range(self.plan.g):
            for m in range(self.chips):
                v = rows(j, m)
                left, right = v[:, :wide], v[:, wide:]
                self.mine[k, m, j] = jnp.where(self.c == 0, left, right).astype(BF16)
                self.give[k, m, j] = jnp.where(self.c == 0, right, left).astype(BF16)

    def step0(self, b):
        taps = self.taps(b)
        self.copy(b, 0, self.give.at[taps], self.got.at[taps], self.pair()).start()

    def step1(self, b):
        taps = self.taps(b)
        self.finish(b, 0, self.got.at[taps], self.pair())
        first, count = self.batches[b]
        for k in range(first, first + count):
            v = self.mine[k].astype(F32) + self.got[k].astype(F32)
            self.mine[k] = v.astype(BF16)
        for off in range(1, self.chips):
            src = self.mine.at[taps, wrap(self.m + off, self.chips)]
            self.copy(b, 1, src, self.spread.at[taps, self.m], self.far(off)).start()

    def step2(self, b):
        taps = self.taps(b)
        self.finish(b, 1, self.spread.at[taps, pl.ds(0, self.chips - 1)], self.far(1))
        first, count = self.batches[b]
        for k in range(first, first + count):
            self.spread[k, self.m] = self.mine[k, self.m]
            v = self.spread[k, 0].astype(F32)
            for n in range(1, self.chips):
                v = v + self.spread[k, n].astype(F32)
            self.half[k] = v.astype(BF16)
        for off in range(1, self.plan.g):
            src = self.half.at[taps, wrap(self.i + off, self.plan.g)]
            self.copy(b, 2, src, self.mate.at[taps, off], self.member(off)).start()

    def step3(self, b):
        taps = self.taps(b)
        self.finish(b, 2, self.mate.at[taps, pl.ds(1, self.plan.g - 1)], self.member(1))
        first, count = self.batches[b]
        for k in range(first, first + count):
            v = self.half[k, self.i].astype(F32)
            for off in range(1, self.plan.g):
                v = v + self.mate[k, off].astype(F32)
            self.out[k, self.c, self.m] = v.astype(BF16)
        mine = self.out.at[taps, self.c, self.m]
        for off in range(1, self.chips):
            self.copy(b, 3, mine, mine, self.far(off)).start()

    def step4(self, b):
        taps = self.taps(b)
        self.finish(b, 3, self.out.at[taps, self.c, pl.ds(0, self.chips - 1)], self.far(1))
        mine = self.out.at[taps, self.c]
        self.copy(b, 4, mine, mine, self.pair()).start()

    def step5(self, b):
        self.finish(b, 4, self.out.at[self.taps(b), self.c], self.pair())


def tail_turns(plan):
    nD, T1 = plan.steps, plan.T1
    turns = [("x", 0)] + [("d", n) for n in range(1, nD)]
    xs, ws = [("x", n) for n in range(1, nD)], [("w", n) for n in range(T1)]
    for count in (2, 2, T1):
        turns += ws[:count] + xs[:1]
        xs, ws = xs[1:], ws[count:]
    return turns + xs


def tail_batches(plan):
    return [(plan.T1, 2), (0, 2)] + [(k, 1) for k in range(2, plan.T1)]


def tail_kernel(plan, lens, dz2, dzland, x2, x2land, cot, beyond, x, X5_hbm, taps_hbm, grads, pgrad,
                old, half_state,
                gz, gz_got, sums, summed,
                ext, D3, D0T, wcat, pick, eye, cols, y, part, split, acc, X5, X5_sems,
                taps, bulk_sems, *rest):
    t = pl.program_id(0)
    s, z, i, h = plan.place()
    L, Lp, C, wb, g, nw = plan.L, plan.Lp, plan.C, plan.wb, plan.g, plan.nw
    Ch, cs, T1 = plan.Ch, plan.cs, plan.T1
    M = wb * Lp
    nD = plan.steps
    turns = tail_turns(plan)
    last = len(turns) - 1
    peers = group_peers(plan)
    red = Reduction(plan, tail_batches(plan), *rest[:8])
    link = rest[8:]

    def member(off):
        return (s, h * g + wrap(i + off, g))

    def send(first, count):
        rows = pl.ds(first, count)
        for off in range(1, g):
            remote(
                part.at[off - 1, rows],
                gz_got.at[off, rows],
                bulk_sems.at[0, off],
                bulk_sems.at[1, off],
                member(off),
            ).start()

    def X5_copy(k):
        return pltpu.make_async_copy(X5_hbm.at[k], X5.at[k % 2], X5_sems.at[k % 2])

    def when(at):
        return pl.when(t == min(at, last))

    def turn(kind, k):
        return turns.index((kind, k)) if (kind, k) in turns else last

    def turn_of(kind):
        index = jnp.int32(0)
        here = False
        for n, (what, k) in enumerate(turns):
            if what == kind:
                index = jnp.where(t == n, k, index)
                here = (t == n) | here
        return here, index

    taps_copy = pltpu.make_async_copy(
        taps_hbm.at[:, pl.ds(pl.multiple_of(h * Ch, 128), Ch)], taps, X5_sems.at[2]
    )

    @when(0)
    def _():
        taps_copy.start()
        greet(peers.others)
        acc[...] = jnp.zeros_like(acc)
        pick[...] = pick_matrix(L)
        eye[...] = eye_matrix(Ch, Ch, 0)
        mean, rho = norm_of(half_state[ST1 : ST1 + 2], 2.0 * total_of(lens))
        scale = half_state[GAIN1 : GAIN1 + 1] * rho
        offset = half_state[SHIFT1 : SHIFT1 + 1] - mean * scale
        for k, row in enumerate((scale, offset)):
            cols[k] = column(row, L)

    @pl.when(t < nD)
    def _():
        total = total_of(lens)
        mean, rho = norm_of(old[ST2 : ST2 + 2], total)
        gr = old[GAIN2 : GAIN2 + 1] * rho
        sg = old[SU2 : SU2 + 1] / total
        gg = old[SU2 + 1 : SU2 + 2] / total
        rowc = rows_of((Lp, C))
        row1 = rows_of((1, C))

        by_dz = 0.5 * gr
        by_v = -0.5 * gr * rho * gg
        by_1 = 0.5 * gr * (mean * rho * gg - sg)

        def back(dout, dz, v):
            return 0.5 * dout + by_dz * dz + by_v * v + by_1

        def grad_of(w):
            at = t * wb + w
            valid = lens[i * nw + at] - s * Lp
            d = back(cot[w].astype(F32), dz2[w], x2[w])
            d = jnp.where(rowc < valid, d, 0.0)
            one = pl.ds(at, 1)
            dl = back(beyond[0, 2, one, :], dzland[0, one, :], x2land[0, w, EDGE - 1 : EDGE].astype(F32))
            dl = jnp.where((row1 - 1 < valid) & (s > 0), dl, 0.0)
            dh = back(beyond[1, 2, one, :], dzland[1, one, :], x2land[1, w, 0:1].astype(F32))
            dh = jnp.where(row1 + Lp < valid, dh, 0.0)
            ext[w, 7:8] = dl
            ext[w, 8 : 8 + Lp] = d
            ext[w, 8 + Lp : 9 + Lp] = dh
            top, end = w * Lp, (w + 1) * Lp
            D3[t, top:end, 0:C] = ext[w, 9 : 9 + Lp].astype(BF16)
            D3[t, top:end, C : 2 * C] = d.astype(BF16)
            D3[t, top:end, 2 * C : 3 * C] = ext[w, 7 : 7 + Lp].astype(BF16)

        for w in range(wb):
            grad_of(w)
        half = D3[t, :, pl.ds(pl.multiple_of(C + h * Ch, 128), Ch)]
        D0T[:, pl.ds(pl.multiple_of(t * M, 128), M)] = half.T

    @when(0)
    def _():
        taps_copy.wait()
        for first in range(0, Ch, 64):
            rows = slice(first, min(first + 64, Ch))
            for r, parts in enumerate((((0,), (1, 2), (3, 4)), ((0, 1), (2, 3), (4,)))):
                for k, which in enumerate(parts):
                    v = taps[which[0], rows]
                    if len(which) > 1:
                        v = (v.astype(F32) + taps[which[1], rows].astype(F32)).astype(BF16)
                    at = r * Ch
                    wcat[at + rows.start : at + rows.stop, k * C : (k + 1) * C] = v
        meet(peers.others)

    here_x, bx = turn_of("x")

    def gradient(hf, nh):
        lanes = lanes_of((Ch, L))

        def through(w):
            valid = 2 * lens[i * nw + bx * wb + w] - s * L
            top, end = w * Lp, (w + 1) * Lp
            v = mm_nt(eye[...], x[w])
            da = jnp.concatenate([y[0:Ch, top:end], y[Ch:, top:end]], axis=1)
            da = mm(da.astype(BF16), pick[...])
            zv = v * cols[0] + cols[1]
            dzw = da * gelu_slope(zv)
            dzw = jnp.where(lanes < valid, dzw, 0.0)
            acc[0] += fold_lanes(dzw)
            acc[1] += fold_lanes(dzw * zv)
            split[w % 2] = dzw.astype(BF16)
            for off in range(g):
                rows = pl.ds(pl.multiple_of(lax.rem(i + off, g) * cs, 16), cs)
                if off == 0:
                    gz[w] = split[w % 2, rows]
                else:
                    part[off - 1, bx * wb + w] = split[w % 2, rows]

        n = wb // nh
        rows = slice(hf * n * Lp, (hf + 1) * n * Lp)
        y[:, rows] = mm_nt(wcat[...], D3[bx, rows])
        for w in range(hf * n, (hf + 1) * n):
            through(w)

    nh = 2 if wb % 2 == 0 and wb * Lp // 2 % 128 == 0 else 1

    @pl.when(here_x)
    def _():
        gradient(0, nh)
        send(bx * wb, wb // nh)

    first = min(1, last)
    table = (
        (first, 1, red.step1, 0),
        (max(turn("w", 1), first + 1), 1, red.step2, 0),
        (turn("w", 1), 1, red.step0, 1),
        (turn("x", 1), 0, red.step1, 1),
        (turn("w", 2), 1, red.step0, 2),
        (turn("w", 2), 1, red.step3, 0),
        (turn("w", 3), 1, red.step0, 3),
        (turn("w", 3), 1, red.step1, 2),
        (max(turn("w", 3), turn("x", 1)), 1, red.step2, 1),
        (turn("x", 2), 0, red.step1, 3),
        (turn("x", 2), 0, red.step4, 0),
        (turn("x", 2), 1, red.step2, 2),
        (turn("w", 4), 1, red.step0, 4),
        (max(turn("w", 4), turn("x", 2)), 1, red.step3, 1),
        (turn("x", 3), 0, red.step1, 4),
        (turn("x", 3), 0, red.step2, 3),
        (last, 1, red.step3, 2),
        (last, 1, red.step2, 4),
    )

    def between(at, end):
        return end == 0 and nh == 2 and turns[at][0] == "x"

    def go_on(entries):
        for at, _, step, batch in entries:

            @when(at)
            def _():
                step(batch)

    go_on([e for e in table if between(*e[:2])])

    if nh == 2:

        @pl.when(here_x)
        def _():
            gradient(1, nh)

    @when(0)
    def _():
        hs = plan.H // plan.nz
        rb = plan.rb
        for u in range(2):

            def rows(j, m, u=u):
                side, r = m * rb // hs, m * rb % hs
                n = 2 * side + u
                rows = slice(j * hs + r, j * hs + r + rb)
                v = grads[rows, n * C : (n + 1) * C] if n < plan.T2 else pgrad[rows]
                return v.astype(F32)

            red.put(T1 + u, rows)
        red.step0(0)

    @when(1)
    def _():
        X5_copy(0).start()
        X5_copy(1).start()

    here_w, k = turn_of("w")

    @pl.when(here_w)
    def _():
        X5_copy(k).wait()
        y[0:Ch, 0:C] = mm(D0T[...], X5[lax.rem(k, 2)])

        @pl.when(k < T1 - 2)
        def _():
            X5_copy(k + 2).start()

        rb = plan.rb
        red.put(k, lambda j, m: y[j * cs + m * rb : j * cs + (m + 1) * rb, 0:C])

    @when(turn("x", nD - 1))
    def _():
        packet = link[0]
        packet[...] = jnp.zeros_like(packet)
        packet[0:1, 0:Ch] = jnp.sum(acc[0].T, axis=0, keepdims=True)
        packet[1:2, 0:Ch] = jnp.sum(acc[1].T, axis=0, keepdims=True)
        peers.start(link)

    go_on([e for e in table if not between(*e[:2])])

    @pl.when(here_x & (bx < nD - 1))
    def _():
        if nh == 2:
            send(bx * wb + wb // nh, wb // nh)

    @when(last)
    def _():
        if nh == 2:
            send(nw - wb // 2, wb // 2)

    @when(last)
    def _():
        red.step3(3)
        red.step4(1)
        red.step4(2)
        red.step3(4)
        red.step4(3)
        got = peers.finish(link)[:, 0:Ch]
        shift, gain = half_state[SHIFT1 : SHIFT1 + 1], half_state[GAIN1 : GAIN1 + 1]
        sums[0:1] = got[0:1]
        sums[1:2] = (got[1:2] - shift * got[0:1]) / gain
        red.step4(4)
        for b in range(5):
            red.step5(b)
        own = pltpu.make_async_copy(red.out, summed, X5_sems.at[0])
        own.start()
        for off in range(1, g):
            done = remote(
                part.at[off - 1],
                gz_got.at[off],
                bulk_sems.at[0, off],
                bulk_sems.at[1, off],
                member(off),
            )
            done.wait_recv()
            done.wait_send()
        own.wait()


def input_grad_kernel(plan, wg, lens, x, gz, gz_got, sums, res, res_got, summed,
                      state, half_state,
                      out, out_result, conv_grad, dil_grad, point_grad,
                      g1, b1, g2, b2, g3, b3, pb, eye, cols, xt):
    t = pl.program_id(0)
    s, z, i, h = plan.place()
    L, Ch, cs = plan.L, plan.Ch, plan.cs
    turn = plan.nw // wg
    mine = pl.ds(pl.multiple_of(i * cs, 16), cs)

    @pl.when(first_step())
    def _():
        n = 2.0 * total_of(lens)
        mean, rho = norm_of(half_state[ST1 : ST1 + 2], n)
        gr = half_state[GAIN1 : GAIN1 + 1] * rho
        gg = sums[1:2] / n * rho
        for k, row in enumerate((gr, -gr * gg, gr * (mean * gg - sums[0:1] / n))):
            xt[...] = column(row, L)
            cols[k] = xt[mine]
        eye[...] = eye_matrix(cs, Ch, i * cs)

        def mine_of(src, at, which, count, *dsts):
            n = dsts[0].shape[1]
            for k in range(count):

                @pl.when(which == k)
                def _():
                    for dst, r in zip(dsts, at):
                        dst[...] = src[r : r + 1, k * n : (k + 1) * n]

        mine_of(sums, (1, 0), i, plan.g, g1, b1)
        mine_of(state, (SU2 + 1, SU2), z, plan.nz, g2, b2)
        mine_of(state, (SU3 + 1, SU3), z, plan.nz, g3, b3)
        mine_of(state, (BSUM,), z, plan.nz, pb)

    own = lax.div(t, turn) == i
    for w in range(wg):
        out_result[w] = jnp.where(own, res[0, w], res_got[0, w])

    C, T1, hs, rb, wide = plan.C, plan.T1, plan.H // plan.nz, plan.rb, plan.C // 2
    count = plan.NW // wg
    turns = min(count, plan.chips)
    per, every = plan.chips // turns, count // turns

    def spread(chunk):
        for n in range(per):
            m = chunk * per + n
            side, r = m * rb // hs, m * rb % hs
            for c in range(2):
                at = slice(c * wide, (c + 1) * wide)
                for k in range(T1):
                    conv_grad[k, n * rb : (n + 1) * rb, at] = summed[k, c, n].astype(F32)
                for u in range(2):
                    v = summed[T1 + u, c, n].astype(F32)
                    if 2 * side + u < plan.T2:
                        dil_grad[2 * side + u, r : r + rb, at] = v
                    else:
                        point_grad[r : r + rb, at] = v

    for chunk in range(turns):
        pl.when(t == chunk * every)(partial(spread, chunk))

    lanes = lanes_of((cs, L))
    for w in range(wg):
        valid = 2 * lens[t * wg + w] - s * L
        v = mm_nt(eye[...], x[w])
        dz = jnp.where(own, gz[w], gz_got[0, w]).astype(F32)
        r = cols[0] * dz + v * cols[1] + cols[2]
        out[w] = jnp.where(lanes < valid, r, 0.0).astype(BF16)


def call(kernel, plan, name, steps, ins, outs, scratch, flops, nbytes, cid=None):
    extra = {} if cid is None else dict(collective_id=cid, has_side_effects=True)
    return pl.pallas_call(
        partial(kernel, plan),
        grid=(steps,),
        in_specs=[SMEM] + [spec for spec, _ in ins],
        out_specs=[spec for spec, _, _ in outs],
        out_shape=[jax.ShapeDtypeStruct(shape, dtype) for _, shape, dtype in outs],
        scratch_shapes=scratch,
        compiler_params=pltpu.CompilerParams(vmem_limit_bytes=VMEM_LIMIT, **extra),
        cost_estimate=pl.CostEstimate(
            flops=int(flops), bytes_accessed=int(nbytes), transcendentals=0
        ),
        name=name,
    )


def per_device(
    inputs,
    lengths,
    input_gain,
    input_shift,
    conv_weight,
    branch_gain,
    branch_shift,
    dilated_tap_weight,
    mixer_gain,
    mixer_shift,
    point_weight,
    point_bias,
    cotangent,
):
    NW, L, C = inputs.shape
    Lp = L // 2
    nz = lax.axis_size("ch")
    R = 2
    plan = Plan(
        ns=lax.axis_size("seq"),
        nz=nz,
        R=R,
        NW=NW,
        L=L,
        C=C,
        H=mixer_gain.shape[0] * nz,
        T1=conv_weight.shape[0],
        T2=dilated_tap_weight.shape[0],
        wb=min(NW * R // nz, max(1, 512 // Lp)),
    )
    g, nw, cs, Ch, H, Hh, wb = plan.g, plan.nw, plan.cs, plan.Ch, plan.H, plan.Hh, plan.wb
    T1, T2, steps = plan.T1, plan.T2, plan.steps
    M = wb * Lp
    hs = H // nz
    lens = lengths.astype(jnp.int32)

    def row(a):
        return a.reshape(1, a.shape[0])

    def grp():
        return lax.rem(lax.axis_index("ch"), g)

    def half():
        return lax.div(lax.axis_index("ch"), g)

    def core():
        return lax.rem(lax.axis_index("seq"), 2)

    def chip4():
        return lax.div(lax.axis_index("seq"), plan.ns // 4)

    def whole(*shape):
        return pl.BlockSpec(shape, lambda t: (0,) * len(shape), pipeline_mode=pl.Buffered(1))

    def const(*shape):
        return pl.BlockSpec(shape, lambda t: (0,) * len(shape))

    def win(*shape):
        return pl.BlockSpec(shape, lambda t: (t,) + (0,) * (len(shape) - 1))

    def arg_win(n, width):
        return pl.BlockSpec((wb, n, width), lambda t: (grp() * steps + t, 0, 0))

    def ins(*pairs):
        return [p for p in pairs]

    share = NW // nz
    nm = max(1, share // wb)

    def edge_spec(n):
        return pl.BlockSpec(
            (nw, 16, C), lambda t: (grp(), n, 0), pipeline_mode=pl.Buffered(1)
        )

    def head_block(t):
        own = lax.div(lax.axis_index("ch") * share, wb) + t
        return jnp.where(t < nm, own, grp() * steps + t - nm), 0, 0

    def after(*shape):
        return pl.BlockSpec(
            shape, lambda t: (jnp.maximum(t - nm, 0),) + (0,) * (len(shape) - 1)
        )

    pairs = ins(
        (pl.BlockSpec((wb, L, C), head_block), inputs),
        (edge_spec(0), inputs),
        (edge_spec(L // 16 - 1), inputs),
        (edge_spec(0), cotangent),
        (edge_spec(Lp // 16 - 1), cotangent),
        (whole(1, cs), row(branch_gain)),
        (whole(1, cs), row(branch_shift)),
        (whole(1, cs), row(point_bias)),
        (whole(1, H // nz), row(mixer_gain)),
        (whole(1, H // nz), row(mixer_shift)),
        (ANY, conv_weight.reshape(T1 * C, C)),
        (whole(C), input_gain),
        (whole(C), input_shift),
        (
            pl.BlockSpec(
                (1, hs, C // 2),
                lambda t: (jnp.minimum(chip4(), T2 - 1), 0, core()),
                pipeline_mode=pl.Buffered(1),
            ),
            jnp.swapaxes(dilated_tap_weight, 1, 2),
        ),
        (
            pl.BlockSpec(
                (hs, C // 2), lambda t: (0, core()), pipeline_mode=pl.Buffered(1)
            ),
            point_weight,
        ),
    )
    plane, line, group = plane_peers(plan), line_peers(plan), group_peers(plan)
    state_shape = (STATE, C)
    edges2, edges3 = (2, nw, EDGE, C), (2, nw, EDGE, H)
    X5, x2, land2, state, beyond, full = call(
        lambda plan, *refs: head_kernel(plan, nm, *refs),
        plan,
        "head",
        nm + steps,
        pairs,
        [
            (
                pl.BlockSpec((T1, M, C), lambda t: (0, jnp.maximum(t - nm, 0), 0)),
                (T1, nw * Lp, C),
                BF16,
            ),
            (after(wb, Lp, C), (nw, Lp, C), F32),
            (ANY, edges2, BF16),
            (const(*state_shape), state_shape, F32),
            (const(2, 3, nw, C), (2, 3, nw, C), F32),
            (ANY, (2, T2 + 1, nz, hs, C // 2), BF16),
        ],
        [
            pltpu.VMEM((2, 8, C), F32),
            pltpu.VMEM((2, 3, nw, C), F32),
            pltpu.VMEM((2, 3, nw, C), F32),
            pltpu.VMEM((L, L), BF16),
            pltpu.VMEM(edges2, BF16),
            pltpu.VMEM((2, C), F32),
            pltpu.VMEM((T1 * C, C), BF16),
            pltpu.SemaphoreType.DMA,
            pltpu.VMEM((hs, C // 2), BF16),
            pltpu.SemaphoreType.DMA((2, 4)),
            HALO_SEMS,
            HALO_SEMS,
        ]
        + plane.scratch(2, C)
        + line.scratch(3, C)
        + group.scratch(2, C),
        2 * nw * Lp * T1 * C * C,
        nw * Lp * C * 20,
        cid=1,
    )(lens, *[a for _, a in pairs])

    taps_spec = whole(2, T2, nz, hs, C // 2)
    pw_spec = pl.BlockSpec(
        (2, 1, nz, hs, C // 2), lambda t: (0, T2, 0, 0, 0), pipeline_mode=pl.Buffered(1)
    )

    def early(*shape):
        return pl.BlockSpec(
            shape, lambda t: (jnp.minimum(t, steps - 1),) + (0,) * (len(shape) - 1)
        )

    def early_land(width):
        return pl.BlockSpec(
            (2, wb, EDGE, width), lambda t: (0, jnp.minimum(t, steps - 1), 0, 0)
        )

    def half_of(n):
        return pl.BlockSpec((n, Ch), lambda t: (0, half()), pipeline_mode=pl.Buffered(1))

    cot_spec = pl.BlockSpec(
        (wb, Lp, C), lambda t: (grp() * steps + jnp.minimum(t, steps - 1), 0, 0)
    )

    p0, r0, b0, g0, block_steps = block_phases(plan)

    def at_phase(first):
        return lambda t: jnp.clip(t - first, 0, steps - 1)

    in_p, in_b = at_phase(p0), at_phase(b0)
    pairs = ins(
        (
            pl.BlockSpec(
                (wb, Lp, C),
                lambda t: (jnp.where(t < p0 + steps, jnp.minimum(t, steps - 1), in_b(t)), 0, 0),
            ),
            x2,
        ),
        (ANY, x2),
        (early_land(C), land2),
        (pl.BlockSpec((wb, Lp, C), lambda t: (grp() * steps + in_p(t), 0, 0)), cotangent),
        (taps_spec, full),
        (pw_spec, full),
        (whole(T2, hs, C), jnp.swapaxes(dilated_tap_weight, 1, 2)),
        (whole(hs, C), point_weight),
        (whole(*state_shape), state),
        (half_of(STATE), state),
    )
    dz2, grads, pgrad, res, dland2, state, res_got = call(
        block_kernel,
        plan,
        "block",
        block_steps,
        pairs,
        [
            (pl.BlockSpec((wb, Lp, C), lambda t: (in_b(t), 0, 0)), (nw, Lp, C), F32),
            (const(Hh, T2 * C), (Hh, T2 * C), BF16),
            (const(Hh, C), (Hh, C), BF16),
            (const(g, nw, cs, Lp), (g, nw, cs, Lp), BF16),
            (ANY, (2, nw, C), F32),
            (const(*state_shape), state_shape, F32),
            (ANY, (g, nw, cs, Lp), BF16),
        ],
        [
            pltpu.VMEM((wb, Lp + 2 * EDGE, C), F32),
            pltpu.VMEM((H, T2 * C), BF16),
            pltpu.VMEM((T2 * H, C), BF16),
            pltpu.VMEM((H, C), BF16),
            pltpu.VMEM((nw * Lp, T2 * C), BF16),
            pltpu.VMEM((nw, Lp, H), F32),
            pltpu.VMEM((nw, Lp, H), F32),
            pltpu.VMEM((M, H), F32),
            pltpu.VMEM((nw * Lp, H), BF16),
            pltpu.VMEM((H, nw * Lp), BF16),
            pltpu.VMEM((nw * Lp, C), BF16),
            pltpu.VMEM((M, T2 * H), BF16),
            pltpu.VMEM((H, nw * Lp), BF16),
            pltpu.VMEM(edges3, BF16),
            pltpu.VMEM(edges3, BF16),
            pltpu.VMEM((1, 2 * H), F32),
            pltpu.VMEM(edges3, BF16),
            pltpu.VMEM(edges3, BF16),
            pltpu.VMEM((2, C), F32),
            pltpu.VMEM((2, nw, C), F32),
            pltpu.VMEM((2, C), F32),
            pltpu.SemaphoreType.DMA((3, 2, 2)),
            pltpu.SemaphoreType.DMA((2, g)),
            pltpu.VMEM((nw, Lp, Ch), F32),
            pltpu.SemaphoreType.DMA,
        ]
        + group.scratch(1, 2 * H)
        + group.scratch(2, C)
        + group.scratch(2, C),
        nw * Lp * C * H * (6 * T2 + 6),
        nw * Lp * C * 30,
        cid=3,
    )(lens, *[a for _, a in pairs])

    chips, rb = plan.chips, plan.rb
    turns_t = tail_turns(plan)

    def x_block(t):
        block = jnp.int32(0)
        for n, (what, k) in enumerate(turns_t):
            if what == "x":
                block = jnp.where(t >= n, k, block)
        return block

    sshape = (T1 + 2, 2, chips, rb, C // 2)
    pairs = ins(
        (early(wb, Lp, C), dz2),
        (whole(2, nw, C), dland2),
        (early(wb, Lp, C), x2),
        (early_land(C), land2),
        (cot_spec, cotangent),
        (whole(2, 3, nw, C), beyond),
        (
            pl.BlockSpec(
                (wb, L, Ch), lambda t: (grp() * steps + x_block(t), 0, half())
            ),
            inputs,
        ),
        (ANY, X5),
        (ANY, conv_weight),
        (whole(Hh, T2 * C), grads),
        (whole(Hh, C), pgrad),
        (whole(*state_shape), state),
        (half_of(STATE), state),
    )
    gz, gz_got, sums1, summed = call(
        tail_kernel,
        plan,
        "tail",
        len(turns_t),
        pairs,
        [
            (pl.BlockSpec((wb, cs, L), lambda t: (x_block(t), 0, 0)), (nw, cs, L), BF16),
            (ANY, (g, nw, cs, L), BF16),
            (const(2, Ch), (2, Ch), F32),
            (ANY, sshape, BF16),
        ],
        [
            pltpu.VMEM((wb, Lp + 16, C), F32),
            pltpu.VMEM((steps, M, 3 * C), BF16),
            pltpu.VMEM((Ch, nw * Lp), BF16),
            pltpu.VMEM((2 * Ch, 3 * C), BF16),
            pltpu.VMEM((L, L), BF16),
            pltpu.VMEM((Ch, Ch), BF16),
            pltpu.VMEM((2, Ch, L), F32),
            pltpu.VMEM((2 * Ch, max(M, C)), F32),
            pltpu.VMEM((g - 1, nw, cs, L), BF16),
            pltpu.VMEM((2, Ch, L), BF16),
            pltpu.VMEM((2, Ch, min(L, 128)), F32),
            pltpu.VMEM((2, nw * Lp, C), BF16),
            pltpu.SemaphoreType.DMA((3,)),
            pltpu.VMEM((T1, Ch, C), BF16),
            pltpu.SemaphoreType.DMA((2, g)),
        ]
        + Reduction.scratch(plan, tail_batches(plan))
        + group.scratch(2, C),
        2 * nw * Lp * (6 + T1) * C * Ch,
        nw * Lp * C * 40,
        cid=6,
    )(lens, *[a for _, a in pairs])

    wg = min(2 * wb, nw)
    count = NW // wg
    turn = nw // wg
    turns = min(count, chips)

    def own_block(t):
        return jnp.where(lax.div(t, turn) == grp(), lax.rem(t, turn), 0)

    def got_slot(t):
        off = lax.rem(grp() - lax.div(t, turn) + g, g)
        return jnp.maximum(off, 1), jnp.where(off > 0, lax.rem(t, turn), 0)

    pairs = ins(
        (pl.BlockSpec((wg, L, Ch), lambda t: (t, 0, half())), inputs),
        (pl.BlockSpec((wg, cs, L), lambda t: (own_block(t), 0, 0)), gz),
        (pl.BlockSpec((1, wg, cs, L), lambda t: got_slot(t) + (0, 0)), gz_got),
        (whole(2, Ch), sums1),
        (pl.BlockSpec((1, wg, cs, Lp), lambda t: (grp(), own_block(t), 0, 0)), res),
        (pl.BlockSpec((1, wg, cs, Lp), lambda t: got_slot(t) + (0, 0)), res_got),
        (
            pl.BlockSpec(
                (T1 + 2, 2, chips // turns, rb, C // 2),
                lambda t: (0, 0, t * turns // count, 0, 0),
            ),
            summed,
        ),
        (whole(*state_shape), state),
        (half_of(STATE), state),
    )
    outs = call(
        lambda plan, *refs: input_grad_kernel(plan, wg, *refs),
        plan,
        "input_grad",
        count,
        pairs,
        [
            (win(wg, cs, L), (NW, cs, L), BF16),
            (win(wg, cs, Lp), (NW, cs, Lp), BF16),
            (
                pl.BlockSpec((T1, cs // turns, C), lambda t: (0, t * turns // count, 0)),
                (T1, cs, C),
                F32,
            ),
            (const(T2, hs, C), (T2, hs, C), F32),
            (const(hs, C), (hs, C), F32),
        ]
        + [(const(1, n), (1, n), F32) for n in (cs, cs, cs, cs, hs, hs, cs)],
        [
            pltpu.VMEM((cs, Ch), BF16),
            pltpu.VMEM((3, cs, L), F32),
            pltpu.VMEM((Ch, L), F32),
        ],
        2 * NW * L * Ch * cs,
        NW * L * cs * 8,
    )(lens, *[a for _, a in pairs])
    grad, result, conv_grad, dil_grad, point_grad = outs[:5]
    g1, b1, g2, b2, g3, b3, pb = [a[0] for a in outs[5:]]
    return (
        jnp.swapaxes(result, 1, 2),
        jnp.swapaxes(grad, 1, 2),
        jnp.swapaxes(conv_grad, 1, 2),
        g1,
        b1,
        g2,
        b2,
        jnp.swapaxes(dil_grad, 1, 2),
        g3,
        b3,
        point_grad,
        pb,
    )


def solution(mesh):
    in_specs = (
        P(None, "seq", None),
        P(),
        P(),
        P(),
        P(),
        P("ch"),
        P("ch"),
        P(None, None, "ch"),
        P("ch"),
        P("ch"),
        P("ch", None),
        P("ch"),
        P(None, "seq", None),
    )
    out_specs = (
        P(None, "seq", "ch"),
        P(None, "seq", "ch"),
        P(None, None, "ch"),
        P("ch"),
        P("ch"),
        P("ch"),
        P("ch"),
        P(None, None, "ch"),
        P("ch"),
        P("ch"),
        P("ch", None),
        P("ch"),
    )
    return jax.shard_map(
        per_device, mesh=mesh, in_specs=in_specs, out_specs=out_specs, check_vma=False
    )
```

```python
from functools import partial
from typing import NamedTuple

import jax
import jax.numpy as jnp
from jax import lax
from jax.experimental import pallas as pl
from jax.experimental.pallas import tpu as pltpu
from jax.sharding import PartitionSpec as P

DIL = 14
EDGE = 16
EPS = 1e-05
GC0 = 0.7978845608028654
GC1 = 0.044715
F32 = jnp.float32
BF16 = jnp.bfloat16
MESH = pl.DeviceIdType.MESH
VMEM_LIMIT = 58 * 1024 * 1024
ANY = pl.BlockSpec(memory_space=pl.ANY)
SMEM = pl.BlockSpec(memory_space=pltpu.SMEM)


ST1, GAIN2, SHIFT2, BIAS, GAIN3, SHIFT3, GAIN1, SHIFT1, ST2, ST3, SU3, BSUM, SU2 = (
    0, 2, 3, 4, 5, 6, 7, 8, 9, 11, 13, 15, 16
)
STATE = 24


class Plan(NamedTuple):
    ns: int
    nz: int
    R: int
    NW: int
    L: int
    C: int
    H: int
    T1: int
    T2: int
    wb: int

    @property
    def g(self):
        return self.nz // self.R

    @property
    def nw(self):
        return self.NW // self.g

    @property
    def Lp(self):
        return self.L // 2

    @property
    def cs(self):
        return self.C // self.nz

    @property
    def Ch(self):
        return self.C // self.R

    @property
    def Hh(self):
        return self.H // self.R

    @property
    def steps(self):
        return self.nw // self.wb

    @property
    def chips(self):
        return self.ns // 2

    @property
    def rb(self):
        return self.cs // self.chips

    def place(self):
        s, z = lax.axis_index("seq"), lax.axis_index("ch")
        return s, z, lax.rem(z, self.g), lax.div(z, self.g)


def gelu(z):
    t = jnp.tanh(z * (GC0 + (GC0 * GC1) * (z * z)))
    return z * (0.5 + 0.5 * t)


def gelu_both(z):
    sq = z * z
    t = jnp.tanh(z * (GC0 + (GC0 * GC1) * sq))
    h = 0.5 + 0.5 * t
    v = z * h
    return v, h + v * (1.0 - t) * (GC0 + (3.0 * GC0 * GC1) * sq)


def gelu_slope(z):
    return gelu_both(z)[1]


def fold(v):
    return jnp.sum(v.reshape(v.shape[0] // 8, 8, v.shape[1]), axis=0)


def fold_lanes(v):
    out = v[:, 0:128]
    for k in range(128, v.shape[1], 128):
        out = out + v[:, k : k + 128]
    return out


def unfold(v):
    return jnp.sum(v, axis=0, keepdims=True)


def rows_of(shape):
    return lax.broadcasted_iota(jnp.int32, shape, 0)


def lanes_of(shape):
    return lax.broadcasted_iota(jnp.int32, shape, 1)


def total_of(lens):
    n = lens[0]
    for k in range(1, lens.shape[0]):
        n = n + lens[k]
    return n.astype(F32)


def norm_of(stats, total):
    mean = stats[0:1] / total
    square = stats[1:2] / total
    return mean, lax.rsqrt(square - mean * mean + EPS)


def flat(ref):
    return ref[...].reshape(1, ref.shape[0])


def column(row, n):
    return jnp.broadcast_to(row, (n, row.shape[1])).T


def mm(a, b):
    return jnp.dot(a, b, preferred_element_type=F32)


def mm_nt(a, b):
    return lax.dot_general(a, b, (((1,), (1,)), ((), ())), preferred_element_type=F32)


def mm_tn(a, b):
    return lax.dot_general(a, b, (((0,), (0,)), ((), ())), preferred_element_type=F32)


def mm_tt(a, b):
    return lax.dot_general(a, b, (((0,), (1,)), ((), ())), preferred_element_type=F32)


def eye_matrix(n, m, first):
    return jnp.where(lanes_of((n, m)) == rows_of((n, m)) + first, 1.0, 0.0).astype(BF16)


def pick_matrix(L):
    r, n = rows_of((L, L)), lanes_of((L, L))
    bin_of = 2 * r - jnp.where(r >= L // 2, L - 1, 0)
    return jnp.where(n == bin_of, 1.0, 0.0).astype(BF16)


def remote(src, dst, send, recv, device):
    return pltpu.make_async_remote_copy(
        src_ref=src,
        dst_ref=dst,
        send_sem=send,
        recv_sem=recv,
        device_id=device,
        device_id_type=MESH,
    )


def wrap(v, n):
    return jnp.where(v >= n, v - n, v)


def greet(devices):
    barrier = pltpu.get_barrier_semaphore()
    for device in devices:
        pl.semaphore_signal(barrier, inc=1, device_id=device, device_id_type=MESH)


def meet(devices):
    pl.semaphore_wait(pltpu.get_barrier_semaphore(), len(devices))


class Peers:
    def __init__(self, me, others):
        self.me, self.others = me, others
        self.count = len(others) + 1

    def start(self, link):
        packet, buf, sems = link
        for device in self.others:
            remote(packet, buf.at[self.me], sems.at[0], sems.at[1], device).start()

    def finish(self, link):
        packet, buf, sems = link
        buf[self.me] = packet[...]
        rest = buf.at[pl.ds(0, self.count - 1)]
        done = remote(rest, rest, sems.at[0], sems.at[1], self.others[0])
        done.wait_recv()
        acc = buf[0]
        for q in range(1, self.count):
            acc = acc + buf[q]
        done.wait_send()
        return acc

    def scratch(self, rows, width):
        return [
            pltpu.VMEM((rows, width), F32),
            pltpu.VMEM((self.count, rows, width), F32),
            pltpu.SemaphoreType.DMA((2,)),
        ]


def group_peers(plan):
    s, z, i, h = plan.place()
    g = plan.g
    others = [
        (wrap(s + a, plan.ns), h * g + wrap(i + b, g))
        for a in range(plan.ns)
        for b in range(g)
        if a or b
    ]
    return Peers(s * g + i, others)


def plane_peers(plan):
    s, z, i, h = plan.place()
    return Peers(s, [(wrap(s + a, plan.ns), z) for a in range(1, plan.ns)])


def line_peers(plan):
    s, z, i, h = plan.place()
    return Peers(z, [(s, wrap(z + a, plan.nz)) for a in range(1, plan.nz)])


class Halo:
    def __init__(self, plan, edge, land, sems):
        self.edge, self.land, self.sems = edge, land, sems
        s, z, _, _ = plan.place()
        self.to = ((wrap(s + plan.ns - 1, plan.ns), z), (wrap(s + 1, plan.ns), z))

    def copy(self, side, rows):
        return remote(
            self.edge.at[side, rows],
            self.land.at[1 - side, rows],
            self.sems.at[0, side],
            self.sems.at[1, side],
            self.to[side],
        )

    def start(self, first, count):
        for side in range(2):
            self.copy(side, pl.ds(first, count)).start()

    def finish(self):
        for side in range(2):
            done = self.copy(side, pl.ds(0, self.land.shape[1]))
            done.wait_recv()
            done.wait_send()


HALO_SEMS = pltpu.SemaphoreType.DMA((2, 2))


class Gather:
    def __init__(self, plan, part, full, sems):
        self.plan, self.part, self.full, self.sems = plan, part, full, sems
        self.s, self.z, self.i, self.h = plan.place()
        self.c, self.m = lax.rem(self.s, 2), lax.div(self.s, 2)
        self.chips = plan.chips
        self.every = self.chips // 4
        self.tap = lax.div(self.m, self.every)
        self.owner = lax.rem(self.m, self.every) == 0
        self.mine = full.at[self.c, self.tap]

    def others(self):
        g, nz = self.plan.g, self.plan.nz
        return [(self.s, wrap(self.h * g + g + r, nz)) for r in range(nz - g)]

    def far(self, off):
        return (2 * wrap(self.m + off, self.chips) + self.c, self.z)

    def line(self, off):
        nz = self.plan.nz
        device = (self.s, wrap(self.z + off, nz))
        dst = self.mine.at[nz - off]
        return remote(self.part, dst, self.sems.at[0, 1], self.sems.at[1, 1], device)

    def far_rows(self, taps):
        return self.full.at[self.c, taps, pl.ds(1, self.plan.nz - 1)]

    def chip(self, off):
        rows = self.far_rows(self.tap)
        return remote(rows, rows, self.sems.at[0, 2], self.sems.at[1, 2], self.far(off))

    def pair(self):
        half = self.far_rows(pl.ds(0, 4))
        device = (2 * self.m + 1 - self.c, self.z)
        return remote(half, half, self.sems.at[0, 3], self.sems.at[1, 3], device)

    def line_start(self):
        @pl.when(self.owner)
        def _():
            for off in range(1, self.plan.nz):
                self.line(off).start()

    def line_finish(self):
        @pl.when(self.owner)
        def _():
            rest = self.far_rows(self.tap)
            device = (self.s, wrap(self.z + 1, self.plan.nz))
            done = remote(rest, rest, self.sems.at[0, 1], self.sems.at[1, 1], device)
            done.wait_recv()
            done.wait_send()

    def chips_start(self):
        @pl.when(self.owner)
        def _():
            for off in range(1, self.chips):
                self.chip(off).start()

    def pair_start(self):
        def taken(count):
            rest = self.far_rows(pl.ds(0, count))
            return remote(rest, rest, self.sems.at[0, 2], self.sems.at[1, 2], self.far(1))

        @pl.when(self.owner)
        def _():
            taken(3).wait_recv()
            for off in range(1, self.chips):
                self.chip(off).wait_send()

        if self.every > 1:

            @pl.when(jnp.logical_not(self.owner))
            def _():
                taken(4).wait_recv()

        self.pair().start()

    def pair_finish(self):
        done = self.pair()
        done.wait_recv()
        done.wait_send()


def first_step():
    return pl.program_id(0) == 0


def last_step():
    return pl.program_id(0) == pl.num_programs(0) - 1


def head_kernel(plan, nm, lens, x, xtop, xend, ctop, cend, g2, s2, pb, g3, s3,
                w_hbm, gain, shift, taps, pw,
                X5, x2, land, state, beyond_out, full,
                macc, beyond, xedge, sel, edge, acc, w_ref, w_sem, part,
                gather_sems, xhalo_sems, halo_sems, *links):
    t = pl.program_id(0)
    peers, plane, line = group_peers(plan), plane_peers(plan), line_peers(plan)
    xhalo = Halo(plan, xedge, beyond, xhalo_sems)
    halo = Halo(plan, edge, land, halo_sems)
    gather = Gather(plan, part, full, gather_sems)
    w_copy = pltpu.make_async_copy(w_hbm, w_ref, w_sem)
    plane_link, line_link, link = links[:3], links[3:6], links[6:]
    s, z, i, h = plan.place()
    L, Lp, C, nw, nz, wb = plan.L, plan.Lp, plan.C, plan.nw, plan.nz, plan.wb
    share = plan.NW // nz
    c = t - nm
    everyone = peers.others + gather.others()

    @pl.when(first_step())
    def _():
        w_copy.start()
        greet(everyone)
        part[...] = jnp.where(gather.tap == 3, pw[...], taps[0])
        macc[...] = jnp.zeros_like(macc)
        acc[...] = jnp.zeros_like(acc)
        state[...] = jnp.zeros_like(state)
        state[GAIN1 : GAIN1 + 1] = flat(gain)
        state[SHIFT1 : SHIFT1 + 1] = flat(shift)
        n16 = nw * 16
        for side, (xe, ce, places) in enumerate(
            ((xtop, ctop, (0, 1, 0)), (xend, cend, (14, 15, 15)))
        ):
            for k, at in enumerate(places):
                rows, lanes = rows_of((nw, n16)), lanes_of((nw, n16))
                one = jnp.where(lanes == 16 * rows + at, 1.0, 0.0).astype(BF16)
                block = (xe if k < 2 else ce)[...].reshape(n16, C)
                xedge[side, k] = mm(one, block)
        shape = (Lp, L)
        for odd in range(2):
            at = lanes_of(shape) - (2 * rows_of(shape) + odd)
            one = jnp.where((at == 0) | (at == 1), 1.0, 0.0)
            sel[odd * Lp : (odd + 1) * Lp] = one.astype(BF16)

    @pl.when(c < 0)
    def _():
        rows = rows_of((L, C))
        for w in range(min(share, wb)):
            at = lax.rem(z * share, wb) + w
            valid = 2 * lens[z * share + t * wb + w] - s * L
            v = jnp.where(rows < valid, x[at].astype(F32), 0.0)
            macc[0] += fold(v)
            macc[1] += fold(v * v)

    @pl.when(c == -1)
    def _():
        packet, more = plane_link[0], line_link[0]
        packet[0:1] = unfold(macc[0])
        packet[1:2] = unfold(macc[1])
        meet(everyone)
        plane.start(plane_link)
        xhalo.start(0, 3)
        at = 0
        spans = []
        more[2:3] = jnp.zeros((1, C), F32)
        for ref in (g2, s2, pb, g3, s3):
            n = ref.shape[1]
            more[2:3, at : at + n] = ref[...]
            spans.append((at, n))
            at += n
        more[0:2] = plane.finish(plane_link)
        line.start(line_link)
        gather.line_start()
        state[ST1 : ST1 + 2] = line.finish(line_link)[0:2]
        for k in range(nz):
            row = line_link[1][k]
            for r, (at, n) in zip((GAIN2, SHIFT2, BIAS, GAIN3, SHIFT3), spans):
                state[r : r + 1, k * n : (k + 1) * n] = row[2:3, at : at + n]
        xhalo.finish()
        beyond_out[...] = beyond[...]
        w_copy.wait()

    @pl.when(c >= 0)
    def _():
        mean, rho = norm_of(state[ST1 : ST1 + 2], 2.0 * total_of(lens))
        scale = state[GAIN1 : GAIN1 + 1] * rho
        offset = state[SHIFT1 : SHIFT1 + 1] - mean * scale
        rows = rows_of((L, C))
        row1 = rows_of((1, C))
        row16 = rows_of((16, C))
        def activate(w):
            at = c * wb + w
            valid = 2 * lens[i * nw + at] - s * L
            a = gelu(x[w].astype(F32) * scale + offset)
            a = jnp.where(rows < valid, a, 0.0).astype(BF16)
            picked = mm(sel[...], a)
            even, odd = picked[0:Lp], picked[Lp:]
            top, end = w * Lp, (w + 1) * Lp
            before = [pltpu.roll(v, 1, 0) for v in (even, odd)]
            behind = pltpu.roll(even, Lp - 1, 0)
            for k, v in enumerate((*before, even, odd, behind)):
                X5[k, top:end] = v.astype(BF16)

            def beside(side, k, bin_at):
                a = gelu(beyond[side, k, pl.ds(at, 1), :] * scale + offset)
                here = (row1 + bin_at < valid) & (row1 + (s * L + bin_at) >= 0)
                return jnp.where(here, a, 0.0).astype(BF16).astype(F32)

            l0, l1 = beside(0, 0, -2), beside(0, 1, -1)
            r0, r1 = beside(1, 0, L), beside(1, 1, L + 1)
            start = a[0:1].astype(F32)
            for k, row in ((0, l0 + l1), (1, l1 + start)):
                X5[k, top : top + 16] = jnp.where(row16 == 0, row, before[k][0:16]).astype(BF16)
            X5[3, end - 16 : end] = (
                odd[Lp - 16 :] + jnp.where(row16 == 15, r0, 0.0)
            ).astype(BF16)
            X5[4, end - 16 : end] = jnp.where(row16 == 15, r0 + r1, behind[Lp - 16 :]).astype(BF16)

        nc = 256
        rowp = rows_of((Lp, nc))

        def convolve(first, count):
            span = slice(first * Lp, (first + count) * Lp)
            for n in range(C // nc):
                cols = slice(n * nc, (n + 1) * nc)
                taps = [X5[k, span] for k in range(plan.T1)]
                y = 0.5 * mm(jnp.concatenate(taps, axis=1), w_ref[:, cols])
                s0 = jnp.zeros((8, nc), F32)
                s1 = jnp.zeros((8, nc), F32)
                for w in range(first, first + count):
                    at = c * wb + w
                    valid = lens[i * nw + at] - s * Lp
                    v = y[(w - first) * Lp : (w - first + 1) * Lp]
                    x2[w, :, cols] = v
                    edge[0, at, :, cols] = v[:EDGE].astype(BF16)
                    edge[1, at, :, cols] = v[Lp - EDGE :].astype(BF16)
                    v = jnp.where(rowp < valid, v, 0.0)
                    s0 = s0 + fold(v)
                    s1 = s1 + fold(v * v)
                acc[0:1, cols] += unfold(s0)
                acc[1:2, cols] += unfold(s1)

        count = max(1, wb // 2)
        for first in range(0, wb, count):
            for w in range(first, first + count):
                activate(w)
            convolve(first, count)
        halo.start(c * wb, wb)

    @pl.when(c == 0)
    def _():
        gather.line_finish()
        gather.chips_start()

    @pl.when(last_step())
    def _():
        link[0][...] = acc[...]
        peers.start(link)
        gather.pair_start()
        state[ST2 : ST2 + 2] = peers.finish(link)
        halo.finish()
        gather.pair_finish()


def block_kernel(plan, lens, x2, x2_hbm, x2land, cot, w_ref, pw_ref, own_w, own_pw, old, half_state,
                 dz2, grads, pgrad, res, land, state, res_got,
                 ext, wf, wt, pw, Y3, c2, dz3, das, a3s, a3T, dos, Z3, dcT,
                 cedge, cland, cacc, dedge, dland, dacc, bedge, bacc, halo_sems, bulk_sems,
                 x2half, x2_sem, eye, *links):
    t = pl.program_id(0)
    peers = group_peers(plan)
    s, z, i, h = plan.place()
    Lp, C, H, wb, nw, cs, g = plan.Lp, plan.C, plan.H, plan.wb, plan.nw, plan.cs, plan.g
    M = wb * Lp
    steps = plan.steps
    p0, r0, b0, g0 = block_phases(plan)[:4]
    c_link, d_link, b_link = links[:3], links[3:6], links[6:]
    c_halo = Halo(plan, cedge, cland, halo_sems.at[0])
    d_halo = Halo(plan, dedge, dland, halo_sems.at[1])
    b_halo = Halo(plan, bedge, land, halo_sems.at[2])

    def flip(v):
        return mm_nt(eye[...], v).astype(BF16)

    def bulk(off, rows):
        to = wrap(i + off, g)
        return remote(
            res.at[to, rows],
            res_got.at[off, rows],
            bulk_sems.at[0, off],
            bulk_sems.at[1, off],
            (s, h * g + to),
        )

    def result_of(block):
        y = mm(a3s[pl.ds(pl.multiple_of(block * M, 128), M)], pw[:, pl.ds(pl.multiple_of(h * plan.Ch, 128), plan.Ch)])
        rowr = rows_of((Lp, y.shape[1]))
        for w in range(wb):
            at = block * wb + w
            valid = lens[i * plan.nw + at] - s * Lp
            r = x2half[at] + y[w * Lp : (w + 1) * Lp] + half_state[BIAS : BIAS + 1]
            r = flip(jnp.where(rowr < valid, r, 0.0).astype(BF16))
            for k in range(g):
                res[k, at] = r[k * cs : (k + 1) * cs]

    def send_result(block):
        result_of(block)
        for off in range(1, g):
            bulk(off, pl.ds(block * wb, wb)).start()

    half_copy = pltpu.make_async_copy(
        x2_hbm.at[:, :, pl.ds(pl.multiple_of(h * plan.Ch, 128), plan.Ch)], x2half, x2_sem
    )

    @pl.when(first_step())
    def _():
        half_copy.start()
        greet(peers.others)
        state[...] = old[...]
        eye[...] = eye_matrix(H, H, 0)
        cacc[...] = jnp.zeros_like(cacc)
        dacc[...] = jnp.zeros_like(dacc)
        bacc[...] = jnp.zeros_like(bacc)
        hs = H // plan.nz

        def rows_at(which, first=0):
            return pl.ds(pl.multiple_of(first + which * hs, 16), hs)

        for r in range(plan.nz):
            at = wrap(z + r, plan.nz)
            for c in range(2):
                cols = slice(c * (C // 2), (c + 1) * (C // 2))
                pw[rows_at(at), cols] = own_pw[:, cols] if r == 0 else pw_ref[c, 0, r]
                for k in range(plan.T2):
                    v = own_w[k, :, cols] if r == 0 else w_ref[c, k, r]
                    wf[rows_at(at), k * C + cols.start : k * C + cols.stop] = v
                    wt[rows_at(at, k * H), cols] = v

    @pl.when(t < p0)
    def _():
        base = pl.multiple_of(t * M, 128)
        mean, rho = norm_of(state[ST2 : ST2 + 2], total_of(lens))
        scale = state[GAIN2 : GAIN2 + 1] * rho
        offset = state[SHIFT2 : SHIFT2 + 1] - mean * scale
        rows = rows_of((Lp, C))
        rowe = rows_of((EDGE, C))

        rowh = rows_of((Lp, H))
        sums0, sums1 = jnp.zeros((8, H), F32), jnp.zeros((8, H), F32)
        nh = min(2, wb)
        for first in range(0, wb, wb // nh):
            span = range(first, first + wb // nh)
            for w in span:
                valid = lens[i * plan.nw + t * wb + w] - s * Lp
                a = jnp.where(rows < valid, gelu(x2[w] * scale + offset), 0.0)
                al = gelu(x2land[0, w].astype(F32) * scale + offset)
                al = jnp.where((rowe - EDGE < valid) & (s > 0), al, 0.0)
                ah = gelu(x2land[1, w].astype(F32) * scale + offset)
                ah = jnp.where(rowe + Lp < valid, ah, 0.0)
                ext[w, 0:EDGE] = al
                ext[w, EDGE : EDGE + Lp] = a
                ext[w, EDGE + Lp :] = ah
                top, end = w * Lp, (w + 1) * Lp
                Y3[pl.ds(base + top, Lp), 0:C] = ext[w, EDGE - DIL : EDGE - DIL + Lp].astype(BF16)
                Y3[pl.ds(base + top, Lp), C : 2 * C] = a.astype(BF16)
                Y3[pl.ds(base + top, Lp), 2 * C : 3 * C] = ext[w, EDGE + DIL : EDGE + DIL + Lp].astype(BF16)
            y = mm_nt(Y3[pl.ds(base + first * Lp, wb // nh * Lp)], wf[...])
            for w in span:
                at = t * wb + w
                valid = lens[i * plan.nw + at] - s * Lp
                v = y[(w - first) * Lp : (w - first + 1) * Lp]
                c2[at] = v
                cedge[0, at] = v[:EDGE].astype(BF16)
                cedge[1, at] = v[Lp - EDGE :].astype(BF16)
                v = jnp.where(rowh < valid, v, 0.0)
                sums0 = sums0 + fold(v)
                sums1 = sums1 + fold(v * v)
        cacc[0:1, 0:H] += unfold(sums0)
        cacc[0:1, H:] += unfold(sums1)

    @pl.when(first_step())
    def _():
        meet(peers.others)

    @pl.when(t < p0)
    def _():
        c_halo.start(t * wb, wb)

    @pl.when(t == p0 - 1)
    def _():
        c_link[0][...] = cacc[...]
        peers.start(c_link)

    here_p = (t >= p0) & (t < p0 + steps)

    @pl.when(here_p)
    def _():
        u = t - p0
        rowc = rows_of((Lp, C))
        block = pl.ds(pl.multiple_of(u * M, 128), M)
        bias = jnp.zeros((8, C), F32)
        parts = []
        for w in range(wb):
            valid = lens[i * plan.nw + u * wb + w] - s * Lp
            d = jnp.where(rowc < valid, cot[w].astype(F32), 0.0)
            bias = bias + fold(d)
            parts.append(d.astype(BF16))
        d = jnp.concatenate(parts, axis=0)
        dos[block] = d
        das[...] = mm_nt(d, pw[...])
        dacc[1:2] += unfold(bias)

    @pl.when(t == p0)
    def _():
        got = peers.finish(c_link)
        state[ST3 : ST3 + 1, 0:H] = got[:, 0:H]
        state[ST3 + 1 : ST3 + 2, 0:H] = got[:, H:]

    @pl.when(here_p)
    def _():
        u = t - p0
        block = pl.ds(pl.multiple_of(u * M, 128), M)
        rowh = rows_of((Lp, H))
        mean, rho = norm_of(state[ST3 : ST3 + 2, 0:H], total_of(lens))
        scale = state[GAIN3 : GAIN3 + 1, 0:H] * rho
        offset = state[SHIFT3 : SHIFT3 + 1, 0:H] - mean * scale
        s0, s1 = jnp.zeros((8, H), F32), jnp.zeros((8, H), F32)
        parts = []
        for w in range(wb):
            at = u * wb + w
            valid = lens[i * plan.nw + at] - s * Lp
            top, end = w * Lp, (w + 1) * Lp
            v = c2[at]
            zv = v * scale + offset
            act, slope = gelu_both(zv)
            parts.append(jnp.where(rowh < valid, act, 0.0).astype(BF16))
            dzw = das[top:end] * slope
            dz3[at] = dzw
            dedge[0, at] = dzw[:EDGE].astype(BF16)
            dedge[1, at] = dzw[Lp - EDGE :].astype(BF16)
            s0 = s0 + fold(dzw)
            s1 = s1 + fold(dzw * zv)
        a3 = jnp.concatenate(parts, axis=0)
        a3s[block] = a3
        a3T[:, block] = flip(a3)
        dacc[0:1, 0:H] += unfold(s0)
        dacc[0:1, H : 2 * H] += unfold(s1)
        d_halo.start(u * wb, wb)

    @pl.when(t == p0)
    def _():
        half_copy.wait()
        send_result(0)

    @pl.when(t == p0 + steps - 1)
    def _():
        d_link[0][...] = dacc[...]
        peers.start(d_link)

    @pl.when(t == r0)
    def _():
        for block in range(1, steps):
            send_result(block)
        rows = pl.ds(pl.multiple_of(h * plan.Hh, 16), plan.Hh)
        pgrad[...] = mm(a3T[rows], dos[...]).astype(BF16)

    @pl.when(t == b0)
    def _():
        got = peers.finish(d_link)
        shift = state[SHIFT3 : SHIFT3 + 1, 0:H]
        gain = state[GAIN3 : GAIN3 + 1, 0:H]
        state[SU3 : SU3 + 1, 0:H] = got[0:1, 0:H]
        state[SU3 + 1 : SU3 + 2, 0:H] = (got[0:1, H : 2 * H] - shift * got[0:1, 0:H]) / gain
        state[BSUM : BSUM + 1] = got[1:2]
        c_halo.finish()
        d_halo.finish()

    @pl.when((t >= b0) & (t < g0))
    def _():
        u = t - b0
        total = total_of(lens)
        mean3, rho3 = norm_of(state[ST3 : ST3 + 2, 0:H], total)
        gr3 = state[GAIN3 : GAIN3 + 1, 0:H] * rho3
        sg3 = state[SU3 : SU3 + 1, 0:H] / total
        gg3 = state[SU3 + 1 : SU3 + 2, 0:H] / total
        mean2, rho2 = norm_of(state[ST2 : ST2 + 2], total)
        scale2 = state[GAIN2 : GAIN2 + 1] * rho2
        offset2 = state[SHIFT2 : SHIFT2 + 1] - mean2 * scale2
        rowh = rows_of((Lp, H))
        rowe = rows_of((EDGE, H))
        rowc = rows_of((Lp, C))

        by_v = -gr3 * rho3 * gg3
        by_1 = gr3 * (mean3 * rho3 * gg3 - sg3)

        def back(dz, v):
            return gr3 * dz + by_v * v + by_1

        for w in range(wb):
            valid = lens[i * nw + u * wb + w] - s * Lp
            d = jnp.where(rowh < valid, back(dz3[u * wb + w], c2[u * wb + w]), 0.0)
            dl = back(dland[0, u * wb + w].astype(F32), cland[0, u * wb + w].astype(F32))
            dl = jnp.where((rowe - EDGE < valid) & (s > 0), dl, 0.0)
            dh = back(dland[1, u * wb + w].astype(F32), cland[1, u * wb + w].astype(F32))
            dh = jnp.where(rowe + Lp < valid, dh, 0.0)
            ext[w, 0:EDGE, 0:H] = dl
            ext[w, EDGE : EDGE + Lp, 0:H] = d
            ext[w, EDGE + Lp :, 0:H] = dh
            top, end = w * Lp, (w + 1) * Lp
            Z3[top:end, 0:H] = ext[w, EDGE + DIL : EDGE + DIL + Lp, 0:H].astype(BF16)
            Z3[top:end, H : 2 * H] = d.astype(BF16)
            Z3[top:end, 2 * H : 3 * H] = ext[w, EDGE - DIL : EDGE - DIL + Lp, 0:H].astype(BF16)

        y = mm(Z3[...], wt[...])

        M = wb * Lp
        dcT[:, pl.ds(pl.multiple_of(u * M, 128), M)] = flip(Z3[:, H : 2 * H])
        s0, s1 = jnp.zeros((8, C), F32), jnp.zeros((8, C), F32)
        for w in range(wb):
            at = u * wb + w
            valid = lens[i * nw + at] - s * Lp
            v = x2[w]
            zv = v * scale2 + offset2
            dzw = y[w * Lp : (w + 1) * Lp] * gelu_slope(zv)
            dzw = jnp.where(rowc < valid, dzw, 0.0)
            dz2[w] = dzw
            bedge[0, pl.ds(at, 1)] = dzw[0:1]
            bedge[1, pl.ds(at, 1)] = dzw[Lp - 1 : Lp]
            s0 = s0 + fold(dzw)
            s1 = s1 + fold(dzw * zv)
        bacc[0:1] += unfold(s0)
        bacc[1:2] += unfold(s1)

    @pl.when(t == g0 - 1)
    def _():
        b_link[0][...] = bacc[...]
        peers.start(b_link)
        b_halo.start(0, nw)

    @pl.when(last_step())
    def _():
        rows = pl.ds(pl.multiple_of(h * plan.Hh, 16), plan.Hh)
        for n in range(plan.T2):
            cols = slice(n * C, (n + 1) * C)
            grads[:, cols] = mm(dcT[rows], Y3[:, cols]).astype(BF16)

    @pl.when(last_step())
    def _():
        got = peers.finish(b_link)
        shift, gain = state[SHIFT2 : SHIFT2 + 1], state[GAIN2 : GAIN2 + 1]
        state[SU2 : SU2 + 1] = got[0:1]
        state[SU2 + 1 : SU2 + 2] = (got[1:2] - shift * got[0:1]) / gain
        b_halo.finish()
        for off in range(1, g):
            bulk(off, pl.ds(0, nw)).wait()


def block_phases(plan):
    n = plan.steps
    return n, 2 * n, 2 * n + 1, 3 * n + 1, 3 * n + 2


class Reduction:
    def __init__(self, plan, batches, out, give, mine, got, spread, half, mate, sems):
        self.plan, self.batches, self.out = plan, batches, out
        self.give, self.mine, self.got, self.spread = give, mine, got, spread
        self.half, self.mate = half, mate
        self.sems = sems
        self.s, self.z, self.i, self.h = plan.place()
        self.c = lax.rem(self.s, 2)
        self.m = lax.div(self.s, 2)
        self.chips = plan.chips

    @staticmethod
    def scratch(plan, batches):
        taps, wide = plan.T1 + 2, plan.C // 2
        full = (taps, plan.chips, plan.g, plan.rb, wide)
        part = (taps, plan.g, plan.rb, wide)
        return [
            pltpu.VMEM((taps, 2, plan.chips, plan.rb, wide), BF16),
            *[pltpu.VMEM(full, BF16)] * 4,
            *[pltpu.VMEM(part, BF16)] * 2,
            pltpu.SemaphoreType.DMA((2, len(batches), 5)),
        ]

    def copy(self, b, phase, src, dst, device):
        return remote(src, dst, self.sems.at[0, b, phase], self.sems.at[1, b, phase], device)

    def finish(self, b, phase, ref, device):
        done = self.copy(b, phase, ref, ref, device)
        done.wait_recv()
        done.wait_send()

    def taps(self, b):
        return pl.ds(*self.batches[b])

    def pair(self):
        return (2 * self.m + (1 - self.c), self.z)

    def far(self, off):
        return (2 * wrap(self.m + off, self.chips) + self.c, self.z)

    def member(self, off):
        return (self.s, self.h * self.plan.g + wrap(self.i + off, self.plan.g))

    def put(self, k, rows):
        wide = self.plan.C // 2
        for j in range(self.plan.g):
            for m in range(self.chips):
                v = rows(j, m)
                left, right = v[:, :wide], v[:, wide:]
                self.mine[k, m, j] = jnp.where(self.c == 0, left, right).astype(BF16)
                self.give[k, m, j] = jnp.where(self.c == 0, right, left).astype(BF16)

    def step0(self, b):
        taps = self.taps(b)
        self.copy(b, 0, self.give.at[taps], self.got.at[taps], self.pair()).start()

    def step1(self, b):
        taps = self.taps(b)
        self.finish(b, 0, self.got.at[taps], self.pair())
        first, count = self.batches[b]
        for k in range(first, first + count):
            v = self.mine[k].astype(F32) + self.got[k].astype(F32)
            self.mine[k] = v.astype(BF16)
        for off in range(1, self.chips):
            src = self.mine.at[taps, wrap(self.m + off, self.chips)]
            self.copy(b, 1, src, self.spread.at[taps, self.m], self.far(off)).start()

    def step2(self, b):
        taps = self.taps(b)
        self.finish(b, 1, self.spread.at[taps, pl.ds(0, self.chips - 1)], self.far(1))
        first, count = self.batches[b]
        for k in range(first, first + count):
            self.spread[k, self.m] = self.mine[k, self.m]
            v = self.spread[k, 0].astype(F32)
            for n in range(1, self.chips):
                v = v + self.spread[k, n].astype(F32)
            self.half[k] = v.astype(BF16)
        for off in range(1, self.plan.g):
            src = self.half.at[taps, wrap(self.i + off, self.plan.g)]
            self.copy(b, 2, src, self.mate.at[taps, off], self.member(off)).start()

    def step3(self, b):
        taps = self.taps(b)
        self.finish(b, 2, self.mate.at[taps, pl.ds(1, self.plan.g - 1)], self.member(1))
        first, count = self.batches[b]
        for k in range(first, first + count):
            v = self.half[k, self.i].astype(F32)
            for off in range(1, self.plan.g):
                v = v + self.mate[k, off].astype(F32)
            self.out[k, self.c, self.m] = v.astype(BF16)
        mine = self.out.at[taps, self.c, self.m]
        for off in range(1, self.chips):
            self.copy(b, 3, mine, mine, self.far(off)).start()

    def step4(self, b):
        taps = self.taps(b)
        self.finish(b, 3, self.out.at[taps, self.c, pl.ds(0, self.chips - 1)], self.far(1))
        mine = self.out.at[taps, self.c]
        self.copy(b, 4, mine, mine, self.pair()).start()

    def step5(self, b):
        self.finish(b, 4, self.out.at[self.taps(b), self.c], self.pair())


def tail_turns(plan):
    nD, T1 = plan.steps, plan.T1
    turns = [("x", 0)] + [("d", n) for n in range(1, nD)]
    xs, ws = [("x", n) for n in range(1, nD)], [("w", n) for n in range(T1)]
    for count in (2, 1, T1):
        turns += ws[:count] + xs[:1]
        xs, ws = xs[1:], ws[count:]
    return turns + xs


def tail_batches(plan):
    return [(plan.T1, 2), (0, 2)] + [(k, 1) for k in range(2, plan.T1)]


def tail_kernel(plan, lens, dz2, dzland, x2, x2land, cot, beyond, x, X5_hbm, taps_hbm, grads, pgrad,
                old, half_state,
                gz, gz_got, sums, summed,
                ext, D3, D0T, wcat, pick, eye, cols, y, part, split, acc, X5, X5_sems,
                taps, bulk_sems, *rest):
    t = pl.program_id(0)
    s, z, i, h = plan.place()
    L, Lp, C, wb, g, nw = plan.L, plan.Lp, plan.C, plan.wb, plan.g, plan.nw
    Ch, cs, T1 = plan.Ch, plan.cs, plan.T1
    M = wb * Lp
    nD = plan.steps
    turns = tail_turns(plan)
    last = len(turns) - 1
    peers = group_peers(plan)
    red = Reduction(plan, tail_batches(plan), *rest[:8])
    link = rest[8:]

    def member(off):
        return (s, h * g + wrap(i + off, g))

    def send(first, count):
        rows = pl.ds(first, count)
        for off in range(1, g):
            remote(
                part.at[off - 1, rows],
                gz_got.at[off, rows],
                bulk_sems.at[0, off],
                bulk_sems.at[1, off],
                member(off),
            ).start()

    def X5_copy(k):
        return pltpu.make_async_copy(X5_hbm.at[k], X5.at[k % 2], X5_sems.at[k % 2])

    def when(at):
        return pl.when(t == min(at, last))

    def turn(kind, k):
        return turns.index((kind, k)) if (kind, k) in turns else last

    def turn_of(kind):
        index = jnp.int32(0)
        here = False
        for n, (what, k) in enumerate(turns):
            if what == kind:
                index = jnp.where(t == n, k, index)
                here = (t == n) | here
        return here, index

    taps_copy = pltpu.make_async_copy(
        taps_hbm.at[:, pl.ds(pl.multiple_of(h * Ch, 128), Ch)], taps, X5_sems.at[2]
    )

    @when(0)
    def _():
        taps_copy.start()
        greet(peers.others)
        acc[...] = jnp.zeros_like(acc)
        pick[...] = pick_matrix(L)
        eye[...] = eye_matrix(Ch, Ch, 0)
        mean, rho = norm_of(half_state[ST1 : ST1 + 2], 2.0 * total_of(lens))
        scale = half_state[GAIN1 : GAIN1 + 1] * rho
        offset = half_state[SHIFT1 : SHIFT1 + 1] - mean * scale
        for k, row in enumerate((scale, offset)):
            cols[k] = column(row, L)

    @pl.when(t < nD)
    def _():
        total = total_of(lens)
        mean, rho = norm_of(old[ST2 : ST2 + 2], total)
        gr = old[GAIN2 : GAIN2 + 1] * rho
        sg = old[SU2 : SU2 + 1] / total
        gg = old[SU2 + 1 : SU2 + 2] / total
        rowc = rows_of((Lp, C))
        row1 = rows_of((1, C))

        by_dz = 0.5 * gr
        by_v = -0.5 * gr * rho * gg
        by_1 = 0.5 * gr * (mean * rho * gg - sg)

        def back(dout, dz, v):
            return 0.5 * dout + by_dz * dz + by_v * v + by_1

        def grad_of(w):
            at = t * wb + w
            valid = lens[i * nw + at] - s * Lp
            d = back(cot[w].astype(F32), dz2[w], x2[w])
            d = jnp.where(rowc < valid, d, 0.0)
            one = pl.ds(at, 1)
            dl = back(beyond[0, 2, one, :], dzland[0, one, :], x2land[0, w, EDGE - 1 : EDGE].astype(F32))
            dl = jnp.where((row1 - 1 < valid) & (s > 0), dl, 0.0)
            dh = back(beyond[1, 2, one, :], dzland[1, one, :], x2land[1, w, 0:1].astype(F32))
            dh = jnp.where(row1 + Lp < valid, dh, 0.0)
            ext[w, 7:8] = dl
            ext[w, 8 : 8 + Lp] = d
            ext[w, 8 + Lp : 9 + Lp] = dh
            top, end = w * Lp, (w + 1) * Lp
            D3[t, top:end, 0:C] = ext[w, 9 : 9 + Lp].astype(BF16)
            D3[t, top:end, C : 2 * C] = d.astype(BF16)
            D3[t, top:end, 2 * C : 3 * C] = ext[w, 7 : 7 + Lp].astype(BF16)

        for w in range(wb):
            grad_of(w)
        half = D3[t, :, pl.ds(pl.multiple_of(C + h * Ch, 128), Ch)]
        D0T[:, pl.ds(pl.multiple_of(t * M, 128), M)] = mm_nt(eye[...], half).astype(BF16)

    @when(0)
    def _():
        taps_copy.wait()
        for first in range(0, Ch, 64):
            rows = slice(first, min(first + 64, Ch))
            for r, parts in enumerate((((0,), (1, 2), (3, 4)), ((0, 1), (2, 3), (4,)))):
                for k, which in enumerate(parts):
                    v = taps[which[0], rows]
                    if len(which) > 1:
                        v = (v.astype(F32) + taps[which[1], rows].astype(F32)).astype(BF16)
                    at = r * Ch
                    wcat[at + rows.start : at + rows.stop, k * C : (k + 1) * C] = v
        meet(peers.others)

    here_x, bx = turn_of("x")

    def gradient(hf, nh):
        lanes = lanes_of((Ch, L))

        def through(w):
            valid = 2 * lens[i * nw + bx * wb + w] - s * L
            top, end = w * Lp, (w + 1) * Lp
            v = mm_nt(eye[...], x[w])
            da = jnp.concatenate([y[0:Ch, top:end], y[Ch:, top:end]], axis=1)
            da = mm(da.astype(BF16), pick[...])
            zv = v * cols[0] + cols[1]
            dzw = da * gelu_slope(zv)
            dzw = jnp.where(lanes < valid, dzw, 0.0)
            acc[0] += fold_lanes(dzw)
            acc[1] += fold_lanes(dzw * zv)
            split[w % 2] = dzw.astype(BF16)
            for off in range(g):
                rows = pl.ds(pl.multiple_of(lax.rem(i + off, g) * cs, 16), cs)
                if off == 0:
                    gz[w] = split[w % 2, rows]
                else:
                    part[off - 1, bx * wb + w] = split[w % 2, rows]

        n = wb // nh
        rows = slice(hf * n * Lp, (hf + 1) * n * Lp)
        y[:, rows] = mm_nt(wcat[...], D3[bx, rows])
        for w in range(hf * n, (hf + 1) * n):
            through(w)

    nh = 2 if wb % 2 == 0 and wb * Lp // 2 % 128 == 0 else 1

    @pl.when(here_x)
    def _():
        gradient(0, nh)
        send(bx * wb, wb // nh)

    first = min(1, last)
    table = (
        (first, 1, red.step1, 0),
        (max(turn("w", 1), first + 1), 1, red.step2, 0),
        (turn("w", 1), 1, red.step0, 1),
        (turn("x", 1), 0, red.step1, 1),
        (turn("w", 2), 1, red.step0, 2),
        (turn("x", 2), 0, red.step1, 2),
        (turn("x", 2), 1, red.step3, 0),
        (turn("x", 2), 1, red.step2, 1),
        (turn("w", 3), 1, red.step0, 3),
        (turn("w", 4), 1, red.step0, 4),
        (turn("w", 4), 1, red.step1, 3),
        (turn("w", 4), 1, red.step2, 2),
        (turn("x", 3), 0, red.step1, 4),
        (turn("x", 3), 0, red.step4, 0),
        (turn("x", 3), 0, red.step3, 1),
        (last, 1, red.step2, 3),
        (last, 1, red.step3, 2),
        (last, 1, red.step2, 4),
    )

    def between(at, end):
        return end == 0 and nh == 2 and turns[at][0] == "x"

    def go_on(entries):
        for at, _, step, batch in entries:

            @when(at)
            def _():
                step(batch)

    go_on([e for e in table if between(*e[:2])])

    if nh == 2:

        @pl.when(here_x)
        def _():
            gradient(1, nh)

    @when(0)
    def _():
        hs = plan.H // plan.nz
        rb = plan.rb
        for u in range(2):

            def rows(j, m, u=u):
                side, r = m * rb // hs, m * rb % hs
                n = 2 * side + u
                rows = slice(j * hs + r, j * hs + r + rb)
                v = grads[rows, n * C : (n + 1) * C] if n < plan.T2 else pgrad[rows]
                return v.astype(F32)

            red.put(T1 + u, rows)
        red.step0(0)

    @when(1)
    def _():
        X5_copy(0).start()
        X5_copy(1).start()

    here_w, k = turn_of("w")

    @pl.when(here_w)
    def _():
        X5_copy(k).wait()
        y[0:Ch, 0:C] = mm(D0T[...], X5[lax.rem(k, 2)])

        @pl.when(k < T1 - 2)
        def _():
            X5_copy(k + 2).start()

        rb = plan.rb
        red.put(k, lambda j, m: y[j * cs + m * rb : j * cs + (m + 1) * rb, 0:C])

    @when(turn("x", nD - 1))
    def _():
        packet = link[0]
        packet[...] = jnp.zeros_like(packet)
        packet[0:1, 0:Ch] = jnp.sum(acc[0].T, axis=0, keepdims=True)
        packet[1:2, 0:Ch] = jnp.sum(acc[1].T, axis=0, keepdims=True)
        peers.start(link)

    go_on([e for e in table if not between(*e[:2])])

    @pl.when(here_x & (bx < nD - 1))
    def _():
        if nh == 2:
            send(bx * wb + wb // nh, wb // nh)

    @when(last)
    def _():
        if nh == 2:
            send(nw - wb // 2, wb // 2)

    @when(last)
    def _():
        red.step3(3)
        red.step4(1)
        red.step4(2)
        red.step3(4)
        red.step4(3)
        got = peers.finish(link)[:, 0:Ch]
        shift, gain = half_state[SHIFT1 : SHIFT1 + 1], half_state[GAIN1 : GAIN1 + 1]
        sums[0:1] = got[0:1]
        sums[1:2] = (got[1:2] - shift * got[0:1]) / gain
        red.step4(4)
        for b in range(5):
            red.step5(b)
        own = pltpu.make_async_copy(red.out, summed, X5_sems.at[0])
        own.start()
        for off in range(1, g):
            done = remote(
                part.at[off - 1],
                gz_got.at[off],
                bulk_sems.at[0, off],
                bulk_sems.at[1, off],
                member(off),
            )
            done.wait_recv()
            done.wait_send()
        own.wait()


def input_grad_kernel(plan, wg, lens, x, gz, gz_got, sums, res, res_got, summed,
                      state, half_state,
                      out, out_result, conv_grad, dil_grad, point_grad,
                      g1, b1, g2, b2, g3, b3, pb, eye, cols, xt):
    t = pl.program_id(0)
    s, z, i, h = plan.place()
    L, Ch, cs = plan.L, plan.Ch, plan.cs
    turn = plan.nw // wg
    mine = pl.ds(pl.multiple_of(i * cs, 16), cs)

    @pl.when(first_step())
    def _():
        n = 2.0 * total_of(lens)
        mean, rho = norm_of(half_state[ST1 : ST1 + 2], n)
        gr = half_state[GAIN1 : GAIN1 + 1] * rho
        gg = sums[1:2] / n * rho
        for k, row in enumerate((gr, -gr * gg, gr * (mean * gg - sums[0:1] / n))):
            xt[...] = column(row, L)
            cols[k] = xt[mine]
        eye[...] = eye_matrix(cs, Ch, i * cs)

        def mine_of(src, at, which, count, *dsts):
            n = dsts[0].shape[1]
            for k in range(count):

                @pl.when(which == k)
                def _():
                    for dst, r in zip(dsts, at):
                        dst[...] = src[r : r + 1, k * n : (k + 1) * n]

        mine_of(sums, (1, 0), i, plan.g, g1, b1)
        mine_of(state, (SU2 + 1, SU2), z, plan.nz, g2, b2)
        mine_of(state, (SU3 + 1, SU3), z, plan.nz, g3, b3)
        mine_of(state, (BSUM,), z, plan.nz, pb)

    own = lax.div(t, turn) == i
    for w in range(wg):
        out_result[w] = jnp.where(own, res[0, w], res_got[0, w])

    C, T1, hs, rb, wide = plan.C, plan.T1, plan.H // plan.nz, plan.rb, plan.C // 2
    count = plan.NW // wg
    turns = min(count, plan.chips)
    per, every = plan.chips // turns, count // turns

    def spread(chunk):
        for n in range(per):
            m = chunk * per + n
            side, r = m * rb // hs, m * rb % hs
            for c in range(2):
                at = slice(c * wide, (c + 1) * wide)
                for k in range(T1):
                    conv_grad[k, n * rb : (n + 1) * rb, at] = summed[k, c, n].astype(F32)
                for u in range(2):
                    v = summed[T1 + u, c, n].astype(F32)
                    if 2 * side + u < plan.T2:
                        dil_grad[2 * side + u, r : r + rb, at] = v
                    else:
                        point_grad[r : r + rb, at] = v

    for chunk in range(turns):
        pl.when(t == chunk * every)(partial(spread, chunk))

    lanes = lanes_of((cs, L))
    for w in range(wg):
        valid = 2 * lens[t * wg + w] - s * L
        v = mm_nt(eye[...], x[w])
        dz = jnp.where(own, gz[w], gz_got[0, w]).astype(F32)
        r = cols[0] * dz + v * cols[1] + cols[2]
        out[w] = jnp.where(lanes < valid, r, 0.0).astype(BF16)


def call(kernel, plan, name, steps, ins, outs, scratch, flops, nbytes, cid=None):
    extra = {} if cid is None else dict(collective_id=cid, has_side_effects=True)
    return pl.pallas_call(
        partial(kernel, plan),
        grid=(steps,),
        in_specs=[SMEM] + [spec for spec, _ in ins],
        out_specs=[spec for spec, _, _ in outs],
        out_shape=[jax.ShapeDtypeStruct(shape, dtype) for _, shape, dtype in outs],
        scratch_shapes=scratch,
        compiler_params=pltpu.CompilerParams(vmem_limit_bytes=VMEM_LIMIT, **extra),
        cost_estimate=pl.CostEstimate(
            flops=int(flops), bytes_accessed=int(nbytes), transcendentals=0
        ),
        name=name,
    )


def per_device(
    inputs,
    lengths,
    input_gain,
    input_shift,
    conv_weight,
    branch_gain,
    branch_shift,
    dilated_tap_weight,
    mixer_gain,
    mixer_shift,
    point_weight,
    point_bias,
    cotangent,
):
    NW, L, C = inputs.shape
    Lp = L // 2
    nz = lax.axis_size("ch")
    R = 2
    plan = Plan(
        ns=lax.axis_size("seq"),
        nz=nz,
        R=R,
        NW=NW,
        L=L,
        C=C,
        H=mixer_gain.shape[0] * nz,
        T1=conv_weight.shape[0],
        T2=dilated_tap_weight.shape[0],
        wb=min(NW * R // nz, max(1, 512 // Lp)),
    )
    g, nw, cs, Ch, H, Hh, wb = plan.g, plan.nw, plan.cs, plan.Ch, plan.H, plan.Hh, plan.wb
    T1, T2, steps = plan.T1, plan.T2, plan.steps
    M = wb * Lp
    hs = H // nz
    lens = lengths.astype(jnp.int32)

    def row(a):
        return a.reshape(1, a.shape[0])

    def grp():
        return lax.rem(lax.axis_index("ch"), g)

    def half():
        return lax.div(lax.axis_index("ch"), g)

    def core():
        return lax.rem(lax.axis_index("seq"), 2)

    def chip4():
        return lax.div(lax.axis_index("seq"), plan.ns // 4)

    def whole(*shape):
        return pl.BlockSpec(shape, lambda t: (0,) * len(shape), pipeline_mode=pl.Buffered(1))

    def const(*shape):
        return pl.BlockSpec(shape, lambda t: (0,) * len(shape))

    def win(*shape):
        return pl.BlockSpec(shape, lambda t: (t,) + (0,) * (len(shape) - 1))

    def arg_win(n, width):
        return pl.BlockSpec((wb, n, width), lambda t: (grp() * steps + t, 0, 0))

    def ins(*pairs):
        return [p for p in pairs]

    share = NW // nz
    nm = max(1, share // wb)

    def edge_spec(n):
        return pl.BlockSpec(
            (nw, 16, C), lambda t: (grp(), n, 0), pipeline_mode=pl.Buffered(1)
        )

    def head_block(t):
        own = lax.div(lax.axis_index("ch") * share, wb) + t
        return jnp.where(t < nm, own, grp() * steps + t - nm), 0, 0

    def after(*shape):
        return pl.BlockSpec(
            shape, lambda t: (jnp.maximum(t - nm, 0),) + (0,) * (len(shape) - 1)
        )

    pairs = ins(
        (pl.BlockSpec((wb, L, C), head_block), inputs),
        (edge_spec(0), inputs),
        (edge_spec(L // 16 - 1), inputs),
        (edge_spec(0), cotangent),
        (edge_spec(Lp // 16 - 1), cotangent),
        (whole(1, cs), row(branch_gain)),
        (whole(1, cs), row(branch_shift)),
        (whole(1, cs), row(point_bias)),
        (whole(1, H // nz), row(mixer_gain)),
        (whole(1, H // nz), row(mixer_shift)),
        (ANY, conv_weight.reshape(T1 * C, C)),
        (whole(C), input_gain),
        (whole(C), input_shift),
        (
            pl.BlockSpec(
                (1, hs, C // 2),
                lambda t: (jnp.minimum(chip4(), T2 - 1), 0, core()),
                pipeline_mode=pl.Buffered(1),
            ),
            jnp.swapaxes(dilated_tap_weight, 1, 2),
        ),
        (
            pl.BlockSpec(
                (hs, C // 2), lambda t: (0, core()), pipeline_mode=pl.Buffered(1)
            ),
            point_weight,
        ),
    )
    plane, line, group = plane_peers(plan), line_peers(plan), group_peers(plan)
    state_shape = (STATE, C)
    edges2, edges3 = (2, nw, EDGE, C), (2, nw, EDGE, H)
    X5, x2, land2, state, beyond, full = call(
        lambda plan, *refs: head_kernel(plan, nm, *refs),
        plan,
        "head",
        nm + steps,
        pairs,
        [
            (
                pl.BlockSpec((T1, M, C), lambda t: (0, jnp.maximum(t - nm, 0), 0)),
                (T1, nw * Lp, C),
                BF16,
            ),
            (after(wb, Lp, C), (nw, Lp, C), F32),
            (ANY, edges2, BF16),
            (const(*state_shape), state_shape, F32),
            (const(2, 3, nw, C), (2, 3, nw, C), F32),
            (ANY, (2, T2 + 1, nz, hs, C // 2), BF16),
        ],
        [
            pltpu.VMEM((2, 8, C), F32),
            pltpu.VMEM((2, 3, nw, C), F32),
            pltpu.VMEM((2, 3, nw, C), F32),
            pltpu.VMEM((L, L), BF16),
            pltpu.VMEM(edges2, BF16),
            pltpu.VMEM((2, C), F32),
            pltpu.VMEM((T1 * C, C), BF16),
            pltpu.SemaphoreType.DMA,
            pltpu.VMEM((hs, C // 2), BF16),
            pltpu.SemaphoreType.DMA((2, 4)),
            HALO_SEMS,
            HALO_SEMS,
        ]
        + plane.scratch(2, C)
        + line.scratch(3, C)
        + group.scratch(2, C),
        2 * nw * Lp * T1 * C * C,
        nw * Lp * C * 20,
        cid=1,
    )(lens, *[a for _, a in pairs])

    taps_spec = whole(2, T2, nz, hs, C // 2)
    pw_spec = pl.BlockSpec(
        (2, 1, nz, hs, C // 2), lambda t: (0, T2, 0, 0, 0), pipeline_mode=pl.Buffered(1)
    )

    def early(*shape):
        return pl.BlockSpec(
            shape, lambda t: (jnp.minimum(t, steps - 1),) + (0,) * (len(shape) - 1)
        )

    def early_land(width):
        return pl.BlockSpec(
            (2, wb, EDGE, width), lambda t: (0, jnp.minimum(t, steps - 1), 0, 0)
        )

    def half_of(n):
        return pl.BlockSpec((n, Ch), lambda t: (0, half()), pipeline_mode=pl.Buffered(1))

    cot_spec = pl.BlockSpec(
        (wb, Lp, C), lambda t: (grp() * steps + jnp.minimum(t, steps - 1), 0, 0)
    )

    p0, r0, b0, g0, block_steps = block_phases(plan)

    def at_phase(first):
        return lambda t: jnp.clip(t - first, 0, steps - 1)

    in_p, in_b = at_phase(p0), at_phase(b0)
    pairs = ins(
        (
            pl.BlockSpec(
                (wb, Lp, C),
                lambda t: (jnp.where(t < p0 + steps, jnp.minimum(t, steps - 1), in_b(t)), 0, 0),
            ),
            x2,
        ),
        (ANY, x2),
        (early_land(C), land2),
        (pl.BlockSpec((wb, Lp, C), lambda t: (grp() * steps + in_p(t), 0, 0)), cotangent),
        (taps_spec, full),
        (pw_spec, full),
        (whole(T2, hs, C), jnp.swapaxes(dilated_tap_weight, 1, 2)),
        (whole(hs, C), point_weight),
        (whole(*state_shape), state),
        (half_of(STATE), state),
    )
    dz2, grads, pgrad, res, dland2, state, res_got = call(
        block_kernel,
        plan,
        "block",
        block_steps,
        pairs,
        [
            (pl.BlockSpec((wb, Lp, C), lambda t: (in_b(t), 0, 0)), (nw, Lp, C), F32),
            (const(Hh, T2 * C), (Hh, T2 * C), BF16),
            (const(Hh, C), (Hh, C), BF16),
            (const(g, nw, cs, Lp), (g, nw, cs, Lp), BF16),
            (ANY, (2, nw, C), F32),
            (const(*state_shape), state_shape, F32),
            (ANY, (g, nw, cs, Lp), BF16),
        ],
        [
            pltpu.VMEM((wb, Lp + 2 * EDGE, C), F32),
            pltpu.VMEM((H, T2 * C), BF16),
            pltpu.VMEM((T2 * H, C), BF16),
            pltpu.VMEM((H, C), BF16),
            pltpu.VMEM((nw * Lp, T2 * C), BF16),
            pltpu.VMEM((nw, Lp, H), F32),
            pltpu.VMEM((nw, Lp, H), F32),
            pltpu.VMEM((M, H), F32),
            pltpu.VMEM((nw * Lp, H), BF16),
            pltpu.VMEM((H, nw * Lp), BF16),
            pltpu.VMEM((nw * Lp, C), BF16),
            pltpu.VMEM((M, T2 * H), BF16),
            pltpu.VMEM((H, nw * Lp), BF16),
            pltpu.VMEM(edges3, BF16),
            pltpu.VMEM(edges3, BF16),
            pltpu.VMEM((1, 2 * H), F32),
            pltpu.VMEM(edges3, BF16),
            pltpu.VMEM(edges3, BF16),
            pltpu.VMEM((2, C), F32),
            pltpu.VMEM((2, nw, C), F32),
            pltpu.VMEM((2, C), F32),
            pltpu.SemaphoreType.DMA((3, 2, 2)),
            pltpu.SemaphoreType.DMA((2, g)),
            pltpu.VMEM((nw, Lp, Ch), F32),
            pltpu.SemaphoreType.DMA,
            pltpu.VMEM((H, H), BF16),
        ]
        + group.scratch(1, 2 * H)
        + group.scratch(2, C)
        + group.scratch(2, C),
        nw * Lp * C * H * (6 * T2 + 6),
        nw * Lp * C * 30,
        cid=3,
    )(lens, *[a for _, a in pairs])

    chips, rb = plan.chips, plan.rb
    turns_t = tail_turns(plan)

    def x_block(t):
        block = jnp.int32(0)
        for n, (what, k) in enumerate(turns_t):
            if what == "x":
                block = jnp.where(t >= n, k, block)
        return block

    sshape = (T1 + 2, 2, chips, rb, C // 2)
    pairs = ins(
        (early(wb, Lp, C), dz2),
        (whole(2, nw, C), dland2),
        (early(wb, Lp, C), x2),
        (early_land(C), land2),
        (cot_spec, cotangent),
        (whole(2, 3, nw, C), beyond),
        (
            pl.BlockSpec(
                (wb, L, Ch), lambda t: (grp() * steps + x_block(t), 0, half())
            ),
            inputs,
        ),
        (ANY, X5),
        (ANY, conv_weight),
        (whole(Hh, T2 * C), grads),
        (whole(Hh, C), pgrad),
        (whole(*state_shape), state),
        (half_of(STATE), state),
    )
    gz, gz_got, sums1, summed = call(
        tail_kernel,
        plan,
        "tail",
        len(turns_t),
        pairs,
        [
            (pl.BlockSpec((wb, cs, L), lambda t: (x_block(t), 0, 0)), (nw, cs, L), BF16),
            (ANY, (g, nw, cs, L), BF16),
            (const(2, Ch), (2, Ch), F32),
            (ANY, sshape, BF16),
        ],
        [
            pltpu.VMEM((wb, Lp + 16, C), F32),
            pltpu.VMEM((steps, M, 3 * C), BF16),
            pltpu.VMEM((Ch, nw * Lp), BF16),
            pltpu.VMEM((2 * Ch, 3 * C), BF16),
            pltpu.VMEM((L, L), BF16),
            pltpu.VMEM((Ch, Ch), BF16),
            pltpu.VMEM((2, Ch, L), F32),
            pltpu.VMEM((2 * Ch, max(M, C)), F32),
            pltpu.VMEM((g - 1, nw, cs, L), BF16),
            pltpu.VMEM((2, Ch, L), BF16),
            pltpu.VMEM((2, Ch, min(L, 128)), F32),
            pltpu.VMEM((2, nw * Lp, C), BF16),
            pltpu.SemaphoreType.DMA((3,)),
            pltpu.VMEM((T1, Ch, C), BF16),
            pltpu.SemaphoreType.DMA((2, g)),
        ]
        + Reduction.scratch(plan, tail_batches(plan))
        + group.scratch(2, C),
        2 * nw * Lp * (6 + T1) * C * Ch,
        nw * Lp * C * 40,
        cid=6,
    )(lens, *[a for _, a in pairs])

    wg = min(2 * wb, nw)
    count = NW // wg
    turn = nw // wg
    turns = min(count, chips)

    def own_block(t):
        return jnp.where(lax.div(t, turn) == grp(), lax.rem(t, turn), 0)

    def got_slot(t):
        off = lax.rem(grp() - lax.div(t, turn) + g, g)
        return jnp.maximum(off, 1), jnp.where(off > 0, lax.rem(t, turn), 0)

    pairs = ins(
        (pl.BlockSpec((wg, L, Ch), lambda t: (t, 0, half())), inputs),
        (pl.BlockSpec((wg, cs, L), lambda t: (own_block(t), 0, 0)), gz),
        (pl.BlockSpec((1, wg, cs, L), lambda t: got_slot(t) + (0, 0)), gz_got),
        (whole(2, Ch), sums1),
        (pl.BlockSpec((1, wg, cs, Lp), lambda t: (grp(), own_block(t), 0, 0)), res),
        (pl.BlockSpec((1, wg, cs, Lp), lambda t: got_slot(t) + (0, 0)), res_got),
        (
            pl.BlockSpec(
                (T1 + 2, 2, chips // turns, rb, C // 2),
                lambda t: (0, 0, t * turns // count, 0, 0),
            ),
            summed,
        ),
        (whole(*state_shape), state),
        (half_of(STATE), state),
    )
    outs = call(
        lambda plan, *refs: input_grad_kernel(plan, wg, *refs),
        plan,
        "input_grad",
        count,
        pairs,
        [
            (win(wg, cs, L), (NW, cs, L), BF16),
            (win(wg, cs, Lp), (NW, cs, Lp), BF16),
            (
                pl.BlockSpec((T1, cs // turns, C), lambda t: (0, t * turns // count, 0)),
                (T1, cs, C),
                F32,
            ),
            (const(T2, hs, C), (T2, hs, C), F32),
            (const(hs, C), (hs, C), F32),
        ]
        + [(const(1, n), (1, n), F32) for n in (cs, cs, cs, cs, hs, hs, cs)],
        [
            pltpu.VMEM((cs, Ch), BF16),
            pltpu.VMEM((3, cs, L), F32),
            pltpu.VMEM((Ch, L), F32),
        ],
        2 * NW * L * Ch * cs,
        NW * L * cs * 8,
    )(lens, *[a for _, a in pairs])
    grad, result, conv_grad, dil_grad, point_grad = outs[:5]
    g1, b1, g2, b2, g3, b3, pb = [a[0] for a in outs[5:]]
    return (
        jnp.swapaxes(result, 1, 2),
        jnp.swapaxes(grad, 1, 2),
        jnp.swapaxes(conv_grad, 1, 2),
        g1,
        b1,
        g2,
        b2,
        jnp.swapaxes(dil_grad, 1, 2),
        g3,
        b3,
        point_grad,
        pb,
    )


def solution(mesh):
    in_specs = (
        P(None, "seq", None),
        P(),
        P(),
        P(),
        P(),
        P("ch"),
        P("ch"),
        P(None, None, "ch"),
        P("ch"),
        P("ch"),
        P("ch", None),
        P("ch"),
        P(None, "seq", None),
    )
    out_specs = (
        P(None, "seq", "ch"),
        P(None, "seq", "ch"),
        P(None, None, "ch"),
        P("ch"),
        P("ch"),
        P("ch"),
        P("ch"),
        P(None, None, "ch"),
        P("ch"),
        P("ch"),
        P("ch", None),
        P("ch"),
    )
    return jax.shard_map(
        per_device, mesh=mesh, in_specs=in_specs, out_specs=out_specs, check_vma=False
    )
```

```python
from functools import partial
from typing import NamedTuple

import jax
import jax.numpy as jnp
from jax import lax
from jax.experimental import pallas as pl
from jax.experimental.pallas import tpu as pltpu
from jax.sharding import PartitionSpec as P

DIL = 14
EDGE = 16
EPS = 1e-05
GC0 = 0.7978845608028654
GC1 = 0.044715
F32 = jnp.float32
BF16 = jnp.bfloat16
MESH = pl.DeviceIdType.MESH
VMEM_LIMIT = 58 * 1024 * 1024
ANY = pl.BlockSpec(memory_space=pl.ANY)
SMEM = pl.BlockSpec(memory_space=pltpu.SMEM)


ST1, GAIN2, SHIFT2, BIAS, GAIN3, SHIFT3, GAIN1, SHIFT1, ST2, ST3, SU3, BSUM, SU2 = (
    0, 2, 3, 4, 5, 6, 7, 8, 9, 11, 13, 15, 16
)
STATE = 24


class Plan(NamedTuple):
    ns: int
    nz: int
    R: int
    NW: int
    L: int
    C: int
    H: int
    T1: int
    T2: int
    wb: int

    @property
    def g(self):
        return self.nz // self.R

    @property
    def nw(self):
        return self.NW // self.g

    @property
    def Lp(self):
        return self.L // 2

    @property
    def cs(self):
        return self.C // self.nz

    @property
    def Ch(self):
        return self.C // self.R

    @property
    def Hh(self):
        return self.H // self.R

    @property
    def steps(self):
        return self.nw // self.wb

    @property
    def chips(self):
        return self.ns // 2

    @property
    def rb(self):
        return self.cs // self.chips

    def place(self):
        s, z = lax.axis_index("seq"), lax.axis_index("ch")
        return s, z, lax.rem(z, self.g), lax.div(z, self.g)


def gelu(z):
    t = jnp.tanh(z * (GC0 + (GC0 * GC1) * (z * z)))
    return z * (0.5 + 0.5 * t)


def gelu_both(z):
    sq = z * z
    t = jnp.tanh(z * (GC0 + (GC0 * GC1) * sq))
    h = 0.5 + 0.5 * t
    v = z * h
    return v, h + v * (1.0 - t) * (GC0 + (3.0 * GC0 * GC1) * sq)


def gelu_slope(z):
    return gelu_both(z)[1]


def fold(v):
    return jnp.sum(v.reshape(v.shape[0] // 8, 8, v.shape[1]), axis=0)


def fold_lanes(v):
    out = v[:, 0:128]
    for k in range(128, v.shape[1], 128):
        out = out + v[:, k : k + 128]
    return out


def unfold(v):
    return jnp.sum(v, axis=0, keepdims=True)


def rows_of(shape):
    return lax.broadcasted_iota(jnp.int32, shape, 0)


def lanes_of(shape):
    return lax.broadcasted_iota(jnp.int32, shape, 1)


def total_of(lens):
    n = lens[0]
    for k in range(1, lens.shape[0]):
        n = n + lens[k]
    return n.astype(F32)


def norm_of(stats, total):
    mean = stats[0:1] / total
    square = stats[1:2] / total
    return mean, lax.rsqrt(square - mean * mean + EPS)


def flat(ref):
    return ref[...].reshape(1, ref.shape[0])


def column(row, n):
    return jnp.broadcast_to(row, (n, row.shape[1])).T


def mm(a, b):
    return jnp.dot(a, b, preferred_element_type=F32)


def mm_nt(a, b):
    return lax.dot_general(a, b, (((1,), (1,)), ((), ())), preferred_element_type=F32)


def mm_tn(a, b):
    return lax.dot_general(a, b, (((0,), (0,)), ((), ())), preferred_element_type=F32)


def mm_tt(a, b):
    return lax.dot_general(a, b, (((0,), (1,)), ((), ())), preferred_element_type=F32)


def eye_matrix(n, m, first):
    return jnp.where(lanes_of((n, m)) == rows_of((n, m)) + first, 1.0, 0.0).astype(BF16)


def pick_matrix(L):
    r, n = rows_of((L, L)), lanes_of((L, L))
    bin_of = 2 * r - jnp.where(r >= L // 2, L - 1, 0)
    return jnp.where(n == bin_of, 1.0, 0.0).astype(BF16)


def remote(src, dst, send, recv, device):
    return pltpu.make_async_remote_copy(
        src_ref=src,
        dst_ref=dst,
        send_sem=send,
        recv_sem=recv,
        device_id=device,
        device_id_type=MESH,
    )


def wrap(v, n):
    return jnp.where(v >= n, v - n, v)


def greet(devices):
    barrier = pltpu.get_barrier_semaphore()
    for device in devices:
        pl.semaphore_signal(barrier, inc=1, device_id=device, device_id_type=MESH)


def meet(devices):
    pl.semaphore_wait(pltpu.get_barrier_semaphore(), len(devices))


class Peers:
    def __init__(self, me, others):
        self.me, self.others = me, others
        self.count = len(others) + 1

    def start(self, link):
        packet, buf, sems = link
        for device in self.others:
            remote(packet, buf.at[self.me], sems.at[0], sems.at[1], device).start()

    def finish(self, link):
        packet, buf, sems = link
        buf[self.me] = packet[...]
        rest = buf.at[pl.ds(0, self.count - 1)]
        done = remote(rest, rest, sems.at[0], sems.at[1], self.others[0])
        done.wait_recv()
        acc = buf[0]
        for q in range(1, self.count):
            acc = acc + buf[q]
        done.wait_send()
        return acc

    def scratch(self, rows, width):
        return [
            pltpu.VMEM((rows, width), F32),
            pltpu.VMEM((self.count, rows, width), F32),
            pltpu.SemaphoreType.DMA((2,)),
        ]


def group_peers(plan):
    s, z, i, h = plan.place()
    g = plan.g
    others = [
        (wrap(s + a, plan.ns), h * g + wrap(i + b, g))
        for a in range(plan.ns)
        for b in range(g)
        if a or b
    ]
    return Peers(s * g + i, others)


def plane_peers(plan):
    s, z, i, h = plan.place()
    return Peers(s, [(wrap(s + a, plan.ns), z) for a in range(1, plan.ns)])


def line_peers(plan):
    s, z, i, h = plan.place()
    return Peers(z, [(s, wrap(z + a, plan.nz)) for a in range(1, plan.nz)])


class Halo:
    def __init__(self, plan, edge, land, sems):
        self.edge, self.land, self.sems = edge, land, sems
        s, z, _, _ = plan.place()
        self.to = ((wrap(s + plan.ns - 1, plan.ns), z), (wrap(s + 1, plan.ns), z))

    def copy(self, side, rows):
        return remote(
            self.edge.at[side, rows],
            self.land.at[1 - side, rows],
            self.sems.at[0, side],
            self.sems.at[1, side],
            self.to[side],
        )

    def start(self, first, count):
        for side in range(2):
            self.copy(side, pl.ds(first, count)).start()

    def finish(self):
        for side in range(2):
            done = self.copy(side, pl.ds(0, self.land.shape[1]))
            done.wait_recv()
            done.wait_send()


HALO_SEMS = pltpu.SemaphoreType.DMA((2, 2))


class Gather:
    def __init__(self, plan, part, full, sems):
        self.plan, self.part, self.full, self.sems = plan, part, full, sems
        self.s, self.z, self.i, self.h = plan.place()
        self.c, self.m = lax.rem(self.s, 2), lax.div(self.s, 2)
        self.chips = plan.chips
        self.every = self.chips // 4
        self.tap = lax.div(self.m, self.every)
        self.owner = lax.rem(self.m, self.every) == 0
        self.mine = full.at[self.c, self.tap]

    def others(self):
        g, nz = self.plan.g, self.plan.nz
        return [(self.s, wrap(self.h * g + g + r, nz)) for r in range(nz - g)]

    def far(self, off):
        return (2 * wrap(self.m + off, self.chips) + self.c, self.z)

    def line(self, off):
        nz = self.plan.nz
        device = (self.s, wrap(self.z + off, nz))
        dst = self.mine.at[nz - off]
        return remote(self.part, dst, self.sems.at[0, 1], self.sems.at[1, 1], device)

    def far_rows(self, taps):
        return self.full.at[self.c, taps, pl.ds(1, self.plan.nz - 1)]

    def chip(self, off):
        rows = self.far_rows(self.tap)
        return remote(rows, rows, self.sems.at[0, 2], self.sems.at[1, 2], self.far(off))

    def pair(self):
        half = self.far_rows(pl.ds(0, 4))
        device = (2 * self.m + 1 - self.c, self.z)
        return remote(half, half, self.sems.at[0, 3], self.sems.at[1, 3], device)

    def line_start(self):
        @pl.when(self.owner)
        def _():
            for off in range(1, self.plan.nz):
                self.line(off).start()

    def line_finish(self):
        @pl.when(self.owner)
        def _():
            rest = self.far_rows(self.tap)
            device = (self.s, wrap(self.z + 1, self.plan.nz))
            done = remote(rest, rest, self.sems.at[0, 1], self.sems.at[1, 1], device)
            done.wait_recv()
            done.wait_send()

    def chips_start(self):
        @pl.when(self.owner)
        def _():
            for off in range(1, self.chips):
                self.chip(off).start()

    def pair_start(self):
        def taken(count):
            rest = self.far_rows(pl.ds(0, count))
            return remote(rest, rest, self.sems.at[0, 2], self.sems.at[1, 2], self.far(1))

        @pl.when(self.owner)
        def _():
            taken(3).wait_recv()
            for off in range(1, self.chips):
                self.chip(off).wait_send()

        if self.every > 1:

            @pl.when(jnp.logical_not(self.owner))
            def _():
                taken(4).wait_recv()

        self.pair().start()

    def pair_finish(self):
        done = self.pair()
        done.wait_recv()
        done.wait_send()


def first_step():
    return pl.program_id(0) == 0


def last_step():
    return pl.program_id(0) == pl.num_programs(0) - 1


def head_kernel(plan, nm, lens, x, xtop, xend, ctop, cend, g2, s2, pb, g3, s3,
                w_hbm, gain, shift, taps, pw,
                X5, x2, land, state, beyond_out, full,
                macc, beyond, xedge, sel, edge, acc, w_ref, w_sem, part,
                gather_sems, xhalo_sems, halo_sems, *links):
    t = pl.program_id(0)
    peers, plane, line = group_peers(plan), plane_peers(plan), line_peers(plan)
    xhalo = Halo(plan, xedge, beyond, xhalo_sems)
    halo = Halo(plan, edge, land, halo_sems)
    gather = Gather(plan, part, full, gather_sems)
    w_copy = pltpu.make_async_copy(w_hbm, w_ref, w_sem)
    plane_link, line_link, link = links[:3], links[3:6], links[6:]
    s, z, i, h = plan.place()
    L, Lp, C, nw, nz, wb = plan.L, plan.Lp, plan.C, plan.nw, plan.nz, plan.wb
    share = plan.NW // nz
    c = t - nm
    everyone = peers.others + gather.others()

    @pl.when(first_step())
    def _():
        w_copy.start()
        greet(everyone)
        part[...] = jnp.where(gather.tap == 3, pw[...], taps[0])
        macc[...] = jnp.zeros_like(macc)
        acc[...] = jnp.zeros_like(acc)
        state[...] = jnp.zeros_like(state)
        state[GAIN1 : GAIN1 + 1] = flat(gain)
        state[SHIFT1 : SHIFT1 + 1] = flat(shift)
        n16 = nw * 16
        for side, (xe, ce, places) in enumerate(
            ((xtop, ctop, (0, 1, 0)), (xend, cend, (14, 15, 15)))
        ):
            for k, at in enumerate(places):
                rows, lanes = rows_of((nw, n16)), lanes_of((nw, n16))
                one = jnp.where(lanes == 16 * rows + at, 1.0, 0.0).astype(BF16)
                block = (xe if k < 2 else ce)[...].reshape(n16, C)
                xedge[side, k] = mm(one, block)
        shape = (Lp, L)
        for odd in range(2):
            at = lanes_of(shape) - (2 * rows_of(shape) + odd)
            one = jnp.where((at == 0) | (at == 1), 1.0, 0.0)
            sel[odd * Lp : (odd + 1) * Lp] = one.astype(BF16)

    @pl.when(c < 0)
    def _():
        rows = rows_of((L, C))
        for w in range(min(share, wb)):
            at = lax.rem(z * share, wb) + w
            valid = 2 * lens[z * share + t * wb + w] - s * L
            v = jnp.where(rows < valid, x[at].astype(F32), 0.0)
            macc[0] += fold(v)
            macc[1] += fold(v * v)

    @pl.when(c == -1)
    def _():
        packet, more = plane_link[0], line_link[0]
        packet[0:1] = unfold(macc[0])
        packet[1:2] = unfold(macc[1])
        meet(everyone)
        plane.start(plane_link)
        xhalo.start(0, 3)
        at = 0
        spans = []
        more[2:3] = jnp.zeros((1, C), F32)
        for ref in (g2, s2, pb, g3, s3):
            n = ref.shape[1]
            more[2:3, at : at + n] = ref[...]
            spans.append((at, n))
            at += n
        more[0:2] = plane.finish(plane_link)
        line.start(line_link)
        gather.line_start()
        state[ST1 : ST1 + 2] = line.finish(line_link)[0:2]
        for k in range(nz):
            row = line_link[1][k]
            for r, (at, n) in zip((GAIN2, SHIFT2, BIAS, GAIN3, SHIFT3), spans):
                state[r : r + 1, k * n : (k + 1) * n] = row[2:3, at : at + n]
        xhalo.finish()
        beyond_out[...] = beyond[...]
        w_copy.wait()

    @pl.when(c >= 0)
    def _():
        mean, rho = norm_of(state[ST1 : ST1 + 2], 2.0 * total_of(lens))
        scale = state[GAIN1 : GAIN1 + 1] * rho
        offset = state[SHIFT1 : SHIFT1 + 1] - mean * scale
        rows = rows_of((L, C))
        row1 = rows_of((1, C))
        row16 = rows_of((16, C))
        def activate(w):
            at = c * wb + w
            valid = 2 * lens[i * nw + at] - s * L
            a = gelu(x[w].astype(F32) * scale + offset)
            a = jnp.where(rows < valid, a, 0.0).astype(BF16)
            picked = mm(sel[...], a)
            even, odd = picked[0:Lp], picked[Lp:]
            top, end = w * Lp, (w + 1) * Lp
            before = [pltpu.roll(v, 1, 0) for v in (even, odd)]
            behind = pltpu.roll(even, Lp - 1, 0)
            for k, v in enumerate((*before, even, odd, behind)):
                X5[k, top:end] = v.astype(BF16)

            def beside(side, k, bin_at):
                a = gelu(beyond[side, k, pl.ds(at, 1), :] * scale + offset)
                here = (row1 + bin_at < valid) & (row1 + (s * L + bin_at) >= 0)
                return jnp.where(here, a, 0.0).astype(BF16).astype(F32)

            l0, l1 = beside(0, 0, -2), beside(0, 1, -1)
            r0, r1 = beside(1, 0, L), beside(1, 1, L + 1)
            start = a[0:1].astype(F32)
            for k, row in ((0, l0 + l1), (1, l1 + start)):
                X5[k, top : top + 16] = jnp.where(row16 == 0, row, before[k][0:16]).astype(BF16)
            X5[3, end - 16 : end] = (
                odd[Lp - 16 :] + jnp.where(row16 == 15, r0, 0.0)
            ).astype(BF16)
            X5[4, end - 16 : end] = jnp.where(row16 == 15, r0 + r1, behind[Lp - 16 :]).astype(BF16)

        nc = 256
        rowp = rows_of((Lp, nc))

        def convolve(first, count):
            span = slice(first * Lp, (first + count) * Lp)
            for n in range(C // nc):
                cols = slice(n * nc, (n + 1) * nc)
                taps = [X5[k, span] for k in range(plan.T1)]
                y = 0.5 * mm(jnp.concatenate(taps, axis=1), w_ref[:, cols])
                s0 = jnp.zeros((8, nc), F32)
                s1 = jnp.zeros((8, nc), F32)
                for w in range(first, first + count):
                    at = c * wb + w
                    valid = lens[i * nw + at] - s * Lp
                    v = y[(w - first) * Lp : (w - first + 1) * Lp]
                    x2[w, :, cols] = v
                    edge[0, at, :, cols] = v[:EDGE].astype(BF16)
                    edge[1, at, :, cols] = v[Lp - EDGE :].astype(BF16)
                    v = jnp.where(rowp < valid, v, 0.0)
                    s0 = s0 + fold(v)
                    s1 = s1 + fold(v * v)
                acc[0:1, cols] += unfold(s0)
                acc[1:2, cols] += unfold(s1)

        count = max(1, wb // 2)
        for first in range(0, wb, count):
            for w in range(first, first + count):
                activate(w)
            convolve(first, count)
        halo.start(c * wb, wb)

    @pl.when(c == 0)
    def _():
        gather.line_finish()
        gather.chips_start()

    @pl.when(last_step())
    def _():
        link[0][...] = acc[...]
        peers.start(link)
        gather.pair_start()
        state[ST2 : ST2 + 2] = peers.finish(link)
        halo.finish()
        gather.pair_finish()


def block_kernel(plan, lens, x2, x2_hbm, x2land, cot, w_ref, pw_ref, own_w, own_pw, old, half_state,
                 dz2, grads, pgrad, res, land, state, res_got,
                 ext, wf, wt, pw, Y3, c2, dz3, das, a3s, a3T, dos, Z3, dcT,
                 cedge, cland, cacc, dedge, dland, dacc, bedge, bacc, halo_sems, bulk_sems,
                 x2half, x2_sem, *links):
    t = pl.program_id(0)
    peers = group_peers(plan)
    s, z, i, h = plan.place()
    Lp, C, H, wb, nw, cs, g = plan.Lp, plan.C, plan.H, plan.wb, plan.nw, plan.cs, plan.g
    M = wb * Lp
    steps = plan.steps
    p0, r0, b0, g0 = block_phases(plan)[:4]
    c_link, d_link, b_link = links[:3], links[3:6], links[6:]
    c_halo = Halo(plan, cedge, cland, halo_sems.at[0])
    d_halo = Halo(plan, dedge, dland, halo_sems.at[1])
    b_halo = Halo(plan, bedge, land, halo_sems.at[2])

    def bulk(off, rows):
        to = wrap(i + off, g)
        return remote(
            res.at[to, rows],
            res_got.at[off, rows],
            bulk_sems.at[0, off],
            bulk_sems.at[1, off],
            (s, h * g + to),
        )

    def result_of(block):
        y = mm(a3s[pl.ds(pl.multiple_of(block * M, 128), M)], pw[:, pl.ds(pl.multiple_of(h * plan.Ch, 128), plan.Ch)])
        rowr = rows_of((Lp, y.shape[1]))
        for w in range(wb):
            at = block * wb + w
            valid = lens[i * plan.nw + at] - s * Lp
            r = x2half[at] + y[w * Lp : (w + 1) * Lp] + half_state[BIAS : BIAS + 1]
            r = jnp.where(rowr < valid, r, 0.0).astype(BF16).T
            for k in range(g):
                res[k, at] = r[k * cs : (k + 1) * cs]

    def send_result(block):
        result_of(block)
        for off in range(1, g):
            bulk(off, pl.ds(block * wb, wb)).start()

    half_copy = pltpu.make_async_copy(
        x2_hbm.at[:, :, pl.ds(pl.multiple_of(h * plan.Ch, 128), plan.Ch)], x2half, x2_sem
    )

    @pl.when(first_step())
    def _():
        half_copy.start()
        greet(peers.others)
        state[...] = old[...]
        cacc[...] = jnp.zeros_like(cacc)
        dacc[...] = jnp.zeros_like(dacc)
        bacc[...] = jnp.zeros_like(bacc)
        hs = H // plan.nz

        def rows_at(which, first=0):
            return pl.ds(pl.multiple_of(first + which * hs, 16), hs)

        for r in range(plan.nz):
            at = wrap(z + r, plan.nz)
            for c in range(2):
                cols = slice(c * (C // 2), (c + 1) * (C // 2))
                pw[rows_at(at), cols] = own_pw[:, cols] if r == 0 else pw_ref[c, 0, r]
                for k in range(plan.T2):
                    v = own_w[k, :, cols] if r == 0 else w_ref[c, k, r]
                    wf[rows_at(at), k * C + cols.start : k * C + cols.stop] = v
                    wt[rows_at(at, k * H), cols] = v

    @pl.when(t < p0)
    def _():
        base = pl.multiple_of(t * M, 128)
        mean, rho = norm_of(state[ST2 : ST2 + 2], total_of(lens))
        scale = state[GAIN2 : GAIN2 + 1] * rho
        offset = state[SHIFT2 : SHIFT2 + 1] - mean * scale
        rows = rows_of((Lp, C))
        rowe = rows_of((EDGE, C))

        rowh = rows_of((Lp, H))
        sums0, sums1 = jnp.zeros((8, H), F32), jnp.zeros((8, H), F32)
        nh = min(2, wb)
        for first in range(0, wb, wb // nh):
            span = range(first, first + wb // nh)
            for w in span:
                valid = lens[i * plan.nw + t * wb + w] - s * Lp
                a = jnp.where(rows < valid, gelu(x2[w] * scale + offset), 0.0)
                al = gelu(x2land[0, w].astype(F32) * scale + offset)
                al = jnp.where((rowe - EDGE < valid) & (s > 0), al, 0.0)
                ah = gelu(x2land[1, w].astype(F32) * scale + offset)
                ah = jnp.where(rowe + Lp < valid, ah, 0.0)
                ext[w, 0:EDGE] = al
                ext[w, EDGE : EDGE + Lp] = a
                ext[w, EDGE + Lp :] = ah
                top, end = w * Lp, (w + 1) * Lp
                Y3[pl.ds(base + top, Lp), 0:C] = ext[w, EDGE - DIL : EDGE - DIL + Lp].astype(BF16)
                Y3[pl.ds(base + top, Lp), C : 2 * C] = a.astype(BF16)
                Y3[pl.ds(base + top, Lp), 2 * C : 3 * C] = ext[w, EDGE + DIL : EDGE + DIL + Lp].astype(BF16)
            y = mm_nt(Y3[pl.ds(base + first * Lp, wb // nh * Lp)], wf[...])
            for w in span:
                at = t * wb + w
                valid = lens[i * plan.nw + at] - s * Lp
                v = y[(w - first) * Lp : (w - first + 1) * Lp]
                c2[at] = v
                cedge[0, at] = v[:EDGE].astype(BF16)
                cedge[1, at] = v[Lp - EDGE :].astype(BF16)
                v = jnp.where(rowh < valid, v, 0.0)
                sums0 = sums0 + fold(v)
                sums1 = sums1 + fold(v * v)
        cacc[0:1, 0:H] += unfold(sums0)
        cacc[0:1, H:] += unfold(sums1)

    @pl.when(first_step())
    def _():
        meet(peers.others)

    @pl.when(t < p0)
    def _():
        c_halo.start(t * wb, wb)

    @pl.when(t == p0 - 1)
    def _():
        c_link[0][...] = cacc[...]
        peers.start(c_link)

    here_p = (t >= p0) & (t < p0 + steps)

    @pl.when(here_p)
    def _():
        u = t - p0
        rowc = rows_of((Lp, C))
        block = pl.ds(pl.multiple_of(u * M, 128), M)
        bias = jnp.zeros((8, C), F32)
        parts = []
        for w in range(wb):
            valid = lens[i * plan.nw + u * wb + w] - s * Lp
            d = jnp.where(rowc < valid, cot[w].astype(F32), 0.0)
            bias = bias + fold(d)
            parts.append(d.astype(BF16))
        d = jnp.concatenate(parts, axis=0)
        dos[block] = d
        das[...] = mm_nt(d, pw[...])
        dacc[1:2] += unfold(bias)

    @pl.when(t == p0)
    def _():
        got = peers.finish(c_link)
        state[ST3 : ST3 + 1, 0:H] = got[:, 0:H]
        state[ST3 + 1 : ST3 + 2, 0:H] = got[:, H:]

    @pl.when(here_p)
    def _():
        u = t - p0
        block = pl.ds(pl.multiple_of(u * M, 128), M)
        rowh = rows_of((Lp, H))
        mean, rho = norm_of(state[ST3 : ST3 + 2, 0:H], total_of(lens))
        scale = state[GAIN3 : GAIN3 + 1, 0:H] * rho
        offset = state[SHIFT3 : SHIFT3 + 1, 0:H] - mean * scale
        s0, s1 = jnp.zeros((8, H), F32), jnp.zeros((8, H), F32)
        parts = []
        for w in range(wb):
            at = u * wb + w
            valid = lens[i * plan.nw + at] - s * Lp
            top, end = w * Lp, (w + 1) * Lp
            v = c2[at]
            zv = v * scale + offset
            act, slope = gelu_both(zv)
            parts.append(jnp.where(rowh < valid, act, 0.0).astype(BF16))
            dzw = das[top:end] * slope
            dz3[at] = dzw
            dedge[0, at] = dzw[:EDGE].astype(BF16)
            dedge[1, at] = dzw[Lp - EDGE :].astype(BF16)
            s0 = s0 + fold(dzw)
            s1 = s1 + fold(dzw * zv)
        a3 = jnp.concatenate(parts, axis=0)
        a3s[block] = a3
        a3T[:, block] = a3.T
        dacc[0:1, 0:H] += unfold(s0)
        dacc[0:1, H : 2 * H] += unfold(s1)
        d_halo.start(u * wb, wb)

    @pl.when(t == p0)
    def _():
        half_copy.wait()
        send_result(0)

    @pl.when(t == p0 + steps - 1)
    def _():
        d_link[0][...] = dacc[...]
        peers.start(d_link)

    @pl.when(t == r0)
    def _():
        for block in range(1, steps):
            send_result(block)
        rows = pl.ds(pl.multiple_of(h * plan.Hh, 16), plan.Hh)
        pgrad[...] = mm(a3T[rows], dos[...]).astype(BF16)

    @pl.when(t == b0)
    def _():
        got = peers.finish(d_link)
        shift = state[SHIFT3 : SHIFT3 + 1, 0:H]
        gain = state[GAIN3 : GAIN3 + 1, 0:H]
        state[SU3 : SU3 + 1, 0:H] = got[0:1, 0:H]
        state[SU3 + 1 : SU3 + 2, 0:H] = (got[0:1, H : 2 * H] - shift * got[0:1, 0:H]) / gain
        state[BSUM : BSUM + 1] = got[1:2]
        c_halo.finish()
        d_halo.finish()

    @pl.when((t >= b0) & (t < g0))
    def _():
        u = t - b0
        total = total_of(lens)
        mean3, rho3 = norm_of(state[ST3 : ST3 + 2, 0:H], total)
        gr3 = state[GAIN3 : GAIN3 + 1, 0:H] * rho3
        sg3 = state[SU3 : SU3 + 1, 0:H] / total
        gg3 = state[SU3 + 1 : SU3 + 2, 0:H] / total
        mean2, rho2 = norm_of(state[ST2 : ST2 + 2], total)
        scale2 = state[GAIN2 : GAIN2 + 1] * rho2
        offset2 = state[SHIFT2 : SHIFT2 + 1] - mean2 * scale2
        rowh = rows_of((Lp, H))
        rowe = rows_of((EDGE, H))
        rowc = rows_of((Lp, C))

        by_v = -gr3 * rho3 * gg3
        by_1 = gr3 * (mean3 * rho3 * gg3 - sg3)

        def back(dz, v):
            return gr3 * dz + by_v * v + by_1

        for w in range(wb):
            valid = lens[i * nw + u * wb + w] - s * Lp
            d = jnp.where(rowh < valid, back(dz3[u * wb + w], c2[u * wb + w]), 0.0)
            dl = back(dland[0, u * wb + w].astype(F32), cland[0, u * wb + w].astype(F32))
            dl = jnp.where((rowe - EDGE < valid) & (s > 0), dl, 0.0)
            dh = back(dland[1, u * wb + w].astype(F32), cland[1, u * wb + w].astype(F32))
            dh = jnp.where(rowe + Lp < valid, dh, 0.0)
            ext[w, 0:EDGE, 0:H] = dl
            ext[w, EDGE : EDGE + Lp, 0:H] = d
            ext[w, EDGE + Lp :, 0:H] = dh
            top, end = w * Lp, (w + 1) * Lp
            Z3[top:end, 0:H] = ext[w, EDGE + DIL : EDGE + DIL + Lp, 0:H].astype(BF16)
            Z3[top:end, H : 2 * H] = d.astype(BF16)
            Z3[top:end, 2 * H : 3 * H] = ext[w, EDGE - DIL : EDGE - DIL + Lp, 0:H].astype(BF16)

        y = mm(Z3[...], wt[...])

        M = wb * Lp
        dcT[:, pl.ds(pl.multiple_of(u * M, 128), M)] = Z3[:, H : 2 * H].T
        s0, s1 = jnp.zeros((8, C), F32), jnp.zeros((8, C), F32)
        for w in range(wb):
            at = u * wb + w
            valid = lens[i * nw + at] - s * Lp
            v = x2[w]
            zv = v * scale2 + offset2
            dzw = y[w * Lp : (w + 1) * Lp] * gelu_slope(zv)
            dzw = jnp.where(rowc < valid, dzw, 0.0)
            dz2[w] = dzw
            bedge[0, pl.ds(at, 1)] = dzw[0:1]
            bedge[1, pl.ds(at, 1)] = dzw[Lp - 1 : Lp]
            s0 = s0 + fold(dzw)
            s1 = s1 + fold(dzw * zv)
        bacc[0:1] += unfold(s0)
        bacc[1:2] += unfold(s1)

    @pl.when(t == g0 - 1)
    def _():
        b_link[0][...] = bacc[...]
        peers.start(b_link)
        b_halo.start(0, nw)

    @pl.when(last_step())
    def _():
        rows = pl.ds(pl.multiple_of(h * plan.Hh, 16), plan.Hh)
        for n in range(plan.T2):
            cols = slice(n * C, (n + 1) * C)
            grads[:, cols] = mm(dcT[rows], Y3[:, cols]).astype(BF16)

    @pl.when(last_step())
    def _():
        got = peers.finish(b_link)
        shift, gain = state[SHIFT2 : SHIFT2 + 1], state[GAIN2 : GAIN2 + 1]
        state[SU2 : SU2 + 1] = got[0:1]
        state[SU2 + 1 : SU2 + 2] = (got[1:2] - shift * got[0:1]) / gain
        b_halo.finish()
        for off in range(1, g):
            bulk(off, pl.ds(0, nw)).wait()


def block_phases(plan):
    n = plan.steps
    return n, 2 * n, 2 * n + 1, 3 * n + 1, 3 * n + 2


class Reduction:
    def __init__(self, plan, batches, out, give, mine, got, spread, half, mate, sems):
        self.plan, self.batches, self.out = plan, batches, out
        self.give, self.mine, self.got, self.spread = give, mine, got, spread
        self.half, self.mate = half, mate
        self.sems = sems
        self.s, self.z, self.i, self.h = plan.place()
        self.c = lax.rem(self.s, 2)
        self.m = lax.div(self.s, 2)
        self.chips = plan.chips

    @staticmethod
    def scratch(plan, batches):
        taps, wide = plan.T1 + 2, plan.C // 2
        full = (taps, plan.chips, plan.g, plan.rb, wide)
        part = (taps, plan.g, plan.rb, wide)
        return [
            pltpu.VMEM((taps, 2, plan.chips, plan.rb, wide), BF16),
            *[pltpu.VMEM(full, BF16)] * 4,
            *[pltpu.VMEM(part, BF16)] * 2,
            pltpu.SemaphoreType.DMA((2, len(batches), 5)),
        ]

    def copy(self, b, phase, src, dst, device):
        return remote(src, dst, self.sems.at[0, b, phase], self.sems.at[1, b, phase], device)

    def finish(self, b, phase, ref, device):
        done = self.copy(b, phase, ref, ref, device)
        done.wait_recv()
        done.wait_send()

    def taps(self, b):
        return pl.ds(*self.batches[b])

    def pair(self):
        return (2 * self.m + (1 - self.c), self.z)

    def far(self, off):
        return (2 * wrap(self.m + off, self.chips) + self.c, self.z)

    def member(self, off):
        return (self.s, self.h * self.plan.g + wrap(self.i + off, self.plan.g))

    def put(self, k, rows):
        wide = self.plan.C // 2
        for j in range(self.plan.g):
            for m in range(self.chips):
                v = rows(j, m)
                left, right = v[:, :wide], v[:, wide:]
                self.mine[k, m, j] = jnp.where(self.c == 0, left, right).astype(BF16)
                self.give[k, m, j] = jnp.where(self.c == 0, right, left).astype(BF16)

    def step0(self, b):
        taps = self.taps(b)
        self.copy(b, 0, self.give.at[taps], self.got.at[taps], self.pair()).start()

    def step1(self, b):
        taps = self.taps(b)
        self.finish(b, 0, self.got.at[taps], self.pair())
        first, count = self.batches[b]
        for k in range(first, first + count):
            v = self.mine[k].astype(F32) + self.got[k].astype(F32)
            self.mine[k] = v.astype(BF16)
        for off in range(1, self.chips):
            src = self.mine.at[taps, wrap(self.m + off, self.chips)]
            self.copy(b, 1, src, self.spread.at[taps, self.m], self.far(off)).start()

    def step2(self, b):
        taps = self.taps(b)
        self.finish(b, 1, self.spread.at[taps, pl.ds(0, self.chips - 1)], self.far(1))
        first, count = self.batches[b]
        for k in range(first, first + count):
            self.spread[k, self.m] = self.mine[k, self.m]
            v = self.spread[k, 0].astype(F32)
            for n in range(1, self.chips):
                v = v + self.spread[k, n].astype(F32)
            self.half[k] = v.astype(BF16)
        for off in range(1, self.plan.g):
            src = self.half.at[taps, wrap(self.i + off, self.plan.g)]
            self.copy(b, 2, src, self.mate.at[taps, off], self.member(off)).start()

    def step3(self, b):
        taps = self.taps(b)
        self.finish(b, 2, self.mate.at[taps, pl.ds(1, self.plan.g - 1)], self.member(1))
        first, count = self.batches[b]
        for k in range(first, first + count):
            v = self.half[k, self.i].astype(F32)
            for off in range(1, self.plan.g):
                v = v + self.mate[k, off].astype(F32)
            self.out[k, self.c, self.m] = v.astype(BF16)
        mine = self.out.at[taps, self.c, self.m]
        for off in range(1, self.chips):
            self.copy(b, 3, mine, mine, self.far(off)).start()

    def step4(self, b):
        taps = self.taps(b)
        self.finish(b, 3, self.out.at[taps, self.c, pl.ds(0, self.chips - 1)], self.far(1))
        mine = self.out.at[taps, self.c]
        self.copy(b, 4, mine, mine, self.pair()).start()

    def step5(self, b):
        self.finish(b, 4, self.out.at[self.taps(b), self.c], self.pair())


def tail_turns(plan):
    nD, T1 = plan.steps, plan.T1
    turns = [("x", 0)] + [("d", n) for n in range(1, nD)]
    xs, ws = [("x", n) for n in range(1, nD)], [("w", n) for n in range(T1)]
    for count in (2, 1, T1):
        turns += ws[:count] + xs[:1]
        xs, ws = xs[1:], ws[count:]
    return turns + xs


def tail_batches(plan):
    return [(plan.T1, 2), (0, 2)] + [(k, 1) for k in range(2, plan.T1)]


def tail_kernel(plan, lens, dz2, dzland, x2, x2land, cot, beyond, x, X5_hbm, taps_hbm, grads, pgrad,
                old, half_state,
                gz, gz_got, sums, summed,
                D3, D0T, wcat, pick, cols, y, part, split, acc, X5, X5_sems,
                taps, bulk_sems, *rest):
    t = pl.program_id(0)
    s, z, i, h = plan.place()
    L, Lp, C, wb, g, nw = plan.L, plan.Lp, plan.C, plan.wb, plan.g, plan.nw
    Ch, cs, T1 = plan.Ch, plan.cs, plan.T1
    M = wb * Lp
    nD = plan.steps
    turns = tail_turns(plan)
    last = len(turns) - 1
    peers = group_peers(plan)
    red = Reduction(plan, tail_batches(plan), *rest[:8])
    link = rest[8:]

    def member(off):
        return (s, h * g + wrap(i + off, g))

    def send(first, count):
        rows = pl.ds(first, count)
        for off in range(1, g):
            remote(
                part.at[off - 1, rows],
                gz_got.at[off, rows],
                bulk_sems.at[0, off],
                bulk_sems.at[1, off],
                member(off),
            ).start()

    def X5_copy(k):
        return pltpu.make_async_copy(X5_hbm.at[k], X5.at[k % 2], X5_sems.at[k % 2])

    def when(at):
        return pl.when(t == min(at, last))

    def turn(kind, k):
        return turns.index((kind, k)) if (kind, k) in turns else last

    def turn_of(kind):
        index = jnp.int32(0)
        here = False
        for n, (what, k) in enumerate(turns):
            if what == kind:
                index = jnp.where(t == n, k, index)
                here = (t == n) | here
        return here, index

    taps_copy = pltpu.make_async_copy(
        taps_hbm.at[:, pl.ds(pl.multiple_of(h * Ch, 128), Ch)], taps, X5_sems.at[2]
    )

    @when(0)
    def _():
        taps_copy.start()
        greet(peers.others)
        acc[...] = jnp.zeros_like(acc)
        pick[...] = pick_matrix(L)
        mean, rho = norm_of(half_state[ST1 : ST1 + 2], 2.0 * total_of(lens))
        scale = half_state[GAIN1 : GAIN1 + 1] * rho
        offset = half_state[SHIFT1 : SHIFT1 + 1] - mean * scale
        for k, row in enumerate((scale, offset)):
            cols[k] = column(row, L)

    @pl.when(t < nD)
    def _():
        total = total_of(lens)
        mean, rho = norm_of(old[ST2 : ST2 + 2], total)
        gr = old[GAIN2 : GAIN2 + 1] * rho
        sg = old[SU2 : SU2 + 1] / total
        gg = old[SU2 + 1 : SU2 + 2] / total
        rowc = rows_of((Lp, C))
        row1 = rows_of((1, C))
        row16 = rows_of((16, C))

        by_dz = 0.5 * gr
        by_v = -0.5 * gr * rho * gg
        by_1 = 0.5 * gr * (mean * rho * gg - sg)

        def back(dout, dz, v):
            return 0.5 * dout + by_dz * dz + by_v * v + by_1

        def grad_of(w):
            at = t * wb + w
            valid = lens[i * nw + at] - s * Lp
            d = back(cot[w].astype(F32), dz2[w], x2[w])
            d = jnp.where(rowc < valid, d, 0.0)
            one = pl.ds(at, 1)
            dl = back(beyond[0, 2, one, :], dzland[0, one, :], x2land[0, w, EDGE - 1 : EDGE].astype(F32))
            dl = jnp.where((row1 - 1 < valid) & (s > 0), dl, 0.0)
            dh = back(beyond[1, 2, one, :], dzland[1, one, :], x2land[1, w, 0:1].astype(F32))
            dh = jnp.where(row1 + Lp < valid, dh, 0.0)
            top, end = w * Lp, (w + 1) * Lp
            after, before = pltpu.roll(d, Lp - 1, 0), pltpu.roll(d, 1, 0)
            for n, v in enumerate((after, d, before)):
                D3[t, top:end, n * C : (n + 1) * C] = v.astype(BF16)
            D3[t, end - 16 : end, 0:C] = jnp.where(row16 == 15, dh, after[Lp - 16 :]).astype(BF16)
            D3[t, top : top + 16, 2 * C :] = jnp.where(row16 == 0, dl, before[0:16]).astype(BF16)

        for w in range(wb):
            grad_of(w)
        half = D3[t, :, pl.ds(pl.multiple_of(C + h * Ch, 128), Ch)]
        D0T[:, pl.ds(pl.multiple_of(t * M, 128), M)] = half.T

    @when(0)
    def _():
        taps_copy.wait()
        for first in range(0, Ch, 64):
            rows = slice(first, min(first + 64, Ch))
            for r, parts in enumerate((((0,), (1, 2), (3, 4)), ((0, 1), (2, 3), (4,)))):
                for k, which in enumerate(parts):
                    v = taps[which[0], rows]
                    if len(which) > 1:
                        v = (v.astype(F32) + taps[which[1], rows].astype(F32)).astype(BF16)
                    at = r * Ch
                    wcat[at + rows.start : at + rows.stop, k * C : (k + 1) * C] = v
        meet(peers.others)

    here_x, bx = turn_of("x")

    def gradient(hf, nh):
        lanes = lanes_of((Ch, L))

        def through(w):
            valid = 2 * lens[i * nw + bx * wb + w] - s * L
            top, end = w * Lp, (w + 1) * Lp
            v = x[w].T.astype(F32)
            da = jnp.concatenate([y[0:Ch, top:end], y[Ch:, top:end]], axis=1)
            da = mm(da.astype(BF16), pick[...])
            zv = v * cols[0] + cols[1]
            dzw = da * gelu_slope(zv)
            dzw = jnp.where(lanes < valid, dzw, 0.0)
            acc[0] += fold_lanes(dzw)
            acc[1] += fold_lanes(dzw * zv)
            split[w % 2] = dzw.astype(BF16)
            for off in range(g):
                rows = pl.ds(pl.multiple_of(lax.rem(i + off, g) * cs, 16), cs)
                if off == 0:
                    gz[w] = split[w % 2, rows]
                else:
                    part[off - 1, bx * wb + w] = split[w % 2, rows]

        n = wb // nh
        rows = slice(hf * n * Lp, (hf + 1) * n * Lp)
        y[:, rows] = mm_nt(wcat[...], D3[bx, rows])
        for w in range(hf * n, (hf + 1) * n):
            through(w)

    nh = 2 if wb % 2 == 0 and wb * Lp // 2 % 128 == 0 else 1

    @pl.when(here_x)
    def _():
        gradient(0, nh)
        send(bx * wb, wb // nh)

    first = min(1, last)
    table = (
        (first, 1, red.step1, 0),
        (max(turn("w", 1), first + 1), 1, red.step2, 0),
        (turn("w", 1), 1, red.step0, 1),
        (turn("x", 1), 0, red.step1, 1),
        (turn("w", 2), 1, red.step0, 2),
        (turn("x", 2), 0, red.step1, 2),
        (turn("x", 2), 1, red.step3, 0),
        (turn("x", 2), 1, red.step2, 1),
        (turn("w", 3), 1, red.step0, 3),
        (turn("w", 4), 1, red.step0, 4),
        (turn("w", 4), 1, red.step1, 3),
        (turn("w", 4), 1, red.step2, 2),
        (turn("x", 3), 0, red.step1, 4),
        (turn("x", 3), 0, red.step4, 0),
        (turn("x", 3), 0, red.step3, 1),
        (last, 1, red.step2, 3),
        (last, 1, red.step3, 2),
        (last, 1, red.step2, 4),
    )

    def between(at, end):
        return end == 0 and nh == 2 and turns[at][0] == "x"

    def go_on(entries):
        for at, _, step, batch in entries:

            @when(at)
            def _():
                step(batch)

    go_on([e for e in table if between(*e[:2])])

    if nh == 2:

        @pl.when(here_x)
        def _():
            gradient(1, nh)

    @when(0)
    def _():
        hs = plan.H // plan.nz
        rb = plan.rb
        for u in range(2):

            def rows(j, m, u=u):
                side, r = m * rb // hs, m * rb % hs
                n = 2 * side + u
                rows = slice(j * hs + r, j * hs + r + rb)
                v = grads[rows, n * C : (n + 1) * C] if n < plan.T2 else pgrad[rows]
                return v.astype(F32)

            red.put(T1 + u, rows)
        red.step0(0)

    @when(1)
    def _():
        X5_copy(0).start()
        X5_copy(1).start()

    here_w, k = turn_of("w")

    @pl.when(here_w)
    def _():
        X5_copy(k).wait()
        y[0:Ch, 0:C] = mm(D0T[...], X5[lax.rem(k, 2)])

        @pl.when(k < T1 - 2)
        def _():
            X5_copy(k + 2).start()

        rb = plan.rb
        red.put(k, lambda j, m: y[j * cs + m * rb : j * cs + (m + 1) * rb, 0:C])

    @when(turn("x", nD - 1))
    def _():
        packet = link[0]
        packet[...] = jnp.zeros_like(packet)
        packet[0:1, 0:Ch] = jnp.sum(acc[0].T, axis=0, keepdims=True)
        packet[1:2, 0:Ch] = jnp.sum(acc[1].T, axis=0, keepdims=True)
        peers.start(link)

    go_on([e for e in table if not between(*e[:2])])

    @pl.when(here_x & (bx < nD - 1))
    def _():
        if nh == 2:
            send(bx * wb + wb // nh, wb // nh)

    @when(last)
    def _():
        if nh == 2:
            send(nw - wb // 2, wb // 2)

    @when(last)
    def _():
        red.step3(3)
        red.step4(1)
        red.step4(2)
        red.step3(4)
        red.step4(3)
        got = peers.finish(link)[:, 0:Ch]
        shift, gain = half_state[SHIFT1 : SHIFT1 + 1], half_state[GAIN1 : GAIN1 + 1]
        sums[0:1] = got[0:1]
        sums[1:2] = (got[1:2] - shift * got[0:1]) / gain
        red.step4(4)
        for b in range(5):
            red.step5(b)
        own = pltpu.make_async_copy(red.out, summed, X5_sems.at[0])
        own.start()
        for off in range(1, g):
            done = remote(
                part.at[off - 1],
                gz_got.at[off],
                bulk_sems.at[0, off],
                bulk_sems.at[1, off],
                member(off),
            )
            done.wait_recv()
            done.wait_send()
        own.wait()


def input_grad_kernel(plan, wg, lens, x, gz, gz_got, sums, res, res_got, summed,
                      state, half_state,
                      out, out_result, conv_grad, dil_grad, point_grad,
                      g1, b1, g2, b2, g3, b3, pb, eye, cols, xt):
    t = pl.program_id(0)
    s, z, i, h = plan.place()
    L, Ch, cs = plan.L, plan.Ch, plan.cs
    turn = plan.nw // wg
    mine = pl.ds(pl.multiple_of(i * cs, 16), cs)

    @pl.when(first_step())
    def _():
        n = 2.0 * total_of(lens)
        mean, rho = norm_of(half_state[ST1 : ST1 + 2], n)
        gr = half_state[GAIN1 : GAIN1 + 1] * rho
        gg = sums[1:2] / n * rho
        for k, row in enumerate((gr, -gr * gg, gr * (mean * gg - sums[0:1] / n))):
            xt[...] = column(row, L)
            cols[k] = xt[mine]
        eye[...] = eye_matrix(cs, Ch, i * cs)

        def mine_of(src, at, which, count, *dsts):
            n = dsts[0].shape[1]
            for k in range(count):

                @pl.when(which == k)
                def _():
                    for dst, r in zip(dsts, at):
                        dst[...] = src[r : r + 1, k * n : (k + 1) * n]

        mine_of(sums, (1, 0), i, plan.g, g1, b1)
        mine_of(state, (SU2 + 1, SU2), z, plan.nz, g2, b2)
        mine_of(state, (SU3 + 1, SU3), z, plan.nz, g3, b3)
        mine_of(state, (BSUM,), z, plan.nz, pb)

    own = lax.div(t, turn) == i
    for w in range(wg):
        out_result[w] = jnp.where(own, res[0, w], res_got[0, w])

    C, T1, hs, rb, wide = plan.C, plan.T1, plan.H // plan.nz, plan.rb, plan.C // 2
    count = plan.NW // wg
    turns = min(count, plan.chips)
    per, every = plan.chips // turns, count // turns

    def spread(chunk):
        for n in range(per):
            m = chunk * per + n
            side, r = m * rb // hs, m * rb % hs
            for c in range(2):
                at = slice(c * wide, (c + 1) * wide)
                for k in range(T1):
                    conv_grad[k, n * rb : (n + 1) * rb, at] = summed[k, c, n].astype(F32)
                for u in range(2):
                    v = summed[T1 + u, c, n].astype(F32)
                    if 2 * side + u < plan.T2:
                        dil_grad[2 * side + u, r : r + rb, at] = v
                    else:
                        point_grad[r : r + rb, at] = v

    for chunk in range(turns):
        pl.when(t == chunk * every)(partial(spread, chunk))

    lanes = lanes_of((cs, L))
    for w in range(wg):
        valid = 2 * lens[t * wg + w] - s * L
        v = mm_nt(eye[...], x[w])
        dz = jnp.where(own, gz[w], gz_got[0, w]).astype(F32)
        r = cols[0] * dz + v * cols[1] + cols[2]
        out[w] = jnp.where(lanes < valid, r, 0.0).astype(BF16)


def call(kernel, plan, name, steps, ins, outs, scratch, flops, nbytes, cid=None):
    extra = {} if cid is None else dict(collective_id=cid, has_side_effects=True)
    return pl.pallas_call(
        partial(kernel, plan),
        grid=(steps,),
        in_specs=[SMEM] + [spec for spec, _ in ins],
        out_specs=[spec for spec, _, _ in outs],
        out_shape=[jax.ShapeDtypeStruct(shape, dtype) for _, shape, dtype in outs],
        scratch_shapes=scratch,
        compiler_params=pltpu.CompilerParams(vmem_limit_bytes=VMEM_LIMIT, **extra),
        cost_estimate=pl.CostEstimate(
            flops=int(flops), bytes_accessed=int(nbytes), transcendentals=0
        ),
        name=name,
    )


def per_device(
    inputs,
    lengths,
    input_gain,
    input_shift,
    conv_weight,
    branch_gain,
    branch_shift,
    dilated_tap_weight,
    mixer_gain,
    mixer_shift,
    point_weight,
    point_bias,
    cotangent,
):
    NW, L, C = inputs.shape
    Lp = L // 2
    nz = lax.axis_size("ch")
    R = 2
    plan = Plan(
        ns=lax.axis_size("seq"),
        nz=nz,
        R=R,
        NW=NW,
        L=L,
        C=C,
        H=mixer_gain.shape[0] * nz,
        T1=conv_weight.shape[0],
        T2=dilated_tap_weight.shape[0],
        wb=min(NW * R // nz, max(1, 512 // Lp)),
    )
    g, nw, cs, Ch, H, Hh, wb = plan.g, plan.nw, plan.cs, plan.Ch, plan.H, plan.Hh, plan.wb
    T1, T2, steps = plan.T1, plan.T2, plan.steps
    M = wb * Lp
    hs = H // nz
    lens = lengths.astype(jnp.int32)

    def row(a):
        return a.reshape(1, a.shape[0])

    def grp():
        return lax.rem(lax.axis_index("ch"), g)

    def half():
        return lax.div(lax.axis_index("ch"), g)

    def core():
        return lax.rem(lax.axis_index("seq"), 2)

    def chip4():
        return lax.div(lax.axis_index("seq"), plan.ns // 4)

    def whole(*shape):
        return pl.BlockSpec(shape, lambda t: (0,) * len(shape), pipeline_mode=pl.Buffered(1))

    def const(*shape):
        return pl.BlockSpec(shape, lambda t: (0,) * len(shape))

    def win(*shape):
        return pl.BlockSpec(shape, lambda t: (t,) + (0,) * (len(shape) - 1))

    def arg_win(n, width):
        return pl.BlockSpec((wb, n, width), lambda t: (grp() * steps + t, 0, 0))

    def ins(*pairs):
        return [p for p in pairs]

    share = NW // nz
    nm = max(1, share // wb)

    def edge_spec(n):
        return pl.BlockSpec(
            (nw, 16, C), lambda t: (grp(), n, 0), pipeline_mode=pl.Buffered(1)
        )

    def head_block(t):
        own = lax.div(lax.axis_index("ch") * share, wb) + t
        return jnp.where(t < nm, own, grp() * steps + t - nm), 0, 0

    def after(*shape):
        return pl.BlockSpec(
            shape, lambda t: (jnp.maximum(t - nm, 0),) + (0,) * (len(shape) - 1)
        )

    pairs = ins(
        (pl.BlockSpec((wb, L, C), head_block), inputs),
        (edge_spec(0), inputs),
        (edge_spec(L // 16 - 1), inputs),
        (edge_spec(0), cotangent),
        (edge_spec(Lp // 16 - 1), cotangent),
        (whole(1, cs), row(branch_gain)),
        (whole(1, cs), row(branch_shift)),
        (whole(1, cs), row(point_bias)),
        (whole(1, H // nz), row(mixer_gain)),
        (whole(1, H // nz), row(mixer_shift)),
        (ANY, conv_weight.reshape(T1 * C, C)),
        (whole(C), input_gain),
        (whole(C), input_shift),
        (
            pl.BlockSpec(
                (1, hs, C // 2),
                lambda t: (jnp.minimum(chip4(), T2 - 1), 0, core()),
                pipeline_mode=pl.Buffered(1),
            ),
            jnp.swapaxes(dilated_tap_weight, 1, 2),
        ),
        (
            pl.BlockSpec(
                (hs, C // 2), lambda t: (0, core()), pipeline_mode=pl.Buffered(1)
            ),
            point_weight,
        ),
    )
    plane, line, group = plane_peers(plan), line_peers(plan), group_peers(plan)
    state_shape = (STATE, C)
    edges2, edges3 = (2, nw, EDGE, C), (2, nw, EDGE, H)
    X5, x2, land2, state, beyond, full = call(
        lambda plan, *refs: head_kernel(plan, nm, *refs),
        plan,
        "head",
        nm + steps,
        pairs,
        [
            (
                pl.BlockSpec((T1, M, C), lambda t: (0, jnp.maximum(t - nm, 0), 0)),
                (T1, nw * Lp, C),
                BF16,
            ),
            (after(wb, Lp, C), (nw, Lp, C), F32),
            (ANY, edges2, BF16),
            (const(*state_shape), state_shape, F32),
            (const(2, 3, nw, C), (2, 3, nw, C), F32),
            (ANY, (2, T2 + 1, nz, hs, C // 2), BF16),
        ],
        [
            pltpu.VMEM((2, 8, C), F32),
            pltpu.VMEM((2, 3, nw, C), F32),
            pltpu.VMEM((2, 3, nw, C), F32),
            pltpu.VMEM((L, L), BF16),
            pltpu.VMEM(edges2, BF16),
            pltpu.VMEM((2, C), F32),
            pltpu.VMEM((T1 * C, C), BF16),
            pltpu.SemaphoreType.DMA,
            pltpu.VMEM((hs, C // 2), BF16),
            pltpu.SemaphoreType.DMA((2, 4)),
            HALO_SEMS,
            HALO_SEMS,
        ]
        + plane.scratch(2, C)
        + line.scratch(3, C)
        + group.scratch(2, C),
        2 * nw * Lp * T1 * C * C,
        nw * Lp * C * 20,
        cid=1,
    )(lens, *[a for _, a in pairs])

    taps_spec = whole(2, T2, nz, hs, C // 2)
    pw_spec = pl.BlockSpec(
        (2, 1, nz, hs, C // 2), lambda t: (0, T2, 0, 0, 0), pipeline_mode=pl.Buffered(1)
    )

    def early(*shape):
        return pl.BlockSpec(
            shape, lambda t: (jnp.minimum(t, steps - 1),) + (0,) * (len(shape) - 1)
        )

    def early_land(width):
        return pl.BlockSpec(
            (2, wb, EDGE, width), lambda t: (0, jnp.minimum(t, steps - 1), 0, 0)
        )

    def half_of(n):
        return pl.BlockSpec((n, Ch), lambda t: (0, half()), pipeline_mode=pl.Buffered(1))

    cot_spec = pl.BlockSpec(
        (wb, Lp, C), lambda t: (grp() * steps + jnp.minimum(t, steps - 1), 0, 0)
    )

    p0, r0, b0, g0, block_steps = block_phases(plan)

    def at_phase(first):
        return lambda t: jnp.clip(t - first, 0, steps - 1)

    in_p, in_b = at_phase(p0), at_phase(b0)
    pairs = ins(
        (
            pl.BlockSpec(
                (wb, Lp, C),
                lambda t: (jnp.where(t < p0 + steps, jnp.minimum(t, steps - 1), in_b(t)), 0, 0),
            ),
            x2,
        ),
        (ANY, x2),
        (early_land(C), land2),
        (pl.BlockSpec((wb, Lp, C), lambda t: (grp() * steps + in_p(t), 0, 0)), cotangent),
        (taps_spec, full),
        (pw_spec, full),
        (whole(T2, hs, C), jnp.swapaxes(dilated_tap_weight, 1, 2)),
        (whole(hs, C), point_weight),
        (whole(*state_shape), state),
        (half_of(STATE), state),
    )
    dz2, grads, pgrad, res, dland2, state, res_got = call(
        block_kernel,
        plan,
        "block",
        block_steps,
        pairs,
        [
            (pl.BlockSpec((wb, Lp, C), lambda t: (in_b(t), 0, 0)), (nw, Lp, C), F32),
            (const(Hh, T2 * C), (Hh, T2 * C), BF16),
            (const(Hh, C), (Hh, C), BF16),
            (const(g, nw, cs, Lp), (g, nw, cs, Lp), BF16),
            (ANY, (2, nw, C), F32),
            (const(*state_shape), state_shape, F32),
            (ANY, (g, nw, cs, Lp), BF16),
        ],
        [
            pltpu.VMEM((wb, Lp + 2 * EDGE, C), F32),
            pltpu.VMEM((H, T2 * C), BF16),
            pltpu.VMEM((T2 * H, C), BF16),
            pltpu.VMEM((H, C), BF16),
            pltpu.VMEM((nw * Lp, T2 * C), BF16),
            pltpu.VMEM((nw, Lp, H), F32),
            pltpu.VMEM((nw, Lp, H), F32),
            pltpu.VMEM((M, H), F32),
            pltpu.VMEM((nw * Lp, H), BF16),
            pltpu.VMEM((H, nw * Lp), BF16),
            pltpu.VMEM((nw * Lp, C), BF16),
            pltpu.VMEM((M, T2 * H), BF16),
            pltpu.VMEM((H, nw * Lp), BF16),
            pltpu.VMEM(edges3, BF16),
            pltpu.VMEM(edges3, BF16),
            pltpu.VMEM((1, 2 * H), F32),
            pltpu.VMEM(edges3, BF16),
            pltpu.VMEM(edges3, BF16),
            pltpu.VMEM((2, C), F32),
            pltpu.VMEM((2, nw, C), F32),
            pltpu.VMEM((2, C), F32),
            pltpu.SemaphoreType.DMA((3, 2, 2)),
            pltpu.SemaphoreType.DMA((2, g)),
            pltpu.VMEM((nw, Lp, Ch), F32),
            pltpu.SemaphoreType.DMA,
        ]
        + group.scratch(1, 2 * H)
        + group.scratch(2, C)
        + group.scratch(2, C),
        nw * Lp * C * H * (6 * T2 + 6),
        nw * Lp * C * 30,
        cid=3,
    )(lens, *[a for _, a in pairs])

    chips, rb = plan.chips, plan.rb
    turns_t = tail_turns(plan)

    def x_block(t):
        block = jnp.int32(0)
        for n, (what, k) in enumerate(turns_t):
            if what == "x":
                block = jnp.where(t >= n, k, block)
        return block

    sshape = (T1 + 2, 2, chips, rb, C // 2)
    pairs = ins(
        (early(wb, Lp, C), dz2),
        (whole(2, nw, C), dland2),
        (early(wb, Lp, C), x2),
        (early_land(C), land2),
        (cot_spec, cotangent),
        (whole(2, 3, nw, C), beyond),
        (
            pl.BlockSpec(
                (wb, L, Ch), lambda t: (grp() * steps + x_block(t), 0, half())
            ),
            inputs,
        ),
        (ANY, X5),
        (ANY, conv_weight),
        (whole(Hh, T2 * C), grads),
        (whole(Hh, C), pgrad),
        (whole(*state_shape), state),
        (half_of(STATE), state),
    )
    gz, gz_got, sums1, summed = call(
        tail_kernel,
        plan,
        "tail",
        len(turns_t),
        pairs,
        [
            (pl.BlockSpec((wb, cs, L), lambda t: (x_block(t), 0, 0)), (nw, cs, L), BF16),
            (ANY, (g, nw, cs, L), BF16),
            (const(2, Ch), (2, Ch), F32),
            (ANY, sshape, BF16),
        ],
        [
            pltpu.VMEM((steps, M, 3 * C), BF16),
            pltpu.VMEM((Ch, nw * Lp), BF16),
            pltpu.VMEM((2 * Ch, 3 * C), BF16),
            pltpu.VMEM((L, L), BF16),
            pltpu.VMEM((2, Ch, L), F32),
            pltpu.VMEM((2 * Ch, max(M, C)), F32),
            pltpu.VMEM((g - 1, nw, cs, L), BF16),
            pltpu.VMEM((2, Ch, L), BF16),
            pltpu.VMEM((2, Ch, min(L, 128)), F32),
            pltpu.VMEM((2, nw * Lp, C), BF16),
            pltpu.SemaphoreType.DMA((3,)),
            pltpu.VMEM((T1, Ch, C), BF16),
            pltpu.SemaphoreType.DMA((2, g)),
        ]
        + Reduction.scratch(plan, tail_batches(plan))
        + group.scratch(2, C),
        2 * nw * Lp * (6 + T1) * C * Ch,
        nw * Lp * C * 40,
        cid=6,
    )(lens, *[a for _, a in pairs])

    wg = min(2 * wb, nw)
    count = NW // wg
    turn = nw // wg
    turns = min(count, chips)

    def own_block(t):
        return jnp.where(lax.div(t, turn) == grp(), lax.rem(t, turn), 0)

    def got_slot(t):
        off = lax.rem(grp() - lax.div(t, turn) + g, g)
        return jnp.maximum(off, 1), jnp.where(off > 0, lax.rem(t, turn), 0)

    pairs = ins(
        (pl.BlockSpec((wg, L, Ch), lambda t: (t, 0, half())), inputs),
        (pl.BlockSpec((wg, cs, L), lambda t: (own_block(t), 0, 0)), gz),
        (pl.BlockSpec((1, wg, cs, L), lambda t: got_slot(t) + (0, 0)), gz_got),
        (whole(2, Ch), sums1),
        (pl.BlockSpec((1, wg, cs, Lp), lambda t: (grp(), own_block(t), 0, 0)), res),
        (pl.BlockSpec((1, wg, cs, Lp), lambda t: got_slot(t) + (0, 0)), res_got),
        (
            pl.BlockSpec(
                (T1 + 2, 2, chips // turns, rb, C // 2),
                lambda t: (0, 0, t * turns // count, 0, 0),
            ),
            summed,
        ),
        (whole(*state_shape), state),
        (half_of(STATE), state),
    )
    outs = call(
        lambda plan, *refs: input_grad_kernel(plan, wg, *refs),
        plan,
        "input_grad",
        count,
        pairs,
        [
            (win(wg, cs, L), (NW, cs, L), BF16),
            (win(wg, cs, Lp), (NW, cs, Lp), BF16),
            (
                pl.BlockSpec((T1, cs // turns, C), lambda t: (0, t * turns // count, 0)),
                (T1, cs, C),
                F32,
            ),
            (const(T2, hs, C), (T2, hs, C), F32),
            (const(hs, C), (hs, C), F32),
        ]
        + [(const(1, n), (1, n), F32) for n in (cs, cs, cs, cs, hs, hs, cs)],
        [
            pltpu.VMEM((cs, Ch), BF16),
            pltpu.VMEM((3, cs, L), F32),
            pltpu.VMEM((Ch, L), F32),
        ],
        2 * NW * L * Ch * cs,
        NW * L * cs * 8,
    )(lens, *[a for _, a in pairs])
    grad, result, conv_grad, dil_grad, point_grad = outs[:5]
    g1, b1, g2, b2, g3, b3, pb = [a[0] for a in outs[5:]]
    return (
        jnp.swapaxes(result, 1, 2),
        jnp.swapaxes(grad, 1, 2),
        jnp.swapaxes(conv_grad, 1, 2),
        g1,
        b1,
        g2,
        b2,
        jnp.swapaxes(dil_grad, 1, 2),
        g3,
        b3,
        point_grad,
        pb,
    )


def solution(mesh):
    in_specs = (
        P(None, "seq", None),
        P(),
        P(),
        P(),
        P(),
        P("ch"),
        P("ch"),
        P(None, None, "ch"),
        P("ch"),
        P("ch"),
        P("ch", None),
        P("ch"),
        P(None, "seq", None),
    )
    out_specs = (
        P(None, "seq", "ch"),
        P(None, "seq", "ch"),
        P(None, None, "ch"),
        P("ch"),
        P("ch"),
        P("ch"),
        P("ch"),
        P(None, None, "ch"),
        P("ch"),
        P("ch"),
        P("ch", None),
        P("ch"),
    )
    return jax.shard_map(
        per_device, mesh=mesh, in_specs=in_specs, out_specs=out_specs, check_vma=False
    )
```
